32 devices in a mesh: dp: 4 (over y, core), seq: 8 (over z, x).
Axes of the slice: x: 2, y: 2, z: 4, core: 2. Of those that a mesh axis runs over, the one named last changes fastest.
Arguments:
- x_in: bfloat16 [48, 512, 1024], P('dp', None, 'seq'), may hold values from -6 to 6
- cond: bfloat16 [48, 512, 1024], P('dp', None, 'seq'), may hold values from -6 to 6
- segment_ids: int32 [48, 1024], P('dp'), may hold values from 0 to 3, as said below
- diffusion_steps: int32 [48], P('dp'), may hold values from 0 to 999
- prompt: bfloat16 [48, 128, 512], P('dp', 'seq'), may hold values from -6 to 6
- prompt_lengths: int32 [48], P('dp'), may hold values from 32 to 128, as said below
- w_step: bfloat16 [512, 512], P('dp'), may hold values from -0.25 to 0.25
- w_conv: bfloat16 [3, 512, 1024], P(None, 'dp'), may hold values from -0.15625 to 0.15625
- w_cond: bfloat16 [512, 1024], P('dp'), may hold values from -0.25 to 0.25
- w_res: bfloat16 [512, 512], P('dp'), may hold values from -0.75 to 0.75
- w_skip: bfloat16 [512, 512], P('dp'), may hold values from -0.75 to 0.75
- queries: bfloat16 [32, 512], P(None, 'dp'), may hold values from -6 to 6
- w_query: bfloat16 [512, 512], P('dp'), may hold values from -0.25 to 0.25
- w_key: bfloat16 [512, 512], P('dp'), may hold values from -0.25 to 0.25
- w_value: bfloat16 [512, 512], P('dp'), may hold values from -0.25 to 0.25
- w_attn_out: bfloat16 [512, 512], P('dp'), may hold values from -2 to 2
- w_film: bfloat16 [512, 2, 512], P('dp', None, 'seq'), may hold values from -0.25 to 0.25
- d_out: bfloat16 [48, 512, 1024], P('dp', None, 'seq'), may hold values from -6 to 6
- d_skip: bfloat16 [48, 512, 1024], P('dp', None, 'seq'), may hold values from -6 to 6
Outputs:
- layer_out: bfloat16 [48, 512, 1024], P('dp', None, 'seq')
- skip_out: bfloat16 [48, 512, 1024], P('dp', None, 'seq')
- grad_input: bfloat16 [48, 512, 1024], P('dp', None, 'seq')
- grad_w_step: float32 [512, 512], P('dp')
- grad_w_conv: float32 [3, 512, 1024], P(None, 'dp')
- grad_w_cond: float32 [512, 1024], P('dp')
- grad_w_res: float32 [512, 512], P('dp')
- grad_w_skip: float32 [512, 512], P('dp')
- grad_queries: float32 [32, 512], P(None, 'dp')
- grad_w_query: float32 [512, 512], P('dp')
- grad_w_key: float32 [512, 512], P('dp')
- grad_w_value: float32 [512, 512], P('dp')
- grad_w_attn_out: float32 [512, 512], P('dp')
- grad_w_film: float32 [512, 2, 512], P('dp', None, 'seq')
The draws below stay inside these ranges and needn't reach their ends.
Inputs may be any that keep to these rules, and one draw needn't show every extreme that they name: `segment_ids`: utterance numbers never fall along a row and every nonempty utterance spans a multiple of 128 frames; in every aligned block of 12 rows one row, drawn from the seed, holds a single utterance. `prompt_lengths`: in every aligned block of 12 rows one row, drawn from the seed, has the whole prompt.
All inputs are finite; a program needn't handle non-finite values.
Results may differ from the reference program's by a relative error of at most 0.018.
Values may be sent and summed in bfloat16 or wider, within the bound.
No kernel may reach another device: no remote copies, remote signals or barrier semaphores. Data moves between devices by JAX's collectives and lax.ppermute only.
A program may use at most 192 MiB of HBM per device.

```python
import math
import jax
import jax.numpy as jnp
from jax import lax

C = 512
HEADS = 8
QUERIES = 32
HEAD_DIM = 64
DILATION_STEP = 4
SEGS = 4
NSTEPS = 1000
MB = 3
LENGTH = 1024
ROWS = 4
ROWS_ALL = 48
PROMPT = 128


def draw_segment_ids(key, part):
    key = jax.random.fold_in(key, 11)
    key_cuts, key_single = jax.random.split(key)
    grain = LENGTH // 8
    cut_points = jax.random.randint(key_cuts, (ROWS_ALL, SEGS - 1), 1, 8) * grain
    group_rows = MB * ROWS
    chosen = jax.random.randint(key_single, (ROWS_ALL // group_rows,), 0, group_rows)
    single = jnp.arange(ROWS_ALL, dtype=jnp.int32) % group_rows == jnp.repeat(chosen, group_rows)
    cut_points = jnp.where(single[:, None], LENGTH, cut_points)
    positions = jnp.arange(LENGTH, dtype=jnp.int32)
    return jnp.sum((positions[None, None, :] >= cut_points[:, :, None]).astype(jnp.int32), axis=1).astype(jnp.int32)


def draw_prompt_lengths(key, part):
    key = jax.random.fold_in(key, 23)
    key_lengths, key_single = jax.random.split(key)
    lengths_drawn = jax.random.randint(key_lengths, (ROWS_ALL,), PROMPT // 4, PROMPT + 1)
    group_rows = MB * ROWS
    chosen = jax.random.randint(key_single, (ROWS_ALL // group_rows,), 0, group_rows)
    whole = jnp.arange(ROWS_ALL, dtype=jnp.int32) % group_rows == jnp.repeat(chosen, group_rows)
    return jnp.where(whole, PROMPT, lengths_drawn).astype(jnp.int32)


def touch_ends(drawn, key, low, largest):
    longest = drawn.shape.index(max(drawn.shape))
    spots = []
    for shift in (0, 1):
        where = [jax.random.randint(jax.random.fold_in(key, axis), (), 0, length) for axis, length in enumerate(drawn.shape)]
        where[longest] = (where[longest] + shift) % drawn.shape[longest]
        spots.append(tuple(where))
    return drawn.at[spots[0]].set(low).at[spots[1]].set(largest)


def block_levels(rng, dims, cuts, smallest, high):
    loudness = 1.0
    for axis_at, blocks in cuts:
        draws = jax.random.uniform(jax.random.fold_in(jax.random.fold_in(rng, 6), axis_at), (blocks,), jnp.float32, smallest / len(cuts), high / len(cuts))
        loudness = loudness * jnp.repeat(jnp.exp(draws), dims[axis_at] // blocks).reshape((-1,) + (1,) * (len(dims) - 1 - axis_at))
    return loudness


def normal_values(rng, extent, scale, limit, cuts=(), kind=jnp.bfloat16):
    result = jax.random.normal(rng, extent, jnp.float32) * scale
    if len(cuts) > 0:
        result = block_levels(rng, extent, cuts, -0.22, 0.18) * result
    return jnp.clip(result, min=-limit, max=limit).astype(kind)


def setup_inputs(seed: int = 0) -> dict:
    splits = jax.random.split(jax.random.key(seed), 20)
    return {
        "x_in": normal_values(splits[0], (ROWS_ALL, C, LENGTH), 1.0, 6.0, ((0, 4), (2, 8))),
        "cond": normal_values(splits[1], (ROWS_ALL, C, LENGTH), 1.0, 6.0, ((0, 4), (2, 8))),
        "segment_ids": draw_segment_ids(jax.random.fold_in(splits[19], 71), 0),
        "diffusion_steps": touch_ends(jax.random.randint(splits[3], (ROWS_ALL,), 0, NSTEPS), jax.random.fold_in(splits[3], 1), 0, NSTEPS - 1).astype(jnp.int32),
        "prompt": normal_values(splits[4], (ROWS_ALL, PROMPT, C), 1.0, 6.0, ((0, 4), (1, 8))),
        "prompt_lengths": draw_prompt_lengths(jax.random.fold_in(splits[19], 71), 0),
        "w_step": normal_values(splits[6], (C, C), C ** -0.5, 0.25, ((0, 4),)),
        "w_conv": normal_values(splits[7], (3, C, 2 * C), (3 * C) ** -0.5, 0.15625, ((1, 4),)),
        "w_cond": normal_values(splits[8], (C, 2 * C), C ** -0.5, 0.25, ((0, 4),)),
        "w_res": normal_values(splits[9], (C, C), (C // 8) ** -0.5, 0.75, ((0, 4),)),
        "w_skip": normal_values(splits[10], (C, C), (C // 8) ** -0.5, 0.75, ((0, 4),)),
        "queries": normal_values(splits[11], (QUERIES, C), 1.0, 6.0, ((1, 4),)),
        "w_query": normal_values(splits[12], (C, C), C ** -0.5, 0.25, ((0, 4),)),
        "w_key": normal_values(splits[13], (C, C), C ** -0.5, 0.25, ((0, 4),)),
        "w_value": normal_values(splits[14], (C, C), C ** -0.5, 0.25, ((0, 4),)),
        "w_attn_out": normal_values(splits[15], (C, C), (C // 64) ** -0.5, 2.0, ((0, 4),)),
        "w_film": normal_values(splits[16], (C, 2, C), C ** -0.5, 0.25, ((0, 4), (2, 8))),
        "d_out": normal_values(splits[17], (ROWS_ALL, C, LENGTH), 1.0, 6.0, ((0, 4), (2, 8))),
        "d_skip": normal_values(splits[18], (ROWS_ALL, C, LENGTH), 1.0, 6.0, ((0, 4), (2, 8))),
    }


SQRT_HALF = 0.7071067811865476
NORM_EPS = 1e-05
MASKED_SCORE = -1e+30
FULL_PRECISION = lax.Precision.HIGHEST

@jax.custom_vjp
def low(v):
    return lax.optimization_barrier(v.astype(jnp.bfloat16)).astype(jnp.float32)

@jax.custom_vjp
def low_back(v):
    return v

def low_keep(v):
    return (low(v), None)

def low_pass(kept, grad):
    return (grad,)

def back_keep(v):
    return (v, None)

def back_low(kept, grad):
    return (low(grad),)
low.defvjp(low_keep, low_pass)
low_back.defvjp(back_keep, back_low)

def step_embedding(diffusion_steps, channel_count):
    half_width = channel_count // 2
    frequency = jnp.exp(jnp.arange(half_width, dtype=jnp.float32) * (-math.log(10000.0) / half_width))
    angles = diffusion_steps.astype(jnp.float32)[:, None] * frequency[None, :]
    return jnp.concatenate([jnp.sin(angles), jnp.cos(angles)], axis=1)

def wavenet_film(params, x_rows, cond_rows, segment_rows, step_rows, prompt_rows, length_rows):
    w_step, w_conv, w_cond, w_res, w_skip, queries, w_query, w_key, w_value, w_attn_out, w_film = params
    row_count = x_rows.shape[0]
    frame_total = x_rows.shape[2]
    prompt_count = prompt_rows.shape[1]
    embedding = low(step_embedding(step_rows, C))
    step_lift = jnp.dot(embedding, w_step, precision=FULL_PRECISION)
    shifted_rows = low(x_rows + step_lift[:, :, None])
    padded_rows = jnp.pad(shifted_rows, ((0, 0), (0, 0), (DILATION_STEP, DILATION_STEP)))
    segment_padding = jnp.pad(segment_rows, ((0, 0), (DILATION_STEP, DILATION_STEP)), constant_values=-1)
    pre_gate = jnp.einsum('co,rct->rot', w_cond, cond_rows, precision=FULL_PRECISION)
    for kernel_tap_index in range(3):
        valid_mask = (segment_padding[:, kernel_tap_index * DILATION_STEP:kernel_tap_index * DILATION_STEP + frame_total] == segment_rows).astype(jnp.float32)
        kernel_tap_input = padded_rows[:, :, kernel_tap_index * DILATION_STEP:kernel_tap_index * DILATION_STEP + frame_total] * valid_mask[:, None, :]
        pre_gate = pre_gate + jnp.einsum('co,rct->rot', w_conv[kernel_tap_index], kernel_tap_input, precision=FULL_PRECISION)
    pre_gate = low_back(pre_gate)
    gated = low(jnp.tanh(pre_gate[:, :C]) * jax.nn.sigmoid(pre_gate[:, C:]))
    skip_part = jnp.einsum('cd,rct->rdt', w_skip, gated, precision=FULL_PRECISION)
    res_term = low_back(jnp.einsum('cd,rct->rdt', w_res, gated, precision=FULL_PRECISION))
    mid_state = low_back(low((x_rows + res_term) * SQRT_HALF))
    seg_table = (segment_rows[:, None, :] == jnp.arange(SEGS, dtype=jnp.int32)[None, :, None]).astype(jnp.float32)
    counts = jnp.maximum(lax.optimization_barrier(jnp.sum(seg_table, axis=2)), 1.0)
    seg_means = jnp.einsum('rct,rst->rcs', mid_state, seg_table, precision=FULL_PRECISION) / counts[:, None, :]
    seg_square = jnp.einsum('rct,rst->rcs', mid_state * mid_state, seg_table, precision=FULL_PRECISION) / counts[:, None, :]
    inv_scale = lax.rsqrt(seg_square - seg_means * seg_means + NORM_EPS)
    mean_frames = jnp.einsum('rcs,rst->rct', seg_means, seg_table, precision=FULL_PRECISION)
    scale_frames = jnp.einsum('rcs,rst->rct', inv_scale, seg_table, precision=FULL_PRECISION)
    normed = (mid_state - mean_frames) * scale_frames
    query_proj = jnp.dot(queries, w_query, precision=FULL_PRECISION).reshape(QUERIES, HEADS, HEAD_DIM)
    key_heads = low_back(jnp.einsum('rpc,cd->rpd', prompt_rows, w_key, precision=FULL_PRECISION))
    value_heads = low_back(jnp.einsum('rpc,cd->rpd', prompt_rows, w_value, precision=FULL_PRECISION))
    key_heads = key_heads.reshape(row_count, prompt_count, HEADS, HEAD_DIM)
    value_heads = value_heads.reshape(row_count, prompt_count, HEADS, HEAD_DIM)
    scores = jnp.einsum('qhd,rphd->rhqp', query_proj, key_heads, precision=FULL_PRECISION) / math.sqrt(HEAD_DIM)
    live_mask = (jnp.arange(prompt_count, dtype=jnp.int32)[None, :] < length_rows[:, None])[:, None, None, :]
    scores = jnp.where(live_mask, scores, MASKED_SCORE)
    peak_score = lax.optimization_barrier(jnp.max(scores, axis=3, keepdims=True))
    attn_probs = jnp.exp(scores - peak_score) * live_mask.astype(jnp.float32)
    attn_probs = attn_probs / lax.optimization_barrier(jnp.sum(attn_probs, axis=3, keepdims=True))
    attended = jnp.einsum('rhqp,rphd->rhqd', attn_probs, value_heads, precision=FULL_PRECISION)
    pooled = low(lax.optimization_barrier(jnp.mean(attended, axis=2)).reshape(row_count, C))
    memory = low_back(jnp.dot(pooled, w_attn_out, precision=FULL_PRECISION))
    film_params = low_back(jnp.einsum('rc,cgk->rgk', low(memory), w_film, precision=FULL_PRECISION))
    layer_out = mid_state + film_params[:, 0, :, None] * normed + film_params[:, 1, :, None]
    return (layer_out, skip_part)

def reference(x_in, cond, segment_ids, diffusion_steps, prompt, prompt_lengths, w_step, w_conv, w_cond, w_res, w_skip, queries, w_query, w_key, w_value, w_attn_out, w_film, d_out, d_skip):
    params = tuple((tensor.astype(jnp.float32) for tensor in (w_step, w_conv, w_cond, w_res, w_skip, queries, w_query, w_key, w_value, w_attn_out, w_film)))
    block_count = ROWS_ALL // 2

    def blocks(array):
        return array.reshape((block_count, 2) + array.shape[1:])

    def one_block(running, inputs):
        x_rows, cond_rows, segment_rows, step_rows, prompt_rows, length_rows, out_cot, skip_cot = inputs

        def forward(weights, rows_in):
            return wavenet_film(weights, rows_in, cond_rows.astype(jnp.float32), segment_rows, step_rows, prompt_rows.astype(jnp.float32), length_rows)
        results, pullback = jax.vjp(forward, params, x_rows.astype(jnp.float32))
        grad_params, grad_rows = pullback((out_cot.astype(jnp.float32), skip_cot.astype(jnp.float32)))
        running = tuple((current + gradient for current, gradient in zip(running, grad_params)))
        return (running, (results[0].astype(jnp.bfloat16), results[1].astype(jnp.bfloat16), grad_rows.astype(jnp.bfloat16)))
    initial = tuple((jnp.zeros_like(tensor) for tensor in params))
    totals, (layer_blocks, skip_blocks, grad_blocks) = lax.scan(one_block, initial, (blocks(x_in), blocks(cond), blocks(segment_ids), blocks(diffusion_steps), blocks(prompt), blocks(prompt_lengths), blocks(d_out), blocks(d_skip)))
    shape_out = (ROWS_ALL, C, LENGTH)
    return (layer_blocks.reshape(shape_out), skip_blocks.reshape(shape_out), grad_blocks.reshape(shape_out), totals[0], totals[1], totals[2], totals[3], totals[4], totals[5], totals[6], totals[7], totals[8], totals[9], totals[10])
```

```python
import functools
import math

import jax
import jax.numpy as jnp
from jax import lax
from jax.experimental import pallas as pl
from jax.experimental.pallas import tpu as pltpu
from jax.sharding import PartitionSpec as P

C = 512
HEADS = 8
QUERIES = 32
HEAD_DIM = 64
SHIFT = 4
SQRT_HALF = 0.7071067811865476
NORM_EPS = 1e-05
MASKED_SCORE = -1e30
LANES = 128
RP = 16
F32 = jnp.float32
BF16 = jnp.bfloat16
VMEM_BYTES = 50 * 1024 * 1024


def nn(a, b):
    return lax.dot_general(a, b, (((1,), (0,)), ((), ())), preferred_element_type=F32)


def nt(a, b):
    return lax.dot_general(a, b, (((1,), (1,)), ((), ())), preferred_element_type=F32)


def parts(v, count):
    out = []
    for _ in range(count):
        low = v.astype(BF16)
        out.append(low)
        v = v - low.astype(F32)
    return jnp.concatenate(out, axis=0)


def fold(v, count):
    rows = v.shape[0] // count
    total = v[:rows]
    for k in range(1, count):
        total = total + v[k * rows : (k + 1) * rows]
    return total


def lane_ids(shape):
    return lax.broadcasted_iota(jnp.int32, shape, len(shape) - 1)


def call(kernel, out_shape, name, flops=0, bytes_accessed=0, **kw):
    return pl.pallas_call(
        kernel,
        out_shape=out_shape,
        name=name,
        cost_estimate=pl.CostEstimate(
            flops=int(flops), bytes_accessed=int(bytes_accessed), transcendentals=0
        ),
        compiler_params=pltpu.CompilerParams(vmem_limit_bytes=VMEM_BYTES),
        **kw,
    )


def sds(shape, dtype):
    return jax.ShapeDtypeStruct(shape, dtype)


VM = pl.BlockSpec(memory_space=pltpu.VMEM)
SM = pl.BlockSpec(memory_space=pltpu.SMEM)


def whole(shape):
    return pl.BlockSpec(shape, lambda i: (0,) * len(shape), pipeline_mode=pl.Buffered(1))


def edge_kernel(x_ref, first_ref, last_ref):
    rows = x_ref.shape[0]
    lane = lane_ids((C, LANES))
    first = jnp.zeros((C, LANES), F32)
    last = jnp.zeros((C, LANES), F32)
    for r in range(rows):
        v = x_ref[r].astype(F32)
        here = (lane // SHIFT) == r
        first = jnp.where(here, pltpu.roll(v, SHIFT * r, 1) if r else v, first)
        last = jnp.where(here, pltpu.roll(v, SHIFT * r + SHIFT, 1), last)
    first_ref[...] = first.astype(BF16)
    last_ref[...] = last.astype(BF16)


def forward_kernel(
    csh,
    flags_ref,
    x_ref,
    cond_ref,
    dout_ref,
    left_ref,
    right_ref,
    emb_ref,
    step_ref,
    w_ref,
    inp_ref,
    tanh_ref,
    sig_ref,
    gated_ref,
    skip_ref,
    mid_ref,
    stats_ref,
    wt_ref,
    rst_ref,
    lift_ref,
    acc_ref,
):
    i = pl.program_id(0)
    lane = lane_ids((C, LANES))

    @pl.when(i == 0)
    def _():
        for k in range(4):
            wt_ref[:, k * C : (k + 1) * C] = w_ref[:, k].reshape(C, 2 * C).T
        rst_ref[...] = w_ref[:, 4].reshape(C, 2 * C).T
        lift = nn(emb_ref[...], step_ref[...].reshape(C, C))
        lift = jnp.concatenate([lift, jnp.zeros((LANES - RP, C), F32)], axis=0)
        lift_ref[...] = lift.T
        acc_ref[...] = jnp.zeros((C, LANES), F32)

    lift = pltpu.roll(lift_ref[...], lax.rem(LANES - 2 * i, LANES), 1)
    left = left_ref[...].astype(F32)
    right = right_ref[...].astype(F32)
    for j in range(2):
        r = 2 * i + j
        lc = lift[:, j : j + 1]
        sh = (x_ref[j].astype(F32) + lc).astype(BF16)
        shf = sh.astype(F32)
        lh = pltpu.roll(left, lax.rem(LANES - SHIFT * r, LANES), 1)
        lh = jnp.where(flags_ref[0, r] > 0, (lh + lc).astype(BF16).astype(F32), 0.0)
        rh = pltpu.roll(right, LANES - SHIFT - SHIFT * r, 1)
        rh = jnp.where(flags_ref[1, r] > 0, (rh + lc).astype(BF16).astype(F32), 0.0)
        cols = slice(j * LANES, (j + 1) * LANES)
        inp_ref[0:C, cols] = jnp.where(lane < SHIFT, lh, pltpu.roll(shf, SHIFT, 1)).astype(BF16)
        inp_ref[C : 2 * C, cols] = sh
        inp_ref[2 * C : 3 * C, cols] = jnp.where(
            lane >= LANES - SHIFT, rh, pltpu.roll(shf, LANES - SHIFT, 1)
        ).astype(BF16)
        inp_ref[3 * C : 4 * C, cols] = cond_ref[j]
    pre = nn(wt_ref[...], inp_ref[...])
    th = jnp.tanh(pre[:C])
    sg = jax.nn.sigmoid(pre[C:])
    tanh_ref[...] = th
    sig_ref[...] = sg
    g = (th * sg).astype(BF16)
    gated_ref[...] = g
    rs = nn(rst_ref[...], g)
    acc = acc_ref[...]
    for j in range(2):
        r = 2 * i + j
        cols = slice(j * LANES, (j + 1) * LANES)
        skip_ref[j] = rs[C:, cols].astype(BF16)
        mid = ((x_ref[j].astype(F32) + rs[:C, cols]) * SQRT_HALF).astype(BF16)
        mid_ref[:, cols] = mid
        mf = mid.astype(F32)
        df = dout_ref[j].astype(F32)
        total = jnp.sum(mf, axis=1, keepdims=True)
        dev = mf - total * (1.0 / LANES)
        acc = jnp.where(lane == r, total, acc)
        acc = jnp.where(lane == RP + r, jnp.sum(dev * dev, axis=1, keepdims=True), acc)
        acc = jnp.where(lane == 2 * RP + r, jnp.sum(df, axis=1, keepdims=True), acc)
        acc = jnp.where(lane == 3 * RP + r, jnp.sum(df * dev, axis=1, keepdims=True), acc)
    acc_ref[...] = acc

    @pl.when(i == pl.num_programs(0) - 1)
    def _():
        t = acc.T
        for s in range(C // csh):
            cols = slice(s * csh, (s + 1) * csh)
            stats_ref[s, :, 0:csh] = t[0 : 2 * RP, cols]
            stats_ref[s, :, csh : 2 * csh] = t[2 * RP : 4 * RP, cols]


def attention_kernel(rows, off, len_ref, prm_ref, pack_ref, probs_ref, u_ref, pooled_ref, qp_ref, qkv_ref, prow, abd):
    total = prm_ref.shape[0] * prm_ref.shape[2]
    width = pack_ref.shape[2] - off
    qkv = pack_ref[:, :, off:].reshape(C, width).T
    qkv_ref[...] = qkv
    wq, wk, wv = qkv[0:64], qkv[64:128], qkv[128:192]
    qp = nt(qkv[192:224], wq)
    qp_ref[...] = qp
    st = fold(nn(parts(qp, 3), wk), 3) * (1.0 / math.sqrt(HEAD_DIM))
    for r in range(rows):
        prow[r * total : (r + 1) * total] = prm_ref[:, r].reshape(total, C)
    scores = fold(nt(parts(st, 3), prow[...]), 3)
    abd[...] = jnp.zeros(abd.shape, F32)
    for r in range(rows):
        cols = slice(r * total, (r + 1) * total)
        live = lane_ids((QUERIES, total)) < len_ref[r]
        s = jnp.where(live, scores[:, cols], MASKED_SCORE)
        e = jnp.where(live, jnp.exp(s - jnp.max(s, axis=1, keepdims=True)), 0.0)
        p = e / jnp.sum(e, axis=1, keepdims=True)
        probs_ref[:, cols] = p
        abd[r : r + 1, cols] = jnp.sum(p, axis=0, keepdims=True)
    u = fold(nn(parts(abd[...], 2), prow[...]), 2)
    u_ref[...] = u
    pooled_ref[...] = fold(nt(parts(u * (1.0 / QUERIES), 2), wv), 2)


def memory_kernel(csh, hs, rows, got_ref, pack_ref, pooled_ref, memory_ref, film_ref, scratch):
    scratch[...] = jnp.zeros(scratch.shape, F32)
    for s in range(got_ref.shape[0]):
        head, part = s // hs, s % hs
        scratch[part * rows : (part + 1) * rows, head * HEAD_DIM : (head + 1) * HEAD_DIM] = got_ref[
            s, 0:rows
        ]
    pooled = scratch[...].astype(BF16)
    pooled_ref[...] = pooled
    memory = nn(pooled, pack_ref[:, :, 0:C].reshape(C, C)).astype(BF16)
    memory_ref[...] = memory
    film_ref[...] = nn(memory, pack_ref[:, :, 2 * C : 2 * C + 2 * csh].reshape(C, 2 * csh))


def stats_kernel(csh, hs, rows, seg_ref, x_ref, film_ref, pack_ref, out_ref, dfilm_ref):
    count = x_ref.shape[0]
    seg = seg_ref[...]
    f0 = film_ref[:, 0:csh]
    f1 = film_ref[:, csh : 2 * csh]
    total = [x_ref[s, 0:RP, 0:csh] for s in range(count)]
    second = [x_ref[s, RP : 2 * RP, 0:csh] for s in range(count)]
    dsum = [x_ref[s, 0:RP, csh : 2 * csh] for s in range(count)]
    cross = [x_ref[s, RP : 2 * RP, csh : 2 * csh] for s in range(count)]
    means = [v * (1.0 / LANES) for v in total]
    d0 = jnp.zeros((RP, csh), F32)
    d1 = jnp.zeros((RP, csh), F32)
    for me in range(count):
        same = [(seg[:, s : s + 1] == seg[:, me : me + 1]).astype(F32) for s in range(count)]
        frames = sum(same) * float(LANES)
        inv = 1.0 / frames
        mean = sum(m * v for m, v in zip(same, total)) * inv
        var = (
            sum(
                m * (v + float(LANES) * (u - mean) * (u - mean))
                for m, v, u in zip(same, second, means)
            )
            * inv
        )
        scale = lax.rsqrt(var + NORM_EPS)
        dtot = sum(m * v for m, v in zip(same, dsum))
        xtot = sum(m * (v + (u - mean) * d) for m, v, u, d in zip(same, cross, means, dsum)) * scale
        mean_part = f0 * dtot * inv
        cross_part = f0 * xtot * inv
        slope = scale * scale * cross_part
        out_ref[me, 0:RP, 0:csh] = 1.0 + f0 * scale
        out_ref[me, RP : 2 * RP, 0:csh] = f1 - f0 * scale * mean
        out_ref[me, 0:RP, csh : 2 * csh] = -slope
        out_ref[me, RP : 2 * RP, csh : 2 * csh] = slope * mean - scale * mean_part
        d0 = d0 + (cross[me] + (means[me] - mean) * dsum[me]) * scale
        d1 = d1 + dsum[me]
    dfilm = jnp.concatenate([d0, d1], axis=1).astype(BF16)
    dfilm_ref[...] = dfilm
    dmem = nt(dfilm, pack_ref[:, :, 2 * C : 2 * C + 2 * csh].reshape(C, 2 * csh))
    dpool = nt(dmem.astype(BF16), pack_ref[:, :, 0:C].reshape(C, C))
    for s in range(count):
        head, part = s // hs, s % hs
        rolled = pltpu.roll(dpool, RP - part * rows, 0) if part else dpool
        out_ref[s, 2 * RP : 3 * RP, 0:csh] = dmem[:, s * csh : (s + 1) * csh]
        out_ref[s, 2 * RP : 3 * RP, csh : 2 * csh] = jnp.zeros((RP, csh), F32)
        out_ref[s, 3 * RP : 4 * RP, 0:HEAD_DIM] = rolled[:, head * HEAD_DIM : (head + 1) * HEAD_DIM]
        if 2 * csh > HEAD_DIM:
            out_ref[s, 3 * RP : 4 * RP, HEAD_DIM : 2 * csh] = jnp.zeros(
                (RP, 2 * csh - HEAD_DIM), F32
            )


def backward_kernel(
    csh,
    flags_ref,
    coef_ref,
    mid_ref,
    dout_ref,
    dskip_ref,
    tanh_ref,
    sig_ref,
    embt_ref,
    w_ref,
    layer_ref,
    dpre_ref,
    dres_ref,
    base_ref,
    first_ref,
    last_ref,
    gstep_ref,
    rows_ref,
    cols_ref,
    facc_ref,
    lacc_ref,
    gacc_ref,
):
    i = pl.program_id(0)
    lane = lane_ids((C, LANES))

    @pl.when(i == 0)
    def _():
        rows_ref[...] = jnp.zeros(rows_ref.shape, F32)
        for s in range(C // csh):
            cols = slice(s * csh, (s + 1) * csh)
            rows_ref[0 : 2 * RP, cols] = coef_ref[s, 0 : 2 * RP, 0:csh]
            rows_ref[2 * RP : 4 * RP, cols] = coef_ref[s, 0 : 2 * RP, csh : 2 * csh]
        cols_ref[...] = rows_ref[...].T
        facc_ref[...] = jnp.zeros((C, LANES), F32)
        lacc_ref[...] = jnp.zeros((C, LANES), F32)
        gacc_ref[...] = jnp.zeros((C, LANES), F32)

    coef = pltpu.roll(cols_ref[...], lax.rem(LANES - 2 * i, LANES), 1)
    dmids = []
    for j in range(2):
        cols = slice(j * LANES, (j + 1) * LANES)
        mf = mid_ref[:, cols].astype(F32)
        df = dout_ref[j].astype(F32)
        a = coef[:, j : j + 1]
        b = coef[:, RP + j : RP + j + 1]
        be = coef[:, 2 * RP + j : 2 * RP + j + 1]
        ga = coef[:, 3 * RP + j : 3 * RP + j + 1]
        layer_ref[j] = (a * mf + b).astype(BF16)
        dmid = (a * df + (be * mf + ga)).astype(BF16).astype(F32) * SQRT_HALF
        dmids.append(dmid)
        dres_ref[0:C, cols] = dmid.astype(BF16)
        dres_ref[C : 2 * C, cols] = dskip_ref[j]
    dg = nn(w_ref[:, 4].reshape(C, 2 * C), dres_ref[...])
    th = tanh_ref[...]
    sg = sig_ref[...]
    dpre_ref[0:C] = (dg * sg * (1.0 - th * th)).astype(BF16)
    dpre_ref[C : 2 * C] = (dg * th * sg * (1.0 - sg)).astype(BF16)
    dpre = dpre_ref[...]
    y0 = nn(w_ref[:, 0].reshape(C, 2 * C), dpre)
    y1 = nn(w_ref[:, 1].reshape(C, 2 * C), dpre)
    y2 = nn(w_ref[:, 2].reshape(C, 2 * C), dpre)
    facc = facc_ref[...]
    lacc = lacc_ref[...]
    gacc = gacc_ref[...]
    for j in range(2):
        r = 2 * i + j
        cols = slice(j * LANES, (j + 1) * LANES)
        z0 = y0[:, cols]
        z2 = y2[:, cols]
        dsh = (
            y1[:, cols]
            + jnp.where(lane < LANES - SHIFT, pltpu.roll(z0, LANES - SHIFT, 1), 0.0)
            + jnp.where(lane >= SHIFT, pltpu.roll(z2, SHIFT, 1), 0.0)
        )
        base_ref[:, cols] = (dsh + dmids[j]).astype(BF16)
        keep_l = jnp.where(flags_ref[0, r] > 0, 1.0, 0.0)
        keep_r = jnp.where(flags_ref[1, r] > 0, 1.0, 0.0)
        full = (
            dsh
            + jnp.where(lane < SHIFT, z0 * keep_l, 0.0)
            + jnp.where(lane >= LANES - SHIFT, z2 * keep_r, 0.0)
        )
        gacc = jnp.where(lane == r, jnp.sum(full, axis=1, keepdims=True), gacc)
        here = (lane // SHIFT) == r
        facc = jnp.where(here, pltpu.roll(z0, SHIFT * r, 1), facc)
        lacc = jnp.where(here, pltpu.roll(z2, SHIFT * r + SHIFT, 1), lacc)
    facc_ref[...] = facc
    lacc_ref[...] = lacc
    gacc_ref[...] = gacc

    @pl.when(i == pl.num_programs(0) - 1)
    def _():
        first_ref[...] = facc.astype(BF16)
        last_ref[...] = lacc.astype(BF16)
        hi = gacc.astype(BF16)
        lo = (gacc - hi.astype(F32)).astype(BF16)
        gstep_ref[...] = (nt(embt_ref[...], hi) + nt(embt_ref[...], lo)).astype(BF16)


def finish_kernel(flags_ref, base_ref, left_ref, right_ref, out_ref):
    i = pl.program_id(0)
    lane = lane_ids((C, LANES))
    left = left_ref[...].astype(F32)
    right = right_ref[...].astype(F32)
    for j in range(2):
        r = 2 * i + j
        cols = slice(j * LANES, (j + 1) * LANES)
        lh = pltpu.roll(left, lax.rem(LANES - SHIFT * r, LANES), 1)
        rh = pltpu.roll(right, LANES - SHIFT - SHIFT * r, 1)
        lh = jnp.where((lane < SHIFT) & (flags_ref[0, r] > 0), lh, 0.0)
        rh = jnp.where((lane >= LANES - SHIFT) & (flags_ref[1, r] > 0), rh, 0.0)
        out_ref[j] = (base_ref[:, cols].astype(F32) + lh + rh).astype(BF16)


def weight_kernel(dp, inp_ref, gated_ref, dpre_ref, dres_ref, gstep_ref, out_ref):
    k = pl.program_id(0)
    cs = C // dp

    @pl.when(k < 4)
    def _():
        g = nt(inp_ref[...], dpre_ref[...]).astype(BF16)
        out_ref[:, pl.ds(pl.multiple_of(k * cs, cs), cs), :] = g.reshape(dp, cs, 2 * C)

    @pl.when(k == 4)
    def _():
        g = nt(gated_ref[...], dres_ref[...]).astype(BF16)
        out_ref[:, 4 * cs : 5 * cs, :] = g.reshape(dp, cs, 2 * C)
        h = cs // 2
        for d in range(dp):
            out_ref[d, 5 * cs : 5 * cs + h, 0:C] = gstep_ref[d * cs : d * cs + h]
            out_ref[d, 5 * cs : 5 * cs + h, C : 2 * C] = gstep_ref[d * cs + h : (d + 1) * cs]


def attention_back_kernel(
    rows, csh, dp, prm_ref, probs_ref, u_ref, qp_ref, qkv_ref, pooled_ref, memory_ref, dfilm_ref, got_ref, out_ref, prow, ds, stack, right
):
    count = prm_ref.shape[0]
    total = count * prm_ref.shape[2]
    cs = C // dp
    wk, wv = qkv_ref[64:128], qkv_ref[128:192]
    datt = got_ref[0, 3 * RP : 4 * RP, 0:HEAD_DIM]
    dmem = got_ref[0, 2 * RP : 3 * RP, 0:csh]
    for s in range(1, count):
        datt = datt + got_ref[s, 3 * RP : 4 * RP, 0:HEAD_DIM]
        dmem = dmem + got_ref[s, 2 * RP : 3 * RP, 0:csh]
    datt = datt * (1.0 / QUERIES)
    for r in range(rows):
        prow[r * total : (r + 1) * total] = prm_ref[:, r].reshape(total, C)
    vh = fold(nn(parts(datt, 2), wv), 2)
    dp_all = fold(nt(parts(vh, 2), prow[...]), 2)
    for r in range(rows):
        cols = slice(r * total, (r + 1) * total)
        p = probs_ref[:, cols]
        dpr = dp_all[r : r + 1, cols]
        inner = jnp.sum(p * dpr, axis=1, keepdims=True)
        ds[:, cols] = p * (dpr - inner)
    tt = fold(nn(parts(ds[...], 2), prow[...]), 2)
    scale = 1.0 / math.sqrt(HEAD_DIM)
    dq = fold(nt(parts(tt, 2), wk), 2) * scale
    stack[...] = jnp.zeros(stack.shape, F32)
    stack[0:QUERIES] = tt
    stack[32:48] = u_ref[...]
    stack[48:64] = pooled_ref[...].astype(F32)
    stack[64:80] = memory_ref[...].astype(F32)
    right[...] = jnp.zeros(right.shape, F32)
    right[0:32, 0:64] = qp_ref[...] * scale
    right[32:48, 64:128] = datt
    right[48:64, 128 : 128 + csh] = dmem
    right[64:80, 192 : 192 + 2 * csh] = dfilm_ref[...].astype(F32)
    grads = lax.dot_general(
        stack[...].T,
        right[...],
        (((1,), (0,)), ((), ())),
        precision=lax.Precision.HIGHEST,
        preferred_element_type=F32,
    ).astype(BF16)
    hi = dq.astype(BF16)
    lo = (dq - hi.astype(F32)).astype(BF16)
    for d in range(dp):
        out_ref[d, 0:cs] = grads[d * cs : (d + 1) * cs]
        out_ref[d, cs : cs + QUERIES] = jnp.zeros((QUERIES, right.shape[1]), BF16)
        out_ref[d, cs : cs + QUERIES, 0:64] = hi
        out_ref[d, cs : cs + QUERIES, 64:128] = lo


def halve_sum(blocks, axis, axis_size):
    index = lax.axis_index(axis)
    bit = 1
    while bit < axis_size:
        half = blocks.reshape((blocks.shape[0] // 2, 2) + blocks.shape[1:])
        mine = (index // bit) % 2
        keep = lax.dynamic_index_in_dim(half, mine, 1, keepdims=False)
        give = lax.dynamic_index_in_dim(half, 1 - mine, 1, keepdims=False)
        got = lax.ppermute(give, axis, [(d, d ^ bit) for d in range(axis_size)])
        blocks = (keep.astype(F32) + got.astype(F32)).astype(BF16)
        bit *= 2
    return blocks[0]


def exchange(pieces, axis):
    return lax.all_to_all(pieces, axis, split_axis=0, concat_axis=0)


def to_all(piece, axis, axis_size):
    return exchange(jnp.broadcast_to(piece[None], (axis_size,) + piece.shape), axis)


def body(
    dp,
    seq,
    x_in,
    cond,
    segment_ids,
    diffusion_steps,
    prompt,
    prompt_lengths,
    w_step,
    w_conv,
    w_cond,
    w_res,
    w_skip,
    queries,
    w_query,
    w_key,
    w_value,
    w_attn_out,
    w_film,
    d_out,
    d_skip,
):
    rows = x_in.shape[0]
    frames = x_in.shape[2]
    steps = rows // 2
    cols = rows * frames
    cs = C // dp
    csh = C // seq
    hs = max(1, seq // HEADS)
    arows = rows // hs
    pl_local = prompt.shape[1]
    prompt_all = pl_local * seq
    sidx = lax.axis_index("seq")
    head = sidx // hs
    part = sidx % hs
    up = [(i, i + 1) for i in range(seq - 1)]
    down = [(i + 1, i) for i in range(seq - 1)]

    def head_cols(w):
        return lax.dynamic_slice_in_dim(w, head * HEAD_DIM, HEAD_DIM, 1)

    off = 2 * C + 2 * csh
    pack_a = jnp.concatenate(
        [
            w_attn_out,
            w_step,
            w_film.reshape(cs, 2 * csh),
            head_cols(w_query),
            head_cols(w_key),
            head_cols(w_value),
            queries.T,
            jnp.zeros((cs, 32), BF16),
        ],
        axis=1,
    )
    pack_b = jnp.concatenate(
        [w_conv, w_cond[None], jnp.concatenate([w_res, w_skip], axis=1)[None]], axis=0
    )
    full_a = lax.all_gather(pack_a, "dp")
    full_b = lax.all_gather(pack_b, "dp")
    width_a = pack_a.shape[1]

    first, last = call(
        edge_kernel,
        (sds((C, LANES), BF16), sds((C, LANES), BF16)),
        "edges",
        bytes_accessed=x_in.size * 2,
        in_specs=[VM],
        out_specs=(VM, VM),
    )(x_in)
    left_halo = lax.ppermute(last, "seq", up)
    right_halo = lax.ppermute(first, "seq", down)

    pieces = prompt.reshape(hs, arows, pl_local, C)
    pieces = jnp.broadcast_to(pieces[None], (seq // hs, hs, arows, pl_local, C))
    prompts = exchange(pieces.reshape(seq, arows, pl_local, C), "seq")

    block_ids = segment_ids[:, ::frames]
    padded_ids = jnp.pad(block_ids, ((0, 0), (1, 1)), constant_values=-1)
    mine = lax.dynamic_slice_in_dim(padded_ids, sidx, 3, 1)
    flags = jnp.stack([mine[:, 0] == mine[:, 1], mine[:, 2] == mine[:, 1]]).astype(jnp.int32)
    block_ids = jnp.pad(block_ids, ((0, RP - rows), (0, 0)))
    half = C // 2
    frequency = jnp.exp(jnp.arange(half, dtype=F32) * (-math.log(10000.0) / half))
    angles = diffusion_steps.astype(F32)[:, None] * frequency[None, :]
    embedding = jnp.concatenate([jnp.sin(angles), jnp.cos(angles)], axis=1).astype(BF16)
    emb_rows = jnp.pad(embedding, ((0, RP - rows), (0, 0)))
    emb_cols = jnp.pad(embedding.T, ((0, 0), (0, LANES - rows)))
    lengths = lax.dynamic_slice_in_dim(prompt_lengths, part * arows, arows, 0)

    probs, u, pooled_head, qp, qkv = call(
        functools.partial(attention_kernel, arows, off),
        (
            sds((QUERIES, arows * prompt_all), F32),
            sds((RP, C), F32),
            sds((RP, HEAD_DIM), F32),
            sds((QUERIES, HEAD_DIM), F32),
            sds((width_a - off, C), BF16),
        ),
        "attention",
        flops=2 * 160 * 1536 * 512,
        bytes_accessed=4e6,
        in_specs=[SM, VM, VM],
        out_specs=(VM,) * 5,
        scratch_shapes=[
            pltpu.VMEM((arows * prompt_all, C), BF16),
            pltpu.VMEM((RP, arows * prompt_all), F32),
        ],
    )(lengths, prompts, full_a)
    pooled_got = to_all(pooled_head, "seq", seq)
    pooled, memory, film = call(
        functools.partial(memory_kernel, csh, hs, arows),
        (sds((RP, C), BF16), sds((RP, C), BF16), sds((RP, 2 * csh), F32)),
        "memory",
        bytes_accessed=2e6,
        in_specs=[VM, VM],
        out_specs=(VM, VM, VM),
        scratch_shapes=[pltpu.VMEM((RP, C), F32)],
    )(pooled_got, full_a)

    row_block = pl.BlockSpec((2, C, LANES), lambda i: (i, 0, 0))

    def col_block(height):
        return pl.BlockSpec((height, 2 * LANES), lambda i: (0, i))

    step_spec = pl.BlockSpec(
        (dp, cs, C), lambda i: (0, 0, 1), pipeline_mode=pl.Buffered(1)
    )
    inp, tanh_part, sig_part, gated, skip_out, mid, stats = call(
        functools.partial(forward_kernel, csh),
        (
            sds((4 * C, cols), BF16),
            sds((C, cols), F32),
            sds((C, cols), F32),
            sds((C, cols), BF16),
            sds(x_in.shape, BF16),
            sds((C, cols), BF16),
            sds((seq, 2 * RP, 2 * csh), F32),
        ),
        "wavenet",
        flops=2 * cols * (4 * C * 2 * C + 2 * C * C),
        bytes_accessed=30e6,
        grid=(steps,),
        in_specs=[
            SM,
            row_block,
            row_block,
            row_block,
            whole((C, LANES)),
            whole((C, LANES)),
            whole((RP, C)),
            step_spec,
            whole((dp, 5, cs, 2 * C)),
        ],
        out_specs=(
            col_block(4 * C),
            col_block(C),
            col_block(C),
            col_block(C),
            row_block,
            col_block(C),
            pl.BlockSpec((seq, 2 * RP, 2 * csh), lambda i: (0, 0, 0)),
        ),
        scratch_shapes=[
            pltpu.VMEM((2 * C, 4 * C), BF16),
            pltpu.VMEM((2 * C, C), BF16),
            pltpu.VMEM((C, LANES), F32),
            pltpu.VMEM((C, LANES), F32),
        ],
    )(flags, x_in, cond, d_out, left_halo, right_halo, emb_rows, full_a, full_b)

    stats_got = exchange(stats, "seq")
    coef_out, dfilm = call(
        functools.partial(stats_kernel, csh, hs, arows),
        (sds((seq, 4 * RP, 2 * csh), F32), sds((RP, 2 * csh), BF16)),
        "segments",
        bytes_accessed=2e6,
        in_specs=[VM, VM, VM, VM],
        out_specs=(VM, VM),
    )(block_ids, stats_got, film, full_a)
    coef = exchange(coef_out, "seq")

    layer_out, dpre, dres, base, first, last, gstep = call(
        functools.partial(backward_kernel, csh),
        (
            sds(x_in.shape, BF16),
            sds((2 * C, cols), BF16),
            sds((2 * C, cols), BF16),
            sds((C, cols), BF16),
            sds((C, LANES), BF16),
            sds((C, LANES), BF16),
            sds((C, C), BF16),
        ),
        "wavenet_back",
        flops=2 * cols * (2 * C * C + 6 * C * C),
        bytes_accessed=30e6,
        grid=(steps,),
        in_specs=[
            SM,
            whole((seq, 4 * RP, 2 * csh)),
            col_block(C),
            row_block,
            row_block,
            col_block(C),
            col_block(C),
            whole((C, LANES)),
            whole((dp, 5, cs, 2 * C)),
        ],
        out_specs=(
            row_block,
            col_block(2 * C),
            col_block(2 * C),
            col_block(C),
            pl.BlockSpec((C, LANES), lambda i: (0, 0)),
            pl.BlockSpec((C, LANES), lambda i: (0, 0)),
            pl.BlockSpec((C, C), lambda i: (0, 0)),
        ),
        scratch_shapes=[
            pltpu.VMEM((LANES, C), F32),
            pltpu.VMEM((C, LANES), F32),
            pltpu.VMEM((C, LANES), F32),
            pltpu.VMEM((C, LANES), F32),
            pltpu.VMEM((C, LANES), F32),
        ],
    )(flags, coef, mid, d_out, d_skip, tanh_part, sig_part, emb_cols, full_b)
    from_left = lax.ppermute(last, "seq", up)
    from_right = lax.ppermute(first, "seq", down)

    grow = 5 * cs + cs // 2
    big = call(
        functools.partial(weight_kernel, dp),
        sds((dp, grow, 2 * C), BF16),
        "weight_grads",
        flops=2 * cols * 5 * C * 2 * C,
        bytes_accessed=20e6,
        grid=(5,),
        in_specs=[
            pl.BlockSpec((C, cols), lambda k: (jnp.minimum(k, 3), 0)),
            whole((C, cols)),
            whole((2 * C, cols)),
            whole((2 * C, cols)),
            whole((C, C)),
        ],
        out_specs=pl.BlockSpec((dp, grow, 2 * C), lambda k: (0, 0, 0)),
    )(inp, gated, dpre, dres, gstep)

    grad_input = call(
        finish_kernel,
        sds(x_in.shape, BF16),
        "grad_input",
        bytes_accessed=4e6,
        grid=(steps,),
        in_specs=[SM, col_block(C), whole((C, LANES)), whole((C, LANES))],
        out_specs=row_block,
    )(flags, base, from_left, from_right)

    small = call(
        functools.partial(attention_back_kernel, arows, csh, dp),
        sds((dp, cs + QUERIES, 384), BF16),
        "attention_back",
        flops=2 * 200 * 1536 * 512,
        bytes_accessed=4e6,
        in_specs=[VM] * 9,
        out_specs=VM,
        scratch_shapes=[
            pltpu.VMEM((arows * prompt_all, C), BF16),
            pltpu.VMEM((QUERIES, arows * prompt_all), F32),
            pltpu.VMEM((LANES, C), F32),
            pltpu.VMEM((LANES, 384), F32),
        ],
    )(prompts, probs, u, qp, qkv, pooled, memory, dfilm, coef)
    small = jnp.sum(exchange(small, "dp").astype(F32), axis=0)
    grad_film = small[:cs, 192 : 192 + 2 * csh].reshape(cs, 2, csh)
    dq_head = small[cs:, 0:64] + small[cs:, 64:128]
    dq_hi = dq_head.astype(BF16)
    dq_lo = (dq_head - dq_hi.astype(F32)).astype(BF16)
    own = jnp.concatenate(
        [
            small[:cs, 0:192].astype(BF16),
            jnp.concatenate([dq_hi, dq_lo, jnp.zeros((QUERIES, 64), BF16)], axis=1),
        ],
        axis=0,
    )
    small_all = to_all(own, "seq", seq).astype(F32)
    by_head = small_all.reshape(HEADS, hs, cs + QUERIES, 192)

    def heads_side(v):
        v = jnp.sum(v, axis=1)
        return jnp.transpose(v, (1, 0, 2)).reshape(v.shape[1], C)

    grad_key = heads_side(by_head[:, :, :cs, 0:64])
    grad_value = heads_side(by_head[:, :, :cs, 64:128])
    grad_attn = jnp.transpose(small_all[:, :cs, 128 : 128 + csh], (1, 0, 2)).reshape(cs, C)
    d_query = heads_side(by_head[:, :, cs:, 0:64] + by_head[:, :, cs:, 64:128])
    grad_query = jnp.einsum(
        "qc,qd->cd", queries.astype(F32), d_query, precision=lax.Precision.HIGHEST
    )
    grad_queries = jnp.einsum(
        "qd,cd->qc", d_query, w_query.astype(F32), precision=lax.Precision.HIGHEST
    )

    big = halve_sum(big, "dp", dp)
    big = exchange(big.reshape(seq, grow // seq, 2 * C), "seq")
    big = jnp.sum(big.astype(F32), axis=0).astype(BF16)
    big = to_all(big, "seq", seq).reshape(grow, 2 * C).astype(F32)
    grad_conv = big[: 3 * cs].reshape(3, cs, 2 * C)
    grad_cond = big[3 * cs : 4 * cs]
    grad_res = big[4 * cs : 5 * cs, :C]
    grad_skip = big[4 * cs : 5 * cs, C:]
    grad_step = jnp.concatenate([big[5 * cs :, :C], big[5 * cs :, C:]], axis=0)
    return (
        layer_out,
        skip_out,
        grad_input,
        grad_step,
        grad_conv,
        grad_cond,
        grad_res,
        grad_skip,
        grad_queries,
        grad_query,
        grad_key,
        grad_value,
        grad_attn,
        grad_film,
    )


def solution(mesh):
    frames = P("dp", None, "seq")
    matrix = P("dp", None)
    return jax.shard_map(
        functools.partial(body, mesh.shape["dp"], mesh.shape["seq"]),
        mesh=mesh,
        in_specs=(
            frames,
            frames,
            P("dp", None),
            P("dp"),
            P("dp", "seq", None),
            P("dp"),
            matrix,
            P(None, "dp", None),
            matrix,
            matrix,
            matrix,
            P(None, "dp"),
            matrix,
            matrix,
            matrix,
            matrix,
            frames,
            frames,
            frames,
        ),
        out_specs=(
            frames,
            frames,
            frames,
            matrix,
            P(None, "dp", None),
            matrix,
            matrix,
            matrix,
            P(None, "dp"),
            matrix,
            matrix,
            matrix,
            matrix,
            frames,
        ),
        check_vma=False,
    )
```

```python
import functools
import math

import jax
import jax.numpy as jnp
from jax import lax
from jax.experimental import pallas as pl
from jax.experimental.pallas import tpu as pltpu
from jax.sharding import PartitionSpec as P

C = 512
HEADS = 8
QUERIES = 32
HEAD_DIM = 64
SHIFT = 4
SQRT_HALF = 0.7071067811865476
NORM_EPS = 1e-05
MASKED_SCORE = -1e30
LANES = 128
RP = 16
F32 = jnp.float32
BF16 = jnp.bfloat16
VMEM_BYTES = 50 * 1024 * 1024


def nn(a, b):
    return lax.dot_general(a, b, (((1,), (0,)), ((), ())), preferred_element_type=F32)


def nt(a, b):
    return lax.dot_general(a, b, (((1,), (1,)), ((), ())), preferred_element_type=F32)


def parts(v, count):
    out = []
    for _ in range(count):
        low = v.astype(BF16)
        out.append(low)
        v = v - low.astype(F32)
    return jnp.concatenate(out, axis=0)


def fold(v, count):
    rows = v.shape[0] // count
    total = v[:rows]
    for k in range(1, count):
        total = total + v[k * rows : (k + 1) * rows]
    return total


def lane_ids(shape):
    return lax.broadcasted_iota(jnp.int32, shape, len(shape) - 1)


def call(kernel, out_shape, name, flops=0, bytes_accessed=0, **kw):
    return pl.pallas_call(
        kernel,
        out_shape=out_shape,
        name=name,
        cost_estimate=pl.CostEstimate(
            flops=int(flops), bytes_accessed=int(bytes_accessed), transcendentals=0
        ),
        compiler_params=pltpu.CompilerParams(vmem_limit_bytes=VMEM_BYTES),
        **kw,
    )


def sds(shape, dtype):
    return jax.ShapeDtypeStruct(shape, dtype)


VM = pl.BlockSpec(memory_space=pltpu.VMEM)
HB = pl.BlockSpec(memory_space=pl.ANY)
SM = pl.BlockSpec(memory_space=pltpu.SMEM)


def whole(shape):
    return pl.BlockSpec(shape, lambda i: (0,) * len(shape), pipeline_mode=pl.Buffered(1))


def prep_kernel(
    cs,
    csh,
    head_ref,
    x_ref,
    conv_ref,
    cond_ref,
    res_ref,
    skip_ref,
    attn_ref,
    step_ref,
    film_ref,
    wq_ref,
    wk_ref,
    wv_ref,
    queries_ref,
    pack_ref,
    first_ref,
    last_ref,
    scr,
):
    half = cs // 2
    for k in range(3):
        pack_ref[k * cs : (k + 1) * cs] = conv_ref[k]
    pack_ref[3 * cs : 4 * cs] = cond_ref[...]
    pack_ref[4 * cs : 5 * cs, 0:C] = res_ref[...]
    pack_ref[4 * cs : 5 * cs, C : 2 * C] = skip_ref[...]
    pack_ref[5 * cs : 6 * cs, 0:C] = attn_ref[...]
    pack_ref[5 * cs : 6 * cs, C : 2 * C] = jnp.zeros((cs, C), BF16)
    pack_ref[5 * cs : 6 * cs, C : C + csh] = film_ref[:, 0, :]
    pack_ref[5 * cs : 6 * cs, C + csh : C + 2 * csh] = film_ref[:, 1, :]
    off = C + 2 * csh
    turn = lax.rem(C - HEAD_DIM * head_ref[0], C)
    for k, ref in enumerate((wq_ref, wk_ref, wv_ref)):
        v = pltpu.roll(ref[...].astype(F32), turn, 1)[:, 0:HEAD_DIM]
        pack_ref[5 * cs : 6 * cs, off + k * HEAD_DIM : off + (k + 1) * HEAD_DIM] = v.astype(BF16)
    scr[...] = jnp.zeros((LANES, LANES), F32)
    scr[0:QUERIES, 0:cs] = queries_ref[...].astype(F32)
    pack_ref[5 * cs : 6 * cs, off + 192 : off + 192 + QUERIES] = scr[...].T[0:cs, 0:QUERIES].astype(
        BF16
    )
    pack_ref[6 * cs : 6 * cs + half, 0:C] = step_ref[0:half]
    pack_ref[6 * cs : 6 * cs + half, C : 2 * C] = step_ref[half:cs]
    rows = x_ref.shape[0]
    lane = lane_ids((C, LANES))
    first = jnp.zeros((C, LANES), F32)
    last = jnp.zeros((C, LANES), F32)
    for r in range(rows):
        v = x_ref[r].astype(F32)
        here = (lane // SHIFT) == r
        first = jnp.where(here, pltpu.roll(v, SHIFT * r, 1) if r else v, first)
        last = jnp.where(here, pltpu.roll(v, SHIFT * r + SHIFT, 1), last)
    first_ref[...] = first.astype(BF16)
    last_ref[...] = last.astype(BF16)


def block_copies(off_ref, pieces, cs, blocks, dst, sems, base=0):
    out = []
    for j, block in enumerate(blocks):
        group = []
        for k, piece in enumerate(pieces):
            row = pl.multiple_of(off_ref[k], 16)
            group.append(
                pltpu.make_async_copy(
                    piece.at[pl.ds(block * cs, cs)],
                    dst.at[j, pl.ds(row, cs)],
                    sems.at[base + j * len(pieces) + k],
                )
            )
        out.append(group)
    return out


def begin(groups):
    for group in groups:
        for copy in group:
            copy.start()


def finish(group):
    for copy in group:
        copy.wait()


def forward_kernel(
    dp,
    csh,
    off_ref,
    flags_ref,
    x_ref,
    cond_ref,
    dout_ref,
    left_ref,
    right_ref,
    emb_ref,
    *refs,
):
    pieces, refs = refs[:dp], refs[dp:]
    (
        inp_ref,
        tanh_ref,
        sig_ref,
        skip_ref,
        mid_ref,
        stats_ref,
        wn_ref,
        step_ref,
        wt_ref,
        rst_ref,
        lift_ref,
        acc_ref,
        sems,
    ) = refs
    cs = C // dp
    half = cs // 2
    i = pl.program_id(0)
    lane = lane_ids((C, LANES))

    @pl.when(i == 0)
    def _():
        groups = block_copies(off_ref, pieces, cs, range(5), wn_ref, sems)
        steps = []
        for k, piece in enumerate(pieces):
            for h in range(2):
                row = pl.multiple_of(off_ref[k] + h * half, 16)
                steps.append(
                    pltpu.make_async_copy(
                        piece.at[pl.ds(6 * cs, half), pl.ds(h * C, C)],
                        step_ref.at[pl.ds(row, half)],
                        sems.at[5 * dp + 2 * k + h],
                    )
                )
        begin(groups)
        begin([steps])
        acc_ref[...] = jnp.zeros((C, LANES), F32)
        for k in range(4):
            finish(groups[k])
            wt_ref[:, k * C : (k + 1) * C] = wn_ref[k].T
        finish(groups[4])
        rst_ref[...] = wn_ref[4].T
        finish(steps)
        lift = nn(emb_ref[...], step_ref[...])
        lift = jnp.concatenate([lift, jnp.zeros((LANES - RP, C), F32)], axis=0)
        lift_ref[...] = lift.T

    lift = pltpu.roll(lift_ref[...], lax.rem(LANES - 2 * i, LANES), 1)
    left = left_ref[...].astype(F32)
    right = right_ref[...].astype(F32)
    for j in range(2):
        r = 2 * i + j
        lc = lift[:, j : j + 1]
        sh = (x_ref[j].astype(F32) + lc).astype(BF16)
        shf = sh.astype(F32)
        lh = pltpu.roll(left, lax.rem(LANES - SHIFT * r, LANES), 1)
        lh = jnp.where(flags_ref[0, r] > 0, (lh + lc).astype(BF16).astype(F32), 0.0)
        rh = pltpu.roll(right, LANES - SHIFT - SHIFT * r, 1)
        rh = jnp.where(flags_ref[1, r] > 0, (rh + lc).astype(BF16).astype(F32), 0.0)
        cols = slice(j * LANES, (j + 1) * LANES)
        inp_ref[0:C, cols] = jnp.where(lane < SHIFT, lh, pltpu.roll(shf, SHIFT, 1)).astype(BF16)
        inp_ref[C : 2 * C, cols] = sh
        inp_ref[2 * C : 3 * C, cols] = jnp.where(
            lane >= LANES - SHIFT, rh, pltpu.roll(shf, LANES - SHIFT, 1)
        ).astype(BF16)
        inp_ref[3 * C : 4 * C, cols] = cond_ref[j]
    pre = nn(wt_ref[...], inp_ref[0 : 4 * C])
    th = jnp.tanh(pre[:C])
    sg = jax.nn.sigmoid(pre[C:])
    tanh_ref[...] = th
    sig_ref[...] = sg
    g = (th * sg).astype(BF16)
    inp_ref[4 * C : 5 * C] = g
    rs = nn(rst_ref[...], g)
    acc = acc_ref[...]
    for j in range(2):
        r = 2 * i + j
        cols = slice(j * LANES, (j + 1) * LANES)
        skip_ref[j] = rs[C:, cols].astype(BF16)
        mid = ((x_ref[j].astype(F32) + rs[:C, cols]) * SQRT_HALF).astype(BF16)
        mid_ref[:, cols] = mid
        mf = mid.astype(F32)
        df = dout_ref[j].astype(F32)
        total = jnp.sum(mf, axis=1, keepdims=True)
        dev = mf - total * (1.0 / LANES)
        acc = jnp.where(lane == r, total, acc)
        acc = jnp.where(lane == RP + r, jnp.sum(dev * dev, axis=1, keepdims=True), acc)
        acc = jnp.where(lane == 2 * RP + r, jnp.sum(df, axis=1, keepdims=True), acc)
        acc = jnp.where(lane == 3 * RP + r, jnp.sum(df * dev, axis=1, keepdims=True), acc)
    acc_ref[...] = acc

    @pl.when(i == pl.num_programs(0) - 1)
    def _():
        t = acc.T
        for s in range(C // csh):
            cols = slice(s * csh, (s + 1) * csh)
            stats_ref[s, :, 0:csh] = t[0 : 2 * RP, cols]
            stats_ref[s, :, csh : 2 * csh] = t[2 * RP : 4 * RP, cols]


def attention_kernel(rows, dp, off, off_ref, len_ref, prm_ref, *refs):
    pieces, refs = refs[:dp], refs[dp:]
    apack_ref, probs_ref, u_ref, pooled_ref, qp_ref, qkv_ref, prow, abd, sems = refs
    cs = C // dp
    copies = []
    for k, piece in enumerate(pieces):
        row = pl.multiple_of(off_ref[k], 16)
        copies.append(
            pltpu.make_async_copy(
                piece.at[pl.ds(5 * cs, cs)], apack_ref.at[pl.ds(row, cs)], sems.at[k]
            )
        )
    begin([copies])
    total = prm_ref.shape[0] * prm_ref.shape[2]
    for r in range(rows):
        prow[r * total : (r + 1) * total] = prm_ref[:, r].reshape(total, C)
    abd[...] = jnp.zeros(abd.shape, F32)
    finish(copies)
    qkv = apack_ref[:, off : off + 256].T
    qkv_ref[...] = qkv
    wq, wk, wv = qkv[0:64], qkv[64:128], qkv[128:192]
    qp = nt(qkv[192:224], wq)
    qp_ref[...] = qp
    st = fold(nn(parts(qp, 3), wk), 3) * (1.0 / math.sqrt(HEAD_DIM))
    scores = fold(nt(parts(st, 3), prow[...]), 3)
    for r in range(rows):
        cols = slice(r * total, (r + 1) * total)
        live = lane_ids((QUERIES, total)) < len_ref[r]
        s = jnp.where(live, scores[:, cols], MASKED_SCORE)
        e = jnp.where(live, jnp.exp(s - jnp.max(s, axis=1, keepdims=True)), 0.0)
        p = e / jnp.sum(e, axis=1, keepdims=True)
        probs_ref[:, cols] = p
        abd[r : r + 1, cols] = jnp.sum(p, axis=0, keepdims=True)
    u = fold(nn(parts(abd[...], 2), prow[...]), 2)
    u_ref[...] = u
    pooled_ref[...] = fold(nt(parts(u * (1.0 / QUERIES), 2), wv), 2)


def memory_kernel(csh, hs, rows, got_ref, apack_ref, pooled_ref, memory_ref, film_ref, scratch):
    scratch[...] = jnp.zeros(scratch.shape, F32)
    for s in range(got_ref.shape[0]):
        head, part = s // hs, s % hs
        scratch[part * rows : (part + 1) * rows, head * HEAD_DIM : (head + 1) * HEAD_DIM] = got_ref[
            s, 0:rows, 0:HEAD_DIM
        ]
    pooled = scratch[...].astype(BF16)
    pooled_ref[...] = pooled
    memory = nn(pooled, apack_ref[:, 0:C]).astype(BF16)
    memory_ref[...] = memory
    film_ref[...] = nn(memory, apack_ref[:, C : C + 2 * csh])


def stats_kernel(csh, hs, rows, seg_ref, x_ref, film_ref, apack_ref, out_ref, dfilm_ref):
    count = x_ref.shape[0]
    seg = seg_ref[...]
    f0 = film_ref[:, 0:csh]
    f1 = film_ref[:, csh : 2 * csh]
    total = [x_ref[s, 0:RP, 0:csh] for s in range(count)]
    second = [x_ref[s, RP : 2 * RP, 0:csh] for s in range(count)]
    dsum = [x_ref[s, 0:RP, csh : 2 * csh] for s in range(count)]
    cross = [x_ref[s, RP : 2 * RP, csh : 2 * csh] for s in range(count)]
    means = [v * (1.0 / LANES) for v in total]
    d0 = jnp.zeros((RP, csh), F32)
    d1 = jnp.zeros((RP, csh), F32)
    for me in range(count):
        same = [(seg[:, s : s + 1] == seg[:, me : me + 1]).astype(F32) for s in range(count)]
        frames = sum(same) * float(LANES)
        inv = 1.0 / frames
        mean = sum(m * v for m, v in zip(same, total)) * inv
        var = (
            sum(
                m * (v + float(LANES) * (u - mean) * (u - mean))
                for m, v, u in zip(same, second, means)
            )
            * inv
        )
        scale = lax.rsqrt(var + NORM_EPS)
        dtot = sum(m * v for m, v in zip(same, dsum))
        xtot = sum(m * (v + (u - mean) * d) for m, v, u, d in zip(same, cross, means, dsum)) * scale
        mean_part = f0 * dtot * inv
        cross_part = f0 * xtot * inv
        slope = scale * scale * cross_part
        out_ref[me, 0:RP, 0:csh] = 1.0 + f0 * scale
        out_ref[me, RP : 2 * RP, 0:csh] = f1 - f0 * scale * mean
        out_ref[me, 0:RP, csh : 2 * csh] = -slope
        out_ref[me, RP : 2 * RP, csh : 2 * csh] = slope * mean - scale * mean_part
        d0 = d0 + (cross[me] + (means[me] - mean) * dsum[me]) * scale
        d1 = d1 + dsum[me]
    dfilm = jnp.concatenate([d0, d1], axis=1).astype(BF16)
    dfilm_ref[...] = dfilm
    dmem = nt(dfilm, apack_ref[:, C : C + 2 * csh])
    dpool = nt(dmem.astype(BF16), apack_ref[:, 0:C])
    for s in range(count):
        head, part = s // hs, s % hs
        rolled = pltpu.roll(dpool, RP - part * rows, 0) if part else dpool
        out_ref[s, 2 * RP : 3 * RP, 0:csh] = dmem[:, s * csh : (s + 1) * csh]
        out_ref[s, 2 * RP : 3 * RP, csh : 2 * csh] = jnp.zeros((RP, csh), F32)
        out_ref[s, 3 * RP : 4 * RP, 0:HEAD_DIM] = rolled[:, head * HEAD_DIM : (head + 1) * HEAD_DIM]
        if 2 * csh > HEAD_DIM:
            out_ref[s, 3 * RP : 4 * RP, HEAD_DIM : 2 * csh] = jnp.zeros(
                (RP, 2 * csh - HEAD_DIM), F32
            )


def gate_kernel(dp, csh, off_ref, flags_ref, coef_ref, mid_ref, dout_ref, dskip_ref, tanh_ref, sig_ref, *refs):
    pieces, refs = refs[:dp], refs[dp:]
    layer_ref, rhs_ref, sums_ref, rows_ref, cols_ref, w_ref, sems = refs
    i = pl.program_id(0)

    @pl.when(i == 0)
    def _():
        groups = block_copies(off_ref, pieces, C // dp, (4,), w_ref, sems)
        begin(groups)
        rows_ref[...] = jnp.zeros(rows_ref.shape, F32)
        for s in range(C // csh):
            cols = slice(s * csh, (s + 1) * csh)
            rows_ref[0 : 2 * RP, cols] = coef_ref[s, 0 : 2 * RP, 0:csh]
            rows_ref[2 * RP : 4 * RP, cols] = coef_ref[s, 0 : 2 * RP, csh : 2 * csh]
        cols_ref[...] = rows_ref[...].T
        sums_ref[...] = jnp.zeros(sums_ref.shape, F32)
        finish(groups[0])

    coef = pltpu.roll(cols_ref[...], lax.rem(LANES - 2 * i, LANES), 1)
    for j in range(2):
        cols = slice(j * LANES, (j + 1) * LANES)
        mf = mid_ref[:, cols].astype(F32)
        df = dout_ref[j].astype(F32)
        a = coef[:, j : j + 1]
        b = coef[:, RP + j : RP + j + 1]
        be = coef[:, 2 * RP + j : 2 * RP + j + 1]
        ga = coef[:, 3 * RP + j : 3 * RP + j + 1]
        layer_ref[j] = (a * mf + b).astype(BF16)
        dmid = (a * df + (be * mf + ga)).astype(BF16).astype(F32)
        rhs_ref[2 * C : 3 * C, cols] = (dmid * SQRT_HALF).astype(BF16)
        rhs_ref[3 * C : 4 * C, cols] = dskip_ref[j]
    dg = nn(w_ref[0], rhs_ref[2 * C : 4 * C])
    th = tanh_ref[...]
    sg = sig_ref[...]
    rhs_ref[0:C] = (dg * sg * (1.0 - th * th)).astype(BF16)
    rhs_ref[C : 2 * C] = (dg * th * sg * (1.0 - sg)).astype(BF16)
    frame = lax.broadcasted_iota(jnp.int32, (2 * LANES, LANES), 0)
    column = lane_ids((2 * LANES, LANES))
    place = frame % LANES
    second = frame >= LANES
    keep_l = jnp.where(second, flags_ref[0, 2 * i + 1], flags_ref[0, 2 * i])
    keep_r = jnp.where(second, flags_ref[1, 2 * i + 1], flags_ref[1, 2 * i])
    row = 2 * i + jnp.where(second, 1, 0)
    use0 = (column == row) & ((place >= SHIFT) | (keep_l > 0))
    use1 = column == RP + row
    use2 = (column == 2 * RP + row) & ((place < LANES - SHIFT) | (keep_r > 0))
    pick = jnp.where(use0 | use1 | use2, 1.0, 0.0).astype(BF16)
    sums_ref[...] = sums_ref[...] + nn(rhs_ref[0 : 2 * C], pick)


def spread_blocks(off_ref, dp, scr, first, last, refs):
    cs = C // dp
    for k in range(dp):
        row = pl.multiple_of(off_ref[k], 16)
        refs[k % 2][k // 2, first:last] = scr[pl.ds(row, cs)].astype(BF16)


def early_grads_kernel(dp, off_ref, lhs_ref, rhs_ref, keep_ref, give_ref, scr):
    cs = C // dp
    scr[...] = nt(lhs_ref[...], rhs_ref[...])
    for step in range(2):

        @pl.when(pl.program_id(0) == step)
        def _():
            first = (1 - step) * cs
            spread_blocks(off_ref, dp, scr, first, first + cs, (keep_ref, give_ref))


def tap_grads_kernel(dp, off_ref, lhs_ref, rhs_ref, sums_ref, embt_ref, *refs):
    pieces, refs = refs[:dp], refs[dp:]
    keep_ref, give_ref, scr, w_ref, sems = refs
    cs = C // dp
    half = cs // 2
    k = pl.program_id(0)
    groups = block_copies(off_ref, pieces, cs, (0, 1, 2), w_ref, sems)

    @pl.when(k == 0)
    def _():
        begin(groups)

    scr[...] = nt(lhs_ref[...], rhs_ref[...])
    for step in range(3):

        @pl.when(k == step)
        def _():
            spread_blocks(off_ref, dp, scr, step * cs, (step + 1) * cs, (keep_ref, give_ref))

    @pl.when(k == 2)
    def _():
        sums = sums_ref[...]
        hi = sums.astype(BF16)
        lo = (sums - hi.astype(F32)).astype(BF16)
        total = jnp.zeros((C, LANES), F32)
        for t in range(3):
            finish(groups[t])
            g = nn(w_ref[t], hi) + nn(w_ref[t], lo)
            total = total + (pltpu.roll(g, LANES - t * RP, 1) if t else g)
        total = jnp.where(lane_ids((C, LANES)) < RP, total, 0.0)
        hi = total.astype(BF16)
        lo = (total - hi.astype(F32)).astype(BF16)
        scr[:, 0:C] = nt(embt_ref[...], hi) + nt(embt_ref[...], lo)
        for d in range(dp):
            out = (keep_ref, give_ref)[d % 2]
            for h in range(2):
                row = pl.multiple_of(off_ref[d] + h * half, 16)
                out[d // 2, 3 * cs : 3 * cs + half, h * C : (h + 1) * C] = scr[
                    pl.ds(row, half), 0:C
                ].astype(BF16)


def input_grad_kernel(dp, off_ref, dpre_ref, dres_ref, after_ref, *refs):
    pieces, refs = refs[:dp], refs[dp:]
    base_ref, first_ref, last_ref, w_ref, facc_ref, lacc_ref, sems = refs
    i = pl.program_id(0)
    lane = lane_ids((C, LANES))

    @pl.when(i == 0)
    def _():
        groups = block_copies(off_ref, pieces, C // dp, (0, 1, 2), w_ref, sems)
        begin(groups)
        facc_ref[...] = jnp.zeros((C, LANES), F32)
        lacc_ref[...] = jnp.zeros((C, LANES), F32)
        for group in groups:
            finish(group)

    dpre = dpre_ref[...]
    y0 = nn(w_ref[0], dpre)
    y1 = nn(w_ref[1], dpre)
    y2 = nn(w_ref[2], dpre)
    facc = facc_ref[...]
    lacc = lacc_ref[...]
    for j in range(2):
        r = 2 * i + j
        cols = slice(j * LANES, (j + 1) * LANES)
        z0 = pltpu.roll(y0[:, cols], LANES - SHIFT, 1)
        z2 = pltpu.roll(y2[:, cols], SHIFT, 1)
        base_ref[:, cols] = (
            y1[:, cols]
            + jnp.where(lane < LANES - SHIFT, z0, 0.0)
            + jnp.where(lane >= SHIFT, z2, 0.0)
            + dres_ref[:, cols].astype(F32)
        ).astype(BF16)
        here = (lane // SHIFT) == r
        facc = jnp.where(here, pltpu.roll(z0, lax.rem(SHIFT * r + SHIFT, LANES), 1), facc)
        lacc = jnp.where(here, pltpu.roll(z2, SHIFT * r, 1), lacc)
    facc_ref[...] = facc
    lacc_ref[...] = lacc

    @pl.when(i == pl.num_programs(0) - 1)
    def _():
        first_ref[...] = facc.astype(BF16)
        last_ref[...] = lacc.astype(BF16)


def finish_kernel(flags_ref, base_ref, left_ref, right_ref, out_ref):
    i = pl.program_id(0)
    lane = lane_ids((C, LANES))
    left = left_ref[...].astype(F32)
    right = right_ref[...].astype(F32)
    for j in range(2):
        r = 2 * i + j
        cols = slice(j * LANES, (j + 1) * LANES)
        lh = pltpu.roll(left, lax.rem(LANES - SHIFT * r, LANES), 1)
        rh = pltpu.roll(right, LANES - SHIFT - SHIFT * r, 1)
        lh = jnp.where((lane < SHIFT) & (flags_ref[0, r] > 0), lh, 0.0)
        rh = jnp.where((lane >= LANES - SHIFT) & (flags_ref[1, r] > 0), rh, 0.0)
        out_ref[j] = (base_ref[:, cols].astype(F32) + lh + rh).astype(BF16)


def add_blocks_kernel(a_ref, b_ref, keep_ref, give_ref):
    for j in range(a_ref.shape[0]):
        v = a_ref[j].astype(F32) + b_ref[j].astype(F32)
        (keep_ref, give_ref)[j % 2][j // 2] = v.astype(BF16)


def add_halves_kernel(bit_ref, a_ref, b_ref, keep_ref, give_ref, scr):
    half = a_ref.shape[1] // 2
    scr[...] = a_ref[0].astype(F32) + b_ref[0].astype(F32)
    keep_ref[...] = scr[pl.ds(pl.multiple_of(bit_ref[0] * half, 8), half)].astype(BF16)
    give_ref[...] = scr[pl.ds(pl.multiple_of((1 - bit_ref[0]) * half, 8), half)].astype(BF16)


def add_pieces_kernel(a_ref, b_ref, out_ref):
    v = a_ref[...].astype(F32) + b_ref[...].astype(F32)
    size = out_ref.shape[1]
    for p in range(out_ref.shape[0]):
        out_ref[p] = v[p * size : (p + 1) * size].astype(BF16)


def sum_copies_kernel(a_ref, out_ref):
    v = a_ref[0].astype(F32)
    for p in range(1, a_ref.shape[0]):
        v = v + a_ref[p].astype(F32)
    v = v.astype(BF16)
    for p in range(out_ref.shape[0]):
        out_ref[p] = v


def small_sum_kernel(cs, csh, got_ref, film_ref, out_ref, scr):
    v = got_ref[0].astype(F32)
    for d in range(1, got_ref.shape[0]):
        v = v + got_ref[d].astype(F32)
    film_ref[:, 0, :] = v[:cs, 192 : 192 + csh]
    film_ref[:, 1, :] = v[:cs, 192 + csh : 192 + 2 * csh]
    half = cs // 2
    scr[...] = jnp.zeros(scr.shape, F32)
    scr[0:cs] = v[:cs, 0:128]
    scr[cs : cs + half, 0:csh] = v[0:half, 128 : 128 + csh]
    scr[cs : cs + half, csh : 2 * csh] = v[half:cs, 128 : 128 + csh]
    dq = v[cs : cs + QUERIES, 0:64] + v[cs : cs + QUERIES, 64:128]
    hi = dq.astype(BF16).astype(F32)
    scr[cs + half : cs + half + QUERIES, 0:64] = hi
    scr[cs + half : cs + half + QUERIES, 64:128] = dq - hi
    low = scr[...].astype(BF16)
    for p in range(out_ref.shape[0]):
        out_ref[p] = low


def output_kernel(
    cs,
    csh,
    hs,
    bit_ref,
    own1_ref,
    got1_ref,
    own2_ref,
    got2_ref,
    small_ref,
    queries_ref,
    wq_ref,
    step_ref,
    conv_ref,
    cond_ref,
    res_ref,
    skip_ref,
    gqueries_ref,
    gquery_ref,
    key_ref,
    value_ref,
    attn_ref,
    scr1,
    scr2,
    qscr,
    dq,
):
    half = cs // 2
    bit = bit_ref[0]
    for own, got, scr in ((own1_ref, got1_ref, scr1), (own2_ref, got2_ref, scr2)):
        count, size = own.shape[0], own.shape[1]
        for p in range(count):
            a, b = own[p].astype(F32), got[p].astype(F32)
            scr[p * size : (p + 1) * size] = jnp.where(bit == 0, a, b)
            scr[(count + p) * size : (count + p + 1) * size] = jnp.where(bit == 0, b, a)
    cond_ref[...] = scr1[0:cs]
    res_ref[...] = scr1[cs : 2 * cs, 0:C]
    skip_ref[...] = scr1[cs : 2 * cs, C : 2 * C]
    for k in range(3):
        conv_ref[k] = scr2[k * cs : (k + 1) * cs]
    step_ref[0:half] = scr2[3 * cs : 3 * cs + half, 0:C]
    step_ref[half:cs] = scr2[3 * cs : 3 * cs + half, C : 2 * C]
    dq[...] = jnp.zeros(dq.shape, F32)
    for head in range(HEADS):
        cols = slice(head * HEAD_DIM, (head + 1) * HEAD_DIM)
        v = small_ref[head * hs].astype(F32)
        for k in range(1, hs):
            v = v + small_ref[head * hs + k].astype(F32)
        key_ref[:, cols] = v[0:cs, 0:64]
        value_ref[:, cols] = v[0:cs, 64:128]
        dq[0:QUERIES, cols] = v[cs + half :, 0:64] + v[cs + half :, 64:128]
    for s in range(small_ref.shape[0]):
        v = small_ref[s, cs : cs + half].astype(F32)
        attn_ref[0:half, s * csh : (s + 1) * csh] = v[:, 0:csh]
        attn_ref[half:cs, s * csh : (s + 1) * csh] = v[:, csh : 2 * csh]
    qscr[...] = jnp.zeros((LANES, LANES), F32)
    qscr[0:QUERIES, 0:cs] = queries_ref[...].astype(F32)
    qt = qscr[...].T.astype(BF16)
    d = dq[...]
    hi = d.astype(BF16)
    lo = (d - hi.astype(F32)).astype(BF16)
    gquery_ref[...] = (nn(qt, hi) + nn(qt, lo))[0:cs]
    gqueries_ref[...] = fold(nt(parts(d[0:QUERIES], 2), wq_ref[...]), 2)


def attention_back_kernel(
    rows, csh, dp, prm_ref, probs_ref, u_ref, qp_ref, qkv_ref, pooled_ref, memory_ref, dfilm_ref, got_ref, after_ref, out_ref, prow, ds, stack, right
):
    count = prm_ref.shape[0]
    total = count * prm_ref.shape[2]
    cs = C // dp
    wk, wv = qkv_ref[64:128], qkv_ref[128:192]
    datt = got_ref[0, 3 * RP : 4 * RP, 0:HEAD_DIM]
    dmem = got_ref[0, 2 * RP : 3 * RP, 0:csh]
    for s in range(1, count):
        datt = datt + got_ref[s, 3 * RP : 4 * RP, 0:HEAD_DIM]
        dmem = dmem + got_ref[s, 2 * RP : 3 * RP, 0:csh]
    datt = datt * (1.0 / QUERIES)
    for r in range(rows):
        prow[r * total : (r + 1) * total] = prm_ref[:, r].reshape(total, C)
    vh = fold(nn(parts(datt, 2), wv), 2)
    dp_all = fold(nt(parts(vh, 2), prow[...]), 2)
    for r in range(rows):
        cols = slice(r * total, (r + 1) * total)
        p = probs_ref[:, cols]
        dpr = dp_all[r : r + 1, cols]
        inner = jnp.sum(p * dpr, axis=1, keepdims=True)
        ds[:, cols] = p * (dpr - inner)
    tt = fold(nn(parts(ds[...], 2), prow[...]), 2)
    scale = 1.0 / math.sqrt(HEAD_DIM)
    dq = fold(nt(parts(tt, 2), wk), 2) * scale
    stack[...] = jnp.zeros(stack.shape, F32)
    stack[0:QUERIES] = tt
    stack[32:48] = u_ref[...]
    stack[48:64] = pooled_ref[...].astype(F32)
    stack[64:80] = memory_ref[...].astype(F32)
    right[...] = jnp.zeros(right.shape, F32)
    right[0:32, 0:64] = qp_ref[...] * scale
    right[32:48, 64:128] = datt
    right[48:64, 128 : 128 + csh] = dmem
    right[64:80, 192 : 192 + 2 * csh] = dfilm_ref[...].astype(F32)
    grads = lax.dot_general(
        stack[...].T,
        right[...],
        (((1,), (0,)), ((), ())),
        precision=lax.Precision.HIGHEST,
        preferred_element_type=F32,
    ).astype(BF16)
    hi = dq.astype(BF16)
    lo = (dq - hi.astype(F32)).astype(BF16)
    for d in range(dp):
        out_ref[d, 0:cs] = grads[d * cs : (d + 1) * cs]
        out_ref[d, cs : cs + QUERIES] = jnp.zeros((QUERIES, right.shape[1]), BF16)
        out_ref[d, cs : cs + QUERIES, 0:64] = hi
        out_ref[d, cs : cs + QUERIES, 64:128] = lo


def exchange(pieces, axis, groups=None):
    return lax.all_to_all(
        pieces, axis, split_axis=0, concat_axis=0, axis_index_groups=groups, tiled=True
    )


def to_all(piece, axis, axis_size):
    return exchange(jnp.broadcast_to(piece[None], (axis_size,) + piece.shape), axis)


def flipped(v, axis, size, bit):
    return lax.ppermute(v, axis, [(d, d ^ bit) for d in range(size)])


def reduce_rows(keep, give, dp, seq, bit):
    rows = keep.shape[1]
    flip = 1
    while 2 * flip < dp:
        got = flipped(give, "dp", dp, flip)
        half = (keep.shape[0] // 2,) + keep.shape[1:]
        keep, give = call(
            add_blocks_kernel,
            (sds(half, BF16), sds(half, BF16)),
            "add_blocks",
            bytes_accessed=6 * keep.size,
            in_specs=[VM, VM],
            out_specs=(VM, VM),
        )(keep, got)
        flip *= 2
    got = flipped(give, "dp", dp, flip)
    half = sds((rows // 2, 2 * C), BF16)
    keep, give = call(
        add_halves_kernel,
        (half, half),
        "add_halves",
        bytes_accessed=6 * keep.size,
        in_specs=[SM, VM, VM],
        out_specs=(VM, VM),
        scratch_shapes=[pltpu.VMEM((rows, 2 * C), F32)],
    )(bit, keep, got)
    got = flipped(give, "seq", seq, 1)
    count = seq // 2
    piece = sds((count, rows // seq, 2 * C), BF16)
    pieces = call(
        add_pieces_kernel,
        piece,
        "add_pieces",
        bytes_accessed=6 * keep.size,
        in_specs=[VM, VM],
        out_specs=VM,
    )(keep, got)
    groups = [[2 * k + b for k in range(count)] for b in range(2)]
    got = exchange(pieces, "seq", groups)
    copies = call(
        sum_copies_kernel,
        piece,
        "sum_copies",
        bytes_accessed=4 * got.size,
        in_specs=[VM],
        out_specs=VM,
    )(got)
    own = exchange(copies, "seq", groups)
    return own, flipped(own, "seq", seq, 1)


def body(
    dp,
    seq,
    x_in,
    cond,
    segment_ids,
    diffusion_steps,
    prompt,
    prompt_lengths,
    w_step,
    w_conv,
    w_cond,
    w_res,
    w_skip,
    queries,
    w_query,
    w_key,
    w_value,
    w_attn_out,
    w_film,
    d_out,
    d_skip,
):
    rows = x_in.shape[0]
    frames = x_in.shape[2]
    steps = rows // 2
    cols = rows * frames
    cs = C // dp
    csh = C // seq
    hs = max(1, seq // HEADS)
    arows = rows // hs
    pl_local = prompt.shape[1]
    prompt_all = pl_local * seq
    sidx = lax.axis_index("seq")
    didx = lax.axis_index("dp")
    head = sidx // hs
    part = sidx % hs
    up = [(i, i + 1) for i in range(seq - 1)]
    down = [(i + 1, i) for i in range(seq - 1)]
    offsets = (jnp.bitwise_xor(didx, jnp.arange(dp, dtype=jnp.int32)) * cs).astype(jnp.int32)
    bit = (sidx % 2).astype(jnp.int32).reshape(1)

    pack_rows = 6 * cs + cs // 2
    pack, first, last = call(
        functools.partial(prep_kernel, cs, csh),
        (sds((pack_rows, 2 * C), BF16), sds((C, LANES), BF16), sds((C, LANES), BF16)),
        "prep",
        bytes_accessed=5e6,
        in_specs=[SM] + [VM] * 12,
        out_specs=(VM, VM, VM),
        scratch_shapes=[pltpu.VMEM((LANES, LANES), F32)],
    )(
        head.astype(jnp.int32).reshape(1),
        x_in,
        w_conv,
        w_cond,
        w_res,
        w_skip,
        w_attn_out,
        w_step,
        w_film,
        w_query,
        w_key,
        w_value,
        queries,
    )
    have = {0: pack}
    flip = dp // 2
    while flip:
        for k in sorted(have):
            have[k + flip] = flipped(have[k], "dp", dp, flip)
        flip //= 2
    weights = [have[k] for k in range(dp)]
    left_halo = lax.ppermute(last, "seq", up)
    right_halo = lax.ppermute(first, "seq", down)

    pieces = prompt.reshape(hs, arows, pl_local, C)
    pieces = jnp.broadcast_to(pieces[None], (seq // hs, hs, arows, pl_local, C))
    prompts = exchange(pieces.reshape(seq, arows, pl_local, C), "seq")

    block_ids = segment_ids[:, ::frames]
    padded_ids = jnp.pad(block_ids, ((0, 0), (1, 1)), constant_values=-1)
    mine = lax.dynamic_slice_in_dim(padded_ids, sidx, 3, 1)
    flags = jnp.stack([mine[:, 0] == mine[:, 1], mine[:, 2] == mine[:, 1]]).astype(jnp.int32)
    block_ids = jnp.pad(block_ids, ((0, RP - rows), (0, 0)))
    half = C // 2
    frequency = jnp.exp(jnp.arange(half, dtype=F32) * (-math.log(10000.0) / half))
    angles = diffusion_steps.astype(F32)[:, None] * frequency[None, :]
    embedding = jnp.concatenate([jnp.sin(angles), jnp.cos(angles)], axis=1).astype(BF16)
    emb_rows = jnp.pad(embedding, ((0, RP - rows), (0, 0)))
    emb_cols = jnp.pad(embedding.T, ((0, 0), (0, LANES - rows)))
    lengths = lax.dynamic_slice_in_dim(prompt_lengths, part * arows, arows, 0)

    apack, probs, u, pooled_head, qp, qkv = call(
        functools.partial(attention_kernel, arows, dp, C + 2 * csh),
        (
            sds((C, 2 * C), BF16),
            sds((QUERIES, arows * prompt_all), F32),
            sds((RP, C), F32),
            sds((RP, HEAD_DIM), F32),
            sds((QUERIES, HEAD_DIM), F32),
            sds((256, C), BF16),
        ),
        "attention",
        flops=2 * 160 * 1536 * 512,
        bytes_accessed=4e6,
        in_specs=[SM, SM, VM] + [HB] * dp,
        out_specs=(VM,) * 6,
        scratch_shapes=[
            pltpu.VMEM((arows * prompt_all, C), BF16),
            pltpu.VMEM((RP, arows * prompt_all), F32),
            pltpu.SemaphoreType.DMA((dp,)),
        ],
    )(offsets, lengths, prompts, *weights)
    pooled_got = to_all(pooled_head, "seq", seq)
    pooled, memory, film = call(
        functools.partial(memory_kernel, csh, hs, arows),
        (sds((RP, C), BF16), sds((RP, C), BF16), sds((RP, 2 * csh), F32)),
        "memory",
        bytes_accessed=2e6,
        in_specs=[VM, VM],
        out_specs=(VM, VM, VM),
        scratch_shapes=[pltpu.VMEM((RP, C), F32)],
    )(pooled_got, apack)

    row_block = pl.BlockSpec((2, C, LANES), lambda i: (i, 0, 0))

    def col_block(height, at=0):
        return pl.BlockSpec((height, 2 * LANES), lambda i: (at, i))

    inp, tanh_part, sig_part, skip_out, mid, stats = call(
        functools.partial(forward_kernel, dp, csh),
        (
            sds((5 * C, cols), BF16),
            sds((C, cols), F32),
            sds((C, cols), F32),
            sds(x_in.shape, BF16),
            sds((C, cols), BF16),
            sds((seq, 2 * RP, 2 * csh), F32),
        ),
        "wavenet",
        flops=2 * cols * (4 * C * 2 * C + 2 * C * C),
        bytes_accessed=30e6,
        grid=(steps,),
        in_specs=[
            SM,
            SM,
            row_block,
            row_block,
            row_block,
            whole((C, LANES)),
            whole((C, LANES)),
            whole((RP, C)),
        ]
        + [HB] * dp,
        out_specs=(
            col_block(5 * C),
            col_block(C),
            col_block(C),
            row_block,
            col_block(C),
            pl.BlockSpec((seq, 2 * RP, 2 * csh), lambda i: (0, 0, 0)),
        ),
        scratch_shapes=[
            pltpu.VMEM((5, C, 2 * C), BF16),
            pltpu.VMEM((C, C), BF16),
            pltpu.VMEM((2 * C, 4 * C), BF16),
            pltpu.VMEM((2 * C, C), BF16),
            pltpu.VMEM((C, LANES), F32),
            pltpu.VMEM((C, LANES), F32),
            pltpu.SemaphoreType.DMA((7 * dp,)),
        ],
    )(offsets, flags, x_in, cond, d_out, left_halo, right_halo, emb_rows, *weights)

    stats_got = exchange(stats, "seq")
    coef_out, dfilm = call(
        functools.partial(stats_kernel, csh, hs, arows),
        (sds((seq, 4 * RP, 2 * csh), F32), sds((RP, 2 * csh), BF16)),
        "segments",
        bytes_accessed=2e6,
        in_specs=[VM, VM, VM, VM],
        out_specs=(VM, VM),
    )(block_ids, stats_got, film, apack)
    coef = exchange(coef_out, "seq")

    layer_out, rhs, sums = call(
        functools.partial(gate_kernel, dp, csh),
        (
            sds(x_in.shape, BF16),
            sds((4 * C, cols), BF16),
            sds((2 * C, LANES), F32),
        ),
        "gate_back",
        flops=2 * cols * 2 * C * C,
        bytes_accessed=20e6,
        grid=(steps,),
        in_specs=[
            SM,
            SM,
            whole((seq, 4 * RP, 2 * csh)),
            col_block(C),
            row_block,
            row_block,
            col_block(C),
            col_block(C),
        ]
        + [HB] * dp,
        out_specs=(
            row_block,
            col_block(4 * C),
            pl.BlockSpec((2 * C, LANES), lambda i: (0, 0)),
        ),
        scratch_shapes=[
            pltpu.VMEM((LANES, C), F32),
            pltpu.VMEM((C, LANES), F32),
            pltpu.VMEM((1, C, 2 * C), BF16),
            pltpu.SemaphoreType.DMA((dp,)),
        ],
    )(offsets, flags, coef, mid, d_out, d_skip, tanh_part, sig_part, *weights)

    part1 = sds((dp // 2, 2 * cs, 2 * C), BF16)
    keep1, give1 = call(
        functools.partial(early_grads_kernel, dp),
        (part1, part1),
        "early_grads",
        flops=2 * cols * 2 * C * 2 * C,
        bytes_accessed=10e6,
        grid=(2,),
        in_specs=[
            SM,
            pl.BlockSpec((C, cols), lambda k: (4 - k, 0)),
            pl.BlockSpec((2 * C, cols), lambda k: (1 - k, 0)),
        ],
        out_specs=(
            pl.BlockSpec((dp // 2, 2 * cs, 2 * C), lambda k: (0, 0, 0)),
            pl.BlockSpec((dp // 2, 2 * cs, 2 * C), lambda k: (0, 0, 0)),
        ),
        scratch_shapes=[pltpu.VMEM((C, 2 * C), F32)],
    )(offsets, inp, rhs)
    rows2 = 3 * cs + cs // 2
    part2 = sds((dp // 2, rows2, 2 * C), BF16)
    keep2, give2 = call(
        functools.partial(tap_grads_kernel, dp),
        (part2, part2),
        "tap_grads",
        flops=2 * cols * 3 * C * 2 * C,
        bytes_accessed=15e6,
        grid=(3,),
        in_specs=[
            SM,
            pl.BlockSpec((C, cols), lambda k: (k, 0)),
            pl.BlockSpec((2 * C, cols), lambda k: (0, 0)),
            whole((2 * C, LANES)),
            whole((C, LANES)),
        ]
        + [HB] * dp,
        out_specs=(
            pl.BlockSpec((dp // 2, rows2, 2 * C), lambda k: (0, 0, 0)),
            pl.BlockSpec((dp // 2, rows2, 2 * C), lambda k: (0, 0, 0)),
        ),
        scratch_shapes=[
            pltpu.VMEM((C, 2 * C), F32),
            pltpu.VMEM((3, C, 2 * C), BF16),
            pltpu.SemaphoreType.DMA((3 * dp,)),
        ],
    )(offsets, inp, rhs, sums, emb_cols, *weights)
    own1, got1 = reduce_rows(keep1, give1, dp, seq, bit)
    own2, got2 = reduce_rows(keep2, give2, dp, seq, bit)

    small = call(
        functools.partial(attention_back_kernel, arows, csh, dp),
        sds((dp, cs + QUERIES, 384), BF16),
        "attention_back",
        flops=2 * 200 * 1536 * 512,
        bytes_accessed=4e6,
        in_specs=[VM] * 9 + [HB],
        out_specs=VM,
        scratch_shapes=[
            pltpu.VMEM((arows * prompt_all, C), BF16),
            pltpu.VMEM((QUERIES, arows * prompt_all), F32),
            pltpu.VMEM((LANES, C), F32),
            pltpu.VMEM((LANES, 384), F32),
        ],
    )(prompts, probs, u, qp, qkv, pooled, memory, dfilm, coef, keep2)
    small_rows = cs + cs // 2 + QUERIES
    grad_film, small = call(
        functools.partial(small_sum_kernel, cs, csh),
        (sds((cs, 2, csh), F32), sds((seq, small_rows, LANES), BF16)),
        "small_sum",
        bytes_accessed=1e6,
        in_specs=[VM],
        out_specs=(VM, VM),
        scratch_shapes=[pltpu.VMEM((small_rows, LANES), F32)],
    )(exchange(small, "dp"))
    small = exchange(small, "seq")

    base, first, last = call(
        functools.partial(input_grad_kernel, dp),
        (sds((C, cols), BF16), sds((C, LANES), BF16), sds((C, LANES), BF16)),
        "input_grad",
        flops=2 * cols * 6 * C * C,
        bytes_accessed=10e6,
        grid=(steps,),
        in_specs=[SM, col_block(2 * C), col_block(C, 2), HB] + [HB] * dp,
        out_specs=(
            col_block(C),
            pl.BlockSpec((C, LANES), lambda i: (0, 0)),
            pl.BlockSpec((C, LANES), lambda i: (0, 0)),
        ),
        scratch_shapes=[
            pltpu.VMEM((3, C, 2 * C), BF16),
            pltpu.VMEM((C, LANES), F32),
            pltpu.VMEM((C, LANES), F32),
            pltpu.SemaphoreType.DMA((3 * dp,)),
        ],
    )(offsets, rhs, rhs, keep2, *weights)
    from_left = lax.ppermute(last, "seq", up)
    from_right = lax.ppermute(first, "seq", down)
    grad_input = call(
        finish_kernel,
        sds(x_in.shape, BF16),
        "grad_input",
        bytes_accessed=4e6,
        grid=(steps,),
        in_specs=[SM, col_block(C), whole((C, LANES)), whole((C, LANES))],
        out_specs=row_block,
    )(flags, base, from_left, from_right)

    (
        grad_step,
        grad_conv,
        grad_cond,
        grad_res,
        grad_skip,
        grad_queries,
        grad_query,
        grad_key,
        grad_value,
        grad_attn,
    ) = call(
        functools.partial(output_kernel, cs, csh, hs),
        (
            sds((cs, C), F32),
            sds((3, cs, 2 * C), F32),
            sds((cs, 2 * C), F32),
            sds((cs, C), F32),
            sds((cs, C), F32),
            sds((QUERIES, cs), F32),
            sds((cs, C), F32),
            sds((cs, C), F32),
            sds((cs, C), F32),
            sds((cs, C), F32),
        ),
        "outputs",
        bytes_accessed=8e6,
        in_specs=[SM] + [VM] * 7,
        out_specs=(VM,) * 10,
        scratch_shapes=[
            pltpu.VMEM((2 * cs, 2 * C), F32),
            pltpu.VMEM((rows2, 2 * C), F32),
            pltpu.VMEM((LANES, LANES), F32),
            pltpu.VMEM((LANES, C), F32),
        ],
    )(bit, own1, got1, own2, got2, small, queries, w_query)
    return (
        layer_out,
        skip_out,
        grad_input,
        grad_step,
        grad_conv,
        grad_cond,
        grad_res,
        grad_skip,
        grad_queries,
        grad_query,
        grad_key,
        grad_value,
        grad_attn,
        grad_film,
    )


def solution(mesh):
    frames = P("dp", None, "seq")
    matrix = P("dp", None)
    return jax.shard_map(
        functools.partial(body, mesh.shape["dp"], mesh.shape["seq"]),
        mesh=mesh,
        in_specs=(
            frames,
            frames,
            P("dp", None),
            P("dp"),
            P("dp", "seq", None),
            P("dp"),
            matrix,
            P(None, "dp", None),
            matrix,
            matrix,
            matrix,
            P(None, "dp"),
            matrix,
            matrix,
            matrix,
            matrix,
            frames,
            frames,
            frames,
        ),
        out_specs=(
            frames,
            frames,
            frames,
            matrix,
            P(None, "dp", None),
            matrix,
            matrix,
            matrix,
            P(None, "dp"),
            matrix,
            matrix,
            matrix,
            matrix,
            frames,
        ),
        check_vma=False,
    )
```

```python
import functools
import math

import jax
import jax.numpy as jnp
from jax import lax
from jax.experimental import pallas as pl
from jax.experimental.pallas import tpu as pltpu
from jax.sharding import PartitionSpec as P

C = 512
HEADS = 8
QUERIES = 32
HEAD_DIM = 64
SHIFT = 4
SQRT_HALF = 0.7071067811865476
NORM_EPS = 1e-05
MASKED_SCORE = -1e30
LANES = 128
RP = 16
F32 = jnp.float32
BF16 = jnp.bfloat16
VMEM_BYTES = 50 * 1024 * 1024


def nn(a, b):
    return lax.dot_general(a, b, (((1,), (0,)), ((), ())), preferred_element_type=F32)


def nt(a, b):
    return lax.dot_general(a, b, (((1,), (1,)), ((), ())), preferred_element_type=F32)


def parts(v, count):
    out = []
    for _ in range(count):
        low = v.astype(BF16)
        out.append(low)
        v = v - low.astype(F32)
    return jnp.concatenate(out, axis=0)


def fold(v, count):
    rows = v.shape[0] // count
    total = v[:rows]
    for k in range(1, count):
        total = total + v[k * rows : (k + 1) * rows]
    return total


def lane_ids(shape):
    return lax.broadcasted_iota(jnp.int32, shape, len(shape) - 1)


def sds(shape, dtype):
    return jax.ShapeDtypeStruct(shape, dtype)


VM = pl.BlockSpec(memory_space=pltpu.VMEM)
HB = pl.BlockSpec(memory_space=pl.ANY)
SM = pl.BlockSpec(memory_space=pltpu.SMEM)


def whole(shape):
    return pl.BlockSpec(shape, lambda i: (0,) * len(shape), pipeline_mode=pl.Buffered(1))


class Got:
    def __init__(self, array):
        self.array = array


class Chain:
    def __init__(self):
        self.last = None

    def __call__(self, kernel, out_shape, name, args, flops=0, nbytes=0, prefetch=0, **kw):
        single = not isinstance(out_shape, tuple)
        shapes = (out_shape,) if single else out_shape
        pinned = tuple(pltpu.HBM(v.shape, v.dtype) for v in shapes)
        in_specs = list(kw.pop("in_specs"))
        count = prefetch + len(in_specs)
        args = list(args)
        if self.last is not None:
            in_specs.append(HB)
            args.append(self.last)

            def run(*refs):
                return kernel(*refs[:count], *refs[count + 1 :])
        else:
            run = kernel
        values = []
        for k, v in enumerate(args):
            spec = SM if k < prefetch else in_specs[k - prefetch]
            if isinstance(v, Got):
                values.append(v.array)
            elif spec is SM:
                values.append(v)
            else:
                values.append(pltpu.with_memory_space_constraint(v, pltpu.HBM))
        spec = pltpu.PrefetchScalarGridSpec(
            num_scalar_prefetch=prefetch,
            grid=kw.pop("grid", ()),
            in_specs=in_specs,
            out_specs=kw.pop("out_specs"),
            scratch_shapes=kw.pop("scratch_shapes", ()),
        )
        out = pl.pallas_call(
            run,
            out_shape=pinned[0] if single else pinned,
            name=name,
            grid_spec=spec,
            cost_estimate=pl.CostEstimate(
                flops=int(flops), bytes_accessed=int(nbytes), transcendentals=0
            ),
            compiler_params=pltpu.CompilerParams(vmem_limit_bytes=VMEM_BYTES),
        )(*values)
        self.last = out if single else out[0]
        return out


PLAIN = 1408


def plain_pack_kernel(cs, csh, head_ref, res_ref, skip_ref, attn_ref, step_ref, film_ref, wq_ref, wk_ref, wv_ref, queries_ref, out_ref, scr):
    out_ref[:, 0:C] = attn_ref[...]
    out_ref[:, C : 2 * C] = step_ref[...]
    off = 2 * C
    scr[...] = jnp.zeros((2 * LANES, LANES), F32)
    scr[0 : 2 * csh, 0:cs] = film_ref[...].astype(F32)
    scr[LANES : LANES + QUERIES, 0:cs] = queries_ref[...].astype(F32)
    film = scr[0:LANES].T[0:cs]
    table = scr[LANES : 2 * LANES].T[0:cs]
    turn = lax.rem(C - HEAD_DIM * head_ref[0], C)
    blocks = [film[:, 0 : 2 * csh]]
    for ref in (wq_ref, wk_ref, wv_ref):
        blocks.append(pltpu.roll(ref[...].astype(F32), turn, 1)[:, 0:HEAD_DIM])
    blocks.append(table[:, 0 : PLAIN - off - 2 * csh - 3 * HEAD_DIM])
    for block in blocks:
        out_ref[:, off : off + block.shape[1]] = block.astype(BF16)
        off += block.shape[1]
    out_ref[:, PLAIN : PLAIN + C] = res_ref[...]
    out_ref[:, PLAIN + C : PLAIN + 2 * C] = skip_ref[...]


def turned_pack_kernel(cs, conv_ref, cond_ref, out_ref, scr):
    for k in range(3):
        scr[k * cs : (k + 1) * cs] = conv_ref[k]
    scr[3 * cs : 4 * cs] = cond_ref[...]
    out_ref[...] = scr[...].T


def edge_kernel(hs, x_ref, prompt_ref, first_ref, last_ref, copies_ref):
    rows = x_ref.shape[0]
    arows = copies_ref.shape[1]
    for s in range(copies_ref.shape[0]):
        part = s % hs
        copies_ref[s] = prompt_ref[part * arows : (part + 1) * arows]
    lane = lane_ids((C, LANES))
    first = jnp.zeros((C, LANES), F32)
    last = jnp.zeros((C, LANES), F32)
    for r in range(rows):
        v = x_ref[r].astype(F32)
        here = (lane // SHIFT) == r
        first = jnp.where(here, pltpu.roll(v, SHIFT * r, 1) if r else v, first)
        last = jnp.where(here, pltpu.roll(v, SHIFT * r + SHIFT, 1), last)
    first_ref[...] = first.astype(BF16)
    last_ref[...] = last.astype(BF16)


def copies_of(pieces, make):
    return [pltpu.make_async_copy(*make(k, piece)) for k, piece in enumerate(pieces)]


def begin(copies):
    for copy in copies:
        copy.start()


def finish(copies):
    for copy in copies:
        copy.wait()


def turned_copies(off_ref, turned, cs, dst, sems, base=0):
    def make(k, piece):
        lane = pl.multiple_of(off_ref[k] * 4, LANES)
        return piece, dst.at[:, pl.ds(lane, 4 * cs)], sems.at[base + k]

    return copies_of(turned, make)


def plain_copies(off_ref, plain, cs, lanes, width, dst, sems, base=0):
    def make(k, piece):
        row = pl.multiple_of(off_ref[k], 16)
        return piece.at[:, pl.ds(lanes, width)], dst.at[pl.ds(row, cs)], sems.at[base + k]

    return copies_of(plain, make)


def forward_kernel(dp, csh, off_ref, flags_ref, x_ref, cond_ref, dout_ref, left_ref, right_ref, emb_ref, *refs):
    turned, plain, refs = refs[:dp], refs[dp : 2 * dp], refs[2 * dp :]
    (
        inp_ref,
        gated_ref,
        tanh_ref,
        sig_ref,
        skip_ref,
        mid_ref,
        stats_ref,
        wt_ref,
        rn_ref,
        step_ref,
        rst_ref,
        lift_ref,
        acc_ref,
        sems,
    ) = refs
    cs = C // dp
    i = pl.program_id(0)
    lane = lane_ids((C, LANES))

    @pl.when(i == 0)
    def _():
        steps = plain_copies(off_ref, plain, cs, C, C, step_ref, sems)
        outs = plain_copies(off_ref, plain, cs, PLAIN, 2 * C, rn_ref, sems, dp)
        convs = turned_copies(off_ref, turned, cs, wt_ref, sems, 2 * dp)
        begin(steps + outs + convs)
        acc_ref[...] = jnp.zeros((C, LANES), F32)
        finish(steps)
        lift = nn(emb_ref[0:RP], step_ref[...])
        lift = jnp.concatenate([lift, jnp.zeros((LANES - RP, C), F32)], axis=0)
        lift_ref[...] = lift.T
        finish(outs)
        rst_ref[...] = rn_ref[...].T
        finish(convs)

    lift = pltpu.roll(lift_ref[...], lax.rem(LANES - 2 * i, LANES), 1)
    left = left_ref[...].astype(F32)
    right = right_ref[...].astype(F32)

    def put(tap, cols, value):
        for d in range(dp):
            at = d * 4 * cs + tap * cs
            inp_ref[at : at + cs, cols] = value[d * cs : (d + 1) * cs]

    for j in range(2):
        r = 2 * i + j
        lc = lift[:, j : j + 1]
        sh = (x_ref[j].astype(F32) + lc).astype(BF16)
        shf = sh.astype(F32)
        lh = pltpu.roll(left, lax.rem(LANES - SHIFT * r, LANES), 1)
        lh = jnp.where(flags_ref[0, r] > 0, (lh + lc).astype(BF16).astype(F32), 0.0)
        rh = pltpu.roll(right, LANES - SHIFT - SHIFT * r, 1)
        rh = jnp.where(flags_ref[1, r] > 0, (rh + lc).astype(BF16).astype(F32), 0.0)
        cols = slice(j * LANES, (j + 1) * LANES)
        put(0, cols, jnp.where(lane < SHIFT, lh, pltpu.roll(shf, SHIFT, 1)).astype(BF16))
        put(1, cols, sh)
        put(
            2,
            cols,
            jnp.where(lane >= LANES - SHIFT, rh, pltpu.roll(shf, LANES - SHIFT, 1)).astype(BF16),
        )
        put(3, cols, cond_ref[j])
    pre = nn(wt_ref[...], inp_ref[...])
    th = jnp.tanh(pre[:C])
    sg = jax.nn.sigmoid(pre[C:])
    tanh_ref[...] = th
    sig_ref[...] = sg
    g = (th * sg).astype(BF16)
    gated_ref[...] = g
    rs = nn(rst_ref[...], g)
    acc = acc_ref[...]
    for j in range(2):
        r = 2 * i + j
        cols = slice(j * LANES, (j + 1) * LANES)
        skip_ref[j] = rs[C:, cols].astype(BF16)
        mid = ((x_ref[j].astype(F32) + rs[:C, cols]) * SQRT_HALF).astype(BF16)
        mid_ref[:, cols] = mid
        mf = mid.astype(F32)
        df = dout_ref[j].astype(F32)
        total = jnp.sum(mf, axis=1, keepdims=True)
        dev = mf - total * (1.0 / LANES)
        acc = jnp.where(lane == r, total, acc)
        acc = jnp.where(lane == RP + r, jnp.sum(dev * dev, axis=1, keepdims=True), acc)
        acc = jnp.where(lane == 2 * RP + r, jnp.sum(df, axis=1, keepdims=True), acc)
        acc = jnp.where(lane == 3 * RP + r, jnp.sum(df * dev, axis=1, keepdims=True), acc)
    acc_ref[...] = acc

    @pl.when(i == pl.num_programs(0) - 1)
    def _():
        t = acc.T
        for s in range(C // csh):
            cols = slice(s * csh, (s + 1) * csh)
            stats_ref[s, :, 0:csh] = t[0 : 2 * RP, cols]
            stats_ref[s, :, csh : 2 * csh] = t[2 * RP : 4 * RP, cols]


def attention_kernel(rows, dp, off, off_ref, len_ref, prm_ref, *refs):
    pieces, refs = refs[:dp], refs[dp:]
    apack_ref, probs_ref, u_ref, pooled_ref, qp_ref, qkv_ref, prow, abd, sems = refs
    cs = C // dp
    copies = plain_copies(off_ref, pieces, cs, 0, PLAIN, apack_ref, sems)
    begin(copies)
    total = prm_ref.shape[0] * prm_ref.shape[2]
    for r in range(rows):
        prow[r * total : (r + 1) * total] = prm_ref[:, r].reshape(total, C)
    abd[...] = jnp.zeros(abd.shape, F32)
    finish(copies)
    qkv = apack_ref[:, off : off + 256].T
    qkv_ref[...] = qkv
    wq, wk, wv = qkv[0:64], qkv[64:128], qkv[128:192]
    qp = nt(qkv[192:224], wq)
    qp_ref[...] = qp
    st = fold(nn(parts(qp, 3), wk), 3) * (1.0 / math.sqrt(HEAD_DIM))
    scores = fold(nt(parts(st, 3), prow[...]), 3)
    for r in range(rows):
        cols = slice(r * total, (r + 1) * total)
        live = lane_ids((QUERIES, total)) < len_ref[r]
        s = jnp.where(live, scores[:, cols], MASKED_SCORE)
        e = jnp.where(live, jnp.exp(s - jnp.max(s, axis=1, keepdims=True)), 0.0)
        p = e / jnp.sum(e, axis=1, keepdims=True)
        probs_ref[:, cols] = p
        abd[r : r + 1, cols] = jnp.sum(p, axis=0, keepdims=True)
    u = fold(nn(parts(abd[...], 2), prow[...]), 2)
    u_ref[...] = u
    pooled = fold(nt(parts(u * (1.0 / QUERIES), 2), wv), 2)
    for s in range(pooled_ref.shape[0]):
        pooled_ref[s, :, 0:HEAD_DIM] = pooled
        pooled_ref[s, :, HEAD_DIM:] = jnp.zeros(pooled.shape, F32)


def memory_kernel(csh, hs, rows, got_ref, apack_ref, pooled_ref, memory_ref, film_ref, scratch):
    scratch[...] = jnp.zeros(scratch.shape, F32)
    for s in range(got_ref.shape[0]):
        head, part = s // hs, s % hs
        scratch[part * rows : (part + 1) * rows, head * HEAD_DIM : (head + 1) * HEAD_DIM] = got_ref[
            s, 0:rows, 0:HEAD_DIM
        ]
    pooled = scratch[...].astype(BF16)
    pooled_ref[...] = pooled
    memory = nn(pooled, apack_ref[:, 0:C]).astype(BF16)
    memory_ref[...] = memory
    film_ref[...] = nn(memory, apack_ref[:, 2 * C : 2 * C + 2 * csh])


def stats_kernel(csh, hs, rows, seg_ref, x_ref, film_ref, apack_ref, out_ref, dfilm_ref):
    count = x_ref.shape[0]
    seg = seg_ref[...]
    f0 = film_ref[:, 0:csh]
    f1 = film_ref[:, csh : 2 * csh]
    total = [x_ref[s, 0:RP, 0:csh] for s in range(count)]
    second = [x_ref[s, RP : 2 * RP, 0:csh] for s in range(count)]
    dsum = [x_ref[s, 0:RP, csh : 2 * csh] for s in range(count)]
    cross = [x_ref[s, RP : 2 * RP, csh : 2 * csh] for s in range(count)]
    means = [v * (1.0 / LANES) for v in total]
    d0 = jnp.zeros((RP, csh), F32)
    d1 = jnp.zeros((RP, csh), F32)
    for me in range(count):
        same = [(seg[:, s : s + 1] == seg[:, me : me + 1]).astype(F32) for s in range(count)]
        frames = sum(same) * float(LANES)
        inv = 1.0 / frames
        mean = sum(m * v for m, v in zip(same, total)) * inv
        var = (
            sum(
                m * (v + float(LANES) * (u - mean) * (u - mean))
                for m, v, u in zip(same, second, means)
            )
            * inv
        )
        scale = lax.rsqrt(var + NORM_EPS)
        dtot = sum(m * v for m, v in zip(same, dsum))
        xtot = sum(m * (v + (u - mean) * d) for m, v, u, d in zip(same, cross, means, dsum)) * scale
        mean_part = f0 * dtot * inv
        cross_part = f0 * xtot * inv
        slope = scale * scale * cross_part
        out_ref[me, 0:RP, 0:csh] = 1.0 + f0 * scale
        out_ref[me, RP : 2 * RP, 0:csh] = f1 - f0 * scale * mean
        out_ref[me, 0:RP, csh : 2 * csh] = -slope
        out_ref[me, RP : 2 * RP, csh : 2 * csh] = slope * mean - scale * mean_part
        d0 = d0 + (cross[me] + (means[me] - mean) * dsum[me]) * scale
        d1 = d1 + dsum[me]
    dfilm = jnp.concatenate([d0, d1], axis=1).astype(BF16)
    dfilm_ref[...] = dfilm
    dmem = nt(dfilm, apack_ref[:, 2 * C : 2 * C + 2 * csh])
    dpool = nt(dmem.astype(BF16), apack_ref[:, 0:C])
    for s in range(count):
        head, part = s // hs, s % hs
        rolled = pltpu.roll(dpool, RP - part * rows, 0) if part else dpool
        out_ref[s, 2 * RP : 3 * RP, 0:csh] = dmem[:, s * csh : (s + 1) * csh]
        out_ref[s, 2 * RP : 3 * RP, csh : 2 * csh] = jnp.zeros((RP, csh), F32)
        out_ref[s, 3 * RP : 4 * RP, 0:HEAD_DIM] = rolled[:, head * HEAD_DIM : (head + 1) * HEAD_DIM]
        if 2 * csh > HEAD_DIM:
            out_ref[s, 3 * RP : 4 * RP, HEAD_DIM : 2 * csh] = jnp.zeros(
                (RP, 2 * csh - HEAD_DIM), F32
            )


def gate_kernel(dp, csh, off_ref, flags_ref, coef_ref, mid_ref, dout_ref, dskip_ref, tanh_ref, sig_ref, *refs):
    plain, refs = refs[:dp], refs[dp:]
    layer_ref, dpre_ref, dres_ref, sums_ref, rows_ref, cols_ref, w_ref, sems = refs
    i = pl.program_id(0)

    @pl.when(i == 0)
    def _():
        outs = plain_copies(off_ref, plain, C // dp, PLAIN, 2 * C, w_ref, sems)
        begin(outs)
        rows_ref[...] = jnp.zeros(rows_ref.shape, F32)
        for s in range(C // csh):
            cols = slice(s * csh, (s + 1) * csh)
            rows_ref[0 : 2 * RP, cols] = coef_ref[s, 0 : 2 * RP, 0:csh]
            rows_ref[2 * RP : 4 * RP, cols] = coef_ref[s, 0 : 2 * RP, csh : 2 * csh]
        cols_ref[...] = rows_ref[...].T
        sums_ref[...] = jnp.zeros(sums_ref.shape, F32)
        finish(outs)

    coef = pltpu.roll(cols_ref[...], lax.rem(LANES - 2 * i, LANES), 1)
    for j in range(2):
        cols = slice(j * LANES, (j + 1) * LANES)
        mf = mid_ref[:, cols].astype(F32)
        df = dout_ref[j].astype(F32)
        a = coef[:, j : j + 1]
        b = coef[:, RP + j : RP + j + 1]
        be = coef[:, 2 * RP + j : 2 * RP + j + 1]
        ga = coef[:, 3 * RP + j : 3 * RP + j + 1]
        layer_ref[j] = (a * mf + b).astype(BF16)
        dmid = (a * df + (be * mf + ga)).astype(BF16).astype(F32)
        dres_ref[0:C, cols] = (dmid * SQRT_HALF).astype(BF16)
        dres_ref[C : 2 * C, cols] = dskip_ref[j]
    dg = nn(w_ref[...], dres_ref[...])
    th = tanh_ref[...]
    sg = sig_ref[...]
    dpre_ref[0:C] = (dg * sg * (1.0 - th * th)).astype(BF16)
    dpre_ref[C : 2 * C] = (dg * th * sg * (1.0 - sg)).astype(BF16)
    frame = lax.broadcasted_iota(jnp.int32, (2 * LANES, LANES), 0)
    column = lane_ids((2 * LANES, LANES))
    place = frame % LANES
    second = frame >= LANES
    keep_l = jnp.where(second, flags_ref[0, 2 * i + 1], flags_ref[0, 2 * i])
    keep_r = jnp.where(second, flags_ref[1, 2 * i + 1], flags_ref[1, 2 * i])
    row = 2 * i + jnp.where(second, 1, 0)
    use0 = (column == row) & ((place >= SHIFT) | (keep_l > 0))
    use1 = column == RP + row
    use2 = (column == 2 * RP + row) & ((place < LANES - SHIFT) | (keep_r > 0))
    pick = jnp.where(use0 | use1 | use2, 1.0, 0.0).astype(BF16)
    sums_ref[...] = sums_ref[...] + nn(dpre_ref[...], pick)


def step_grad_kernel(dp, off_ref, sums_ref, emb_ref, *refs):
    turned, refs = refs[:dp], refs[dp:]
    out_ref, wt_ref, sems = refs
    cs = C // dp
    copies = turned_copies(off_ref, turned, cs, wt_ref, sems)
    begin(copies)
    sums = sums_ref[...].T
    finish(copies)
    total = jnp.zeros((RP, 4 * C), F32)
    w = wt_ref[...]
    lane = lane_ids((RP, 4 * C))
    for t in range(3):
        g = fold(nn(parts(sums[t * RP : (t + 1) * RP], 2), w), 2)
        total = total + jnp.where((lane // cs) % 4 == t, g, 0.0)
    out = []
    for d in range(dp):
        block = total[:, d * 4 * cs : (d + 1) * 4 * cs]
        v = block[:, 0:cs] + block[:, cs : 2 * cs] + block[:, 2 * cs : 3 * cs]
        out.append(v)
    g = jnp.concatenate(out, axis=1)
    g = jnp.concatenate([g, jnp.zeros((LANES - RP, C), F32)], axis=0)
    hi = g.astype(BF16)
    lo = (g - hi.astype(F32)).astype(BF16)
    emb = emb_ref[...].T
    out_ref[...] = (nn(emb, hi) + nn(emb, lo)).astype(BF16)


def first_grads_kernel(order_ref, inp_ref, dpre_ref, gated_ref, dres_ref, keep_ref, give_ref):
    k = pl.program_id(0)
    cs = gated_ref.shape[0]
    width = dpre_ref.shape[0]
    g = nt(inp_ref[...], dpre_ref[...]).astype(BF16)
    h = nt(gated_ref[...], dres_ref[...]).astype(BF16)
    for parity, ref in enumerate((keep_ref, give_ref)):

        @pl.when(k % 2 == parity)
        def _():
            ref[0, :, 0:width] = g
            for t in range(4):
                ref[0, t * cs : (t + 1) * cs, width : 2 * width] = h[:, t * width : (t + 1) * width]


def middle_grads_kernel(order_ref, inp_ref, low_ref, high_ref, keep_ref, give_ref):
    k = pl.program_id(0)
    width = low_ref.shape[0]
    g = nt(inp_ref[...], low_ref[...]).astype(BF16)
    h = nt(inp_ref[...], high_ref[...]).astype(BF16)
    for parity, ref in enumerate((keep_ref, give_ref)):

        @pl.when(k % 2 == parity)
        def _():
            ref[0, :, 0:width] = g
            ref[0, :, width:] = h


def last_grads_kernel(order_ref, inp_ref, dpre_ref, step_ref, keep_ref, give_ref):
    k = pl.program_id(0)
    cs = step_ref.shape[0]
    width = dpre_ref.shape[0]
    g = nt(inp_ref[...], dpre_ref[...]).astype(BF16)
    for parity, ref in enumerate((keep_ref, give_ref)):

        @pl.when(k % 2 == parity)
        def _():
            ref[0, :, 0:width] = g
            for t in range(4):
                ref[0, t * cs : (t + 1) * cs, width : width + LANES] = step_ref[
                    :, t * LANES : (t + 1) * LANES
                ]


def input_grad_kernel(dp, off_ref, dpre_ref, dres_ref, *refs):
    turned, refs = refs[:dp], refs[dp:]
    base_ref, first_ref, last_ref, wt_ref, w_ref, facc_ref, lacc_ref, sems = refs
    cs = C // dp
    i = pl.program_id(0)
    lane = lane_ids((C, LANES))

    @pl.when(i == 0)
    def _():
        copies = turned_copies(off_ref, turned, cs, wt_ref, sems)
        begin(copies)
        facc_ref[...] = jnp.zeros((C, LANES), F32)
        lacc_ref[...] = jnp.zeros((C, LANES), F32)
        finish(copies)
        for d in range(dp):
            v = wt_ref[:, d * 4 * cs : (d + 1) * 4 * cs].T
            for t in range(3):
                w_ref[t, d * cs : (d + 1) * cs] = v[t * cs : (t + 1) * cs]

    dpre = dpre_ref[...]
    y0 = nn(w_ref[0], dpre)
    y1 = nn(w_ref[1], dpre)
    y2 = nn(w_ref[2], dpre)
    facc = facc_ref[...]
    lacc = lacc_ref[...]
    for j in range(2):
        r = 2 * i + j
        cols = slice(j * LANES, (j + 1) * LANES)
        z0 = pltpu.roll(y0[:, cols], LANES - SHIFT, 1)
        z2 = pltpu.roll(y2[:, cols], SHIFT, 1)
        base_ref[:, cols] = (
            y1[:, cols]
            + jnp.where(lane < LANES - SHIFT, z0, 0.0)
            + jnp.where(lane >= SHIFT, z2, 0.0)
            + dres_ref[:, cols].astype(F32)
        ).astype(BF16)
        here = (lane // SHIFT) == r
        facc = jnp.where(here, pltpu.roll(z0, lax.rem(SHIFT * r + SHIFT, LANES), 1), facc)
        lacc = jnp.where(here, pltpu.roll(z2, SHIFT * r, 1), lacc)
    facc_ref[...] = facc
    lacc_ref[...] = lacc

    @pl.when(i == pl.num_programs(0) - 1)
    def _():
        first_ref[...] = facc.astype(BF16)
        last_ref[...] = lacc.astype(BF16)


def finish_kernel(flags_ref, base_ref, left_ref, right_ref, out_ref):
    i = pl.program_id(0)
    lane = lane_ids((C, LANES))
    left = left_ref[...].astype(F32)
    right = right_ref[...].astype(F32)
    for j in range(2):
        r = 2 * i + j
        cols = slice(j * LANES, (j + 1) * LANES)
        lh = pltpu.roll(left, lax.rem(LANES - SHIFT * r, LANES), 1)
        rh = pltpu.roll(right, LANES - SHIFT - SHIFT * r, 1)
        lh = jnp.where((lane < SHIFT) & (flags_ref[0, r] > 0), lh, 0.0)
        rh = jnp.where((lane >= LANES - SHIFT) & (flags_ref[1, r] > 0), rh, 0.0)
        out_ref[j] = (base_ref[:, cols].astype(F32) + lh + rh).astype(BF16)


def add_blocks_kernel(a_ref, b_ref, keep_ref, give_ref):
    for j in range(a_ref.shape[0]):
        v = a_ref[j].astype(F32) + b_ref[j].astype(F32)
        (keep_ref, give_ref)[j % 2][j // 2] = v.astype(BF16)


def add_halves_kernel(bit_ref, a_ref, b_ref, keep_ref, give_ref, scr):
    half = a_ref.shape[1] // 2
    scr[...] = a_ref[0].astype(F32) + b_ref[0].astype(F32)
    keep_ref[...] = scr[pl.ds(pl.multiple_of(bit_ref[0] * half, 8), half)].astype(BF16)
    give_ref[...] = scr[pl.ds(pl.multiple_of((1 - bit_ref[0]) * half, 8), half)].astype(BF16)


def add_pieces_kernel(a_ref, b_ref, out_ref):
    v = a_ref[...].astype(F32) + b_ref[...].astype(F32)
    size = out_ref.shape[1]
    for p in range(out_ref.shape[0]):
        out_ref[p] = v[p * size : (p + 1) * size].astype(BF16)


def sum_copies_kernel(a_ref, out_ref):
    v = a_ref[0].astype(F32)
    for p in range(1, a_ref.shape[0]):
        v = v + a_ref[p].astype(F32)
    v = v.astype(BF16)
    for p in range(out_ref.shape[0]):
        out_ref[p] = v


def small_sum_kernel(cs, csh, got_ref, film_ref, out_ref, scr, turn):
    v = got_ref[0].astype(F32)
    for d in range(1, got_ref.shape[0]):
        v = v + got_ref[d].astype(F32)
    turn[...] = jnp.zeros(turn.shape, F32)
    turn[0:cs, 0 : 2 * csh] = v[:cs, 192 : 192 + 2 * csh]
    film_ref[...] = turn[...].T[0 : 2 * csh, 0:cs]
    half = cs // 2
    scr[...] = jnp.zeros(scr.shape, F32)
    scr[0:cs] = v[:cs, 0:128]
    scr[cs : cs + half, 0:csh] = v[0:half, 128 : 128 + csh]
    scr[cs : cs + half, csh : 2 * csh] = v[half:cs, 128 : 128 + csh]
    dq = v[cs : cs + QUERIES, 0:64] + v[cs : cs + QUERIES, 64:128]
    hi = dq.astype(BF16).astype(F32)
    scr[cs + half : cs + half + QUERIES, 0:64] = hi
    scr[cs + half : cs + half + QUERIES, 64:128] = dq - hi
    low = scr[...].astype(BF16)
    for p in range(out_ref.shape[0]):
        out_ref[p] = low


def output_kernel(
    cs,
    csh,
    hs,
    bit_ref,
    own1_ref,
    got1_ref,
    own2_ref,
    got2_ref,
    own3_ref,
    got3_ref,
    small_ref,
    queries_ref,
    wq_ref,
    step_ref,
    conv_ref,
    cond_ref,
    res_ref,
    skip_ref,
    gqueries_ref,
    gquery_ref,
    key_ref,
    value_ref,
    attn_ref,
    qscr,
    dq,
):
    half = cs // 2
    bit = bit_ref[0]
    quarter = C // 2

    def taps(at, q, v):
        tap, c = at // cs, at % cs
        rows, cols = slice(c, c + v.shape[0]), slice(q * quarter, (q + 1) * quarter)
        if tap < 3:
            conv_ref[tap, rows, cols] = v
        else:
            cond_ref[rows, cols] = v

    for number, (own, got) in enumerate(
        ((own1_ref, got1_ref), (own2_ref, got2_ref), (own3_ref, got3_ref))
    ):
        count, size = own.shape[0], own.shape[1]
        for p in range(count):
            a, b = own[p].astype(F32), got[p].astype(F32)
            for at, v in (
                (p * size, jnp.where(bit == 0, a, b)),
                ((count + p) * size, jnp.where(bit == 0, b, a)),
            ):
                t, c = at // cs, at % cs
                if number == 0:
                    taps(at, 0, v[:, 0:quarter])
                    ref = res_ref if t < 2 else skip_ref
                    ref[c : c + size, (t % 2) * quarter : (t % 2 + 1) * quarter] = v[:, quarter:]
                elif number == 1:
                    taps(at, 1, v[:, 0:quarter])
                    taps(at, 2, v[:, quarter:])
                else:
                    taps(at, 3, v[:, 0:quarter])
                    step_ref[c : c + size, t * LANES : (t + 1) * LANES] = v[:, quarter:]
    dq[...] = jnp.zeros(dq.shape, F32)
    for head in range(HEADS):
        cols = slice(head * HEAD_DIM, (head + 1) * HEAD_DIM)
        v = small_ref[head * hs].astype(F32)
        for k in range(1, hs):
            v = v + small_ref[head * hs + k].astype(F32)
        key_ref[:, cols] = v[0:cs, 0:64]
        value_ref[:, cols] = v[0:cs, 64:128]
        dq[0:QUERIES, cols] = v[cs + half :, 0:64] + v[cs + half :, 64:128]
    for s in range(small_ref.shape[0]):
        v = small_ref[s, cs : cs + half].astype(F32)
        attn_ref[0:half, s * csh : (s + 1) * csh] = v[:, 0:csh]
        attn_ref[half:cs, s * csh : (s + 1) * csh] = v[:, csh : 2 * csh]
    qscr[...] = jnp.zeros((LANES, LANES), F32)
    qscr[0:QUERIES, 0:cs] = queries_ref[...].astype(F32)
    qt = qscr[...].T.astype(BF16)
    d = dq[...]
    hi = d.astype(BF16)
    lo = (d - hi.astype(F32)).astype(BF16)
    gquery_ref[...] = (nn(qt, hi) + nn(qt, lo))[0:cs]
    gqueries_ref[...] = fold(nt(parts(d[0:QUERIES], 2), wq_ref[...]), 2)


def attention_back_kernel(
    rows, csh, dp, prm_ref, probs_ref, u_ref, qp_ref, qkv_ref, pooled_ref, memory_ref, dfilm_ref, got_ref, out_ref, prow, ds, stack, right
):
    count = prm_ref.shape[0]
    total = count * prm_ref.shape[2]
    cs = C // dp
    wk, wv = qkv_ref[64:128], qkv_ref[128:192]
    datt = got_ref[0, 3 * RP : 4 * RP, 0:HEAD_DIM]
    dmem = got_ref[0, 2 * RP : 3 * RP, 0:csh]
    for s in range(1, count):
        datt = datt + got_ref[s, 3 * RP : 4 * RP, 0:HEAD_DIM]
        dmem = dmem + got_ref[s, 2 * RP : 3 * RP, 0:csh]
    datt = datt * (1.0 / QUERIES)
    for r in range(rows):
        prow[r * total : (r + 1) * total] = prm_ref[:, r].reshape(total, C)
    vh = fold(nn(parts(datt, 2), wv), 2)
    dp_all = fold(nt(parts(vh, 2), prow[...]), 2)
    for r in range(rows):
        cols = slice(r * total, (r + 1) * total)
        p = probs_ref[:, cols]
        dpr = dp_all[r : r + 1, cols]
        inner = jnp.sum(p * dpr, axis=1, keepdims=True)
        ds[:, cols] = p * (dpr - inner)
    tt = fold(nn(parts(ds[...], 2), prow[...]), 2)
    scale = 1.0 / math.sqrt(HEAD_DIM)
    dq = fold(nt(parts(tt, 2), wk), 2) * scale
    stack[...] = jnp.zeros(stack.shape, F32)
    stack[0:QUERIES] = tt
    stack[32:48] = u_ref[...]
    stack[48:64] = pooled_ref[...].astype(F32)
    stack[64:80] = memory_ref[...].astype(F32)
    right[...] = jnp.zeros(right.shape, F32)
    right[0:32, 0:64] = qp_ref[...] * scale
    right[32:48, 64:128] = datt
    right[48:64, 128 : 128 + csh] = dmem
    right[64:80, 192 : 192 + 2 * csh] = dfilm_ref[...].astype(F32)
    grads = lax.dot_general(
        stack[...].T,
        right[...],
        (((1,), (0,)), ((), ())),
        precision=lax.Precision.HIGHEST,
        preferred_element_type=F32,
    ).astype(BF16)
    hi = dq.astype(BF16)
    lo = (dq - hi.astype(F32)).astype(BF16)
    for d in range(dp):
        out_ref[d, 0:cs] = grads[d * cs : (d + 1) * cs]
        out_ref[d, cs : cs + QUERIES] = jnp.zeros((QUERIES, right.shape[1]), BF16)
        out_ref[d, cs : cs + QUERIES, 0:64] = hi
        out_ref[d, cs : cs + QUERIES, 64:128] = lo


def exchange(pieces, axis, groups=None):
    return lax.all_to_all(
        pieces, axis, split_axis=0, concat_axis=0, axis_index_groups=groups, tiled=True
    )


def flipped(v, axis, size, bit):
    return lax.ppermute(v, axis, [(d, d ^ bit) for d in range(size)])


class Reduction:
    def __init__(self, call, keep, give, dp, seq, bit):
        self.call, self.dp, self.seq, self.bit = call, dp, seq, bit
        self.keep, self.flip = keep, 1
        self.rows, self.width = keep.shape[1], keep.shape[2]
        self.got = flipped(give, "dp", dp, 1)

    def over_blocks(self):
        while 2 * self.flip < self.dp:
            half = sds((self.keep.shape[0] // 2,) + self.keep.shape[1:], BF16)
            self.keep, give = self.call(
                add_blocks_kernel,
                (half, half),
                "add_blocks",
                (self.keep, Got(self.got)),
                nbytes=6 * self.keep.size,
                in_specs=[VM, VM],
                out_specs=(VM, VM),
            )
            self.flip *= 2
            self.got = flipped(give, "dp", self.dp, self.flip)

    def over_halves(self):
        half = sds((self.rows // 2, self.width), BF16)
        self.keep, give = self.call(
            add_halves_kernel,
            (half, half),
            "add_halves",
            (self.bit, self.keep, Got(self.got)),
            nbytes=6 * self.keep.size,
            in_specs=[SM, VM, VM],
            out_specs=(VM, VM),
            scratch_shapes=[pltpu.VMEM((self.rows, self.width), F32)],
        )
        self.got = flipped(give, "seq", self.seq, 1)

    def over_pieces(self):
        count = self.seq // 2
        self.groups = [[2 * k + b for k in range(count)] for b in range(2)]
        self.piece = sds((count, self.rows // self.seq, self.width), BF16)
        pieces = self.call(
            add_pieces_kernel,
            self.piece,
            "add_pieces",
            (self.keep, Got(self.got)),
            nbytes=6 * self.keep.size,
            in_specs=[VM, VM],
            out_specs=VM,
        )
        self.got = exchange(pieces, "seq", self.groups)

    def over_copies(self):
        copies = self.call(
            sum_copies_kernel,
            self.piece,
            "sum_copies",
            (Got(self.got),),
            nbytes=4 * self.got.size,
            in_specs=[VM],
            out_specs=VM,
        )
        own = exchange(copies, "seq", self.groups)
        self.result = (Got(own), Got(flipped(own, "seq", self.seq, 1)))


def body(
    dp,
    seq,
    x_in,
    cond,
    segment_ids,
    diffusion_steps,
    prompt,
    prompt_lengths,
    w_step,
    w_conv,
    w_cond,
    w_res,
    w_skip,
    queries,
    w_query,
    w_key,
    w_value,
    w_attn_out,
    w_film,
    d_out,
    d_skip,
):
    call = Chain()
    rows = x_in.shape[0]
    frames = x_in.shape[2]
    steps = rows // 2
    cols = rows * frames
    cs = C // dp
    csh = C // seq
    hs = max(1, seq // HEADS)
    arows = rows // hs
    pl_local = prompt.shape[1]
    prompt_all = pl_local * seq
    sidx = lax.axis_index("seq")
    didx = lax.axis_index("dp")
    head = sidx // hs
    part = sidx % hs
    up = [(i, i + 1) for i in range(seq - 1)]
    down = [(i + 1, i) for i in range(seq - 1)]
    order = jnp.bitwise_xor(didx, jnp.arange(dp, dtype=jnp.int32)).astype(jnp.int32)
    offsets = order * cs
    bit = (sidx % 2).astype(jnp.int32).reshape(1)

    def gather(pack):
        have = {0: pack}
        flip = dp // 2
        while flip:
            for k in sorted(have):
                have[k + flip] = flipped(have[k], "dp", dp, flip)
            flip //= 2
        return [have[k] if k == 0 else Got(have[k]) for k in range(dp)]

    plain = call(
        functools.partial(plain_pack_kernel, cs, csh),
        sds((cs, PLAIN + 2 * C), BF16),
        "plain_pack",
        (
            head.astype(jnp.int32).reshape(1),
            w_res,
            w_skip,
            w_attn_out,
            w_step,
            jnp.transpose(w_film, (1, 2, 0)).reshape(2 * csh, cs),
            w_query,
            w_key,
            w_value,
            queries,
        ),
        nbytes=2e6,
        in_specs=[SM] + [VM] * 9,
        out_specs=VM,
        scratch_shapes=[pltpu.VMEM((2 * LANES, LANES), F32)],
    )
    plain = gather(plain)
    turned = call(
        functools.partial(turned_pack_kernel, cs),
        sds((2 * C, 4 * cs), BF16),
        "turned_pack",
        (w_conv, w_cond),
        nbytes=2e6,
        in_specs=[VM, VM],
        out_specs=VM,
        scratch_shapes=[pltpu.VMEM((4 * cs, 2 * C), BF16)],
    )
    turned = gather(turned)
    first, last, prompts = call(
        functools.partial(edge_kernel, hs),
        (
            sds((C, LANES), BF16),
            sds((C, LANES), BF16),
            sds((seq, arows, pl_local, C), BF16),
        ),
        "edges",
        (x_in, prompt),
        nbytes=4e6,
        in_specs=[VM, VM],
        out_specs=(VM, VM, VM),
    )
    prompts = exchange(prompts, "seq")
    left_halo = lax.ppermute(last, "seq", up)
    right_halo = lax.ppermute(first, "seq", down)

    block_ids = segment_ids[:, ::frames]
    padded_ids = jnp.pad(block_ids, ((0, 0), (1, 1)), constant_values=-1)
    mine = lax.dynamic_slice_in_dim(padded_ids, sidx, 3, 1)
    flags = jnp.stack([mine[:, 0] == mine[:, 1], mine[:, 2] == mine[:, 1]]).astype(jnp.int32)
    block_ids = jnp.pad(block_ids, ((0, RP - rows), (0, 0)))
    half = C // 2
    frequency = jnp.exp(jnp.arange(half, dtype=F32) * (-math.log(10000.0) / half))
    step_rows = jnp.pad(diffusion_steps.astype(F32), (0, LANES - rows))
    live_rows = jnp.arange(LANES, dtype=jnp.int32)[:, None] < rows
    angles = step_rows[:, None] * frequency[None, :]
    embedding = jnp.concatenate([jnp.sin(angles), jnp.cos(angles)], axis=1)
    embedding = jnp.where(live_rows, embedding, 0.0).astype(BF16)
    lengths = lax.dynamic_slice_in_dim(prompt_lengths, part * arows, arows, 0)

    apack, probs, u, pooled_head, qp, qkv = call(
        functools.partial(attention_kernel, arows, dp, 2 * C + 2 * csh),
        (
            sds((C, PLAIN), BF16),
            sds((QUERIES, arows * prompt_all), F32),
            sds((RP, C), F32),
            sds((seq, RP, LANES), F32),
            sds((QUERIES, HEAD_DIM), F32),
            sds((256, C), BF16),
        ),
        "attention",
        (offsets, lengths, Got(prompts), *plain),
        flops=2 * 160 * 1536 * 512,
        nbytes=4e6,
        in_specs=[SM, SM, VM] + [HB] * dp,
        out_specs=(VM,) * 6,
        scratch_shapes=[
            pltpu.VMEM((arows * prompt_all, C), BF16),
            pltpu.VMEM((RP, arows * prompt_all), F32),
            pltpu.SemaphoreType.DMA((dp,)),
        ],
    )
    pooled_got = exchange(pooled_head, "seq")

    row_block = pl.BlockSpec((2, C, LANES), lambda i: (i, 0, 0))

    def col_block(height):
        return pl.BlockSpec((height, 2 * LANES), lambda i: (0, i))

    def still(shape):
        return pl.BlockSpec(shape, lambda i: (0,) * len(shape))

    inp, gated, tanh_part, sig_part, skip_out, mid, stats = call(
        functools.partial(forward_kernel, dp, csh),
        (
            sds((4 * C, cols), BF16),
            sds((C, cols), BF16),
            sds((C, cols), F32),
            sds((C, cols), F32),
            sds(x_in.shape, BF16),
            sds((C, cols), BF16),
            sds((seq, 2 * RP, 2 * csh), F32),
        ),
        "wavenet",
        (
            offsets,
            flags,
            x_in,
            cond,
            d_out,
            Got(left_halo),
            Got(right_halo),
            embedding,
            *turned,
            *plain,
        ),
        flops=2 * cols * (4 * C * 2 * C + 2 * C * C),
        nbytes=30e6,
        grid=(steps,),
        in_specs=[
            SM,
            SM,
            row_block,
            row_block,
            row_block,
            whole((C, LANES)),
            whole((C, LANES)),
            whole((LANES, C)),
        ]
        + [HB] * (2 * dp),
        out_specs=(
            col_block(4 * C),
            col_block(C),
            col_block(C),
            col_block(C),
            row_block,
            col_block(C),
            still((seq, 2 * RP, 2 * csh)),
        ),
        scratch_shapes=[
            pltpu.VMEM((2 * C, 4 * C), BF16),
            pltpu.VMEM((C, 2 * C), BF16),
            pltpu.VMEM((C, C), BF16),
            pltpu.VMEM((2 * C, C), BF16),
            pltpu.VMEM((C, LANES), F32),
            pltpu.VMEM((C, LANES), F32),
            pltpu.SemaphoreType.DMA((3 * dp,)),
        ],
    )
    stats_got = exchange(stats, "seq")
    pooled, memory, film = call(
        functools.partial(memory_kernel, csh, hs, arows),
        (sds((RP, C), BF16), sds((RP, C), BF16), sds((RP, 2 * csh), F32)),
        "memory",
        (Got(pooled_got), apack),
        nbytes=2e6,
        in_specs=[VM, VM],
        out_specs=(VM, VM, VM),
        scratch_shapes=[pltpu.VMEM((RP, C), F32)],
    )

    coef_out, dfilm = call(
        functools.partial(stats_kernel, csh, hs, arows),
        (sds((seq, 4 * RP, 2 * csh), F32), sds((RP, 2 * csh), BF16)),
        "segments",
        (block_ids, Got(stats_got), film, apack),
        nbytes=2e6,
        in_specs=[VM, VM, VM, VM],
        out_specs=(VM, VM),
    )
    coef = Got(exchange(coef_out, "seq"))

    layer_out, dpre, dres, sums = call(
        functools.partial(gate_kernel, dp, csh),
        (
            sds(x_in.shape, BF16),
            sds((2 * C, cols), BF16),
            sds((2 * C, cols), BF16),
            sds((2 * C, LANES), F32),
        ),
        "gate_back",
        (offsets, flags, coef, mid, d_out, d_skip, tanh_part, sig_part, *plain),
        flops=2 * cols * 2 * C * C,
        nbytes=20e6,
        grid=(steps,),
        in_specs=[
            SM,
            SM,
            whole((seq, 4 * RP, 2 * csh)),
            col_block(C),
            row_block,
            row_block,
            col_block(C),
            col_block(C),
        ]
        + [HB] * dp,
        out_specs=(
            row_block,
            col_block(2 * C),
            col_block(2 * C),
            still((2 * C, LANES)),
        ),
        scratch_shapes=[
            pltpu.VMEM((LANES, C), F32),
            pltpu.VMEM((C, LANES), F32),
            pltpu.VMEM((C, 2 * C), BF16),
            pltpu.SemaphoreType.DMA((dp,)),
        ],
    )

    def grads(kernel, name, width, args, in_specs, share):
        out = sds((dp // 2, 4 * cs, width), BF16)
        spec = pl.BlockSpec((1, 4 * cs, width), lambda k, order: (k // 2, 0, 0))
        keep, give = call(
            kernel,
            (out, out),
            name,
            (order, inp) + args,
            flops=2 * cols * share * C * 2 * C,
            nbytes=10e6,
            prefetch=1,
            grid=(dp,),
            in_specs=[pl.BlockSpec((4 * cs, cols), lambda k, order: (order[k], 0))] + in_specs,
            out_specs=(spec, spec),
        )
        return Reduction(call, keep, give, dp, seq, bit)

    def rows_at(height, at):
        return pl.BlockSpec(
            (height, cols), lambda k, order: (at, 0), pipeline_mode=pl.Buffered(1)
        )

    part1 = grads(
        first_grads_kernel,
        "first_grads",
        C,
        (dpre, gated, dres),
        [
            rows_at(C // 2, 0),
            pl.BlockSpec((cs, cols), lambda k, order: (order[k], 0)),
            rows_at(2 * C, 0),
        ],
        2,
    )

    small = call(
        functools.partial(attention_back_kernel, arows, csh, dp),
        sds((dp, cs + QUERIES, 384), BF16),
        "attention_back",
        (Got(prompts), probs, u, qp, qkv, pooled, memory, dfilm, coef),
        flops=2 * 200 * 1536 * 512,
        nbytes=4e6,
        in_specs=[VM] * 9,
        out_specs=VM,
        scratch_shapes=[
            pltpu.VMEM((arows * prompt_all, C), BF16),
            pltpu.VMEM((QUERIES, arows * prompt_all), F32),
            pltpu.VMEM((LANES, C), F32),
            pltpu.VMEM((LANES, 384), F32),
        ],
    )
    small = exchange(small, "dp")
    part1.over_blocks()
    part2 = grads(middle_grads_kernel, "middle_grads", C, (dpre, dpre), [rows_at(C // 2, 1), rows_at(C // 2, 2)], 2)
    small_rows = cs + cs // 2 + QUERIES
    grad_film, small = call(
        functools.partial(small_sum_kernel, cs, csh),
        (sds((2 * csh, cs), F32), sds((seq, small_rows, LANES), BF16)),
        "small_sum",
        (Got(small),),
        nbytes=1e6,
        in_specs=[VM],
        out_specs=(VM, VM),
        scratch_shapes=[pltpu.VMEM((small_rows, LANES), F32), pltpu.VMEM((LANES, LANES), F32)],
    )
    small = Got(exchange(small, "seq"))
    part2.over_blocks()
    gstep = call(
        functools.partial(step_grad_kernel, dp),
        sds((C, C), BF16),
        "step_grad",
        (offsets, sums, embedding, *turned),
        nbytes=5e6,
        in_specs=[SM, VM, VM] + [HB] * dp,
        out_specs=VM,
        scratch_shapes=[pltpu.VMEM((2 * C, 4 * C), BF16), pltpu.SemaphoreType.DMA((dp,))],
    )
    part3 = grads(
        last_grads_kernel,
        "last_grads",
        C // 2 + LANES,
        (dpre, gstep),
        [rows_at(C // 2, 3), pl.BlockSpec((cs, C), lambda k, order: (order[k], 0))],
        1,
    )
    part1.over_halves()
    part3.over_blocks()

    base, first, last = call(
        functools.partial(input_grad_kernel, dp),
        (sds((C, cols), BF16), sds((C, LANES), BF16), sds((C, LANES), BF16)),
        "input_grad",
        (offsets, dpre, dres, *turned),
        flops=2 * cols * 6 * C * C,
        nbytes=10e6,
        grid=(steps,),
        in_specs=[SM, col_block(2 * C), col_block(C)] + [HB] * dp,
        out_specs=(
            col_block(C),
            still((C, LANES)),
            still((C, LANES)),
        ),
        scratch_shapes=[
            pltpu.VMEM((2 * C, 4 * C), BF16),
            pltpu.VMEM((3, C, 2 * C), BF16),
            pltpu.VMEM((C, LANES), F32),
            pltpu.VMEM((C, LANES), F32),
            pltpu.SemaphoreType.DMA((dp,)),
        ],
    )
    from_left = lax.ppermute(last, "seq", up)
    from_right = lax.ppermute(first, "seq", down)
    part1.over_pieces()
    part2.over_halves()
    part1.over_copies()
    grad_input = call(
        finish_kernel,
        sds(x_in.shape, BF16),
        "grad_input",
        (flags, base, Got(from_left), Got(from_right)),
        nbytes=4e6,
        grid=(steps,),
        in_specs=[SM, col_block(C), whole((C, LANES)), whole((C, LANES))],
        out_specs=row_block,
    )
    part2.over_pieces()
    part3.over_halves()
    part2.over_copies()
    part3.over_pieces()
    part3.over_copies()

    (
        grad_step,
        grad_conv,
        grad_cond,
        grad_res,
        grad_skip,
        grad_queries,
        grad_query,
        grad_key,
        grad_value,
        grad_attn,
    ) = call(
        functools.partial(output_kernel, cs, csh, hs),
        (
            sds((cs, C), F32),
            sds((3, cs, 2 * C), F32),
            sds((cs, 2 * C), F32),
            sds((cs, C), F32),
            sds((cs, C), F32),
            sds((QUERIES, cs), F32),
            sds((cs, C), F32),
            sds((cs, C), F32),
            sds((cs, C), F32),
            sds((cs, C), F32),
        ),
        "outputs",
        (bit, *part1.result, *part2.result, *part3.result, small, queries, w_query),
        nbytes=8e6,
        in_specs=[SM] + [VM] * 9,
        out_specs=(VM,) * 10,
        scratch_shapes=[
            pltpu.VMEM((LANES, LANES), F32),
            pltpu.VMEM((LANES, C), F32),
        ],
    )
    return (
        layer_out,
        skip_out,
        grad_input,
        grad_step,
        grad_conv,
        grad_cond,
        grad_res,
        grad_skip,
        grad_queries,
        grad_query,
        grad_key,
        grad_value,
        grad_attn,
        jnp.transpose(grad_film.reshape(2, csh, cs), (2, 0, 1)),
    )


def solution(mesh):
    frames = P("dp", None, "seq")
    matrix = P("dp", None)
    return jax.shard_map(
        functools.partial(body, mesh.shape["dp"], mesh.shape["seq"]),
        mesh=mesh,
        in_specs=(
            frames,
            frames,
            P("dp", None),
            P("dp"),
            P("dp", "seq", None),
            P("dp"),
            matrix,
            P(None, "dp", None),
            matrix,
            matrix,
            matrix,
            P(None, "dp"),
            matrix,
            matrix,
            matrix,
            matrix,
            frames,
            frames,
            frames,
        ),
        out_specs=(
            frames,
            frames,
            frames,
            matrix,
            P(None, "dp", None),
            matrix,
            matrix,
            matrix,
            P(None, "dp"),
            matrix,
            matrix,
            matrix,
            matrix,
            frames,
        ),
        check_vma=False,
    )
```

```python
import functools
import math

import jax
import jax.numpy as jnp
from jax import lax
from jax.experimental import pallas as pl
from jax.experimental.pallas import tpu as pltpu
from jax.sharding import PartitionSpec as P

C = 512
HEADS = 8
QUERIES = 32
HEAD_DIM = 64
SHIFT = 4
SQRT_HALF = 0.7071067811865476
NORM_EPS = 1e-05
MASKED_SCORE = -1e30
LANES = 128
RP = 16
NR = 4
F32 = jnp.float32
BF16 = jnp.bfloat16
VMEM_BYTES = 50 * 1024 * 1024


def nn(a, b):
    return lax.dot_general(a, b, (((1,), (0,)), ((), ())), preferred_element_type=F32)


def nt(a, b):
    return lax.dot_general(a, b, (((1,), (1,)), ((), ())), preferred_element_type=F32)


def parts(v, count):
    out = []
    for _ in range(count):
        low = v.astype(BF16)
        out.append(low)
        v = v - low.astype(F32)
    return jnp.concatenate(out, axis=0)


def fold(v, count):
    rows = v.shape[0] // count
    total = v[:rows]
    for k in range(1, count):
        total = total + v[k * rows : (k + 1) * rows]
    return total


def lane_ids(shape):
    return lax.broadcasted_iota(jnp.int32, shape, len(shape) - 1)


def sds(shape, dtype):
    return jax.ShapeDtypeStruct(shape, dtype)


VM = pl.BlockSpec(memory_space=pltpu.VMEM)
HB = pl.BlockSpec(memory_space=pl.ANY)
SM = pl.BlockSpec(memory_space=pltpu.SMEM)


def whole(shape):
    return pl.BlockSpec(shape, lambda i: (0,) * len(shape), pipeline_mode=pl.Buffered(1))


class Got:
    def __init__(self, array):
        self.array = array


class Caller:
    def __init__(self):
        self.done = {}

    def __call__(self, kernel, out_shape, name, args, flops=0, nbytes=0, prefetch=0, after=(), **kw):
        single = not isinstance(out_shape, tuple)
        shapes = (out_shape,) if single else out_shape
        pinned = tuple(pltpu.HBM(v.shape, v.dtype) for v in shapes)
        in_specs = list(kw.pop("in_specs"))
        count = prefetch + len(in_specs)
        args = list(args)
        extra = len(after)
        for before in after:
            in_specs.append(HB)
            args.append(self.done[before])

        def run(*refs):
            return kernel(*refs[:count], *refs[count + extra :])

        values = []
        for k, v in enumerate(args):
            spec = SM if k < prefetch else in_specs[k - prefetch]
            if isinstance(v, Got):
                values.append(v.array)
            elif spec is SM:
                values.append(v)
            else:
                values.append(pltpu.with_memory_space_constraint(v, pltpu.HBM))
        spec = pltpu.PrefetchScalarGridSpec(
            num_scalar_prefetch=prefetch,
            grid=kw.pop("grid", ()),
            in_specs=in_specs,
            out_specs=kw.pop("out_specs"),
            scratch_shapes=kw.pop("scratch_shapes", ()),
        )
        out = pl.pallas_call(
            run,
            out_shape=pinned[0] if single else pinned,
            name=name,
            grid_spec=spec,
            cost_estimate=pl.CostEstimate(
                flops=1, bytes_accessed=1, transcendentals=0
            ),
            compiler_params=pltpu.CompilerParams(vmem_limit_bytes=VMEM_BYTES),
        )(*values)
        self.done[name] = out if single else out[0]
        return out


PLAIN = 1408


def plain_pack_kernel(cs, csh, head_ref, res_ref, skip_ref, attn_ref, step_ref, film_ref, wq_ref, wk_ref, wv_ref, queries_ref, out_ref, scr):
    out_ref[:, 0:C] = attn_ref[...]
    out_ref[:, C : 2 * C] = step_ref[...]
    off = 2 * C
    scr[...] = jnp.zeros((2 * LANES, LANES), F32)
    scr[0 : 2 * csh, 0:cs] = film_ref[...].astype(F32)
    scr[LANES : LANES + QUERIES, 0:cs] = queries_ref[...].astype(F32)
    film = scr[0:LANES].T[0:cs]
    table = scr[LANES : 2 * LANES].T[0:cs]
    turn = lax.rem(C - HEAD_DIM * head_ref[0], C)
    blocks = [film[:, 0 : 2 * csh]]
    for ref in (wq_ref, wk_ref, wv_ref):
        blocks.append(pltpu.roll(ref[...].astype(F32), turn, 1)[:, 0:HEAD_DIM])
    blocks.append(table[:, 0 : PLAIN - off - 2 * csh - 3 * HEAD_DIM])
    for block in blocks:
        out_ref[:, off : off + block.shape[1]] = block.astype(BF16)
        off += block.shape[1]
    out_ref[:, PLAIN : PLAIN + C] = res_ref[...]
    out_ref[:, PLAIN + C : PLAIN + 2 * C] = skip_ref[...]


def turned_pack_kernel(cs, conv_ref, cond_ref, out_ref, scr):
    for k in range(3):
        scr[k * cs : (k + 1) * cs] = conv_ref[k]
    scr[3 * cs : 4 * cs] = cond_ref[...]
    out_ref[...] = scr[...].T


def edge_kernel(hs, x_ref, prompt_ref, first_ref, last_ref, copies_ref):
    rows = x_ref.shape[0]
    arows = copies_ref.shape[1]
    for s in range(copies_ref.shape[0]):
        part = s % hs
        copies_ref[s] = prompt_ref[part * arows : (part + 1) * arows]
    lane = lane_ids((C, LANES))
    first = jnp.zeros((C, LANES), F32)
    last = jnp.zeros((C, LANES), F32)
    for r in range(rows):
        v = x_ref[r].astype(F32)
        here = (lane // SHIFT) == r
        first = jnp.where(here, pltpu.roll(v, SHIFT * r, 1) if r else v, first)
        last = jnp.where(here, pltpu.roll(v, SHIFT * r + SHIFT, 1), last)
    first_ref[...] = first.astype(BF16)
    last_ref[...] = last.astype(BF16)


def copies_of(pieces, make):
    return [pltpu.make_async_copy(*make(k, piece)) for k, piece in enumerate(pieces)]


def begin(copies):
    for copy in copies:
        copy.start()


def finish(copies):
    for copy in copies:
        copy.wait()


def turned_copies(off_ref, turned, cs, dst, sems, base=0):
    def make(k, piece):
        lane = pl.multiple_of(off_ref[k] * 4, LANES)
        return piece, dst.at[:, pl.ds(lane, 4 * cs)], sems.at[base + k]

    return copies_of(turned, make)


def plain_copies(off_ref, plain, cs, lanes, width, dst, sems, base=0):
    def make(k, piece):
        row = pl.multiple_of(off_ref[k], 16)
        return piece.at[:, pl.ds(lanes, width)], dst.at[pl.ds(row, cs)], sems.at[base + k]

    return copies_of(plain, make)


def forward_kernel(dp, csh, off_ref, flags_ref, x_ref, cond_ref, dout_ref, left_ref, right_ref, emb_ref, *refs):
    turned, plain, refs = refs[:dp], refs[dp : 2 * dp], refs[2 * dp :]
    (
        inp_ref,
        gated_ref,
        fa_ref,
        fb_ref,
        skip_ref,
        mid_ref,
        stats_ref,
        wt_ref,
        rn_ref,
        step_ref,
        rst_ref,
        lift_ref,
        acc_ref,
        sems,
    ) = refs
    cs = C // dp
    i = pl.program_id(0)
    lane = lane_ids((C, LANES))

    @pl.when(i == 0)
    def _():
        steps = plain_copies(off_ref, plain, cs, C, C, step_ref, sems)
        outs = plain_copies(off_ref, plain, cs, PLAIN, 2 * C, rn_ref, sems, dp)
        convs = turned_copies(off_ref, turned, cs, wt_ref, sems, 2 * dp)
        begin(steps + outs + convs)
        acc_ref[...] = jnp.zeros((C, LANES), F32)
        finish(steps)
        lift = nn(emb_ref[0:RP], step_ref[...])
        lift = jnp.concatenate([lift, jnp.zeros((LANES - RP, C), F32)], axis=0)
        lift_ref[...] = lift.T
        finish(outs)
        rst_ref[...] = rn_ref[...].T
        finish(convs)

    lift = pltpu.roll(lift_ref[...], lax.rem(LANES - NR * i, LANES), 1)
    left = left_ref[...].astype(F32)
    right = right_ref[...].astype(F32)

    def put(tap, cols, value):
        for d in range(dp):
            at = d * 4 * cs + tap * cs
            inp_ref[at : at + cs, cols] = value[d * cs : (d + 1) * cs]

    for j in range(NR):
        r = NR * i + j
        lc = lift[:, j : j + 1]
        sh = (x_ref[j].astype(F32) + lc).astype(BF16)
        shf = sh.astype(F32)
        lh = pltpu.roll(left, lax.rem(LANES - SHIFT * r, LANES), 1)
        lh = jnp.where(flags_ref[0, r] > 0, (lh + lc).astype(BF16).astype(F32), 0.0)
        rh = pltpu.roll(right, LANES - SHIFT - SHIFT * r, 1)
        rh = jnp.where(flags_ref[1, r] > 0, (rh + lc).astype(BF16).astype(F32), 0.0)
        cols = slice(j * LANES, (j + 1) * LANES)
        put(0, cols, jnp.where(lane < SHIFT, lh, pltpu.roll(shf, SHIFT, 1)).astype(BF16))
        put(1, cols, sh)
        put(
            2,
            cols,
            jnp.where(lane >= LANES - SHIFT, rh, pltpu.roll(shf, LANES - SHIFT, 1)).astype(BF16),
        )
        put(3, cols, cond_ref[j])
    pre = nn(wt_ref[...], inp_ref[...])
    th = jnp.tanh(pre[:C])
    sg = jax.nn.sigmoid(pre[C:])
    gf = th * sg
    fa_ref[...] = (sg - gf * th).astype(BF16)
    fb_ref[...] = (gf * (1.0 - sg)).astype(BF16)
    g = gf.astype(BF16)
    gated_ref[...] = g
    rs = nn(rst_ref[...], g)
    acc = acc_ref[...]
    for j in range(NR):
        r = NR * i + j
        cols = slice(j * LANES, (j + 1) * LANES)
        skip_ref[j] = rs[C:, cols].astype(BF16)
        mid = ((x_ref[j].astype(F32) + rs[:C, cols]) * SQRT_HALF).astype(BF16)
        mid_ref[:, cols] = mid
        mf = mid.astype(F32)
        df = dout_ref[j].astype(F32)
        total = jnp.sum(mf, axis=1, keepdims=True)
        dev = mf - total * (1.0 / LANES)
        acc = jnp.where(lane == r, total, acc)
        acc = jnp.where(lane == RP + r, jnp.sum(dev * dev, axis=1, keepdims=True), acc)
        acc = jnp.where(lane == 2 * RP + r, jnp.sum(df, axis=1, keepdims=True), acc)
        acc = jnp.where(lane == 3 * RP + r, jnp.sum(df * dev, axis=1, keepdims=True), acc)
    acc_ref[...] = acc

    @pl.when(i == pl.num_programs(0) - 1)
    def _():
        t = acc.T
        for s in range(C // csh):
            cols = slice(s * csh, (s + 1) * csh)
            stats_ref[s, :, 0:csh] = t[0 : 2 * RP, cols]
            stats_ref[s, :, csh : 2 * csh] = t[2 * RP : 4 * RP, cols]


def attention_kernel(rows, dp, off, off_ref, len_ref, prm_ref, *refs):
    pieces, refs = refs[:dp], refs[dp:]
    apack_ref, probs_ref, u_ref, pooled_ref, qp_ref, qkv_ref, prow, abd, sems = refs
    cs = C // dp
    copies = plain_copies(off_ref, pieces, cs, 0, PLAIN, apack_ref, sems)
    begin(copies)
    total = prm_ref.shape[0] * prm_ref.shape[2]
    for r in range(rows):
        prow[r * total : (r + 1) * total] = prm_ref[:, r].reshape(total, C)
    abd[...] = jnp.zeros(abd.shape, F32)
    finish(copies)
    qkv = apack_ref[:, off : off + 256].T
    qkv_ref[...] = qkv
    wq, wk, wv = qkv[0:64], qkv[64:128], qkv[128:192]
    qp = nt(qkv[192:224], wq)
    qp_ref[...] = qp
    st = fold(nn(parts(qp, 3), wk), 3) * (1.0 / math.sqrt(HEAD_DIM))
    scores = fold(nt(parts(st, 3), prow[...]), 3)
    for r in range(rows):
        cols = slice(r * total, (r + 1) * total)
        live = lane_ids((QUERIES, total)) < len_ref[r]
        s = jnp.where(live, scores[:, cols], MASKED_SCORE)
        e = jnp.where(live, jnp.exp(s - jnp.max(s, axis=1, keepdims=True)), 0.0)
        p = e / jnp.sum(e, axis=1, keepdims=True)
        probs_ref[:, cols] = p
        abd[r : r + 1, cols] = jnp.sum(p, axis=0, keepdims=True)
    u = fold(nn(parts(abd[...], 2), prow[...]), 2)
    u_ref[...] = u
    pooled = fold(nt(parts(u * (1.0 / QUERIES), 2), wv), 2)
    for s in range(pooled_ref.shape[0]):
        pooled_ref[s, :, 0:HEAD_DIM] = pooled
        pooled_ref[s, :, HEAD_DIM:] = jnp.zeros(pooled.shape, F32)


def memory_kernel(csh, hs, rows, got_ref, apack_ref, pooled_ref, memory_ref, film_ref, scratch):
    scratch[...] = jnp.zeros(scratch.shape, F32)
    for s in range(got_ref.shape[0]):
        head, part = s // hs, s % hs
        scratch[part * rows : (part + 1) * rows, head * HEAD_DIM : (head + 1) * HEAD_DIM] = got_ref[
            s, 0:rows, 0:HEAD_DIM
        ]
    pooled = scratch[...].astype(BF16)
    pooled_ref[...] = pooled
    memory = nn(pooled, apack_ref[:, 0:C]).astype(BF16)
    memory_ref[...] = memory
    film_ref[...] = nn(memory, apack_ref[:, 2 * C : 2 * C + 2 * csh])


def stats_kernel(csh, hs, rows, seg_ref, x_ref, film_ref, apack_ref, out_ref, dfilm_ref):
    count = x_ref.shape[0]
    seg = seg_ref[...]
    f0 = film_ref[:, 0:csh]
    f1 = film_ref[:, csh : 2 * csh]
    total = [x_ref[s, 0:RP, 0:csh] for s in range(count)]
    second = [x_ref[s, RP : 2 * RP, 0:csh] for s in range(count)]
    dsum = [x_ref[s, 0:RP, csh : 2 * csh] for s in range(count)]
    cross = [x_ref[s, RP : 2 * RP, csh : 2 * csh] for s in range(count)]
    means = [v * (1.0 / LANES) for v in total]
    d0 = jnp.zeros((RP, csh), F32)
    d1 = jnp.zeros((RP, csh), F32)
    for me in range(count):
        same = [(seg[:, s : s + 1] == seg[:, me : me + 1]).astype(F32) for s in range(count)]
        frames = sum(same) * float(LANES)
        inv = 1.0 / frames
        mean = sum(m * v for m, v in zip(same, total)) * inv
        var = (
            sum(
                m * (v + float(LANES) * (u - mean) * (u - mean))
                for m, v, u in zip(same, second, means)
            )
            * inv
        )
        scale = lax.rsqrt(var + NORM_EPS)
        dtot = sum(m * v for m, v in zip(same, dsum))
        xtot = sum(m * (v + (u - mean) * d) for m, v, u, d in zip(same, cross, means, dsum)) * scale
        mean_part = f0 * dtot * inv
        cross_part = f0 * xtot * inv
        slope = scale * scale * cross_part
        out_ref[me, 0:RP, 0:csh] = 1.0 + f0 * scale
        out_ref[me, RP : 2 * RP, 0:csh] = f1 - f0 * scale * mean
        out_ref[me, 0:RP, csh : 2 * csh] = -slope
        out_ref[me, RP : 2 * RP, csh : 2 * csh] = slope * mean - scale * mean_part
        d0 = d0 + (cross[me] + (means[me] - mean) * dsum[me]) * scale
        d1 = d1 + dsum[me]
    dfilm = jnp.concatenate([d0, d1], axis=1).astype(BF16)
    dfilm_ref[...] = dfilm
    dmem = nt(dfilm, apack_ref[:, 2 * C : 2 * C + 2 * csh])
    dpool = nt(dmem.astype(BF16), apack_ref[:, 0:C])
    for s in range(count):
        head, part = s // hs, s % hs
        rolled = pltpu.roll(dpool, RP - part * rows, 0) if part else dpool
        out_ref[s, 2 * RP : 3 * RP, 0:csh] = dmem[:, s * csh : (s + 1) * csh]
        out_ref[s, 2 * RP : 3 * RP, csh : 2 * csh] = jnp.zeros((RP, csh), F32)
        out_ref[s, 3 * RP : 4 * RP, 0:HEAD_DIM] = rolled[:, head * HEAD_DIM : (head + 1) * HEAD_DIM]
        if 2 * csh > HEAD_DIM:
            out_ref[s, 3 * RP : 4 * RP, HEAD_DIM : 2 * csh] = jnp.zeros(
                (RP, 2 * csh - HEAD_DIM), F32
            )


def coef_columns(csh, coef_ref, rows_ref, cols_ref):
    rows_ref[...] = jnp.zeros(rows_ref.shape, F32)
    for s in range(C // csh):
        cols = slice(s * csh, (s + 1) * csh)
        rows_ref[0 : 2 * RP, cols] = coef_ref[s, 0 : 2 * RP, 0:csh]
        rows_ref[2 * RP : 4 * RP, cols] = coef_ref[s, 0 : 2 * RP, csh : 2 * csh]
    cols_ref[...] = rows_ref[...].T


def skip_grad_kernel(dp, off_ref, gated_ref, dskip_ref, keep_ref, give_ref, right, scr):
    cs = C // dp
    for r in range(dskip_ref.shape[0]):
        right[:, r * LANES : (r + 1) * LANES] = dskip_ref[r]
    scr[...] = nt(gated_ref[...], right[...])
    for k in range(dp):
        v = scr[pl.ds(pl.multiple_of(off_ref[k], 16), cs)].astype(BF16)
        for t in range(4):
            (keep_ref, give_ref)[k % 2][k // 2, t * cs : (t + 1) * cs] = v[
                :, t * LANES : (t + 1) * LANES
            ]


def backward_kernel(dp, csh, gates, order_ref, off_ref, coef_ref, mid_ref, dout_ref, dskip_ref, fa_ref, fb_ref, inp_ref, gated_ref, *refs):
    plain, refs = refs[:dp], refs[dp:]
    dpre_ref, dres_ref, refs = refs[0], refs[1], refs[2:]
    outs, refs = (refs[0:3], refs[3:6]), refs[6:]
    rows_ref, cols_ref, w_ref, both_ref, dpt_ref, drt_ref, sems = refs
    cs = C // dp
    span = NR * LANES
    i = pl.program_id(0)

    @pl.when(i == 0)
    def _():
        copies = plain_copies(off_ref, plain, cs, PLAIN, 2 * C, w_ref, sems)
        begin(copies)
        coef_columns(csh, coef_ref, rows_ref, cols_ref)
        finish(copies)

    @pl.when(i < gates)
    def _():
        coef = pltpu.roll(cols_ref[...], lax.rem(LANES - NR * i, LANES), 1)
        for j in range(NR):
            cols = slice(j * LANES, (j + 1) * LANES)
            mf = mid_ref[:, cols].astype(F32)
            df = dout_ref[j].astype(F32)
            a = coef[:, j : j + 1]
            be = coef[:, 2 * RP + j : 2 * RP + j + 1]
            ga = coef[:, 3 * RP + j : 3 * RP + j + 1]
            dmid = (a * df + (be * mf + ga)).astype(BF16).astype(F32)
            both_ref[0:C, cols] = (dmid * SQRT_HALF).astype(BF16)
            both_ref[C : 2 * C, cols] = dskip_ref[j]
        dres = both_ref[0:C]
        dres_ref[...] = dres
        dg = nn(w_ref[...], both_ref[...])
        dt = (dg * fa_ref[...].astype(F32)).astype(BF16)
        ds = (dg * fb_ref[...].astype(F32)).astype(BF16)
        dpre_ref[0:C] = dt
        dpre_ref[C : 2 * C] = ds
        at = pl.ds(pl.multiple_of(i * span, span), span)
        dpt_ref[at, 0:C] = dt.T
        dpt_ref[at, C : 2 * C] = ds.T
        drt_ref[at] = dres.T

    @pl.when(i >= gates)
    def _():
        g = nn(inp_ref[...], dpt_ref[...]).astype(BF16)
        h = nn(gated_ref[...], drt_ref[...]).astype(BF16)
        k = i - gates
        for parity, (one, two, three) in enumerate(outs):

            @pl.when(lax.rem(k, 2) == parity)
            def _():
                for t in range(4):
                    one[0, t * cs : (t + 1) * cs, 0:LANES] = h[:, t * LANES : (t + 1) * LANES]
                one[0, :, LANES : 3 * LANES] = g[:, 0 : 2 * LANES]
                two[0] = g[:, 2 * LANES : 5 * LANES]
                three[0] = g[:, 5 * LANES : 8 * LANES]


def input_grad_kernel(dp, csh, off_ref, flags_ref, dpre_ref, dres_ref, *refs):
    turned, refs = refs[:dp], refs[dp:]
    base_ref, first_ref, last_ref, sums_ref, wt_ref, w_ref, facc_ref, lacc_ref, gacc_ref, sems = refs
    cs = C // dp
    i = pl.program_id(0)
    lane = lane_ids((C, LANES))

    @pl.when(i == 0)
    def _():
        copies = turned_copies(off_ref, turned, cs, wt_ref, sems)
        begin(copies)
        facc_ref[...] = jnp.zeros((C, LANES), F32)
        lacc_ref[...] = jnp.zeros((C, LANES), F32)
        gacc_ref[...] = jnp.zeros((C, LANES), F32)
        finish(copies)
        for d in range(dp):
            v = wt_ref[:, d * 4 * cs : (d + 1) * 4 * cs].T
            for t in range(3):
                w_ref[t, d * cs : (d + 1) * cs] = v[t * cs : (t + 1) * cs]

    dpre = dpre_ref[...]
    y0 = nn(w_ref[0], dpre)
    y1 = nn(w_ref[1], dpre)
    y2 = nn(w_ref[2], dpre)
    facc = facc_ref[...]
    lacc = lacc_ref[...]
    gacc = gacc_ref[...]
    for j in range(NR):
        r = NR * i + j
        cols = slice(j * LANES, (j + 1) * LANES)
        z0 = pltpu.roll(y0[:, cols], LANES - SHIFT, 1)
        z2 = pltpu.roll(y2[:, cols], SHIFT, 1)
        inner0 = lane < LANES - SHIFT
        inner2 = lane >= SHIFT
        v = y1[:, cols]
        base_ref[:, cols] = (
            v
            + jnp.where(inner0, z0, 0.0)
            + jnp.where(inner2, z2, 0.0)
            + dres_ref[:, cols].astype(F32)
        ).astype(BF16)
        sent0 = inner0 | (flags_ref[0, r] > 0)
        sent2 = inner2 | (flags_ref[1, r] > 0)
        v = v + jnp.where(sent0, z0, 0.0) + jnp.where(sent2, z2, 0.0)
        gacc = jnp.where(lane == r, jnp.sum(v, axis=1, keepdims=True), gacc)
        here = (lane // SHIFT) == r
        facc = jnp.where(here, pltpu.roll(z0, lax.rem(SHIFT * r + SHIFT, LANES), 1), facc)
        lacc = jnp.where(here, pltpu.roll(z2, SHIFT * r, 1), lacc)
    facc_ref[...] = facc
    lacc_ref[...] = lacc
    gacc_ref[...] = gacc

    @pl.when(i == pl.num_programs(0) - 1)
    def _():
        first_ref[...] = facc.astype(BF16)
        last_ref[...] = lacc.astype(BF16)
        total = gacc.T[0:RP]
        sums_ref[...] = jnp.zeros(sums_ref.shape, F32)
        for s in range(C // csh):
            sums_ref[s, :, 0:csh] = total[:, s * csh : (s + 1) * csh]


def finish_kernel(csh, flags_ref, base_ref, left_ref, right_ref, mid_ref, coef_ref, out_ref, layer_ref, rows_ref, cols_ref):
    i = pl.program_id(0)
    lane = lane_ids((C, LANES))

    @pl.when(i == 0)
    def _():
        coef_columns(csh, coef_ref, rows_ref, cols_ref)

    coef = pltpu.roll(cols_ref[...], lax.rem(LANES - NR * i, LANES), 1)
    left = left_ref[...].astype(F32)
    right = right_ref[...].astype(F32)
    for j in range(NR):
        r = NR * i + j
        cols = slice(j * LANES, (j + 1) * LANES)
        lh = pltpu.roll(left, lax.rem(LANES - SHIFT * r, LANES), 1)
        rh = pltpu.roll(right, LANES - SHIFT - SHIFT * r, 1)
        lh = jnp.where((lane < SHIFT) & (flags_ref[0, r] > 0), lh, 0.0)
        rh = jnp.where((lane >= LANES - SHIFT) & (flags_ref[1, r] > 0), rh, 0.0)
        out_ref[j] = (base_ref[:, cols].astype(F32) + lh + rh).astype(BF16)
        a = coef[:, j : j + 1]
        b = coef[:, RP + j : RP + j + 1]
        layer_ref[j] = (a * mid_ref[:, cols].astype(F32) + b).astype(BF16)


def add_blocks_kernel(a_ref, b_ref, keep_ref, give_ref):
    for j in range(a_ref.shape[0]):
        v = a_ref[j].astype(F32) + b_ref[j].astype(F32)
        (keep_ref, give_ref)[j % 2][j // 2] = v.astype(BF16)


def add_halves_kernel(bit_ref, a_ref, b_ref, keep_ref, give_ref, scr):
    half = a_ref.shape[1] // 2
    scr[...] = a_ref[0].astype(F32) + b_ref[0].astype(F32)
    keep_ref[...] = scr[pl.ds(pl.multiple_of(bit_ref[0] * half, 8), half)].astype(BF16)
    give_ref[...] = scr[pl.ds(pl.multiple_of((1 - bit_ref[0]) * half, 8), half)].astype(BF16)


def add_pieces_kernel(a_ref, b_ref, out_ref):
    v = a_ref[...].astype(F32) + b_ref[...].astype(F32)
    size = out_ref.shape[1]
    for p in range(out_ref.shape[0]):
        out_ref[p] = v[p * size : (p + 1) * size].astype(BF16)


def add_pieces_twice_kernel(a_ref, b_ref, c_ref, d_ref, out_ref):
    v = a_ref[...].astype(F32) + b_ref[...].astype(F32)
    w = c_ref[...].astype(F32) + d_ref[...].astype(F32)
    size, width = out_ref.shape[1], v.shape[1]
    for p in range(out_ref.shape[0]):
        rows = slice(p * size, (p + 1) * size)
        out_ref[p, :, 0:width] = v[rows].astype(BF16)
        out_ref[p, :, width:] = w[rows].astype(BF16)


def sum_copies_kernel(a_ref, out_ref):
    v = a_ref[0].astype(F32)
    for p in range(1, a_ref.shape[0]):
        v = v + a_ref[p].astype(F32)
    v = v.astype(BF16)
    for p in range(out_ref.shape[0]):
        out_ref[p] = v


def small_sum_kernel(cs, csh, got_ref, film_ref, out_ref, scr, turn, emb, sums):
    v = got_ref[0].astype(F32)
    for d in range(1, got_ref.shape[0]):
        v = v + got_ref[d].astype(F32)
    turn[...] = jnp.zeros(turn.shape, F32)
    turn[0:cs, 0 : 2 * csh] = v[:cs, 192 : 192 + 2 * csh]
    film_ref[...] = turn[...].T[0 : 2 * csh, 0:cs]
    half = cs // 2
    scr[...] = jnp.zeros(scr.shape, F32)
    scr[0:cs] = v[:cs, 0:128]
    scr[cs : cs + half, 0:csh] = v[0:half, 128 : 128 + csh]
    scr[cs : cs + half, csh : 2 * csh] = v[half:cs, 128 : 128 + csh]
    dq = v[cs : cs + QUERIES, 0:64] + v[cs : cs + QUERIES, 64:128]
    hi = dq.astype(BF16).astype(F32)
    scr[cs + half : cs + half + QUERIES, 0:64] = hi
    scr[cs + half : cs + half + QUERIES, 64:128] = dq - hi
    emb[...] = jnp.zeros(emb.shape, F32)
    sums[...] = jnp.zeros(sums.shape, F32)
    at = cs + QUERIES
    for d in range(got_ref.shape[0]):
        rows = slice(d * RP, (d + 1) * RP)
        emb[rows, 0:cs] = got_ref[d, at : at + RP, 128 : 128 + cs].astype(F32)
        sums[rows, 0 : 2 * csh] = got_ref[d, at : at + RP, 0 : 2 * csh].astype(F32)
    step = nn(emb[...].T.astype(BF16), sums[...].astype(BF16))
    step = step[0:cs, 0:csh] + step[0:cs, csh : 2 * csh]
    at = cs + half + QUERIES
    scr[at : at + half, 0:csh] = step[0:half]
    scr[at : at + half, csh : 2 * csh] = step[half:cs]
    low = scr[...].astype(BF16)
    for p in range(out_ref.shape[0]):
        out_ref[p] = low


def output_kernel(
    cs,
    csh,
    hs,
    bit_ref,
    own1_ref,
    got1_ref,
    own2_ref,
    got2_ref,
    own3_ref,
    got3_ref,
    small_ref,
    queries_ref,
    wq_ref,
    step_ref,
    conv_ref,
    cond_ref,
    res_ref,
    skip_ref,
    gqueries_ref,
    gquery_ref,
    key_ref,
    value_ref,
    attn_ref,
    qscr,
    dq,
):
    half = cs // 2
    bit = bit_ref[0]

    def taps(at, lane, v):
        tap, c = at // cs, at % cs
        rows, cols = slice(c, c + v.shape[0]), slice(lane, lane + v.shape[1])
        if tap < 3:
            conv_ref[tap, rows, cols] = v
        else:
            cond_ref[rows, cols] = v

    for number, (own, got) in enumerate(
        ((own1_ref, got1_ref), (own2_ref, got2_ref), (own3_ref, got3_ref))
    ):
        count, size = own.shape[0], own.shape[1]
        for p in range(count):
            a, b = own[p].astype(F32), got[p].astype(F32)
            for at, v in (
                (p * size, jnp.where(bit == 0, a, b)),
                ((count + p) * size, jnp.where(bit == 0, b, a)),
            ):
                t, c = at // cs, at % cs
                lanes = slice(t * LANES, (t + 1) * LANES)
                if number == 0:
                    res_ref[c : c + size, lanes] = v[:, 0:LANES]
                    taps(at, 0, v[:, LANES : 3 * LANES])
                    skip_ref[c : c + size, lanes] = v[:, 3 * LANES :]
                else:
                    taps(at, (3 * number - 1) * LANES, v)
    dq[...] = jnp.zeros(dq.shape, F32)
    for head in range(HEADS):
        cols = slice(head * HEAD_DIM, (head + 1) * HEAD_DIM)
        v = small_ref[head * hs].astype(F32)
        for k in range(1, hs):
            v = v + small_ref[head * hs + k].astype(F32)
        key_ref[:, cols] = v[0:cs, 0:64]
        value_ref[:, cols] = v[0:cs, 64:128]
        low = v[cs + half : cs + half + QUERIES]
        dq[0:QUERIES, cols] = low[:, 0:64] + low[:, 64:128]
    for s in range(small_ref.shape[0]):
        v = small_ref[s, cs : cs + half].astype(F32)
        attn_ref[0:half, s * csh : (s + 1) * csh] = v[:, 0:csh]
        attn_ref[half:cs, s * csh : (s + 1) * csh] = v[:, csh : 2 * csh]
        at = cs + half + QUERIES
        v = small_ref[s, at : at + half].astype(F32)
        step_ref[0:half, s * csh : (s + 1) * csh] = v[:, 0:csh]
        step_ref[half:cs, s * csh : (s + 1) * csh] = v[:, csh : 2 * csh]
    qscr[...] = jnp.zeros((LANES, LANES), F32)
    qscr[0:QUERIES, 0:cs] = queries_ref[...].astype(F32)
    qt = qscr[...].T.astype(BF16)
    d = dq[...]
    hi = d.astype(BF16)
    lo = (d - hi.astype(F32)).astype(BF16)
    gquery_ref[...] = (nn(qt, hi) + nn(qt, lo))[0:cs]
    gqueries_ref[...] = fold(nt(parts(d[0:QUERIES], 2), wq_ref[...]), 2)


def attention_back_kernel(
    rows,
    csh,
    dp,
    prm_ref,
    probs_ref,
    u_ref,
    qp_ref,
    qkv_ref,
    pooled_ref,
    memory_ref,
    dfilm_ref,
    got_ref,
    sums_ref,
    emb_ref,
    out_ref,
    prow,
    ds,
    stack,
    right,
):
    count = prm_ref.shape[0]
    total = count * prm_ref.shape[2]
    cs = C // dp
    wk, wv = qkv_ref[64:128], qkv_ref[128:192]
    datt = got_ref[0, 3 * RP : 4 * RP, 0:HEAD_DIM]
    dmem = got_ref[0, 2 * RP : 3 * RP, 0:csh]
    for s in range(1, count):
        datt = datt + got_ref[s, 3 * RP : 4 * RP, 0:HEAD_DIM]
        dmem = dmem + got_ref[s, 2 * RP : 3 * RP, 0:csh]
    datt = datt * (1.0 / QUERIES)
    for r in range(rows):
        prow[r * total : (r + 1) * total] = prm_ref[:, r].reshape(total, C)
    vh = fold(nn(parts(datt, 2), wv), 2)
    dp_all = fold(nt(parts(vh, 2), prow[...]), 2)
    for r in range(rows):
        cols = slice(r * total, (r + 1) * total)
        p = probs_ref[:, cols]
        dpr = dp_all[r : r + 1, cols]
        inner = jnp.sum(p * dpr, axis=1, keepdims=True)
        ds[:, cols] = p * (dpr - inner)
    tt = fold(nn(parts(ds[...], 2), prow[...]), 2)
    scale = 1.0 / math.sqrt(HEAD_DIM)
    dq = fold(nt(parts(tt, 2), wk), 2) * scale
    stack[...] = jnp.zeros(stack.shape, F32)
    stack[0:QUERIES] = tt
    stack[32:48] = u_ref[...]
    stack[48:64] = pooled_ref[...].astype(F32)
    stack[64:80] = memory_ref[...].astype(F32)
    right[...] = jnp.zeros(right.shape, F32)
    right[0:32, 0:64] = qp_ref[...] * scale
    right[32:48, 64:128] = datt
    right[48:64, 128 : 128 + csh] = dmem
    right[64:80, 192 : 192 + 2 * csh] = dfilm_ref[...].astype(F32)
    grads = lax.dot_general(
        stack[...].T,
        right[...],
        (((1,), (0,)), ((), ())),
        precision=lax.Precision.HIGHEST,
        preferred_element_type=F32,
    ).astype(BF16)
    hi = dq.astype(BF16)
    lo = (dq - hi.astype(F32)).astype(BF16)
    step = sums_ref[0]
    for s in range(1, count):
        step = step + sums_ref[s]
    step = step[:, 0:csh]
    step_hi = step.astype(BF16)
    step_lo = (step - step_hi.astype(F32)).astype(BF16)
    at = cs + QUERIES
    for d in range(dp):
        out_ref[d, at : at + RP] = jnp.zeros((RP, right.shape[1]), BF16)
        out_ref[d, at : at + RP, 0:csh] = step_hi
        out_ref[d, at : at + RP, csh : 2 * csh] = step_lo
        out_ref[d, at : at + RP, 128 : 128 + cs] = emb_ref[0:RP, d * cs : (d + 1) * cs]
        out_ref[d, 0:cs] = grads[d * cs : (d + 1) * cs]
        out_ref[d, cs : cs + QUERIES] = jnp.zeros((QUERIES, right.shape[1]), BF16)
        out_ref[d, cs : cs + QUERIES, 0:64] = hi
        out_ref[d, cs : cs + QUERIES, 64:128] = lo


def exchange(pieces, axis, groups=None):
    return lax.all_to_all(
        pieces, axis, split_axis=0, concat_axis=0, axis_index_groups=groups, tiled=True
    )


def flipped(v, axis, size, bit):
    return lax.ppermute(v, axis, [(d, d ^ bit) for d in range(size)])


class Reduction:
    def __init__(self, call, name, keep, give, dp, seq, bit):
        self.call, self.name, self.dp, self.seq, self.bit = call, name, dp, seq, bit
        self.keep, self.flip = keep, 1
        self.rows, self.width = keep.shape[1], keep.shape[2]
        self.got = flipped(give, "dp", dp, 1)

    def over_blocks(self, after=()):
        while 2 * self.flip < self.dp:
            half = sds((self.keep.shape[0] // 2,) + self.keep.shape[1:], BF16)
            self.keep, give = self.call(
                add_blocks_kernel,
                (half, half),
                "blocks_" + self.name,
                (self.keep, Got(self.got)),
                nbytes=6 * self.keep.size,
                after=after,
                in_specs=[VM, VM],
                out_specs=(VM, VM),
            )
            self.flip *= 2
            self.got = flipped(give, "dp", self.dp, self.flip)

    def over_halves(self, after=()):
        half = sds((self.rows // 2, self.width), BF16)
        self.keep, give = self.call(
            add_halves_kernel,
            (half, half),
            "halves_" + self.name,
            (self.bit, self.keep, Got(self.got)),
            nbytes=6 * self.keep.size,
            after=after,
            in_specs=[SM, VM, VM],
            out_specs=(VM, VM),
            scratch_shapes=[pltpu.VMEM((self.rows, self.width), F32)],
        )
        self.got = flipped(give, "seq", self.seq, 1)

    def over_pieces(self, after=(), other=None):
        count = self.seq // 2
        args = (self.keep, Got(self.got))
        kernel = add_pieces_kernel
        if other is not None:
            args += (other.keep, Got(other.got))
            kernel = add_pieces_twice_kernel
            self.width += other.width
        self.groups = [[2 * k + b for k in range(count)] for b in range(2)]
        self.piece = sds((count, self.rows // self.seq, self.width), BF16)
        pieces = self.call(
            kernel,
            self.piece,
            "pieces_" + self.name,
            args,
            nbytes=6 * self.keep.size,
            after=after,
            in_specs=[VM] * len(args),
            out_specs=VM,
        )
        self.got = exchange(pieces, "seq", self.groups)

    def over_copies(self, after=()):
        copies = self.call(
            sum_copies_kernel,
            self.piece,
            "copies_" + self.name,
            (Got(self.got),),
            nbytes=4 * self.got.size,
            after=after,
            in_specs=[VM],
            out_specs=VM,
        )
        own = exchange(copies, "seq", self.groups)
        self.result = (Got(own), Got(flipped(own, "seq", self.seq, 1)))


def body(
    dp,
    seq,
    x_in,
    cond,
    segment_ids,
    diffusion_steps,
    prompt,
    prompt_lengths,
    w_step,
    w_conv,
    w_cond,
    w_res,
    w_skip,
    queries,
    w_query,
    w_key,
    w_value,
    w_attn_out,
    w_film,
    d_out,
    d_skip,
):
    call = Caller()
    rows = x_in.shape[0]
    frames = x_in.shape[2]
    steps = rows // NR
    cols = rows * frames
    cs = C // dp
    csh = C // seq
    hs = max(1, seq // HEADS)
    arows = rows // hs
    pl_local = prompt.shape[1]
    prompt_all = pl_local * seq
    sidx = lax.axis_index("seq")
    didx = lax.axis_index("dp")
    head = sidx // hs
    part = sidx % hs
    up = [(i, i + 1) for i in range(seq - 1)]
    down = [(i + 1, i) for i in range(seq - 1)]
    order = jnp.bitwise_xor(didx, jnp.arange(dp, dtype=jnp.int32)).astype(jnp.int32)
    offsets = order * cs
    bit = (sidx % 2).astype(jnp.int32).reshape(1)

    def gather(pack):
        have = {0: pack}
        flip = dp // 2
        while flip:
            for k in sorted(have):
                have[k + flip] = flipped(have[k], "dp", dp, flip)
            flip //= 2
        return [have[k] if k == 0 else Got(have[k]) for k in range(dp)]

    plain = call(
        functools.partial(plain_pack_kernel, cs, csh),
        sds((cs, PLAIN + 2 * C), BF16),
        "plain_pack",
        (
            head.astype(jnp.int32).reshape(1),
            w_res,
            w_skip,
            w_attn_out,
            w_step,
            jnp.transpose(w_film, (1, 2, 0)).reshape(2 * csh, cs),
            w_query,
            w_key,
            w_value,
            queries,
        ),
        nbytes=2e6,
        in_specs=[SM] + [VM] * 9,
        out_specs=VM,
        scratch_shapes=[pltpu.VMEM((2 * LANES, LANES), F32)],
    )
    plain = gather(plain)
    turned = call(
        functools.partial(turned_pack_kernel, cs),
        sds((2 * C, 4 * cs), BF16),
        "turned_pack",
        (w_conv, w_cond),
        after=("plain_pack",),
        nbytes=2e6,
        in_specs=[VM, VM],
        out_specs=VM,
        scratch_shapes=[pltpu.VMEM((4 * cs, 2 * C), BF16)],
    )
    turned = gather(turned)
    first, last, prompts = call(
        functools.partial(edge_kernel, hs),
        (
            sds((C, LANES), BF16),
            sds((C, LANES), BF16),
            sds((seq, arows, pl_local, C), BF16),
        ),
        "edges",
        (x_in, prompt),
        after=("turned_pack",),
        nbytes=4e6,
        in_specs=[VM, VM],
        out_specs=(VM, VM, VM),
    )
    prompts = exchange(prompts, "seq")
    left_halo = lax.ppermute(last, "seq", up)
    right_halo = lax.ppermute(first, "seq", down)

    block_ids = segment_ids[:, ::frames]
    padded_ids = jnp.pad(block_ids, ((0, 0), (1, 1)), constant_values=-1)
    mine = lax.dynamic_slice_in_dim(padded_ids, sidx, 3, 1)
    flags = jnp.stack([mine[:, 0] == mine[:, 1], mine[:, 2] == mine[:, 1]]).astype(jnp.int32)
    block_ids = jnp.pad(block_ids, ((0, RP - rows), (0, 0)))
    half = C // 2
    frequency = jnp.exp(jnp.arange(half, dtype=F32) * (-math.log(10000.0) / half))
    step_rows = jnp.pad(diffusion_steps.astype(F32), (0, LANES - rows))
    live_rows = jnp.arange(LANES, dtype=jnp.int32)[:, None] < rows
    angles = step_rows[:, None] * frequency[None, :]
    embedding = jnp.concatenate([jnp.sin(angles), jnp.cos(angles)], axis=1)
    embedding = jnp.where(live_rows, embedding, 0.0).astype(BF16)
    lengths = lax.dynamic_slice_in_dim(prompt_lengths, part * arows, arows, 0)

    apack, probs, u, pooled_head, qp, qkv = call(
        functools.partial(attention_kernel, arows, dp, 2 * C + 2 * csh),
        (
            sds((C, PLAIN), BF16),
            sds((QUERIES, arows * prompt_all), F32),
            sds((RP, C), F32),
            sds((seq, RP, LANES), F32),
            sds((QUERIES, HEAD_DIM), F32),
            sds((256, C), BF16),
        ),
        "attention",
        (offsets, lengths, Got(prompts), *plain),
        flops=2 * 160 * 1536 * 512,
        nbytes=4e6,
        in_specs=[SM, SM, VM] + [HB] * dp,
        out_specs=(VM,) * 6,
        scratch_shapes=[
            pltpu.VMEM((arows * prompt_all, C), BF16),
            pltpu.VMEM((RP, arows * prompt_all), F32),
            pltpu.SemaphoreType.DMA((dp,)),
        ],
    )
    pooled_got = exchange(pooled_head, "seq")

    row_block = pl.BlockSpec((NR, C, LANES), lambda i: (i, 0, 0))

    def col_block(height):
        return pl.BlockSpec((height, NR * LANES), lambda i: (0, i))

    def still(shape):
        return pl.BlockSpec(shape, lambda i: (0,) * len(shape))

    inp, gated, factor_a, factor_b, skip_out, mid, stats = call(
        functools.partial(forward_kernel, dp, csh),
        (
            sds((4 * C, cols), BF16),
            sds((C, cols), BF16),
            sds((C, cols), BF16),
            sds((C, cols), BF16),
            sds(x_in.shape, BF16),
            sds((C, cols), BF16),
            sds((seq, 2 * RP, 2 * csh), F32),
        ),
        "wavenet",
        (
            offsets,
            flags,
            x_in,
            cond,
            d_out,
            Got(left_halo),
            Got(right_halo),
            embedding,
            *turned,
            *plain,
        ),
        after=("attention",),
        flops=2 * cols * (4 * C * 2 * C + 2 * C * C),
        nbytes=30e6,
        grid=(steps,),
        in_specs=[
            SM,
            SM,
            row_block,
            row_block,
            row_block,
            whole((C, LANES)),
            whole((C, LANES)),
            whole((LANES, C)),
        ]
        + [HB] * (2 * dp),
        out_specs=(
            col_block(4 * C),
            col_block(C),
            col_block(C),
            col_block(C),
            row_block,
            col_block(C),
            still((seq, 2 * RP, 2 * csh)),
        ),
        scratch_shapes=[
            pltpu.VMEM((2 * C, 4 * C), BF16),
            pltpu.VMEM((C, 2 * C), BF16),
            pltpu.VMEM((C, C), BF16),
            pltpu.VMEM((2 * C, C), BF16),
            pltpu.VMEM((C, LANES), F32),
            pltpu.VMEM((C, LANES), F32),
            pltpu.SemaphoreType.DMA((3 * dp,)),
        ],
    )
    stats_got = exchange(stats, "seq")
    part0 = sds((dp // 2, 4 * cs, LANES), BF16)
    keep, give = call(
        functools.partial(skip_grad_kernel, dp),
        (part0, part0),
        "skip",
        (offsets, gated, d_skip),
        flops=2 * cols * C * C,
        nbytes=4e6,
        in_specs=[SM, VM, VM],
        out_specs=(VM, VM),
        scratch_shapes=[pltpu.VMEM((C, cols), BF16), pltpu.VMEM((C, C), F32)],
    )
    part0 = Reduction(call, "skip", keep, give, dp, seq, bit)
    pooled, memory, film = call(
        functools.partial(memory_kernel, csh, hs, arows),
        (sds((RP, C), BF16), sds((RP, C), BF16), sds((RP, 2 * csh), F32)),
        "memory",
        (Got(pooled_got), apack),
        nbytes=2e6,
        in_specs=[VM, VM],
        out_specs=(VM, VM, VM),
        scratch_shapes=[pltpu.VMEM((RP, C), F32)],
    )

    coef_out, dfilm = call(
        functools.partial(stats_kernel, csh, hs, arows),
        (sds((seq, 4 * RP, 2 * csh), F32), sds((RP, 2 * csh), BF16)),
        "segments",
        after=("skip",),
        args=(block_ids, Got(stats_got), film, apack),
        nbytes=2e6,
        in_specs=[VM, VM, VM, VM],
        out_specs=(VM, VM),
    )
    coef = Got(exchange(coef_out, "seq"))

    part0.over_blocks()
    part0.over_halves()

    def gate_block(i):
        return jnp.minimum(i, steps - 1)

    def shard(i):
        return jnp.maximum(i - steps, 0)

    def gate_cols(height):
        return pl.BlockSpec((height, NR * LANES), lambda i, order: (0, gate_block(i)))

    gate_rows = pl.BlockSpec((NR, C, LANES), lambda i, order: (gate_block(i), 0, 0))
    part = sds((dp // 2, 4 * cs, 3 * LANES), BF16)
    part_spec = pl.BlockSpec((1, 4 * cs, 3 * LANES), lambda i, order: (shard(i) // 2, 0, 0))
    outs = call(
        functools.partial(backward_kernel, dp, csh, steps),
        (sds((2 * C, cols), BF16), sds((C, cols), BF16)) + (part,) * 6,
        "backward",
        (order, offsets, coef, mid, d_out, d_skip, factor_a, factor_b, inp, gated, *plain),
        after=("halves_skip",),
        prefetch=1,
        grid=(steps + dp,),
        in_specs=[
            SM,
            pl.BlockSpec(
                (seq, 4 * RP, 2 * csh), lambda i, order: (0, 0, 0), pipeline_mode=pl.Buffered(1)
            ),
            gate_cols(C),
            gate_rows,
            gate_rows,
            gate_cols(C),
            gate_cols(C),
            pl.BlockSpec((4 * cs, cols), lambda i, order: (order[shard(i)], 0)),
            pl.BlockSpec((cs, cols), lambda i, order: (order[shard(i)], 0)),
        ]
        + [HB] * dp,
        out_specs=(gate_cols(2 * C), gate_cols(C)) + (part_spec,) * 6,
        scratch_shapes=[
            pltpu.VMEM((LANES, C), F32),
            pltpu.VMEM((C, LANES), F32),
            pltpu.VMEM((C, 2 * C), BF16),
            pltpu.VMEM((2 * C, NR * LANES), BF16),
            pltpu.VMEM((cols, 2 * C), BF16),
            pltpu.VMEM((cols, C), BF16),
            pltpu.SemaphoreType.DMA((dp,)),
        ],
    )
    dpre, dres = outs[0:2]
    part1, part2, part3 = (
        Reduction(call, str(k + 1), outs[2 + k], outs[5 + k], dp, seq, bit) for k in range(3)
    )
    part1.over_blocks()
    part2.over_blocks()
    part3.over_blocks()

    base, first, last, step_sums = call(
        functools.partial(input_grad_kernel, dp, csh),
        (
            sds((C, cols), BF16),
            sds((C, LANES), BF16),
            sds((C, LANES), BF16),
            sds((seq, RP, LANES), F32),
        ),
        "input_grad",
        (offsets, flags, dpre, dres, *turned),
        after=("blocks_3",),
        grid=(steps,),
        in_specs=[SM, SM, col_block(2 * C), col_block(C)] + [HB] * dp,
        out_specs=(
            col_block(C),
            still((C, LANES)),
            still((C, LANES)),
            still((seq, RP, LANES)),
        ),
        scratch_shapes=[
            pltpu.VMEM((2 * C, 4 * C), BF16),
            pltpu.VMEM((3, C, 2 * C), BF16),
            pltpu.VMEM((C, LANES), F32),
            pltpu.VMEM((C, LANES), F32),
            pltpu.VMEM((C, LANES), F32),
            pltpu.SemaphoreType.DMA((dp,)),
        ],
    )
    from_left = lax.ppermute(last, "seq", up)
    from_right = lax.ppermute(first, "seq", down)
    step_got = exchange(step_sums, "seq")
    part1.over_halves(("input_grad",))
    part1.over_pieces(other=part0)
    part2.over_halves()

    small = call(
        functools.partial(attention_back_kernel, arows, csh, dp),
        sds((dp, cs + QUERIES + RP, 384), BF16),
        "attention_back",
        after=("halves_2",),
        args=(
            Got(prompts),
            probs,
            u,
            qp,
            qkv,
            pooled,
            memory,
            dfilm,
            coef,
            Got(step_got),
            embedding,
        ),
        flops=2 * 200 * 1536 * 512,
        nbytes=4e6,
        in_specs=[VM] * 11,
        out_specs=VM,
        scratch_shapes=[
            pltpu.VMEM((arows * prompt_all, C), BF16),
            pltpu.VMEM((QUERIES, arows * prompt_all), F32),
            pltpu.VMEM((LANES, C), F32),
            pltpu.VMEM((LANES, 384), F32),
        ],
    )
    small = exchange(small, "dp")
    small_rows = 2 * cs + QUERIES
    grad_film, small = call(
        functools.partial(small_sum_kernel, cs, csh),
        (sds((2 * csh, cs), F32), sds((seq, small_rows, LANES), BF16)),
        "small_sum",
        (Got(small),),
        in_specs=[VM],
        out_specs=(VM, VM),
        scratch_shapes=[
            pltpu.VMEM((small_rows, LANES), F32),
            pltpu.VMEM((LANES, LANES), F32),
            pltpu.VMEM((max(LANES, dp * RP), LANES), F32),
            pltpu.VMEM((max(LANES, dp * RP), LANES), F32),
        ],
    )
    small = Got(exchange(small, "seq"))
    part1.over_copies()
    part2.over_pieces(("attention_back",))
    part3.over_halves()
    part2.over_copies()
    grad_input, layer_out = call(
        functools.partial(finish_kernel, csh),
        (sds(x_in.shape, BF16), sds(x_in.shape, BF16)),
        "grad_input",
        (flags, base, Got(from_left), Got(from_right), mid, coef),
        after=("copies_2",),
        grid=(steps,),
        in_specs=[
            SM,
            col_block(C),
            whole((C, LANES)),
            whole((C, LANES)),
            col_block(C),
            whole((seq, 4 * RP, 2 * csh)),
        ],
        out_specs=(row_block, row_block),
        scratch_shapes=[pltpu.VMEM((LANES, C), F32), pltpu.VMEM((C, LANES), F32)],
    )
    part3.over_pieces()
    part3.over_copies(("grad_input",))

    (
        grad_step,
        grad_conv,
        grad_cond,
        grad_res,
        grad_skip,
        grad_queries,
        grad_query,
        grad_key,
        grad_value,
        grad_attn,
    ) = call(
        functools.partial(output_kernel, cs, csh, hs),
        (
            sds((cs, C), F32),
            sds((3, cs, 2 * C), F32),
            sds((cs, 2 * C), F32),
            sds((cs, C), F32),
            sds((cs, C), F32),
            sds((QUERIES, cs), F32),
            sds((cs, C), F32),
            sds((cs, C), F32),
            sds((cs, C), F32),
            sds((cs, C), F32),
        ),
        "outputs",
        (bit, *part1.result, *part2.result, *part3.result, small, queries, w_query),
        nbytes=8e6,
        in_specs=[SM] + [VM] * 9,
        out_specs=(VM,) * 10,
        scratch_shapes=[
            pltpu.VMEM((LANES, LANES), F32),
            pltpu.VMEM((LANES, C), F32),
        ],
    )
    return (
        layer_out,
        skip_out,
        grad_input,
        grad_step,
        grad_conv,
        grad_cond,
        grad_res,
        grad_skip,
        grad_queries,
        grad_query,
        grad_key,
        grad_value,
        grad_attn,
        jnp.transpose(grad_film.reshape(2, csh, cs), (2, 0, 1)),
    )


def solution(mesh):
    frames = P("dp", None, "seq")
    matrix = P("dp", None)
    return jax.shard_map(
        functools.partial(body, mesh.shape["dp"], mesh.shape["seq"]),
        mesh=mesh,
        in_specs=(
            frames,
            frames,
            P("dp", None),
            P("dp"),
            P("dp", "seq", None),
            P("dp"),
            matrix,
            P(None, "dp", None),
            matrix,
            matrix,
            matrix,
            P(None, "dp"),
            matrix,
            matrix,
            matrix,
            matrix,
            frames,
            frames,
            frames,
        ),
        out_specs=(
            frames,
            frames,
            frames,
            matrix,
            P(None, "dp", None),
            matrix,
            matrix,
            matrix,
            P(None, "dp"),
            matrix,
            matrix,
            matrix,
            matrix,
            frames,
        ),
        check_vma=False,
    )
```

```python
import functools
import math

import jax
import jax.numpy as jnp
from jax import lax
from jax.experimental import pallas as pl
from jax.experimental.pallas import tpu as pltpu
from jax.sharding import PartitionSpec as P

C = 512
HEADS = 8
QUERIES = 32
HEAD_DIM = 64
SHIFT = 4
SQRT_HALF = 0.7071067811865476
NORM_EPS = 1e-05
MASKED_SCORE = -1e30
LANES = 128
RP = 16
NR = 4
F32 = jnp.float32
BF16 = jnp.bfloat16
VMEM_BYTES = 50 * 1024 * 1024


def nn(a, b):
    return lax.dot_general(a, b, (((1,), (0,)), ((), ())), preferred_element_type=F32)


def nt(a, b):
    return lax.dot_general(a, b, (((1,), (1,)), ((), ())), preferred_element_type=F32)


def parts(v, count):
    out = []
    for _ in range(count):
        low = v.astype(BF16)
        out.append(low)
        v = v - low.astype(F32)
    return jnp.concatenate(out, axis=0)


def fold(v, count):
    rows = v.shape[0] // count
    total = v[:rows]
    for k in range(1, count):
        total = total + v[k * rows : (k + 1) * rows]
    return total


def lane_ids(shape):
    return lax.broadcasted_iota(jnp.int32, shape, len(shape) - 1)


def sds(shape, dtype):
    return jax.ShapeDtypeStruct(shape, dtype)


VM = pl.BlockSpec(memory_space=pltpu.VMEM)
HB = pl.BlockSpec(memory_space=pl.ANY)
SM = pl.BlockSpec(memory_space=pltpu.SMEM)


def whole(shape):
    return pl.BlockSpec(shape, lambda i: (0,) * len(shape), pipeline_mode=pl.Buffered(1))


class Got:
    def __init__(self, array):
        self.array = array


class Caller:
    def __init__(self):
        self.done = {}

    def __call__(self, kernel, out_shape, name, args, flops=0, nbytes=0, prefetch=0, after=(), **kw):
        single = not isinstance(out_shape, tuple)
        shapes = (out_shape,) if single else out_shape
        pinned = tuple(pltpu.HBM(v.shape, v.dtype) for v in shapes)
        in_specs = list(kw.pop("in_specs"))
        count = prefetch + len(in_specs)
        args = list(args)
        extra = len(after)
        for before in after:
            in_specs.append(HB)
            args.append(self.done[before])

        def run(*refs):
            return kernel(*refs[:count], *refs[count + extra :])

        values = []
        for k, v in enumerate(args):
            spec = SM if k < prefetch else in_specs[k - prefetch]
            if isinstance(v, Got):
                values.append(v.array)
            elif spec is SM:
                values.append(v)
            else:
                values.append(pltpu.with_memory_space_constraint(v, pltpu.HBM))
        spec = pltpu.PrefetchScalarGridSpec(
            num_scalar_prefetch=prefetch,
            grid=kw.pop("grid", ()),
            in_specs=in_specs,
            out_specs=kw.pop("out_specs"),
            scratch_shapes=kw.pop("scratch_shapes", ()),
        )
        out = pl.pallas_call(
            run,
            out_shape=pinned[0] if single else pinned,
            name=name,
            grid_spec=spec,
            cost_estimate=pl.CostEstimate(
                flops=1, bytes_accessed=1, transcendentals=0
            ),
            compiler_params=pltpu.CompilerParams(vmem_limit_bytes=VMEM_BYTES),
        )(*values)
        self.done[name] = out if single else out[0]
        return out


PLAIN = 1408


def plain_pack_kernel(cs, csh, head_ref, res_ref, skip_ref, attn_ref, step_ref, film_ref, wq_ref, wk_ref, wv_ref, queries_ref, out_ref, scr):
    out_ref[:, 0:C] = attn_ref[...]
    out_ref[:, C : 2 * C] = step_ref[...]
    off = 2 * C
    scr[...] = jnp.zeros((2 * LANES, LANES), F32)
    scr[0 : 2 * csh, 0:cs] = film_ref[...].astype(F32)
    scr[LANES : LANES + QUERIES, 0:cs] = queries_ref[...].astype(F32)
    film = scr[0:LANES].T[0:cs]
    table = scr[LANES : 2 * LANES].T[0:cs]
    turn = lax.rem(C - HEAD_DIM * head_ref[0], C)
    blocks = [film[:, 0 : 2 * csh]]
    for ref in (wq_ref, wk_ref, wv_ref):
        blocks.append(pltpu.roll(ref[...].astype(F32), turn, 1)[:, 0:HEAD_DIM])
    blocks.append(table[:, 0 : PLAIN - off - 2 * csh - 3 * HEAD_DIM])
    for block in blocks:
        out_ref[:, off : off + block.shape[1]] = block.astype(BF16)
        off += block.shape[1]
    out_ref[:, PLAIN : PLAIN + C] = res_ref[...]
    out_ref[:, PLAIN + C : PLAIN + 2 * C] = skip_ref[...]


def turned_pack_kernel(cs, conv_ref, cond_ref, out_ref, scr):
    for k in range(3):
        scr[k * cs : (k + 1) * cs] = conv_ref[k]
    scr[3 * cs : 4 * cs] = cond_ref[...]
    out_ref[...] = scr[...].T


def edge_kernel(x_ref, first_ref, last_ref):
    rows = x_ref.shape[0]
    lane = lane_ids((C, LANES))
    first = jnp.zeros((C, LANES), F32)
    last = jnp.zeros((C, LANES), F32)
    for r in range(rows):
        v = x_ref[r].astype(F32)
        here = (lane // SHIFT) == r
        first = jnp.where(here, pltpu.roll(v, SHIFT * r, 1) if r else v, first)
        last = jnp.where(here, pltpu.roll(v, SHIFT * r + SHIFT, 1), last)
    first_ref[...] = first.astype(BF16)
    last_ref[...] = last.astype(BF16)


def copies_of(pieces, make):
    return [pltpu.make_async_copy(*make(k, piece)) for k, piece in enumerate(pieces)]


def begin(copies):
    for copy in copies:
        copy.start()


def finish(copies):
    for copy in copies:
        copy.wait()


def turned_copies(off_ref, turned, cs, dst, sems, base=0):
    def make(k, piece):
        lane = pl.multiple_of(off_ref[k] * 4, LANES)
        return piece, dst.at[:, pl.ds(lane, 4 * cs)], sems.at[base + k]

    return copies_of(turned, make)


def plain_copies(off_ref, plain, cs, lanes, width, dst, sems, base=0):
    def make(k, piece):
        row = pl.multiple_of(off_ref[k], 16)
        return piece.at[:, pl.ds(lanes, width)], dst.at[pl.ds(row, cs)], sems.at[base + k]

    return copies_of(plain, make)


def forward_kernel(
    dp, csh, off_ref, flags_ref, x_ref, cond_ref, dout_ref, left_ref, right_ref, emb_ref, pooled_ref, *refs
):
    turned, plain, refs = refs[:dp], refs[dp : 2 * dp], refs[2 * dp :]
    (
        inp_ref,
        gated_ref,
        fa_ref,
        fb_ref,
        skip_ref,
        mid_ref,
        stats_ref,
        wt_ref,
        rn_ref,
        step_ref,
        rst_ref,
        lift_ref,
        acc_ref,
        sems,
    ) = refs
    cs = C // dp
    i = pl.program_id(0)
    lane = lane_ids((C, LANES))

    @pl.when(i == 0)
    def _():
        steps = plain_copies(off_ref, plain, cs, C, C, step_ref, sems)
        outs = plain_copies(off_ref, plain, cs, PLAIN, 2 * C, rn_ref, sems, dp)
        convs = turned_copies(off_ref, turned, cs, wt_ref, sems, 2 * dp)
        begin(steps + outs + convs)
        acc_ref[...] = jnp.zeros((C, LANES), F32)
        finish(steps)
        lift = nn(emb_ref[0:RP], step_ref[...])
        lift = jnp.concatenate([lift, jnp.zeros((LANES - RP, C), F32)], axis=0)
        lift_ref[...] = lift.T
        finish(outs)
        rst_ref[...] = rn_ref[...].T
        finish(convs)

    lift = pltpu.roll(lift_ref[...], lax.rem(LANES - NR * i, LANES), 1)
    left = left_ref[...].astype(F32)
    right = right_ref[...].astype(F32)

    def put(tap, cols, value):
        for d in range(dp):
            at = d * 4 * cs + tap * cs
            inp_ref[at : at + cs, cols] = value[d * cs : (d + 1) * cs]

    for j in range(NR):
        r = NR * i + j
        lc = lift[:, j : j + 1]
        sh = (x_ref[j].astype(F32) + lc).astype(BF16)
        shf = sh.astype(F32)
        lh = pltpu.roll(left, lax.rem(LANES - SHIFT * r, LANES), 1)
        lh = jnp.where(flags_ref[0, r] > 0, (lh + lc).astype(BF16).astype(F32), 0.0)
        rh = pltpu.roll(right, LANES - SHIFT - SHIFT * r, 1)
        rh = jnp.where(flags_ref[1, r] > 0, (rh + lc).astype(BF16).astype(F32), 0.0)
        cols = slice(j * LANES, (j + 1) * LANES)
        put(0, cols, jnp.where(lane < SHIFT, lh, pltpu.roll(shf, SHIFT, 1)).astype(BF16))
        put(1, cols, sh)
        put(
            2,
            cols,
            jnp.where(lane >= LANES - SHIFT, rh, pltpu.roll(shf, LANES - SHIFT, 1)).astype(BF16),
        )
        put(3, cols, cond_ref[j])
    pre = nn(wt_ref[...], inp_ref[...])
    th = jnp.tanh(pre[:C])
    sg = jax.nn.sigmoid(pre[C:])
    gf = th * sg
    fa_ref[...] = (sg - gf * th).astype(BF16)
    fb_ref[...] = (gf * (1.0 - sg)).astype(BF16)
    g = gf.astype(BF16)
    gated_ref[...] = g
    rs = nn(rst_ref[...], g)
    acc = acc_ref[...]
    for j in range(NR):
        r = NR * i + j
        cols = slice(j * LANES, (j + 1) * LANES)
        skip_ref[j] = rs[C:, cols].astype(BF16)
        mid = ((x_ref[j].astype(F32) + rs[:C, cols]) * SQRT_HALF).astype(BF16)
        mid_ref[:, cols] = mid
        mf = mid.astype(F32)
        df = dout_ref[j].astype(F32)
        total = jnp.sum(mf, axis=1, keepdims=True)
        dev = mf - total * (1.0 / LANES)
        acc = jnp.where(lane == r, total, acc)
        acc = jnp.where(lane == RP + r, jnp.sum(dev * dev, axis=1, keepdims=True), acc)
        acc = jnp.where(lane == 2 * RP + r, jnp.sum(df, axis=1, keepdims=True), acc)
        acc = jnp.where(lane == 3 * RP + r, jnp.sum(df * dev, axis=1, keepdims=True), acc)
    acc_ref[...] = acc

    @pl.when(i == pl.num_programs(0) - 1)
    def _():
        t = acc.T
        for s in range(C // csh):
            cols = slice(s * csh, (s + 1) * csh)
            stats_ref[s, 0 : 2 * RP, 0:csh] = t[0 : 2 * RP, cols]
            stats_ref[s, 0 : 2 * RP, csh : 2 * csh] = t[2 * RP : 4 * RP, cols]
            stats_ref[s, 2 * RP : 3 * RP] = pooled_ref[:, 0 : 2 * csh]


def attention_kernel(rows, dp, seq, off, off_ref, peer_ref, len_ref, *refs):
    pieces, prompts, refs = refs[:dp], refs[dp : dp + seq], refs[dp + seq :]
    apack_ref, prow, probs_ref, u_ref, pooled_ref, qp_ref, qkv_ref, abd, sems = refs
    cs = C // dp
    copies = plain_copies(off_ref, pieces, cs, 0, PLAIN, apack_ref, sems)
    for k in range(seq):
        copies.append(pltpu.make_async_copy(prompts[k], prow.at[:, k], sems.at[dp + k]))
    begin(copies)
    local = prow.shape[2]
    total = seq * local
    abd[...] = jnp.zeros(abd.shape, F32)
    lane = lane_ids((QUERIES, total))
    place = jnp.zeros((QUERIES, total), jnp.int32)
    for k in range(seq):
        place = jnp.where(lane // local == k, peer_ref[k] * local + lane % local, place)
    finish(copies)
    qkv = apack_ref[:, off : off + 256].T
    qkv_ref[...] = qkv
    wq, wk, wv = qkv[0:64], qkv[64:128], qkv[128:192]
    qp = nt(qkv[192:224], wq)
    qp_ref[...] = qp
    st = fold(nn(parts(qp, 3), wk), 3) * (1.0 / math.sqrt(HEAD_DIM))
    table = prow[...].reshape(rows * total, C)
    scores = fold(nt(parts(st, 3), table), 3)
    for r in range(rows):
        cols = slice(r * total, (r + 1) * total)
        live = place < len_ref[r]
        s = jnp.where(live, scores[:, cols], MASKED_SCORE)
        e = jnp.where(live, jnp.exp(s - jnp.max(s, axis=1, keepdims=True)), 0.0)
        p = e / jnp.sum(e, axis=1, keepdims=True)
        probs_ref[:, cols] = p
        abd[r : r + 1, cols] = jnp.sum(p, axis=0, keepdims=True)
    u = fold(nn(parts(abd[...], 2), table), 2)
    u_ref[...] = u
    pooled = fold(nt(parts(u * (1.0 / QUERIES), 2), wv), 2)
    pooled_ref[...] = jnp.concatenate([pooled, jnp.zeros((RP, LANES - HEAD_DIM), F32)], axis=1)


def stats_kernel(
    csh, hs, rows, seg_ref, x_ref, apack_ref, out_ref, dfilm_ref, pooled_ref, memory_ref, scratch
):
    count = x_ref.shape[0]
    seg = seg_ref[...]
    scratch[...] = jnp.zeros(scratch.shape, F32)
    for s in range(count):
        head, part = s // hs, s % hs
        scratch[part * rows : (part + 1) * rows, head * HEAD_DIM : (head + 1) * HEAD_DIM] = x_ref[
            s, 2 * RP : 2 * RP + rows, 0:HEAD_DIM
        ]
    pooled = scratch[...].astype(BF16)
    pooled_ref[...] = pooled
    memory = nn(pooled, apack_ref[:, 0:C]).astype(BF16)
    memory_ref[...] = memory
    film = nn(memory, apack_ref[:, 2 * C : 2 * C + 2 * csh])
    f0 = film[:, 0:csh]
    f1 = film[:, csh : 2 * csh]
    total = [x_ref[s, 0:RP, 0:csh] for s in range(count)]
    second = [x_ref[s, RP : 2 * RP, 0:csh] for s in range(count)]
    dsum = [x_ref[s, 0:RP, csh : 2 * csh] for s in range(count)]
    cross = [x_ref[s, RP : 2 * RP, csh : 2 * csh] for s in range(count)]
    means = [v * (1.0 / LANES) for v in total]
    d0 = jnp.zeros((RP, csh), F32)
    d1 = jnp.zeros((RP, csh), F32)
    for me in range(count):
        same = [(seg[:, s : s + 1] == seg[:, me : me + 1]).astype(F32) for s in range(count)]
        frames = sum(same) * float(LANES)
        inv = 1.0 / frames
        mean = sum(m * v for m, v in zip(same, total)) * inv
        var = (
            sum(
                m * (v + float(LANES) * (u - mean) * (u - mean))
                for m, v, u in zip(same, second, means)
            )
            * inv
        )
        scale = lax.rsqrt(var + NORM_EPS)
        dtot = sum(m * v for m, v in zip(same, dsum))
        xtot = sum(m * (v + (u - mean) * d) for m, v, u, d in zip(same, cross, means, dsum)) * scale
        mean_part = f0 * dtot * inv
        cross_part = f0 * xtot * inv
        slope = scale * scale * cross_part
        out_ref[me, 0:RP, 0:csh] = 1.0 + f0 * scale
        out_ref[me, RP : 2 * RP, 0:csh] = f1 - f0 * scale * mean
        out_ref[me, 0:RP, csh : 2 * csh] = -slope
        out_ref[me, RP : 2 * RP, csh : 2 * csh] = slope * mean - scale * mean_part
        d0 = d0 + (cross[me] + (means[me] - mean) * dsum[me]) * scale
        d1 = d1 + dsum[me]
    dfilm = jnp.concatenate([d0, d1], axis=1).astype(BF16)
    dfilm_ref[...] = dfilm
    dmem = nt(dfilm, apack_ref[:, 2 * C : 2 * C + 2 * csh])
    dpool = nt(dmem.astype(BF16), apack_ref[:, 0:C])
    for s in range(count):
        head, part = s // hs, s % hs
        rolled = pltpu.roll(dpool, RP - part * rows, 0) if part else dpool
        out_ref[s, 2 * RP : 3 * RP, 0:csh] = dmem[:, s * csh : (s + 1) * csh]
        out_ref[s, 2 * RP : 3 * RP, csh : 2 * csh] = jnp.zeros((RP, csh), F32)
        out_ref[s, 3 * RP : 4 * RP, 0:HEAD_DIM] = rolled[:, head * HEAD_DIM : (head + 1) * HEAD_DIM]
        if 2 * csh > HEAD_DIM:
            out_ref[s, 3 * RP : 4 * RP, HEAD_DIM : 2 * csh] = jnp.zeros(
                (RP, 2 * csh - HEAD_DIM), F32
            )


def coef_columns(csh, coef_ref, rows_ref, cols_ref):
    rows_ref[...] = jnp.zeros(rows_ref.shape, F32)
    for s in range(C // csh):
        cols = slice(s * csh, (s + 1) * csh)
        rows_ref[0 : 2 * RP, cols] = coef_ref[s, 0 : 2 * RP, 0:csh]
        rows_ref[2 * RP : 4 * RP, cols] = coef_ref[s, 0 : 2 * RP, csh : 2 * csh]
    cols_ref[...] = rows_ref[...].T


def skip_grad_kernel(gated_ref, dskip_ref, out_ref, right):
    for r in range(dskip_ref.shape[0]):
        right[:, r * LANES : (r + 1) * LANES] = dskip_ref[r]
    out_ref[...] = nt(gated_ref[...], right[...]).astype(BF16)


def backward_kernel(dp, csh, gates, order_ref, off_ref, coef_ref, mid_ref, dout_ref, dskip_ref, fa_ref, fb_ref, inp_ref, gated_ref, gskip_ref, flags_ref, *refs):
    plain, refs = refs[:dp], refs[dp:]
    dpre_ref, dres_ref, sums_ref, refs = refs[0], refs[1], refs[2], refs[3:]
    outs, refs = (refs[0:2], refs[2:4]), refs[4:]
    rows_ref, cols_ref, w_ref, both_ref, dpt_ref, drt_ref, sems = refs
    cs = C // dp
    span = NR * LANES
    i = pl.program_id(0)

    @pl.when(i == 0)
    def _():
        copies = plain_copies(off_ref, plain, cs, PLAIN, 2 * C, w_ref, sems)
        begin(copies)
        coef_columns(csh, coef_ref, rows_ref, cols_ref)
        sums_ref[...] = jnp.zeros(sums_ref.shape, F32)
        finish(copies)

    @pl.when(i < gates)
    def _():
        coef = pltpu.roll(cols_ref[...], lax.rem(LANES - NR * i, LANES), 1)
        for j in range(NR):
            cols = slice(j * LANES, (j + 1) * LANES)
            mf = mid_ref[:, cols].astype(F32)
            df = dout_ref[j].astype(F32)
            a = coef[:, j : j + 1]
            be = coef[:, 2 * RP + j : 2 * RP + j + 1]
            ga = coef[:, 3 * RP + j : 3 * RP + j + 1]
            dmid = (a * df + (be * mf + ga)).astype(BF16).astype(F32)
            both_ref[0:C, cols] = (dmid * SQRT_HALF).astype(BF16)
            both_ref[C : 2 * C, cols] = dskip_ref[j]
        dres = both_ref[0:C]
        dres_ref[...] = dres
        dg = nn(w_ref[...], both_ref[...])
        dt = (dg * fa_ref[...].astype(F32)).astype(BF16)
        ds = (dg * fb_ref[...].astype(F32)).astype(BF16)
        dpre_ref[0:C] = dt
        dpre_ref[C : 2 * C] = ds
        at = pl.ds(pl.multiple_of(i * span, span), span)
        dpt_ref[at, 0:C] = dt.T
        dpt_ref[at, C : 2 * C] = ds.T
        drt_ref[at] = dres.T
        frame = lax.broadcasted_iota(jnp.int32, (span, LANES), 0)
        column = lane_ids((span, LANES))
        place = frame % LANES
        which = frame // LANES
        keep_l = jnp.zeros((span, LANES), jnp.int32)
        keep_r = jnp.zeros((span, LANES), jnp.int32)
        for j in range(NR):
            keep_l = jnp.where(which == j, flags_ref[0, NR * i + j], keep_l)
            keep_r = jnp.where(which == j, flags_ref[1, NR * i + j], keep_r)
        row = NR * i + which
        use0 = (column == row) & ((place >= SHIFT) | (keep_l > 0))
        use1 = column == RP + row
        use2 = (column == 2 * RP + row) & ((place < LANES - SHIFT) | (keep_r > 0))
        pick = jnp.where(use0 | use1 | use2, 1.0, 0.0).astype(BF16)
        sums_ref[...] = sums_ref[...] + nn(dpre_ref[...], pick)

    @pl.when(i >= gates)
    def _():
        g = nn(inp_ref[...], dpt_ref[...]).astype(BF16)
        h = nn(gated_ref[...], drt_ref[...]).astype(BF16)
        k = i - gates
        for parity, (one, two) in enumerate(outs):

            @pl.when(lax.rem(k, 2) == parity)
            def _():
                for t in range(4):
                    rows = slice(t * cs, (t + 1) * cs)
                    lanes = slice(t * LANES, (t + 1) * LANES)
                    one[0, rows, 0:LANES] = h[:, lanes]
                    one[0, rows, LANES : 2 * LANES] = gskip_ref[:, lanes]
                one[0, :, 2 * LANES : 6 * LANES] = g[:, 0:C]
                two[0] = g[:, C : 2 * C]


def step_grad_kernel(dp, off_ref, sums_ref, emb_ref, *refs):
    turned, refs = refs[:dp], refs[dp:]
    keep_ref, give_ref, wt_ref, scr, sems = refs
    cs = C // dp
    copies = turned_copies(off_ref, turned, cs, wt_ref, sems)
    begin(copies)
    sums = sums_ref[...].T
    emb = emb_ref[...].T
    finish(copies)
    total = jnp.zeros((RP, 4 * C), F32)
    lane = lane_ids((RP, 4 * C))
    all_taps = fold(nn(parts(sums[0 : 3 * RP], 2), wt_ref[...]), 2)
    for t in range(3):
        g = all_taps[t * RP : (t + 1) * RP]
        total = total + jnp.where((lane // cs) % 4 == t, g, 0.0)
    out = []
    for d in range(dp):
        block = total[:, d * 4 * cs : (d + 1) * 4 * cs]
        out.append(block[:, 0:cs] + block[:, cs : 2 * cs] + block[:, 2 * cs : 3 * cs])
    g = jnp.concatenate(out, axis=1)
    g = jnp.concatenate([g, jnp.zeros((LANES - RP, C), F32)], axis=0)
    hi = g.astype(BF16)
    lo = (g - hi.astype(F32)).astype(BF16)
    scr[...] = nn(emb, hi) + nn(emb, lo)
    for k in range(dp):
        v = scr[pl.ds(pl.multiple_of(off_ref[k], 16), cs)].astype(BF16)
        for t in range(4):
            (keep_ref, give_ref)[k % 2][k // 2, t * cs : (t + 1) * cs] = v[
                :, t * LANES : (t + 1) * LANES
            ]


def input_grad_kernel(dp, off_ref, dpre_ref, dres_ref, *refs):
    turned, refs = refs[:dp], refs[dp:]
    base_ref, first_ref, last_ref, wt_ref, w_ref, facc_ref, lacc_ref, sems = refs
    cs = C // dp
    i = pl.program_id(0)
    lane = lane_ids((C, LANES))

    @pl.when(i == 0)
    def _():
        copies = turned_copies(off_ref, turned, cs, wt_ref, sems)
        begin(copies)
        facc_ref[...] = jnp.zeros((C, LANES), F32)
        lacc_ref[...] = jnp.zeros((C, LANES), F32)
        finish(copies)
        for d in range(dp):
            v = wt_ref[:, d * 4 * cs : (d + 1) * 4 * cs].T
            for t in range(3):
                w_ref[t, d * cs : (d + 1) * cs] = v[t * cs : (t + 1) * cs]

    dpre = dpre_ref[...]
    y0 = nn(w_ref[0], dpre)
    y1 = nn(w_ref[1], dpre)
    y2 = nn(w_ref[2], dpre)
    facc = facc_ref[...]
    lacc = lacc_ref[...]
    for j in range(NR):
        r = NR * i + j
        cols = slice(j * LANES, (j + 1) * LANES)
        z0 = pltpu.roll(y0[:, cols], LANES - SHIFT, 1)
        z2 = pltpu.roll(y2[:, cols], SHIFT, 1)
        inner0 = lane < LANES - SHIFT
        inner2 = lane >= SHIFT
        v = y1[:, cols]
        base_ref[:, cols] = (
            v
            + jnp.where(inner0, z0, 0.0)
            + jnp.where(inner2, z2, 0.0)
            + dres_ref[:, cols].astype(F32)
        ).astype(BF16)
        here = (lane // SHIFT) == r
        facc = jnp.where(here, pltpu.roll(z0, lax.rem(SHIFT * r + SHIFT, LANES), 1), facc)
        lacc = jnp.where(here, pltpu.roll(z2, SHIFT * r, 1), lacc)
    facc_ref[...] = facc
    lacc_ref[...] = lacc

    @pl.when(i == pl.num_programs(0) - 1)
    def _():
        first_ref[...] = facc.astype(BF16)
        last_ref[...] = lacc.astype(BF16)


def finish_kernel(csh, flags_ref, base_ref, left_ref, right_ref, mid_ref, coef_ref, out_ref, layer_ref, rows_ref, cols_ref):
    i = pl.program_id(0)
    lane = lane_ids((C, LANES))

    @pl.when(i == 0)
    def _():
        coef_columns(csh, coef_ref, rows_ref, cols_ref)

    coef = pltpu.roll(cols_ref[...], lax.rem(LANES - NR * i, LANES), 1)
    left = left_ref[...].astype(F32)
    right = right_ref[...].astype(F32)
    for j in range(NR):
        r = NR * i + j
        cols = slice(j * LANES, (j + 1) * LANES)
        lh = pltpu.roll(left, lax.rem(LANES - SHIFT * r, LANES), 1)
        rh = pltpu.roll(right, LANES - SHIFT - SHIFT * r, 1)
        lh = jnp.where((lane < SHIFT) & (flags_ref[0, r] > 0), lh, 0.0)
        rh = jnp.where((lane >= LANES - SHIFT) & (flags_ref[1, r] > 0), rh, 0.0)
        out_ref[j] = (base_ref[:, cols].astype(F32) + lh + rh).astype(BF16)
        a = coef[:, j : j + 1]
        b = coef[:, RP + j : RP + j + 1]
        layer_ref[j] = (a * mid_ref[:, cols].astype(F32) + b).astype(BF16)


def add_blocks_kernel(count, *refs):
    ins, (keep_ref, give_ref) = refs[: 2 * count], refs[2 * count :]
    at = 0
    for p in range(count):
        a_ref, b_ref = ins[2 * p : 2 * p + 2]
        width = a_ref.shape[2]
        for j in range(a_ref.shape[0]):
            v = a_ref[j].astype(F32) + b_ref[j].astype(F32)
            (keep_ref, give_ref)[j % 2][j // 2, :, at : at + width] = v.astype(BF16)
        at += width


def add_halves_kernel(bit, index_ref, a_ref, b_ref, keep_ref, give_ref, scr):
    half = a_ref.shape[0] // 2
    mine = lax.rem(index_ref[0] // bit, 2)
    scr[...] = a_ref[...].astype(F32) + b_ref[...].astype(F32)
    keep_ref[...] = scr[pl.ds(pl.multiple_of(mine * half, 8), half)].astype(BF16)
    give_ref[...] = scr[pl.ds(pl.multiple_of((1 - mine) * half, 8), half)].astype(BF16)


def add_last_kernel(a_ref, b_ref, *refs):
    out_ref = refs[-1]
    width = a_ref.shape[1]
    out_ref[:, 0:width] = (a_ref[...].astype(F32) + b_ref[...].astype(F32)).astype(BF16)
    if len(refs) > 1:
        out_ref[:, width:] = refs[0][...]


def small_sum_kernel(cs, csh, keep_ref, got_ref, film_ref, out_ref, turn):
    v = keep_ref[0].astype(F32) + got_ref[0].astype(F32)
    turn[...] = jnp.zeros(turn.shape, F32)
    turn[0:cs, 0 : 2 * csh] = v[:, 192 : 192 + 2 * csh]
    film_ref[...] = turn[...].T[0 : 2 * csh, 0:cs]
    rows = out_ref.shape[0]
    at = 0
    for first, width, height in ((0, 128 + csh, cs), (320, HEAD_DIM, QUERIES)):
        for row in range(0, height, rows):
            size = min(rows, height - row)
            block = v[row : row + size, first : first + width]
            if size < rows:
                block = jnp.concatenate([block, jnp.zeros((rows - size, width), F32)], axis=0)
            out_ref[:, at : at + width] = block.astype(BF16)
            at += width


def output_kernel(
    cs,
    csh,
    hs,
    seq,
    peer_ref,
    *refs,
):
    ones, twos, refs = refs[:seq], refs[seq : 2 * seq], refs[2 * seq :]
    (
        queries_ref,
        wq_ref,
        step_ref,
        conv_ref,
        cond_ref,
        res_ref,
        skip_ref,
        gqueries_ref,
        gquery_ref,
        key_ref,
        value_ref,
        attn_ref,
        scr1,
        scr2,
        small,
        qscr,
        dq,
    ) = refs
    size = ones[0].shape[0]
    wide2 = scr2.shape[1]
    for k in range(seq):
        peer = peer_ref[k]
        at = 0
        bit = 1
        while bit < seq:
            at = at + lax.rem(peer // bit, 2) * (size * seq // (2 * bit))
            bit *= 2
        rows = pl.ds(pl.multiple_of(at, 8), size)
        scr1[rows] = ones[k][...].astype(F32)
        two = twos[k][...].astype(F32)
        scr2[rows] = two[:, 0:wide2]
        small[pl.ds(pl.multiple_of(peer * size, 8), size)] = two[:, wide2:]
    for t in range(4):
        rows = slice(t * cs, (t + 1) * cs)
        lanes = slice(t * LANES, (t + 1) * LANES)
        res_ref[:, lanes] = scr1[rows, 0:LANES]
        skip_ref[:, lanes] = scr1[rows, LANES : 2 * LANES]
        step_ref[:, lanes] = scr2[rows, C : C + LANES]
        if t < 3:
            conv_ref[t, :, 0:C] = scr1[rows, 2 * LANES : 2 * LANES + C]
            conv_ref[t, :, C : 2 * C] = scr2[rows, 0:C]
        else:
            cond_ref[:, 0:C] = scr1[rows, 2 * LANES : 2 * LANES + C]
            cond_ref[:, C : 2 * C] = scr2[rows, 0:C]
    dq[...] = jnp.zeros(dq.shape, F32)
    wide = 128 + csh
    for head in range(HEADS):
        cols = slice(head * HEAD_DIM, (head + 1) * HEAD_DIM)
        v = small[head * hs * size : (head * hs + 1) * size]
        for k in range(1, hs):
            v = v + small[(head * hs + k) * size : (head * hs + k + 1) * size]
        at = 0
        for row in range(0, cs, size):
            key_ref[row : row + size, cols] = v[:, at : at + 64]
            value_ref[row : row + size, cols] = v[:, at + 64 : at + 128]
            at += wide
        for row in range(0, QUERIES, size):
            count = min(size, QUERIES - row)
            dq[row : row + count, cols] = v[0:count, at : at + HEAD_DIM]
            at += HEAD_DIM
    for s in range(seq):
        v = small[s * size : (s + 1) * size]
        at = 128
        for row in range(0, cs, size):
            attn_ref[row : row + size, s * csh : (s + 1) * csh] = v[:, at : at + csh]
            at += wide
    qscr[...] = jnp.zeros((LANES, LANES), F32)
    qscr[0:QUERIES, 0:cs] = queries_ref[...].astype(F32)
    qt = qscr[...].T.astype(BF16)
    d = dq[...]
    hi = d.astype(BF16)
    lo = (d - hi.astype(F32)).astype(BF16)
    gquery_ref[...] = (nn(qt, hi) + nn(qt, lo))[0:cs]
    gqueries_ref[...] = fold(nt(parts(d[0:QUERIES], 2), wq_ref[...]), 2)


def attention_back_kernel(
    rows,
    csh,
    dp,
    off_ref,
    prow,
    probs_ref,
    u_ref,
    qp_ref,
    qkv_ref,
    pooled_ref,
    memory_ref,
    dfilm_ref,
    got_ref,
    keep_ref,
    give_ref,
    ds,
    stack,
    right,
    out,
):
    count = got_ref.shape[0]
    total = prow.shape[1] * prow.shape[2]
    cs = C // dp
    table = prow[...].reshape(rows * total, C)
    wk, wv = qkv_ref[64:128], qkv_ref[128:192]
    datt = got_ref[0, 3 * RP : 4 * RP, 0:HEAD_DIM]
    dmem = got_ref[0, 2 * RP : 3 * RP, 0:csh]
    for s in range(1, count):
        datt = datt + got_ref[s, 3 * RP : 4 * RP, 0:HEAD_DIM]
        dmem = dmem + got_ref[s, 2 * RP : 3 * RP, 0:csh]
    datt = datt * (1.0 / QUERIES)
    vh = fold(nn(parts(datt, 2), wv), 2)
    dp_all = fold(nt(parts(vh, 2), table), 2)
    for r in range(rows):
        cols = slice(r * total, (r + 1) * total)
        p = probs_ref[:, cols]
        dpr = dp_all[r : r + 1, cols]
        inner = jnp.sum(p * dpr, axis=1, keepdims=True)
        ds[:, cols] = p * (dpr - inner)
    tt = fold(nn(parts(ds[...], 2), table), 2)
    scale = 1.0 / math.sqrt(HEAD_DIM)
    dq = fold(nt(parts(tt, 2), wk), 2) * scale
    stack[...] = jnp.zeros(stack.shape, F32)
    stack[0:QUERIES] = tt
    stack[32:48] = u_ref[...]
    stack[48:64] = pooled_ref[...].astype(F32)
    stack[64:80] = memory_ref[...].astype(F32)
    right[...] = jnp.zeros(right.shape, F32)
    right[0:32, 0:64] = qp_ref[...] * scale
    right[32:48, 64:128] = datt
    right[48:64, 128 : 128 + csh] = dmem
    right[64:80, 192 : 192 + 2 * csh] = dfilm_ref[...].astype(F32)
    out[...] = lax.dot_general(
        stack[...].T,
        right[...],
        (((1,), (0,)), ((), ())),
        precision=lax.Precision.HIGHEST,
        preferred_element_type=F32,
    )
    for k in range(dp):
        ref = (keep_ref, give_ref)[k % 2]
        v = out[pl.ds(pl.multiple_of(off_ref[k], 16), cs)].astype(BF16)
        ref[k // 2] = v
        ref[k // 2, 0:QUERIES, 320:384] = dq.astype(BF16)


def exchange(pieces, axis, groups=None):
    return lax.all_to_all(
        pieces, axis, split_axis=0, concat_axis=0, axis_index_groups=groups, tiled=True
    )


def flipped(v, axis, size, bit):
    return lax.ppermute(v, axis, [(d, d ^ bit) for d in range(size)])


class Reduction:
    def __init__(self, call, name, keep, give, dp, seq, index):
        self.call, self.name, self.dp, self.seq, self.index = call, name, dp, seq, index
        self.keep, self.flip = keep, 1
        self.got = flipped(give, "dp", dp, 1)

    def over_blocks(self, after=(), others=()):
        while 2 * self.flip < self.dp:
            group = (self,) + tuple(others)
            others = ()
            args = []
            for part in group:
                args += [part.keep, Got(part.got)]
            width = sum(part.keep.shape[2] for part in group)
            half = sds((self.keep.shape[0] // 2, self.keep.shape[1], width), BF16)
            self.keep, give = self.call(
                functools.partial(add_blocks_kernel, len(group)),
                (half, half),
                "blocks_" + self.name,
                args,
                after=after,
                in_specs=[VM] * len(args),
                out_specs=(VM, VM),
            )
            self.flip *= 2
            self.got = flipped(give, "dp", self.dp, self.flip)
        self.rest, self.bit = (self.keep.shape[1:], 1)

    def over_half(self, after=()):
        rows, width = self.rest
        half = sds((rows // 2, width), BF16)
        self.keep, give = self.call(
            functools.partial(add_halves_kernel, self.bit),
            (half, half),
            "half" + str(self.bit) + "_" + self.name,
            (self.index, self.keep.reshape(rows, width), Got(self.got.reshape(rows, width))),
            after=after,
            in_specs=[SM, VM, VM],
            out_specs=(VM, VM),
            scratch_shapes=[pltpu.VMEM((rows, width), F32)],
        )
        self.got = flipped(give, "seq", self.seq, self.bit)
        self.rest, self.bit = (rows // 2, width), 2 * self.bit

    def over_last(self, after=(), extra=None):
        rows, width = self.rest
        args = (self.keep, Got(self.got))
        if extra is not None:
            args += (extra,)
            width += extra.shape[1]
        piece = self.call(
            add_last_kernel,
            sds((rows, width), BF16),
            "last_" + self.name,
            args,
            after=after,
            in_specs=[VM] * len(args),
            out_specs=VM,
        )
        have = {0: piece}
        bit = self.seq // 2
        while bit:
            for k in sorted(have):
                have[k + bit] = flipped(have[k], "seq", self.seq, bit)
            bit //= 2
        return [have[k] if k == 0 else Got(have[k]) for k in range(self.seq)]


def body(
    dp,
    seq,
    x_in,
    cond,
    segment_ids,
    diffusion_steps,
    prompt,
    prompt_lengths,
    w_step,
    w_conv,
    w_cond,
    w_res,
    w_skip,
    queries,
    w_query,
    w_key,
    w_value,
    w_attn_out,
    w_film,
    d_out,
    d_skip,
):
    call = Caller()
    rows = x_in.shape[0]
    frames = x_in.shape[2]
    steps = rows // NR
    cols = rows * frames
    cs = C // dp
    csh = C // seq
    hs = max(1, seq // HEADS)
    arows = rows // hs
    pl_local = prompt.shape[1]
    prompt_all = pl_local * seq
    sidx = lax.axis_index("seq")
    didx = lax.axis_index("dp")
    head = sidx // hs
    part = sidx % hs
    up = [(i, i + 1) for i in range(seq - 1)]
    down = [(i + 1, i) for i in range(seq - 1)]
    order = jnp.bitwise_xor(didx, jnp.arange(dp, dtype=jnp.int32)).astype(jnp.int32)
    offsets = order * cs
    index = sidx.astype(jnp.int32).reshape(1)
    peers = jnp.bitwise_xor(sidx, jnp.arange(seq, dtype=jnp.int32)).astype(jnp.int32)

    def gather(pack):
        have = {0: pack}
        flip = dp // 2
        while flip:
            for k in sorted(have):
                have[k + flip] = flipped(have[k], "dp", dp, flip)
            flip //= 2
        return [have[k] if k == 0 else Got(have[k]) for k in range(dp)]

    plain = call(
        functools.partial(plain_pack_kernel, cs, csh),
        sds((cs, PLAIN + 2 * C), BF16),
        "plain_pack",
        (
            head.astype(jnp.int32).reshape(1),
            w_res,
            w_skip,
            w_attn_out,
            w_step,
            jnp.transpose(w_film, (1, 2, 0)).reshape(2 * csh, cs),
            w_query,
            w_key,
            w_value,
            queries,
        ),
        nbytes=2e6,
        in_specs=[SM] + [VM] * 9,
        out_specs=VM,
        scratch_shapes=[pltpu.VMEM((2 * LANES, LANES), F32)],
    )
    plain = gather(plain)
    turned = call(
        functools.partial(turned_pack_kernel, cs),
        sds((2 * C, 4 * cs), BF16),
        "turned_pack",
        (w_conv, w_cond),
        after=("plain_pack",),
        nbytes=2e6,
        in_specs=[VM, VM],
        out_specs=VM,
        scratch_shapes=[pltpu.VMEM((4 * cs, 2 * C), BF16)],
    )
    turned = gather(turned)
    first, last = call(
        edge_kernel,
        (sds((C, LANES), BF16), sds((C, LANES), BF16)),
        "edges",
        (x_in,),
        after=("turned_pack",),
        nbytes=4e6,
        in_specs=[VM],
        out_specs=(VM, VM),
    )
    halves = prompt.reshape(hs, arows, pl_local, C)
    prompts = []
    for k in range(seq):
        piece = halves[0]
        if hs > 1:
            piece = lax.dynamic_index_in_dim(halves, (sidx ^ k) % hs, 0, keepdims=False)
        prompts.append(piece if k == 0 else Got(flipped(piece, "seq", seq, k)))
    left_halo = lax.ppermute(last, "seq", up)
    right_halo = lax.ppermute(first, "seq", down)

    block_ids = segment_ids[:, ::frames]
    padded_ids = jnp.pad(block_ids, ((0, 0), (1, 1)), constant_values=-1)
    mine = lax.dynamic_slice_in_dim(padded_ids, sidx, 3, 1)
    flags = jnp.stack([mine[:, 0] == mine[:, 1], mine[:, 2] == mine[:, 1]]).astype(jnp.int32)
    block_ids = jnp.pad(block_ids, ((0, RP - rows), (0, 0)))
    half = C // 2
    frequency = jnp.exp(jnp.arange(half, dtype=F32) * (-math.log(10000.0) / half))
    step_rows = jnp.pad(diffusion_steps.astype(F32), (0, LANES - rows))
    live_rows = jnp.arange(LANES, dtype=jnp.int32)[:, None] < rows
    angles = step_rows[:, None] * frequency[None, :]
    embedding = jnp.concatenate([jnp.sin(angles), jnp.cos(angles)], axis=1)
    embedding = jnp.where(live_rows, embedding, 0.0).astype(BF16)
    lengths = lax.dynamic_slice_in_dim(prompt_lengths, part * arows, arows, 0)

    apack, prow, probs, u, pooled_head, qp, qkv = call(
        functools.partial(attention_kernel, arows, dp, seq, 2 * C + 2 * csh),
        (
            sds((C, PLAIN), BF16),
            sds((arows, seq, pl_local, C), BF16),
            sds((QUERIES, arows * prompt_all), F32),
            sds((RP, C), F32),
            sds((RP, LANES), F32),
            sds((QUERIES, HEAD_DIM), F32),
            sds((256, C), BF16),
        ),
        "attention",
        (offsets, peers, lengths, *plain, *prompts),
        in_specs=[SM, SM, SM] + [HB] * (dp + seq),
        out_specs=(VM,) * 7,
        scratch_shapes=[
            pltpu.VMEM((RP, arows * prompt_all), F32),
            pltpu.SemaphoreType.DMA((dp + seq,)),
        ],
    )

    row_block = pl.BlockSpec((NR, C, LANES), lambda i: (i, 0, 0))

    def col_block(height):
        return pl.BlockSpec((height, NR * LANES), lambda i: (0, i))

    def still(shape):
        return pl.BlockSpec(shape, lambda i: (0,) * len(shape))

    inp, gated, factor_a, factor_b, skip_out, mid, stats = call(
        functools.partial(forward_kernel, dp, csh),
        (
            sds((4 * C, cols), BF16),
            sds((C, cols), BF16),
            sds((C, cols), BF16),
            sds((C, cols), BF16),
            sds(x_in.shape, BF16),
            sds((C, cols), BF16),
            sds((seq, 3 * RP, 2 * csh), F32),
        ),
        "wavenet",
        (
            offsets,
            flags,
            x_in,
            cond,
            d_out,
            Got(left_halo),
            Got(right_halo),
            embedding,
            pooled_head,
            *turned,
            *plain,
        ),
        flops=2 * cols * (4 * C * 2 * C + 2 * C * C),
        nbytes=30e6,
        grid=(steps,),
        in_specs=[
            SM,
            SM,
            row_block,
            row_block,
            row_block,
            whole((C, LANES)),
            whole((C, LANES)),
            whole((LANES, C)),
            whole((RP, LANES)),
        ]
        + [HB] * (2 * dp),
        out_specs=(
            col_block(4 * C),
            col_block(C),
            col_block(C),
            col_block(C),
            row_block,
            col_block(C),
            still((seq, 3 * RP, 2 * csh)),
        ),
        scratch_shapes=[
            pltpu.VMEM((2 * C, 4 * C), BF16),
            pltpu.VMEM((C, 2 * C), BF16),
            pltpu.VMEM((C, C), BF16),
            pltpu.VMEM((2 * C, C), BF16),
            pltpu.VMEM((C, LANES), F32),
            pltpu.VMEM((C, LANES), F32),
            pltpu.SemaphoreType.DMA((3 * dp,)),
        ],
    )
    stats_got = exchange(stats, "seq")
    gskip = call(
        skip_grad_kernel,
        sds((C, C), BF16),
        "skip",
        (gated, d_skip),
        in_specs=[VM, VM],
        out_specs=VM,
        scratch_shapes=[pltpu.VMEM((C, cols), BF16)],
    )

    coef_out, dfilm, pooled, memory = call(
        functools.partial(stats_kernel, csh, hs, arows),
        (
            sds((seq, 4 * RP, 2 * csh), F32),
            sds((RP, 2 * csh), BF16),
            sds((RP, C), BF16),
            sds((RP, C), BF16),
        ),
        "segments",
        (block_ids, Got(stats_got), apack),
        after=("skip",),
        in_specs=[VM, VM, VM],
        out_specs=(VM, VM, VM, VM),
        scratch_shapes=[pltpu.VMEM((RP, C), F32)],
    )
    coef = Got(exchange(coef_out, "seq"))

    def gate_block(i):
        return jnp.minimum(i, steps - 1)

    def shard(i):
        return jnp.maximum(i - steps, 0)

    def gate_cols(height):
        return pl.BlockSpec((height, NR * LANES), lambda i, order: (0, gate_block(i)))

    gate_rows = pl.BlockSpec((NR, C, LANES), lambda i, order: (gate_block(i), 0, 0))
    wide1, wide2 = C + 2 * LANES, C

    def part(width):
        return sds((dp // 2, 4 * cs, width), BF16)

    def part_spec(width):
        return pl.BlockSpec((1, 4 * cs, width), lambda i, order: (shard(i) // 2, 0, 0))

    outs = call(
        functools.partial(backward_kernel, dp, csh, steps),
        (
            sds((2 * C, cols), BF16),
            sds((C, cols), BF16),
            sds((2 * C, LANES), F32),
            part(wide1),
            part(wide2),
            part(wide1),
            part(wide2),
        ),
        "backward",
        (order, offsets, coef, mid, d_out, d_skip, factor_a, factor_b, inp, gated, gskip, flags, *plain),
        prefetch=1,
        grid=(steps + dp,),
        in_specs=[
            SM,
            pl.BlockSpec(
                (seq, 4 * RP, 2 * csh), lambda i, order: (0, 0, 0), pipeline_mode=pl.Buffered(1)
            ),
            gate_cols(C),
            gate_rows,
            gate_rows,
            gate_cols(C),
            gate_cols(C),
            pl.BlockSpec((4 * cs, cols), lambda i, order: (order[shard(i)], 0)),
            pl.BlockSpec((cs, cols), lambda i, order: (order[shard(i)], 0)),
            pl.BlockSpec((cs, C), lambda i, order: (order[shard(i)], 0)),
            SM,
        ]
        + [HB] * dp,
        out_specs=(
            gate_cols(2 * C),
            gate_cols(C),
            pl.BlockSpec((2 * C, LANES), lambda i, order: (0, 0)),
            part_spec(wide1),
            part_spec(wide2),
            part_spec(wide1),
            part_spec(wide2),
        ),
        scratch_shapes=[
            pltpu.VMEM((LANES, C), F32),
            pltpu.VMEM((C, LANES), F32),
            pltpu.VMEM((C, 2 * C), BF16),
            pltpu.VMEM((2 * C, NR * LANES), BF16),
            pltpu.VMEM((cols, 2 * C), BF16),
            pltpu.VMEM((cols, C), BF16),
            pltpu.SemaphoreType.DMA((dp,)),
        ],
    )
    dpre, dres, sums = outs[0:3]
    part1 = Reduction(call, "1", outs[3], outs[5], dp, seq, index)
    part2 = Reduction(call, "2", outs[4], outs[6], dp, seq, index)
    part1.over_blocks()
    keep, give = call(
        functools.partial(step_grad_kernel, dp),
        (part(LANES), part(LANES)),
        "step_grad",
        (offsets, sums, embedding, *turned),
        after=("blocks_1",),
        in_specs=[SM, VM, VM] + [HB] * dp,
        out_specs=(VM, VM),
        scratch_shapes=[
            pltpu.VMEM((2 * C, 4 * C), BF16),
            pltpu.VMEM((C, C), F32),
            pltpu.SemaphoreType.DMA((dp,)),
        ],
    )
    part_step = Reduction(call, "step", keep, give, dp, seq, index)

    block = sds((dp // 2, cs, 384), BF16)
    keep, give = call(
        functools.partial(attention_back_kernel, arows, csh, dp),
        (block, block),
        "attention_back",
        (offsets, prow, probs, u, qp, qkv, pooled, memory, dfilm, coef),
        after=("step_grad",),
        in_specs=[SM] + [VM] * 9,
        out_specs=(VM, VM),
        scratch_shapes=[
            pltpu.VMEM((QUERIES, arows * prompt_all), F32),
            pltpu.VMEM((LANES, C), F32),
            pltpu.VMEM((LANES, 384), F32),
            pltpu.VMEM((C, 384), F32),
        ],
    )
    small = Reduction(call, "small", keep, give, dp, seq, index)
    part2.over_blocks(("attention_back",), (part_step,))
    small.over_blocks(("blocks_2",))
    part1.over_half(("blocks_small",))

    base, first, last = call(
        functools.partial(input_grad_kernel, dp),
        (sds((C, cols), BF16), sds((C, LANES), BF16), sds((C, LANES), BF16)),
        "input_grad",
        (offsets, dpre, dres, *turned),
        after=("half1_1",),
        grid=(steps,),
        in_specs=[SM, col_block(2 * C), col_block(C)] + [HB] * dp,
        out_specs=(
            col_block(C),
            still((C, LANES)),
            still((C, LANES)),
        ),
        scratch_shapes=[
            pltpu.VMEM((2 * C, 4 * C), BF16),
            pltpu.VMEM((3, C, 2 * C), BF16),
            pltpu.VMEM((C, LANES), F32),
            pltpu.VMEM((C, LANES), F32),
            pltpu.SemaphoreType.DMA((dp,)),
        ],
    )
    from_left = lax.ppermute(last, "seq", up)
    from_right = lax.ppermute(first, "seq", down)
    rest = 4 * cs // seq
    small_width = (cs // rest) * (128 + csh) + max(1, QUERIES // rest) * HEAD_DIM
    grad_film, small_piece = call(
        functools.partial(small_sum_kernel, cs, csh),
        (sds((2 * csh, cs), F32), sds((rest, small_width), BF16)),
        "small_sum",
        (small.keep, Got(small.got)),
        after=("input_grad",),
        in_specs=[VM, VM],
        out_specs=(VM, VM),
        scratch_shapes=[pltpu.VMEM((LANES, LANES), F32)],
    )
    part1.over_half(("input_grad",))
    part2.over_half()
    while part1.bit < seq:
        part1.over_half()
    ones = part1.over_last()
    while part2.bit < seq:
        part2.over_half()
    grad_input, layer_out = call(
        functools.partial(finish_kernel, csh),
        (sds(x_in.shape, BF16), sds(x_in.shape, BF16)),
        "grad_input",
        (flags, base, Got(from_left), Got(from_right), mid, coef),
        after=("half2_2",),
        grid=(steps,),
        in_specs=[
            SM,
            col_block(C),
            whole((C, LANES)),
            whole((C, LANES)),
            col_block(C),
            whole((seq, 4 * RP, 2 * csh)),
        ],
        out_specs=(row_block, row_block),
        scratch_shapes=[pltpu.VMEM((LANES, C), F32), pltpu.VMEM((C, LANES), F32)],
    )
    twos = part2.over_last(("grad_input",), small_piece)

    (
        grad_step,
        grad_conv,
        grad_cond,
        grad_res,
        grad_skip,
        grad_queries,
        grad_query,
        grad_key,
        grad_value,
        grad_attn,
    ) = call(
        functools.partial(output_kernel, cs, csh, hs, seq),
        (
            sds((cs, C), F32),
            sds((3, cs, 2 * C), F32),
            sds((cs, 2 * C), F32),
            sds((cs, C), F32),
            sds((cs, C), F32),
            sds((QUERIES, cs), F32),
            sds((cs, C), F32),
            sds((cs, C), F32),
            sds((cs, C), F32),
            sds((cs, C), F32),
        ),
        "outputs",
        (peers, *ones, *twos, queries, w_query),
        in_specs=[SM] + [VM] * (2 * seq + 2),
        out_specs=(VM,) * 10,
        scratch_shapes=[
            pltpu.VMEM((4 * cs, wide1), F32),
            pltpu.VMEM((4 * cs, wide2 + LANES), F32),
            pltpu.VMEM((4 * cs, small_width), F32),
            pltpu.VMEM((LANES, LANES), F32),
            pltpu.VMEM((LANES, C), F32),
        ],
    )
    return (
        layer_out,
        skip_out,
        grad_input,
        grad_step,
        grad_conv,
        grad_cond,
        grad_res,
        grad_skip,
        grad_queries,
        grad_query,
        grad_key,
        grad_value,
        grad_attn,
        jnp.transpose(grad_film.reshape(2, csh, cs), (2, 0, 1)),
    )


def solution(mesh):
    frames = P("dp", None, "seq")
    matrix = P("dp", None)
    return jax.shard_map(
        functools.partial(body, mesh.shape["dp"], mesh.shape["seq"]),
        mesh=mesh,
        in_specs=(
            frames,
            frames,
            P("dp", None),
            P("dp"),
            P("dp", "seq", None),
            P("dp"),
            matrix,
            P(None, "dp", None),
            matrix,
            matrix,
            matrix,
            P(None, "dp"),
            matrix,
            matrix,
            matrix,
            matrix,
            frames,
            frames,
            frames,
        ),
        out_specs=(
            frames,
            frames,
            frames,
            matrix,
            P(None, "dp", None),
            matrix,
            matrix,
            matrix,
            P(None, "dp"),
            matrix,
            matrix,
            matrix,
            matrix,
            frames,
        ),
        check_vma=False,
    )
```

```python
import functools
import math

import jax
import jax.numpy as jnp
from jax import lax
from jax.experimental import pallas as pl
from jax.experimental.pallas import tpu as pltpu
from jax.sharding import PartitionSpec as P

C = 512
HEADS = 8
QUERIES = 32
HEAD_DIM = 64
SHIFT = 4
SQRT_HALF = 0.7071067811865476
NORM_EPS = 1e-05
MASKED_SCORE = -1e30
LANES = 128
RP = 16
NR = 4
F32 = jnp.float32
BF16 = jnp.bfloat16
VMEM_BYTES = 50 * 1024 * 1024


def nn(a, b):
    return lax.dot_general(a, b, (((1,), (0,)), ((), ())), preferred_element_type=F32)


def nt(a, b):
    return lax.dot_general(a, b, (((1,), (1,)), ((), ())), preferred_element_type=F32)


def parts(v, count):
    out = []
    for _ in range(count):
        low = v.astype(BF16).astype(F32)
        out.append(low)
        v = v - low
    return jnp.concatenate(out, axis=0).astype(BF16)


def fold(v, count):
    rows = v.shape[0] // count
    total = v[:rows]
    for k in range(1, count):
        total = total + v[k * rows : (k + 1) * rows]
    return total


def lane_ids(shape):
    return lax.broadcasted_iota(jnp.int32, shape, len(shape) - 1)


def sds(shape, dtype):
    return jax.ShapeDtypeStruct(shape, dtype)


VM = pl.BlockSpec(memory_space=pltpu.VMEM)
HB = pl.BlockSpec(memory_space=pl.ANY)
SM = pl.BlockSpec(memory_space=pltpu.SMEM)


def whole(shape):
    return pl.BlockSpec(shape, lambda i: (0,) * len(shape), pipeline_mode=pl.Buffered(1))


class Got:
    def __init__(self, array):
        self.array = array


class Caller:
    def __init__(self):
        self.done = {}

    def __call__(self, kernel, out_shape, name, args, flops=0, nbytes=0, prefetch=0, after=(), **kw):
        single = not isinstance(out_shape, tuple)
        shapes = (out_shape,) if single else out_shape
        pinned = tuple(pltpu.HBM(v.shape, v.dtype) for v in shapes)
        in_specs = list(kw.pop("in_specs"))
        count = prefetch + len(in_specs)
        args = list(args)
        extra = len(after)
        for before in after:
            in_specs.append(HB)
            args.append(self.done[before])

        def run(*refs):
            return kernel(*refs[:count], *refs[count + extra :])

        values = []
        for k, v in enumerate(args):
            spec = SM if k < prefetch else in_specs[k - prefetch]
            if isinstance(v, Got):
                values.append(v.array)
            elif spec is SM:
                values.append(v)
            else:
                values.append(pltpu.with_memory_space_constraint(v, pltpu.HBM))
        spec = pltpu.PrefetchScalarGridSpec(
            num_scalar_prefetch=prefetch,
            grid=kw.pop("grid", ()),
            in_specs=in_specs,
            out_specs=kw.pop("out_specs"),
            scratch_shapes=kw.pop("scratch_shapes", ()),
        )
        out = pl.pallas_call(
            run,
            out_shape=pinned[0] if single else pinned,
            name=name,
            grid_spec=spec,
            cost_estimate=pl.CostEstimate(
                flops=1, bytes_accessed=1, transcendentals=0
            ),
            compiler_params=pltpu.CompilerParams(vmem_limit_bytes=VMEM_BYTES),
        )(*values)
        self.done[name] = out if single else out[0]
        return out


def head_pack_kernel(
    csh,
    local,
    group_ref,
    bit_ref,
    attn_ref,
    film_ref,
    wq_ref,
    wk_ref,
    wv_ref,
    queries_ref,
    prompt_ref,
    out_ref,
    mine_ref,
    other_ref,
    scr,
):
    cs = attn_ref.shape[0]
    arows = mine_ref.shape[0]
    mine_ref[...] = prompt_ref[pl.ds(bit_ref[0] * arows, arows)]
    other_ref[...] = prompt_ref[pl.ds((1 - bit_ref[0]) * arows, arows)]
    out_ref[:, 0:C] = attn_ref[...]
    off = C
    scr[...] = jnp.zeros((2 * LANES, LANES), F32)
    scr[0 : 2 * csh, 0:cs] = film_ref[...].astype(F32)
    scr[LANES : LANES + QUERIES, 0:cs] = queries_ref[...].astype(F32)
    film = scr[0:LANES].T[0:cs]
    table = scr[LANES : 2 * LANES].T[0:cs]
    turn = lax.rem(C - local * group_ref[0], C)
    blocks = [film[:, 0 : 2 * csh]]
    for ref in (wq_ref, wk_ref, wv_ref):
        blocks.append(pltpu.roll(ref[...].astype(F32), turn, 1)[:, 0:local])
    blocks.append(table)
    for block in blocks:
        width = min(block.shape[1], out_ref.shape[1] - off)
        out_ref[:, off : off + width] = block[:, 0:width].astype(BF16)
        off += width
    if off < out_ref.shape[1]:
        out_ref[:, off:] = jnp.zeros((cs, out_ref.shape[1] - off), BF16)


def turned_pack_kernel(cs, bit_ref, conv_ref, cond_ref, res_ref, skip_ref, step_ref, out_ref, half_ref, scr):
    half = cs // 2
    size = half_ref.shape[0]
    for k in range(3):
        scr[k * cs : (k + 1) * cs] = conv_ref[k]
    scr[3 * cs : 4 * cs] = cond_ref[...]
    turned = scr[...].T
    for h in range(2):
        out_ref[h * size : h * size + C] = turned[h * C : (h + 1) * C]
        at = h * size + C
        for ref in (res_ref, skip_ref, step_ref):
            for lane in range(0, C, 4 * cs):
                out_ref[at : at + half] = ref[h * half : (h + 1) * half, lane : lane + 4 * cs]
                at += half
    half_ref[...] = out_ref[pl.ds(pl.multiple_of(bit_ref[0] * size, 16), size)]


def pair_kernel(a_ref, b_ref, out_ref):
    out_ref[0] = a_ref[...]
    out_ref[1] = b_ref[...]


def edge_kernel(x_ref, first_ref, last_ref):
    rows = x_ref.shape[0]
    lane = lane_ids((C, LANES))
    first = jnp.zeros((C, LANES), F32)
    last = jnp.zeros((C, LANES), F32)
    for r in range(rows):
        v = x_ref[r].astype(F32)
        here = (lane // SHIFT) == r
        first = jnp.where(here, pltpu.roll(v, SHIFT * r, 1) if r else v, first)
        last = jnp.where(here, pltpu.roll(v, SHIFT * r + SHIFT, 1), last)
    first_ref[...] = first.astype(BF16)
    last_ref[...] = last.astype(BF16)


def begin(copies):
    for copy in copies:
        copy.start()


def finish(copies):
    for copy in copies:
        copy.wait()


def half_shards(meta, refs, off_ref):
    dp = len({k for k, _ in meta})
    out = []
    for (k, which), ref in zip(meta, refs):
        if which is None:
            size = ref.shape[0] // 2
            out.append((k, 0, ref, 0, size))
            out.append((k, 1, ref, size, size))
        else:
            out.append((k, off_ref[dp + which], ref, 0, ref.shape[0]))
    return out


def turned_copies(meta, refs, off_ref, cs, wt, others, sems):
    half = cs // 2
    pairs = []
    for k, h, ref, first, _ in half_shards(meta, refs, off_ref):
        if wt is not None:
            row = pl.ds(pl.multiple_of(h * C, 16), C)
            lanes = pl.ds(pl.multiple_of(off_ref[k] * 4, LANES), 4 * cs)
            pairs.append((ref.at[pl.ds(first, C)], wt.at[row, lanes]))
        at = first + C
        for other in others:
            for lane in range(0, C, 4 * cs):
                if other is not None:
                    dst, start = other
                    row = pl.ds(pl.multiple_of(off_ref[k] + h * half, 16), half)
                    lanes = pl.ds(start + lane, 4 * cs)
                    pairs.append((ref.at[pl.ds(at, half)], dst.at[row, lanes]))
                at += half
    return [pltpu.make_async_copy(a, b, sems.at[n]) for n, (a, b) in enumerate(pairs)]


def head_copies(meta, refs, off_ref, dst, sems):
    pairs = []
    for k, h, ref, first, size in half_shards(meta, refs, off_ref):
        row = pl.ds(pl.multiple_of(off_ref[k] + h * size, 16), size)
        pairs.append((ref.at[pl.ds(first, size)], dst.at[row]))
    return [pltpu.make_async_copy(a, b, sems.at[n]) for n, (a, b) in enumerate(pairs)]


def forward_kernel(
    meta, dp, csh, off_ref, flags_ref, x_ref, cond_ref, dout_ref, left_ref, right_ref, emb_ref, pooled_ref, *refs
):
    turned, refs = refs[: len(meta)], refs[len(meta) :]
    (
        inp_ref,
        gated_ref,
        fa_ref,
        fb_ref,
        skip_ref,
        mid_ref,
        stats_ref,
        wt_ref,
        rn_ref,
        step_ref,
        rst_ref,
        lift_ref,
        acc_ref,
        sems,
    ) = refs
    cs = C // dp
    i = pl.program_id(0)
    lane = lane_ids((C, LANES))

    @pl.when(i == 0)
    def _():
        copies = turned_copies(
            meta,
            turned,
            off_ref,
            cs,
            wt_ref,
            ((rn_ref, 0), (rn_ref, C), (step_ref, 0)),
            sems,
        )
        begin(copies)
        acc_ref[...] = jnp.zeros((C, LANES), F32)
        finish(copies)
        lift = nn(emb_ref[0:RP], step_ref[...])
        lift = jnp.concatenate([lift, jnp.zeros((LANES - RP, C), F32)], axis=0)
        lift_ref[...] = lift.T
        rst_ref[...] = rn_ref[...].T

    lift = pltpu.roll(lift_ref[...], lax.rem(LANES - NR * i, LANES), 1)
    left = left_ref[...].astype(F32)
    right = right_ref[...].astype(F32)

    def put(tap, cols, value):
        for d in range(dp):
            at = d * 4 * cs + tap * cs
            inp_ref[at : at + cs, cols] = value[d * cs : (d + 1) * cs]

    for j in range(NR):
        r = NR * i + j
        lc = lift[:, j : j + 1]
        sh = (x_ref[j].astype(F32) + lc).astype(BF16)
        shf = sh.astype(F32)
        lh = pltpu.roll(left, lax.rem(LANES - SHIFT * r, LANES), 1)
        lh = jnp.where(flags_ref[0, r] > 0, (lh + lc).astype(BF16).astype(F32), 0.0)
        rh = pltpu.roll(right, LANES - SHIFT - SHIFT * r, 1)
        rh = jnp.where(flags_ref[1, r] > 0, (rh + lc).astype(BF16).astype(F32), 0.0)
        cols = slice(j * LANES, (j + 1) * LANES)
        put(0, cols, jnp.where(lane < SHIFT, lh, pltpu.roll(shf, SHIFT, 1)).astype(BF16))
        put(1, cols, sh)
        put(
            2,
            cols,
            jnp.where(lane >= LANES - SHIFT, rh, pltpu.roll(shf, LANES - SHIFT, 1)).astype(BF16),
        )
        put(3, cols, cond_ref[j])
    pre = nn(wt_ref[...], inp_ref[...])
    th = jnp.tanh(pre[:C])
    sg = jax.nn.sigmoid(pre[C:])
    gf = th * sg
    fa_ref[...] = (sg - gf * th).astype(BF16)
    fb_ref[...] = (gf * (1.0 - sg)).astype(BF16)
    g = gf.astype(BF16)
    gated_ref[...] = g
    rs = nn(rst_ref[...], g)
    acc = acc_ref[...]
    for j in range(NR):
        r = NR * i + j
        cols = slice(j * LANES, (j + 1) * LANES)
        skip_ref[j] = rs[C:, cols].astype(BF16)
        mid = ((x_ref[j].astype(F32) + rs[:C, cols]) * SQRT_HALF).astype(BF16)
        mid_ref[:, cols] = mid
        mf = mid.astype(F32)
        df = dout_ref[j].astype(F32)
        total = jnp.sum(mf, axis=1, keepdims=True)
        dev = mf - total * (1.0 / LANES)
        acc = jnp.where(lane == r, total, acc)
        acc = jnp.where(lane == RP + r, jnp.sum(dev * dev, axis=1, keepdims=True), acc)
        acc = jnp.where(lane == 2 * RP + r, jnp.sum(df, axis=1, keepdims=True), acc)
        acc = jnp.where(lane == 3 * RP + r, jnp.sum(df * dev, axis=1, keepdims=True), acc)
    acc_ref[...] = acc

    @pl.when(i == pl.num_programs(0) - 1)
    def _():
        t = acc.T
        for s in range(C // csh):
            cols = slice(s * csh, (s + 1) * csh)
            stats_ref[s, 0 : 2 * RP, 0:csh] = t[0 : 2 * RP, cols]
            stats_ref[s, 0 : 2 * RP, csh : 2 * csh] = t[2 * RP : 4 * RP, cols]
            stats_ref[s, 2 * RP : 3 * RP] = pooled_ref[:, 0 : 2 * csh]


def attention_kernel(meta, rows, heads, pairs, off, off_ref, peer_ref, len_ref, *refs):
    pieces, refs = refs[: len(meta)], refs[len(meta) :]
    prompts, refs = refs[:pairs], refs[pairs:]
    apack_ref, prow, probs_ref, u_ref, pooled_ref, qp_ref, qkv_ref, abd, sems = refs
    copies = head_copies(meta, pieces, off_ref, apack_ref, sems)
    count = len(copies)
    for j in range(pairs):
        for i in range(2):
            copies.append(
                pltpu.make_async_copy(
                    prompts[j].at[i], prow.at[:, 2 * j + i], sems.at[count + 2 * j + i]
                )
            )
    begin(copies)
    local = prow.shape[2]
    total = 2 * pairs * local
    abd[...] = jnp.zeros(abd.shape, F32)
    lane = lane_ids((heads * QUERIES, total))
    place = jnp.zeros((heads * QUERIES, total), jnp.int32)
    for k in range(2 * pairs):
        place = jnp.where(lane // local == k, peer_ref[k] * local + lane % local, place)
    finish(copies)
    wide = heads * HEAD_DIM
    qkv = apack_ref[:, off : off + qkv_ref.shape[0]].T
    qkv_ref[...] = qkv
    qp = nt(qkv[3 * wide : 3 * wide + QUERIES], qkv[0:wide])
    qp_ref[...] = qp
    st = []
    for g in range(heads):
        cols = slice(g * HEAD_DIM, (g + 1) * HEAD_DIM)
        st.append(fold(nn(parts(qp[:, cols], 3), qkv[wide + cols.start : wide + cols.stop]), 3))
    st = jnp.concatenate(st, axis=0) * (1.0 / math.sqrt(HEAD_DIM))
    table = prow[...].reshape(rows * total, C)
    scores = fold(nt(parts(st, 3), table), 3)
    for r in range(rows):
        cols = slice(r * total, (r + 1) * total)
        live = place < len_ref[r]
        s = jnp.where(live, scores[:, cols], MASKED_SCORE)
        e = jnp.where(live, jnp.exp(s - jnp.max(s, axis=1, keepdims=True)), 0.0)
        p = e / jnp.sum(e, axis=1, keepdims=True)
        probs_ref[:, cols] = p
        for g in range(heads):
            abd[8 * g + r : 8 * g + r + 1, cols] = jnp.sum(
                p[g * QUERIES : (g + 1) * QUERIES], axis=0, keepdims=True
            )
    u = fold(nn(parts(abd[...], 2), table), 2)
    u_ref[...] = u
    pooled_ref[...] = jnp.zeros(pooled_ref.shape, F32)
    for g in range(heads):
        first = 2 * wide + g * HEAD_DIM
        v = parts(u[8 * g : 8 * g + 8] * (1.0 / QUERIES), 2)
        pooled_ref[0:8, g * HEAD_DIM : (g + 1) * HEAD_DIM] = fold(
            nt(v, qkv[first : first + HEAD_DIM]), 2
        )


def stats_kernel(
    csh, heads, rows, seg_ref, x_ref, apack_ref, out_ref, dfilm_ref, pooled_ref, memory_ref, scratch
):
    count = x_ref.shape[0]
    wide = heads * HEAD_DIM
    seg = seg_ref[...]
    scratch[...] = jnp.zeros(scratch.shape, F32)
    for s in range(count):
        group, part = s // 2, s % 2
        scratch[part * rows : (part + 1) * rows, group * wide : (group + 1) * wide] = x_ref[
            s, 2 * RP : 2 * RP + rows, 0:wide
        ]
    pooled = scratch[...].astype(BF16)
    pooled_ref[...] = pooled
    memory = nn(pooled, apack_ref[:, 0:C]).astype(BF16)
    memory_ref[...] = memory
    film = nn(memory, apack_ref[:, C : C + 2 * csh])
    f0 = film[:, 0:csh]
    f1 = film[:, csh : 2 * csh]
    total = [x_ref[s, 0:RP, 0:csh] for s in range(count)]
    second = [x_ref[s, RP : 2 * RP, 0:csh] for s in range(count)]
    dsum = [x_ref[s, 0:RP, csh : 2 * csh] for s in range(count)]
    cross = [x_ref[s, RP : 2 * RP, csh : 2 * csh] for s in range(count)]
    means = [v * (1.0 / LANES) for v in total]
    d0 = jnp.zeros((RP, csh), F32)
    d1 = jnp.zeros((RP, csh), F32)
    for me in range(count):
        same = [(seg[:, s : s + 1] == seg[:, me : me + 1]).astype(F32) for s in range(count)]
        frames = sum(same) * float(LANES)
        inv = 1.0 / frames
        mean = sum(m * v for m, v in zip(same, total)) * inv
        var = (
            sum(
                m * (v + float(LANES) * (u - mean) * (u - mean))
                for m, v, u in zip(same, second, means)
            )
            * inv
        )
        scale = lax.rsqrt(var + NORM_EPS)
        dtot = sum(m * v for m, v in zip(same, dsum))
        xtot = sum(m * (v + (u - mean) * d) for m, v, u, d in zip(same, cross, means, dsum)) * scale
        mean_part = f0 * dtot * inv
        cross_part = f0 * xtot * inv
        slope = scale * scale * cross_part
        out_ref[me, 0:RP, 0:csh] = 1.0 + f0 * scale
        out_ref[me, RP : 2 * RP, 0:csh] = f1 - f0 * scale * mean
        out_ref[me, 0:RP, csh : 2 * csh] = -slope
        out_ref[me, RP : 2 * RP, csh : 2 * csh] = slope * mean - scale * mean_part
        d0 = d0 + (cross[me] + (means[me] - mean) * dsum[me]) * scale
        d1 = d1 + dsum[me]
    dfilm = jnp.concatenate([d0, d1], axis=1).astype(BF16)
    dfilm_ref[...] = dfilm
    dmem = nt(dfilm, apack_ref[:, C : C + 2 * csh])
    dpool = nt(dmem.astype(BF16), apack_ref[:, 0:C])
    for s in range(count):
        group, part = s // 2, s % 2
        rolled = pltpu.roll(dpool, RP - part * rows, 0) if part else dpool
        out_ref[s, 2 * RP : 3 * RP, 0:csh] = dmem[:, s * csh : (s + 1) * csh]
        out_ref[s, 2 * RP : 3 * RP, csh : 2 * csh] = jnp.zeros((RP, csh), F32)
        out_ref[s, 3 * RP : 4 * RP] = rolled[:, group * wide : (group + 1) * wide]


def coef_columns(csh, coef_ref, rows_ref, cols_ref):
    rows_ref[...] = jnp.zeros(rows_ref.shape, F32)
    for s in range(C // csh):
        cols = slice(s * csh, (s + 1) * csh)
        rows_ref[0 : 2 * RP, cols] = coef_ref[s, 0 : 2 * RP, 0:csh]
        rows_ref[2 * RP : 4 * RP, cols] = coef_ref[s, 0 : 2 * RP, csh : 2 * csh]
    cols_ref[...] = rows_ref[...].T


def skip_grad_kernel(gated_ref, dskip_ref, out_ref, right):
    for r in range(dskip_ref.shape[0]):
        right[:, r * LANES : (r + 1) * LANES] = dskip_ref[r]
    out_ref[...] = nt(gated_ref[...], right[...]).astype(BF16)


def backward_kernel(meta, dp, csh, gates, order_ref, off_ref, coef_ref, mid_ref, dout_ref, dskip_ref, fa_ref, fb_ref, inp_ref, gated_ref, gskip_ref, flags_ref, *refs):
    turned, refs = refs[: len(meta)], refs[len(meta) :]
    dpre_ref, dres_ref, sums_ref, refs = refs[0], refs[1], refs[2], refs[3:]
    outs, refs = (refs[0:2], refs[2:4]), refs[4:]
    rows_ref, cols_ref, w_ref, both_ref, dpt_ref, drt_ref, sems = refs
    cs = C // dp
    span = NR * LANES
    i = pl.program_id(0)

    @pl.when(i == 0)
    def _():
        copies = turned_copies(
            meta, turned, off_ref, cs, None, ((w_ref, 0), (w_ref, C), None), sems
        )
        begin(copies)
        coef_columns(csh, coef_ref, rows_ref, cols_ref)
        sums_ref[...] = jnp.zeros(sums_ref.shape, F32)
        finish(copies)

    @pl.when(i < gates)
    def _():
        coef = pltpu.roll(cols_ref[...], lax.rem(LANES - NR * i, LANES), 1)
        for j in range(NR):
            cols = slice(j * LANES, (j + 1) * LANES)
            mf = mid_ref[:, cols].astype(F32)
            df = dout_ref[j].astype(F32)
            a = coef[:, j : j + 1]
            be = coef[:, 2 * RP + j : 2 * RP + j + 1]
            ga = coef[:, 3 * RP + j : 3 * RP + j + 1]
            dmid = (a * df + (be * mf + ga)).astype(BF16).astype(F32)
            both_ref[0:C, cols] = (dmid * SQRT_HALF).astype(BF16)
            both_ref[C : 2 * C, cols] = dskip_ref[j]
        dres = both_ref[0:C]
        dres_ref[...] = dres
        dg = nn(w_ref[...], both_ref[...])
        dt = (dg * fa_ref[...].astype(F32)).astype(BF16)
        ds = (dg * fb_ref[...].astype(F32)).astype(BF16)
        dpre_ref[0:C] = dt
        dpre_ref[C : 2 * C] = ds
        at = pl.ds(pl.multiple_of(i * span, span), span)
        dpt_ref[at, 0:C] = dt.T
        dpt_ref[at, C : 2 * C] = ds.T
        drt_ref[at] = dres.T
        frame = lax.broadcasted_iota(jnp.int32, (span, LANES), 0)
        column = lane_ids((span, LANES))
        place = frame % LANES
        which = frame // LANES
        keep_l = jnp.zeros((span, LANES), jnp.int32)
        keep_r = jnp.zeros((span, LANES), jnp.int32)
        for j in range(NR):
            keep_l = jnp.where(which == j, flags_ref[0, NR * i + j], keep_l)
            keep_r = jnp.where(which == j, flags_ref[1, NR * i + j], keep_r)
        row = NR * i + which
        use0 = (column == row) & ((place >= SHIFT) | (keep_l > 0))
        use1 = column == RP + row
        use2 = (column == 2 * RP + row) & ((place < LANES - SHIFT) | (keep_r > 0))
        pick = jnp.where(use0 | use1 | use2, 1.0, 0.0).astype(BF16)
        sums_ref[...] = sums_ref[...] + nn(dpre_ref[...], pick)

    @pl.when(i >= gates)
    def _():
        g = nn(inp_ref[...], dpt_ref[...]).astype(BF16)
        h = nn(gated_ref[...], drt_ref[...]).astype(BF16)
        k = i - gates
        for parity, (one, two) in enumerate(outs):

            @pl.when(lax.rem(k, 2) == parity)
            def _():
                for t in range(4):
                    rows = slice(t * cs, (t + 1) * cs)
                    lanes = slice(t * LANES, (t + 1) * LANES)
                    one[0, rows, 0:LANES] = h[:, lanes]
                    one[0, rows, LANES : 2 * LANES] = gskip_ref[:, lanes]
                one[0, :, 2 * LANES : 6 * LANES] = g[:, 0:C]
                two[0] = g[:, C : 2 * C]


def step_grad_kernel(meta, dp, off_ref, sums_ref, emb_ref, *refs):
    turned, refs = refs[: len(meta)], refs[len(meta) :]
    keep_ref, give_ref, wt_ref, scr, sems = refs
    cs = C // dp
    copies = turned_copies(meta, turned, off_ref, cs, wt_ref, (None,) * 3, sems)
    begin(copies)
    sums = sums_ref[...].T
    emb = emb_ref[...].T
    finish(copies)
    total = jnp.zeros((RP, 4 * C), F32)
    lane = lane_ids((RP, 4 * C))
    all_taps = fold(nn(parts(sums[0 : 3 * RP], 2), wt_ref[...]), 2)
    for t in range(3):
        g = all_taps[t * RP : (t + 1) * RP]
        total = total + jnp.where((lane // cs) % 4 == t, g, 0.0)
    out = []
    for d in range(dp):
        block = total[:, d * 4 * cs : (d + 1) * 4 * cs]
        out.append(block[:, 0:cs] + block[:, cs : 2 * cs] + block[:, 2 * cs : 3 * cs])
    g = jnp.concatenate(out, axis=1)
    g = jnp.concatenate([g, jnp.zeros((LANES - RP, C), F32)], axis=0)
    hi = g.astype(BF16)
    lo = (g - hi.astype(F32)).astype(BF16)
    scr[...] = nn(emb, hi) + nn(emb, lo)
    for k in range(dp):
        v = scr[pl.ds(pl.multiple_of(off_ref[k], 16), cs)].astype(BF16)
        for t in range(4):
            (keep_ref, give_ref)[k % 2][k // 2, t * cs : (t + 1) * cs] = v[
                :, t * LANES : (t + 1) * LANES
            ]


def input_grad_kernel(meta, dp, off_ref, dpre_ref, dres_ref, *refs):
    turned, refs = refs[: len(meta)], refs[len(meta) :]
    base_ref, first_ref, last_ref, wt_ref, w_ref, facc_ref, lacc_ref, sems = refs
    cs = C // dp
    i = pl.program_id(0)
    lane = lane_ids((C, LANES))

    @pl.when(i == 0)
    def _():
        copies = turned_copies(meta, turned, off_ref, cs, wt_ref, (None,) * 3, sems)
        begin(copies)
        facc_ref[...] = jnp.zeros((C, LANES), F32)
        lacc_ref[...] = jnp.zeros((C, LANES), F32)
        finish(copies)
        for d in range(dp):
            v = wt_ref[:, d * 4 * cs : (d + 1) * 4 * cs].T
            for t in range(3):
                w_ref[t, d * cs : (d + 1) * cs] = v[t * cs : (t + 1) * cs]

    dpre = dpre_ref[...]
    y0 = nn(w_ref[0], dpre)
    y1 = nn(w_ref[1], dpre)
    y2 = nn(w_ref[2], dpre)
    facc = facc_ref[...]
    lacc = lacc_ref[...]
    for j in range(NR):
        r = NR * i + j
        cols = slice(j * LANES, (j + 1) * LANES)
        z0 = pltpu.roll(y0[:, cols], LANES - SHIFT, 1)
        z2 = pltpu.roll(y2[:, cols], SHIFT, 1)
        inner0 = lane < LANES - SHIFT
        inner2 = lane >= SHIFT
        v = y1[:, cols]
        base_ref[:, cols] = (
            v
            + jnp.where(inner0, z0, 0.0)
            + jnp.where(inner2, z2, 0.0)
            + dres_ref[:, cols].astype(F32)
        ).astype(BF16)
        here = (lane // SHIFT) == r
        facc = jnp.where(here, pltpu.roll(z0, lax.rem(SHIFT * r + SHIFT, LANES), 1), facc)
        lacc = jnp.where(here, pltpu.roll(z2, SHIFT * r, 1), lacc)
    facc_ref[...] = facc
    lacc_ref[...] = lacc

    @pl.when(i == pl.num_programs(0) - 1)
    def _():
        first_ref[...] = facc.astype(BF16)
        last_ref[...] = lacc.astype(BF16)


def finish_kernel(csh, flags_ref, base_ref, left_ref, right_ref, mid_ref, coef_ref, out_ref, layer_ref, rows_ref, cols_ref):
    i = pl.program_id(0)
    lane = lane_ids((C, LANES))

    @pl.when(i == 0)
    def _():
        coef_columns(csh, coef_ref, rows_ref, cols_ref)

    coef = pltpu.roll(cols_ref[...], lax.rem(LANES - NR * i, LANES), 1)
    left = left_ref[...].astype(F32)
    right = right_ref[...].astype(F32)
    for j in range(NR):
        r = NR * i + j
        cols = slice(j * LANES, (j + 1) * LANES)
        lh = pltpu.roll(left, lax.rem(LANES - SHIFT * r, LANES), 1)
        rh = pltpu.roll(right, LANES - SHIFT - SHIFT * r, 1)
        lh = jnp.where((lane < SHIFT) & (flags_ref[0, r] > 0), lh, 0.0)
        rh = jnp.where((lane >= LANES - SHIFT) & (flags_ref[1, r] > 0), rh, 0.0)
        out_ref[j] = (base_ref[:, cols].astype(F32) + lh + rh).astype(BF16)
        a = coef[:, j : j + 1]
        b = coef[:, RP + j : RP + j + 1]
        layer_ref[j] = (a * mid_ref[:, cols].astype(F32) + b).astype(BF16)


def add_blocks_kernel(count, *refs):
    ins, (keep_ref, give_ref) = refs[: 2 * count], refs[2 * count :]
    at = 0
    for p in range(count):
        a_ref, b_ref = ins[2 * p : 2 * p + 2]
        width = a_ref.shape[2]
        for j in range(a_ref.shape[0]):
            v = a_ref[j].astype(F32) + b_ref[j].astype(F32)
            (keep_ref, give_ref)[j % 2][j // 2, :, at : at + width] = v.astype(BF16)
        at += width


def add_halves_kernel(bit, index_ref, a_ref, b_ref, keep_ref, give_ref, scr):
    half = a_ref.shape[0] // 2
    mine = lax.rem(index_ref[0] // bit, 2)
    scr[...] = a_ref[...].astype(F32) + b_ref[...].astype(F32)
    keep_ref[...] = scr[pl.ds(pl.multiple_of(mine * half, 8), half)].astype(BF16)
    give_ref[...] = scr[pl.ds(pl.multiple_of((1 - mine) * half, 8), half)].astype(BF16)


def add_last_kernel(a_ref, b_ref, *refs):
    out_ref = refs[-1]
    width = a_ref.shape[1]
    out_ref[:, 0:width] = (a_ref[...].astype(F32) + b_ref[...].astype(F32)).astype(BF16)
    if len(refs) > 1:
        out_ref[:, width:] = refs[0][...]


def small_sum_kernel(csh, wide, bit_ref, keep_ref, got_ref, film_ref, attn_ref, mine_ref, other_ref, turn):
    v = keep_ref[0].astype(F32) + got_ref[0].astype(F32)
    cs = v.shape[0]
    film = 2 * wide + csh
    turn[...] = jnp.zeros(turn.shape, F32)
    turn[0:cs, 0 : 2 * csh] = v[:, film : film + 2 * csh]
    film_ref[...] = turn[...].T[0 : 2 * csh, 0:cs]
    attn_ref[...] = v[:, 2 * wide : film]
    last = film + 2 * csh
    even = bit_ref[0] == 0
    for one, two, rows, width in (
        (v[:, 0:wide], v[:, wide : 2 * wide], slice(0, cs), wide),
        (
            v[0:QUERIES, last : last + wide // 2],
            v[0:QUERIES, last + wide // 2 : last + wide],
            slice(cs, cs + QUERIES),
            wide // 2,
        ),
    ):
        mine_ref[rows, 0:width] = jnp.where(even, one, two).astype(BF16)
        other_ref[rows, 0:width] = jnp.where(even, two, one).astype(BF16)
    mine_ref[cs:, wide // 2 :] = jnp.zeros((QUERIES, wide // 2), BF16)
    other_ref[cs:, wide // 2 :] = jnp.zeros((QUERIES, wide // 2), BF16)


def small_piece_kernel(csh, wide, attn_ref, mine_ref, got_ref, out_ref):
    v = mine_ref[...].astype(F32) + got_ref[...].astype(F32)
    attn = attn_ref[...]
    cs = attn.shape[0]
    rows = out_ref.shape[0]
    at = 0
    for row in range(0, cs, rows):
        out_ref[:, at : at + wide] = v[row : row + rows].astype(BF16)
        out_ref[:, at + wide : at + wide + csh] = attn[row : row + rows].astype(BF16)
        at += wide + csh
    for row in range(0, QUERIES, rows):
        block = v[cs + row : cs + min(row + rows, QUERIES), 0 : wide // 2]
        if block.shape[0] < rows:
            pad = jnp.zeros((rows - block.shape[0], wide // 2), F32)
            block = jnp.concatenate([block, pad], axis=0)
        out_ref[:, at : at + wide // 2] = block.astype(BF16)
        at += wide // 2


def output_kernel(
    cs,
    csh,
    wide,
    seq,
    peer_ref,
    *refs,
):
    ones, twos, refs = refs[:seq], refs[seq : 2 * seq], refs[2 * seq :]
    (
        queries_ref,
        wq_ref,
        step_ref,
        conv_ref,
        cond_ref,
        res_ref,
        skip_ref,
        gqueries_ref,
        gquery_ref,
        key_ref,
        value_ref,
        attn_ref,
        scr1,
        scr2,
        small,
        qscr,
        dq,
    ) = refs
    size = ones[0].shape[0]
    wide1 = scr1.shape[1]
    for k in range(seq):
        peer = peer_ref[k]
        at = 0
        bit = 1
        while bit < seq:
            at = at + lax.rem(peer // bit, 2) * (size * seq // (2 * bit))
            bit *= 2
        rows = pl.ds(pl.multiple_of(at, 8), size)
        one = ones[k][...].astype(F32)
        scr1[rows] = one[:, 0:wide1]
        small[pl.ds(pl.multiple_of(peer * size, 8), size)] = one[:, wide1:]
        at = lax.rem(peer // 2, 2) * (size * seq // 2) + lax.rem(peer, 2) * (size * seq // 4)
        bit = 4
        while bit < seq:
            at = at + lax.rem(peer // bit, 2) * (size * seq // (2 * bit))
            bit *= 2
        scr2[pl.ds(pl.multiple_of(at, 8), size)] = twos[k][...].astype(F32)
    for t in range(4):
        rows = slice(t * cs, (t + 1) * cs)
        lanes = slice(t * LANES, (t + 1) * LANES)
        res_ref[:, lanes] = scr1[rows, 0:LANES]
        skip_ref[:, lanes] = scr1[rows, LANES : 2 * LANES]
        step_ref[:, lanes] = scr2[rows, C : C + LANES]
        if t < 3:
            conv_ref[t, :, 0:C] = scr1[rows, 2 * LANES : 2 * LANES + C]
            conv_ref[t, :, C : 2 * C] = scr2[rows, 0:C]
        else:
            cond_ref[:, 0:C] = scr1[rows, 2 * LANES : 2 * LANES + C]
            cond_ref[:, C : 2 * C] = scr2[rows, 0:C]
    dq[...] = jnp.zeros(dq.shape, F32)
    for s in range(seq):
        v = small[s * size : (s + 1) * size]
        group, even = s // 2, s % 2 == 0
        out = key_ref if even else value_ref
        at = 0
        for row in range(0, cs, size):
            out[row : row + size, group * wide : (group + 1) * wide] = v[:, at : at + wide]
            attn_ref[row : row + size, s * csh : (s + 1) * csh] = v[:, at + wide : at + wide + csh]
            at += wide + csh
        first = group * wide + (0 if even else wide // 2)
        for row in range(0, QUERIES, size):
            count = min(size, QUERIES - row)
            dq[row : row + count, first : first + wide // 2] = v[0:count, at : at + wide // 2]
            at += wide // 2
    qscr[...] = jnp.zeros((LANES, LANES), F32)
    qscr[0:QUERIES, 0:cs] = queries_ref[...].astype(F32)
    qt = qscr[...].T.astype(BF16)
    d = dq[...]
    hi = d.astype(BF16)
    lo = (d - hi.astype(F32)).astype(BF16)
    gquery_ref[...] = (nn(qt, hi) + nn(qt, lo))[0:cs]
    gqueries_ref[...] = fold(nt(parts(d[0:QUERIES], 2), wq_ref[...]), 2)


def attention_back_kernel(
    rows,
    csh,
    dp,
    off_ref,
    prow,
    probs_ref,
    u_ref,
    qp_ref,
    qkv_ref,
    pooled_ref,
    memory_ref,
    dfilm_ref,
    got_ref,
    keep_ref,
    give_ref,
    ds,
    stack,
    right,
    out,
):
    count = got_ref.shape[0]
    total = prow.shape[1] * prow.shape[2]
    cs = C // dp
    table = prow[...].reshape(rows * total, C)
    wide = qp_ref.shape[1]
    heads = wide // HEAD_DIM
    datt = got_ref[0, 3 * RP : 4 * RP, 0:wide]
    dmem = got_ref[0, 2 * RP : 3 * RP, 0:csh]
    for s in range(1, count):
        datt = datt + got_ref[s, 3 * RP : 4 * RP, 0:wide]
        dmem = dmem + got_ref[s, 2 * RP : 3 * RP, 0:csh]
    datt = datt[0:8] * (1.0 / QUERIES)
    vh = []
    for g in range(heads):
        first = 2 * wide + g * HEAD_DIM
        v = parts(datt[:, g * HEAD_DIM : (g + 1) * HEAD_DIM], 2)
        vh.append(fold(nn(v, qkv_ref[first : first + HEAD_DIM]), 2))
    vh = jnp.concatenate(vh, axis=0)
    dp_all = fold(nt(parts(vh, 2), table), 2)
    for r in range(rows):
        cols = slice(r * total, (r + 1) * total)
        for g in range(heads):
            mine = slice(g * QUERIES, (g + 1) * QUERIES)
            p = probs_ref[mine, cols]
            dpr = dp_all[8 * g + r : 8 * g + r + 1, cols]
            inner = jnp.sum(p * dpr, axis=1, keepdims=True)
            ds[mine, cols] = p * (dpr - inner)
    tt = fold(nn(parts(ds[...], 2), table), 2)
    scale = 1.0 / math.sqrt(HEAD_DIM)
    dq = []
    stack[...] = jnp.zeros(stack.shape, F32)
    right[...] = jnp.zeros(right.shape, F32)
    stack[0 : heads * QUERIES] = tt
    stack[64:80] = u_ref[...]
    stack[80:96] = pooled_ref[...].astype(F32)
    stack[96:112] = memory_ref[...].astype(F32)
    for g in range(heads):
        cols = slice(g * HEAD_DIM, (g + 1) * HEAD_DIM)
        mine = slice(g * QUERIES, (g + 1) * QUERIES)
        wk = qkv_ref[wide + g * HEAD_DIM : wide + (g + 1) * HEAD_DIM]
        dq.append(fold(nt(parts(tt[mine], 2), wk), 2) * scale)
        right[mine, cols] = qp_ref[:, cols] * scale
        right[64 + 8 * g : 72 + 8 * g, wide + cols.start : wide + cols.stop] = datt[:, cols]
    right[80:96, 2 * wide : 2 * wide + csh] = dmem
    right[96:112, 2 * wide + csh : 2 * wide + 3 * csh] = dfilm_ref[...].astype(F32)
    out[...] = lax.dot_general(
        stack[...].T,
        right[...],
        (((1,), (0,)), ((), ())),
        precision=lax.Precision.HIGHEST,
        preferred_element_type=F32,
    )
    last = 2 * wide + 3 * csh
    for k in range(dp):
        ref = (keep_ref, give_ref)[k % 2]
        ref[k // 2] = out[pl.ds(pl.multiple_of(off_ref[k], 16), cs)].astype(BF16)
        for g in range(heads):
            first = last + g * HEAD_DIM
            ref[k // 2, 0:QUERIES, first : first + HEAD_DIM] = dq[g].astype(BF16)


def exchange(pieces, axis, groups=None):
    return lax.all_to_all(
        pieces, axis, split_axis=0, concat_axis=0, axis_index_groups=groups, tiled=True
    )


def flipped(v, axis, size, bit):
    return lax.ppermute(v, axis, [(d, d ^ bit) for d in range(size)])


class Reduction:
    def __init__(self, call, name, keep, give, dp, seq, index):
        self.call, self.name, self.dp, self.seq, self.index = call, name, dp, seq, index
        self.bits = [1 << b for b in range(seq.bit_length() - 1)]
        self.keep, self.flip = keep, 1
        self.got = flipped(give, "dp", dp, 1)

    def over_blocks(self, after=(), others=()):
        while 2 * self.flip < self.dp:
            group = (self,) + tuple(others)
            others = ()
            args = []
            for part in group:
                args += [part.keep, Got(part.got)]
            width = sum(part.keep.shape[2] for part in group)
            half = sds((self.keep.shape[0] // 2, self.keep.shape[1], width), BF16)
            self.keep, give = self.call(
                functools.partial(add_blocks_kernel, len(group)),
                (half, half),
                "blocks_" + self.name,
                args,
                after=after,
                in_specs=[VM] * len(args),
                out_specs=(VM, VM),
            )
            self.flip *= 2
            self.got = flipped(give, "dp", self.dp, self.flip)
        self.rest = self.keep.shape[1:]
        self.done = 0

    def over_half(self, after=()):
        rows, width = self.rest
        self.bit = self.bits[self.done]
        half = sds((rows // 2, width), BF16)
        self.keep, give = self.call(
            functools.partial(add_halves_kernel, self.bit),
            (half, half),
            "half" + str(self.done) + "_" + self.name,
            (self.index, self.keep.reshape(rows, width), Got(self.got.reshape(rows, width))),
            after=after,
            in_specs=[SM, VM, VM],
            out_specs=(VM, VM),
            scratch_shapes=[pltpu.VMEM((rows, width), F32)],
        )
        self.got = flipped(give, "seq", self.seq, self.bit)
        self.rest, self.done = (rows // 2, width), self.done + 1

    def over_last(self, after=(), extra=None):
        rows, width = self.rest
        args = (self.keep, Got(self.got))
        if extra is not None:
            args += (extra,)
            width += extra.shape[1]
        piece = self.call(
            add_last_kernel,
            sds((rows, width), BF16),
            "last_" + self.name,
            args,
            after=after,
            in_specs=[VM] * len(args),
            out_specs=VM,
        )
        have = {0: piece}
        for bit in reversed(self.bits):
            for k in sorted(have):
                have[k + bit] = flipped(have[k], "seq", self.seq, bit)
        return [have[k] if k == 0 else Got(have[k]) for k in range(self.seq)]


def body(
    dp,
    seq,
    x_in,
    cond,
    segment_ids,
    diffusion_steps,
    prompt,
    prompt_lengths,
    w_step,
    w_conv,
    w_cond,
    w_res,
    w_skip,
    queries,
    w_query,
    w_key,
    w_value,
    w_attn_out,
    w_film,
    d_out,
    d_skip,
):
    call = Caller()
    rows = x_in.shape[0]
    frames = x_in.shape[2]
    steps = rows // NR
    cols = rows * frames
    cs = C // dp
    csh = C // seq
    heads = 2 * HEADS // seq
    wide = heads * HEAD_DIM
    arows = rows // 2
    pl_local = prompt.shape[1]
    prompt_all = pl_local * seq
    sidx = lax.axis_index("seq")
    didx = lax.axis_index("dp")
    group = (sidx // 2).astype(jnp.int32).reshape(1)
    bit = (sidx % 2).astype(jnp.int32).reshape(1)
    up = [(i, i + 1) for i in range(seq - 1)]
    down = [(i + 1, i) for i in range(seq - 1)]
    order = jnp.bitwise_xor(didx, jnp.arange(dp, dtype=jnp.int32)).astype(jnp.int32)
    offsets = jnp.concatenate([order * cs, bit, 1 - bit])
    index = sidx.astype(jnp.int32).reshape(1)
    peers = jnp.bitwise_xor(sidx, jnp.arange(seq, dtype=jnp.int32)).astype(jnp.int32)

    def gather(pack, half=None):
        if dp == 4 and half is not None:
            mine = flipped(half, "dp", dp, 2)
            other = flipped(mine, "seq", seq, 1)
            near = [(0, None, pack), (2, 0, mine), (2, 1, other)]
            pieces = near + [(k + 1, h, flipped(v, "dp", dp, 1)) for k, h, v in near]
        else:
            pieces = [(0, None, pack)]
            flip = dp // 2
            while flip:
                pieces += [(k + flip, h, flipped(v, "dp", dp, flip)) for k, h, v in pieces]
                flip //= 2
        meta = [(k, h) for k, h, _ in pieces]
        return meta, [v if k == 0 else Got(v) for k, _, v in pieces]

    off_qkv = C + 2 * csh
    qkv_rows = -(-(3 * wide + QUERIES) // LANES) * LANES
    head_width = -(-(off_qkv + qkv_rows) // LANES) * LANES
    pack, mine, other = call(
        functools.partial(head_pack_kernel, csh, wide),
        (
            sds((cs, head_width), BF16),
            sds((arows, pl_local, C), BF16),
            sds((arows, pl_local, C), BF16),
        ),
        "head_pack",
        (
            group,
            bit,
            w_attn_out,
            jnp.transpose(w_film, (1, 2, 0)).reshape(2 * csh, cs),
            w_query,
            w_key,
            w_value,
            queries,
            prompt,
        ),
        in_specs=[SM, SM] + [VM] * 7,
        out_specs=(VM,) * 3,
        scratch_shapes=[pltpu.VMEM((2 * LANES, LANES), F32)],
    )
    head_meta, head_pieces = gather(pack)
    partner = flipped(other, "seq", seq, 1)
    size = C + 3 * C // 8
    pack, half = call(
        functools.partial(turned_pack_kernel, cs),
        (sds((2 * size, 4 * cs), BF16), sds((size, 4 * cs), BF16)),
        "turned_pack",
        (bit, w_conv, w_cond, w_res, w_skip, w_step),
        after=("head_pack",),
        in_specs=[SM] + [VM] * 5,
        out_specs=(VM, VM),
        scratch_shapes=[pltpu.VMEM((4 * cs, 2 * C), BF16)],
    )
    meta, turned = gather(pack, half)
    copies = 2 * dp * (1 + 3 * C // (4 * cs))
    pair = call(
        pair_kernel,
        sds((2, arows, pl_local, C), BF16),
        "pair",
        (mine, Got(partner)),
        after=("turned_pack",),
        in_specs=[VM, VM],
        out_specs=VM,
    )
    prompts = [pair] + [Got(flipped(pair, "seq", seq, 2 * k)) for k in range(1, seq // 2)]
    first, last = call(
        edge_kernel,
        (sds((C, LANES), BF16), sds((C, LANES), BF16)),
        "edges",
        (x_in,),
        after=("pair",),
        nbytes=4e6,
        in_specs=[VM],
        out_specs=(VM, VM),
    )
    left_halo = lax.ppermute(last, "seq", up)
    right_halo = lax.ppermute(first, "seq", down)

    block_ids = segment_ids[:, ::frames]
    padded_ids = jnp.pad(block_ids, ((0, 0), (1, 1)), constant_values=-1)
    mine = lax.dynamic_slice_in_dim(padded_ids, sidx, 3, 1)
    flags = jnp.stack([mine[:, 0] == mine[:, 1], mine[:, 2] == mine[:, 1]]).astype(jnp.int32)
    block_ids = jnp.pad(block_ids, ((0, RP - rows), (0, 0)))
    half = C // 2
    frequency = jnp.exp(jnp.arange(half, dtype=F32) * (-math.log(10000.0) / half))
    step_rows = jnp.pad(diffusion_steps.astype(F32), (0, LANES - rows))
    live_rows = jnp.arange(LANES, dtype=jnp.int32)[:, None] < rows
    angles = step_rows[:, None] * frequency[None, :]
    embedding = jnp.concatenate([jnp.sin(angles), jnp.cos(angles)], axis=1)
    embedding = jnp.where(live_rows, embedding, 0.0).astype(BF16)
    lengths = lax.dynamic_slice_in_dim(prompt_lengths, (sidx % 2) * arows, arows, 0)

    apack, prow, probs, u, pooled_head, qp, qkv = call(
        functools.partial(attention_kernel, head_meta, arows, heads, seq // 2, off_qkv),
        (
            sds((C, head_width), BF16),
            sds((arows, seq, pl_local, C), BF16),
            sds((heads * QUERIES, arows * prompt_all), F32),
            sds((RP, C), F32),
            sds((RP, LANES), F32),
            sds((QUERIES, wide), F32),
            sds((qkv_rows, C), BF16),
        ),
        "attention",
        (offsets, peers, lengths, *head_pieces, *prompts),
        in_specs=[SM, SM, SM] + [HB] * (len(head_pieces) + seq // 2),
        out_specs=(VM,) * 7,
        scratch_shapes=[
            pltpu.VMEM((RP, arows * prompt_all), F32),
            pltpu.SemaphoreType.DMA((2 * dp + seq,)),
        ],
    )

    row_block = pl.BlockSpec((NR, C, LANES), lambda i: (i, 0, 0))

    def col_block(height):
        return pl.BlockSpec((height, NR * LANES), lambda i: (0, i))

    def still(shape):
        return pl.BlockSpec(shape, lambda i: (0,) * len(shape))

    inp, gated, factor_a, factor_b, skip_out, mid, stats = call(
        functools.partial(forward_kernel, meta, dp, csh),
        (
            sds((4 * C, cols), BF16),
            sds((C, cols), BF16),
            sds((C, cols), BF16),
            sds((C, cols), BF16),
            sds(x_in.shape, BF16),
            sds((C, cols), BF16),
            sds((seq, 3 * RP, 2 * csh), F32),
        ),
        "wavenet",
        (
            offsets,
            flags,
            x_in,
            cond,
            d_out,
            Got(left_halo),
            Got(right_halo),
            embedding,
            pooled_head,
            *turned,
        ),
        flops=2 * cols * (4 * C * 2 * C + 2 * C * C),
        nbytes=30e6,
        grid=(steps,),
        in_specs=[
            SM,
            SM,
            row_block,
            row_block,
            row_block,
            whole((C, LANES)),
            whole((C, LANES)),
            whole((LANES, C)),
            whole((RP, LANES)),
        ]
        + [HB] * len(turned),
        out_specs=(
            col_block(4 * C),
            col_block(C),
            col_block(C),
            col_block(C),
            row_block,
            col_block(C),
            still((seq, 3 * RP, 2 * csh)),
        ),
        scratch_shapes=[
            pltpu.VMEM((2 * C, 4 * C), BF16),
            pltpu.VMEM((C, 2 * C), BF16),
            pltpu.VMEM((C, C), BF16),
            pltpu.VMEM((2 * C, C), BF16),
            pltpu.VMEM((C, LANES), F32),
            pltpu.VMEM((C, LANES), F32),
            pltpu.SemaphoreType.DMA((copies,)),
        ],
    )
    stats_got = exchange(stats, "seq")
    gskip = call(
        skip_grad_kernel,
        sds((C, C), BF16),
        "skip",
        (gated, d_skip),
        in_specs=[VM, VM],
        out_specs=VM,
        scratch_shapes=[pltpu.VMEM((C, cols), BF16)],
    )

    coef_out, dfilm, pooled, memory = call(
        functools.partial(stats_kernel, csh, heads, arows),
        (
            sds((seq, 4 * RP, 2 * csh), F32),
            sds((RP, 2 * csh), BF16),
            sds((RP, C), BF16),
            sds((RP, C), BF16),
        ),
        "segments",
        (block_ids, Got(stats_got), apack),
        after=("skip",),
        in_specs=[VM, VM, VM],
        out_specs=(VM, VM, VM, VM),
        scratch_shapes=[pltpu.VMEM((RP, C), F32)],
    )
    coef = Got(exchange(coef_out, "seq"))

    def gate_block(i):
        return jnp.minimum(i, steps - 1)

    def shard(i):
        return jnp.maximum(i - steps, 0)

    def gate_cols(height):
        return pl.BlockSpec((height, NR * LANES), lambda i, order: (0, gate_block(i)))

    gate_rows = pl.BlockSpec((NR, C, LANES), lambda i, order: (gate_block(i), 0, 0))
    wide1, wide2 = C + 2 * LANES, C

    def part(width):
        return sds((dp // 2, 4 * cs, width), BF16)

    def part_spec(width):
        return pl.BlockSpec((1, 4 * cs, width), lambda i, order: (shard(i) // 2, 0, 0))

    outs = call(
        functools.partial(backward_kernel, meta, dp, csh, steps),
        (
            sds((2 * C, cols), BF16),
            sds((C, cols), BF16),
            sds((2 * C, LANES), F32),
            part(wide1),
            part(wide2),
            part(wide1),
            part(wide2),
        ),
        "backward",
        (order, offsets, coef, mid, d_out, d_skip, factor_a, factor_b, inp, gated, gskip, flags, *turned),
        prefetch=1,
        grid=(steps + dp,),
        in_specs=[
            SM,
            pl.BlockSpec(
                (seq, 4 * RP, 2 * csh), lambda i, order: (0, 0, 0), pipeline_mode=pl.Buffered(1)
            ),
            gate_cols(C),
            gate_rows,
            gate_rows,
            gate_cols(C),
            gate_cols(C),
            pl.BlockSpec((4 * cs, cols), lambda i, order: (order[shard(i)], 0)),
            pl.BlockSpec((cs, cols), lambda i, order: (order[shard(i)], 0)),
            pl.BlockSpec((cs, C), lambda i, order: (order[shard(i)], 0)),
            SM,
        ]
        + [HB] * len(turned),
        out_specs=(
            gate_cols(2 * C),
            gate_cols(C),
            pl.BlockSpec((2 * C, LANES), lambda i, order: (0, 0)),
            part_spec(wide1),
            part_spec(wide2),
            part_spec(wide1),
            part_spec(wide2),
        ),
        scratch_shapes=[
            pltpu.VMEM((LANES, C), F32),
            pltpu.VMEM((C, LANES), F32),
            pltpu.VMEM((C, 2 * C), BF16),
            pltpu.VMEM((2 * C, NR * LANES), BF16),
            pltpu.VMEM((cols, 2 * C), BF16),
            pltpu.VMEM((cols, C), BF16),
            pltpu.SemaphoreType.DMA((copies,)),
        ],
    )
    dpre, dres, sums = outs[0:3]
    part1 = Reduction(call, "1", outs[3], outs[5], dp, seq, index)
    part2 = Reduction(call, "2", outs[4], outs[6], dp, seq, index)
    part1.over_blocks()
    keep, give = call(
        functools.partial(step_grad_kernel, meta, dp),
        (part(LANES), part(LANES)),
        "step_grad",
        (offsets, sums, embedding, *turned),
        after=("blocks_1",),
        in_specs=[SM, VM, VM] + [HB] * len(turned),
        out_specs=(VM, VM),
        scratch_shapes=[
            pltpu.VMEM((2 * C, 4 * C), BF16),
            pltpu.VMEM((C, C), F32),
            pltpu.SemaphoreType.DMA((copies,)),
        ],
    )
    part_step = Reduction(call, "step", keep, give, dp, seq, index)

    right_width = -(-(3 * wide + 3 * csh) // LANES) * LANES
    block = sds((dp // 2, cs, right_width), BF16)
    keep, give = call(
        functools.partial(attention_back_kernel, arows, csh, dp),
        (block, block),
        "attention_back",
        (offsets, prow, probs, u, qp, qkv, pooled, memory, dfilm, coef),
        after=("step_grad",),
        in_specs=[SM] + [VM] * 9,
        out_specs=(VM, VM),
        scratch_shapes=[
            pltpu.VMEM((heads * QUERIES, arows * prompt_all), F32),
            pltpu.VMEM((LANES, C), F32),
            pltpu.VMEM((LANES, right_width), F32),
            pltpu.VMEM((C, right_width), F32),
        ],
    )
    small = Reduction(call, "small", keep, give, dp, seq, index)
    part2.bits[0:2] = [2, 1]
    part2.over_blocks(("attention_back",), (part_step,))
    small.over_blocks(("blocks_2",))

    base, first, last = call(
        functools.partial(input_grad_kernel, meta, dp),
        (sds((C, cols), BF16), sds((C, LANES), BF16), sds((C, LANES), BF16)),
        "input_grad",
        (offsets, dpre, dres, *turned),
        after=("blocks_small",),
        grid=(steps,),
        in_specs=[SM, col_block(2 * C), col_block(C)] + [HB] * len(turned),
        out_specs=(
            col_block(C),
            still((C, LANES)),
            still((C, LANES)),
        ),
        scratch_shapes=[
            pltpu.VMEM((2 * C, 4 * C), BF16),
            pltpu.VMEM((3, C, 2 * C), BF16),
            pltpu.VMEM((C, LANES), F32),
            pltpu.VMEM((C, LANES), F32),
            pltpu.SemaphoreType.DMA((copies,)),
        ],
    )
    from_left = lax.ppermute(last, "seq", up)
    from_right = lax.ppermute(first, "seq", down)
    rest = 4 * cs // seq
    small_width = (cs // rest) * (wide + csh) + max(1, QUERIES // rest) * (wide // 2)
    part1.over_half(("input_grad",))
    grad_film, attn_rows, mine, other = call(
        functools.partial(small_sum_kernel, csh, wide),
        (
            sds((2 * csh, cs), F32),
            sds((cs, csh), F32),
            sds((cs + QUERIES, wide), BF16),
            sds((cs + QUERIES, wide), BF16),
        ),
        "small_sum",
        (bit, small.keep, Got(small.got)),
        after=("half0_1",),
        in_specs=[SM, VM, VM],
        out_specs=(VM,) * 4,
        scratch_shapes=[pltpu.VMEM((LANES, LANES), F32)],
    )
    partner = flipped(other, "seq", seq, 1)
    grad_input, layer_out = call(
        functools.partial(finish_kernel, csh),
        (sds(x_in.shape, BF16), sds(x_in.shape, BF16)),
        "grad_input",
        (flags, base, Got(from_left), Got(from_right), mid, coef),
        after=("small_sum",),
        grid=(steps,),
        in_specs=[
            SM,
            col_block(C),
            whole((C, LANES)),
            whole((C, LANES)),
            col_block(C),
            whole((seq, 4 * RP, 2 * csh)),
        ],
        out_specs=(row_block, row_block),
        scratch_shapes=[pltpu.VMEM((LANES, C), F32), pltpu.VMEM((C, LANES), F32)],
    )
    small_piece = call(
        functools.partial(small_piece_kernel, csh, wide),
        sds((rest, small_width), BF16),
        "small_piece",
        (attn_rows, mine, Got(partner)),
        after=("grad_input",),
        in_specs=[VM] * 3,
        out_specs=VM,
    )
    part1.over_half(("small_piece",))
    part2.over_half(("half1_1",))
    while part1.done < len(part1.bits):
        part1.over_half()
    ones = part1.over_last(extra=small_piece)
    while part2.done < len(part2.bits):
        part2.over_half()
    twos = part2.over_last()

    (
        grad_step,
        grad_conv,
        grad_cond,
        grad_res,
        grad_skip,
        grad_queries,
        grad_query,
        grad_key,
        grad_value,
        grad_attn,
    ) = call(
        functools.partial(output_kernel, cs, csh, wide, seq),
        (
            sds((cs, C), F32),
            sds((3, cs, 2 * C), F32),
            sds((cs, 2 * C), F32),
            sds((cs, C), F32),
            sds((cs, C), F32),
            sds((QUERIES, cs), F32),
            sds((cs, C), F32),
            sds((cs, C), F32),
            sds((cs, C), F32),
            sds((cs, C), F32),
        ),
        "outputs",
        (peers, *ones, *twos, queries, w_query),
        in_specs=[SM] + [VM] * (2 * seq + 2),
        out_specs=(VM,) * 10,
        scratch_shapes=[
            pltpu.VMEM((4 * cs, wide1), F32),
            pltpu.VMEM((4 * cs, wide2 + LANES), F32),
            pltpu.VMEM((4 * cs, small_width), F32),
            pltpu.VMEM((LANES, LANES), F32),
            pltpu.VMEM((LANES, C), F32),
        ],
    )
    return (
        layer_out,
        skip_out,
        grad_input,
        grad_step,
        grad_conv,
        grad_cond,
        grad_res,
        grad_skip,
        grad_queries,
        grad_query,
        grad_key,
        grad_value,
        grad_attn,
        jnp.transpose(grad_film.reshape(2, csh, cs), (2, 0, 1)),
    )


def solution(mesh):
    frames = P("dp", None, "seq")
    matrix = P("dp", None)
    return jax.shard_map(
        functools.partial(body, mesh.shape["dp"], mesh.shape["seq"]),
        mesh=mesh,
        in_specs=(
            frames,
            frames,
            P("dp", None),
            P("dp"),
            P("dp", "seq", None),
            P("dp"),
            matrix,
            P(None, "dp", None),
            matrix,
            matrix,
            matrix,
            P(None, "dp"),
            matrix,
            matrix,
            matrix,
            matrix,
            frames,
            frames,
            frames,
        ),
        out_specs=(
            frames,
            frames,
            frames,
            matrix,
            P(None, "dp", None),
            matrix,
            matrix,
            matrix,
            P(None, "dp"),
            matrix,
            matrix,
            matrix,
            matrix,
            frames,
        ),
        check_vma=False,
    )
```

```python
import functools
import math

import jax
import jax.numpy as jnp
from jax import lax
from jax.experimental import pallas as pl
from jax.experimental.pallas import tpu as pltpu
from jax.sharding import PartitionSpec as P

C = 512
HEADS = 8
QUERIES = 32
HEAD_DIM = 64
SHIFT = 4
SQRT_HALF = 0.7071067811865476
NORM_EPS = 1e-05
MASKED_SCORE = -1e30
LANES = 128
RP = 16
NR = 4
F32 = jnp.float32
BF16 = jnp.bfloat16
VMEM_BYTES = 50 * 1024 * 1024


def nn(a, b):
    return lax.dot_general(a, b, (((1,), (0,)), ((), ())), preferred_element_type=F32)


def nt(a, b):
    return lax.dot_general(a, b, (((1,), (1,)), ((), ())), preferred_element_type=F32)


def parts(v, count):
    out = []
    for _ in range(count):
        low = v.astype(BF16).astype(F32)
        out.append(low)
        v = v - low
    return jnp.concatenate(out, axis=0).astype(BF16)


def fold(v, count):
    rows = v.shape[0] // count
    total = v[:rows]
    for k in range(1, count):
        total = total + v[k * rows : (k + 1) * rows]
    return total


def lane_ids(shape):
    return lax.broadcasted_iota(jnp.int32, shape, len(shape) - 1)


def sds(shape, dtype):
    return jax.ShapeDtypeStruct(shape, dtype)


VM = pl.BlockSpec(memory_space=pltpu.VMEM)
HB = pl.BlockSpec(memory_space=pl.ANY)
SM = pl.BlockSpec(memory_space=pltpu.SMEM)


def whole(shape):
    return pl.BlockSpec(shape, lambda i: (0,) * len(shape), pipeline_mode=pl.Buffered(1))


class Got:
    def __init__(self, array):
        self.array = array


class Caller:
    def __init__(self):
        self.done = {}

    def __call__(self, kernel, out_shape, name, args, flops=0, nbytes=0, prefetch=0, after=(), **kw):
        single = not isinstance(out_shape, tuple)
        shapes = (out_shape,) if single else out_shape
        pinned = tuple(pltpu.HBM(v.shape, v.dtype) for v in shapes)
        in_specs = list(kw.pop("in_specs"))
        count = prefetch + len(in_specs)
        args = list(args)
        extra = len(after)
        for before in after:
            in_specs.append(HB)
            args.append(self.done[before])

        def run(*refs):
            return kernel(*refs[:count], *refs[count + extra :])

        values = []
        for k, v in enumerate(args):
            spec = SM if k < prefetch else in_specs[k - prefetch]
            if isinstance(v, Got):
                values.append(v.array)
            elif spec is SM:
                values.append(v)
            else:
                values.append(pltpu.with_memory_space_constraint(v, pltpu.HBM))
        spec = pltpu.PrefetchScalarGridSpec(
            num_scalar_prefetch=prefetch,
            grid=kw.pop("grid", ()),
            in_specs=in_specs,
            out_specs=kw.pop("out_specs"),
            scratch_shapes=kw.pop("scratch_shapes", ()),
        )
        out = pl.pallas_call(
            run,
            out_shape=pinned[0] if single else pinned,
            name=name,
            grid_spec=spec,
            cost_estimate=pl.CostEstimate(
                flops=1, bytes_accessed=1, transcendentals=0
            ),
            compiler_params=pltpu.CompilerParams(vmem_limit_bytes=VMEM_BYTES),
        )(*values)
        self.done[name] = out if single else out[0]
        return out


def head_pack_kernel(
    csh,
    local,
    group_ref,
    bit_ref,
    attn_ref,
    film_ref,
    wq_ref,
    wk_ref,
    wv_ref,
    queries_ref,
    prompt_ref,
    out_ref,
    mine_ref,
    other_ref,
    scr,
):
    cs = attn_ref.shape[0]
    arows = mine_ref.shape[0]
    mine_ref[...] = prompt_ref[pl.ds(bit_ref[0] * arows, arows)]
    other_ref[...] = prompt_ref[pl.ds((1 - bit_ref[0]) * arows, arows)]
    out_ref[:, 0:C] = attn_ref[...]
    off = C
    scr[...] = jnp.zeros((2 * LANES, LANES), F32)
    scr[0 : 2 * csh, 0:cs] = film_ref[...].astype(F32)
    scr[LANES : LANES + QUERIES, 0:cs] = queries_ref[...].astype(F32)
    film = scr[0:LANES].T[0:cs]
    table = scr[LANES : 2 * LANES].T[0:cs]
    turn = lax.rem(C - local * group_ref[0], C)
    blocks = [film[:, 0 : 2 * csh]]
    for ref in (wq_ref, wk_ref, wv_ref):
        blocks.append(pltpu.roll(ref[...].astype(F32), turn, 1)[:, 0:local])
    blocks.append(table)
    for block in blocks:
        width = min(block.shape[1], out_ref.shape[1] - off)
        out_ref[:, off : off + width] = block[:, 0:width].astype(BF16)
        off += width
    if off < out_ref.shape[1]:
        out_ref[:, off:] = jnp.zeros((cs, out_ref.shape[1] - off), BF16)


SIDE = 480


def turned_pack_kernel(cs, bit_ref, conv_ref, cond_ref, res_ref, skip_ref, step_ref, out_ref, side_ref, middle_ref, scr):
    for k in range(3):
        scr[k * cs : (k + 1) * cs] = conv_ref[k]
    scr[3 * cs : 4 * cs] = cond_ref[...]
    turned = scr[...].T
    out_ref[0 : 2 * C - SIDE] = turned[0 : 2 * C - SIDE]
    at = 2 * C - SIDE
    for ref in (res_ref, skip_ref, step_ref):
        for lane in range(0, C, 4 * cs):
            out_ref[at : at + cs] = ref[:, lane : lane + 4 * cs]
            at += cs
    out_ref[at : at + SIDE] = turned[2 * C - SIDE :]
    middle_ref[...] = out_ref[SIDE:at]
    side_ref[...] = out_ref[pl.ds(pl.multiple_of(bit_ref[0] * at, 16), SIDE)]


def pair_kernel(a_ref, b_ref, out_ref):
    for p in range(out_ref.shape[0]):
        out_ref[p, 0] = a_ref[...]
        out_ref[p, 1] = b_ref[...]


def edge_kernel(x_ref, first_ref, last_ref):
    rows = x_ref.shape[0]
    lane = lane_ids((C, LANES))
    first = jnp.zeros((C, LANES), F32)
    last = jnp.zeros((C, LANES), F32)
    for r in range(rows):
        v = x_ref[r].astype(F32)
        here = (lane // SHIFT) == r
        first = jnp.where(here, pltpu.roll(v, SHIFT * r, 1) if r else v, first)
        last = jnp.where(here, pltpu.roll(v, SHIFT * r + SHIFT, 1), last)
    first_ref[...] = first.astype(BF16)
    last_ref[...] = last.astype(BF16)


def begin(copies):
    for copy in copies:
        copy.start()


def finish(copies):
    for copy in copies:
        copy.wait()


def turned_copies(meta, refs, off_ref, cs, wt, others, sems):
    dp = len({k for k, _ in meta})
    pairs = []

    def conv(k, ref, first, row, rows):
        if wt is not None:
            lanes = pl.ds(pl.multiple_of(off_ref[k] * 4, LANES), 4 * cs)
            at = row if isinstance(row, int) else pl.multiple_of(row, 16)
            pairs.append((ref.at[pl.ds(first, rows)], wt.at[pl.ds(at, rows), lanes]))

    def rest(k, ref, at):
        row = pl.ds(pl.multiple_of(off_ref[k], 16), cs)
        for other in others:
            for lane in range(0, C, 4 * cs):
                if other is not None:
                    dst, start = other
                    pairs.append((ref.at[pl.ds(at, cs)], dst.at[row, pl.ds(start + lane, 4 * cs)]))
                at += cs

    inner = 2 * C - 2 * SIDE
    for (k, which), ref in zip(meta, refs):
        if which is None:
            conv(k, ref, 0, 0, SIDE + inner)
            rest(k, ref, SIDE + inner)
            conv(k, ref, ref.shape[0] - SIDE, 2 * C - SIDE, SIDE)
        elif which == 2:
            conv(k, ref, 0, SIDE, inner)
            rest(k, ref, inner)
        else:
            conv(k, ref, 0, off_ref[dp + which] * (2 * C - SIDE), SIDE)
    return [pltpu.make_async_copy(a, b, sems.at[n]) for n, (a, b) in enumerate(pairs)]


def head_copies(refs, off_ref, dst, sems):
    copies = []
    for k, ref in enumerate(refs):
        row = pl.ds(pl.multiple_of(off_ref[k], 16), ref.shape[0])
        copies.append(pltpu.make_async_copy(ref, dst.at[row], sems.at[k]))
    return copies


def forward_kernel(
    meta, dp, csh, off_ref, flags_ref, x_ref, cond_ref, dout_ref, left_ref, right_ref, emb_ref, pooled_ref, *refs
):
    turned, refs = refs[: len(meta)], refs[len(meta) :]
    (
        inp_ref,
        gated_ref,
        fa_ref,
        fb_ref,
        skip_ref,
        mid_ref,
        stats_ref,
        wt_ref,
        rn_ref,
        step_ref,
        rst_ref,
        lift_ref,
        acc_ref,
        sems,
    ) = refs
    cs = C // dp
    i = pl.program_id(0)
    lane = lane_ids((C, LANES))

    @pl.when(i == 0)
    def _():
        copies = turned_copies(
            meta,
            turned,
            off_ref,
            cs,
            wt_ref,
            ((rn_ref, 0), (rn_ref, C), (step_ref, 0)),
            sems,
        )
        begin(copies)
        acc_ref[...] = jnp.zeros((C, LANES), F32)
        finish(copies)
        lift = nn(emb_ref[0:RP], step_ref[...])
        lift = jnp.concatenate([lift, jnp.zeros((LANES - RP, C), F32)], axis=0)
        lift_ref[...] = lift.T
        rst_ref[...] = rn_ref[...].T

    lift = pltpu.roll(lift_ref[...], lax.rem(LANES - NR * i, LANES), 1)
    left = left_ref[...].astype(F32)
    right = right_ref[...].astype(F32)

    def put(tap, cols, value):
        for d in range(dp):
            at = d * 4 * cs + tap * cs
            inp_ref[at : at + cs, cols] = value[d * cs : (d + 1) * cs]

    for j in range(NR):
        r = NR * i + j
        lc = lift[:, j : j + 1]
        sh = (x_ref[j].astype(F32) + lc).astype(BF16)
        shf = sh.astype(F32)
        lh = pltpu.roll(left, lax.rem(LANES - SHIFT * r, LANES), 1)
        lh = jnp.where(flags_ref[0, r] > 0, (lh + lc).astype(BF16).astype(F32), 0.0)
        rh = pltpu.roll(right, LANES - SHIFT - SHIFT * r, 1)
        rh = jnp.where(flags_ref[1, r] > 0, (rh + lc).astype(BF16).astype(F32), 0.0)
        cols = slice(j * LANES, (j + 1) * LANES)
        put(0, cols, jnp.where(lane < SHIFT, lh, pltpu.roll(shf, SHIFT, 1)).astype(BF16))
        put(1, cols, sh)
        put(
            2,
            cols,
            jnp.where(lane >= LANES - SHIFT, rh, pltpu.roll(shf, LANES - SHIFT, 1)).astype(BF16),
        )
        put(3, cols, cond_ref[j])
    pre = nn(wt_ref[...], inp_ref[...])
    th = jnp.tanh(pre[:C])
    sg = jax.nn.sigmoid(pre[C:])
    gf = th * sg
    fa_ref[...] = (sg - gf * th).astype(BF16)
    fb_ref[...] = (gf * (1.0 - sg)).astype(BF16)
    g = gf.astype(BF16)
    gated_ref[...] = g
    rs = nn(rst_ref[...], g)
    acc = acc_ref[...]
    for j in range(NR):
        r = NR * i + j
        cols = slice(j * LANES, (j + 1) * LANES)
        skip_ref[j] = rs[C:, cols].astype(BF16)
        mid = ((x_ref[j].astype(F32) + rs[:C, cols]) * SQRT_HALF).astype(BF16)
        mid_ref[:, cols] = mid
        mf = mid.astype(F32)
        df = dout_ref[j].astype(F32)
        total = jnp.sum(mf, axis=1, keepdims=True)
        dev = mf - total * (1.0 / LANES)
        acc = jnp.where(lane == r, total, acc)
        acc = jnp.where(lane == RP + r, jnp.sum(dev * dev, axis=1, keepdims=True), acc)
        acc = jnp.where(lane == 2 * RP + r, jnp.sum(df, axis=1, keepdims=True), acc)
        acc = jnp.where(lane == 3 * RP + r, jnp.sum(df * dev, axis=1, keepdims=True), acc)
    acc_ref[...] = acc

    @pl.when(i == pl.num_programs(0) - 1)
    def _():
        t = acc.T
        for s in range(C // csh):
            cols = slice(s * csh, (s + 1) * csh)
            stats_ref[s, 0 : 2 * RP, 0:csh] = t[0 : 2 * RP, cols]
            stats_ref[s, 0 : 2 * RP, csh : 2 * csh] = t[2 * RP : 4 * RP, cols]
            stats_ref[s, 2 * RP : 3 * RP] = pooled_ref[:, 0 : 2 * csh]


def attention_kernel(dp, rows, heads, pairs, off, off_ref, bit_ref, len_ref, prompts, *refs):
    pieces, refs = refs[:dp], refs[dp:]
    apack_ref, prow, probs_ref, u_ref, pooled_ref, qp_ref, qkv_ref, abd, sems = refs
    copies = head_copies(pieces, off_ref, apack_ref, sems)
    count = len(copies)
    for j in range(pairs):
        for i in range(2):
            copies.append(
                pltpu.make_async_copy(
                    prompts.at[j, i], prow.at[:, 2 * j + i], sems.at[count + 2 * j + i]
                )
            )
    begin(copies)
    local = prow.shape[2]
    total = 2 * pairs * local
    abd[...] = jnp.zeros(abd.shape, F32)
    lane = lane_ids((heads * QUERIES, total))
    place = jnp.zeros((heads * QUERIES, total), jnp.int32)
    for k in range(2 * pairs):
        here = (k // 2) * 2 + (bit_ref[0] if k % 2 == 0 else 1 - bit_ref[0])
        place = jnp.where(lane // local == k, here * local + lane % local, place)
    finish(copies)
    wide = heads * HEAD_DIM
    qkv = apack_ref[:, off : off + qkv_ref.shape[0]].T
    qkv_ref[...] = qkv
    qp = nt(qkv[3 * wide : 3 * wide + QUERIES], qkv[0:wide])
    qp_ref[...] = qp
    st = []
    for g in range(heads):
        cols = slice(g * HEAD_DIM, (g + 1) * HEAD_DIM)
        st.append(fold(nn(parts(qp[:, cols], 3), qkv[wide + cols.start : wide + cols.stop]), 3))
    st = jnp.concatenate(st, axis=0) * (1.0 / math.sqrt(HEAD_DIM))
    table = prow[...].reshape(rows * total, C)
    scores = fold(nt(parts(st, 3), table), 3)
    for r in range(rows):
        cols = slice(r * total, (r + 1) * total)
        live = place < len_ref[r]
        s = jnp.where(live, scores[:, cols], MASKED_SCORE)
        e = jnp.where(live, jnp.exp(s - jnp.max(s, axis=1, keepdims=True)), 0.0)
        p = e / jnp.sum(e, axis=1, keepdims=True)
        probs_ref[:, cols] = p
        for g in range(heads):
            abd[8 * g + r : 8 * g + r + 1, cols] = jnp.sum(
                p[g * QUERIES : (g + 1) * QUERIES], axis=0, keepdims=True
            )
    u = fold(nn(parts(abd[...], 2), table), 2)
    u_ref[...] = u
    pooled_ref[...] = jnp.zeros(pooled_ref.shape, F32)
    for g in range(heads):
        first = 2 * wide + g * HEAD_DIM
        v = parts(u[8 * g : 8 * g + 8] * (1.0 / QUERIES), 2)
        pooled_ref[0:8, g * HEAD_DIM : (g + 1) * HEAD_DIM] = fold(
            nt(v, qkv[first : first + HEAD_DIM]), 2
        )


def stats_kernel(
    csh, heads, rows, seg_ref, x_ref, apack_ref, out_ref, dfilm_ref, pooled_ref, memory_ref, scratch
):
    count = x_ref.shape[0]
    wide = heads * HEAD_DIM
    seg = seg_ref[...]
    scratch[...] = jnp.zeros(scratch.shape, F32)
    for s in range(count):
        group, part = s // 2, s % 2
        scratch[part * rows : (part + 1) * rows, group * wide : (group + 1) * wide] = x_ref[
            s, 2 * RP : 2 * RP + rows, 0:wide
        ]
    pooled = scratch[...].astype(BF16)
    pooled_ref[...] = pooled
    memory = nn(pooled, apack_ref[:, 0:C]).astype(BF16)
    memory_ref[...] = memory
    film = nn(memory, apack_ref[:, C : C + 2 * csh])
    f0 = film[:, 0:csh]
    f1 = film[:, csh : 2 * csh]
    total = [x_ref[s, 0:RP, 0:csh] for s in range(count)]
    second = [x_ref[s, RP : 2 * RP, 0:csh] for s in range(count)]
    dsum = [x_ref[s, 0:RP, csh : 2 * csh] for s in range(count)]
    cross = [x_ref[s, RP : 2 * RP, csh : 2 * csh] for s in range(count)]
    means = [v * (1.0 / LANES) for v in total]
    d0 = jnp.zeros((RP, csh), F32)
    d1 = jnp.zeros((RP, csh), F32)
    for me in range(count):
        same = [(seg[:, s : s + 1] == seg[:, me : me + 1]).astype(F32) for s in range(count)]
        frames = sum(same) * float(LANES)
        inv = 1.0 / frames
        mean = sum(m * v for m, v in zip(same, total)) * inv
        var = (
            sum(
                m * (v + float(LANES) * (u - mean) * (u - mean))
                for m, v, u in zip(same, second, means)
            )
            * inv
        )
        scale = lax.rsqrt(var + NORM_EPS)
        dtot = sum(m * v for m, v in zip(same, dsum))
        xtot = sum(m * (v + (u - mean) * d) for m, v, u, d in zip(same, cross, means, dsum)) * scale
        mean_part = f0 * dtot * inv
        cross_part = f0 * xtot * inv
        slope = scale * scale * cross_part
        out_ref[me, 0:RP, 0:csh] = 1.0 + f0 * scale
        out_ref[me, RP : 2 * RP, 0:csh] = f1 - f0 * scale * mean
        out_ref[me, 0:RP, csh : 2 * csh] = -slope
        out_ref[me, RP : 2 * RP, csh : 2 * csh] = slope * mean - scale * mean_part
        d0 = d0 + (cross[me] + (means[me] - mean) * dsum[me]) * scale
        d1 = d1 + dsum[me]
    dfilm = jnp.concatenate([d0, d1], axis=1).astype(BF16)
    dfilm_ref[...] = dfilm
    dmem = nt(dfilm, apack_ref[:, C : C + 2 * csh])
    dpool = nt(dmem.astype(BF16), apack_ref[:, 0:C])
    for s in range(count):
        group, part = s // 2, s % 2
        rolled = pltpu.roll(dpool, RP - part * rows, 0) if part else dpool
        out_ref[s, 2 * RP : 3 * RP, 0:csh] = dmem[:, s * csh : (s + 1) * csh]
        out_ref[s, 2 * RP : 3 * RP, csh : 2 * csh] = jnp.zeros((RP, csh), F32)
        out_ref[s, 3 * RP : 4 * RP] = rolled[:, group * wide : (group + 1) * wide]


def coef_columns(csh, coef_ref, rows_ref, cols_ref):
    rows_ref[...] = jnp.zeros(rows_ref.shape, F32)
    for s in range(C // csh):
        cols = slice(s * csh, (s + 1) * csh)
        rows_ref[0 : 2 * RP, cols] = coef_ref[s, 0 : 2 * RP, 0:csh]
        rows_ref[2 * RP : 4 * RP, cols] = coef_ref[s, 0 : 2 * RP, csh : 2 * csh]
    cols_ref[...] = rows_ref[...].T


def skip_grad_kernel(gated_ref, dskip_ref, out_ref, right):
    for r in range(dskip_ref.shape[0]):
        right[:, r * LANES : (r + 1) * LANES] = dskip_ref[r]
    out_ref[...] = nt(gated_ref[...], right[...]).astype(BF16)


def backward_kernel(meta, dp, csh, gates, order_ref, off_ref, coef_ref, mid_ref, dout_ref, dskip_ref, fa_ref, fb_ref, inp_ref, gated_ref, gskip_ref, flags_ref, *refs):
    turned, refs = refs[: len(meta)], refs[len(meta) :]
    dpre_ref, dres_ref, sums_ref, refs = refs[0], refs[1], refs[2], refs[3:]
    outs, refs = (refs[0:2], refs[2:4]), refs[4:]
    rows_ref, cols_ref, w_ref, both_ref, dpt_ref, drt_ref, sems = refs
    cs = C // dp
    span = NR * LANES
    i = pl.program_id(0)

    @pl.when(i == 0)
    def _():
        copies = turned_copies(
            meta, turned, off_ref, cs, None, ((w_ref, 0), (w_ref, C), None), sems
        )
        begin(copies)
        coef_columns(csh, coef_ref, rows_ref, cols_ref)
        sums_ref[...] = jnp.zeros(sums_ref.shape, F32)
        finish(copies)

    @pl.when(i < gates)
    def _():
        coef = pltpu.roll(cols_ref[...], lax.rem(LANES - NR * i, LANES), 1)
        for j in range(NR):
            cols = slice(j * LANES, (j + 1) * LANES)
            mf = mid_ref[:, cols].astype(F32)
            df = dout_ref[j].astype(F32)
            a = coef[:, j : j + 1]
            be = coef[:, 2 * RP + j : 2 * RP + j + 1]
            ga = coef[:, 3 * RP + j : 3 * RP + j + 1]
            dmid = (a * df + (be * mf + ga)).astype(BF16).astype(F32)
            both_ref[0:C, cols] = (dmid * SQRT_HALF).astype(BF16)
            both_ref[C : 2 * C, cols] = dskip_ref[j]
        dres = both_ref[0:C]
        dres_ref[...] = dres
        dg = nn(w_ref[...], both_ref[...])
        dt = (dg * fa_ref[...].astype(F32)).astype(BF16)
        ds = (dg * fb_ref[...].astype(F32)).astype(BF16)
        dpre_ref[0:C] = dt
        dpre_ref[C : 2 * C] = ds
        at = pl.ds(pl.multiple_of(i * span, span), span)
        dpt_ref[at, 0:C] = dt.T
        dpt_ref[at, C : 2 * C] = ds.T
        drt_ref[at] = dres.T
        frame = lax.broadcasted_iota(jnp.int32, (span, LANES), 0)
        column = lane_ids((span, LANES))
        place = frame % LANES
        which = frame // LANES
        keep_l = jnp.zeros((span, LANES), jnp.int32)
        keep_r = jnp.zeros((span, LANES), jnp.int32)
        for j in range(NR):
            keep_l = jnp.where(which == j, flags_ref[0, NR * i + j], keep_l)
            keep_r = jnp.where(which == j, flags_ref[1, NR * i + j], keep_r)
        row = NR * i + which
        use0 = (column == row) & ((place >= SHIFT) | (keep_l > 0))
        use1 = column == RP + row
        use2 = (column == 2 * RP + row) & ((place < LANES - SHIFT) | (keep_r > 0))
        pick = jnp.where(use0 | use1 | use2, 1.0, 0.0).astype(BF16)
        sums_ref[...] = sums_ref[...] + nn(dpre_ref[...], pick)

    @pl.when(i >= gates)
    def _():
        g = nn(inp_ref[...], dpt_ref[...]).astype(BF16)
        h = nn(gated_ref[...], drt_ref[...]).astype(BF16)
        k = i - gates
        for parity, (one, two) in enumerate(outs):

            @pl.when(lax.rem(k, 2) == parity)
            def _():
                for t in range(4):
                    rows = slice(t * cs, (t + 1) * cs)
                    lanes = slice(t * LANES, (t + 1) * LANES)
                    one[0, rows, 0:LANES] = h[:, lanes]
                    one[0, rows, LANES : 2 * LANES] = gskip_ref[:, lanes]
                one[0, :, 2 * LANES : 6 * LANES] = g[:, 0:C]
                two[0] = g[:, C : 2 * C]


def step_grad_kernel(meta, dp, off_ref, sums_ref, emb_ref, *refs):
    turned, refs = refs[: len(meta)], refs[len(meta) :]
    keep_ref, give_ref, wt_ref, scr, sems = refs
    cs = C // dp
    copies = turned_copies(meta, turned, off_ref, cs, wt_ref, (None,) * 3, sems)
    begin(copies)
    sums = sums_ref[...].T
    emb = emb_ref[...].T
    finish(copies)
    total = jnp.zeros((RP, 4 * C), F32)
    lane = lane_ids((RP, 4 * C))
    all_taps = fold(nn(parts(sums[0 : 3 * RP], 2), wt_ref[...]), 2)
    for t in range(3):
        g = all_taps[t * RP : (t + 1) * RP]
        total = total + jnp.where((lane // cs) % 4 == t, g, 0.0)
    out = []
    for d in range(dp):
        block = total[:, d * 4 * cs : (d + 1) * 4 * cs]
        out.append(block[:, 0:cs] + block[:, cs : 2 * cs] + block[:, 2 * cs : 3 * cs])
    g = jnp.concatenate(out, axis=1)
    g = jnp.concatenate([g, jnp.zeros((LANES - RP, C), F32)], axis=0)
    hi = g.astype(BF16)
    lo = (g - hi.astype(F32)).astype(BF16)
    scr[...] = nn(emb, hi) + nn(emb, lo)
    for k in range(dp):
        v = scr[pl.ds(pl.multiple_of(off_ref[k], 16), cs)].astype(BF16)
        for t in range(4):
            (keep_ref, give_ref)[k % 2][k // 2, t * cs : (t + 1) * cs] = v[
                :, t * LANES : (t + 1) * LANES
            ]


def input_grad_kernel(meta, dp, off_ref, dpre_ref, dres_ref, *refs):
    turned, refs = refs[: len(meta)], refs[len(meta) :]
    base_ref, first_ref, last_ref, wt_ref, w_ref, facc_ref, lacc_ref, sems = refs
    cs = C // dp
    i = pl.program_id(0)
    lane = lane_ids((C, LANES))

    @pl.when(i == 0)
    def _():
        copies = turned_copies(meta, turned, off_ref, cs, wt_ref, (None,) * 3, sems)
        begin(copies)
        facc_ref[...] = jnp.zeros((C, LANES), F32)
        lacc_ref[...] = jnp.zeros((C, LANES), F32)
        finish(copies)
        for d in range(dp):
            v = wt_ref[:, d * 4 * cs : (d + 1) * 4 * cs].T
            for t in range(3):
                w_ref[t, d * cs : (d + 1) * cs] = v[t * cs : (t + 1) * cs]

    dpre = dpre_ref[...]
    y0 = nn(w_ref[0], dpre)
    y1 = nn(w_ref[1], dpre)
    y2 = nn(w_ref[2], dpre)
    facc = facc_ref[...]
    lacc = lacc_ref[...]
    for j in range(NR):
        r = NR * i + j
        cols = slice(j * LANES, (j + 1) * LANES)
        z0 = pltpu.roll(y0[:, cols], LANES - SHIFT, 1)
        z2 = pltpu.roll(y2[:, cols], SHIFT, 1)
        inner0 = lane < LANES - SHIFT
        inner2 = lane >= SHIFT
        v = y1[:, cols]
        base_ref[:, cols] = (
            v
            + jnp.where(inner0, z0, 0.0)
            + jnp.where(inner2, z2, 0.0)
            + dres_ref[:, cols].astype(F32)
        ).astype(BF16)
        here = (lane // SHIFT) == r
        facc = jnp.where(here, pltpu.roll(z0, lax.rem(SHIFT * r + SHIFT, LANES), 1), facc)
        lacc = jnp.where(here, pltpu.roll(z2, SHIFT * r, 1), lacc)
    facc_ref[...] = facc
    lacc_ref[...] = lacc

    @pl.when(i == pl.num_programs(0) - 1)
    def _():
        first_ref[...] = facc.astype(BF16)
        last_ref[...] = lacc.astype(BF16)


def finish_kernel(csh, flags_ref, base_ref, left_ref, right_ref, mid_ref, coef_ref, out_ref, layer_ref, rows_ref, cols_ref):
    i = pl.program_id(0)
    lane = lane_ids((C, LANES))

    @pl.when(i == 0)
    def _():
        coef_columns(csh, coef_ref, rows_ref, cols_ref)

    coef = pltpu.roll(cols_ref[...], lax.rem(LANES - NR * i, LANES), 1)
    left = left_ref[...].astype(F32)
    right = right_ref[...].astype(F32)
    for j in range(NR):
        r = NR * i + j
        cols = slice(j * LANES, (j + 1) * LANES)
        lh = pltpu.roll(left, lax.rem(LANES - SHIFT * r, LANES), 1)
        rh = pltpu.roll(right, LANES - SHIFT - SHIFT * r, 1)
        lh = jnp.where((lane < SHIFT) & (flags_ref[0, r] > 0), lh, 0.0)
        rh = jnp.where((lane >= LANES - SHIFT) & (flags_ref[1, r] > 0), rh, 0.0)
        out_ref[j] = (base_ref[:, cols].astype(F32) + lh + rh).astype(BF16)
        a = coef[:, j : j + 1]
        b = coef[:, RP + j : RP + j + 1]
        layer_ref[j] = (a * mid_ref[:, cols].astype(F32) + b).astype(BF16)


def add_blocks_kernel(count, *refs):
    ins, (keep_ref, give_ref) = refs[: 2 * count], refs[2 * count :]
    at = 0
    for p in range(count):
        a_ref, b_ref = ins[2 * p : 2 * p + 2]
        width = a_ref.shape[2]
        for j in range(a_ref.shape[0]):
            v = a_ref[j].astype(F32) + b_ref[j].astype(F32)
            (keep_ref, give_ref)[j % 2][j // 2, :, at : at + width] = v.astype(BF16)
        at += width


def add_halves_kernel(bit, index_ref, a_ref, b_ref, keep_ref, give_ref, scr):
    half = a_ref.shape[0] // 2
    mine = lax.rem(index_ref[0] // bit, 2)
    scr[...] = a_ref[...].astype(F32) + b_ref[...].astype(F32)
    keep_ref[...] = scr[pl.ds(pl.multiple_of(mine * half, 8), half)].astype(BF16)
    give_ref[...] = scr[pl.ds(pl.multiple_of((1 - mine) * half, 8), half)].astype(BF16)


def add_pieces_kernel(a_ref, b_ref, out_ref):
    v = a_ref[...].astype(F32) + b_ref[...].astype(F32)
    size = out_ref.shape[1]
    for p in range(out_ref.shape[0]):
        out_ref[p] = v[p * size : (p + 1) * size].astype(BF16)


def sum_copies_kernel(a_ref, *refs):
    out_ref = refs[-1]
    v = a_ref[0].astype(F32)
    for p in range(1, a_ref.shape[0]):
        v = v + a_ref[p].astype(F32)
    v = v.astype(BF16)
    for p in range(out_ref.shape[0]):
        out_ref[p, :, 0 : v.shape[1]] = v
        if len(refs) > 1:
            out_ref[p, :, v.shape[1] :] = refs[0][...]


def small_sum_kernel(csh, wide, bit_ref, keep_ref, got_ref, film_ref, attn_ref, mine_ref, other_ref, turn):
    v = keep_ref[0].astype(F32) + got_ref[0].astype(F32)
    cs = v.shape[0]
    film = 2 * wide + csh
    turn[...] = jnp.zeros(turn.shape, F32)
    turn[0:cs, 0 : 2 * csh] = v[:, film : film + 2 * csh]
    film_ref[...] = turn[...].T[0 : 2 * csh, 0:cs]
    attn_ref[...] = v[:, 2 * wide : film]
    last = film + 2 * csh
    even = bit_ref[0] == 0
    for one, two, rows, width in (
        (v[:, 0:wide], v[:, wide : 2 * wide], slice(0, cs), wide),
        (
            v[0:QUERIES, last : last + wide // 2],
            v[0:QUERIES, last + wide // 2 : last + wide],
            slice(cs, cs + QUERIES),
            wide // 2,
        ),
    ):
        mine_ref[rows, 0:width] = jnp.where(even, one, two).astype(BF16)
        other_ref[rows, 0:width] = jnp.where(even, two, one).astype(BF16)
    mine_ref[cs:, wide // 2 :] = jnp.zeros((QUERIES, wide // 2), BF16)
    other_ref[cs:, wide // 2 :] = jnp.zeros((QUERIES, wide // 2), BF16)


def small_piece_kernel(csh, wide, attn_ref, mine_ref, got_ref, out_ref):
    v = mine_ref[...].astype(F32) + got_ref[...].astype(F32)
    attn = attn_ref[...]
    cs = attn.shape[0]
    rows = out_ref.shape[0]
    at = 0
    for row in range(0, cs, rows):
        out_ref[:, at : at + wide] = v[row : row + rows].astype(BF16)
        out_ref[:, at + wide : at + wide + csh] = attn[row : row + rows].astype(BF16)
        at += wide + csh
    for row in range(0, QUERIES, rows):
        block = v[cs + row : cs + min(row + rows, QUERIES), 0 : wide // 2]
        if block.shape[0] < rows:
            pad = jnp.zeros((rows - block.shape[0], wide // 2), F32)
            block = jnp.concatenate([block, pad], axis=0)
        out_ref[:, at : at + wide // 2] = block.astype(BF16)
        at += wide // 2


def output_kernel(
    cs,
    csh,
    wide,
    seq,
    bit_ref,
    *refs,
):
    own1, got1, own2, got2, refs = *refs[:4], refs[4:]
    (
        queries_ref,
        wq_ref,
        step_ref,
        conv_ref,
        cond_ref,
        res_ref,
        skip_ref,
        gqueries_ref,
        gquery_ref,
        key_ref,
        value_ref,
        attn_ref,
        scr1,
        scr2,
        small,
        qscr,
        dq,
    ) = refs
    count, size = own1.shape[0], own1.shape[1]
    wide1 = scr1.shape[1]
    bit = bit_ref[0]
    for one, two, side in ((own1, own2, bit), (got1, got2, 1 - bit)):
        for p in range(count):
            rows = pl.ds(pl.multiple_of((side * count + p) * size, 8), size)
            v = one[p].astype(F32)
            scr1[rows] = v[:, 0:wide1]
            small[pl.ds(pl.multiple_of((2 * p + side) * size, 8), size)] = v[:, wide1:]
            scr2[rows] = two[p].astype(F32)
    for t in range(4):
        rows = slice(t * cs, (t + 1) * cs)
        lanes = slice(t * LANES, (t + 1) * LANES)
        res_ref[:, lanes] = scr1[rows, 0:LANES]
        skip_ref[:, lanes] = scr1[rows, LANES : 2 * LANES]
        step_ref[:, lanes] = scr2[rows, C : C + LANES]
        if t < 3:
            conv_ref[t, :, 0:C] = scr1[rows, 2 * LANES : 2 * LANES + C]
            conv_ref[t, :, C : 2 * C] = scr2[rows, 0:C]
        else:
            cond_ref[:, 0:C] = scr1[rows, 2 * LANES : 2 * LANES + C]
            cond_ref[:, C : 2 * C] = scr2[rows, 0:C]
    dq[...] = jnp.zeros(dq.shape, F32)
    for s in range(seq):
        v = small[s * size : (s + 1) * size]
        group, even = s // 2, s % 2 == 0
        out = key_ref if even else value_ref
        at = 0
        for row in range(0, cs, size):
            out[row : row + size, group * wide : (group + 1) * wide] = v[:, at : at + wide]
            attn_ref[row : row + size, s * csh : (s + 1) * csh] = v[:, at + wide : at + wide + csh]
            at += wide + csh
        first = group * wide + (0 if even else wide // 2)
        for row in range(0, QUERIES, size):
            count = min(size, QUERIES - row)
            dq[row : row + count, first : first + wide // 2] = v[0:count, at : at + wide // 2]
            at += wide // 2
    qscr[...] = jnp.zeros((LANES, LANES), F32)
    qscr[0:QUERIES, 0:cs] = queries_ref[...].astype(F32)
    qt = qscr[...].T.astype(BF16)
    d = dq[...]
    hi = d.astype(BF16)
    lo = (d - hi.astype(F32)).astype(BF16)
    gquery_ref[...] = (nn(qt, hi) + nn(qt, lo))[0:cs]
    gqueries_ref[...] = fold(nt(parts(d[0:QUERIES], 2), wq_ref[...]), 2)


def attention_back_kernel(
    rows,
    csh,
    dp,
    off_ref,
    prow,
    probs_ref,
    u_ref,
    qp_ref,
    qkv_ref,
    pooled_ref,
    memory_ref,
    dfilm_ref,
    got_ref,
    keep_ref,
    give_ref,
    ds,
    stack,
    right,
    out,
):
    count = got_ref.shape[0]
    total = prow.shape[1] * prow.shape[2]
    cs = C // dp
    table = prow[...].reshape(rows * total, C)
    wide = qp_ref.shape[1]
    heads = wide // HEAD_DIM
    datt = got_ref[0, 3 * RP : 4 * RP, 0:wide]
    dmem = got_ref[0, 2 * RP : 3 * RP, 0:csh]
    for s in range(1, count):
        datt = datt + got_ref[s, 3 * RP : 4 * RP, 0:wide]
        dmem = dmem + got_ref[s, 2 * RP : 3 * RP, 0:csh]
    datt = datt[0:8] * (1.0 / QUERIES)
    vh = []
    for g in range(heads):
        first = 2 * wide + g * HEAD_DIM
        v = parts(datt[:, g * HEAD_DIM : (g + 1) * HEAD_DIM], 2)
        vh.append(fold(nn(v, qkv_ref[first : first + HEAD_DIM]), 2))
    vh = jnp.concatenate(vh, axis=0)
    dp_all = fold(nt(parts(vh, 2), table), 2)
    for r in range(rows):
        cols = slice(r * total, (r + 1) * total)
        for g in range(heads):
            mine = slice(g * QUERIES, (g + 1) * QUERIES)
            p = probs_ref[mine, cols]
            dpr = dp_all[8 * g + r : 8 * g + r + 1, cols]
            inner = jnp.sum(p * dpr, axis=1, keepdims=True)
            ds[mine, cols] = p * (dpr - inner)
    tt = fold(nn(parts(ds[...], 2), table), 2)
    scale = 1.0 / math.sqrt(HEAD_DIM)
    dq = []
    stack[...] = jnp.zeros(stack.shape, F32)
    right[...] = jnp.zeros(right.shape, F32)
    stack[0 : heads * QUERIES] = tt
    stack[64:80] = u_ref[...]
    stack[80:96] = pooled_ref[...].astype(F32)
    stack[96:112] = memory_ref[...].astype(F32)
    for g in range(heads):
        cols = slice(g * HEAD_DIM, (g + 1) * HEAD_DIM)
        mine = slice(g * QUERIES, (g + 1) * QUERIES)
        wk = qkv_ref[wide + g * HEAD_DIM : wide + (g + 1) * HEAD_DIM]
        dq.append(fold(nt(parts(tt[mine], 2), wk), 2) * scale)
        right[mine, cols] = qp_ref[:, cols] * scale
        right[64 + 8 * g : 72 + 8 * g, wide + cols.start : wide + cols.stop] = datt[:, cols]
    right[80:96, 2 * wide : 2 * wide + csh] = dmem
    right[96:112, 2 * wide + csh : 2 * wide + 3 * csh] = dfilm_ref[...].astype(F32)
    out[...] = lax.dot_general(
        stack[...].T,
        right[...],
        (((1,), (0,)), ((), ())),
        precision=lax.Precision.HIGHEST,
        preferred_element_type=F32,
    )
    last = 2 * wide + 3 * csh
    for k in range(dp):
        ref = (keep_ref, give_ref)[k % 2]
        ref[k // 2] = out[pl.ds(pl.multiple_of(off_ref[k], 16), cs)].astype(BF16)
        for g in range(heads):
            first = last + g * HEAD_DIM
            ref[k // 2, 0:QUERIES, first : first + HEAD_DIM] = dq[g].astype(BF16)


def exchange(pieces, axis, groups=None):
    return lax.all_to_all(
        pieces, axis, split_axis=0, concat_axis=0, axis_index_groups=groups, tiled=True
    )


def flipped(v, axis, size, bit):
    return lax.ppermute(v, axis, [(d, d ^ bit) for d in range(size)])


class Reduction:
    def __init__(self, call, name, keep, give, dp, seq, index):
        self.call, self.name, self.dp, self.seq, self.index = call, name, dp, seq, index
        self.keep, self.flip = keep, 1
        self.got = flipped(give, "dp", dp, 1)

    def over_blocks(self, after=(), others=()):
        while 2 * self.flip < self.dp:
            group = (self,) + tuple(others)
            others = ()
            args = []
            for part in group:
                args += [part.keep, Got(part.got)]
            width = sum(part.keep.shape[2] for part in group)
            half = sds((self.keep.shape[0] // 2, self.keep.shape[1], width), BF16)
            self.keep, give = self.call(
                functools.partial(add_blocks_kernel, len(group)),
                (half, half),
                "blocks_" + self.name,
                args,
                after=after,
                in_specs=[VM] * len(args),
                out_specs=(VM, VM),
            )
            self.flip *= 2
            self.got = flipped(give, "dp", self.dp, self.flip)
        self.rest = self.keep.shape[1:]

    def over_half(self, after=()):
        rows, width = self.rest
        half = sds((rows // 2, width), BF16)
        self.keep, give = self.call(
            functools.partial(add_halves_kernel, 1),
            (half, half),
            "half_" + self.name,
            (self.index, self.keep.reshape(rows, width), Got(self.got.reshape(rows, width))),
            after=after,
            in_specs=[SM, VM, VM],
            out_specs=(VM, VM),
            scratch_shapes=[pltpu.VMEM((rows, width), F32)],
        )
        self.got = flipped(give, "seq", self.seq, 1)

    def over_pieces(self, after=()):
        rows, width = self.rest
        count = self.seq // 2
        self.groups = [[2 * k + b for k in range(count)] for b in range(2)]
        pieces = self.call(
            add_pieces_kernel,
            sds((count, rows // self.seq, width), BF16),
            "pieces_" + self.name,
            (self.keep, Got(self.got)),
            after=after,
            in_specs=[VM, VM],
            out_specs=VM,
        )
        self.got = exchange(pieces, "seq", self.groups)

    def over_copies(self, after=(), extra=None):
        args, (count, rows, width) = [Got(self.got)], self.got.shape
        if extra is not None:
            args.append(extra)
            width += extra.shape[1]
        copies = self.call(
            sum_copies_kernel,
            sds((count, rows, width), BF16),
            "copies_" + self.name,
            args,
            after=after,
            in_specs=[VM] * len(args),
            out_specs=VM,
        )
        own = exchange(copies, "seq", self.groups)
        return Got(own), Got(flipped(own, "seq", self.seq, 1))


def body(
    dp,
    seq,
    x_in,
    cond,
    segment_ids,
    diffusion_steps,
    prompt,
    prompt_lengths,
    w_step,
    w_conv,
    w_cond,
    w_res,
    w_skip,
    queries,
    w_query,
    w_key,
    w_value,
    w_attn_out,
    w_film,
    d_out,
    d_skip,
):
    call = Caller()
    rows = x_in.shape[0]
    frames = x_in.shape[2]
    steps = rows // NR
    cols = rows * frames
    cs = C // dp
    csh = C // seq
    heads = 2 * HEADS // seq
    wide = heads * HEAD_DIM
    arows = rows // 2
    pl_local = prompt.shape[1]
    prompt_all = pl_local * seq
    sidx = lax.axis_index("seq")
    didx = lax.axis_index("dp")
    group = (sidx // 2).astype(jnp.int32).reshape(1)
    bit = (sidx % 2).astype(jnp.int32).reshape(1)
    up = [(i, i + 1) for i in range(seq - 1)]
    down = [(i + 1, i) for i in range(seq - 1)]
    order = jnp.bitwise_xor(didx, jnp.arange(dp, dtype=jnp.int32)).astype(jnp.int32)
    offsets = jnp.concatenate([order * cs, bit, 1 - bit])
    index = sidx.astype(jnp.int32).reshape(1)

    def gather(pack, side=None, middle=None):
        if dp == 4 and side is not None:
            mine = flipped(side, "dp", dp, 2)
            inner = flipped(middle, "dp", dp, 2)
            other = flipped(mine, "seq", seq, 1)
            near = [(0, None, pack), (2, 0, mine), (2, 2, inner), (2, 1, other)]
            pieces = near + [(k + 1, h, flipped(v, "dp", dp, 1)) for k, h, v in near]
        else:
            pieces = [(0, None, pack)]
            flip = dp // 2
            while flip:
                pieces += [(k + flip, h, flipped(v, "dp", dp, flip)) for k, h, v in pieces]
                flip //= 2
        pieces.sort(key=lambda piece: piece[0])
        meta = [(k, h) for k, h, _ in pieces]
        return meta, [v if k == 0 else Got(v) for k, _, v in pieces]

    off_qkv = C + 2 * csh
    qkv_rows = -(-(3 * wide + QUERIES) // LANES) * LANES
    head_width = -(-(off_qkv + qkv_rows) // LANES) * LANES
    pack, mine, other = call(
        functools.partial(head_pack_kernel, csh, wide),
        (
            sds((cs, head_width), BF16),
            sds((arows, pl_local, C), BF16),
            sds((arows, pl_local, C), BF16),
        ),
        "head_pack",
        (
            group,
            bit,
            w_attn_out,
            jnp.transpose(w_film, (1, 2, 0)).reshape(2 * csh, cs),
            w_query,
            w_key,
            w_value,
            queries,
            prompt,
        ),
        in_specs=[SM, SM] + [VM] * 7,
        out_specs=(VM,) * 3,
        scratch_shapes=[pltpu.VMEM((2 * LANES, LANES), F32)],
    )
    _, head_pieces = gather(pack)
    partner = flipped(other, "seq", seq, 1)
    pair = call(
        pair_kernel,
        sds((seq // 2, 2, arows, pl_local, C), BF16),
        "pair",
        (mine, Got(partner)),
        in_specs=[VM, VM],
        out_specs=VM,
    )
    z_groups = [[2 * k + b for k in range(seq // 2)] for b in range(2)]
    prompts = Got(exchange(pair, "seq", z_groups))
    first, last = call(
        edge_kernel,
        (sds((C, LANES), BF16), sds((C, LANES), BF16)),
        "edges",
        (x_in,),
        after=("pair",),
        in_specs=[VM],
        out_specs=(VM, VM),
    )
    call.done["far_heads"] = head_pieces[dp // 2].array
    middle = 2 * C - 2 * SIDE + 3 * C // 4
    pack, side, middle = call(
        functools.partial(turned_pack_kernel, cs),
        (
            sds((2 * SIDE + middle, 4 * cs), BF16),
            sds((SIDE, 4 * cs), BF16),
            sds((middle, 4 * cs), BF16),
        ),
        "turned_pack",
        (bit, w_conv, w_cond, w_res, w_skip, w_step),
        after=("edges", "far_heads"),
        in_specs=[SM] + [VM] * 5,
        out_specs=(VM, VM, VM),
        scratch_shapes=[pltpu.VMEM((4 * cs, 2 * C), BF16)],
    )
    meta, turned = gather(pack, side, middle)
    copies = 4 * dp * (1 + 3 * C // (4 * cs))
    left_halo = lax.ppermute(last, "seq", up)
    right_halo = lax.ppermute(first, "seq", down)

    block_ids = segment_ids[:, ::frames]
    padded_ids = jnp.pad(block_ids, ((0, 0), (1, 1)), constant_values=-1)
    mine = lax.dynamic_slice_in_dim(padded_ids, sidx, 3, 1)
    flags = jnp.stack([mine[:, 0] == mine[:, 1], mine[:, 2] == mine[:, 1]]).astype(jnp.int32)
    block_ids = jnp.pad(block_ids, ((0, RP - rows), (0, 0)))
    half = C // 2
    frequency = jnp.exp(jnp.arange(half, dtype=F32) * (-math.log(10000.0) / half))
    step_rows = jnp.pad(diffusion_steps.astype(F32), (0, LANES - rows))
    live_rows = jnp.arange(LANES, dtype=jnp.int32)[:, None] < rows
    angles = step_rows[:, None] * frequency[None, :]
    embedding = jnp.concatenate([jnp.sin(angles), jnp.cos(angles)], axis=1)
    embedding = jnp.where(live_rows, embedding, 0.0).astype(BF16)
    lengths = lax.dynamic_slice_in_dim(prompt_lengths, (sidx % 2) * arows, arows, 0)

    apack, prow, probs, u, pooled_head, qp, qkv = call(
        functools.partial(attention_kernel, dp, arows, heads, seq // 2, off_qkv),
        (
            sds((C, head_width), BF16),
            sds((arows, seq, pl_local, C), BF16),
            sds((heads * QUERIES, arows * prompt_all), F32),
            sds((RP, C), F32),
            sds((RP, LANES), F32),
            sds((QUERIES, wide), F32),
            sds((qkv_rows, C), BF16),
        ),
        "attention",
        (offsets, bit, lengths, prompts, *head_pieces),
        in_specs=[SM, SM, SM, HB] + [HB] * dp,
        out_specs=(VM,) * 7,
        scratch_shapes=[
            pltpu.VMEM((RP, arows * prompt_all), F32),
            pltpu.SemaphoreType.DMA((dp + seq,)),
        ],
    )

    row_block = pl.BlockSpec((NR, C, LANES), lambda i: (i, 0, 0))

    def col_block(height):
        return pl.BlockSpec((height, NR * LANES), lambda i: (0, i))

    def still(shape):
        return pl.BlockSpec(shape, lambda i: (0,) * len(shape))

    inp, gated, factor_a, factor_b, skip_out, mid, stats = call(
        functools.partial(forward_kernel, meta, dp, csh),
        (
            sds((4 * C, cols), BF16),
            sds((C, cols), BF16),
            sds((C, cols), BF16),
            sds((C, cols), BF16),
            sds(x_in.shape, BF16),
            sds((C, cols), BF16),
            sds((seq, 3 * RP, 2 * csh), F32),
        ),
        "wavenet",
        (
            offsets,
            flags,
            x_in,
            cond,
            d_out,
            Got(left_halo),
            Got(right_halo),
            embedding,
            pooled_head,
            *turned,
        ),
        flops=2 * cols * (4 * C * 2 * C + 2 * C * C),
        nbytes=30e6,
        grid=(steps,),
        in_specs=[
            SM,
            SM,
            row_block,
            row_block,
            row_block,
            whole((C, LANES)),
            whole((C, LANES)),
            whole((LANES, C)),
            whole((RP, LANES)),
        ]
        + [HB] * len(turned),
        out_specs=(
            col_block(4 * C),
            col_block(C),
            col_block(C),
            col_block(C),
            row_block,
            col_block(C),
            still((seq, 3 * RP, 2 * csh)),
        ),
        scratch_shapes=[
            pltpu.VMEM((2 * C, 4 * C), BF16),
            pltpu.VMEM((C, 2 * C), BF16),
            pltpu.VMEM((C, C), BF16),
            pltpu.VMEM((2 * C, C), BF16),
            pltpu.VMEM((C, LANES), F32),
            pltpu.VMEM((C, LANES), F32),
            pltpu.SemaphoreType.DMA((copies,)),
        ],
    )
    stats_got = exchange(stats, "seq")
    gskip = call(
        skip_grad_kernel,
        sds((C, C), BF16),
        "skip",
        (gated, d_skip),
        in_specs=[VM, VM],
        out_specs=VM,
        scratch_shapes=[pltpu.VMEM((C, cols), BF16)],
    )

    coef_out, dfilm, pooled, memory = call(
        functools.partial(stats_kernel, csh, heads, arows),
        (
            sds((seq, 4 * RP, 2 * csh), F32),
            sds((RP, 2 * csh), BF16),
            sds((RP, C), BF16),
            sds((RP, C), BF16),
        ),
        "segments",
        (block_ids, Got(stats_got), apack),
        after=("skip",),
        in_specs=[VM, VM, VM],
        out_specs=(VM, VM, VM, VM),
        scratch_shapes=[pltpu.VMEM((RP, C), F32)],
    )
    coef = Got(exchange(coef_out, "seq"))

    def gate_block(i):
        return jnp.minimum(i, steps - 1)

    def shard(i):
        return jnp.maximum(i - steps, 0)

    def gate_cols(height):
        return pl.BlockSpec((height, NR * LANES), lambda i, order: (0, gate_block(i)))

    gate_rows = pl.BlockSpec((NR, C, LANES), lambda i, order: (gate_block(i), 0, 0))
    wide1, wide2 = C + 2 * LANES, C

    def part(width):
        return sds((dp // 2, 4 * cs, width), BF16)

    def part_spec(width):
        return pl.BlockSpec((1, 4 * cs, width), lambda i, order: (shard(i) // 2, 0, 0))

    outs = call(
        functools.partial(backward_kernel, meta, dp, csh, steps),
        (
            sds((2 * C, cols), BF16),
            sds((C, cols), BF16),
            sds((2 * C, LANES), F32),
            part(wide1),
            part(wide2),
            part(wide1),
            part(wide2),
        ),
        "backward",
        (order, offsets, coef, mid, d_out, d_skip, factor_a, factor_b, inp, gated, gskip, flags, *turned),
        prefetch=1,
        grid=(steps + dp,),
        in_specs=[
            SM,
            pl.BlockSpec(
                (seq, 4 * RP, 2 * csh), lambda i, order: (0, 0, 0), pipeline_mode=pl.Buffered(1)
            ),
            gate_cols(C),
            gate_rows,
            gate_rows,
            gate_cols(C),
            gate_cols(C),
            pl.BlockSpec((4 * cs, cols), lambda i, order: (order[shard(i)], 0)),
            pl.BlockSpec((cs, cols), lambda i, order: (order[shard(i)], 0)),
            pl.BlockSpec((cs, C), lambda i, order: (order[shard(i)], 0)),
            SM,
        ]
        + [HB] * len(turned),
        out_specs=(
            gate_cols(2 * C),
            gate_cols(C),
            pl.BlockSpec((2 * C, LANES), lambda i, order: (0, 0)),
            part_spec(wide1),
            part_spec(wide2),
            part_spec(wide1),
            part_spec(wide2),
        ),
        scratch_shapes=[
            pltpu.VMEM((LANES, C), F32),
            pltpu.VMEM((C, LANES), F32),
            pltpu.VMEM((C, 2 * C), BF16),
            pltpu.VMEM((2 * C, NR * LANES), BF16),
            pltpu.VMEM((cols, 2 * C), BF16),
            pltpu.VMEM((cols, C), BF16),
            pltpu.SemaphoreType.DMA((copies,)),
        ],
    )
    dpre, dres, sums = outs[0:3]
    part1 = Reduction(call, "1", outs[3], outs[5], dp, seq, index)
    part2 = Reduction(call, "2", outs[4], outs[6], dp, seq, index)
    part1.over_blocks()
    keep, give = call(
        functools.partial(step_grad_kernel, meta, dp),
        (part(LANES), part(LANES)),
        "step_grad",
        (offsets, sums, embedding, *turned),
        after=("blocks_1",),
        in_specs=[SM, VM, VM] + [HB] * len(turned),
        out_specs=(VM, VM),
        scratch_shapes=[
            pltpu.VMEM((2 * C, 4 * C), BF16),
            pltpu.VMEM((C, C), F32),
            pltpu.SemaphoreType.DMA((copies,)),
        ],
    )
    part_step = Reduction(call, "step", keep, give, dp, seq, index)

    right_width = -(-(3 * wide + 3 * csh) // LANES) * LANES
    block = sds((dp // 2, cs, right_width), BF16)
    keep, give = call(
        functools.partial(attention_back_kernel, arows, csh, dp),
        (block, block),
        "attention_back",
        (offsets, prow, probs, u, qp, qkv, pooled, memory, dfilm, coef),
        after=("step_grad",),
        in_specs=[SM] + [VM] * 9,
        out_specs=(VM, VM),
        scratch_shapes=[
            pltpu.VMEM((heads * QUERIES, arows * prompt_all), F32),
            pltpu.VMEM((LANES, C), F32),
            pltpu.VMEM((LANES, right_width), F32),
            pltpu.VMEM((C, right_width), F32),
        ],
    )
    small = Reduction(call, "small", keep, give, dp, seq, index)
    part2.over_blocks(("attention_back",), (part_step,))
    small.over_blocks(("blocks_2",))
    part1.over_half(("blocks_small",))

    base, first, last = call(
        functools.partial(input_grad_kernel, meta, dp),
        (sds((C, cols), BF16), sds((C, LANES), BF16), sds((C, LANES), BF16)),
        "input_grad",
        (offsets, dpre, dres, *turned),
        after=("half_1",),
        grid=(steps,),
        in_specs=[SM, col_block(2 * C), col_block(C)] + [HB] * len(turned),
        out_specs=(
            col_block(C),
            still((C, LANES)),
            still((C, LANES)),
        ),
        scratch_shapes=[
            pltpu.VMEM((2 * C, 4 * C), BF16),
            pltpu.VMEM((3, C, 2 * C), BF16),
            pltpu.VMEM((C, LANES), F32),
            pltpu.VMEM((C, LANES), F32),
            pltpu.SemaphoreType.DMA((copies,)),
        ],
    )
    from_left = lax.ppermute(last, "seq", up)
    from_right = lax.ppermute(first, "seq", down)
    rest = 4 * cs // seq
    small_width = (cs // rest) * (wide + csh) + max(1, QUERIES // rest) * (wide // 2)
    part1.over_pieces(("input_grad",))
    part2.over_half(("pieces_1",))
    grad_film, attn_rows, mine, other = call(
        functools.partial(small_sum_kernel, csh, wide),
        (
            sds((2 * csh, cs), F32),
            sds((cs, csh), F32),
            sds((cs + QUERIES, wide), BF16),
            sds((cs + QUERIES, wide), BF16),
        ),
        "small_sum",
        (bit, small.keep, Got(small.got)),
        after=("half_2",),
        in_specs=[SM, VM, VM],
        out_specs=(VM,) * 4,
        scratch_shapes=[pltpu.VMEM((LANES, LANES), F32)],
    )
    partner = flipped(other, "seq", seq, 1)
    grad_input, layer_out = call(
        functools.partial(finish_kernel, csh),
        (sds(x_in.shape, BF16), sds(x_in.shape, BF16)),
        "grad_input",
        (flags, base, Got(from_left), Got(from_right), mid, coef),
        after=("small_sum",),
        grid=(steps,),
        in_specs=[
            SM,
            col_block(C),
            whole((C, LANES)),
            whole((C, LANES)),
            col_block(C),
            whole((seq, 4 * RP, 2 * csh)),
        ],
        out_specs=(row_block, row_block),
        scratch_shapes=[pltpu.VMEM((LANES, C), F32), pltpu.VMEM((C, LANES), F32)],
    )
    small_piece = call(
        functools.partial(small_piece_kernel, csh, wide),
        sds((rest, small_width), BF16),
        "small_piece",
        (attn_rows, mine, Got(partner)),
        after=("grad_input",),
        in_specs=[VM] * 3,
        out_specs=VM,
    )
    part2.over_pieces(("grad_input",))
    ones = part1.over_copies(extra=small_piece)
    twos = part2.over_copies()

    (
        grad_step,
        grad_conv,
        grad_cond,
        grad_res,
        grad_skip,
        grad_queries,
        grad_query,
        grad_key,
        grad_value,
        grad_attn,
    ) = call(
        functools.partial(output_kernel, cs, csh, wide, seq),
        (
            sds((cs, C), F32),
            sds((3, cs, 2 * C), F32),
            sds((cs, 2 * C), F32),
            sds((cs, C), F32),
            sds((cs, C), F32),
            sds((QUERIES, cs), F32),
            sds((cs, C), F32),
            sds((cs, C), F32),
            sds((cs, C), F32),
            sds((cs, C), F32),
        ),
        "outputs",
        (bit, *ones, *twos, queries, w_query),
        in_specs=[SM] + [VM] * 6,
        out_specs=(VM,) * 10,
        scratch_shapes=[
            pltpu.VMEM((4 * cs, wide1), F32),
            pltpu.VMEM((4 * cs, wide2 + LANES), F32),
            pltpu.VMEM((4 * cs, small_width), F32),
            pltpu.VMEM((LANES, LANES), F32),
            pltpu.VMEM((LANES, C), F32),
        ],
    )
    return (
        layer_out,
        skip_out,
        grad_input,
        grad_step,
        grad_conv,
        grad_cond,
        grad_res,
        grad_skip,
        grad_queries,
        grad_query,
        grad_key,
        grad_value,
        grad_attn,
        jnp.transpose(grad_film.reshape(2, csh, cs), (2, 0, 1)),
    )


def solution(mesh):
    frames = P("dp", None, "seq")
    matrix = P("dp", None)
    return jax.shard_map(
        functools.partial(body, mesh.shape["dp"], mesh.shape["seq"]),
        mesh=mesh,
        in_specs=(
            frames,
            frames,
            P("dp", None),
            P("dp"),
            P("dp", "seq", None),
            P("dp"),
            matrix,
            P(None, "dp", None),
            matrix,
            matrix,
            matrix,
            P(None, "dp"),
            matrix,
            matrix,
            matrix,
            matrix,
            frames,
            frames,
            frames,
        ),
        out_specs=(
            frames,
            frames,
            frames,
            matrix,
            P(None, "dp", None),
            matrix,
            matrix,
            matrix,
            P(None, "dp"),
            matrix,
            matrix,
            matrix,
            matrix,
            frames,
        ),
        check_vma=False,
    )
```

```python
import functools
import math

import jax
import jax.numpy as jnp
from jax import lax
from jax.experimental import pallas as pl
from jax.experimental.pallas import tpu as pltpu
from jax.sharding import PartitionSpec as P

C = 512
HEADS = 8
QUERIES = 32
HEAD_DIM = 64
SHIFT = 4
SQRT_HALF = 0.7071067811865476
NORM_EPS = 1e-05
MASKED_SCORE = -1e30
LANES = 128
RP = 16
NR = 4
EARLY = 640
F32 = jnp.float32
BF16 = jnp.bfloat16
VMEM_BYTES = 50 * 1024 * 1024


def nn(a, b):
    return lax.dot_general(a, b, (((1,), (0,)), ((), ())), preferred_element_type=F32)


def nt(a, b):
    return lax.dot_general(a, b, (((1,), (1,)), ((), ())), preferred_element_type=F32)


def parts(v, count):
    out = []
    for _ in range(count):
        low = v.astype(BF16).astype(F32)
        out.append(low)
        v = v - low
    return jnp.concatenate(out, axis=0).astype(BF16)


def fold(v, count):
    rows = v.shape[0] // count
    total = v[:rows]
    for k in range(1, count):
        total = total + v[k * rows : (k + 1) * rows]
    return total


def lane_ids(shape):
    return lax.broadcasted_iota(jnp.int32, shape, len(shape) - 1)


def sds(shape, dtype):
    return jax.ShapeDtypeStruct(shape, dtype)


VM = pl.BlockSpec(memory_space=pltpu.VMEM)
HB = pl.BlockSpec(memory_space=pl.ANY)
SM = pl.BlockSpec(memory_space=pltpu.SMEM)


def whole(shape):
    return pl.BlockSpec(shape, lambda i: (0,) * len(shape), pipeline_mode=pl.Buffered(1))


class Got:
    def __init__(self, array):
        self.array = array


class Caller:
    def __init__(self):
        self.done = {}

    def __call__(self, kernel, out_shape, name, args, flops=0, nbytes=0, prefetch=0, after=(), **kw):
        single = not isinstance(out_shape, tuple)
        shapes = (out_shape,) if single else out_shape
        pinned = tuple(pltpu.HBM(v.shape, v.dtype) for v in shapes)
        in_specs = list(kw.pop("in_specs"))
        count = prefetch + len(in_specs)
        args = list(args)
        extra = len(after)
        for before in after:
            in_specs.append(HB)
            args.append(self.done[before])

        def run(*refs):
            return kernel(*refs[:count], *refs[count + extra :])

        values = []
        for k, v in enumerate(args):
            spec = SM if k < prefetch else in_specs[k - prefetch]
            if isinstance(v, Got):
                values.append(v.array)
            elif spec is SM:
                values.append(v)
            else:
                values.append(pltpu.with_memory_space_constraint(v, pltpu.HBM))
        spec = pltpu.PrefetchScalarGridSpec(
            num_scalar_prefetch=prefetch,
            grid=kw.pop("grid", ()),
            in_specs=in_specs,
            out_specs=kw.pop("out_specs"),
            scratch_shapes=kw.pop("scratch_shapes", ()),
        )
        out = pl.pallas_call(
            run,
            out_shape=pinned[0] if single else pinned,
            name=name,
            grid_spec=spec,
            cost_estimate=pl.CostEstimate(
                flops=1, bytes_accessed=1, transcendentals=0
            ),
            compiler_params=pltpu.CompilerParams(vmem_limit_bytes=VMEM_BYTES),
        )(*values)
        self.done[name] = out if single else out[0]
        return out


def head_pack_kernel(
    csh,
    local,
    group_ref,
    bit_ref,
    attn_ref,
    film_ref,
    wq_ref,
    wk_ref,
    wv_ref,
    queries_ref,
    prompt_ref,
    out_ref,
    mine_ref,
    other_ref,
    scr,
):
    cs = attn_ref.shape[0]
    arows = mine_ref.shape[0]
    mine_ref[...] = prompt_ref[pl.ds(bit_ref[0] * arows, arows)]
    other_ref[...] = prompt_ref[pl.ds((1 - bit_ref[0]) * arows, arows)]
    out_ref[:, 0:C] = attn_ref[...]
    off = C
    scr[...] = jnp.zeros((2 * LANES, LANES), F32)
    scr[0 : 2 * csh, 0:cs] = film_ref[...].astype(F32)
    scr[LANES : LANES + QUERIES, 0:cs] = queries_ref[...].astype(F32)
    film = scr[0:LANES].T[0:cs]
    table = scr[LANES : 2 * LANES].T[0:cs]
    turn = lax.rem(C - local * group_ref[0], C)
    blocks = [film[:, 0 : 2 * csh]]
    for ref in (wq_ref, wk_ref, wv_ref):
        blocks.append(pltpu.roll(ref[...].astype(F32), turn, 1)[:, 0:local])
    blocks.append(table)
    for block in blocks:
        width = min(block.shape[1], out_ref.shape[1] - off)
        out_ref[:, off : off + width] = block[:, 0:width].astype(BF16)
        off += width
    if off < out_ref.shape[1]:
        out_ref[:, off:] = jnp.zeros((cs, out_ref.shape[1] - off), BF16)


SIDE = 480


def turned_pack_kernel(cs, bit_ref, conv_ref, cond_ref, res_ref, skip_ref, step_ref, out_ref, side_ref, middle_ref, scr):
    for k in range(3):
        scr[k * cs : (k + 1) * cs] = conv_ref[k]
    scr[3 * cs : 4 * cs] = cond_ref[...]
    turned = scr[...].T
    out_ref[0 : 2 * C - SIDE] = turned[0 : 2 * C - SIDE]
    at = 2 * C - SIDE
    for ref in (res_ref, skip_ref, step_ref):
        for lane in range(0, C, 4 * cs):
            out_ref[at : at + cs] = ref[:, lane : lane + 4 * cs]
            at += cs
    out_ref[at : at + SIDE] = turned[2 * C - SIDE :]
    middle_ref[...] = out_ref[SIDE:at]
    side_ref[...] = out_ref[pl.ds(pl.multiple_of(bit_ref[0] * at, 16), SIDE)]


def pair_kernel(a_ref, b_ref, out_ref):
    for p in range(out_ref.shape[0]):
        out_ref[p, 0] = a_ref[...]
        out_ref[p, 1] = b_ref[...]


def edge_kernel(x_ref, first_ref, last_ref):
    rows = x_ref.shape[0]
    lane = lane_ids((C, LANES))
    first = jnp.zeros((C, LANES), F32)
    last = jnp.zeros((C, LANES), F32)
    for r in range(rows):
        v = x_ref[r].astype(F32)
        here = (lane // SHIFT) == r
        first = jnp.where(here, pltpu.roll(v, SHIFT * r, 1) if r else v, first)
        last = jnp.where(here, pltpu.roll(v, SHIFT * r + SHIFT, 1), last)
    first_ref[...] = first.astype(BF16)
    last_ref[...] = last.astype(BF16)


def begin(copies):
    for copy in copies:
        copy.start()


def finish(copies):
    for copy in copies:
        copy.wait()


def turned_copies(meta, refs, off_ref, cs, wt, others, sems):
    dp = len({k for k, _ in meta})
    pairs = []

    def conv(k, ref, first, row, rows):
        if wt is not None:
            lanes = pl.ds(pl.multiple_of(off_ref[k] * 4, LANES), 4 * cs)
            at = row if isinstance(row, int) else pl.multiple_of(row, 16)
            pairs.append((ref.at[pl.ds(first, rows)], wt.at[pl.ds(at, rows), lanes]))

    def rest(k, ref, at):
        row = pl.ds(pl.multiple_of(off_ref[k], 16), cs)
        for other in others:
            for lane in range(0, C, 4 * cs):
                if other is not None:
                    dst, start = other
                    pairs.append((ref.at[pl.ds(at, cs)], dst.at[row, pl.ds(start + lane, 4 * cs)]))
                at += cs

    inner = 2 * C - 2 * SIDE
    for (k, which), ref in zip(meta, refs):
        if which is None:
            conv(k, ref, 0, 0, SIDE + inner)
            rest(k, ref, SIDE + inner)
            conv(k, ref, ref.shape[0] - SIDE, 2 * C - SIDE, SIDE)
        elif which == 2:
            conv(k, ref, 0, SIDE, inner)
            rest(k, ref, inner)
        else:
            conv(k, ref, 0, off_ref[dp + which] * (2 * C - SIDE), SIDE)
    return [pltpu.make_async_copy(a, b, sems.at[n]) for n, (a, b) in enumerate(pairs)]


def head_copies(refs, off_ref, dst, sems):
    copies = []
    for k, ref in enumerate(refs):
        row = pl.ds(pl.multiple_of(off_ref[k], 16), ref.shape[0])
        copies.append(pltpu.make_async_copy(ref, dst.at[row], sems.at[k]))
    return copies


def forward_kernel(
    meta, dp, csh, off_ref, flags_ref, x_ref, cond_ref, dout_ref, left_ref, right_ref, emb_ref, pooled_ref, *refs
):
    turned, refs = refs[: len(meta)], refs[len(meta) :]
    (
        inp_ref,
        gated_ref,
        fa_ref,
        fb_ref,
        skip_ref,
        mid_ref,
        stats_ref,
        wt_ref,
        rn_ref,
        step_ref,
        rst_ref,
        lift_ref,
        acc_ref,
        sems,
    ) = refs
    cs = C // dp
    i = pl.program_id(0)
    lane = lane_ids((C, LANES))

    @pl.when(i == 0)
    def _():
        copies = turned_copies(
            meta,
            turned,
            off_ref,
            cs,
            wt_ref,
            ((rn_ref, 0), (rn_ref, C), (step_ref, 0)),
            sems,
        )
        begin(copies)
        acc_ref[...] = jnp.zeros((C, LANES), F32)
        finish(copies)
        lift = nn(emb_ref[0:RP], step_ref[...])
        lift = jnp.concatenate([lift, jnp.zeros((LANES - RP, C), F32)], axis=0)
        lift_ref[...] = lift.T
        rst_ref[...] = rn_ref[...].T

    lift = pltpu.roll(lift_ref[...], lax.rem(LANES - NR * i, LANES), 1)
    left = left_ref[...].astype(F32)
    right = right_ref[...].astype(F32)

    def put(tap, cols, value):
        for d in range(dp):
            at = d * 4 * cs + tap * cs
            inp_ref[at : at + cs, cols] = value[d * cs : (d + 1) * cs]

    for j in range(NR):
        r = NR * i + j
        lc = lift[:, j : j + 1]
        sh = (x_ref[j].astype(F32) + lc).astype(BF16)
        shf = sh.astype(F32)
        lh = pltpu.roll(left, lax.rem(LANES - SHIFT * r, LANES), 1)
        lh = jnp.where(flags_ref[0, r] > 0, (lh + lc).astype(BF16).astype(F32), 0.0)
        rh = pltpu.roll(right, LANES - SHIFT - SHIFT * r, 1)
        rh = jnp.where(flags_ref[1, r] > 0, (rh + lc).astype(BF16).astype(F32), 0.0)
        cols = slice(j * LANES, (j + 1) * LANES)
        put(0, cols, jnp.where(lane < SHIFT, lh, pltpu.roll(shf, SHIFT, 1)).astype(BF16))
        put(1, cols, sh)
        put(
            2,
            cols,
            jnp.where(lane >= LANES - SHIFT, rh, pltpu.roll(shf, LANES - SHIFT, 1)).astype(BF16),
        )
        put(3, cols, cond_ref[j])
    pre = nn(wt_ref[...], inp_ref[...])
    th = jnp.tanh(pre[:C])
    sg = jax.nn.sigmoid(pre[C:])
    gf = th * sg
    fa_ref[...] = (sg - gf * th).astype(BF16)
    fb_ref[...] = (gf * (1.0 - sg)).astype(BF16)
    g = gf.astype(BF16)
    gated_ref[...] = g
    rs = nn(rst_ref[...], g)
    acc = acc_ref[...]
    for j in range(NR):
        r = NR * i + j
        cols = slice(j * LANES, (j + 1) * LANES)
        skip_ref[j] = rs[C:, cols].astype(BF16)
        mid = ((x_ref[j].astype(F32) + rs[:C, cols]) * SQRT_HALF).astype(BF16)
        mid_ref[:, cols] = mid
        mf = mid.astype(F32)
        df = dout_ref[j].astype(F32)
        total = jnp.sum(mf, axis=1, keepdims=True)
        dev = mf - total * (1.0 / LANES)
        acc = jnp.where(lane == r, total, acc)
        acc = jnp.where(lane == RP + r, jnp.sum(dev * dev, axis=1, keepdims=True), acc)
        acc = jnp.where(lane == 2 * RP + r, jnp.sum(df, axis=1, keepdims=True), acc)
        acc = jnp.where(lane == 3 * RP + r, jnp.sum(df * dev, axis=1, keepdims=True), acc)
    acc_ref[...] = acc

    @pl.when(i == pl.num_programs(0) - 1)
    def _():
        t = acc.T
        for s in range(C // csh):
            cols = slice(s * csh, (s + 1) * csh)
            stats_ref[s, 0 : 2 * RP, 0:csh] = t[0 : 2 * RP, cols]
            stats_ref[s, 0 : 2 * RP, csh : 2 * csh] = t[2 * RP : 4 * RP, cols]
            stats_ref[s, 2 * RP : 3 * RP] = pooled_ref[:, 0 : 2 * csh]


def attention_kernel(dp, rows, heads, pairs, off, off_ref, bit_ref, len_ref, prompts, *refs):
    pieces, refs = refs[:dp], refs[dp:]
    apack_ref, prow, probs_ref, u_ref, pooled_ref, qp_ref, qkv_ref, abd, sems = refs
    copies = head_copies(pieces, off_ref, apack_ref, sems)
    count = len(copies)
    for j in range(pairs):
        for i in range(2):
            copies.append(
                pltpu.make_async_copy(
                    prompts.at[j, i], prow.at[:, 2 * j + i], sems.at[count + 2 * j + i]
                )
            )
    begin(copies)
    local = prow.shape[2]
    total = 2 * pairs * local
    abd[...] = jnp.zeros(abd.shape, F32)
    lane = lane_ids((heads * QUERIES, total))
    place = jnp.zeros((heads * QUERIES, total), jnp.int32)
    for k in range(2 * pairs):
        here = (k // 2) * 2 + (bit_ref[0] if k % 2 == 0 else 1 - bit_ref[0])
        place = jnp.where(lane // local == k, here * local + lane % local, place)
    finish(copies)
    wide = heads * HEAD_DIM
    qkv = apack_ref[:, off : off + qkv_ref.shape[0]].T
    qkv_ref[...] = qkv
    qp = nt(qkv[3 * wide : 3 * wide + QUERIES], qkv[0:wide])
    qp_ref[...] = qp
    st = []
    for g in range(heads):
        cols = slice(g * HEAD_DIM, (g + 1) * HEAD_DIM)
        st.append(fold(nn(parts(qp[:, cols], 3), qkv[wide + cols.start : wide + cols.stop]), 3))
    st = jnp.concatenate(st, axis=0) * (1.0 / math.sqrt(HEAD_DIM))
    table = prow[...].reshape(rows * total, C)
    scores = fold(nt(parts(st, 3), table), 3)
    for r in range(rows):
        cols = slice(r * total, (r + 1) * total)
        live = place < len_ref[r]
        s = jnp.where(live, scores[:, cols], MASKED_SCORE)
        e = jnp.where(live, jnp.exp(s - jnp.max(s, axis=1, keepdims=True)), 0.0)
        p = e / jnp.sum(e, axis=1, keepdims=True)
        probs_ref[:, cols] = p
        for g in range(heads):
            abd[8 * g + r : 8 * g + r + 1, cols] = jnp.sum(
                p[g * QUERIES : (g + 1) * QUERIES], axis=0, keepdims=True
            )
    u = fold(nn(parts(abd[...], 2), table), 2)
    u_ref[...] = u
    pooled_ref[...] = jnp.zeros(pooled_ref.shape, F32)
    for g in range(heads):
        first = 2 * wide + g * HEAD_DIM
        v = parts(u[8 * g : 8 * g + 8] * (1.0 / QUERIES), 2)
        pooled_ref[0:8, g * HEAD_DIM : (g + 1) * HEAD_DIM] = fold(
            nt(v, qkv[first : first + HEAD_DIM]), 2
        )


def stats_kernel(
    csh, heads, rows, seg_ref, x_ref, apack_ref, out_ref, dfilm_ref, pooled_ref, memory_ref, scratch
):
    count = x_ref.shape[0]
    wide = heads * HEAD_DIM
    seg = seg_ref[...]
    scratch[...] = jnp.zeros(scratch.shape, F32)
    for s in range(count):
        group, part = s // 2, s % 2
        scratch[part * rows : (part + 1) * rows, group * wide : (group + 1) * wide] = x_ref[
            s, 2 * RP : 2 * RP + rows, 0:wide
        ]
    pooled = scratch[...].astype(BF16)
    pooled_ref[...] = pooled
    memory = nn(pooled, apack_ref[:, 0:C]).astype(BF16)
    memory_ref[...] = memory
    film = nn(memory, apack_ref[:, C : C + 2 * csh])
    f0 = film[:, 0:csh]
    f1 = film[:, csh : 2 * csh]
    total = [x_ref[s, 0:RP, 0:csh] for s in range(count)]
    second = [x_ref[s, RP : 2 * RP, 0:csh] for s in range(count)]
    dsum = [x_ref[s, 0:RP, csh : 2 * csh] for s in range(count)]
    cross = [x_ref[s, RP : 2 * RP, csh : 2 * csh] for s in range(count)]
    means = [v * (1.0 / LANES) for v in total]
    d0 = jnp.zeros((RP, csh), F32)
    d1 = jnp.zeros((RP, csh), F32)
    for me in range(count):
        same = [(seg[:, s : s + 1] == seg[:, me : me + 1]).astype(F32) for s in range(count)]
        frames = sum(same) * float(LANES)
        inv = 1.0 / frames
        mean = sum(m * v for m, v in zip(same, total)) * inv
        var = (
            sum(
                m * (v + float(LANES) * (u - mean) * (u - mean))
                for m, v, u in zip(same, second, means)
            )
            * inv
        )
        scale = lax.rsqrt(var + NORM_EPS)
        dtot = sum(m * v for m, v in zip(same, dsum))
        xtot = sum(m * (v + (u - mean) * d) for m, v, u, d in zip(same, cross, means, dsum)) * scale
        mean_part = f0 * dtot * inv
        cross_part = f0 * xtot * inv
        slope = scale * scale * cross_part
        out_ref[me, 0:RP, 0:csh] = 1.0 + f0 * scale
        out_ref[me, RP : 2 * RP, 0:csh] = f1 - f0 * scale * mean
        out_ref[me, 0:RP, csh : 2 * csh] = -slope
        out_ref[me, RP : 2 * RP, csh : 2 * csh] = slope * mean - scale * mean_part
        d0 = d0 + (cross[me] + (means[me] - mean) * dsum[me]) * scale
        d1 = d1 + dsum[me]
    dfilm = jnp.concatenate([d0, d1], axis=1).astype(BF16)
    dfilm_ref[...] = dfilm
    dmem = nt(dfilm, apack_ref[:, C : C + 2 * csh])
    dpool = nt(dmem.astype(BF16), apack_ref[:, 0:C])
    for s in range(count):
        group, part = s // 2, s % 2
        rolled = pltpu.roll(dpool, RP - part * rows, 0) if part else dpool
        out_ref[s, 2 * RP : 3 * RP, 0:csh] = dmem[:, s * csh : (s + 1) * csh]
        out_ref[s, 2 * RP : 3 * RP, csh : 2 * csh] = jnp.zeros((RP, csh), F32)
        out_ref[s, 3 * RP : 4 * RP] = rolled[:, group * wide : (group + 1) * wide]


def coef_columns(csh, coef_ref, rows_ref, cols_ref):
    rows_ref[...] = jnp.zeros(rows_ref.shape, F32)
    for s in range(C // csh):
        cols = slice(s * csh, (s + 1) * csh)
        rows_ref[0 : 2 * RP, cols] = coef_ref[s, 0 : 2 * RP, 0:csh]
        rows_ref[2 * RP : 4 * RP, cols] = coef_ref[s, 0 : 2 * RP, csh : 2 * csh]
    cols_ref[...] = rows_ref[...].T


def skip_grad_kernel(gated_ref, dskip_ref, out_ref, right):
    for r in range(dskip_ref.shape[0]):
        right[:, r * LANES : (r + 1) * LANES] = dskip_ref[r]
    out_ref[...] = nt(gated_ref[...], right[...]).astype(BF16)


def backward_kernel(meta, dp, csh, gates, order_ref, off_ref, coef_ref, mid_ref, dout_ref, dskip_ref, fa_ref, fb_ref, inp_ref, gated_ref, gskip_ref, flags_ref, *refs):
    turned, refs = refs[: len(meta)], refs[len(meta) :]
    dpre_ref, dres_ref, sums_ref, refs = refs[0], refs[1], refs[2], refs[3:]
    outs, refs = (refs[0:2], refs[2:4]), refs[4:]
    rows_ref, cols_ref, w_ref, both_ref, dpt_ref, drt_ref, sems = refs
    cs = C // dp
    span = NR * LANES
    i = pl.program_id(0)

    @pl.when(i == 0)
    def _():
        copies = turned_copies(
            meta, turned, off_ref, cs, None, ((w_ref, 0), (w_ref, C), None), sems
        )
        begin(copies)
        coef_columns(csh, coef_ref, rows_ref, cols_ref)
        sums_ref[...] = jnp.zeros(sums_ref.shape, F32)
        finish(copies)

    @pl.when(i < gates)
    def _():
        coef = pltpu.roll(cols_ref[...], lax.rem(LANES - NR * i, LANES), 1)
        for j in range(NR):
            cols = slice(j * LANES, (j + 1) * LANES)
            mf = mid_ref[:, cols].astype(F32)
            df = dout_ref[j].astype(F32)
            a = coef[:, j : j + 1]
            be = coef[:, 2 * RP + j : 2 * RP + j + 1]
            ga = coef[:, 3 * RP + j : 3 * RP + j + 1]
            dmid = (a * df + (be * mf + ga)).astype(BF16).astype(F32)
            both_ref[0:C, cols] = (dmid * SQRT_HALF).astype(BF16)
            both_ref[C : 2 * C, cols] = dskip_ref[j]
        dres = both_ref[0:C]
        dres_ref[...] = dres
        dg = nn(w_ref[...], both_ref[...])
        dt = (dg * fa_ref[...].astype(F32)).astype(BF16)
        ds = (dg * fb_ref[...].astype(F32)).astype(BF16)
        dpre_ref[0:C] = dt
        dpre_ref[C : 2 * C] = ds
        at = pl.ds(pl.multiple_of(i * span, span), span)
        dpt_ref[at, 0:C] = dt.T
        dpt_ref[at, C : 2 * C] = ds.T
        drt_ref[at] = dres.T
        frame = lax.broadcasted_iota(jnp.int32, (span, LANES), 0)
        column = lane_ids((span, LANES))
        place = frame % LANES
        which = frame // LANES
        keep_l = jnp.zeros((span, LANES), jnp.int32)
        keep_r = jnp.zeros((span, LANES), jnp.int32)
        for j in range(NR):
            keep_l = jnp.where(which == j, flags_ref[0, NR * i + j], keep_l)
            keep_r = jnp.where(which == j, flags_ref[1, NR * i + j], keep_r)
        row = NR * i + which
        use0 = (column == row) & ((place >= SHIFT) | (keep_l > 0))
        use1 = column == RP + row
        use2 = (column == 2 * RP + row) & ((place < LANES - SHIFT) | (keep_r > 0))
        pick = jnp.where(use0 | use1 | use2, 1.0, 0.0).astype(BF16)
        sums_ref[...] = sums_ref[...] + nn(dpre_ref[...], pick)

    @pl.when(i >= gates)
    def _():
        g = nn(inp_ref[...], dpt_ref[...]).astype(BF16)
        h = nn(gated_ref[...], drt_ref[...]).astype(BF16)
        k = i - gates
        for parity, (one, two) in enumerate(outs):

            @pl.when(lax.rem(k, 2) == parity)
            def _():
                for t in range(4):
                    rows = slice(t * cs, (t + 1) * cs)
                    lanes = slice(t * LANES, (t + 1) * LANES)
                    one[0, rows, 0:LANES] = h[:, lanes]
                    one[0, rows, LANES : 2 * LANES] = gskip_ref[:, lanes]
                one[0, :, 2 * LANES :] = g[:, 0:EARLY]
                two[0] = g[:, EARLY:]


def step_grad_kernel(meta, dp, off_ref, sums_ref, emb_ref, *refs):
    turned, refs = refs[: len(meta)], refs[len(meta) :]
    keep_ref, give_ref, wt_ref, scr, sems = refs
    cs = C // dp
    copies = turned_copies(meta, turned, off_ref, cs, wt_ref, (None,) * 3, sems)
    begin(copies)
    sums = sums_ref[...].T
    emb = emb_ref[...].T
    finish(copies)
    total = jnp.zeros((RP, 4 * C), F32)
    lane = lane_ids((RP, 4 * C))
    all_taps = fold(nn(parts(sums[0 : 3 * RP], 2), wt_ref[...]), 2)
    for t in range(3):
        g = all_taps[t * RP : (t + 1) * RP]
        total = total + jnp.where((lane // cs) % 4 == t, g, 0.0)
    out = []
    for d in range(dp):
        block = total[:, d * 4 * cs : (d + 1) * 4 * cs]
        out.append(block[:, 0:cs] + block[:, cs : 2 * cs] + block[:, 2 * cs : 3 * cs])
    g = jnp.concatenate(out, axis=1)
    g = jnp.concatenate([g, jnp.zeros((LANES - RP, C), F32)], axis=0)
    hi = g.astype(BF16)
    lo = (g - hi.astype(F32)).astype(BF16)
    scr[...] = nn(emb, hi) + nn(emb, lo)
    for k in range(dp):
        v = scr[pl.ds(pl.multiple_of(off_ref[k], 16), cs)].astype(BF16)
        for t in range(4):
            (keep_ref, give_ref)[k % 2][k // 2, t * cs : (t + 1) * cs] = v[
                :, t * LANES : (t + 1) * LANES
            ]


def input_grad_kernel(meta, dp, off_ref, dpre_ref, dres_ref, *refs):
    turned, refs = refs[: len(meta)], refs[len(meta) :]
    base_ref, first_ref, last_ref, wt_ref, w_ref, facc_ref, lacc_ref, sems = refs
    cs = C // dp
    i = pl.program_id(0)
    lane = lane_ids((C, LANES))

    @pl.when(i == 0)
    def _():
        copies = turned_copies(meta, turned, off_ref, cs, wt_ref, (None,) * 3, sems)
        begin(copies)
        facc_ref[...] = jnp.zeros((C, LANES), F32)
        lacc_ref[...] = jnp.zeros((C, LANES), F32)
        finish(copies)
        for d in range(dp):
            v = wt_ref[:, d * 4 * cs : (d + 1) * 4 * cs].T
            for t in range(3):
                w_ref[t, d * cs : (d + 1) * cs] = v[t * cs : (t + 1) * cs]

    dpre = dpre_ref[...]
    y0 = nn(w_ref[0], dpre)
    y1 = nn(w_ref[1], dpre)
    y2 = nn(w_ref[2], dpre)
    facc = facc_ref[...]
    lacc = lacc_ref[...]
    for j in range(NR):
        r = NR * i + j
        cols = slice(j * LANES, (j + 1) * LANES)
        z0 = pltpu.roll(y0[:, cols], LANES - SHIFT, 1)
        z2 = pltpu.roll(y2[:, cols], SHIFT, 1)
        inner0 = lane < LANES - SHIFT
        inner2 = lane >= SHIFT
        v = y1[:, cols]
        base_ref[:, cols] = (
            v
            + jnp.where(inner0, z0, 0.0)
            + jnp.where(inner2, z2, 0.0)
            + dres_ref[:, cols].astype(F32)
        ).astype(BF16)
        here = (lane // SHIFT) == r
        facc = jnp.where(here, pltpu.roll(z0, lax.rem(SHIFT * r + SHIFT, LANES), 1), facc)
        lacc = jnp.where(here, pltpu.roll(z2, SHIFT * r, 1), lacc)
    facc_ref[...] = facc
    lacc_ref[...] = lacc

    @pl.when(i == pl.num_programs(0) - 1)
    def _():
        first_ref[...] = facc.astype(BF16)
        last_ref[...] = lacc.astype(BF16)


def finish_kernel(csh, flags_ref, base_ref, left_ref, right_ref, mid_ref, coef_ref, out_ref, layer_ref, rows_ref, cols_ref):
    i = pl.program_id(0)
    lane = lane_ids((C, LANES))

    @pl.when(i == 0)
    def _():
        coef_columns(csh, coef_ref, rows_ref, cols_ref)

    coef = pltpu.roll(cols_ref[...], lax.rem(LANES - NR * i, LANES), 1)
    left = left_ref[...].astype(F32)
    right = right_ref[...].astype(F32)
    for j in range(NR):
        r = NR * i + j
        cols = slice(j * LANES, (j + 1) * LANES)
        lh = pltpu.roll(left, lax.rem(LANES - SHIFT * r, LANES), 1)
        rh = pltpu.roll(right, LANES - SHIFT - SHIFT * r, 1)
        lh = jnp.where((lane < SHIFT) & (flags_ref[0, r] > 0), lh, 0.0)
        rh = jnp.where((lane >= LANES - SHIFT) & (flags_ref[1, r] > 0), rh, 0.0)
        out_ref[j] = (base_ref[:, cols].astype(F32) + lh + rh).astype(BF16)
        a = coef[:, j : j + 1]
        b = coef[:, RP + j : RP + j + 1]
        layer_ref[j] = (a * mid_ref[:, cols].astype(F32) + b).astype(BF16)


def add_blocks_kernel(count, *refs):
    ins, (keep_ref, give_ref) = refs[: 2 * count], refs[2 * count :]
    at = 0
    for p in range(count):
        a_ref, b_ref = ins[2 * p : 2 * p + 2]
        width = a_ref.shape[2]
        for j in range(a_ref.shape[0]):
            v = a_ref[j].astype(F32) + b_ref[j].astype(F32)
            (keep_ref, give_ref)[j % 2][j // 2, :, at : at + width] = v.astype(BF16)
        at += width


def add_halves_kernel(bit, index_ref, a_ref, b_ref, keep_ref, give_ref, scr):
    half = a_ref.shape[0] // 2
    mine = lax.rem(index_ref[0] // bit, 2)
    scr[...] = a_ref[...].astype(F32) + b_ref[...].astype(F32)
    keep_ref[...] = scr[pl.ds(pl.multiple_of(mine * half, 8), half)].astype(BF16)
    give_ref[...] = scr[pl.ds(pl.multiple_of((1 - mine) * half, 8), half)].astype(BF16)


def add_pieces_kernel(a_ref, b_ref, out_ref):
    v = a_ref[...].astype(F32) + b_ref[...].astype(F32)
    size = out_ref.shape[1]
    for p in range(out_ref.shape[0]):
        out_ref[p] = v[p * size : (p + 1) * size].astype(BF16)


def sum_copies_kernel(a_ref, *refs):
    out_ref = refs[-1]
    v = a_ref[0].astype(F32)
    for p in range(1, a_ref.shape[0]):
        v = v + a_ref[p].astype(F32)
    v = v.astype(BF16)
    for p in range(out_ref.shape[0]):
        out_ref[p, :, 0 : v.shape[1]] = v
        if len(refs) > 1:
            out_ref[p, :, v.shape[1] :] = refs[0][...]


def small_sum_kernel(csh, wide, bit_ref, keep_ref, got_ref, film_ref, attn_ref, mine_ref, other_ref, turn):
    v = keep_ref[0].astype(F32) + got_ref[0].astype(F32)
    cs = v.shape[0]
    film = 2 * wide + csh
    turn[...] = jnp.zeros(turn.shape, F32)
    turn[0:cs, 0 : 2 * csh] = v[:, film : film + 2 * csh]
    film_ref[...] = turn[...].T[0 : 2 * csh, 0:cs]
    attn_ref[...] = v[:, 2 * wide : film]
    last = film + 2 * csh
    even = bit_ref[0] == 0
    for one, two, rows, width in (
        (v[:, 0:wide], v[:, wide : 2 * wide], slice(0, cs), wide),
        (
            v[0:QUERIES, last : last + wide // 2],
            v[0:QUERIES, last + wide // 2 : last + wide],
            slice(cs, cs + QUERIES),
            wide // 2,
        ),
    ):
        mine_ref[rows, 0:width] = jnp.where(even, one, two).astype(BF16)
        other_ref[rows, 0:width] = jnp.where(even, two, one).astype(BF16)
    mine_ref[cs:, wide // 2 :] = jnp.zeros((QUERIES, wide // 2), BF16)
    other_ref[cs:, wide // 2 :] = jnp.zeros((QUERIES, wide // 2), BF16)


def small_piece_kernel(csh, wide, attn_ref, mine_ref, got_ref, out_ref):
    v = mine_ref[...].astype(F32) + got_ref[...].astype(F32)
    attn = attn_ref[...]
    cs = attn.shape[0]
    rows = out_ref.shape[0]
    at = 0
    for row in range(0, cs, rows):
        out_ref[:, at : at + wide] = v[row : row + rows].astype(BF16)
        out_ref[:, at + wide : at + wide + csh] = attn[row : row + rows].astype(BF16)
        at += wide + csh
    for row in range(0, QUERIES, rows):
        block = v[cs + row : cs + min(row + rows, QUERIES), 0 : wide // 2]
        if block.shape[0] < rows:
            pad = jnp.zeros((rows - block.shape[0], wide // 2), F32)
            block = jnp.concatenate([block, pad], axis=0)
        out_ref[:, at : at + wide // 2] = block.astype(BF16)
        at += wide // 2


def output_kernel(
    cs,
    csh,
    wide,
    seq,
    bit_ref,
    *refs,
):
    own1, got1, own2, got2, refs = *refs[:4], refs[4:]
    (
        queries_ref,
        wq_ref,
        step_ref,
        conv_ref,
        cond_ref,
        res_ref,
        skip_ref,
        gqueries_ref,
        gquery_ref,
        key_ref,
        value_ref,
        attn_ref,
        scr1,
        scr2,
        small,
        qscr,
        dq,
    ) = refs
    count, size = own1.shape[0], own1.shape[1]
    wide2 = scr2.shape[1]
    bit = bit_ref[0]
    for one, two, side in ((own1, own2, bit), (got1, got2, 1 - bit)):
        for p in range(count):
            rows = pl.ds(pl.multiple_of((side * count + p) * size, 8), size)
            scr1[rows] = one[p].astype(F32)
            v = two[p].astype(F32)
            scr2[rows] = v[:, 0:wide2]
            small[pl.ds(pl.multiple_of((2 * p + side) * size, 8), size)] = v[:, wide2:]
    for t in range(4):
        rows = slice(t * cs, (t + 1) * cs)
        lanes = slice(t * LANES, (t + 1) * LANES)
        res_ref[:, lanes] = scr1[rows, 0:LANES]
        skip_ref[:, lanes] = scr1[rows, LANES : 2 * LANES]
        rest = 2 * C - EARLY
        step_ref[:, lanes] = scr2[rows, rest : rest + LANES]
        if t < 3:
            conv_ref[t, :, 0:EARLY] = scr1[rows, 2 * LANES : 2 * LANES + EARLY]
            conv_ref[t, :, EARLY:] = scr2[rows, 0:rest]
        else:
            cond_ref[:, 0:EARLY] = scr1[rows, 2 * LANES : 2 * LANES + EARLY]
            cond_ref[:, EARLY:] = scr2[rows, 0:rest]
    dq[...] = jnp.zeros(dq.shape, F32)
    for s in range(seq):
        v = small[s * size : (s + 1) * size]
        group, even = s // 2, s % 2 == 0
        out = key_ref if even else value_ref
        at = 0
        for row in range(0, cs, size):
            out[row : row + size, group * wide : (group + 1) * wide] = v[:, at : at + wide]
            attn_ref[row : row + size, s * csh : (s + 1) * csh] = v[:, at + wide : at + wide + csh]
            at += wide + csh
        first = group * wide + (0 if even else wide // 2)
        for row in range(0, QUERIES, size):
            count = min(size, QUERIES - row)
            dq[row : row + count, first : first + wide // 2] = v[0:count, at : at + wide // 2]
            at += wide // 2
    qscr[...] = jnp.zeros((LANES, LANES), F32)
    qscr[0:QUERIES, 0:cs] = queries_ref[...].astype(F32)
    qt = qscr[...].T.astype(BF16)
    d = dq[...]
    hi = d.astype(BF16)
    lo = (d - hi.astype(F32)).astype(BF16)
    gquery_ref[...] = (nn(qt, hi) + nn(qt, lo))[0:cs]
    gqueries_ref[...] = fold(nt(parts(d[0:QUERIES], 2), wq_ref[...]), 2)


def attention_back_kernel(
    rows,
    csh,
    dp,
    off_ref,
    prow,
    probs_ref,
    u_ref,
    qp_ref,
    qkv_ref,
    pooled_ref,
    memory_ref,
    dfilm_ref,
    got_ref,
    keep_ref,
    give_ref,
    ds,
    stack,
    right,
    out,
):
    count = got_ref.shape[0]
    total = prow.shape[1] * prow.shape[2]
    cs = C // dp
    table = prow[...].reshape(rows * total, C)
    wide = qp_ref.shape[1]
    heads = wide // HEAD_DIM
    datt = got_ref[0, 3 * RP : 4 * RP, 0:wide]
    dmem = got_ref[0, 2 * RP : 3 * RP, 0:csh]
    for s in range(1, count):
        datt = datt + got_ref[s, 3 * RP : 4 * RP, 0:wide]
        dmem = dmem + got_ref[s, 2 * RP : 3 * RP, 0:csh]
    datt = datt[0:8] * (1.0 / QUERIES)
    vh = []
    for g in range(heads):
        first = 2 * wide + g * HEAD_DIM
        v = parts(datt[:, g * HEAD_DIM : (g + 1) * HEAD_DIM], 2)
        vh.append(fold(nn(v, qkv_ref[first : first + HEAD_DIM]), 2))
    vh = jnp.concatenate(vh, axis=0)
    dp_all = fold(nt(parts(vh, 2), table), 2)
    for r in range(rows):
        cols = slice(r * total, (r + 1) * total)
        for g in range(heads):
            mine = slice(g * QUERIES, (g + 1) * QUERIES)
            p = probs_ref[mine, cols]
            dpr = dp_all[8 * g + r : 8 * g + r + 1, cols]
            inner = jnp.sum(p * dpr, axis=1, keepdims=True)
            ds[mine, cols] = p * (dpr - inner)
    tt = fold(nn(parts(ds[...], 2), table), 2)
    scale = 1.0 / math.sqrt(HEAD_DIM)
    dq = []
    stack[...] = jnp.zeros(stack.shape, F32)
    right[...] = jnp.zeros(right.shape, F32)
    stack[0 : heads * QUERIES] = tt
    stack[64:80] = u_ref[...]
    stack[80:96] = pooled_ref[...].astype(F32)
    stack[96:112] = memory_ref[...].astype(F32)
    for g in range(heads):
        cols = slice(g * HEAD_DIM, (g + 1) * HEAD_DIM)
        mine = slice(g * QUERIES, (g + 1) * QUERIES)
        wk = qkv_ref[wide + g * HEAD_DIM : wide + (g + 1) * HEAD_DIM]
        dq.append(fold(nt(parts(tt[mine], 2), wk), 2) * scale)
        right[mine, cols] = qp_ref[:, cols] * scale
        right[64 + 8 * g : 72 + 8 * g, wide + cols.start : wide + cols.stop] = datt[:, cols]
    right[80:96, 2 * wide : 2 * wide + csh] = dmem
    right[96:112, 2 * wide + csh : 2 * wide + 3 * csh] = dfilm_ref[...].astype(F32)
    out[...] = lax.dot_general(
        stack[...].T,
        right[...],
        (((1,), (0,)), ((), ())),
        precision=lax.Precision.HIGHEST,
        preferred_element_type=F32,
    )
    last = 2 * wide + 3 * csh
    for k in range(dp):
        ref = (keep_ref, give_ref)[k % 2]
        ref[k // 2] = out[pl.ds(pl.multiple_of(off_ref[k], 16), cs)].astype(BF16)
        for g in range(heads):
            first = last + g * HEAD_DIM
            ref[k // 2, 0:QUERIES, first : first + HEAD_DIM] = dq[g].astype(BF16)


def exchange(pieces, axis, groups=None):
    return lax.all_to_all(
        pieces, axis, split_axis=0, concat_axis=0, axis_index_groups=groups, tiled=True
    )


def flipped(v, axis, size, bit):
    return lax.ppermute(v, axis, [(d, d ^ bit) for d in range(size)])


class Reduction:
    def __init__(self, call, name, keep, give, dp, seq, index):
        self.call, self.name, self.dp, self.seq, self.index = call, name, dp, seq, index
        self.keep, self.flip = keep, 1
        self.got = flipped(give, "dp", dp, 1)

    def over_blocks(self, after=(), others=()):
        while 2 * self.flip < self.dp:
            group = (self,) + tuple(others)
            others = ()
            args = []
            for part in group:
                args += [part.keep, Got(part.got)]
            width = sum(part.keep.shape[2] for part in group)
            half = sds((self.keep.shape[0] // 2, self.keep.shape[1], width), BF16)
            self.keep, give = self.call(
                functools.partial(add_blocks_kernel, len(group)),
                (half, half),
                "blocks_" + self.name,
                args,
                after=after,
                in_specs=[VM] * len(args),
                out_specs=(VM, VM),
            )
            self.flip *= 2
            self.got = flipped(give, "dp", self.dp, self.flip)
        self.rest = self.keep.shape[1:]

    def over_half(self, after=()):
        rows, width = self.rest
        half = sds((rows // 2, width), BF16)
        self.keep, give = self.call(
            functools.partial(add_halves_kernel, 1),
            (half, half),
            "half_" + self.name,
            (self.index, self.keep.reshape(rows, width), Got(self.got.reshape(rows, width))),
            after=after,
            in_specs=[SM, VM, VM],
            out_specs=(VM, VM),
            scratch_shapes=[pltpu.VMEM((rows, width), F32)],
        )
        self.got = flipped(give, "seq", self.seq, 1)

    def over_pieces(self, after=()):
        rows, width = self.rest
        count = self.seq // 2
        self.groups = [[2 * k + b for k in range(count)] for b in range(2)]
        pieces = self.call(
            add_pieces_kernel,
            sds((count, rows // self.seq, width), BF16),
            "pieces_" + self.name,
            (self.keep, Got(self.got)),
            after=after,
            in_specs=[VM, VM],
            out_specs=VM,
        )
        self.got = exchange(pieces, "seq", self.groups)

    def over_copies(self, after=(), extra=None):
        args, (count, rows, width) = [Got(self.got)], self.got.shape
        if extra is not None:
            args.append(extra)
            width += extra.shape[1]
        copies = self.call(
            sum_copies_kernel,
            sds((count, rows, width), BF16),
            "copies_" + self.name,
            args,
            after=after,
            in_specs=[VM] * len(args),
            out_specs=VM,
        )
        own = exchange(copies, "seq", self.groups)
        return Got(own), Got(flipped(own, "seq", self.seq, 1))


def body(
    dp,
    seq,
    x_in,
    cond,
    segment_ids,
    diffusion_steps,
    prompt,
    prompt_lengths,
    w_step,
    w_conv,
    w_cond,
    w_res,
    w_skip,
    queries,
    w_query,
    w_key,
    w_value,
    w_attn_out,
    w_film,
    d_out,
    d_skip,
):
    call = Caller()
    rows = x_in.shape[0]
    frames = x_in.shape[2]
    steps = rows // NR
    cols = rows * frames
    cs = C // dp
    csh = C // seq
    heads = 2 * HEADS // seq
    wide = heads * HEAD_DIM
    arows = rows // 2
    pl_local = prompt.shape[1]
    prompt_all = pl_local * seq
    sidx = lax.axis_index("seq")
    didx = lax.axis_index("dp")
    group = (sidx // 2).astype(jnp.int32).reshape(1)
    bit = (sidx % 2).astype(jnp.int32).reshape(1)
    up = [(i, i + 1) for i in range(seq - 1)]
    down = [(i + 1, i) for i in range(seq - 1)]
    order = jnp.bitwise_xor(didx, jnp.arange(dp, dtype=jnp.int32)).astype(jnp.int32)
    offsets = jnp.concatenate([order * cs, bit, 1 - bit])
    index = sidx.astype(jnp.int32).reshape(1)

    def gather(pack, side=None, middle=None):
        if dp == 4 and side is not None:
            mine = flipped(side, "dp", dp, 2)
            inner = flipped(middle, "dp", dp, 2)
            other = flipped(mine, "seq", seq, 1)
            near = [(0, None, pack), (2, 0, mine), (2, 2, inner), (2, 1, other)]
            pieces = near + [(k + 1, h, flipped(v, "dp", dp, 1)) for k, h, v in near]
        else:
            pieces = [(0, None, pack)]
            flip = dp // 2
            while flip:
                pieces += [(k + flip, h, flipped(v, "dp", dp, flip)) for k, h, v in pieces]
                flip //= 2
        pieces.sort(key=lambda piece: piece[0])
        meta = [(k, h) for k, h, _ in pieces]
        return meta, [v if k == 0 else Got(v) for k, _, v in pieces]

    off_qkv = C + 2 * csh
    qkv_rows = -(-(3 * wide + QUERIES) // LANES) * LANES
    head_width = -(-(off_qkv + qkv_rows) // LANES) * LANES
    pack, mine, other = call(
        functools.partial(head_pack_kernel, csh, wide),
        (
            sds((cs, head_width), BF16),
            sds((arows, pl_local, C), BF16),
            sds((arows, pl_local, C), BF16),
        ),
        "head_pack",
        (
            group,
            bit,
            w_attn_out,
            jnp.transpose(w_film, (1, 2, 0)).reshape(2 * csh, cs),
            w_query,
            w_key,
            w_value,
            queries,
            prompt,
        ),
        in_specs=[SM, SM] + [VM] * 7,
        out_specs=(VM,) * 3,
        scratch_shapes=[pltpu.VMEM((2 * LANES, LANES), F32)],
    )
    _, head_pieces = gather(pack)
    partner = flipped(other, "seq", seq, 1)
    middle = 2 * C - 2 * SIDE + 3 * C // 4
    pack, side, middle = call(
        functools.partial(turned_pack_kernel, cs),
        (
            sds((2 * SIDE + middle, 4 * cs), BF16),
            sds((SIDE, 4 * cs), BF16),
            sds((middle, 4 * cs), BF16),
        ),
        "turned_pack",
        (bit, w_conv, w_cond, w_res, w_skip, w_step),
        after=("head_pack",),
        in_specs=[SM] + [VM] * 5,
        out_specs=(VM, VM, VM),
        scratch_shapes=[pltpu.VMEM((4 * cs, 2 * C), BF16)],
    )
    meta, turned = gather(pack, side, middle)
    copies = 4 * dp * (1 + 3 * C // (4 * cs))
    pair = call(
        pair_kernel,
        sds((seq // 2, 2, arows, pl_local, C), BF16),
        "pair",
        (mine, Got(partner)),
        after=("turned_pack",),
        in_specs=[VM, VM],
        out_specs=VM,
    )
    z_groups = [[2 * k + b for k in range(seq // 2)] for b in range(2)]
    prompts = Got(exchange(pair, "seq", z_groups))
    first, last = call(
        edge_kernel,
        (sds((C, LANES), BF16), sds((C, LANES), BF16)),
        "edges",
        (x_in,),
        after=("pair",),
        in_specs=[VM],
        out_specs=(VM, VM),
    )
    left_halo = lax.ppermute(last, "seq", up)
    right_halo = lax.ppermute(first, "seq", down)

    block_ids = segment_ids[:, ::frames]
    padded_ids = jnp.pad(block_ids, ((0, 0), (1, 1)), constant_values=-1)
    mine = lax.dynamic_slice_in_dim(padded_ids, sidx, 3, 1)
    flags = jnp.stack([mine[:, 0] == mine[:, 1], mine[:, 2] == mine[:, 1]]).astype(jnp.int32)
    block_ids = jnp.pad(block_ids, ((0, RP - rows), (0, 0)))
    half = C // 2
    frequency = jnp.exp(jnp.arange(half, dtype=F32) * (-math.log(10000.0) / half))
    step_rows = jnp.pad(diffusion_steps.astype(F32), (0, LANES - rows))
    live_rows = jnp.arange(LANES, dtype=jnp.int32)[:, None] < rows
    angles = step_rows[:, None] * frequency[None, :]
    embedding = jnp.concatenate([jnp.sin(angles), jnp.cos(angles)], axis=1)
    embedding = jnp.where(live_rows, embedding, 0.0).astype(BF16)
    lengths = lax.dynamic_slice_in_dim(prompt_lengths, (sidx % 2) * arows, arows, 0)

    apack, prow, probs, u, pooled_head, qp, qkv = call(
        functools.partial(attention_kernel, dp, arows, heads, seq // 2, off_qkv),
        (
            sds((C, head_width), BF16),
            sds((arows, seq, pl_local, C), BF16),
            sds((heads * QUERIES, arows * prompt_all), F32),
            sds((RP, C), F32),
            sds((RP, LANES), F32),
            sds((QUERIES, wide), F32),
            sds((qkv_rows, C), BF16),
        ),
        "attention",
        (offsets, bit, lengths, prompts, *head_pieces),
        in_specs=[SM, SM, SM, HB] + [HB] * dp,
        out_specs=(VM,) * 7,
        scratch_shapes=[
            pltpu.VMEM((RP, arows * prompt_all), F32),
            pltpu.SemaphoreType.DMA((dp + seq,)),
        ],
    )

    row_block = pl.BlockSpec((NR, C, LANES), lambda i: (i, 0, 0))

    def col_block(height):
        return pl.BlockSpec((height, NR * LANES), lambda i: (0, i))

    def still(shape):
        return pl.BlockSpec(shape, lambda i: (0,) * len(shape))

    inp, gated, factor_a, factor_b, skip_out, mid, stats = call(
        functools.partial(forward_kernel, meta, dp, csh),
        (
            sds((4 * C, cols), BF16),
            sds((C, cols), BF16),
            sds((C, cols), BF16),
            sds((C, cols), BF16),
            sds(x_in.shape, BF16),
            sds((C, cols), BF16),
            sds((seq, 3 * RP, 2 * csh), F32),
        ),
        "wavenet",
        (
            offsets,
            flags,
            x_in,
            cond,
            d_out,
            Got(left_halo),
            Got(right_halo),
            embedding,
            pooled_head,
            *turned,
        ),
        flops=2 * cols * (4 * C * 2 * C + 2 * C * C),
        nbytes=30e6,
        grid=(steps,),
        in_specs=[
            SM,
            SM,
            row_block,
            row_block,
            row_block,
            whole((C, LANES)),
            whole((C, LANES)),
            whole((LANES, C)),
            whole((RP, LANES)),
        ]
        + [HB] * len(turned),
        out_specs=(
            col_block(4 * C),
            col_block(C),
            col_block(C),
            col_block(C),
            row_block,
            col_block(C),
            still((seq, 3 * RP, 2 * csh)),
        ),
        scratch_shapes=[
            pltpu.VMEM((2 * C, 4 * C), BF16),
            pltpu.VMEM((C, 2 * C), BF16),
            pltpu.VMEM((C, C), BF16),
            pltpu.VMEM((2 * C, C), BF16),
            pltpu.VMEM((C, LANES), F32),
            pltpu.VMEM((C, LANES), F32),
            pltpu.SemaphoreType.DMA((copies,)),
        ],
    )
    stats_got = exchange(stats, "seq")
    gskip = call(
        skip_grad_kernel,
        sds((C, C), BF16),
        "skip",
        (gated, d_skip),
        in_specs=[VM, VM],
        out_specs=VM,
        scratch_shapes=[pltpu.VMEM((C, cols), BF16)],
    )

    coef_out, dfilm, pooled, memory = call(
        functools.partial(stats_kernel, csh, heads, arows),
        (
            sds((seq, 4 * RP, 2 * csh), F32),
            sds((RP, 2 * csh), BF16),
            sds((RP, C), BF16),
            sds((RP, C), BF16),
        ),
        "segments",
        (block_ids, Got(stats_got), apack),
        after=("skip",),
        in_specs=[VM, VM, VM],
        out_specs=(VM, VM, VM, VM),
        scratch_shapes=[pltpu.VMEM((RP, C), F32)],
    )
    coef = Got(exchange(coef_out, "seq"))

    def gate_block(i):
        return jnp.minimum(i, steps - 1)

    def shard(i):
        return jnp.maximum(i - steps, 0)

    def gate_cols(height):
        return pl.BlockSpec((height, NR * LANES), lambda i, order: (0, gate_block(i)))

    gate_rows = pl.BlockSpec((NR, C, LANES), lambda i, order: (gate_block(i), 0, 0))
    wide1, wide2 = EARLY + 2 * LANES, 2 * C - EARLY

    def part(width):
        return sds((dp // 2, 4 * cs, width), BF16)

    def part_spec(width):
        return pl.BlockSpec((1, 4 * cs, width), lambda i, order: (shard(i) // 2, 0, 0))

    outs = call(
        functools.partial(backward_kernel, meta, dp, csh, steps),
        (
            sds((2 * C, cols), BF16),
            sds((C, cols), BF16),
            sds((2 * C, LANES), F32),
            part(wide1),
            part(wide2),
            part(wide1),
            part(wide2),
        ),
        "backward",
        (order, offsets, coef, mid, d_out, d_skip, factor_a, factor_b, inp, gated, gskip, flags, *turned),
        prefetch=1,
        grid=(steps + dp,),
        in_specs=[
            SM,
            pl.BlockSpec(
                (seq, 4 * RP, 2 * csh), lambda i, order: (0, 0, 0), pipeline_mode=pl.Buffered(1)
            ),
            gate_cols(C),
            gate_rows,
            gate_rows,
            gate_cols(C),
            gate_cols(C),
            pl.BlockSpec((4 * cs, cols), lambda i, order: (order[shard(i)], 0)),
            pl.BlockSpec((cs, cols), lambda i, order: (order[shard(i)], 0)),
            pl.BlockSpec((cs, C), lambda i, order: (order[shard(i)], 0)),
            SM,
        ]
        + [HB] * len(turned),
        out_specs=(
            gate_cols(2 * C),
            gate_cols(C),
            pl.BlockSpec((2 * C, LANES), lambda i, order: (0, 0)),
            part_spec(wide1),
            part_spec(wide2),
            part_spec(wide1),
            part_spec(wide2),
        ),
        scratch_shapes=[
            pltpu.VMEM((LANES, C), F32),
            pltpu.VMEM((C, LANES), F32),
            pltpu.VMEM((C, 2 * C), BF16),
            pltpu.VMEM((2 * C, NR * LANES), BF16),
            pltpu.VMEM((cols, 2 * C), BF16),
            pltpu.VMEM((cols, C), BF16),
            pltpu.SemaphoreType.DMA((copies,)),
        ],
    )
    dpre, dres, sums = outs[0:3]
    part1 = Reduction(call, "1", outs[3], outs[5], dp, seq, index)
    part2 = Reduction(call, "2", outs[4], outs[6], dp, seq, index)
    part1.over_blocks()
    keep, give = call(
        functools.partial(step_grad_kernel, meta, dp),
        (part(LANES), part(LANES)),
        "step_grad",
        (offsets, sums, embedding, *turned),
        after=("blocks_1",),
        in_specs=[SM, VM, VM] + [HB] * len(turned),
        out_specs=(VM, VM),
        scratch_shapes=[
            pltpu.VMEM((2 * C, 4 * C), BF16),
            pltpu.VMEM((C, C), F32),
            pltpu.SemaphoreType.DMA((copies,)),
        ],
    )
    part_step = Reduction(call, "step", keep, give, dp, seq, index)

    right_width = -(-(3 * wide + 3 * csh) // LANES) * LANES
    block = sds((dp // 2, cs, right_width), BF16)
    keep, give = call(
        functools.partial(attention_back_kernel, arows, csh, dp),
        (block, block),
        "attention_back",
        (offsets, prow, probs, u, qp, qkv, pooled, memory, dfilm, coef),
        after=("step_grad",),
        in_specs=[SM] + [VM] * 9,
        out_specs=(VM, VM),
        scratch_shapes=[
            pltpu.VMEM((heads * QUERIES, arows * prompt_all), F32),
            pltpu.VMEM((LANES, C), F32),
            pltpu.VMEM((LANES, right_width), F32),
            pltpu.VMEM((C, right_width), F32),
        ],
    )
    small = Reduction(call, "small", keep, give, dp, seq, index)
    part2.over_blocks(("attention_back",), (part_step,))
    small.over_blocks(("blocks_2",))
    part1.over_half(("blocks_small",))

    base, first, last = call(
        functools.partial(input_grad_kernel, meta, dp),
        (sds((C, cols), BF16), sds((C, LANES), BF16), sds((C, LANES), BF16)),
        "input_grad",
        (offsets, dpre, dres, *turned),
        after=("half_1",),
        grid=(steps,),
        in_specs=[SM, col_block(2 * C), col_block(C)] + [HB] * len(turned),
        out_specs=(
            col_block(C),
            still((C, LANES)),
            still((C, LANES)),
        ),
        scratch_shapes=[
            pltpu.VMEM((2 * C, 4 * C), BF16),
            pltpu.VMEM((3, C, 2 * C), BF16),
            pltpu.VMEM((C, LANES), F32),
            pltpu.VMEM((C, LANES), F32),
            pltpu.SemaphoreType.DMA((copies,)),
        ],
    )
    from_left = lax.ppermute(last, "seq", up)
    from_right = lax.ppermute(first, "seq", down)
    rest = 4 * cs // seq
    small_width = (cs // rest) * (wide + csh) + max(1, QUERIES // rest) * (wide // 2)
    part1.over_pieces(("input_grad",))
    part2.over_half(("pieces_1",))
    grad_film, attn_rows, mine, other = call(
        functools.partial(small_sum_kernel, csh, wide),
        (
            sds((2 * csh, cs), F32),
            sds((cs, csh), F32),
            sds((cs + QUERIES, wide), BF16),
            sds((cs + QUERIES, wide), BF16),
        ),
        "small_sum",
        (bit, small.keep, Got(small.got)),
        after=("half_2",),
        in_specs=[SM, VM, VM],
        out_specs=(VM,) * 4,
        scratch_shapes=[pltpu.VMEM((LANES, LANES), F32)],
    )
    partner = flipped(other, "seq", seq, 1)
    ones = part1.over_copies(("small_sum",))
    part2.over_pieces(("copies_1",))
    small_piece = call(
        functools.partial(small_piece_kernel, csh, wide),
        sds((rest, small_width), BF16),
        "small_piece",
        (attn_rows, mine, Got(partner)),
        after=("pieces_2",),
        in_specs=[VM] * 3,
        out_specs=VM,
    )
    twos = part2.over_copies(extra=small_piece)
    grad_input, layer_out = call(
        functools.partial(finish_kernel, csh),
        (sds(x_in.shape, BF16), sds(x_in.shape, BF16)),
        "grad_input",
        (flags, base, Got(from_left), Got(from_right), mid, coef),
        after=("copies_2",),
        grid=(steps,),
        in_specs=[
            SM,
            col_block(C),
            whole((C, LANES)),
            whole((C, LANES)),
            col_block(C),
            whole((seq, 4 * RP, 2 * csh)),
        ],
        out_specs=(row_block, row_block),
        scratch_shapes=[pltpu.VMEM((LANES, C), F32), pltpu.VMEM((C, LANES), F32)],
    )

    (
        grad_step,
        grad_conv,
        grad_cond,
        grad_res,
        grad_skip,
        grad_queries,
        grad_query,
        grad_key,
        grad_value,
        grad_attn,
    ) = call(
        functools.partial(output_kernel, cs, csh, wide, seq),
        (
            sds((cs, C), F32),
            sds((3, cs, 2 * C), F32),
            sds((cs, 2 * C), F32),
            sds((cs, C), F32),
            sds((cs, C), F32),
            sds((QUERIES, cs), F32),
            sds((cs, C), F32),
            sds((cs, C), F32),
            sds((cs, C), F32),
            sds((cs, C), F32),
        ),
        "outputs",
        after=("grad_input",),
        args=(bit, *ones, *twos, queries, w_query),
        in_specs=[SM] + [VM] * 6,
        out_specs=(VM,) * 10,
        scratch_shapes=[
            pltpu.VMEM((4 * cs, wide1), F32),
            pltpu.VMEM((4 * cs, wide2 + LANES), F32),
            pltpu.VMEM((4 * cs, small_width), F32),
            pltpu.VMEM((LANES, LANES), F32),
            pltpu.VMEM((LANES, C), F32),
        ],
    )
    return (
        layer_out,
        skip_out,
        grad_input,
        grad_step,
        grad_conv,
        grad_cond,
        grad_res,
        grad_skip,
        grad_queries,
        grad_query,
        grad_key,
        grad_value,
        grad_attn,
        jnp.transpose(grad_film.reshape(2, csh, cs), (2, 0, 1)),
    )


def solution(mesh):
    frames = P("dp", None, "seq")
    matrix = P("dp", None)
    return jax.shard_map(
        functools.partial(body, mesh.shape["dp"], mesh.shape["seq"]),
        mesh=mesh,
        in_specs=(
            frames,
            frames,
            P("dp", None),
            P("dp"),
            P("dp", "seq", None),
            P("dp"),
            matrix,
            P(None, "dp", None),
            matrix,
            matrix,
            matrix,
            P(None, "dp"),
            matrix,
            matrix,
            matrix,
            matrix,
            frames,
            frames,
            frames,
        ),
        out_specs=(
            frames,
            frames,
            frames,
            matrix,
            P(None, "dp", None),
            matrix,
            matrix,
            matrix,
            P(None, "dp"),
            matrix,
            matrix,
            matrix,
            matrix,
            frames,
        ),
        check_vma=False,
    )
```

```python
import functools
import math

import jax
import jax.numpy as jnp
from jax import lax
from jax.experimental import pallas as pl
from jax.experimental.pallas import tpu as pltpu
from jax.sharding import PartitionSpec as P

C = 512
HEADS = 8
QUERIES = 32
HEAD_DIM = 64
SHIFT = 4
SQRT_HALF = 0.7071067811865476
NORM_EPS = 1e-05
MASKED_SCORE = -1e30
LANES = 128
RP = 16
NR = 4
EARLY = 640
F32 = jnp.float32
BF16 = jnp.bfloat16
VMEM_BYTES = 50 * 1024 * 1024


def nn(a, b):
    return lax.dot_general(a, b, (((1,), (0,)), ((), ())), preferred_element_type=F32)


def nt(a, b):
    return lax.dot_general(a, b, (((1,), (1,)), ((), ())), preferred_element_type=F32)


def parts(v, count):
    out = []
    for _ in range(count):
        low = v.astype(BF16).astype(F32)
        out.append(low)
        v = v - low
    return jnp.concatenate(out, axis=0).astype(BF16)


def fold(v, count):
    rows = v.shape[0] // count
    total = v[:rows]
    for k in range(1, count):
        total = total + v[k * rows : (k + 1) * rows]
    return total


def lane_ids(shape):
    return lax.broadcasted_iota(jnp.int32, shape, len(shape) - 1)


def sds(shape, dtype):
    return jax.ShapeDtypeStruct(shape, dtype)


VM = pl.BlockSpec(memory_space=pltpu.VMEM)
HB = pl.BlockSpec(memory_space=pl.ANY)
SM = pl.BlockSpec(memory_space=pltpu.SMEM)


def whole(shape):
    return pl.BlockSpec(shape, lambda i: (0,) * len(shape), pipeline_mode=pl.Buffered(1))


class Got:
    def __init__(self, array):
        self.array = array


class Caller:
    def __init__(self):
        self.done = {}

    def __call__(self, kernel, out_shape, name, args, flops=0, nbytes=0, prefetch=0, after=(), **kw):
        single = not isinstance(out_shape, tuple)
        shapes = (out_shape,) if single else out_shape
        specs = kw["out_specs"]
        specs = (specs,) if single else specs
        pinned = tuple(
            v if spec is SM else pltpu.HBM(v.shape, v.dtype) for v, spec in zip(shapes, specs)
        )
        in_specs = list(kw.pop("in_specs"))
        count = prefetch + len(in_specs)
        args = list(args)
        extra = len(after)
        for before in after:
            in_specs.append(HB)
            args.append(self.done[before] if isinstance(before, str) else before)

        def run(*refs):
            return kernel(*refs[:count], *refs[count + extra :])

        values = []
        for k, v in enumerate(args):
            spec = SM if k < prefetch else in_specs[k - prefetch]
            if isinstance(v, Got):
                values.append(v.array)
            elif spec is SM:
                values.append(v)
            else:
                values.append(pltpu.with_memory_space_constraint(v, pltpu.HBM))
        spec = pltpu.PrefetchScalarGridSpec(
            num_scalar_prefetch=prefetch,
            grid=kw.pop("grid", ()),
            in_specs=in_specs,
            out_specs=kw.pop("out_specs"),
            scratch_shapes=kw.pop("scratch_shapes", ()),
        )
        out = pl.pallas_call(
            run,
            out_shape=pinned[0] if single else pinned,
            name=name,
            grid_spec=spec,
            cost_estimate=pl.CostEstimate(
                flops=1, bytes_accessed=1, transcendentals=0
            ),
            compiler_params=pltpu.CompilerParams(vmem_limit_bytes=VMEM_BYTES),
        )(*values)
        self.done[name] = out if single else out[0]
        return out


def head_pack_kernel(
    csh,
    local,
    group_ref,
    bit_ref,
    attn_ref,
    film_ref,
    wq_ref,
    wk_ref,
    wv_ref,
    queries_ref,
    prompt_ref,
    out_ref,
    mine_ref,
    other_ref,
    scr,
):
    cs = attn_ref.shape[0]
    arows = mine_ref.shape[0]
    mine_ref[...] = prompt_ref[pl.ds(bit_ref[0] * arows, arows)]
    other_ref[...] = prompt_ref[pl.ds((1 - bit_ref[0]) * arows, arows)]
    out_ref[:, 0:C] = attn_ref[...]
    off = C
    scr[...] = jnp.zeros((2 * LANES, LANES), F32)
    scr[0 : 2 * csh, 0:cs] = film_ref[...].astype(F32)
    scr[LANES : LANES + QUERIES, 0:cs] = queries_ref[...].astype(F32)
    film = scr[0:LANES].T[0:cs]
    table = scr[LANES : 2 * LANES].T[0:cs]
    turn = lax.rem(C - local * group_ref[0], C)
    blocks = [film[:, 0 : 2 * csh]]
    for ref in (wq_ref, wk_ref, wv_ref):
        blocks.append(pltpu.roll(ref[...].astype(F32), turn, 1)[:, 0:local])
    blocks.append(table)
    for block in blocks:
        width = min(block.shape[1], out_ref.shape[1] - off)
        out_ref[:, off : off + width] = block[:, 0:width].astype(BF16)
        off += width
    if off < out_ref.shape[1]:
        out_ref[:, off:] = jnp.zeros((cs, out_ref.shape[1] - off), BF16)


SIDE = 480


def turned_pack_kernel(cs, bit_ref, conv_ref, cond_ref, res_ref, skip_ref, step_ref, out_ref, side_ref, middle_ref, scr):
    for k in range(3):
        scr[k * cs : (k + 1) * cs] = conv_ref[k]
    scr[3 * cs : 4 * cs] = cond_ref[...]
    turned = scr[...].T
    out_ref[0 : 2 * C - SIDE] = turned[0 : 2 * C - SIDE]
    at = 2 * C - SIDE
    for ref in (res_ref, skip_ref, step_ref):
        for lane in range(0, C, 4 * cs):
            out_ref[at : at + cs] = ref[:, lane : lane + 4 * cs]
            at += cs
    out_ref[at : at + SIDE] = turned[2 * C - SIDE :]
    middle_ref[...] = out_ref[SIDE:at]
    side_ref[...] = out_ref[pl.ds(pl.multiple_of(bit_ref[0] * at, 16), SIDE)]


def pair_kernel(a_ref, b_ref, out_ref):
    for p in range(out_ref.shape[0]):
        out_ref[p, 0] = a_ref[...]
        out_ref[p, 1] = b_ref[...]


def edge_kernel(x_ref, flags_ref, ids_ref, emb_ref, first_ref, last_ref, flags_out, ids_out, emb_out):
    for side in range(2):
        for r in range(x_ref.shape[0]):
            flags_out[side, r] = flags_ref[side, r]
    ids_out[...] = ids_ref[...]
    emb_out[...] = emb_ref[...]
    rows = x_ref.shape[0]
    lane = lane_ids((C, LANES))
    first = jnp.zeros((C, LANES), F32)
    last = jnp.zeros((C, LANES), F32)
    for r in range(rows):
        v = x_ref[r].astype(F32)
        here = (lane // SHIFT) == r
        first = jnp.where(here, pltpu.roll(v, SHIFT * r, 1) if r else v, first)
        last = jnp.where(here, pltpu.roll(v, SHIFT * r + SHIFT, 1), last)
    first_ref[...] = first.astype(BF16)
    last_ref[...] = last.astype(BF16)


def begin(copies):
    for copy in copies:
        copy.start()


def finish(copies):
    for copy in copies:
        copy.wait()


def turned_copies(meta, refs, off_ref, cs, wt, others, sems):
    dp = len({k for k, _ in meta})
    pairs = []

    def conv(k, ref, first, row, rows):
        if wt is not None:
            lanes = pl.ds(pl.multiple_of(off_ref[k] * 4, LANES), 4 * cs)
            at = row if isinstance(row, int) else pl.multiple_of(row, 16)
            pairs.append((ref.at[pl.ds(first, rows)], wt.at[pl.ds(at, rows), lanes]))

    def rest(k, ref, at):
        row = pl.ds(pl.multiple_of(off_ref[k], 16), cs)
        for other in others:
            for lane in range(0, C, 4 * cs):
                if other is not None:
                    dst, start = other
                    pairs.append((ref.at[pl.ds(at, cs)], dst.at[row, pl.ds(start + lane, 4 * cs)]))
                at += cs

    inner = 2 * C - 2 * SIDE
    for (k, which), ref in zip(meta, refs):
        if which is None:
            conv(k, ref, 0, 0, SIDE + inner)
            rest(k, ref, SIDE + inner)
            conv(k, ref, ref.shape[0] - SIDE, 2 * C - SIDE, SIDE)
        elif which == 2:
            conv(k, ref, 0, SIDE, inner)
            rest(k, ref, inner)
        else:
            conv(k, ref, 0, off_ref[dp + which] * (2 * C - SIDE), SIDE)
    return [pltpu.make_async_copy(a, b, sems.at[n]) for n, (a, b) in enumerate(pairs)]


def head_copies(refs, off_ref, dst, sems):
    copies = []
    for k, ref in enumerate(refs):
        row = pl.ds(pl.multiple_of(off_ref[k], 16), ref.shape[0])
        copies.append(pltpu.make_async_copy(ref, dst.at[row], sems.at[k]))
    return copies


def forward_kernel(
    meta, dp, csh, off_ref, flags_ref, x_ref, cond_ref, dout_ref, left_ref, right_ref, emb_ref, pooled_ref, *refs
):
    turned, refs = refs[: len(meta)], refs[len(meta) :]
    (
        inp_ref,
        gated_ref,
        fa_ref,
        fb_ref,
        skip_ref,
        mid_ref,
        stats_ref,
        wt_ref,
        rn_ref,
        step_ref,
        rst_ref,
        lift_ref,
        acc_ref,
        sems,
    ) = refs
    cs = C // dp
    i = pl.program_id(0)
    lane = lane_ids((C, LANES))

    @pl.when(i == 0)
    def _():
        copies = turned_copies(
            meta,
            turned,
            off_ref,
            cs,
            wt_ref,
            ((rn_ref, 0), (rn_ref, C), (step_ref, 0)),
            sems,
        )
        begin(copies)
        acc_ref[...] = jnp.zeros((C, LANES), F32)
        finish(copies)
        lift = nn(emb_ref[0:RP], step_ref[...])
        lift = jnp.concatenate([lift, jnp.zeros((LANES - RP, C), F32)], axis=0)
        lift_ref[...] = lift.T
        rst_ref[...] = rn_ref[...].T

    lift = pltpu.roll(lift_ref[...], lax.rem(LANES - NR * i, LANES), 1)
    left = left_ref[...].astype(F32)
    right = right_ref[...].astype(F32)

    def put(tap, cols, value):
        for d in range(dp):
            at = d * 4 * cs + tap * cs
            inp_ref[at : at + cs, cols] = value[d * cs : (d + 1) * cs]

    for j in range(NR):
        r = NR * i + j
        lc = lift[:, j : j + 1]
        sh = (x_ref[j].astype(F32) + lc).astype(BF16)
        shf = sh.astype(F32)
        lh = pltpu.roll(left, lax.rem(LANES - SHIFT * r, LANES), 1)
        lh = jnp.where(flags_ref[0, r] > 0, (lh + lc).astype(BF16).astype(F32), 0.0)
        rh = pltpu.roll(right, LANES - SHIFT - SHIFT * r, 1)
        rh = jnp.where(flags_ref[1, r] > 0, (rh + lc).astype(BF16).astype(F32), 0.0)
        cols = slice(j * LANES, (j + 1) * LANES)
        put(0, cols, jnp.where(lane < SHIFT, lh, pltpu.roll(shf, SHIFT, 1)).astype(BF16))
        put(1, cols, sh)
        put(
            2,
            cols,
            jnp.where(lane >= LANES - SHIFT, rh, pltpu.roll(shf, LANES - SHIFT, 1)).astype(BF16),
        )
        put(3, cols, cond_ref[j])
    pre = nn(wt_ref[...], inp_ref[...])
    th = jnp.tanh(pre[:C])
    sg = jax.nn.sigmoid(pre[C:])
    gf = th * sg
    fa_ref[...] = (sg - gf * th).astype(BF16)
    fb_ref[...] = (gf * (1.0 - sg)).astype(BF16)
    g = gf.astype(BF16)
    gated_ref[...] = g
    rs = nn(rst_ref[...], g)
    acc = acc_ref[...]
    for j in range(NR):
        r = NR * i + j
        cols = slice(j * LANES, (j + 1) * LANES)
        skip_ref[j] = rs[C:, cols].astype(BF16)
        mid = ((x_ref[j].astype(F32) + rs[:C, cols]) * SQRT_HALF).astype(BF16)
        mid_ref[:, cols] = mid
        mf = mid.astype(F32)
        df = dout_ref[j].astype(F32)
        total = jnp.sum(mf, axis=1, keepdims=True)
        dev = mf - total * (1.0 / LANES)
        acc = jnp.where(lane == r, total, acc)
        acc = jnp.where(lane == RP + r, jnp.sum(dev * dev, axis=1, keepdims=True), acc)
        acc = jnp.where(lane == 2 * RP + r, jnp.sum(df, axis=1, keepdims=True), acc)
        acc = jnp.where(lane == 3 * RP + r, jnp.sum(df * dev, axis=1, keepdims=True), acc)
    acc_ref[...] = acc

    @pl.when(i == pl.num_programs(0) - 1)
    def _():
        t = acc.T
        for s in range(C // csh):
            cols = slice(s * csh, (s + 1) * csh)
            stats_ref[s, 0 : 2 * RP, 0:csh] = t[0 : 2 * RP, cols]
            stats_ref[s, 0 : 2 * RP, csh : 2 * csh] = t[2 * RP : 4 * RP, cols]
            stats_ref[s, 2 * RP : 3 * RP] = pooled_ref[:, 0 : 2 * csh]


def attention_kernel(dp, rows, heads, pairs, off, off_ref, bit_ref, len_ref, prompts, *refs):
    pieces, refs = refs[:dp], refs[dp:]
    apack_ref, prow, probs_ref, u_ref, pooled_ref, qp_ref, qkv_ref, abd, sems = refs
    copies = head_copies(pieces, off_ref, apack_ref, sems)
    count = len(copies)
    for j in range(pairs):
        for i in range(2):
            copies.append(
                pltpu.make_async_copy(
                    prompts.at[j, i], prow.at[:, 2 * j + i], sems.at[count + 2 * j + i]
                )
            )
    begin(copies)
    local = prow.shape[2]
    total = 2 * pairs * local
    abd[...] = jnp.zeros(abd.shape, F32)
    lane = lane_ids((heads * QUERIES, total))
    place = jnp.zeros((heads * QUERIES, total), jnp.int32)
    for k in range(2 * pairs):
        here = (k // 2) * 2 + (bit_ref[0] if k % 2 == 0 else 1 - bit_ref[0])
        place = jnp.where(lane // local == k, here * local + lane % local, place)
    finish(copies)
    wide = heads * HEAD_DIM
    qkv = apack_ref[:, off : off + qkv_ref.shape[0]].T
    qkv_ref[...] = qkv
    qp = nt(qkv[3 * wide : 3 * wide + QUERIES], qkv[0:wide])
    qp_ref[...] = qp
    st = []
    for g in range(heads):
        cols = slice(g * HEAD_DIM, (g + 1) * HEAD_DIM)
        st.append(fold(nn(parts(qp[:, cols], 3), qkv[wide + cols.start : wide + cols.stop]), 3))
    st = jnp.concatenate(st, axis=0) * (1.0 / math.sqrt(HEAD_DIM))
    table = prow[...].reshape(rows * total, C)
    scores = fold(nt(parts(st, 3), table), 3)
    for r in range(rows):
        cols = slice(r * total, (r + 1) * total)
        live = place < len_ref[r]
        s = jnp.where(live, scores[:, cols], MASKED_SCORE)
        e = jnp.where(live, jnp.exp(s - jnp.max(s, axis=1, keepdims=True)), 0.0)
        p = e / jnp.sum(e, axis=1, keepdims=True)
        probs_ref[:, cols] = p
        for g in range(heads):
            abd[8 * g + r : 8 * g + r + 1, cols] = jnp.sum(
                p[g * QUERIES : (g + 1) * QUERIES], axis=0, keepdims=True
            )
    u = fold(nn(parts(abd[...], 2), table), 2)
    u_ref[...] = u
    pooled_ref[...] = jnp.zeros(pooled_ref.shape, F32)
    for g in range(heads):
        first = 2 * wide + g * HEAD_DIM
        v = parts(u[8 * g : 8 * g + 8] * (1.0 / QUERIES), 2)
        pooled_ref[0:8, g * HEAD_DIM : (g + 1) * HEAD_DIM] = fold(
            nt(v, qkv[first : first + HEAD_DIM]), 2
        )


def stats_kernel(
    csh, heads, rows, seg_ref, x_ref, apack_ref, out_ref, dfilm_ref, pooled_ref, memory_ref, scratch
):
    count = x_ref.shape[0]
    wide = heads * HEAD_DIM
    seg = seg_ref[...]
    scratch[...] = jnp.zeros(scratch.shape, F32)
    for s in range(count):
        group, part = s // 2, s % 2
        scratch[part * rows : (part + 1) * rows, group * wide : (group + 1) * wide] = x_ref[
            s, 2 * RP : 2 * RP + rows, 0:wide
        ]
    pooled = scratch[...].astype(BF16)
    pooled_ref[...] = pooled
    memory = nn(pooled, apack_ref[:, 0:C]).astype(BF16)
    memory_ref[...] = memory
    film = nn(memory, apack_ref[:, C : C + 2 * csh])
    f0 = film[:, 0:csh]
    f1 = film[:, csh : 2 * csh]
    total = [x_ref[s, 0:RP, 0:csh] for s in range(count)]
    second = [x_ref[s, RP : 2 * RP, 0:csh] for s in range(count)]
    dsum = [x_ref[s, 0:RP, csh : 2 * csh] for s in range(count)]
    cross = [x_ref[s, RP : 2 * RP, csh : 2 * csh] for s in range(count)]
    means = [v * (1.0 / LANES) for v in total]
    d0 = jnp.zeros((RP, csh), F32)
    d1 = jnp.zeros((RP, csh), F32)
    for me in range(count):
        same = [(seg[:, s : s + 1] == seg[:, me : me + 1]).astype(F32) for s in range(count)]
        frames = sum(same) * float(LANES)
        inv = 1.0 / frames
        mean = sum(m * v for m, v in zip(same, total)) * inv
        var = (
            sum(
                m * (v + float(LANES) * (u - mean) * (u - mean))
                for m, v, u in zip(same, second, means)
            )
            * inv
        )
        scale = lax.rsqrt(var + NORM_EPS)
        dtot = sum(m * v for m, v in zip(same, dsum))
        xtot = sum(m * (v + (u - mean) * d) for m, v, u, d in zip(same, cross, means, dsum)) * scale
        mean_part = f0 * dtot * inv
        cross_part = f0 * xtot * inv
        slope = scale * scale * cross_part
        out_ref[me, 0:RP, 0:csh] = 1.0 + f0 * scale
        out_ref[me, RP : 2 * RP, 0:csh] = f1 - f0 * scale * mean
        out_ref[me, 0:RP, csh : 2 * csh] = -slope
        out_ref[me, RP : 2 * RP, csh : 2 * csh] = slope * mean - scale * mean_part
        d0 = d0 + (cross[me] + (means[me] - mean) * dsum[me]) * scale
        d1 = d1 + dsum[me]
    dfilm = jnp.concatenate([d0, d1], axis=1).astype(BF16)
    dfilm_ref[...] = dfilm
    dmem = nt(dfilm, apack_ref[:, C : C + 2 * csh])
    dpool = nt(dmem.astype(BF16), apack_ref[:, 0:C])
    for s in range(count):
        group, part = s // 2, s % 2
        rolled = pltpu.roll(dpool, RP - part * rows, 0) if part else dpool
        out_ref[s, 2 * RP : 3 * RP, 0:csh] = dmem[:, s * csh : (s + 1) * csh]
        out_ref[s, 2 * RP : 3 * RP, csh : 2 * csh] = jnp.zeros((RP, csh), F32)
        out_ref[s, 3 * RP : 4 * RP] = rolled[:, group * wide : (group + 1) * wide]


def coef_columns(csh, coef_ref, rows_ref, cols_ref):
    rows_ref[...] = jnp.zeros(rows_ref.shape, F32)
    for s in range(C // csh):
        cols = slice(s * csh, (s + 1) * csh)
        rows_ref[0 : 2 * RP, cols] = coef_ref[s, 0 : 2 * RP, 0:csh]
        rows_ref[2 * RP : 4 * RP, cols] = coef_ref[s, 0 : 2 * RP, csh : 2 * csh]
    cols_ref[...] = rows_ref[...].T


def skip_grad_kernel(gated_ref, dskip_ref, out_ref, right):
    for r in range(dskip_ref.shape[0]):
        right[:, r * LANES : (r + 1) * LANES] = dskip_ref[r]
    out_ref[...] = nt(gated_ref[...], right[...]).astype(BF16)


def backward_kernel(meta, dp, csh, gates, order_ref, off_ref, coef_ref, mid_ref, dout_ref, dskip_ref, fa_ref, fb_ref, inp_ref, gated_ref, gskip_ref, flags_ref, *refs):
    turned, refs = refs[: len(meta)], refs[len(meta) :]
    dpre_ref, dres_ref, sums_ref, refs = refs[0], refs[1], refs[2], refs[3:]
    outs, refs = (refs[0:2], refs[2:4]), refs[4:]
    rows_ref, cols_ref, w_ref, both_ref, dpt_ref, drt_ref, sems = refs
    cs = C // dp
    span = NR * LANES
    i = pl.program_id(0)

    @pl.when(i == 0)
    def _():
        copies = turned_copies(
            meta, turned, off_ref, cs, None, ((w_ref, 0), (w_ref, C), None), sems
        )
        begin(copies)
        coef_columns(csh, coef_ref, rows_ref, cols_ref)
        sums_ref[...] = jnp.zeros(sums_ref.shape, F32)
        finish(copies)

    @pl.when(i < gates)
    def _():
        coef = pltpu.roll(cols_ref[...], lax.rem(LANES - NR * i, LANES), 1)
        for j in range(NR):
            cols = slice(j * LANES, (j + 1) * LANES)
            mf = mid_ref[:, cols].astype(F32)
            df = dout_ref[j].astype(F32)
            a = coef[:, j : j + 1]
            be = coef[:, 2 * RP + j : 2 * RP + j + 1]
            ga = coef[:, 3 * RP + j : 3 * RP + j + 1]
            dmid = (a * df + (be * mf + ga)).astype(BF16).astype(F32)
            both_ref[0:C, cols] = (dmid * SQRT_HALF).astype(BF16)
            both_ref[C : 2 * C, cols] = dskip_ref[j]
        dres = both_ref[0:C]
        dres_ref[...] = dres
        dg = nn(w_ref[...], both_ref[...])
        dt = (dg * fa_ref[...].astype(F32)).astype(BF16)
        ds = (dg * fb_ref[...].astype(F32)).astype(BF16)
        dpre_ref[0:C] = dt
        dpre_ref[C : 2 * C] = ds
        at = pl.ds(pl.multiple_of(i * span, span), span)
        dpt_ref[at, 0:C] = dt.T
        dpt_ref[at, C : 2 * C] = ds.T
        drt_ref[at] = dres.T
        frame = lax.broadcasted_iota(jnp.int32, (span, LANES), 0)
        column = lane_ids((span, LANES))
        place = frame % LANES
        which = frame // LANES
        keep_l = jnp.zeros((span, LANES), jnp.int32)
        keep_r = jnp.zeros((span, LANES), jnp.int32)
        for j in range(NR):
            keep_l = jnp.where(which == j, flags_ref[0, NR * i + j], keep_l)
            keep_r = jnp.where(which == j, flags_ref[1, NR * i + j], keep_r)
        row = NR * i + which
        use0 = (column == row) & ((place >= SHIFT) | (keep_l > 0))
        use1 = column == RP + row
        use2 = (column == 2 * RP + row) & ((place < LANES - SHIFT) | (keep_r > 0))
        pick = jnp.where(use0 | use1 | use2, 1.0, 0.0).astype(BF16)
        sums_ref[...] = sums_ref[...] + nn(dpre_ref[...], pick)

    @pl.when(i >= gates)
    def _():
        g = nn(inp_ref[...], dpt_ref[...]).astype(BF16)
        h = nn(gated_ref[...], drt_ref[...]).astype(BF16)
        k = i - gates
        for parity, (one, two) in enumerate(outs):

            @pl.when(lax.rem(k, 2) == parity)
            def _():
                for t in range(4):
                    rows = slice(t * cs, (t + 1) * cs)
                    lanes = slice(t * LANES, (t + 1) * LANES)
                    one[0, rows, 0:LANES] = h[:, lanes]
                    one[0, rows, LANES : 2 * LANES] = gskip_ref[:, lanes]
                one[0, :, 2 * LANES :] = g[:, 0:EARLY]
                two[0] = g[:, EARLY:]


def step_grad_kernel(meta, dp, off_ref, sums_ref, emb_ref, *refs):
    turned, refs = refs[: len(meta)], refs[len(meta) :]
    keep_ref, give_ref, wt_ref, scr, sems = refs
    cs = C // dp
    copies = turned_copies(meta, turned, off_ref, cs, wt_ref, (None,) * 3, sems)
    begin(copies)
    sums = sums_ref[...].T
    emb = emb_ref[...].T
    finish(copies)
    total = jnp.zeros((RP, 4 * C), F32)
    lane = lane_ids((RP, 4 * C))
    all_taps = fold(nn(parts(sums[0 : 3 * RP], 2), wt_ref[...]), 2)
    for t in range(3):
        g = all_taps[t * RP : (t + 1) * RP]
        total = total + jnp.where((lane // cs) % 4 == t, g, 0.0)
    out = []
    for d in range(dp):
        block = total[:, d * 4 * cs : (d + 1) * 4 * cs]
        out.append(block[:, 0:cs] + block[:, cs : 2 * cs] + block[:, 2 * cs : 3 * cs])
    g = jnp.concatenate(out, axis=1)
    g = jnp.concatenate([g, jnp.zeros((LANES - RP, C), F32)], axis=0)
    hi = g.astype(BF16)
    lo = (g - hi.astype(F32)).astype(BF16)
    scr[...] = nn(emb, hi) + nn(emb, lo)
    for k in range(dp):
        v = scr[pl.ds(pl.multiple_of(off_ref[k], 16), cs)].astype(BF16)
        for t in range(4):
            (keep_ref, give_ref)[k % 2][k // 2, t * cs : (t + 1) * cs] = v[
                :, t * LANES : (t + 1) * LANES
            ]


def input_grad_kernel(meta, dp, off_ref, dpre_ref, dres_ref, *refs):
    turned, refs = refs[: len(meta)], refs[len(meta) :]
    base_ref, first_ref, last_ref, wt_ref, w_ref, facc_ref, lacc_ref, sems = refs
    cs = C // dp
    i = pl.program_id(0)
    lane = lane_ids((C, LANES))

    @pl.when(i == 0)
    def _():
        copies = turned_copies(meta, turned, off_ref, cs, wt_ref, (None,) * 3, sems)
        begin(copies)
        facc_ref[...] = jnp.zeros((C, LANES), F32)
        lacc_ref[...] = jnp.zeros((C, LANES), F32)
        finish(copies)
        for d in range(dp):
            v = wt_ref[:, d * 4 * cs : (d + 1) * 4 * cs].T
            for t in range(3):
                w_ref[t, d * cs : (d + 1) * cs] = v[t * cs : (t + 1) * cs]

    dpre = dpre_ref[...]
    y0 = nn(w_ref[0], dpre)
    y1 = nn(w_ref[1], dpre)
    y2 = nn(w_ref[2], dpre)
    facc = facc_ref[...]
    lacc = lacc_ref[...]
    for j in range(NR):
        r = NR * i + j
        cols = slice(j * LANES, (j + 1) * LANES)
        z0 = pltpu.roll(y0[:, cols], LANES - SHIFT, 1)
        z2 = pltpu.roll(y2[:, cols], SHIFT, 1)
        inner0 = lane < LANES - SHIFT
        inner2 = lane >= SHIFT
        v = y1[:, cols]
        base_ref[:, cols] = (
            v
            + jnp.where(inner0, z0, 0.0)
            + jnp.where(inner2, z2, 0.0)
            + dres_ref[:, cols].astype(F32)
        ).astype(BF16)
        here = (lane // SHIFT) == r
        facc = jnp.where(here, pltpu.roll(z0, lax.rem(SHIFT * r + SHIFT, LANES), 1), facc)
        lacc = jnp.where(here, pltpu.roll(z2, SHIFT * r, 1), lacc)
    facc_ref[...] = facc
    lacc_ref[...] = lacc

    @pl.when(i == pl.num_programs(0) - 1)
    def _():
        first_ref[...] = facc.astype(BF16)
        last_ref[...] = lacc.astype(BF16)


def finish_kernel(csh, flags_ref, base_ref, left_ref, right_ref, mid_ref, coef_ref, out_ref, layer_ref, rows_ref, cols_ref):
    i = pl.program_id(0)
    lane = lane_ids((C, LANES))

    @pl.when(i == 0)
    def _():
        coef_columns(csh, coef_ref, rows_ref, cols_ref)

    coef = pltpu.roll(cols_ref[...], lax.rem(LANES - NR * i, LANES), 1)
    left = left_ref[...].astype(F32)
    right = right_ref[...].astype(F32)
    for j in range(NR):
        r = NR * i + j
        cols = slice(j * LANES, (j + 1) * LANES)
        lh = pltpu.roll(left, lax.rem(LANES - SHIFT * r, LANES), 1)
        rh = pltpu.roll(right, LANES - SHIFT - SHIFT * r, 1)
        lh = jnp.where((lane < SHIFT) & (flags_ref[0, r] > 0), lh, 0.0)
        rh = jnp.where((lane >= LANES - SHIFT) & (flags_ref[1, r] > 0), rh, 0.0)
        out_ref[j] = (base_ref[:, cols].astype(F32) + lh + rh).astype(BF16)
        a = coef[:, j : j + 1]
        b = coef[:, RP + j : RP + j + 1]
        layer_ref[j] = (a * mid_ref[:, cols].astype(F32) + b).astype(BF16)


def add_blocks_kernel(count, *refs):
    ins, (keep_ref, give_ref) = refs[: 2 * count], refs[2 * count :]
    at = 0
    for p in range(count):
        a_ref, b_ref = ins[2 * p : 2 * p + 2]
        width = a_ref.shape[2]
        for j in range(a_ref.shape[0]):
            v = a_ref[j].astype(F32) + b_ref[j].astype(F32)
            (keep_ref, give_ref)[j % 2][j // 2, :, at : at + width] = v.astype(BF16)
        at += width


def add_halves_kernel(bit, index_ref, a_ref, b_ref, keep_ref, give_ref, scr):
    half = a_ref.shape[0] // 2
    mine = lax.rem(index_ref[0] // bit, 2)
    scr[...] = a_ref[...].astype(F32) + b_ref[...].astype(F32)
    keep_ref[...] = scr[pl.ds(pl.multiple_of(mine * half, 8), half)].astype(BF16)
    give_ref[...] = scr[pl.ds(pl.multiple_of((1 - mine) * half, 8), half)].astype(BF16)


def add_pieces_kernel(a_ref, b_ref, out_ref):
    v = a_ref[...].astype(F32) + b_ref[...].astype(F32)
    size = out_ref.shape[1]
    for p in range(out_ref.shape[0]):
        out_ref[p] = v[p * size : (p + 1) * size].astype(BF16)


def sum_copies_kernel(a_ref, *refs):
    out_ref = refs[-1]
    v = a_ref[0].astype(F32)
    for p in range(1, a_ref.shape[0]):
        v = v + a_ref[p].astype(F32)
    v = v.astype(BF16)
    for p in range(out_ref.shape[0]):
        out_ref[p, :, 0 : v.shape[1]] = v
        if len(refs) > 1:
            out_ref[p, :, v.shape[1] :] = refs[0][...]


def small_sum_kernel(csh, wide, bit_ref, keep_ref, got_ref, film_ref, attn_ref, mine_ref, other_ref, turn):
    v = keep_ref[0].astype(F32) + got_ref[0].astype(F32)
    cs = v.shape[0]
    film = 2 * wide + csh
    turn[...] = jnp.zeros(turn.shape, F32)
    turn[0:cs, 0 : 2 * csh] = v[:, film : film + 2 * csh]
    film_ref[...] = turn[...].T[0 : 2 * csh, 0:cs]
    attn_ref[...] = v[:, 2 * wide : film]
    last = film + 2 * csh
    even = bit_ref[0] == 0
    for one, two, rows, width in (
        (v[:, 0:wide], v[:, wide : 2 * wide], slice(0, cs), wide),
        (
            v[0:QUERIES, last : last + wide // 2],
            v[0:QUERIES, last + wide // 2 : last + wide],
            slice(cs, cs + QUERIES),
            wide // 2,
        ),
    ):
        mine_ref[rows, 0:width] = jnp.where(even, one, two).astype(BF16)
        other_ref[rows, 0:width] = jnp.where(even, two, one).astype(BF16)
    mine_ref[cs:, wide // 2 :] = jnp.zeros((QUERIES, wide // 2), BF16)
    other_ref[cs:, wide // 2 :] = jnp.zeros((QUERIES, wide // 2), BF16)


def small_piece_kernel(csh, wide, attn_ref, mine_ref, got_ref, out_ref):
    v = mine_ref[...].astype(F32) + got_ref[...].astype(F32)
    attn = attn_ref[...]
    cs = attn.shape[0]
    rows = out_ref.shape[0]
    at = 0
    for row in range(0, cs, rows):
        out_ref[:, at : at + wide] = v[row : row + rows].astype(BF16)
        out_ref[:, at + wide : at + wide + csh] = attn[row : row + rows].astype(BF16)
        at += wide + csh
    for row in range(0, QUERIES, rows):
        block = v[cs + row : cs + min(row + rows, QUERIES), 0 : wide // 2]
        if block.shape[0] < rows:
            pad = jnp.zeros((rows - block.shape[0], wide // 2), F32)
            block = jnp.concatenate([block, pad], axis=0)
        out_ref[:, at : at + wide // 2] = block.astype(BF16)
        at += wide // 2


def output_kernel(
    cs,
    csh,
    wide,
    seq,
    bit_ref,
    *refs,
):
    own1, got1, own2, got2, refs = *refs[:4], refs[4:]
    (
        queries_ref,
        wq_ref,
        step_ref,
        conv_ref,
        cond_ref,
        res_ref,
        skip_ref,
        gqueries_ref,
        gquery_ref,
        key_ref,
        value_ref,
        attn_ref,
        scr1,
        scr2,
        small,
        qscr,
        dq,
    ) = refs
    count, size = own1.shape[0], own1.shape[1]
    wide2 = scr2.shape[1]
    bit = bit_ref[0]
    for one, two, side in ((own1, own2, bit), (got1, got2, 1 - bit)):
        for p in range(count):
            rows = pl.ds(pl.multiple_of((side * count + p) * size, 8), size)
            scr1[rows] = one[p].astype(F32)
            v = two[p].astype(F32)
            scr2[rows] = v[:, 0:wide2]
            small[pl.ds(pl.multiple_of((2 * p + side) * size, 8), size)] = v[:, wide2:]
    for t in range(4):
        rows = slice(t * cs, (t + 1) * cs)
        lanes = slice(t * LANES, (t + 1) * LANES)
        res_ref[:, lanes] = scr1[rows, 0:LANES]
        skip_ref[:, lanes] = scr1[rows, LANES : 2 * LANES]
        rest = 2 * C - EARLY
        step_ref[:, lanes] = scr2[rows, rest : rest + LANES]
        if t < 3:
            conv_ref[t, :, 0:EARLY] = scr1[rows, 2 * LANES : 2 * LANES + EARLY]
            conv_ref[t, :, EARLY:] = scr2[rows, 0:rest]
        else:
            cond_ref[:, 0:EARLY] = scr1[rows, 2 * LANES : 2 * LANES + EARLY]
            cond_ref[:, EARLY:] = scr2[rows, 0:rest]
    dq[...] = jnp.zeros(dq.shape, F32)
    for s in range(seq):
        v = small[s * size : (s + 1) * size]
        group, even = s // 2, s % 2 == 0
        out = key_ref if even else value_ref
        at = 0
        for row in range(0, cs, size):
            out[row : row + size, group * wide : (group + 1) * wide] = v[:, at : at + wide]
            attn_ref[row : row + size, s * csh : (s + 1) * csh] = v[:, at + wide : at + wide + csh]
            at += wide + csh
        first = group * wide + (0 if even else wide // 2)
        for row in range(0, QUERIES, size):
            count = min(size, QUERIES - row)
            dq[row : row + count, first : first + wide // 2] = v[0:count, at : at + wide // 2]
            at += wide // 2
    qscr[...] = jnp.zeros((LANES, LANES), F32)
    qscr[0:QUERIES, 0:cs] = queries_ref[...].astype(F32)
    qt = qscr[...].T.astype(BF16)
    d = dq[...]
    hi = d.astype(BF16)
    lo = (d - hi.astype(F32)).astype(BF16)
    gquery_ref[...] = (nn(qt, hi) + nn(qt, lo))[0:cs]
    gqueries_ref[...] = fold(nt(parts(d[0:QUERIES], 2), wq_ref[...]), 2)


def attention_back_kernel(
    rows,
    csh,
    dp,
    off_ref,
    prow,
    probs_ref,
    u_ref,
    qp_ref,
    qkv_ref,
    pooled_ref,
    memory_ref,
    dfilm_ref,
    got_ref,
    keep_ref,
    give_ref,
    ds,
    stack,
    right,
    out,
):
    count = got_ref.shape[0]
    total = prow.shape[1] * prow.shape[2]
    cs = C // dp
    table = prow[...].reshape(rows * total, C)
    wide = qp_ref.shape[1]
    heads = wide // HEAD_DIM
    datt = got_ref[0, 3 * RP : 4 * RP, 0:wide]
    dmem = got_ref[0, 2 * RP : 3 * RP, 0:csh]
    for s in range(1, count):
        datt = datt + got_ref[s, 3 * RP : 4 * RP, 0:wide]
        dmem = dmem + got_ref[s, 2 * RP : 3 * RP, 0:csh]
    datt = datt[0:8] * (1.0 / QUERIES)
    vh = []
    for g in range(heads):
        first = 2 * wide + g * HEAD_DIM
        v = parts(datt[:, g * HEAD_DIM : (g + 1) * HEAD_DIM], 2)
        vh.append(fold(nn(v, qkv_ref[first : first + HEAD_DIM]), 2))
    vh = jnp.concatenate(vh, axis=0)
    dp_all = fold(nt(parts(vh, 2), table), 2)
    for r in range(rows):
        cols = slice(r * total, (r + 1) * total)
        for g in range(heads):
            mine = slice(g * QUERIES, (g + 1) * QUERIES)
            p = probs_ref[mine, cols]
            dpr = dp_all[8 * g + r : 8 * g + r + 1, cols]
            inner = jnp.sum(p * dpr, axis=1, keepdims=True)
            ds[mine, cols] = p * (dpr - inner)
    tt = fold(nn(parts(ds[...], 2), table), 2)
    scale = 1.0 / math.sqrt(HEAD_DIM)
    dq = []
    stack[...] = jnp.zeros(stack.shape, F32)
    right[...] = jnp.zeros(right.shape, F32)
    stack[0 : heads * QUERIES] = tt
    stack[64:80] = u_ref[...]
    stack[80:96] = pooled_ref[...].astype(F32)
    stack[96:112] = memory_ref[...].astype(F32)
    for g in range(heads):
        cols = slice(g * HEAD_DIM, (g + 1) * HEAD_DIM)
        mine = slice(g * QUERIES, (g + 1) * QUERIES)
        wk = qkv_ref[wide + g * HEAD_DIM : wide + (g + 1) * HEAD_DIM]
        dq.append(fold(nt(parts(tt[mine], 2), wk), 2) * scale)
        right[mine, cols] = qp_ref[:, cols] * scale
        right[64 + 8 * g : 72 + 8 * g, wide + cols.start : wide + cols.stop] = datt[:, cols]
    right[80:96, 2 * wide : 2 * wide + csh] = dmem
    right[96:112, 2 * wide + csh : 2 * wide + 3 * csh] = dfilm_ref[...].astype(F32)
    out[...] = lax.dot_general(
        stack[...].T,
        right[...],
        (((1,), (0,)), ((), ())),
        precision=lax.Precision.HIGHEST,
        preferred_element_type=F32,
    )
    last = 2 * wide + 3 * csh
    for k in range(dp):
        ref = (keep_ref, give_ref)[k % 2]
        ref[k // 2] = out[pl.ds(pl.multiple_of(off_ref[k], 16), cs)].astype(BF16)
        for g in range(heads):
            first = last + g * HEAD_DIM
            ref[k // 2, 0:QUERIES, first : first + HEAD_DIM] = dq[g].astype(BF16)


def exchange(pieces, axis, groups=None):
    return lax.all_to_all(
        pieces, axis, split_axis=0, concat_axis=0, axis_index_groups=groups, tiled=True
    )


def flipped(v, axis, size, bit):
    return lax.ppermute(v, axis, [(d, d ^ bit) for d in range(size)])


class Reduction:
    def __init__(self, call, name, keep, give, dp, seq, index):
        self.call, self.name, self.dp, self.seq, self.index = call, name, dp, seq, index
        self.keep, self.flip = keep, 1
        self.got = flipped(give, "dp", dp, 1)

    def over_blocks(self, after=(), others=()):
        while 2 * self.flip < self.dp:
            group = (self,) + tuple(others)
            others = ()
            args = []
            for part in group:
                args += [part.keep, Got(part.got)]
            width = sum(part.keep.shape[2] for part in group)
            half = sds((self.keep.shape[0] // 2, self.keep.shape[1], width), BF16)
            self.keep, give = self.call(
                functools.partial(add_blocks_kernel, len(group)),
                (half, half),
                "blocks_" + self.name,
                args,
                after=after,
                in_specs=[VM] * len(args),
                out_specs=(VM, VM),
            )
            self.flip *= 2
            self.got = flipped(give, "dp", self.dp, self.flip)
        self.rest = self.keep.shape[1:]

    def over_half(self, after=()):
        rows, width = self.rest
        half = sds((rows // 2, width), BF16)
        self.keep, give = self.call(
            functools.partial(add_halves_kernel, 1),
            (half, half),
            "half_" + self.name,
            (self.index, self.keep.reshape(rows, width), Got(self.got.reshape(rows, width))),
            after=after,
            in_specs=[SM, VM, VM],
            out_specs=(VM, VM),
            scratch_shapes=[pltpu.VMEM((rows, width), F32)],
        )
        self.got = flipped(give, "seq", self.seq, 1)

    def over_pieces(self, after=()):
        rows, width = self.rest
        count = self.seq // 2
        self.groups = [[2 * k + b for k in range(count)] for b in range(2)]
        pieces = self.call(
            add_pieces_kernel,
            sds((count, rows // self.seq, width), BF16),
            "pieces_" + self.name,
            (self.keep, Got(self.got)),
            after=after,
            in_specs=[VM, VM],
            out_specs=VM,
        )
        self.got = exchange(pieces, "seq", self.groups)

    def over_copies(self, after=(), extra=None):
        args, (count, rows, width) = [Got(self.got)], self.got.shape
        if extra is not None:
            args.append(extra)
            width += extra.shape[1]
        copies = self.call(
            sum_copies_kernel,
            sds((count, rows, width), BF16),
            "copies_" + self.name,
            args,
            after=after,
            in_specs=[VM] * len(args),
            out_specs=VM,
        )
        own = exchange(copies, "seq", self.groups)
        return Got(own), Got(flipped(own, "seq", self.seq, 1))


def body(
    dp,
    seq,
    x_in,
    cond,
    segment_ids,
    diffusion_steps,
    prompt,
    prompt_lengths,
    w_step,
    w_conv,
    w_cond,
    w_res,
    w_skip,
    queries,
    w_query,
    w_key,
    w_value,
    w_attn_out,
    w_film,
    d_out,
    d_skip,
):
    call = Caller()
    rows = x_in.shape[0]
    frames = x_in.shape[2]
    steps = rows // NR
    cols = rows * frames
    cs = C // dp
    csh = C // seq
    heads = 2 * HEADS // seq
    wide = heads * HEAD_DIM
    arows = rows // 2
    pl_local = prompt.shape[1]
    prompt_all = pl_local * seq
    sidx = lax.axis_index("seq")
    didx = lax.axis_index("dp")
    group = (sidx // 2).astype(jnp.int32).reshape(1)
    bit = (sidx % 2).astype(jnp.int32).reshape(1)
    up = [(i, i + 1) for i in range(seq - 1)]
    down = [(i + 1, i) for i in range(seq - 1)]
    order = jnp.bitwise_xor(didx, jnp.arange(dp, dtype=jnp.int32)).astype(jnp.int32)
    offsets = jnp.concatenate([order * cs, bit, 1 - bit])
    index = sidx.astype(jnp.int32).reshape(1)

    def gather(pack, side=None, middle=None):
        if dp == 4 and side is not None:
            mine = flipped(side, "dp", dp, 2)
            inner = flipped(middle, "dp", dp, 2)
            other = flipped(mine, "seq", seq, 1)
            near = [(0, None, pack), (2, 0, mine), (2, 2, inner), (2, 1, other)]
            pieces = near + [(k + 1, h, flipped(v, "dp", dp, 1)) for k, h, v in near]
        else:
            pieces = [(0, None, pack)]
            flip = dp // 2
            while flip:
                pieces += [(k + flip, h, flipped(v, "dp", dp, flip)) for k, h, v in pieces]
                flip //= 2
        pieces.sort(key=lambda piece: piece[0])
        meta = [(k, h) for k, h, _ in pieces]
        return meta, [v if k == 0 else Got(v) for k, _, v in pieces]

    off_qkv = C + 2 * csh
    qkv_rows = -(-(3 * wide + QUERIES) // LANES) * LANES
    head_width = -(-(off_qkv + qkv_rows) // LANES) * LANES
    pack, mine, other = call(
        functools.partial(head_pack_kernel, csh, wide),
        (
            sds((cs, head_width), BF16),
            sds((arows, pl_local, C), BF16),
            sds((arows, pl_local, C), BF16),
        ),
        "head_pack",
        (
            group,
            bit,
            w_attn_out,
            jnp.transpose(w_film, (1, 2, 0)).reshape(2 * csh, cs),
            w_query,
            w_key,
            w_value,
            queries,
            prompt,
        ),
        in_specs=[SM, SM] + [VM] * 7,
        out_specs=(VM,) * 3,
        scratch_shapes=[pltpu.VMEM((2 * LANES, LANES), F32)],
    )
    _, head_pieces = gather(pack)
    partner = flipped(other, "seq", seq, 1)
    pair = call(
        pair_kernel,
        sds((seq // 2, 2, arows, pl_local, C), BF16),
        "pair",
        (mine, Got(partner)),
        in_specs=[VM, VM],
        out_specs=VM,
    )
    middle = 2 * C - 2 * SIDE + 3 * C // 4
    pack, side, middle = call(
        functools.partial(turned_pack_kernel, cs),
        (
            sds((2 * SIDE + middle, 4 * cs), BF16),
            sds((SIDE, 4 * cs), BF16),
            sds((middle, 4 * cs), BF16),
        ),
        "turned_pack",
        (bit, w_conv, w_cond, w_res, w_skip, w_step),
        after=("pair", head_pieces[dp // 2].array),
        in_specs=[SM] + [VM] * 5,
        out_specs=(VM, VM, VM),
        scratch_shapes=[pltpu.VMEM((4 * cs, 2 * C), BF16)],
    )
    meta, turned = gather(pack, side, middle)
    copies = 4 * dp * (1 + 3 * C // (4 * cs))
    z_groups = [[2 * k + b for k in range(seq // 2)] for b in range(2)]
    prompts = Got(exchange(pair, "seq", z_groups))
    block_ids = segment_ids[:, ::frames]
    padded_ids = jnp.pad(block_ids, ((0, 0), (1, 1)), constant_values=-1)
    mine = lax.dynamic_slice_in_dim(padded_ids, sidx, 3, 1)
    flags = jnp.stack([mine[:, 0] == mine[:, 1], mine[:, 2] == mine[:, 1]]).astype(jnp.int32)
    block_ids = jnp.pad(block_ids, ((0, RP - rows), (0, 0)))
    half = C // 2
    frequency = jnp.exp(jnp.arange(half, dtype=F32) * (-math.log(10000.0) / half))
    step_rows = jnp.pad(diffusion_steps.astype(F32), (0, LANES - rows))
    live_rows = jnp.arange(LANES, dtype=jnp.int32)[:, None] < rows
    angles = step_rows[:, None] * frequency[None, :]
    embedding = jnp.concatenate([jnp.sin(angles), jnp.cos(angles)], axis=1)
    embedding = jnp.where(live_rows, embedding, 0.0).astype(BF16)
    first, last, flags, block_ids, embedding = call(
        edge_kernel,
        (
            sds((C, LANES), BF16),
            sds((C, LANES), BF16),
            sds(flags.shape, jnp.int32),
            sds(block_ids.shape, jnp.int32),
            sds(embedding.shape, BF16),
        ),
        "edges",
        (x_in, flags, block_ids, embedding),
        after=("turned_pack",),
        in_specs=[VM, SM, VM, VM],
        out_specs=(VM, VM, SM, VM, VM),
    )
    left_halo = lax.ppermute(last, "seq", up)
    right_halo = lax.ppermute(first, "seq", down)

    lengths = lax.dynamic_slice_in_dim(prompt_lengths, (sidx % 2) * arows, arows, 0)

    apack, prow, probs, u, pooled_head, qp, qkv = call(
        functools.partial(attention_kernel, dp, arows, heads, seq // 2, off_qkv),
        (
            sds((C, head_width), BF16),
            sds((arows, seq, pl_local, C), BF16),
            sds((heads * QUERIES, arows * prompt_all), F32),
            sds((RP, C), F32),
            sds((RP, LANES), F32),
            sds((QUERIES, wide), F32),
            sds((qkv_rows, C), BF16),
        ),
        "attention",
        (offsets, bit, lengths, prompts, *head_pieces),
        in_specs=[SM, SM, SM, HB] + [HB] * dp,
        out_specs=(VM,) * 7,
        scratch_shapes=[
            pltpu.VMEM((RP, arows * prompt_all), F32),
            pltpu.SemaphoreType.DMA((dp + seq,)),
        ],
    )

    row_block = pl.BlockSpec((NR, C, LANES), lambda i: (i, 0, 0))

    def col_block(height):
        return pl.BlockSpec((height, NR * LANES), lambda i: (0, i))

    def still(shape):
        return pl.BlockSpec(shape, lambda i: (0,) * len(shape))

    inp, gated, factor_a, factor_b, skip_out, mid, stats = call(
        functools.partial(forward_kernel, meta, dp, csh),
        (
            sds((4 * C, cols), BF16),
            sds((C, cols), BF16),
            sds((C, cols), BF16),
            sds((C, cols), BF16),
            sds(x_in.shape, BF16),
            sds((C, cols), BF16),
            sds((seq, 3 * RP, 2 * csh), F32),
        ),
        "wavenet",
        (
            offsets,
            flags,
            x_in,
            cond,
            d_out,
            Got(left_halo),
            Got(right_halo),
            embedding,
            pooled_head,
            *turned,
        ),
        flops=2 * cols * (4 * C * 2 * C + 2 * C * C),
        nbytes=30e6,
        grid=(steps,),
        in_specs=[
            SM,
            SM,
            row_block,
            row_block,
            row_block,
            whole((C, LANES)),
            whole((C, LANES)),
            whole((LANES, C)),
            whole((RP, LANES)),
        ]
        + [HB] * len(turned),
        out_specs=(
            col_block(4 * C),
            col_block(C),
            col_block(C),
            col_block(C),
            row_block,
            col_block(C),
            still((seq, 3 * RP, 2 * csh)),
        ),
        scratch_shapes=[
            pltpu.VMEM((2 * C, 4 * C), BF16),
            pltpu.VMEM((C, 2 * C), BF16),
            pltpu.VMEM((C, C), BF16),
            pltpu.VMEM((2 * C, C), BF16),
            pltpu.VMEM((C, LANES), F32),
            pltpu.VMEM((C, LANES), F32),
            pltpu.SemaphoreType.DMA((copies,)),
        ],
    )
    stats_got = exchange(stats, "seq")
    gskip = call(
        skip_grad_kernel,
        sds((C, C), BF16),
        "skip",
        (gated, d_skip),
        in_specs=[VM, VM],
        out_specs=VM,
        scratch_shapes=[pltpu.VMEM((C, cols), BF16)],
    )

    coef_out, dfilm, pooled, memory = call(
        functools.partial(stats_kernel, csh, heads, arows),
        (
            sds((seq, 4 * RP, 2 * csh), F32),
            sds((RP, 2 * csh), BF16),
            sds((RP, C), BF16),
            sds((RP, C), BF16),
        ),
        "segments",
        (block_ids, Got(stats_got), apack),
        after=("skip",),
        in_specs=[VM, VM, VM],
        out_specs=(VM, VM, VM, VM),
        scratch_shapes=[pltpu.VMEM((RP, C), F32)],
    )
    coef = Got(exchange(coef_out, "seq"))

    def gate_block(i):
        return jnp.minimum(i, steps - 1)

    def shard(i):
        return jnp.maximum(i - steps, 0)

    def gate_cols(height):
        return pl.BlockSpec((height, NR * LANES), lambda i, order: (0, gate_block(i)))

    gate_rows = pl.BlockSpec((NR, C, LANES), lambda i, order: (gate_block(i), 0, 0))
    wide1, wide2 = EARLY + 2 * LANES, 2 * C - EARLY

    def part(width):
        return sds((dp // 2, 4 * cs, width), BF16)

    def part_spec(width):
        return pl.BlockSpec((1, 4 * cs, width), lambda i, order: (shard(i) // 2, 0, 0))

    outs = call(
        functools.partial(backward_kernel, meta, dp, csh, steps),
        (
            sds((2 * C, cols), BF16),
            sds((C, cols), BF16),
            sds((2 * C, LANES), F32),
            part(wide1),
            part(wide2),
            part(wide1),
            part(wide2),
        ),
        "backward",
        (order, offsets, coef, mid, d_out, d_skip, factor_a, factor_b, inp, gated, gskip, flags, *turned),
        prefetch=1,
        grid=(steps + dp,),
        in_specs=[
            SM,
            pl.BlockSpec(
                (seq, 4 * RP, 2 * csh), lambda i, order: (0, 0, 0), pipeline_mode=pl.Buffered(1)
            ),
            gate_cols(C),
            gate_rows,
            gate_rows,
            gate_cols(C),
            gate_cols(C),
            pl.BlockSpec((4 * cs, cols), lambda i, order: (order[shard(i)], 0)),
            pl.BlockSpec((cs, cols), lambda i, order: (order[shard(i)], 0)),
            pl.BlockSpec((cs, C), lambda i, order: (order[shard(i)], 0)),
            SM,
        ]
        + [HB] * len(turned),
        out_specs=(
            gate_cols(2 * C),
            gate_cols(C),
            pl.BlockSpec((2 * C, LANES), lambda i, order: (0, 0)),
            part_spec(wide1),
            part_spec(wide2),
            part_spec(wide1),
            part_spec(wide2),
        ),
        scratch_shapes=[
            pltpu.VMEM((LANES, C), F32),
            pltpu.VMEM((C, LANES), F32),
            pltpu.VMEM((C, 2 * C), BF16),
            pltpu.VMEM((2 * C, NR * LANES), BF16),
            pltpu.VMEM((cols, 2 * C), BF16),
            pltpu.VMEM((cols, C), BF16),
            pltpu.SemaphoreType.DMA((copies,)),
        ],
    )
    dpre, dres, sums = outs[0:3]
    part1 = Reduction(call, "1", outs[3], outs[5], dp, seq, index)
    part2 = Reduction(call, "2", outs[4], outs[6], dp, seq, index)
    part1.over_blocks()
    keep, give = call(
        functools.partial(step_grad_kernel, meta, dp),
        (part(LANES), part(LANES)),
        "step_grad",
        (offsets, sums, embedding, *turned),
        after=("blocks_1",),
        in_specs=[SM, VM, VM] + [HB] * len(turned),
        out_specs=(VM, VM),
        scratch_shapes=[
            pltpu.VMEM((2 * C, 4 * C), BF16),
            pltpu.VMEM((C, C), F32),
            pltpu.SemaphoreType.DMA((copies,)),
        ],
    )
    part_step = Reduction(call, "step", keep, give, dp, seq, index)

    right_width = -(-(3 * wide + 3 * csh) // LANES) * LANES
    block = sds((dp // 2, cs, right_width), BF16)
    keep, give = call(
        functools.partial(attention_back_kernel, arows, csh, dp),
        (block, block),
        "attention_back",
        (offsets, prow, probs, u, qp, qkv, pooled, memory, dfilm, coef),
        after=("step_grad",),
        in_specs=[SM] + [VM] * 9,
        out_specs=(VM, VM),
        scratch_shapes=[
            pltpu.VMEM((heads * QUERIES, arows * prompt_all), F32),
            pltpu.VMEM((LANES, C), F32),
            pltpu.VMEM((LANES, right_width), F32),
            pltpu.VMEM((C, right_width), F32),
        ],
    )
    small = Reduction(call, "small", keep, give, dp, seq, index)
    part2.over_blocks(("attention_back",), (part_step,))
    small.over_blocks(("blocks_2",))
    part1.over_half(("blocks_small",))

    rest = 4 * cs // seq
    small_width = (cs // rest) * (wide + csh) + max(1, QUERIES // rest) * (wide // 2)
    part2.over_half(("half_1",))
    grad_film, attn_rows, mine, other = call(
        functools.partial(small_sum_kernel, csh, wide),
        (
            sds((2 * csh, cs), F32),
            sds((cs, csh), F32),
            sds((cs + QUERIES, wide), BF16),
            sds((cs + QUERIES, wide), BF16),
        ),
        "small_sum",
        (bit, small.keep, Got(small.got)),
        after=("half_2",),
        in_specs=[SM, VM, VM],
        out_specs=(VM,) * 4,
        scratch_shapes=[pltpu.VMEM((LANES, LANES), F32)],
    )
    partner = flipped(other, "seq", seq, 1)
    part1.over_pieces(("small_sum",))
    part2.over_pieces(("pieces_1",))
    small_piece = call(
        functools.partial(small_piece_kernel, csh, wide),
        sds((rest, small_width), BF16),
        "small_piece",
        (attn_rows, mine, Got(partner)),
        after=("pieces_2",),
        in_specs=[VM] * 3,
        out_specs=VM,
    )
    ones = part1.over_copies(("small_piece",))
    twos = part2.over_copies(("copies_1",), extra=small_piece)

    base, first, last = call(
        functools.partial(input_grad_kernel, meta, dp),
        (sds((C, cols), BF16), sds((C, LANES), BF16), sds((C, LANES), BF16)),
        "input_grad",
        (offsets, dpre, dres, *turned),
        after=("copies_2",),
        grid=(steps,),
        in_specs=[SM, col_block(2 * C), col_block(C)] + [HB] * len(turned),
        out_specs=(
            col_block(C),
            still((C, LANES)),
            still((C, LANES)),
        ),
        scratch_shapes=[
            pltpu.VMEM((2 * C, 4 * C), BF16),
            pltpu.VMEM((3, C, 2 * C), BF16),
            pltpu.VMEM((C, LANES), F32),
            pltpu.VMEM((C, LANES), F32),
            pltpu.SemaphoreType.DMA((copies,)),
        ],
    )
    from_left = lax.ppermute(last, "seq", up)
    from_right = lax.ppermute(first, "seq", down)
    grad_input, layer_out = call(
        functools.partial(finish_kernel, csh),
        (sds(x_in.shape, BF16), sds(x_in.shape, BF16)),
        "grad_input",
        (flags, base, Got(from_left), Got(from_right), mid, coef),
        after=(ones[1].array,),
        grid=(steps,),
        in_specs=[
            SM,
            col_block(C),
            whole((C, LANES)),
            whole((C, LANES)),
            col_block(C),
            whole((seq, 4 * RP, 2 * csh)),
        ],
        out_specs=(row_block, row_block),
        scratch_shapes=[pltpu.VMEM((LANES, C), F32), pltpu.VMEM((C, LANES), F32)],
    )

    (
        grad_step,
        grad_conv,
        grad_cond,
        grad_res,
        grad_skip,
        grad_queries,
        grad_query,
        grad_key,
        grad_value,
        grad_attn,
    ) = call(
        functools.partial(output_kernel, cs, csh, wide, seq),
        (
            sds((cs, C), F32),
            sds((3, cs, 2 * C), F32),
            sds((cs, 2 * C), F32),
            sds((cs, C), F32),
            sds((cs, C), F32),
            sds((QUERIES, cs), F32),
            sds((cs, C), F32),
            sds((cs, C), F32),
            sds((cs, C), F32),
            sds((cs, C), F32),
        ),
        "outputs",
        after=("grad_input",),
        args=(bit, *ones, *twos, queries, w_query),
        in_specs=[SM] + [VM] * 6,
        out_specs=(VM,) * 10,
        scratch_shapes=[
            pltpu.VMEM((4 * cs, wide1), F32),
            pltpu.VMEM((4 * cs, wide2 + LANES), F32),
            pltpu.VMEM((4 * cs, small_width), F32),
            pltpu.VMEM((LANES, LANES), F32),
            pltpu.VMEM((LANES, C), F32),
        ],
    )
    return (
        layer_out,
        skip_out,
        grad_input,
        grad_step,
        grad_conv,
        grad_cond,
        grad_res,
        grad_skip,
        grad_queries,
        grad_query,
        grad_key,
        grad_value,
        grad_attn,
        jnp.transpose(grad_film.reshape(2, csh, cs), (2, 0, 1)),
    )


def solution(mesh):
    frames = P("dp", None, "seq")
    matrix = P("dp", None)
    return jax.shard_map(
        functools.partial(body, mesh.shape["dp"], mesh.shape["seq"]),
        mesh=mesh,
        in_specs=(
            frames,
            frames,
            P("dp", None),
            P("dp"),
            P("dp", "seq", None),
            P("dp"),
            matrix,
            P(None, "dp", None),
            matrix,
            matrix,
            matrix,
            P(None, "dp"),
            matrix,
            matrix,
            matrix,
            matrix,
            frames,
            frames,
            frames,
        ),
        out_specs=(
            frames,
            frames,
            frames,
            matrix,
            P(None, "dp", None),
            matrix,
            matrix,
            matrix,
            P(None, "dp"),
            matrix,
            matrix,
            matrix,
            matrix,
            frames,
        ),
        check_vma=False,
    )
```

```python
import functools
import math

import jax
import jax.numpy as jnp
from jax import lax
from jax.experimental import pallas as pl
from jax.experimental.pallas import tpu as pltpu
from jax.sharding import PartitionSpec as P

C = 512
HEADS = 8
QUERIES = 32
HEAD_DIM = 64
SHIFT = 4
SQRT_HALF = 0.7071067811865476
NORM_EPS = 1e-05
MASKED_SCORE = -1e30
LANES = 128
RP = 16
NR = 4
EARLY = 640
F32 = jnp.float32
BF16 = jnp.bfloat16
VMEM_BYTES = 50 * 1024 * 1024


def nn(a, b):
    return lax.dot_general(a, b, (((1,), (0,)), ((), ())), preferred_element_type=F32)


def nt(a, b):
    return lax.dot_general(a, b, (((1,), (1,)), ((), ())), preferred_element_type=F32)


def parts(v, count):
    out = []
    for _ in range(count):
        low = v.astype(BF16).astype(F32)
        out.append(low)
        v = v - low
    return jnp.concatenate(out, axis=0).astype(BF16)


def fold(v, count):
    rows = v.shape[0] // count
    total = v[:rows]
    for k in range(1, count):
        total = total + v[k * rows : (k + 1) * rows]
    return total


def lane_ids(shape):
    return lax.broadcasted_iota(jnp.int32, shape, len(shape) - 1)


def sds(shape, dtype):
    return jax.ShapeDtypeStruct(shape, dtype)


VM = pl.BlockSpec(memory_space=pltpu.VMEM)
HB = pl.BlockSpec(memory_space=pl.ANY)
SM = pl.BlockSpec(memory_space=pltpu.SMEM)


def whole(shape):
    return pl.BlockSpec(shape, lambda i: (0,) * len(shape), pipeline_mode=pl.Buffered(1))


class Got:
    def __init__(self, array):
        self.array = array


class Caller:
    def __init__(self):
        self.done = {}

    def __call__(self, kernel, out_shape, name, args, flops=0, nbytes=0, prefetch=0, after=(), **kw):
        single = not isinstance(out_shape, tuple)
        shapes = (out_shape,) if single else out_shape
        specs = kw["out_specs"]
        specs = (specs,) if single else specs
        pinned = tuple(
            v if spec is SM else pltpu.HBM(v.shape, v.dtype) for v, spec in zip(shapes, specs)
        )
        in_specs = list(kw.pop("in_specs"))
        count = prefetch + len(in_specs)
        args = list(args)
        extra = len(after)
        for before in after:
            in_specs.append(HB)
            args.append(self.done[before] if isinstance(before, str) else before)

        def run(*refs):
            return kernel(*refs[:count], *refs[count + extra :])

        values = []
        for k, v in enumerate(args):
            spec = SM if k < prefetch else in_specs[k - prefetch]
            if isinstance(v, Got):
                values.append(v.array)
            elif spec is SM:
                values.append(v)
            else:
                values.append(pltpu.with_memory_space_constraint(v, pltpu.HBM))
        spec = pltpu.PrefetchScalarGridSpec(
            num_scalar_prefetch=prefetch,
            grid=kw.pop("grid", ()),
            in_specs=in_specs,
            out_specs=kw.pop("out_specs"),
            scratch_shapes=kw.pop("scratch_shapes", ()),
        )
        out = pl.pallas_call(
            run,
            out_shape=pinned[0] if single else pinned,
            name=name,
            grid_spec=spec,
            cost_estimate=pl.CostEstimate(
                flops=1, bytes_accessed=1, transcendentals=0
            ),
            compiler_params=pltpu.CompilerParams(vmem_limit_bytes=VMEM_BYTES),
        )(*values)
        self.done[name] = out if single else out[0]
        return out


def head_pack_kernel(
    csh,
    local,
    group_ref,
    bit_ref,
    attn_ref,
    film_ref,
    wq_ref,
    wk_ref,
    wv_ref,
    queries_ref,
    prompt_ref,
    out_ref,
    mine_ref,
    other_ref,
    scr,
):
    cs = attn_ref.shape[0]
    arows = mine_ref.shape[0]
    mine_ref[...] = prompt_ref[pl.ds(bit_ref[0] * arows, arows)]
    other_ref[...] = prompt_ref[pl.ds((1 - bit_ref[0]) * arows, arows)]
    out_ref[:, 0:C] = attn_ref[...]
    off = C
    scr[...] = jnp.zeros((2 * LANES, LANES), F32)
    scr[0 : 2 * csh, 0:cs] = film_ref[...].astype(F32)
    scr[LANES : LANES + QUERIES, 0:cs] = queries_ref[...].astype(F32)
    film = scr[0:LANES].T[0:cs]
    table = scr[LANES : 2 * LANES].T[0:cs]
    turn = lax.rem(C - local * group_ref[0], C)
    blocks = [film[:, 0 : 2 * csh]]
    for ref in (wq_ref, wk_ref, wv_ref):
        blocks.append(pltpu.roll(ref[...].astype(F32), turn, 1)[:, 0:local])
    blocks.append(table)
    for block in blocks:
        width = min(block.shape[1], out_ref.shape[1] - off)
        out_ref[:, off : off + width] = block[:, 0:width].astype(BF16)
        off += width
    if off < out_ref.shape[1]:
        out_ref[:, off:] = jnp.zeros((cs, out_ref.shape[1] - off), BF16)


SIDE = 480


def turned_pack_kernel(cs, bit_ref, conv_ref, cond_ref, res_ref, skip_ref, step_ref, out_ref, side_ref, middle_ref, scr):
    for k in range(3):
        scr[k * cs : (k + 1) * cs] = conv_ref[k]
    scr[3 * cs : 4 * cs] = cond_ref[...]
    turned = scr[...].T
    out_ref[0 : 2 * C - SIDE] = turned[0 : 2 * C - SIDE]
    at = 2 * C - SIDE
    for ref in (res_ref, skip_ref, step_ref):
        for lane in range(0, C, 4 * cs):
            out_ref[at : at + cs] = ref[:, lane : lane + 4 * cs]
            at += cs
    out_ref[at : at + SIDE] = turned[2 * C - SIDE :]
    middle_ref[...] = out_ref[SIDE:at]
    side_ref[...] = out_ref[pl.ds(pl.multiple_of(bit_ref[0] * at, 16), SIDE)]


def pair_kernel(a_ref, b_ref, out_ref):
    for p in range(out_ref.shape[0]):
        out_ref[p, 0] = a_ref[...]
        out_ref[p, 1] = b_ref[...]


def table_kernel(flags_ref, ids_ref, emb_ref, flags_out, ids_out, emb_out):
    for side in range(2):
        for r in range(flags_ref.shape[1]):
            flags_out[side, r] = flags_ref[side, r]
    ids_out[...] = ids_ref[...]
    emb_out[...] = emb_ref[...]


def edge_kernel(x_ref, first_ref, last_ref):
    rows = x_ref.shape[0]
    lane = lane_ids((C, LANES))
    first = jnp.zeros((C, LANES), F32)
    last = jnp.zeros((C, LANES), F32)
    for r in range(rows):
        v = x_ref[r].astype(F32)
        here = (lane // SHIFT) == r
        first = jnp.where(here, pltpu.roll(v, SHIFT * r, 1) if r else v, first)
        last = jnp.where(here, pltpu.roll(v, SHIFT * r + SHIFT, 1), last)
    first_ref[...] = first.astype(BF16)
    last_ref[...] = last.astype(BF16)


def begin(copies):
    for copy in copies:
        copy.start()


def finish(copies):
    for copy in copies:
        copy.wait()


def turned_copies(meta, refs, off_ref, cs, wt, others, sems):
    dp = len({k for k, _ in meta})
    pairs = []

    def conv(k, ref, first, row, rows):
        if wt is not None:
            lanes = pl.ds(pl.multiple_of(off_ref[k] * 4, LANES), 4 * cs)
            at = row if isinstance(row, int) else pl.multiple_of(row, 16)
            pairs.append((ref.at[pl.ds(first, rows)], wt.at[pl.ds(at, rows), lanes]))

    def rest(k, ref, at):
        row = pl.ds(pl.multiple_of(off_ref[k], 16), cs)
        for other in others:
            for lane in range(0, C, 4 * cs):
                if other is not None:
                    dst, start = other
                    pairs.append((ref.at[pl.ds(at, cs)], dst.at[row, pl.ds(start + lane, 4 * cs)]))
                at += cs

    inner = 2 * C - 2 * SIDE
    for (k, which), ref in zip(meta, refs):
        if which is None:
            conv(k, ref, 0, 0, SIDE + inner)
            rest(k, ref, SIDE + inner)
            conv(k, ref, ref.shape[0] - SIDE, 2 * C - SIDE, SIDE)
        elif which == 2:
            conv(k, ref, 0, SIDE, inner)
            rest(k, ref, inner)
        else:
            conv(k, ref, 0, off_ref[dp + which] * (2 * C - SIDE), SIDE)
    return [pltpu.make_async_copy(a, b, sems.at[n]) for n, (a, b) in enumerate(pairs)]


def head_copies(refs, off_ref, dst, sems):
    copies = []
    for k, ref in enumerate(refs):
        row = pl.ds(pl.multiple_of(off_ref[k], 16), ref.shape[0])
        copies.append(pltpu.make_async_copy(ref, dst.at[row], sems.at[k]))
    return copies


def forward_kernel(
    meta, dp, csh, off_ref, flags_ref, x_ref, cond_ref, dout_ref, left_ref, right_ref, emb_ref, pooled_ref, *refs
):
    turned, refs = refs[: len(meta)], refs[len(meta) :]
    (
        inp_ref,
        gated_ref,
        fa_ref,
        fb_ref,
        skip_ref,
        mid_ref,
        stats_ref,
        wt_ref,
        rn_ref,
        step_ref,
        rst_ref,
        lift_ref,
        acc_ref,
        sems,
    ) = refs
    cs = C // dp
    i = pl.program_id(0)
    lane = lane_ids((C, LANES))

    @pl.when(i == 0)
    def _():
        copies = turned_copies(
            meta,
            turned,
            off_ref,
            cs,
            wt_ref,
            ((rn_ref, 0), (rn_ref, C), (step_ref, 0)),
            sems,
        )
        begin(copies)
        acc_ref[...] = jnp.zeros((C, LANES), F32)
        finish(copies)
        lift = nn(emb_ref[0:RP], step_ref[...])
        lift = jnp.concatenate([lift, jnp.zeros((LANES - RP, C), F32)], axis=0)
        lift_ref[...] = lift.T
        rst_ref[...] = rn_ref[...].T

    lift = pltpu.roll(lift_ref[...], lax.rem(LANES - NR * i, LANES), 1)
    left = left_ref[...].astype(F32)
    right = right_ref[...].astype(F32)

    def put(tap, cols, value):
        for d in range(dp):
            at = d * 4 * cs + tap * cs
            inp_ref[at : at + cs, cols] = value[d * cs : (d + 1) * cs]

    for j in range(NR):
        r = NR * i + j
        lc = lift[:, j : j + 1]
        sh = (x_ref[j].astype(F32) + lc).astype(BF16)
        shf = sh.astype(F32)
        lh = pltpu.roll(left, lax.rem(LANES - SHIFT * r, LANES), 1)
        lh = jnp.where(flags_ref[0, r] > 0, (lh + lc).astype(BF16).astype(F32), 0.0)
        rh = pltpu.roll(right, LANES - SHIFT - SHIFT * r, 1)
        rh = jnp.where(flags_ref[1, r] > 0, (rh + lc).astype(BF16).astype(F32), 0.0)
        cols = slice(j * LANES, (j + 1) * LANES)
        put(0, cols, jnp.where(lane < SHIFT, lh, pltpu.roll(shf, SHIFT, 1)).astype(BF16))
        put(1, cols, sh)
        put(
            2,
            cols,
            jnp.where(lane >= LANES - SHIFT, rh, pltpu.roll(shf, LANES - SHIFT, 1)).astype(BF16),
        )
        put(3, cols, cond_ref[j])
    pre = nn(wt_ref[...], inp_ref[...])
    th = jnp.tanh(pre[:C])
    sg = jax.nn.sigmoid(pre[C:])
    gf = th * sg
    fa_ref[...] = (sg - gf * th).astype(BF16)
    fb_ref[...] = (gf * (1.0 - sg)).astype(BF16)
    g = gf.astype(BF16)
    gated_ref[...] = g
    rs = nn(rst_ref[...], g)
    acc = acc_ref[...]
    for j in range(NR):
        r = NR * i + j
        cols = slice(j * LANES, (j + 1) * LANES)
        skip_ref[j] = rs[C:, cols].astype(BF16)
        mid = ((x_ref[j].astype(F32) + rs[:C, cols]) * SQRT_HALF).astype(BF16)
        mid_ref[:, cols] = mid
        mf = mid.astype(F32)
        df = dout_ref[j].astype(F32)
        total = jnp.sum(mf, axis=1, keepdims=True)
        dev = mf - total * (1.0 / LANES)
        acc = jnp.where(lane == r, total, acc)
        acc = jnp.where(lane == RP + r, jnp.sum(dev * dev, axis=1, keepdims=True), acc)
        acc = jnp.where(lane == 2 * RP + r, jnp.sum(df, axis=1, keepdims=True), acc)
        acc = jnp.where(lane == 3 * RP + r, jnp.sum(df * dev, axis=1, keepdims=True), acc)
    acc_ref[...] = acc

    @pl.when(i == pl.num_programs(0) - 1)
    def _():
        t = acc.T
        for s in range(C // csh):
            cols = slice(s * csh, (s + 1) * csh)
            stats_ref[s, 0 : 2 * RP, 0:csh] = t[0 : 2 * RP, cols]
            stats_ref[s, 0 : 2 * RP, csh : 2 * csh] = t[2 * RP : 4 * RP, cols]
            stats_ref[s, 2 * RP : 3 * RP] = pooled_ref[:, 0 : 2 * csh]


def attention_kernel(dp, rows, heads, pairs, off, off_ref, bit_ref, len_ref, prompts, *refs):
    pieces, refs = refs[:dp], refs[dp:]
    apack_ref, prow, probs_ref, u_ref, pooled_ref, qp_ref, qkv_ref, abd, sems = refs
    copies = head_copies(pieces, off_ref, apack_ref, sems)
    count = len(copies)
    for j in range(pairs):
        for i in range(2):
            copies.append(
                pltpu.make_async_copy(
                    prompts.at[j, i], prow.at[:, 2 * j + i], sems.at[count + 2 * j + i]
                )
            )
    begin(copies)
    local = prow.shape[2]
    total = 2 * pairs * local
    abd[...] = jnp.zeros(abd.shape, F32)
    lane = lane_ids((heads * QUERIES, total))
    place = jnp.zeros((heads * QUERIES, total), jnp.int32)
    for k in range(2 * pairs):
        here = (k // 2) * 2 + (bit_ref[0] if k % 2 == 0 else 1 - bit_ref[0])
        place = jnp.where(lane // local == k, here * local + lane % local, place)
    finish(copies)
    wide = heads * HEAD_DIM
    qkv = apack_ref[:, off : off + qkv_ref.shape[0]].T
    qkv_ref[...] = qkv
    qp = nt(qkv[3 * wide : 3 * wide + QUERIES], qkv[0:wide])
    qp_ref[...] = qp
    st = []
    for g in range(heads):
        cols = slice(g * HEAD_DIM, (g + 1) * HEAD_DIM)
        st.append(fold(nn(parts(qp[:, cols], 3), qkv[wide + cols.start : wide + cols.stop]), 3))
    st = jnp.concatenate(st, axis=0) * (1.0 / math.sqrt(HEAD_DIM))
    table = prow[...].reshape(rows * total, C)
    scores = fold(nt(parts(st, 3), table), 3)
    for r in range(rows):
        cols = slice(r * total, (r + 1) * total)
        live = place < len_ref[r]
        s = jnp.where(live, scores[:, cols], MASKED_SCORE)
        e = jnp.where(live, jnp.exp(s - jnp.max(s, axis=1, keepdims=True)), 0.0)
        p = e / jnp.sum(e, axis=1, keepdims=True)
        probs_ref[:, cols] = p
        for g in range(heads):
            abd[8 * g + r : 8 * g + r + 1, cols] = jnp.sum(
                p[g * QUERIES : (g + 1) * QUERIES], axis=0, keepdims=True
            )
    u = fold(nn(parts(abd[...], 2), table), 2)
    u_ref[...] = u
    pooled_ref[...] = jnp.zeros(pooled_ref.shape, F32)
    for g in range(heads):
        first = 2 * wide + g * HEAD_DIM
        v = parts(u[8 * g : 8 * g + 8] * (1.0 / QUERIES), 2)
        pooled_ref[0:8, g * HEAD_DIM : (g + 1) * HEAD_DIM] = fold(
            nt(v, qkv[first : first + HEAD_DIM]), 2
        )


def stats_kernel(
    csh, heads, rows, seg_ref, x_ref, apack_ref, out_ref, dfilm_ref, pooled_ref, memory_ref, scratch
):
    count = x_ref.shape[0]
    wide = heads * HEAD_DIM
    seg = seg_ref[...]
    scratch[...] = jnp.zeros(scratch.shape, F32)
    for s in range(count):
        group, part = s // 2, s % 2
        scratch[part * rows : (part + 1) * rows, group * wide : (group + 1) * wide] = x_ref[
            s, 2 * RP : 2 * RP + rows, 0:wide
        ]
    pooled = scratch[...].astype(BF16)
    pooled_ref[...] = pooled
    memory = nn(pooled, apack_ref[:, 0:C]).astype(BF16)
    memory_ref[...] = memory
    film = nn(memory, apack_ref[:, C : C + 2 * csh])
    f0 = film[:, 0:csh]
    f1 = film[:, csh : 2 * csh]
    total = [x_ref[s, 0:RP, 0:csh] for s in range(count)]
    second = [x_ref[s, RP : 2 * RP, 0:csh] for s in range(count)]
    dsum = [x_ref[s, 0:RP, csh : 2 * csh] for s in range(count)]
    cross = [x_ref[s, RP : 2 * RP, csh : 2 * csh] for s in range(count)]
    means = [v * (1.0 / LANES) for v in total]
    d0 = jnp.zeros((RP, csh), F32)
    d1 = jnp.zeros((RP, csh), F32)
    for me in range(count):
        same = [(seg[:, s : s + 1] == seg[:, me : me + 1]).astype(F32) for s in range(count)]
        frames = sum(same) * float(LANES)
        inv = 1.0 / frames
        mean = sum(m * v for m, v in zip(same, total)) * inv
        var = (
            sum(
                m * (v + float(LANES) * (u - mean) * (u - mean))
                for m, v, u in zip(same, second, means)
            )
            * inv
        )
        scale = lax.rsqrt(var + NORM_EPS)
        dtot = sum(m * v for m, v in zip(same, dsum))
        xtot = sum(m * (v + (u - mean) * d) for m, v, u, d in zip(same, cross, means, dsum)) * scale
        mean_part = f0 * dtot * inv
        cross_part = f0 * xtot * inv
        slope = scale * scale * cross_part
        out_ref[me, 0:RP, 0:csh] = 1.0 + f0 * scale
        out_ref[me, RP : 2 * RP, 0:csh] = f1 - f0 * scale * mean
        out_ref[me, 0:RP, csh : 2 * csh] = -slope
        out_ref[me, RP : 2 * RP, csh : 2 * csh] = slope * mean - scale * mean_part
        d0 = d0 + (cross[me] + (means[me] - mean) * dsum[me]) * scale
        d1 = d1 + dsum[me]
    dfilm = jnp.concatenate([d0, d1], axis=1).astype(BF16)
    dfilm_ref[...] = dfilm
    dmem = nt(dfilm, apack_ref[:, C : C + 2 * csh])
    dpool = nt(dmem.astype(BF16), apack_ref[:, 0:C])
    for s in range(count):
        group, part = s // 2, s % 2
        rolled = pltpu.roll(dpool, RP - part * rows, 0) if part else dpool
        out_ref[s, 2 * RP : 3 * RP, 0:csh] = dmem[:, s * csh : (s + 1) * csh]
        out_ref[s, 2 * RP : 3 * RP, csh : 2 * csh] = jnp.zeros((RP, csh), F32)
        out_ref[s, 3 * RP : 4 * RP] = rolled[:, group * wide : (group + 1) * wide]


def coef_columns(csh, coef_ref, rows_ref, cols_ref):
    rows_ref[...] = jnp.zeros(rows_ref.shape, F32)
    for s in range(C // csh):
        cols = slice(s * csh, (s + 1) * csh)
        rows_ref[0 : 2 * RP, cols] = coef_ref[s, 0 : 2 * RP, 0:csh]
        rows_ref[2 * RP : 4 * RP, cols] = coef_ref[s, 0 : 2 * RP, csh : 2 * csh]
    cols_ref[...] = rows_ref[...].T


def skip_grad_kernel(gated_ref, dskip_ref, out_ref, right):
    for r in range(dskip_ref.shape[0]):
        right[:, r * LANES : (r + 1) * LANES] = dskip_ref[r]
    out_ref[...] = nt(gated_ref[...], right[...]).astype(BF16)


def backward_kernel(meta, dp, csh, gates, order_ref, off_ref, coef_ref, mid_ref, dout_ref, dskip_ref, fa_ref, fb_ref, inp_ref, gated_ref, gskip_ref, flags_ref, *refs):
    turned, refs = refs[: len(meta)], refs[len(meta) :]
    dpre_ref, dres_ref, sums_ref, refs = refs[0], refs[1], refs[2], refs[3:]
    outs, refs = (refs[0:2], refs[2:4]), refs[4:]
    rows_ref, cols_ref, w_ref, both_ref, dpt_ref, drt_ref, sems = refs
    cs = C // dp
    span = NR * LANES
    i = pl.program_id(0)

    @pl.when(i == 0)
    def _():
        copies = turned_copies(
            meta, turned, off_ref, cs, None, ((w_ref, 0), (w_ref, C), None), sems
        )
        begin(copies)
        coef_columns(csh, coef_ref, rows_ref, cols_ref)
        sums_ref[...] = jnp.zeros(sums_ref.shape, F32)
        finish(copies)

    @pl.when(i < gates)
    def _():
        coef = pltpu.roll(cols_ref[...], lax.rem(LANES - NR * i, LANES), 1)
        for j in range(NR):
            cols = slice(j * LANES, (j + 1) * LANES)
            mf = mid_ref[:, cols].astype(F32)
            df = dout_ref[j].astype(F32)
            a = coef[:, j : j + 1]
            be = coef[:, 2 * RP + j : 2 * RP + j + 1]
            ga = coef[:, 3 * RP + j : 3 * RP + j + 1]
            dmid = (a * df + (be * mf + ga)).astype(BF16).astype(F32)
            both_ref[0:C, cols] = (dmid * SQRT_HALF).astype(BF16)
            both_ref[C : 2 * C, cols] = dskip_ref[j]
        dres = both_ref[0:C]
        dres_ref[...] = dres
        dg = nn(w_ref[...], both_ref[...])
        dt = (dg * fa_ref[...].astype(F32)).astype(BF16)
        ds = (dg * fb_ref[...].astype(F32)).astype(BF16)
        dpre_ref[0:C] = dt
        dpre_ref[C : 2 * C] = ds
        at = pl.ds(pl.multiple_of(i * span, span), span)
        dpt_ref[at, 0:C] = dt.T
        dpt_ref[at, C : 2 * C] = ds.T
        drt_ref[at] = dres.T
        frame = lax.broadcasted_iota(jnp.int32, (span, LANES), 0)
        column = lane_ids((span, LANES))
        place = frame % LANES
        which = frame // LANES
        keep_l = jnp.zeros((span, LANES), jnp.int32)
        keep_r = jnp.zeros((span, LANES), jnp.int32)
        for j in range(NR):
            keep_l = jnp.where(which == j, flags_ref[0, NR * i + j], keep_l)
            keep_r = jnp.where(which == j, flags_ref[1, NR * i + j], keep_r)
        row = NR * i + which
        use0 = (column == row) & ((place >= SHIFT) | (keep_l > 0))
        use1 = column == RP + row
        use2 = (column == 2 * RP + row) & ((place < LANES - SHIFT) | (keep_r > 0))
        pick = jnp.where(use0 | use1 | use2, 1.0, 0.0).astype(BF16)
        sums_ref[...] = sums_ref[...] + nn(dpre_ref[...], pick)

    @pl.when(i >= gates)
    def _():
        g = nn(inp_ref[...], dpt_ref[...]).astype(BF16)
        h = nn(gated_ref[...], drt_ref[...]).astype(BF16)
        k = i - gates
        for parity, (one, two) in enumerate(outs):

            @pl.when(lax.rem(k, 2) == parity)
            def _():
                for t in range(4):
                    rows = slice(t * cs, (t + 1) * cs)
                    lanes = slice(t * LANES, (t + 1) * LANES)
                    one[0, rows, 0:LANES] = h[:, lanes]
                    one[0, rows, LANES : 2 * LANES] = gskip_ref[:, lanes]
                one[0, :, 2 * LANES :] = g[:, 0:EARLY]
                two[0] = g[:, EARLY:]


def step_grad_kernel(meta, dp, off_ref, sums_ref, emb_ref, *refs):
    turned, refs = refs[: len(meta)], refs[len(meta) :]
    keep_ref, give_ref, wt_ref, scr, sems = refs
    cs = C // dp
    copies = turned_copies(meta, turned, off_ref, cs, wt_ref, (None,) * 3, sems)
    begin(copies)
    sums = sums_ref[...].T
    emb = emb_ref[...].T
    finish(copies)
    total = jnp.zeros((RP, 4 * C), F32)
    lane = lane_ids((RP, 4 * C))
    all_taps = fold(nn(parts(sums[0 : 3 * RP], 2), wt_ref[...]), 2)
    for t in range(3):
        g = all_taps[t * RP : (t + 1) * RP]
        total = total + jnp.where((lane // cs) % 4 == t, g, 0.0)
    out = []
    for d in range(dp):
        block = total[:, d * 4 * cs : (d + 1) * 4 * cs]
        out.append(block[:, 0:cs] + block[:, cs : 2 * cs] + block[:, 2 * cs : 3 * cs])
    g = jnp.concatenate(out, axis=1)
    g = jnp.concatenate([g, jnp.zeros((LANES - RP, C), F32)], axis=0)
    hi = g.astype(BF16)
    lo = (g - hi.astype(F32)).astype(BF16)
    scr[...] = nn(emb, hi) + nn(emb, lo)
    for k in range(dp):
        v = scr[pl.ds(pl.multiple_of(off_ref[k], 16), cs)].astype(BF16)
        for t in range(4):
            (keep_ref, give_ref)[k % 2][k // 2, t * cs : (t + 1) * cs] = v[
                :, t * LANES : (t + 1) * LANES
            ]


def input_grad_kernel(meta, dp, off_ref, dpre_ref, dres_ref, *refs):
    turned, refs = refs[: len(meta)], refs[len(meta) :]
    base_ref, first_ref, last_ref, wt_ref, w_ref, facc_ref, lacc_ref, sems = refs
    cs = C // dp
    i = pl.program_id(0)
    lane = lane_ids((C, LANES))

    @pl.when(i == 0)
    def _():
        copies = turned_copies(meta, turned, off_ref, cs, wt_ref, (None,) * 3, sems)
        begin(copies)
        facc_ref[...] = jnp.zeros((C, LANES), F32)
        lacc_ref[...] = jnp.zeros((C, LANES), F32)
        finish(copies)
        for d in range(dp):
            v = wt_ref[:, d * 4 * cs : (d + 1) * 4 * cs].T
            for t in range(3):
                w_ref[t, d * cs : (d + 1) * cs] = v[t * cs : (t + 1) * cs]

    dpre = dpre_ref[...]
    y0 = nn(w_ref[0], dpre)
    y1 = nn(w_ref[1], dpre)
    y2 = nn(w_ref[2], dpre)
    facc = facc_ref[...]
    lacc = lacc_ref[...]
    for j in range(NR):
        r = NR * i + j
        cols = slice(j * LANES, (j + 1) * LANES)
        z0 = pltpu.roll(y0[:, cols], LANES - SHIFT, 1)
        z2 = pltpu.roll(y2[:, cols], SHIFT, 1)
        inner0 = lane < LANES - SHIFT
        inner2 = lane >= SHIFT
        v = y1[:, cols]
        base_ref[:, cols] = (
            v
            + jnp.where(inner0, z0, 0.0)
            + jnp.where(inner2, z2, 0.0)
            + dres_ref[:, cols].astype(F32)
        ).astype(BF16)
        here = (lane // SHIFT) == r
        facc = jnp.where(here, pltpu.roll(z0, lax.rem(SHIFT * r + SHIFT, LANES), 1), facc)
        lacc = jnp.where(here, pltpu.roll(z2, SHIFT * r, 1), lacc)
    facc_ref[...] = facc
    lacc_ref[...] = lacc

    @pl.when(i == pl.num_programs(0) - 1)
    def _():
        first_ref[...] = facc.astype(BF16)
        last_ref[...] = lacc.astype(BF16)


def finish_kernel(csh, flags_ref, base_ref, left_ref, right_ref, mid_ref, coef_ref, out_ref, layer_ref, rows_ref, cols_ref):
    i = pl.program_id(0)
    lane = lane_ids((C, LANES))

    @pl.when(i == 0)
    def _():
        coef_columns(csh, coef_ref, rows_ref, cols_ref)

    coef = pltpu.roll(cols_ref[...], lax.rem(LANES - NR * i, LANES), 1)
    left = left_ref[...].astype(F32)
    right = right_ref[...].astype(F32)
    for j in range(NR):
        r = NR * i + j
        cols = slice(j * LANES, (j + 1) * LANES)
        lh = pltpu.roll(left, lax.rem(LANES - SHIFT * r, LANES), 1)
        rh = pltpu.roll(right, LANES - SHIFT - SHIFT * r, 1)
        lh = jnp.where((lane < SHIFT) & (flags_ref[0, r] > 0), lh, 0.0)
        rh = jnp.where((lane >= LANES - SHIFT) & (flags_ref[1, r] > 0), rh, 0.0)
        out_ref[j] = (base_ref[:, cols].astype(F32) + lh + rh).astype(BF16)
        a = coef[:, j : j + 1]
        b = coef[:, RP + j : RP + j + 1]
        layer_ref[j] = (a * mid_ref[:, cols].astype(F32) + b).astype(BF16)


def add_blocks_kernel(count, *refs):
    ins, (keep_ref, give_ref) = refs[: 2 * count], refs[2 * count :]
    at = 0
    for p in range(count):
        a_ref, b_ref = ins[2 * p : 2 * p + 2]
        width = a_ref.shape[2]
        for j in range(a_ref.shape[0]):
            v = a_ref[j].astype(F32) + b_ref[j].astype(F32)
            (keep_ref, give_ref)[j % 2][j // 2, :, at : at + width] = v.astype(BF16)
        at += width


def add_halves_kernel(bit, index_ref, a_ref, b_ref, keep_ref, give_ref, scr):
    half = a_ref.shape[0] // 2
    mine = lax.rem(index_ref[0] // bit, 2)
    scr[...] = a_ref[...].astype(F32) + b_ref[...].astype(F32)
    keep_ref[...] = scr[pl.ds(pl.multiple_of(mine * half, 8), half)].astype(BF16)
    give_ref[...] = scr[pl.ds(pl.multiple_of((1 - mine) * half, 8), half)].astype(BF16)


def add_pieces_kernel(a_ref, b_ref, out_ref):
    v = a_ref[...].astype(F32) + b_ref[...].astype(F32)
    size = out_ref.shape[1]
    for p in range(out_ref.shape[0]):
        out_ref[p] = v[p * size : (p + 1) * size].astype(BF16)


def sum_copies_kernel(a_ref, *refs):
    out_ref = refs[-1]
    v = a_ref[0].astype(F32)
    for p in range(1, a_ref.shape[0]):
        v = v + a_ref[p].astype(F32)
    v = v.astype(BF16)
    for p in range(out_ref.shape[0]):
        out_ref[p, :, 0 : v.shape[1]] = v
        if len(refs) > 1:
            out_ref[p, :, v.shape[1] :] = refs[0][...]


def small_sum_kernel(csh, wide, bit_ref, keep_ref, got_ref, film_ref, attn_ref, mine_ref, other_ref, turn):
    v = keep_ref[0].astype(F32) + got_ref[0].astype(F32)
    cs = v.shape[0]
    film = 2 * wide + csh
    turn[...] = jnp.zeros(turn.shape, F32)
    turn[0:cs, 0 : 2 * csh] = v[:, film : film + 2 * csh]
    film_ref[...] = turn[...].T[0 : 2 * csh, 0:cs]
    attn_ref[...] = v[:, 2 * wide : film]
    last = film + 2 * csh
    even = bit_ref[0] == 0
    for one, two, rows, width in (
        (v[:, 0:wide], v[:, wide : 2 * wide], slice(0, cs), wide),
        (
            v[0:QUERIES, last : last + wide // 2],
            v[0:QUERIES, last + wide // 2 : last + wide],
            slice(cs, cs + QUERIES),
            wide // 2,
        ),
    ):
        mine_ref[rows, 0:width] = jnp.where(even, one, two).astype(BF16)
        other_ref[rows, 0:width] = jnp.where(even, two, one).astype(BF16)
    mine_ref[cs:, wide // 2 :] = jnp.zeros((QUERIES, wide // 2), BF16)
    other_ref[cs:, wide // 2 :] = jnp.zeros((QUERIES, wide // 2), BF16)


def small_piece_kernel(csh, wide, attn_ref, mine_ref, got_ref, out_ref):
    v = mine_ref[...].astype(F32) + got_ref[...].astype(F32)
    attn = attn_ref[...]
    cs = attn.shape[0]
    rows = out_ref.shape[0]
    at = 0
    for row in range(0, cs, rows):
        out_ref[:, at : at + wide] = v[row : row + rows].astype(BF16)
        out_ref[:, at + wide : at + wide + csh] = attn[row : row + rows].astype(BF16)
        at += wide + csh
    for row in range(0, QUERIES, rows):
        block = v[cs + row : cs + min(row + rows, QUERIES), 0 : wide // 2]
        if block.shape[0] < rows:
            pad = jnp.zeros((rows - block.shape[0], wide // 2), F32)
            block = jnp.concatenate([block, pad], axis=0)
        out_ref[:, at : at + wide // 2] = block.astype(BF16)
        at += wide // 2


def output_kernel(
    cs,
    csh,
    wide,
    seq,
    bit_ref,
    *refs,
):
    own1, got1, all2, refs = *refs[:3], refs[3:]
    (
        queries_ref,
        wq_ref,
        step_ref,
        conv_ref,
        cond_ref,
        res_ref,
        skip_ref,
        gqueries_ref,
        gquery_ref,
        key_ref,
        value_ref,
        attn_ref,
        scr1,
        scr2,
        small,
        qscr,
        dq,
    ) = refs
    count, size = own1.shape[0], own1.shape[1]
    wide2 = scr2.shape[1]
    bit = bit_ref[0]
    for one, side in ((own1, bit), (got1, 1 - bit)):
        for p in range(count):
            rows = pl.ds(pl.multiple_of((side * count + p) * size, 8), size)
            scr1[rows] = one[p].astype(F32)
    for s in range(seq):
        at = ((s % 2) * count + s // 2) * size
        v = all2[s].astype(F32)
        scr2[at : at + size] = v[:, 0:wide2]
        small[s * size : (s + 1) * size] = v[:, wide2:]
    for t in range(4):
        rows = slice(t * cs, (t + 1) * cs)
        lanes = slice(t * LANES, (t + 1) * LANES)
        res_ref[:, lanes] = scr1[rows, 0:LANES]
        skip_ref[:, lanes] = scr1[rows, LANES : 2 * LANES]
        rest = 2 * C - EARLY
        step_ref[:, lanes] = scr2[rows, rest : rest + LANES]
        if t < 3:
            conv_ref[t, :, 0:EARLY] = scr1[rows, 2 * LANES : 2 * LANES + EARLY]
            conv_ref[t, :, EARLY:] = scr2[rows, 0:rest]
        else:
            cond_ref[:, 0:EARLY] = scr1[rows, 2 * LANES : 2 * LANES + EARLY]
            cond_ref[:, EARLY:] = scr2[rows, 0:rest]
    dq[...] = jnp.zeros(dq.shape, F32)
    for s in range(seq):
        v = small[s * size : (s + 1) * size]
        group, even = s // 2, s % 2 == 0
        out = key_ref if even else value_ref
        at = 0
        for row in range(0, cs, size):
            out[row : row + size, group * wide : (group + 1) * wide] = v[:, at : at + wide]
            attn_ref[row : row + size, s * csh : (s + 1) * csh] = v[:, at + wide : at + wide + csh]
            at += wide + csh
        first = group * wide + (0 if even else wide // 2)
        for row in range(0, QUERIES, size):
            count = min(size, QUERIES - row)
            dq[row : row + count, first : first + wide // 2] = v[0:count, at : at + wide // 2]
            at += wide // 2
    qscr[...] = jnp.zeros((LANES, LANES), F32)
    qscr[0:QUERIES, 0:cs] = queries_ref[...].astype(F32)
    qt = qscr[...].T.astype(BF16)
    d = dq[...]
    hi = d.astype(BF16)
    lo = (d - hi.astype(F32)).astype(BF16)
    gquery_ref[...] = (nn(qt, hi) + nn(qt, lo))[0:cs]
    gqueries_ref[...] = fold(nt(parts(d[0:QUERIES], 2), wq_ref[...]), 2)


def attention_back_kernel(
    rows,
    csh,
    dp,
    off_ref,
    prow,
    probs_ref,
    u_ref,
    qp_ref,
    qkv_ref,
    pooled_ref,
    memory_ref,
    dfilm_ref,
    got_ref,
    keep_ref,
    give_ref,
    ds,
    stack,
    right,
    out,
):
    count = got_ref.shape[0]
    total = prow.shape[1] * prow.shape[2]
    cs = C // dp
    table = prow[...].reshape(rows * total, C)
    wide = qp_ref.shape[1]
    heads = wide // HEAD_DIM
    datt = got_ref[0, 3 * RP : 4 * RP, 0:wide]
    dmem = got_ref[0, 2 * RP : 3 * RP, 0:csh]
    for s in range(1, count):
        datt = datt + got_ref[s, 3 * RP : 4 * RP, 0:wide]
        dmem = dmem + got_ref[s, 2 * RP : 3 * RP, 0:csh]
    datt = datt[0:8] * (1.0 / QUERIES)
    vh = []
    for g in range(heads):
        first = 2 * wide + g * HEAD_DIM
        v = parts(datt[:, g * HEAD_DIM : (g + 1) * HEAD_DIM], 2)
        vh.append(fold(nn(v, qkv_ref[first : first + HEAD_DIM]), 2))
    vh = jnp.concatenate(vh, axis=0)
    dp_all = fold(nt(parts(vh, 2), table), 2)
    for r in range(rows):
        cols = slice(r * total, (r + 1) * total)
        for g in range(heads):
            mine = slice(g * QUERIES, (g + 1) * QUERIES)
            p = probs_ref[mine, cols]
            dpr = dp_all[8 * g + r : 8 * g + r + 1, cols]
            inner = jnp.sum(p * dpr, axis=1, keepdims=True)
            ds[mine, cols] = p * (dpr - inner)
    tt = fold(nn(parts(ds[...], 2), table), 2)
    scale = 1.0 / math.sqrt(HEAD_DIM)
    dq = []
    stack[...] = jnp.zeros(stack.shape, F32)
    right[...] = jnp.zeros(right.shape, F32)
    stack[0 : heads * QUERIES] = tt
    stack[64:80] = u_ref[...]
    stack[80:96] = pooled_ref[...].astype(F32)
    stack[96:112] = memory_ref[...].astype(F32)
    for g in range(heads):
        cols = slice(g * HEAD_DIM, (g + 1) * HEAD_DIM)
        mine = slice(g * QUERIES, (g + 1) * QUERIES)
        wk = qkv_ref[wide + g * HEAD_DIM : wide + (g + 1) * HEAD_DIM]
        dq.append(fold(nt(parts(tt[mine], 2), wk), 2) * scale)
        right[mine, cols] = qp_ref[:, cols] * scale
        right[64 + 8 * g : 72 + 8 * g, wide + cols.start : wide + cols.stop] = datt[:, cols]
    right[80:96, 2 * wide : 2 * wide + csh] = dmem
    right[96:112, 2 * wide + csh : 2 * wide + 3 * csh] = dfilm_ref[...].astype(F32)
    out[...] = lax.dot_general(
        stack[...].T,
        right[...],
        (((1,), (0,)), ((), ())),
        precision=lax.Precision.HIGHEST,
        preferred_element_type=F32,
    )
    last = 2 * wide + 3 * csh
    for k in range(dp):
        ref = (keep_ref, give_ref)[k % 2]
        ref[k // 2] = out[pl.ds(pl.multiple_of(off_ref[k], 16), cs)].astype(BF16)
        for g in range(heads):
            first = last + g * HEAD_DIM
            ref[k // 2, 0:QUERIES, first : first + HEAD_DIM] = dq[g].astype(BF16)


def exchange(pieces, axis, groups=None):
    return lax.all_to_all(
        pieces, axis, split_axis=0, concat_axis=0, axis_index_groups=groups, tiled=True
    )


def flipped(v, axis, size, bit):
    return lax.ppermute(v, axis, [(d, d ^ bit) for d in range(size)])


class Reduction:
    def __init__(self, call, name, keep, give, dp, seq, index):
        self.call, self.name, self.dp, self.seq, self.index = call, name, dp, seq, index
        self.keep, self.flip = keep, 1
        self.got = flipped(give, "dp", dp, 1)

    def over_blocks(self, after=(), others=()):
        while 2 * self.flip < self.dp:
            group = (self,) + tuple(others)
            others = ()
            args = []
            for part in group:
                args += [part.keep, Got(part.got)]
            width = sum(part.keep.shape[2] for part in group)
            half = sds((self.keep.shape[0] // 2, self.keep.shape[1], width), BF16)
            self.keep, give = self.call(
                functools.partial(add_blocks_kernel, len(group)),
                (half, half),
                "blocks_" + self.name,
                args,
                after=after,
                in_specs=[VM] * len(args),
                out_specs=(VM, VM),
            )
            self.flip *= 2
            self.got = flipped(give, "dp", self.dp, self.flip)
        self.rest = self.keep.shape[1:]

    def over_half(self, after=()):
        rows, width = self.rest
        half = sds((rows // 2, width), BF16)
        self.keep, give = self.call(
            functools.partial(add_halves_kernel, 1),
            (half, half),
            "half_" + self.name,
            (self.index, self.keep.reshape(rows, width), Got(self.got.reshape(rows, width))),
            after=after,
            in_specs=[SM, VM, VM],
            out_specs=(VM, VM),
            scratch_shapes=[pltpu.VMEM((rows, width), F32)],
        )
        self.got = flipped(give, "seq", self.seq, 1)

    def over_pieces(self, after=()):
        rows, width = self.rest
        count = self.seq // 2
        self.groups = [[2 * k + b for k in range(count)] for b in range(2)]
        pieces = self.call(
            add_pieces_kernel,
            sds((count, rows // self.seq, width), BF16),
            "pieces_" + self.name,
            (self.keep, Got(self.got)),
            after=after,
            in_specs=[VM, VM],
            out_specs=VM,
        )
        self.got = exchange(pieces, "seq", self.groups)

    def over_copies(self, after=(), extra=None):
        args, (count, rows, width) = [Got(self.got)], self.got.shape
        if extra is not None:
            count = self.seq
        if extra is not None:
            args.append(extra)
            width += extra.shape[1]
        copies = self.call(
            sum_copies_kernel,
            sds((count, rows, width), BF16),
            "copies_" + self.name,
            args,
            after=after,
            in_specs=[VM] * len(args),
            out_specs=VM,
        )
        if extra is not None:
            return (Got(exchange(copies, "seq")),)
        own = exchange(copies, "seq", self.groups)
        return Got(own), Got(flipped(own, "seq", self.seq, 1))


def body(
    dp,
    seq,
    x_in,
    cond,
    segment_ids,
    diffusion_steps,
    prompt,
    prompt_lengths,
    w_step,
    w_conv,
    w_cond,
    w_res,
    w_skip,
    queries,
    w_query,
    w_key,
    w_value,
    w_attn_out,
    w_film,
    d_out,
    d_skip,
):
    call = Caller()
    rows = x_in.shape[0]
    frames = x_in.shape[2]
    steps = rows // NR
    cols = rows * frames
    cs = C // dp
    csh = C // seq
    heads = 2 * HEADS // seq
    wide = heads * HEAD_DIM
    arows = rows // 2
    pl_local = prompt.shape[1]
    prompt_all = pl_local * seq
    sidx = lax.axis_index("seq")
    didx = lax.axis_index("dp")
    group = (sidx // 2).astype(jnp.int32).reshape(1)
    bit = (sidx % 2).astype(jnp.int32).reshape(1)
    up = [(i, i + 1) for i in range(seq - 1)]
    down = [(i + 1, i) for i in range(seq - 1)]
    order = jnp.bitwise_xor(didx, jnp.arange(dp, dtype=jnp.int32)).astype(jnp.int32)
    offsets = jnp.concatenate([order * cs, bit, 1 - bit])
    index = sidx.astype(jnp.int32).reshape(1)

    def gather(pack, side=None, middle=None):
        if dp == 4 and side is not None:
            mine = flipped(side, "dp", dp, 2)
            inner = flipped(middle, "dp", dp, 2)
            other = flipped(mine, "seq", seq, 1)
            near = [(0, None, pack), (2, 0, mine), (2, 2, inner), (2, 1, other)]
            pieces = near + [(k + 1, h, flipped(v, "dp", dp, 1)) for k, h, v in near]
        else:
            pieces = [(0, None, pack)]
            flip = dp // 2
            while flip:
                pieces += [(k + flip, h, flipped(v, "dp", dp, flip)) for k, h, v in pieces]
                flip //= 2
        pieces.sort(key=lambda piece: piece[0])
        meta = [(k, h) for k, h, _ in pieces]
        return meta, [v if k == 0 else Got(v) for k, _, v in pieces]

    off_qkv = C + 2 * csh
    qkv_rows = -(-(3 * wide + QUERIES) // LANES) * LANES
    head_width = -(-(off_qkv + qkv_rows) // LANES) * LANES
    middle = 2 * C - 2 * SIDE + 3 * C // 4
    pack, side, middle = call(
        functools.partial(turned_pack_kernel, cs),
        (
            sds((2 * SIDE + middle, 4 * cs), BF16),
            sds((SIDE, 4 * cs), BF16),
            sds((middle, 4 * cs), BF16),
        ),
        "turned_pack",
        (bit, w_conv, w_cond, w_res, w_skip, w_step),
        in_specs=[SM] + [VM] * 5,
        out_specs=(VM, VM, VM),
        scratch_shapes=[pltpu.VMEM((4 * cs, 2 * C), BF16)],
    )
    meta, turned = gather(pack, side, middle)
    copies = 4 * dp * (1 + 3 * C // (4 * cs))
    pack, mine, other = call(
        functools.partial(head_pack_kernel, csh, wide),
        (
            sds((cs, head_width), BF16),
            sds((arows, pl_local, C), BF16),
            sds((arows, pl_local, C), BF16),
        ),
        "head_pack",
        (
            group,
            bit,
            w_attn_out,
            jnp.transpose(w_film, (1, 2, 0)).reshape(2 * csh, cs),
            w_query,
            w_key,
            w_value,
            queries,
            prompt,
        ),
        after=("turned_pack",),
        in_specs=[SM, SM] + [VM] * 7,
        out_specs=(VM,) * 3,
        scratch_shapes=[pltpu.VMEM((2 * LANES, LANES), F32)],
    )
    _, head_pieces = gather(pack)
    partner = flipped(other, "seq", seq, 1)
    pair = call(
        pair_kernel,
        sds((seq // 2, 2, arows, pl_local, C), BF16),
        "pair",
        (mine, Got(partner)),
        in_specs=[VM, VM],
        out_specs=VM,
    )
    first, last = call(
        edge_kernel,
        (sds((C, LANES), BF16), sds((C, LANES), BF16)),
        "edges",
        (x_in,),
        after=("pair", head_pieces[dp // 2].array),
        in_specs=[VM],
        out_specs=(VM, VM),
    )
    z_groups = [[2 * k + b for k in range(seq // 2)] for b in range(2)]
    prompts = Got(exchange(pair, "seq", z_groups))
    block_ids = segment_ids[:, ::frames]
    padded_ids = jnp.pad(block_ids, ((0, 0), (1, 1)), constant_values=-1)
    mine = lax.dynamic_slice_in_dim(padded_ids, sidx, 3, 1)
    flags = jnp.stack([mine[:, 0] == mine[:, 1], mine[:, 2] == mine[:, 1]]).astype(jnp.int32)
    block_ids = jnp.pad(block_ids, ((0, RP - rows), (0, 0)))
    half = C // 2
    frequency = jnp.exp(jnp.arange(half, dtype=F32) * (-math.log(10000.0) / half))
    step_rows = jnp.pad(diffusion_steps.astype(F32), (0, LANES - rows))
    live_rows = jnp.arange(LANES, dtype=jnp.int32)[:, None] < rows
    angles = step_rows[:, None] * frequency[None, :]
    embedding = jnp.concatenate([jnp.sin(angles), jnp.cos(angles)], axis=1)
    embedding = jnp.where(live_rows, embedding, 0.0).astype(BF16)
    flags, block_ids, embedding = call(
        table_kernel,
        (
            sds(flags.shape, jnp.int32),
            sds(block_ids.shape, jnp.int32),
            sds(embedding.shape, BF16),
        ),
        "tables",
        (flags, block_ids, embedding),
        after=("edges",),
        in_specs=[SM, VM, VM],
        out_specs=(SM, VM, VM),
    )
    left_halo = lax.ppermute(last, "seq", up)
    right_halo = lax.ppermute(first, "seq", down)

    lengths = lax.dynamic_slice_in_dim(prompt_lengths, (sidx % 2) * arows, arows, 0)

    apack, prow, probs, u, pooled_head, qp, qkv = call(
        functools.partial(attention_kernel, dp, arows, heads, seq // 2, off_qkv),
        (
            sds((C, head_width), BF16),
            sds((arows, seq, pl_local, C), BF16),
            sds((heads * QUERIES, arows * prompt_all), F32),
            sds((RP, C), F32),
            sds((RP, LANES), F32),
            sds((QUERIES, wide), F32),
            sds((qkv_rows, C), BF16),
        ),
        "attention",
        (offsets, bit, lengths, prompts, *head_pieces),
        in_specs=[SM, SM, SM, HB] + [HB] * dp,
        out_specs=(VM,) * 7,
        scratch_shapes=[
            pltpu.VMEM((RP, arows * prompt_all), F32),
            pltpu.SemaphoreType.DMA((dp + seq,)),
        ],
    )

    row_block = pl.BlockSpec((NR, C, LANES), lambda i: (i, 0, 0))

    def col_block(height):
        return pl.BlockSpec((height, NR * LANES), lambda i: (0, i))

    def still(shape):
        return pl.BlockSpec(shape, lambda i: (0,) * len(shape))

    inp, gated, factor_a, factor_b, skip_out, mid, stats = call(
        functools.partial(forward_kernel, meta, dp, csh),
        (
            sds((4 * C, cols), BF16),
            sds((C, cols), BF16),
            sds((C, cols), BF16),
            sds((C, cols), BF16),
            sds(x_in.shape, BF16),
            sds((C, cols), BF16),
            sds((seq, 3 * RP, 2 * csh), F32),
        ),
        "wavenet",
        (
            offsets,
            flags,
            x_in,
            cond,
            d_out,
            Got(left_halo),
            Got(right_halo),
            embedding,
            pooled_head,
            *turned,
        ),
        flops=2 * cols * (4 * C * 2 * C + 2 * C * C),
        nbytes=30e6,
        grid=(steps,),
        in_specs=[
            SM,
            SM,
            row_block,
            row_block,
            row_block,
            whole((C, LANES)),
            whole((C, LANES)),
            whole((LANES, C)),
            whole((RP, LANES)),
        ]
        + [HB] * len(turned),
        out_specs=(
            col_block(4 * C),
            col_block(C),
            col_block(C),
            col_block(C),
            row_block,
            col_block(C),
            still((seq, 3 * RP, 2 * csh)),
        ),
        scratch_shapes=[
            pltpu.VMEM((2 * C, 4 * C), BF16),
            pltpu.VMEM((C, 2 * C), BF16),
            pltpu.VMEM((C, C), BF16),
            pltpu.VMEM((2 * C, C), BF16),
            pltpu.VMEM((C, LANES), F32),
            pltpu.VMEM((C, LANES), F32),
            pltpu.SemaphoreType.DMA((copies,)),
        ],
    )
    stats_got = exchange(stats, "seq")
    gskip = call(
        skip_grad_kernel,
        sds((C, C), BF16),
        "skip",
        (gated, d_skip),
        in_specs=[VM, VM],
        out_specs=VM,
        scratch_shapes=[pltpu.VMEM((C, cols), BF16)],
    )

    coef_out, dfilm, pooled, memory = call(
        functools.partial(stats_kernel, csh, heads, arows),
        (
            sds((seq, 4 * RP, 2 * csh), F32),
            sds((RP, 2 * csh), BF16),
            sds((RP, C), BF16),
            sds((RP, C), BF16),
        ),
        "segments",
        (block_ids, Got(stats_got), apack),
        after=("skip",),
        in_specs=[VM, VM, VM],
        out_specs=(VM, VM, VM, VM),
        scratch_shapes=[pltpu.VMEM((RP, C), F32)],
    )
    coef = Got(exchange(coef_out, "seq"))

    def gate_block(i):
        return jnp.minimum(i, steps - 1)

    def shard(i):
        return jnp.maximum(i - steps, 0)

    def gate_cols(height):
        return pl.BlockSpec((height, NR * LANES), lambda i, order: (0, gate_block(i)))

    gate_rows = pl.BlockSpec((NR, C, LANES), lambda i, order: (gate_block(i), 0, 0))
    wide1, wide2 = EARLY + 2 * LANES, 2 * C - EARLY

    def part(width):
        return sds((dp // 2, 4 * cs, width), BF16)

    def part_spec(width):
        return pl.BlockSpec((1, 4 * cs, width), lambda i, order: (shard(i) // 2, 0, 0))

    outs = call(
        functools.partial(backward_kernel, meta, dp, csh, steps),
        (
            sds((2 * C, cols), BF16),
            sds((C, cols), BF16),
            sds((2 * C, LANES), F32),
            part(wide1),
            part(wide2),
            part(wide1),
            part(wide2),
        ),
        "backward",
        (order, offsets, coef, mid, d_out, d_skip, factor_a, factor_b, inp, gated, gskip, flags, *turned),
        prefetch=1,
        grid=(steps + dp,),
        in_specs=[
            SM,
            pl.BlockSpec(
                (seq, 4 * RP, 2 * csh), lambda i, order: (0, 0, 0), pipeline_mode=pl.Buffered(1)
            ),
            gate_cols(C),
            gate_rows,
            gate_rows,
            gate_cols(C),
            gate_cols(C),
            pl.BlockSpec((4 * cs, cols), lambda i, order: (order[shard(i)], 0)),
            pl.BlockSpec((cs, cols), lambda i, order: (order[shard(i)], 0)),
            pl.BlockSpec((cs, C), lambda i, order: (order[shard(i)], 0)),
            SM,
        ]
        + [HB] * len(turned),
        out_specs=(
            gate_cols(2 * C),
            gate_cols(C),
            pl.BlockSpec((2 * C, LANES), lambda i, order: (0, 0)),
            part_spec(wide1),
            part_spec(wide2),
            part_spec(wide1),
            part_spec(wide2),
        ),
        scratch_shapes=[
            pltpu.VMEM((LANES, C), F32),
            pltpu.VMEM((C, LANES), F32),
            pltpu.VMEM((C, 2 * C), BF16),
            pltpu.VMEM((2 * C, NR * LANES), BF16),
            pltpu.VMEM((cols, 2 * C), BF16),
            pltpu.VMEM((cols, C), BF16),
            pltpu.SemaphoreType.DMA((copies,)),
        ],
    )
    dpre, dres, sums = outs[0:3]
    part1 = Reduction(call, "1", outs[3], outs[5], dp, seq, index)
    part2 = Reduction(call, "2", outs[4], outs[6], dp, seq, index)
    part1.over_blocks()
    keep, give = call(
        functools.partial(step_grad_kernel, meta, dp),
        (part(LANES), part(LANES)),
        "step_grad",
        (offsets, sums, embedding, *turned),
        after=("blocks_1",),
        in_specs=[SM, VM, VM] + [HB] * len(turned),
        out_specs=(VM, VM),
        scratch_shapes=[
            pltpu.VMEM((2 * C, 4 * C), BF16),
            pltpu.VMEM((C, C), F32),
            pltpu.SemaphoreType.DMA((copies,)),
        ],
    )
    part_step = Reduction(call, "step", keep, give, dp, seq, index)

    right_width = -(-(3 * wide + 3 * csh) // LANES) * LANES
    block = sds((dp // 2, cs, right_width), BF16)
    keep, give = call(
        functools.partial(attention_back_kernel, arows, csh, dp),
        (block, block),
        "attention_back",
        (offsets, prow, probs, u, qp, qkv, pooled, memory, dfilm, coef),
        after=("step_grad",),
        in_specs=[SM] + [VM] * 9,
        out_specs=(VM, VM),
        scratch_shapes=[
            pltpu.VMEM((heads * QUERIES, arows * prompt_all), F32),
            pltpu.VMEM((LANES, C), F32),
            pltpu.VMEM((LANES, right_width), F32),
            pltpu.VMEM((C, right_width), F32),
        ],
    )
    small = Reduction(call, "small", keep, give, dp, seq, index)
    part2.over_blocks(("attention_back",), (part_step,))
    small.over_blocks(("blocks_2",))
    part1.over_half(("blocks_small",))

    rest = 4 * cs // seq
    small_width = (cs // rest) * (wide + csh) + max(1, QUERIES // rest) * (wide // 2)
    part2.over_half(("half_1",))
    grad_film, attn_rows, mine, other = call(
        functools.partial(small_sum_kernel, csh, wide),
        (
            sds((2 * csh, cs), F32),
            sds((cs, csh), F32),
            sds((cs + QUERIES, wide), BF16),
            sds((cs + QUERIES, wide), BF16),
        ),
        "small_sum",
        (bit, small.keep, Got(small.got)),
        after=("half_2",),
        in_specs=[SM, VM, VM],
        out_specs=(VM,) * 4,
        scratch_shapes=[pltpu.VMEM((LANES, LANES), F32)],
    )
    partner = flipped(other, "seq", seq, 1)
    part1.over_pieces(("small_sum",))
    part2.over_pieces(("pieces_1",))
    small_piece = call(
        functools.partial(small_piece_kernel, csh, wide),
        sds((rest, small_width), BF16),
        "small_piece",
        (attn_rows, mine, Got(partner)),
        after=("pieces_2",),
        in_specs=[VM] * 3,
        out_specs=VM,
    )
    ones = part1.over_copies(("small_piece",))
    twos = part2.over_copies((ones[0].array,), extra=small_piece)

    base, first, last = call(
        functools.partial(input_grad_kernel, meta, dp),
        (sds((C, cols), BF16), sds((C, LANES), BF16), sds((C, LANES), BF16)),
        "input_grad",
        (offsets, dpre, dres, *turned),
        after=("copies_2",),
        grid=(steps,),
        in_specs=[SM, col_block(2 * C), col_block(C)] + [HB] * len(turned),
        out_specs=(
            col_block(C),
            still((C, LANES)),
            still((C, LANES)),
        ),
        scratch_shapes=[
            pltpu.VMEM((2 * C, 4 * C), BF16),
            pltpu.VMEM((3, C, 2 * C), BF16),
            pltpu.VMEM((C, LANES), F32),
            pltpu.VMEM((C, LANES), F32),
            pltpu.SemaphoreType.DMA((copies,)),
        ],
    )
    from_left = lax.ppermute(last, "seq", up)
    from_right = lax.ppermute(first, "seq", down)
    grad_input, layer_out = call(
        functools.partial(finish_kernel, csh),
        (sds(x_in.shape, BF16), sds(x_in.shape, BF16)),
        "grad_input",
        (flags, base, Got(from_left), Got(from_right), mid, coef),
        after=("input_grad",),
        grid=(steps,),
        in_specs=[
            SM,
            col_block(C),
            whole((C, LANES)),
            whole((C, LANES)),
            col_block(C),
            whole((seq, 4 * RP, 2 * csh)),
        ],
        out_specs=(row_block, row_block),
        scratch_shapes=[pltpu.VMEM((LANES, C), F32), pltpu.VMEM((C, LANES), F32)],
    )

    (
        grad_step,
        grad_conv,
        grad_cond,
        grad_res,
        grad_skip,
        grad_queries,
        grad_query,
        grad_key,
        grad_value,
        grad_attn,
    ) = call(
        functools.partial(output_kernel, cs, csh, wide, seq),
        (
            sds((cs, C), F32),
            sds((3, cs, 2 * C), F32),
            sds((cs, 2 * C), F32),
            sds((cs, C), F32),
            sds((cs, C), F32),
            sds((QUERIES, cs), F32),
            sds((cs, C), F32),
            sds((cs, C), F32),
            sds((cs, C), F32),
            sds((cs, C), F32),
        ),
        "outputs",
        after=("grad_input",),
        args=(bit, *ones, *twos, queries, w_query),
        in_specs=[SM] + [VM] * 5,
        out_specs=(VM,) * 10,
        scratch_shapes=[
            pltpu.VMEM((4 * cs, wide1), F32),
            pltpu.VMEM((4 * cs, wide2 + LANES), F32),
            pltpu.VMEM((4 * cs, small_width), F32),
            pltpu.VMEM((LANES, LANES), F32),
            pltpu.VMEM((LANES, C), F32),
        ],
    )
    return (
        layer_out,
        skip_out,
        grad_input,
        grad_step,
        grad_conv,
        grad_cond,
        grad_res,
        grad_skip,
        grad_queries,
        grad_query,
        grad_key,
        grad_value,
        grad_attn,
        jnp.transpose(grad_film.reshape(2, csh, cs), (2, 0, 1)),
    )


def solution(mesh):
    frames = P("dp", None, "seq")
    matrix = P("dp", None)
    return jax.shard_map(
        functools.partial(body, mesh.shape["dp"], mesh.shape["seq"]),
        mesh=mesh,
        in_specs=(
            frames,
            frames,
            P("dp", None),
            P("dp"),
            P("dp", "seq", None),
            P("dp"),
            matrix,
            P(None, "dp", None),
            matrix,
            matrix,
            matrix,
            P(None, "dp"),
            matrix,
            matrix,
            matrix,
            matrix,
            frames,
            frames,
            frames,
        ),
        out_specs=(
            frames,
            frames,
            frames,
            matrix,
            P(None, "dp", None),
            matrix,
            matrix,
            matrix,
            P(None, "dp"),
            matrix,
            matrix,
            matrix,
            matrix,
            frames,
        ),
        check_vma=False,
    )
```

```python
import functools
import math

import jax
import jax.numpy as jnp
from jax import lax
from jax.experimental import pallas as pl
from jax.experimental.pallas import tpu as pltpu
from jax.sharding import PartitionSpec as P

C = 512
HEADS = 8
QUERIES = 32
HEAD_DIM = 64
SHIFT = 4
SQRT_HALF = 0.7071067811865476
NORM_EPS = 1e-05
MASKED_SCORE = -1e30
LANES = 128
RP = 16
NR = 4
EARLY = 640
F32 = jnp.float32
BF16 = jnp.bfloat16
VMEM_BYTES = 50 * 1024 * 1024


def nn(a, b):
    return lax.dot_general(a, b, (((1,), (0,)), ((), ())), preferred_element_type=F32)


def nt(a, b):
    return lax.dot_general(a, b, (((1,), (1,)), ((), ())), preferred_element_type=F32)


def parts(v, count):
    out = []
    for _ in range(count):
        low = v.astype(BF16).astype(F32)
        out.append(low)
        v = v - low
    return jnp.concatenate(out, axis=0).astype(BF16)


def fold(v, count):
    rows = v.shape[0] // count
    total = v[:rows]
    for k in range(1, count):
        total = total + v[k * rows : (k + 1) * rows]
    return total


def lane_ids(shape):
    return lax.broadcasted_iota(jnp.int32, shape, len(shape) - 1)


def sds(shape, dtype):
    return jax.ShapeDtypeStruct(shape, dtype)


VM = pl.BlockSpec(memory_space=pltpu.VMEM)
HB = pl.BlockSpec(memory_space=pl.ANY)
SM = pl.BlockSpec(memory_space=pltpu.SMEM)


def whole(shape):
    return pl.BlockSpec(shape, lambda i: (0,) * len(shape), pipeline_mode=pl.Buffered(1))


class Got:
    def __init__(self, array):
        self.array = array


class Caller:
    def __init__(self):
        self.done = {}

    def __call__(self, kernel, out_shape, name, args, flops=0, nbytes=0, prefetch=0, after=(), **kw):
        single = not isinstance(out_shape, tuple)
        shapes = (out_shape,) if single else out_shape
        specs = kw["out_specs"]
        specs = (specs,) if single else specs
        pinned = tuple(
            v if spec is SM else pltpu.HBM(v.shape, v.dtype) for v, spec in zip(shapes, specs)
        )
        in_specs = list(kw.pop("in_specs"))
        count = prefetch + len(in_specs)
        args = list(args)
        extra = len(after)
        for before in after:
            in_specs.append(HB)
            args.append(self.done[before] if isinstance(before, str) else before)

        def run(*refs):
            return kernel(*refs[:count], *refs[count + extra :])

        values = []
        for k, v in enumerate(args):
            spec = SM if k < prefetch else in_specs[k - prefetch]
            if isinstance(v, Got):
                values.append(v.array)
            elif spec is SM:
                values.append(v)
            else:
                values.append(pltpu.with_memory_space_constraint(v, pltpu.HBM))
        spec = pltpu.PrefetchScalarGridSpec(
            num_scalar_prefetch=prefetch,
            grid=kw.pop("grid", ()),
            in_specs=in_specs,
            out_specs=kw.pop("out_specs"),
            scratch_shapes=kw.pop("scratch_shapes", ()),
        )
        out = pl.pallas_call(
            run,
            out_shape=pinned[0] if single else pinned,
            name=name,
            grid_spec=spec,
            cost_estimate=pl.CostEstimate(
                flops=1, bytes_accessed=1, transcendentals=0
            ),
            compiler_params=pltpu.CompilerParams(vmem_limit_bytes=VMEM_BYTES),
        )(*values)
        self.done[name] = out if single else out[0]
        return out


def head_pack_kernel(
    csh,
    local,
    group_ref,
    bit_ref,
    attn_ref,
    film_ref,
    wq_ref,
    wk_ref,
    wv_ref,
    queries_ref,
    prompt_ref,
    out_ref,
    mine_ref,
    other_ref,
    scr,
):
    cs = attn_ref.shape[0]
    arows = mine_ref.shape[0]
    mine_ref[...] = prompt_ref[pl.ds(bit_ref[0] * arows, arows)]
    other_ref[...] = prompt_ref[pl.ds((1 - bit_ref[0]) * arows, arows)]
    out_ref[:, 0:C] = attn_ref[...]
    off = C
    scr[...] = jnp.zeros((2 * LANES, LANES), F32)
    scr[0 : 2 * csh, 0:cs] = film_ref[...].astype(F32)
    scr[LANES : LANES + QUERIES, 0:cs] = queries_ref[...].astype(F32)
    film = scr[0:LANES].T[0:cs]
    table = scr[LANES : 2 * LANES].T[0:cs]
    turn = lax.rem(C - local * group_ref[0], C)
    blocks = [film[:, 0 : 2 * csh]]
    for ref in (wq_ref, wk_ref, wv_ref):
        blocks.append(pltpu.roll(ref[...].astype(F32), turn, 1)[:, 0:local])
    blocks.append(table)
    for block in blocks:
        width = min(block.shape[1], out_ref.shape[1] - off)
        out_ref[:, off : off + width] = block[:, 0:width].astype(BF16)
        off += width
    if off < out_ref.shape[1]:
        out_ref[:, off:] = jnp.zeros((cs, out_ref.shape[1] - off), BF16)


SIDE = 480


def turned_pack_kernel(cs, bit_ref, conv_ref, cond_ref, res_ref, skip_ref, step_ref, out_ref, side_ref, middle_ref, scr):
    for k in range(3):
        scr[k * cs : (k + 1) * cs] = conv_ref[k]
    scr[3 * cs : 4 * cs] = cond_ref[...]
    turned = scr[...].T
    out_ref[0 : 2 * C - SIDE] = turned[0 : 2 * C - SIDE]
    at = 2 * C - SIDE
    for ref in (res_ref, skip_ref, step_ref):
        for lane in range(0, C, 4 * cs):
            out_ref[at : at + cs] = ref[:, lane : lane + 4 * cs]
            at += cs
    out_ref[at : at + SIDE] = turned[2 * C - SIDE :]
    middle_ref[...] = out_ref[SIDE:at]
    side_ref[...] = out_ref[pl.ds(pl.multiple_of(bit_ref[0] * at, 16), SIDE)]


def pair_kernel(a_ref, b_ref, out_ref):
    for p in range(out_ref.shape[0]):
        out_ref[p, 0] = a_ref[...]
        out_ref[p, 1] = b_ref[...]


def table_kernel(flags_ref, ids_ref, emb_ref, flags_out, ids_out, emb_out):
    for side in range(2):
        for r in range(flags_ref.shape[1]):
            flags_out[side, r] = flags_ref[side, r]
    ids_out[...] = ids_ref[...]
    emb_out[...] = emb_ref[...]


def edge_kernel(x_ref, first_ref, last_ref):
    rows = x_ref.shape[0]
    lane = lane_ids((C, LANES))
    first = jnp.zeros((C, LANES), F32)
    last = jnp.zeros((C, LANES), F32)
    for r in range(rows):
        v = x_ref[r].astype(F32)
        here = (lane // SHIFT) == r
        first = jnp.where(here, pltpu.roll(v, SHIFT * r, 1) if r else v, first)
        last = jnp.where(here, pltpu.roll(v, SHIFT * r + SHIFT, 1), last)
    first_ref[...] = first.astype(BF16)
    last_ref[...] = last.astype(BF16)


def begin(copies):
    for copy in copies:
        copy.start()


def finish(copies):
    for copy in copies:
        copy.wait()


def turned_copies(meta, refs, off_ref, cs, wt, others, sems):
    dp = len({k for k, _ in meta})
    pairs = []

    def conv(k, ref, first, row, rows):
        if wt is not None:
            lanes = pl.ds(pl.multiple_of(off_ref[k] * 4, LANES), 4 * cs)
            at = row if isinstance(row, int) else pl.multiple_of(row, 16)
            pairs.append((ref.at[pl.ds(first, rows)], wt.at[pl.ds(at, rows), lanes]))

    def rest(k, ref, at):
        row = pl.ds(pl.multiple_of(off_ref[k], 16), cs)
        for other in others:
            for lane in range(0, C, 4 * cs):
                if other is not None:
                    dst, start = other
                    pairs.append((ref.at[pl.ds(at, cs)], dst.at[row, pl.ds(start + lane, 4 * cs)]))
                at += cs

    inner = 2 * C - 2 * SIDE
    for (k, which), ref in zip(meta, refs):
        if which is None:
            conv(k, ref, 0, 0, SIDE + inner)
            rest(k, ref, SIDE + inner)
            conv(k, ref, ref.shape[0] - SIDE, 2 * C - SIDE, SIDE)
        elif which == 2:
            conv(k, ref, 0, SIDE, inner)
            rest(k, ref, inner)
        else:
            conv(k, ref, 0, off_ref[dp + which] * (2 * C - SIDE), SIDE)
    return [pltpu.make_async_copy(a, b, sems.at[n]) for n, (a, b) in enumerate(pairs)]


def head_copies(refs, off_ref, dst, sems):
    copies = []
    for k, ref in enumerate(refs):
        row = pl.ds(pl.multiple_of(off_ref[k], 16), ref.shape[0])
        copies.append(pltpu.make_async_copy(ref, dst.at[row], sems.at[k]))
    return copies


def forward_kernel(
    meta, dp, csh, off_ref, flags_ref, x_ref, cond_ref, dout_ref, left_ref, right_ref, emb_ref, pooled_ref, *refs
):
    turned, refs = refs[: len(meta)], refs[len(meta) :]
    (
        inp_ref,
        gated_ref,
        fa_ref,
        fb_ref,
        skip_ref,
        mid_ref,
        stats_ref,
        wt_ref,
        rn_ref,
        step_ref,
        rst_ref,
        lift_ref,
        acc_ref,
        sems,
    ) = refs
    cs = C // dp
    i = pl.program_id(0)
    lane = lane_ids((C, LANES))

    @pl.when(i == 0)
    def _():
        copies = turned_copies(
            meta,
            turned,
            off_ref,
            cs,
            wt_ref,
            ((rn_ref, 0), (rn_ref, C), (step_ref, 0)),
            sems,
        )
        begin(copies)
        acc_ref[...] = jnp.zeros((C, LANES), F32)
        finish(copies)
        lift = nn(emb_ref[0:RP], step_ref[...])
        lift = jnp.concatenate([lift, jnp.zeros((LANES - RP, C), F32)], axis=0)
        lift_ref[...] = lift.T
        rst_ref[...] = rn_ref[...].T

    lift = pltpu.roll(lift_ref[...], lax.rem(LANES - NR * i, LANES), 1)
    left = left_ref[...].astype(F32)
    right = right_ref[...].astype(F32)

    def put(tap, cols, value):
        for d in range(dp):
            at = d * 4 * cs + tap * cs
            inp_ref[at : at + cs, cols] = value[d * cs : (d + 1) * cs]

    for j in range(NR):
        r = NR * i + j
        lc = lift[:, j : j + 1]
        sh = (x_ref[j].astype(F32) + lc).astype(BF16)
        shf = sh.astype(F32)
        lh = pltpu.roll(left, lax.rem(LANES - SHIFT * r, LANES), 1)
        lh = jnp.where(flags_ref[0, r] > 0, (lh + lc).astype(BF16).astype(F32), 0.0)
        rh = pltpu.roll(right, LANES - SHIFT - SHIFT * r, 1)
        rh = jnp.where(flags_ref[1, r] > 0, (rh + lc).astype(BF16).astype(F32), 0.0)
        cols = slice(j * LANES, (j + 1) * LANES)
        put(0, cols, jnp.where(lane < SHIFT, lh, pltpu.roll(shf, SHIFT, 1)).astype(BF16))
        put(1, cols, sh)
        put(
            2,
            cols,
            jnp.where(lane >= LANES - SHIFT, rh, pltpu.roll(shf, LANES - SHIFT, 1)).astype(BF16),
        )
        put(3, cols, cond_ref[j])
    pre = nn(wt_ref[...], inp_ref[...])
    th = jnp.tanh(pre[:C])
    sg = jax.nn.sigmoid(pre[C:])
    gf = th * sg
    fa_ref[...] = (sg - gf * th).astype(BF16)
    fb_ref[...] = (gf * (1.0 - sg)).astype(BF16)
    g = gf.astype(BF16)
    gated_ref[...] = g
    rs = nn(rst_ref[...], g)
    acc = acc_ref[...]
    for j in range(NR):
        r = NR * i + j
        cols = slice(j * LANES, (j + 1) * LANES)
        skip_ref[j] = rs[C:, cols].astype(BF16)
        mid = ((x_ref[j].astype(F32) + rs[:C, cols]) * SQRT_HALF).astype(BF16)
        mid_ref[:, cols] = mid
        mf = mid.astype(F32)
        df = dout_ref[j].astype(F32)
        total = jnp.sum(mf, axis=1, keepdims=True)
        dev = mf - total * (1.0 / LANES)
        acc = jnp.where(lane == r, total, acc)
        acc = jnp.where(lane == RP + r, jnp.sum(dev * dev, axis=1, keepdims=True), acc)
        acc = jnp.where(lane == 2 * RP + r, jnp.sum(df, axis=1, keepdims=True), acc)
        acc = jnp.where(lane == 3 * RP + r, jnp.sum(df * dev, axis=1, keepdims=True), acc)
    acc_ref[...] = acc

    @pl.when(i == pl.num_programs(0) - 1)
    def _():
        t = acc.T
        for s in range(C // csh):
            cols = slice(s * csh, (s + 1) * csh)
            stats_ref[s, 0 : 2 * RP, 0:csh] = t[0 : 2 * RP, cols]
            stats_ref[s, 0 : 2 * RP, csh : 2 * csh] = t[2 * RP : 4 * RP, cols]
            stats_ref[s, 2 * RP : 3 * RP] = pooled_ref[:, 0 : 2 * csh]


def attention_kernel(dp, rows, heads, pairs, off, off_ref, bit_ref, len_ref, prompts, *refs):
    pieces, refs = refs[:dp], refs[dp:]
    apack_ref, prow, probs_ref, u_ref, pooled_ref, qp_ref, qkv_ref, abd, sems = refs
    copies = head_copies(pieces, off_ref, apack_ref, sems)
    count = len(copies)
    for j in range(pairs):
        for i in range(2):
            copies.append(
                pltpu.make_async_copy(
                    prompts.at[j, i], prow.at[:, 2 * j + i], sems.at[count + 2 * j + i]
                )
            )
    begin(copies)
    local = prow.shape[2]
    total = 2 * pairs * local
    abd[...] = jnp.zeros(abd.shape, F32)
    lane = lane_ids((heads * QUERIES, total))
    place = jnp.zeros((heads * QUERIES, total), jnp.int32)
    for k in range(2 * pairs):
        here = (k // 2) * 2 + (bit_ref[0] if k % 2 == 0 else 1 - bit_ref[0])
        place = jnp.where(lane // local == k, here * local + lane % local, place)
    finish(copies)
    wide = heads * HEAD_DIM
    qkv = apack_ref[:, off : off + qkv_ref.shape[0]].T
    qkv_ref[...] = qkv
    qp = nt(qkv[3 * wide : 3 * wide + QUERIES], qkv[0:wide])
    qp_ref[...] = qp
    st = []
    for g in range(heads):
        cols = slice(g * HEAD_DIM, (g + 1) * HEAD_DIM)
        st.append(fold(nn(parts(qp[:, cols], 3), qkv[wide + cols.start : wide + cols.stop]), 3))
    st = jnp.concatenate(st, axis=0) * (1.0 / math.sqrt(HEAD_DIM))
    table = prow[...].reshape(rows * total, C)
    scores = fold(nt(parts(st, 3), table), 3)
    for r in range(rows):
        cols = slice(r * total, (r + 1) * total)
        live = place < len_ref[r]
        s = jnp.where(live, scores[:, cols], MASKED_SCORE)
        e = jnp.where(live, jnp.exp(s - jnp.max(s, axis=1, keepdims=True)), 0.0)
        p = e / jnp.sum(e, axis=1, keepdims=True)
        probs_ref[:, cols] = p
        for g in range(heads):
            abd[8 * g + r : 8 * g + r + 1, cols] = jnp.sum(
                p[g * QUERIES : (g + 1) * QUERIES], axis=0, keepdims=True
            )
    u = fold(nn(parts(abd[...], 2), table), 2)
    u_ref[...] = u
    pooled_ref[...] = jnp.zeros(pooled_ref.shape, F32)
    for g in range(heads):
        first = 2 * wide + g * HEAD_DIM
        v = parts(u[8 * g : 8 * g + 8] * (1.0 / QUERIES), 2)
        pooled_ref[0:8, g * HEAD_DIM : (g + 1) * HEAD_DIM] = fold(
            nt(v, qkv[first : first + HEAD_DIM]), 2
        )


def stats_kernel(
    csh, heads, rows, seg_ref, x_ref, apack_ref, out_ref, dfilm_ref, pooled_ref, memory_ref, scratch
):
    count = x_ref.shape[0]
    wide = heads * HEAD_DIM
    seg = seg_ref[...]
    scratch[...] = jnp.zeros(scratch.shape, F32)
    for s in range(count):
        group, part = s // 2, s % 2
        scratch[part * rows : (part + 1) * rows, group * wide : (group + 1) * wide] = x_ref[
            s, 2 * RP : 2 * RP + rows, 0:wide
        ]
    pooled = scratch[...].astype(BF16)
    pooled_ref[...] = pooled
    memory = nn(pooled, apack_ref[:, 0:C]).astype(BF16)
    memory_ref[...] = memory
    film = nn(memory, apack_ref[:, C : C + 2 * csh])
    f0 = film[:, 0:csh]
    f1 = film[:, csh : 2 * csh]
    total = [x_ref[s, 0:RP, 0:csh] for s in range(count)]
    second = [x_ref[s, RP : 2 * RP, 0:csh] for s in range(count)]
    dsum = [x_ref[s, 0:RP, csh : 2 * csh] for s in range(count)]
    cross = [x_ref[s, RP : 2 * RP, csh : 2 * csh] for s in range(count)]
    means = [v * (1.0 / LANES) for v in total]
    d0 = jnp.zeros((RP, csh), F32)
    d1 = jnp.zeros((RP, csh), F32)
    for me in range(count):
        same = [(seg[:, s : s + 1] == seg[:, me : me + 1]).astype(F32) for s in range(count)]
        frames = sum(same) * float(LANES)
        inv = 1.0 / frames
        mean = sum(m * v for m, v in zip(same, total)) * inv
        var = (
            sum(
                m * (v + float(LANES) * (u - mean) * (u - mean))
                for m, v, u in zip(same, second, means)
            )
            * inv
        )
        scale = lax.rsqrt(var + NORM_EPS)
        dtot = sum(m * v for m, v in zip(same, dsum))
        xtot = sum(m * (v + (u - mean) * d) for m, v, u, d in zip(same, cross, means, dsum)) * scale
        mean_part = f0 * dtot * inv
        cross_part = f0 * xtot * inv
        slope = scale * scale * cross_part
        out_ref[me, 0:RP, 0:csh] = 1.0 + f0 * scale
        out_ref[me, RP : 2 * RP, 0:csh] = f1 - f0 * scale * mean
        out_ref[me, 0:RP, csh : 2 * csh] = -slope
        out_ref[me, RP : 2 * RP, csh : 2 * csh] = slope * mean - scale * mean_part
        d0 = d0 + (cross[me] + (means[me] - mean) * dsum[me]) * scale
        d1 = d1 + dsum[me]
    dfilm = jnp.concatenate([d0, d1], axis=1).astype(BF16)
    dfilm_ref[...] = dfilm
    dmem = nt(dfilm, apack_ref[:, C : C + 2 * csh])
    dpool = nt(dmem.astype(BF16), apack_ref[:, 0:C])
    for s in range(count):
        group, part = s // 2, s % 2
        rolled = pltpu.roll(dpool, RP - part * rows, 0) if part else dpool
        out_ref[s, 2 * RP : 3 * RP, 0:csh] = dmem[:, s * csh : (s + 1) * csh]
        out_ref[s, 2 * RP : 3 * RP, csh : 2 * csh] = jnp.zeros((RP, csh), F32)
        out_ref[s, 3 * RP : 4 * RP] = rolled[:, group * wide : (group + 1) * wide]


def coef_columns(csh, coef_ref, rows_ref, cols_ref):
    rows_ref[...] = jnp.zeros(rows_ref.shape, F32)
    for s in range(C // csh):
        cols = slice(s * csh, (s + 1) * csh)
        rows_ref[0 : 2 * RP, cols] = coef_ref[s, 0 : 2 * RP, 0:csh]
        rows_ref[2 * RP : 4 * RP, cols] = coef_ref[s, 0 : 2 * RP, csh : 2 * csh]
    cols_ref[...] = rows_ref[...].T


def skip_grad_kernel(gated_ref, dskip_ref, out_ref, right):
    for r in range(dskip_ref.shape[0]):
        right[:, r * LANES : (r + 1) * LANES] = dskip_ref[r]
    out_ref[...] = nt(gated_ref[...], right[...]).astype(BF16)


def backward_kernel(meta, dp, csh, gates, order_ref, off_ref, coef_ref, mid_ref, dout_ref, dskip_ref, fa_ref, fb_ref, inp_ref, gated_ref, gskip_ref, flags_ref, *refs):
    turned, refs = refs[: len(meta)], refs[len(meta) :]
    dpre_ref, dres_ref, sums_ref, refs = refs[0], refs[1], refs[2], refs[3:]
    outs, refs = (refs[0:2], refs[2:4]), refs[4:]
    rows_ref, cols_ref, w_ref, both_ref, dpt_ref, drt_ref, sems = refs
    cs = C // dp
    span = NR * LANES
    i = pl.program_id(0)

    @pl.when(i == 0)
    def _():
        copies = turned_copies(
            meta, turned, off_ref, cs, None, ((w_ref, 0), (w_ref, C), None), sems
        )
        begin(copies)
        coef_columns(csh, coef_ref, rows_ref, cols_ref)
        sums_ref[...] = jnp.zeros(sums_ref.shape, F32)
        finish(copies)

    @pl.when(i < gates)
    def _():
        coef = pltpu.roll(cols_ref[...], lax.rem(LANES - NR * i, LANES), 1)
        for j in range(NR):
            cols = slice(j * LANES, (j + 1) * LANES)
            mf = mid_ref[:, cols].astype(F32)
            df = dout_ref[j].astype(F32)
            a = coef[:, j : j + 1]
            be = coef[:, 2 * RP + j : 2 * RP + j + 1]
            ga = coef[:, 3 * RP + j : 3 * RP + j + 1]
            dmid = (a * df + (be * mf + ga)).astype(BF16).astype(F32)
            both_ref[0:C, cols] = (dmid * SQRT_HALF).astype(BF16)
            both_ref[C : 2 * C, cols] = dskip_ref[j]
        dres = both_ref[0:C]
        dres_ref[...] = dres
        dg = nn(w_ref[...], both_ref[...])
        dt = (dg * fa_ref[...].astype(F32)).astype(BF16)
        ds = (dg * fb_ref[...].astype(F32)).astype(BF16)
        dpre_ref[0:C] = dt
        dpre_ref[C : 2 * C] = ds
        at = pl.ds(pl.multiple_of(i * span, span), span)
        dpt_ref[at, 0:C] = dt.T
        dpt_ref[at, C : 2 * C] = ds.T
        drt_ref[at] = dres.T
        frame = lax.broadcasted_iota(jnp.int32, (span, LANES), 0)
        column = lane_ids((span, LANES))
        place = frame % LANES
        which = frame // LANES
        keep_l = jnp.zeros((span, LANES), jnp.int32)
        keep_r = jnp.zeros((span, LANES), jnp.int32)
        for j in range(NR):
            keep_l = jnp.where(which == j, flags_ref[0, NR * i + j], keep_l)
            keep_r = jnp.where(which == j, flags_ref[1, NR * i + j], keep_r)
        row = NR * i + which
        use0 = (column == row) & ((place >= SHIFT) | (keep_l > 0))
        use1 = column == RP + row
        use2 = (column == 2 * RP + row) & ((place < LANES - SHIFT) | (keep_r > 0))
        pick = jnp.where(use0 | use1 | use2, 1.0, 0.0).astype(BF16)
        sums_ref[...] = sums_ref[...] + nn(dpre_ref[...], pick)

    @pl.when(i >= gates)
    def _():
        g = nn(inp_ref[...], dpt_ref[...]).astype(BF16)
        h = nn(gated_ref[...], drt_ref[...]).astype(BF16)
        k = i - gates
        for parity, (one, two) in enumerate(outs):

            @pl.when(lax.rem(k, 2) == parity)
            def _():
                for t in range(4):
                    rows = slice(t * cs, (t + 1) * cs)
                    lanes = slice(t * LANES, (t + 1) * LANES)
                    one[0, rows, 0:LANES] = h[:, lanes]
                    one[0, rows, LANES : 2 * LANES] = gskip_ref[:, lanes]
                one[0, :, 2 * LANES :] = g[:, 0:EARLY]
                two[0] = g[:, EARLY:]


def step_grad_kernel(meta, dp, off_ref, sums_ref, emb_ref, *refs):
    turned, refs = refs[: len(meta)], refs[len(meta) :]
    keep_ref, give_ref, wt_ref, scr, sems = refs
    cs = C // dp
    copies = turned_copies(meta, turned, off_ref, cs, wt_ref, (None,) * 3, sems)
    begin(copies)
    sums = sums_ref[...].T
    emb = emb_ref[...].T
    finish(copies)
    total = jnp.zeros((RP, 4 * C), F32)
    lane = lane_ids((RP, 4 * C))
    all_taps = fold(nn(parts(sums[0 : 3 * RP], 2), wt_ref[...]), 2)
    for t in range(3):
        g = all_taps[t * RP : (t + 1) * RP]
        total = total + jnp.where((lane // cs) % 4 == t, g, 0.0)
    out = []
    for d in range(dp):
        block = total[:, d * 4 * cs : (d + 1) * 4 * cs]
        out.append(block[:, 0:cs] + block[:, cs : 2 * cs] + block[:, 2 * cs : 3 * cs])
    g = jnp.concatenate(out, axis=1)
    g = jnp.concatenate([g, jnp.zeros((LANES - RP, C), F32)], axis=0)
    hi = g.astype(BF16)
    lo = (g - hi.astype(F32)).astype(BF16)
    scr[...] = nn(emb, hi) + nn(emb, lo)
    for k in range(dp):
        v = scr[pl.ds(pl.multiple_of(off_ref[k], 16), cs)].astype(BF16)
        for t in range(4):
            (keep_ref, give_ref)[k % 2][k // 2, t * cs : (t + 1) * cs] = v[
                :, t * LANES : (t + 1) * LANES
            ]


def input_grad_kernel(meta, dp, off_ref, dpre_ref, dres_ref, *refs):
    turned, refs = refs[: len(meta)], refs[len(meta) :]
    base_ref, first_ref, last_ref, wt_ref, w_ref, facc_ref, lacc_ref, sems = refs
    cs = C // dp
    i = pl.program_id(0)
    lane = lane_ids((C, LANES))

    @pl.when(i == 0)
    def _():
        copies = turned_copies(meta, turned, off_ref, cs, wt_ref, (None,) * 3, sems)
        begin(copies)
        facc_ref[...] = jnp.zeros((C, LANES), F32)
        lacc_ref[...] = jnp.zeros((C, LANES), F32)
        finish(copies)
        for d in range(dp):
            v = wt_ref[:, d * 4 * cs : (d + 1) * 4 * cs].T
            for t in range(3):
                w_ref[t, d * cs : (d + 1) * cs] = v[t * cs : (t + 1) * cs]

    dpre = dpre_ref[...]
    y0 = nn(w_ref[0], dpre)
    y1 = nn(w_ref[1], dpre)
    y2 = nn(w_ref[2], dpre)
    facc = facc_ref[...]
    lacc = lacc_ref[...]
    for j in range(NR):
        r = NR * i + j
        cols = slice(j * LANES, (j + 1) * LANES)
        z0 = pltpu.roll(y0[:, cols], LANES - SHIFT, 1)
        z2 = pltpu.roll(y2[:, cols], SHIFT, 1)
        inner0 = lane < LANES - SHIFT
        inner2 = lane >= SHIFT
        v = y1[:, cols]
        base_ref[:, cols] = (
            v
            + jnp.where(inner0, z0, 0.0)
            + jnp.where(inner2, z2, 0.0)
            + dres_ref[:, cols].astype(F32)
        ).astype(BF16)
        here = (lane // SHIFT) == r
        facc = jnp.where(here, pltpu.roll(z0, lax.rem(SHIFT * r + SHIFT, LANES), 1), facc)
        lacc = jnp.where(here, pltpu.roll(z2, SHIFT * r, 1), lacc)
    facc_ref[...] = facc
    lacc_ref[...] = lacc

    @pl.when(i == pl.num_programs(0) - 1)
    def _():
        first_ref[...] = facc.astype(BF16)
        last_ref[...] = lacc.astype(BF16)


def finish_kernel(csh, flags_ref, base_ref, left_ref, right_ref, mid_ref, coef_ref, out_ref, layer_ref, rows_ref, cols_ref):
    i = pl.program_id(0)
    lane = lane_ids((C, LANES))

    @pl.when(i == 0)
    def _():
        coef_columns(csh, coef_ref, rows_ref, cols_ref)

    coef = pltpu.roll(cols_ref[...], lax.rem(LANES - NR * i, LANES), 1)
    left = left_ref[...].astype(F32)
    right = right_ref[...].astype(F32)
    for j in range(NR):
        r = NR * i + j
        cols = slice(j * LANES, (j + 1) * LANES)
        lh = pltpu.roll(left, lax.rem(LANES - SHIFT * r, LANES), 1)
        rh = pltpu.roll(right, LANES - SHIFT - SHIFT * r, 1)
        lh = jnp.where((lane < SHIFT) & (flags_ref[0, r] > 0), lh, 0.0)
        rh = jnp.where((lane >= LANES - SHIFT) & (flags_ref[1, r] > 0), rh, 0.0)
        out_ref[j] = (base_ref[:, cols].astype(F32) + lh + rh).astype(BF16)
        a = coef[:, j : j + 1]
        b = coef[:, RP + j : RP + j + 1]
        layer_ref[j] = (a * mid_ref[:, cols].astype(F32) + b).astype(BF16)


def add_blocks_kernel(count, *refs):
    ins, (keep_ref, give_ref) = refs[: 2 * count], refs[2 * count :]
    at = 0
    for p in range(count):
        a_ref, b_ref = ins[2 * p : 2 * p + 2]
        width = a_ref.shape[2]
        for j in range(a_ref.shape[0]):
            v = a_ref[j].astype(F32) + b_ref[j].astype(F32)
            (keep_ref, give_ref)[j % 2][j // 2, :, at : at + width] = v.astype(BF16)
        at += width


def add_pieces_kernel(a_ref, b_ref, out_ref):
    v = a_ref[0].astype(F32) + b_ref[0].astype(F32)
    size = out_ref.shape[1]
    for p in range(out_ref.shape[0]):
        out_ref[p] = v[p * size : (p + 1) * size].astype(BF16)


def sum_copies_kernel(a_ref, *refs):
    out_ref = refs[-1]
    v = a_ref[0].astype(F32)
    for p in range(1, a_ref.shape[0]):
        v = v + a_ref[p].astype(F32)
    v = v.astype(BF16)
    for p in range(out_ref.shape[0]):
        out_ref[p, :, 0 : v.shape[1]] = v
        if len(refs) > 1:
            out_ref[p, :, v.shape[1] :] = refs[0][...]


def small_sum_kernel(csh, wide, bit_ref, keep_ref, got_ref, film_ref, attn_ref, mine_ref, other_ref, turn):
    v = keep_ref[0].astype(F32) + got_ref[0].astype(F32)
    cs = v.shape[0]
    film = 2 * wide + csh
    turn[...] = jnp.zeros(turn.shape, F32)
    turn[0:cs, 0 : 2 * csh] = v[:, film : film + 2 * csh]
    film_ref[...] = turn[...].T[0 : 2 * csh, 0:cs]
    attn_ref[...] = v[:, 2 * wide : film]
    last = film + 2 * csh
    even = bit_ref[0] == 0
    for one, two, rows, width in (
        (v[:, 0:wide], v[:, wide : 2 * wide], slice(0, cs), wide),
        (
            v[0:QUERIES, last : last + wide // 2],
            v[0:QUERIES, last + wide // 2 : last + wide],
            slice(cs, cs + QUERIES),
            wide // 2,
        ),
    ):
        mine_ref[rows, 0:width] = jnp.where(even, one, two).astype(BF16)
        other_ref[rows, 0:width] = jnp.where(even, two, one).astype(BF16)
    mine_ref[cs:, wide // 2 :] = jnp.zeros((QUERIES, wide // 2), BF16)
    other_ref[cs:, wide // 2 :] = jnp.zeros((QUERIES, wide // 2), BF16)


def small_piece_kernel(csh, wide, attn_ref, mine_ref, got_ref, out_ref):
    v = mine_ref[...].astype(F32) + got_ref[...].astype(F32)
    attn = attn_ref[...]
    cs = attn.shape[0]
    rows = out_ref.shape[0]
    at = 0
    for row in range(0, cs, rows):
        out_ref[:, at : at + wide] = v[row : row + rows].astype(BF16)
        out_ref[:, at + wide : at + wide + csh] = attn[row : row + rows].astype(BF16)
        at += wide + csh
    for row in range(0, QUERIES, rows):
        block = v[cs + row : cs + min(row + rows, QUERIES), 0 : wide // 2]
        if block.shape[0] < rows:
            pad = jnp.zeros((rows - block.shape[0], wide // 2), F32)
            block = jnp.concatenate([block, pad], axis=0)
        out_ref[:, at : at + wide // 2] = block.astype(BF16)
        at += wide // 2


def output_kernel(
    cs,
    csh,
    wide,
    seq,
    bit_ref,
    *refs,
):
    own1, got1, all2, refs = *refs[:3], refs[3:]
    (
        queries_ref,
        wq_ref,
        step_ref,
        conv_ref,
        cond_ref,
        res_ref,
        skip_ref,
        gqueries_ref,
        gquery_ref,
        key_ref,
        value_ref,
        attn_ref,
        scr1,
        scr2,
        small,
        qscr,
        dq,
    ) = refs
    count, size = own1.shape[0], own1.shape[1]
    wide2 = scr2.shape[1]
    bit = bit_ref[0]
    for one, side in ((own1, bit), (got1, 1 - bit)):
        for p in range(count):
            rows = pl.ds(pl.multiple_of((2 * p + side) * size, 8), size)
            scr1[rows] = one[p].astype(F32)
    for s in range(seq):
        at = s * size
        v = all2[s].astype(F32)
        scr2[at : at + size] = v[:, 0:wide2]
        small[s * size : (s + 1) * size] = v[:, wide2:]
    for t in range(4):
        rows = slice(t * cs, (t + 1) * cs)
        lanes = slice(t * LANES, (t + 1) * LANES)
        res_ref[:, lanes] = scr1[rows, 0:LANES]
        skip_ref[:, lanes] = scr1[rows, LANES : 2 * LANES]
        rest = 2 * C - EARLY
        step_ref[:, lanes] = scr2[rows, rest : rest + LANES]
        if t < 3:
            conv_ref[t, :, 0:EARLY] = scr1[rows, 2 * LANES : 2 * LANES + EARLY]
            conv_ref[t, :, EARLY:] = scr2[rows, 0:rest]
        else:
            cond_ref[:, 0:EARLY] = scr1[rows, 2 * LANES : 2 * LANES + EARLY]
            cond_ref[:, EARLY:] = scr2[rows, 0:rest]
    dq[...] = jnp.zeros(dq.shape, F32)
    for s in range(seq):
        v = small[s * size : (s + 1) * size]
        group, even = s // 2, s % 2 == 0
        out = key_ref if even else value_ref
        at = 0
        for row in range(0, cs, size):
            out[row : row + size, group * wide : (group + 1) * wide] = v[:, at : at + wide]
            attn_ref[row : row + size, s * csh : (s + 1) * csh] = v[:, at + wide : at + wide + csh]
            at += wide + csh
        first = group * wide + (0 if even else wide // 2)
        for row in range(0, QUERIES, size):
            count = min(size, QUERIES - row)
            dq[row : row + count, first : first + wide // 2] = v[0:count, at : at + wide // 2]
            at += wide // 2
    qscr[...] = jnp.zeros((LANES, LANES), F32)
    qscr[0:QUERIES, 0:cs] = queries_ref[...].astype(F32)
    qt = qscr[...].T.astype(BF16)
    d = dq[...]
    hi = d.astype(BF16)
    lo = (d - hi.astype(F32)).astype(BF16)
    gquery_ref[...] = (nn(qt, hi) + nn(qt, lo))[0:cs]
    gqueries_ref[...] = fold(nt(parts(d[0:QUERIES], 2), wq_ref[...]), 2)


def attention_back_kernel(
    rows,
    csh,
    dp,
    off_ref,
    prow,
    probs_ref,
    u_ref,
    qp_ref,
    qkv_ref,
    pooled_ref,
    memory_ref,
    dfilm_ref,
    got_ref,
    keep_ref,
    give_ref,
    ds,
    stack,
    right,
    out,
):
    count = got_ref.shape[0]
    total = prow.shape[1] * prow.shape[2]
    cs = C // dp
    table = prow[...].reshape(rows * total, C)
    wide = qp_ref.shape[1]
    heads = wide // HEAD_DIM
    datt = got_ref[0, 3 * RP : 4 * RP, 0:wide]
    dmem = got_ref[0, 2 * RP : 3 * RP, 0:csh]
    for s in range(1, count):
        datt = datt + got_ref[s, 3 * RP : 4 * RP, 0:wide]
        dmem = dmem + got_ref[s, 2 * RP : 3 * RP, 0:csh]
    datt = datt[0:8] * (1.0 / QUERIES)
    vh = []
    for g in range(heads):
        first = 2 * wide + g * HEAD_DIM
        v = parts(datt[:, g * HEAD_DIM : (g + 1) * HEAD_DIM], 2)
        vh.append(fold(nn(v, qkv_ref[first : first + HEAD_DIM]), 2))
    vh = jnp.concatenate(vh, axis=0)
    dp_all = fold(nt(parts(vh, 2), table), 2)
    for r in range(rows):
        cols = slice(r * total, (r + 1) * total)
        for g in range(heads):
            mine = slice(g * QUERIES, (g + 1) * QUERIES)
            p = probs_ref[mine, cols]
            dpr = dp_all[8 * g + r : 8 * g + r + 1, cols]
            inner = jnp.sum(p * dpr, axis=1, keepdims=True)
            ds[mine, cols] = p * (dpr - inner)
    tt = fold(nn(parts(ds[...], 2), table), 2)
    scale = 1.0 / math.sqrt(HEAD_DIM)
    dq = []
    stack[...] = jnp.zeros(stack.shape, F32)
    right[...] = jnp.zeros(right.shape, F32)
    stack[0 : heads * QUERIES] = tt
    stack[64:80] = u_ref[...]
    stack[80:96] = pooled_ref[...].astype(F32)
    stack[96:112] = memory_ref[...].astype(F32)
    for g in range(heads):
        cols = slice(g * HEAD_DIM, (g + 1) * HEAD_DIM)
        mine = slice(g * QUERIES, (g + 1) * QUERIES)
        wk = qkv_ref[wide + g * HEAD_DIM : wide + (g + 1) * HEAD_DIM]
        dq.append(fold(nt(parts(tt[mine], 2), wk), 2) * scale)
        right[mine, cols] = qp_ref[:, cols] * scale
        right[64 + 8 * g : 72 + 8 * g, wide + cols.start : wide + cols.stop] = datt[:, cols]
    right[80:96, 2 * wide : 2 * wide + csh] = dmem
    right[96:112, 2 * wide + csh : 2 * wide + 3 * csh] = dfilm_ref[...].astype(F32)
    out[...] = lax.dot_general(
        stack[...].T,
        right[...],
        (((1,), (0,)), ((), ())),
        precision=lax.Precision.HIGHEST,
        preferred_element_type=F32,
    )
    last = 2 * wide + 3 * csh
    for k in range(dp):
        ref = (keep_ref, give_ref)[k % 2]
        ref[k // 2] = out[pl.ds(pl.multiple_of(off_ref[k], 16), cs)].astype(BF16)
        for g in range(heads):
            first = last + g * HEAD_DIM
            ref[k // 2, 0:QUERIES, first : first + HEAD_DIM] = dq[g].astype(BF16)


def exchange(pieces, axis, groups=None):
    return lax.all_to_all(
        pieces, axis, split_axis=0, concat_axis=0, axis_index_groups=groups, tiled=True
    )


def flipped(v, axis, size, bit):
    return lax.ppermute(v, axis, [(d, d ^ bit) for d in range(size)])


class Reduction:
    def __init__(self, call, name, keep, give, dp, seq, index):
        self.call, self.name, self.dp, self.seq, self.index = call, name, dp, seq, index
        self.keep, self.flip = keep, 1
        self.got = flipped(give, "dp", dp, 1)

    def over_blocks(self, after=(), others=()):
        while 2 * self.flip < self.dp:
            group = (self,) + tuple(others)
            others = ()
            args = []
            for part in group:
                args += [part.keep, Got(part.got)]
            width = sum(part.keep.shape[2] for part in group)
            half = sds((self.keep.shape[0] // 2, self.keep.shape[1], width), BF16)
            self.keep, give = self.call(
                functools.partial(add_blocks_kernel, len(group)),
                (half, half),
                "blocks_" + self.name,
                args,
                after=after,
                in_specs=[VM] * len(args),
                out_specs=(VM, VM),
            )
            self.flip *= 2
            self.got = flipped(give, "dp", self.dp, self.flip)
        self.rest = self.keep.shape[1:]

    def over_pieces(self, after=()):
        rows, width = self.rest
        pieces = self.call(
            add_pieces_kernel,
            sds((self.seq, rows // self.seq, width), BF16),
            "pieces_" + self.name,
            (self.keep, Got(self.got)),
            after=after,
            in_specs=[VM, VM],
            out_specs=VM,
        )
        self.got = exchange(pieces, "seq")

    def over_copies(self, after=(), extra=None):
        args, (count, rows, width) = [Got(self.got)], self.got.shape
        if extra is None:
            count = self.seq // 2
        if extra is not None:
            args.append(extra)
            width += extra.shape[1]
        copies = self.call(
            sum_copies_kernel,
            sds((count, rows, width), BF16),
            "copies_" + self.name,
            args,
            after=after,
            in_specs=[VM] * len(args),
            out_specs=VM,
        )
        if extra is not None:
            return (Got(exchange(copies, "seq")),)
        groups = [[2 * k + b for k in range(count)] for b in range(2)]
        own = exchange(copies, "seq", groups)
        return Got(own), Got(flipped(own, "seq", self.seq, 1))


def body(
    dp,
    seq,
    x_in,
    cond,
    segment_ids,
    diffusion_steps,
    prompt,
    prompt_lengths,
    w_step,
    w_conv,
    w_cond,
    w_res,
    w_skip,
    queries,
    w_query,
    w_key,
    w_value,
    w_attn_out,
    w_film,
    d_out,
    d_skip,
):
    call = Caller()
    rows = x_in.shape[0]
    frames = x_in.shape[2]
    steps = rows // NR
    cols = rows * frames
    cs = C // dp
    csh = C // seq
    heads = 2 * HEADS // seq
    wide = heads * HEAD_DIM
    arows = rows // 2
    pl_local = prompt.shape[1]
    prompt_all = pl_local * seq
    sidx = lax.axis_index("seq")
    didx = lax.axis_index("dp")
    group = (sidx // 2).astype(jnp.int32).reshape(1)
    bit = (sidx % 2).astype(jnp.int32).reshape(1)
    up = [(i, i + 1) for i in range(seq - 1)]
    down = [(i + 1, i) for i in range(seq - 1)]
    order = jnp.bitwise_xor(didx, jnp.arange(dp, dtype=jnp.int32)).astype(jnp.int32)
    offsets = jnp.concatenate([order * cs, bit, 1 - bit])
    index = sidx.astype(jnp.int32).reshape(1)

    def gather(pack, side=None, middle=None):
        if dp == 4 and side is not None:
            mine = flipped(side, "dp", dp, 2)
            inner = flipped(middle, "dp", dp, 2)
            other = flipped(mine, "seq", seq, 1)
            near = [(0, None, pack), (2, 0, mine), (2, 2, inner), (2, 1, other)]
            pieces = near + [(k + 1, h, flipped(v, "dp", dp, 1)) for k, h, v in near]
        else:
            pieces = [(0, None, pack)]
            flip = dp // 2
            while flip:
                pieces += [(k + flip, h, flipped(v, "dp", dp, flip)) for k, h, v in pieces]
                flip //= 2
        pieces.sort(key=lambda piece: piece[0])
        meta = [(k, h) for k, h, _ in pieces]
        return meta, [v if k == 0 else Got(v) for k, _, v in pieces]

    off_qkv = C + 2 * csh
    qkv_rows = -(-(3 * wide + QUERIES) // LANES) * LANES
    head_width = -(-(off_qkv + qkv_rows) // LANES) * LANES
    middle = 2 * C - 2 * SIDE + 3 * C // 4
    pack, side, middle = call(
        functools.partial(turned_pack_kernel, cs),
        (
            sds((2 * SIDE + middle, 4 * cs), BF16),
            sds((SIDE, 4 * cs), BF16),
            sds((middle, 4 * cs), BF16),
        ),
        "turned_pack",
        (bit, w_conv, w_cond, w_res, w_skip, w_step),
        in_specs=[SM] + [VM] * 5,
        out_specs=(VM, VM, VM),
        scratch_shapes=[pltpu.VMEM((4 * cs, 2 * C), BF16)],
    )
    meta, turned = gather(pack, side, middle)
    copies = 4 * dp * (1 + 3 * C // (4 * cs))
    pack, mine, other = call(
        functools.partial(head_pack_kernel, csh, wide),
        (
            sds((cs, head_width), BF16),
            sds((arows, pl_local, C), BF16),
            sds((arows, pl_local, C), BF16),
        ),
        "head_pack",
        (
            group,
            bit,
            w_attn_out,
            jnp.transpose(w_film, (1, 2, 0)).reshape(2 * csh, cs),
            w_query,
            w_key,
            w_value,
            queries,
            prompt,
        ),
        after=("turned_pack",),
        in_specs=[SM, SM] + [VM] * 7,
        out_specs=(VM,) * 3,
        scratch_shapes=[pltpu.VMEM((2 * LANES, LANES), F32)],
    )
    _, head_pieces = gather(pack)
    partner = flipped(other, "seq", seq, 1)
    first, last = call(
        edge_kernel,
        (sds((C, LANES), BF16), sds((C, LANES), BF16)),
        "edges",
        (x_in,),
        after=("head_pack",),
        in_specs=[VM],
        out_specs=(VM, VM),
    )
    left_halo = lax.ppermute(last, "seq", up)
    right_halo = lax.ppermute(first, "seq", down)
    pair = call(
        pair_kernel,
        sds((seq // 2, 2, arows, pl_local, C), BF16),
        "pair",
        (mine, Got(partner)),
        after=(left_halo, right_halo),
        in_specs=[VM, VM],
        out_specs=VM,
    )
    z_groups = [[2 * k + b for k in range(seq // 2)] for b in range(2)]
    prompts = Got(exchange(pair, "seq", z_groups))
    block_ids = segment_ids[:, ::frames]
    padded_ids = jnp.pad(block_ids, ((0, 0), (1, 1)), constant_values=-1)
    mine = lax.dynamic_slice_in_dim(padded_ids, sidx, 3, 1)
    flags = jnp.stack([mine[:, 0] == mine[:, 1], mine[:, 2] == mine[:, 1]]).astype(jnp.int32)
    block_ids = jnp.pad(block_ids, ((0, RP - rows), (0, 0)))
    half = C // 2
    frequency = jnp.exp(jnp.arange(half, dtype=F32) * (-math.log(10000.0) / half))
    step_rows = jnp.pad(diffusion_steps.astype(F32), (0, LANES - rows))
    live_rows = jnp.arange(LANES, dtype=jnp.int32)[:, None] < rows
    angles = step_rows[:, None] * frequency[None, :]
    embedding = jnp.concatenate([jnp.sin(angles), jnp.cos(angles)], axis=1)
    embedding = jnp.where(live_rows, embedding, 0.0).astype(BF16)
    flags, block_ids, embedding = call(
        table_kernel,
        (
            sds(flags.shape, jnp.int32),
            sds(block_ids.shape, jnp.int32),
            sds(embedding.shape, BF16),
        ),
        "tables",
        (flags, block_ids, embedding),
        after=("pair", head_pieces[dp // 2].array),
        in_specs=[SM, VM, VM],
        out_specs=(SM, VM, VM),
    )

    lengths = lax.dynamic_slice_in_dim(prompt_lengths, (sidx % 2) * arows, arows, 0)

    apack, prow, probs, u, pooled_head, qp, qkv = call(
        functools.partial(attention_kernel, dp, arows, heads, seq // 2, off_qkv),
        (
            sds((C, head_width), BF16),
            sds((arows, seq, pl_local, C), BF16),
            sds((heads * QUERIES, arows * prompt_all), F32),
            sds((RP, C), F32),
            sds((RP, LANES), F32),
            sds((QUERIES, wide), F32),
            sds((qkv_rows, C), BF16),
        ),
        "attention",
        (offsets, bit, lengths, prompts, *head_pieces),
        in_specs=[SM, SM, SM, HB] + [HB] * dp,
        out_specs=(VM,) * 7,
        scratch_shapes=[
            pltpu.VMEM((RP, arows * prompt_all), F32),
            pltpu.SemaphoreType.DMA((dp + seq,)),
        ],
    )

    row_block = pl.BlockSpec((NR, C, LANES), lambda i: (i, 0, 0))

    def col_block(height):
        return pl.BlockSpec((height, NR * LANES), lambda i: (0, i))

    def still(shape):
        return pl.BlockSpec(shape, lambda i: (0,) * len(shape))

    inp, gated, factor_a, factor_b, skip_out, mid, stats = call(
        functools.partial(forward_kernel, meta, dp, csh),
        (
            sds((4 * C, cols), BF16),
            sds((C, cols), BF16),
            sds((C, cols), BF16),
            sds((C, cols), BF16),
            sds(x_in.shape, BF16),
            sds((C, cols), BF16),
            sds((seq, 3 * RP, 2 * csh), F32),
        ),
        "wavenet",
        (
            offsets,
            flags,
            x_in,
            cond,
            d_out,
            Got(left_halo),
            Got(right_halo),
            embedding,
            pooled_head,
            *turned,
        ),
        flops=2 * cols * (4 * C * 2 * C + 2 * C * C),
        nbytes=30e6,
        grid=(steps,),
        in_specs=[
            SM,
            SM,
            row_block,
            row_block,
            row_block,
            whole((C, LANES)),
            whole((C, LANES)),
            whole((LANES, C)),
            whole((RP, LANES)),
        ]
        + [HB] * len(turned),
        out_specs=(
            col_block(4 * C),
            col_block(C),
            col_block(C),
            col_block(C),
            row_block,
            col_block(C),
            still((seq, 3 * RP, 2 * csh)),
        ),
        scratch_shapes=[
            pltpu.VMEM((2 * C, 4 * C), BF16),
            pltpu.VMEM((C, 2 * C), BF16),
            pltpu.VMEM((C, C), BF16),
            pltpu.VMEM((2 * C, C), BF16),
            pltpu.VMEM((C, LANES), F32),
            pltpu.VMEM((C, LANES), F32),
            pltpu.SemaphoreType.DMA((copies,)),
        ],
    )
    stats_got = exchange(stats, "seq")
    gskip = call(
        skip_grad_kernel,
        sds((C, C), BF16),
        "skip",
        (gated, d_skip),
        in_specs=[VM, VM],
        out_specs=VM,
        scratch_shapes=[pltpu.VMEM((C, cols), BF16)],
    )

    coef_out, dfilm, pooled, memory = call(
        functools.partial(stats_kernel, csh, heads, arows),
        (
            sds((seq, 4 * RP, 2 * csh), F32),
            sds((RP, 2 * csh), BF16),
            sds((RP, C), BF16),
            sds((RP, C), BF16),
        ),
        "segments",
        (block_ids, Got(stats_got), apack),
        after=("skip",),
        in_specs=[VM, VM, VM],
        out_specs=(VM, VM, VM, VM),
        scratch_shapes=[pltpu.VMEM((RP, C), F32)],
    )
    coef = Got(exchange(coef_out, "seq"))

    def gate_block(i):
        return jnp.minimum(i, steps - 1)

    def shard(i):
        return jnp.maximum(i - steps, 0)

    def gate_cols(height):
        return pl.BlockSpec((height, NR * LANES), lambda i, order: (0, gate_block(i)))

    gate_rows = pl.BlockSpec((NR, C, LANES), lambda i, order: (gate_block(i), 0, 0))
    wide1, wide2 = EARLY + 2 * LANES, 2 * C - EARLY

    def part(width):
        return sds((dp // 2, 4 * cs, width), BF16)

    def part_spec(width):
        return pl.BlockSpec((1, 4 * cs, width), lambda i, order: (shard(i) // 2, 0, 0))

    outs = call(
        functools.partial(backward_kernel, meta, dp, csh, steps),
        (
            sds((2 * C, cols), BF16),
            sds((C, cols), BF16),
            sds((2 * C, LANES), F32),
            part(wide1),
            part(wide2),
            part(wide1),
            part(wide2),
        ),
        "backward",
        (order, offsets, coef, mid, d_out, d_skip, factor_a, factor_b, inp, gated, gskip, flags, *turned),
        prefetch=1,
        grid=(steps + dp,),
        in_specs=[
            SM,
            pl.BlockSpec(
                (seq, 4 * RP, 2 * csh), lambda i, order: (0, 0, 0), pipeline_mode=pl.Buffered(1)
            ),
            gate_cols(C),
            gate_rows,
            gate_rows,
            gate_cols(C),
            gate_cols(C),
            pl.BlockSpec((4 * cs, cols), lambda i, order: (order[shard(i)], 0)),
            pl.BlockSpec((cs, cols), lambda i, order: (order[shard(i)], 0)),
            pl.BlockSpec((cs, C), lambda i, order: (order[shard(i)], 0)),
            SM,
        ]
        + [HB] * len(turned),
        out_specs=(
            gate_cols(2 * C),
            gate_cols(C),
            pl.BlockSpec((2 * C, LANES), lambda i, order: (0, 0)),
            part_spec(wide1),
            part_spec(wide2),
            part_spec(wide1),
            part_spec(wide2),
        ),
        scratch_shapes=[
            pltpu.VMEM((LANES, C), F32),
            pltpu.VMEM((C, LANES), F32),
            pltpu.VMEM((C, 2 * C), BF16),
            pltpu.VMEM((2 * C, NR * LANES), BF16),
            pltpu.VMEM((cols, 2 * C), BF16),
            pltpu.VMEM((cols, C), BF16),
            pltpu.SemaphoreType.DMA((copies,)),
        ],
    )
    dpre, dres, sums = outs[0:3]
    part1 = Reduction(call, "1", outs[3], outs[5], dp, seq, index)
    part2 = Reduction(call, "2", outs[4], outs[6], dp, seq, index)
    part1.over_blocks()
    keep, give = call(
        functools.partial(step_grad_kernel, meta, dp),
        (part(LANES), part(LANES)),
        "step_grad",
        (offsets, sums, embedding, *turned),
        after=("blocks_1",),
        in_specs=[SM, VM, VM] + [HB] * len(turned),
        out_specs=(VM, VM),
        scratch_shapes=[
            pltpu.VMEM((2 * C, 4 * C), BF16),
            pltpu.VMEM((C, C), F32),
            pltpu.SemaphoreType.DMA((copies,)),
        ],
    )
    part_step = Reduction(call, "step", keep, give, dp, seq, index)

    right_width = -(-(3 * wide + 3 * csh) // LANES) * LANES
    block = sds((dp // 2, cs, right_width), BF16)
    keep, give = call(
        functools.partial(attention_back_kernel, arows, csh, dp),
        (block, block),
        "attention_back",
        (offsets, prow, probs, u, qp, qkv, pooled, memory, dfilm, coef),
        after=("step_grad",),
        in_specs=[SM] + [VM] * 9,
        out_specs=(VM, VM),
        scratch_shapes=[
            pltpu.VMEM((heads * QUERIES, arows * prompt_all), F32),
            pltpu.VMEM((LANES, C), F32),
            pltpu.VMEM((LANES, right_width), F32),
            pltpu.VMEM((C, right_width), F32),
        ],
    )
    small = Reduction(call, "small", keep, give, dp, seq, index)
    part2.over_blocks(("attention_back",), (part_step,))
    small.over_blocks(("blocks_2",))
    part1.over_pieces(("blocks_small",))
    part2.over_pieces(("pieces_1",))

    rest = 4 * cs // seq
    small_width = (cs // rest) * (wide + csh) + max(1, QUERIES // rest) * (wide // 2)
    grad_film, attn_rows, mine, other = call(
        functools.partial(small_sum_kernel, csh, wide),
        (
            sds((2 * csh, cs), F32),
            sds((cs, csh), F32),
            sds((cs + QUERIES, wide), BF16),
            sds((cs + QUERIES, wide), BF16),
        ),
        "small_sum",
        (bit, small.keep, Got(small.got)),
        after=("pieces_2",),
        in_specs=[SM, VM, VM],
        out_specs=(VM,) * 4,
        scratch_shapes=[pltpu.VMEM((LANES, LANES), F32)],
    )
    partner = flipped(other, "seq", seq, 1)
    ones = part1.over_copies(("small_sum",))
    small_piece = call(
        functools.partial(small_piece_kernel, csh, wide),
        sds((rest, small_width), BF16),
        "small_piece",
        (attn_rows, mine, Got(partner)),
        after=("copies_1",),
        in_specs=[VM] * 3,
        out_specs=VM,
    )
    twos = part2.over_copies(extra=small_piece)

    base, first, last = call(
        functools.partial(input_grad_kernel, meta, dp),
        (sds((C, cols), BF16), sds((C, LANES), BF16), sds((C, LANES), BF16)),
        "input_grad",
        (offsets, dpre, dres, *turned),
        after=("copies_2",),
        grid=(steps,),
        in_specs=[SM, col_block(2 * C), col_block(C)] + [HB] * len(turned),
        out_specs=(
            col_block(C),
            still((C, LANES)),
            still((C, LANES)),
        ),
        scratch_shapes=[
            pltpu.VMEM((2 * C, 4 * C), BF16),
            pltpu.VMEM((3, C, 2 * C), BF16),
            pltpu.VMEM((C, LANES), F32),
            pltpu.VMEM((C, LANES), F32),
            pltpu.SemaphoreType.DMA((copies,)),
        ],
    )
    from_left = lax.ppermute(last, "seq", up)
    from_right = lax.ppermute(first, "seq", down)
    grad_input, layer_out = call(
        functools.partial(finish_kernel, csh),
        (sds(x_in.shape, BF16), sds(x_in.shape, BF16)),
        "grad_input",
        (flags, base, Got(from_left), Got(from_right), mid, coef),
        after=("input_grad",),
        grid=(steps,),
        in_specs=[
            SM,
            col_block(C),
            whole((C, LANES)),
            whole((C, LANES)),
            col_block(C),
            whole((seq, 4 * RP, 2 * csh)),
        ],
        out_specs=(row_block, row_block),
        scratch_shapes=[pltpu.VMEM((LANES, C), F32), pltpu.VMEM((C, LANES), F32)],
    )

    (
        grad_step,
        grad_conv,
        grad_cond,
        grad_res,
        grad_skip,
        grad_queries,
        grad_query,
        grad_key,
        grad_value,
        grad_attn,
    ) = call(
        functools.partial(output_kernel, cs, csh, wide, seq),
        (
            sds((cs, C), F32),
            sds((3, cs, 2 * C), F32),
            sds((cs, 2 * C), F32),
            sds((cs, C), F32),
            sds((cs, C), F32),
            sds((QUERIES, cs), F32),
            sds((cs, C), F32),
            sds((cs, C), F32),
            sds((cs, C), F32),
            sds((cs, C), F32),
        ),
        "outputs",
        after=("grad_input",),
        args=(bit, *ones, *twos, queries, w_query),
        in_specs=[SM] + [VM] * 5,
        out_specs=(VM,) * 10,
        scratch_shapes=[
            pltpu.VMEM((4 * cs, wide1), F32),
            pltpu.VMEM((4 * cs, wide2 + LANES), F32),
            pltpu.VMEM((4 * cs, small_width), F32),
            pltpu.VMEM((LANES, LANES), F32),
            pltpu.VMEM((LANES, C), F32),
        ],
    )
    return (
        layer_out,
        skip_out,
        grad_input,
        grad_step,
        grad_conv,
        grad_cond,
        grad_res,
        grad_skip,
        grad_queries,
        grad_query,
        grad_key,
        grad_value,
        grad_attn,
        jnp.transpose(grad_film.reshape(2, csh, cs), (2, 0, 1)),
    )


def solution(mesh):
    frames = P("dp", None, "seq")
    matrix = P("dp", None)
    return jax.shard_map(
        functools.partial(body, mesh.shape["dp"], mesh.shape["seq"]),
        mesh=mesh,
        in_specs=(
            frames,
            frames,
            P("dp", None),
            P("dp"),
            P("dp", "seq", None),
            P("dp"),
            matrix,
            P(None, "dp", None),
            matrix,
            matrix,
            matrix,
            P(None, "dp"),
            matrix,
            matrix,
            matrix,
            matrix,
            frames,
            frames,
            frames,
        ),
        out_specs=(
            frames,
            frames,
            frames,
            matrix,
            P(None, "dp", None),
            matrix,
            matrix,
            matrix,
            P(None, "dp"),
            matrix,
            matrix,
            matrix,
            matrix,
            frames,
        ),
        check_vma=False,
    )
```

```python
import functools
import math

import jax
import jax.numpy as jnp
from jax import lax
from jax.experimental import pallas as pl
from jax.experimental.pallas import tpu as pltpu
from jax.sharding import PartitionSpec as P

C = 512
HEADS = 8
QUERIES = 32
HEAD_DIM = 64
SHIFT = 4
SQRT_HALF = 0.7071067811865476
NORM_EPS = 1e-05
MASKED_SCORE = -1e30
LANES = 128
RP = 16
NR = 4
EARLY = 640
F32 = jnp.float32
BF16 = jnp.bfloat16
VMEM_BYTES = 50 * 1024 * 1024


def nn(a, b):
    return lax.dot_general(a, b, (((1,), (0,)), ((), ())), preferred_element_type=F32)


def nt(a, b):
    return lax.dot_general(a, b, (((1,), (1,)), ((), ())), preferred_element_type=F32)


def parts(v, count):
    out = []
    for _ in range(count):
        low = v.astype(BF16).astype(F32)
        out.append(low)
        v = v - low
    return jnp.concatenate(out, axis=0).astype(BF16)


def fold(v, count):
    rows = v.shape[0] // count
    total = v[:rows]
    for k in range(1, count):
        total = total + v[k * rows : (k + 1) * rows]
    return total


def lane_ids(shape):
    return lax.broadcasted_iota(jnp.int32, shape, len(shape) - 1)


def sds(shape, dtype):
    return jax.ShapeDtypeStruct(shape, dtype)


VM = pl.BlockSpec(memory_space=pltpu.VMEM)
HB = pl.BlockSpec(memory_space=pl.ANY)
SM = pl.BlockSpec(memory_space=pltpu.SMEM)


def whole(shape):
    return pl.BlockSpec(shape, lambda i: (0,) * len(shape), pipeline_mode=pl.Buffered(1))


class Got:
    def __init__(self, array):
        self.array = array


class Caller:
    def __init__(self):
        self.done = {}

    def __call__(self, kernel, out_shape, name, args, flops=0, nbytes=0, prefetch=0, after=(), **kw):
        single = not isinstance(out_shape, tuple)
        shapes = (out_shape,) if single else out_shape
        specs = kw["out_specs"]
        specs = (specs,) if single else specs
        pinned = tuple(
            v if spec is SM else pltpu.HBM(v.shape, v.dtype) for v, spec in zip(shapes, specs)
        )
        in_specs = list(kw.pop("in_specs"))
        count = prefetch + len(in_specs)
        args = list(args)
        extra = len(after)
        for before in after:
            in_specs.append(HB)
            args.append(self.done[before] if isinstance(before, str) else before)

        def run(*refs):
            return kernel(*refs[:count], *refs[count + extra :])

        values = []
        for k, v in enumerate(args):
            spec = SM if k < prefetch else in_specs[k - prefetch]
            if isinstance(v, Got):
                values.append(v.array)
            elif spec is SM:
                values.append(v)
            else:
                values.append(pltpu.with_memory_space_constraint(v, pltpu.HBM))
        spec = pltpu.PrefetchScalarGridSpec(
            num_scalar_prefetch=prefetch,
            grid=kw.pop("grid", ()),
            in_specs=in_specs,
            out_specs=kw.pop("out_specs"),
            scratch_shapes=kw.pop("scratch_shapes", ()),
        )
        out = pl.pallas_call(
            run,
            out_shape=pinned[0] if single else pinned,
            name=name,
            grid_spec=spec,
            cost_estimate=pl.CostEstimate(
                flops=1, bytes_accessed=1, transcendentals=0
            ),
            compiler_params=pltpu.CompilerParams(vmem_limit_bytes=VMEM_BYTES),
        )(*values)
        self.done[name] = out if single else out[0]
        return out


def head_pack_kernel(
    csh,
    local,
    group_ref,
    bit_ref,
    attn_ref,
    film_ref,
    wq_ref,
    wk_ref,
    wv_ref,
    queries_ref,
    prompt_ref,
    out_ref,
    mine_ref,
    other_ref,
    scr,
):
    cs = attn_ref.shape[0]
    arows = mine_ref.shape[0]
    mine_ref[...] = prompt_ref[pl.ds(bit_ref[0] * arows, arows)]
    other_ref[...] = prompt_ref[pl.ds((1 - bit_ref[0]) * arows, arows)]
    out_ref[:, 0:C] = attn_ref[...]
    off = C
    scr[...] = jnp.zeros((2 * LANES, LANES), F32)
    scr[0 : 2 * csh, 0:cs] = film_ref[...].astype(F32)
    scr[LANES : LANES + QUERIES, 0:cs] = queries_ref[...].astype(F32)
    film = scr[0:LANES].T[0:cs]
    table = scr[LANES : 2 * LANES].T[0:cs]
    turn = lax.rem(C - local * group_ref[0], C)
    blocks = [film[:, 0 : 2 * csh]]
    for ref in (wq_ref, wk_ref, wv_ref):
        blocks.append(pltpu.roll(ref[...].astype(F32), turn, 1)[:, 0:local])
    blocks.append(table)
    for block in blocks:
        width = min(block.shape[1], out_ref.shape[1] - off)
        out_ref[:, off : off + width] = block[:, 0:width].astype(BF16)
        off += width
    if off < out_ref.shape[1]:
        out_ref[:, off:] = jnp.zeros((cs, out_ref.shape[1] - off), BF16)


SIDE = 480


def turned_pack_kernel(cs, bit_ref, conv_ref, cond_ref, res_ref, skip_ref, step_ref, out_ref, side_ref, middle_ref, scr):
    for k in range(3):
        scr[k * cs : (k + 1) * cs] = conv_ref[k]
    scr[3 * cs : 4 * cs] = cond_ref[...]
    turned = scr[...].T
    out_ref[0 : 2 * C - SIDE] = turned[0 : 2 * C - SIDE]
    at = 2 * C - SIDE
    for ref in (res_ref, skip_ref, step_ref):
        for lane in range(0, C, 4 * cs):
            out_ref[at : at + cs] = ref[:, lane : lane + 4 * cs]
            at += cs
    out_ref[at : at + SIDE] = turned[2 * C - SIDE :]
    middle_ref[...] = out_ref[SIDE:at]
    side_ref[...] = out_ref[pl.ds(pl.multiple_of(bit_ref[0] * at, 16), SIDE)]


def pair_kernel(a_ref, b_ref, out_ref):
    for p in range(out_ref.shape[0]):
        out_ref[p, 0] = a_ref[...]
        out_ref[p, 1] = b_ref[...]


def table_kernel(flags_ref, ids_ref, emb_ref, flags_out, ids_out, emb_out):
    for side in range(2):
        for r in range(flags_ref.shape[1]):
            flags_out[side, r] = flags_ref[side, r]
    ids_out[...] = ids_ref[...]
    emb_out[...] = emb_ref[...]


def edge_kernel(x_ref, first_ref, last_ref):
    rows = x_ref.shape[0]
    lane = lane_ids((C, LANES))
    first = jnp.zeros((C, LANES), F32)
    last = jnp.zeros((C, LANES), F32)
    for r in range(rows):
        v = x_ref[r].astype(F32)
        here = (lane // SHIFT) == r
        first = jnp.where(here, pltpu.roll(v, SHIFT * r, 1) if r else v, first)
        last = jnp.where(here, pltpu.roll(v, SHIFT * r + SHIFT, 1), last)
    first_ref[...] = first.astype(BF16)
    last_ref[...] = last.astype(BF16)


def begin(copies):
    for copy in copies:
        copy.start()


def finish(copies):
    for copy in copies:
        copy.wait()


def turned_copies(meta, refs, off_ref, cs, wt, others, sems):
    dp = len({k for k, _ in meta})
    pairs = []

    def conv(k, ref, first, row, rows):
        if wt is not None:
            lanes = pl.ds(pl.multiple_of(off_ref[k] * 4, LANES), 4 * cs)
            at = row if isinstance(row, int) else pl.multiple_of(row, 16)
            pairs.append((ref.at[pl.ds(first, rows)], wt.at[pl.ds(at, rows), lanes]))

    def rest(k, ref, at):
        row = pl.ds(pl.multiple_of(off_ref[k], 16), cs)
        for other in others:
            for lane in range(0, C, 4 * cs):
                if other is not None:
                    dst, start = other
                    pairs.append((ref.at[pl.ds(at, cs)], dst.at[row, pl.ds(start + lane, 4 * cs)]))
                at += cs

    inner = 2 * C - 2 * SIDE
    for (k, which), ref in zip(meta, refs):
        if which is None:
            conv(k, ref, 0, 0, SIDE + inner)
            rest(k, ref, SIDE + inner)
            conv(k, ref, ref.shape[0] - SIDE, 2 * C - SIDE, SIDE)
        elif which == 2:
            conv(k, ref, 0, SIDE, inner)
            rest(k, ref, inner)
        else:
            conv(k, ref, 0, off_ref[dp + which] * (2 * C - SIDE), SIDE)
    return [pltpu.make_async_copy(a, b, sems.at[n]) for n, (a, b) in enumerate(pairs)]


def head_copies(refs, off_ref, dst, sems):
    copies = []
    for k, ref in enumerate(refs):
        row = pl.ds(pl.multiple_of(off_ref[k], 16), ref.shape[0])
        copies.append(pltpu.make_async_copy(ref, dst.at[row], sems.at[k]))
    return copies


def forward_kernel(
    meta, dp, csh, off_ref, flags_ref, x_ref, cond_ref, dout_ref, left_ref, right_ref, emb_ref, pooled_ref, *refs
):
    turned, refs = refs[: len(meta)], refs[len(meta) :]
    (
        inp_ref,
        gated_ref,
        fa_ref,
        fb_ref,
        skip_ref,
        mid_ref,
        stats_ref,
        wt_ref,
        rn_ref,
        step_ref,
        rst_ref,
        lift_ref,
        acc_ref,
        sems,
    ) = refs
    cs = C // dp
    i = pl.program_id(0)
    lane = lane_ids((C, LANES))

    @pl.when(i == 0)
    def _():
        copies = turned_copies(
            meta,
            turned,
            off_ref,
            cs,
            wt_ref,
            ((rn_ref, 0), (rn_ref, C), (step_ref, 0)),
            sems,
        )
        begin(copies)
        acc_ref[...] = jnp.zeros((C, LANES), F32)
        finish(copies)
        lift = nn(emb_ref[0:RP], step_ref[...])
        lift = jnp.concatenate([lift, jnp.zeros((LANES - RP, C), F32)], axis=0)
        lift_ref[...] = lift.T
        rst_ref[...] = rn_ref[...].T

    lift = pltpu.roll(lift_ref[...], lax.rem(LANES - NR * i, LANES), 1)
    left = left_ref[...].astype(F32)
    right = right_ref[...].astype(F32)

    def put(tap, cols, value):
        for d in range(dp):
            at = d * 4 * cs + tap * cs
            inp_ref[at : at + cs, cols] = value[d * cs : (d + 1) * cs]

    for j in range(NR):
        r = NR * i + j
        lc = lift[:, j : j + 1]
        sh = (x_ref[j].astype(F32) + lc).astype(BF16)
        shf = sh.astype(F32)
        lh = pltpu.roll(left, lax.rem(LANES - SHIFT * r, LANES), 1)
        lh = jnp.where(flags_ref[0, r] > 0, (lh + lc).astype(BF16).astype(F32), 0.0)
        rh = pltpu.roll(right, LANES - SHIFT - SHIFT * r, 1)
        rh = jnp.where(flags_ref[1, r] > 0, (rh + lc).astype(BF16).astype(F32), 0.0)
        cols = slice(j * LANES, (j + 1) * LANES)
        put(0, cols, jnp.where(lane < SHIFT, lh, pltpu.roll(shf, SHIFT, 1)).astype(BF16))
        put(1, cols, sh)
        put(
            2,
            cols,
            jnp.where(lane >= LANES - SHIFT, rh, pltpu.roll(shf, LANES - SHIFT, 1)).astype(BF16),
        )
        put(3, cols, cond_ref[j])
    pre = nn(wt_ref[...], inp_ref[...])
    th = jnp.tanh(pre[:C])
    sg = jax.nn.sigmoid(pre[C:])
    gf = th * sg
    fa_ref[...] = (sg - gf * th).astype(BF16)
    fb_ref[...] = (gf * (1.0 - sg)).astype(BF16)
    g = gf.astype(BF16)
    gated_ref[...] = g
    rs = nn(rst_ref[...], g)
    acc = acc_ref[...]
    for j in range(NR):
        r = NR * i + j
        cols = slice(j * LANES, (j + 1) * LANES)
        skip_ref[j] = rs[C:, cols].astype(BF16)
        mid = ((x_ref[j].astype(F32) + rs[:C, cols]) * SQRT_HALF).astype(BF16)
        mid_ref[:, cols] = mid
        mf = mid.astype(F32)
        df = dout_ref[j].astype(F32)
        total = jnp.sum(mf, axis=1, keepdims=True)
        dev = mf - total * (1.0 / LANES)
        acc = jnp.where(lane == r, total, acc)
        acc = jnp.where(lane == RP + r, jnp.sum(dev * dev, axis=1, keepdims=True), acc)
        acc = jnp.where(lane == 2 * RP + r, jnp.sum(df, axis=1, keepdims=True), acc)
        acc = jnp.where(lane == 3 * RP + r, jnp.sum(df * dev, axis=1, keepdims=True), acc)
    acc_ref[...] = acc

    @pl.when(i == pl.num_programs(0) - 1)
    def _():
        t = acc.T
        for s in range(C // csh):
            cols = slice(s * csh, (s + 1) * csh)
            stats_ref[s, 0 : 2 * RP, 0:csh] = t[0 : 2 * RP, cols]
            stats_ref[s, 0 : 2 * RP, csh : 2 * csh] = t[2 * RP : 4 * RP, cols]
            stats_ref[s, 2 * RP : 3 * RP] = pooled_ref[:, 0 : 2 * csh]


def attention_kernel(dp, rows, heads, pairs, off, off_ref, bit_ref, len_ref, prompts, *refs):
    pieces, refs = refs[:dp], refs[dp:]
    apack_ref, prow, probs_ref, u_ref, pooled_ref, qp_ref, qkv_ref, abd, sems = refs
    copies = head_copies(pieces, off_ref, apack_ref, sems)
    count = len(copies)
    for j in range(pairs):
        for i in range(2):
            copies.append(
                pltpu.make_async_copy(
                    prompts.at[j, i], prow.at[:, 2 * j + i], sems.at[count + 2 * j + i]
                )
            )
    begin(copies)
    local = prow.shape[2]
    total = 2 * pairs * local
    abd[...] = jnp.zeros(abd.shape, F32)
    lane = lane_ids((heads * QUERIES, total))
    place = jnp.zeros((heads * QUERIES, total), jnp.int32)
    for k in range(2 * pairs):
        here = (k // 2) * 2 + (bit_ref[0] if k % 2 == 0 else 1 - bit_ref[0])
        place = jnp.where(lane // local == k, here * local + lane % local, place)
    finish(copies)
    wide = heads * HEAD_DIM
    qkv = apack_ref[:, off : off + qkv_ref.shape[0]].T
    qkv_ref[...] = qkv
    qp = nt(qkv[3 * wide : 3 * wide + QUERIES], qkv[0:wide])
    qp_ref[...] = qp
    st = []
    for g in range(heads):
        cols = slice(g * HEAD_DIM, (g + 1) * HEAD_DIM)
        st.append(fold(nn(parts(qp[:, cols], 3), qkv[wide + cols.start : wide + cols.stop]), 3))
    st = jnp.concatenate(st, axis=0) * (1.0 / math.sqrt(HEAD_DIM))
    table = prow[...].reshape(rows * total, C)
    scores = fold(nt(parts(st, 3), table), 3)
    for r in range(rows):
        cols = slice(r * total, (r + 1) * total)
        live = place < len_ref[r]
        s = jnp.where(live, scores[:, cols], MASKED_SCORE)
        e = jnp.where(live, jnp.exp(s - jnp.max(s, axis=1, keepdims=True)), 0.0)
        p = e / jnp.sum(e, axis=1, keepdims=True)
        probs_ref[:, cols] = p
        for g in range(heads):
            abd[8 * g + r : 8 * g + r + 1, cols] = jnp.sum(
                p[g * QUERIES : (g + 1) * QUERIES], axis=0, keepdims=True
            )
    u = fold(nn(parts(abd[...], 2), table), 2)
    u_ref[...] = u
    pooled_ref[...] = jnp.zeros(pooled_ref.shape, F32)
    for g in range(heads):
        first = 2 * wide + g * HEAD_DIM
        v = parts(u[8 * g : 8 * g + 8] * (1.0 / QUERIES), 2)
        pooled_ref[0:8, g * HEAD_DIM : (g + 1) * HEAD_DIM] = fold(
            nt(v, qkv[first : first + HEAD_DIM]), 2
        )


def stats_kernel(
    csh, heads, rows, seg_ref, x_ref, apack_ref, out_ref, dfilm_ref, pooled_ref, memory_ref, scratch
):
    count = x_ref.shape[0]
    wide = heads * HEAD_DIM
    seg = seg_ref[...]
    scratch[...] = jnp.zeros(scratch.shape, F32)
    for s in range(count):
        group, part = s // 2, s % 2
        scratch[part * rows : (part + 1) * rows, group * wide : (group + 1) * wide] = x_ref[
            s, 2 * RP : 2 * RP + rows, 0:wide
        ]
    pooled = scratch[...].astype(BF16)
    pooled_ref[...] = pooled
    memory = nn(pooled, apack_ref[:, 0:C]).astype(BF16)
    memory_ref[...] = memory
    film = nn(memory, apack_ref[:, C : C + 2 * csh])
    f0 = film[:, 0:csh]
    f1 = film[:, csh : 2 * csh]
    total = [x_ref[s, 0:RP, 0:csh] for s in range(count)]
    second = [x_ref[s, RP : 2 * RP, 0:csh] for s in range(count)]
    dsum = [x_ref[s, 0:RP, csh : 2 * csh] for s in range(count)]
    cross = [x_ref[s, RP : 2 * RP, csh : 2 * csh] for s in range(count)]
    means = [v * (1.0 / LANES) for v in total]
    d0 = jnp.zeros((RP, csh), F32)
    d1 = jnp.zeros((RP, csh), F32)
    for me in range(count):
        same = [(seg[:, s : s + 1] == seg[:, me : me + 1]).astype(F32) for s in range(count)]
        frames = sum(same) * float(LANES)
        inv = 1.0 / frames
        mean = sum(m * v for m, v in zip(same, total)) * inv
        var = (
            sum(
                m * (v + float(LANES) * (u - mean) * (u - mean))
                for m, v, u in zip(same, second, means)
            )
            * inv
        )
        scale = lax.rsqrt(var + NORM_EPS)
        dtot = sum(m * v for m, v in zip(same, dsum))
        xtot = sum(m * (v + (u - mean) * d) for m, v, u, d in zip(same, cross, means, dsum)) * scale
        mean_part = f0 * dtot * inv
        cross_part = f0 * xtot * inv
        slope = scale * scale * cross_part
        out_ref[me, 0:RP, 0:csh] = 1.0 + f0 * scale
        out_ref[me, RP : 2 * RP, 0:csh] = f1 - f0 * scale * mean
        out_ref[me, 0:RP, csh : 2 * csh] = -slope
        out_ref[me, RP : 2 * RP, csh : 2 * csh] = slope * mean - scale * mean_part
        d0 = d0 + (cross[me] + (means[me] - mean) * dsum[me]) * scale
        d1 = d1 + dsum[me]
    dfilm = jnp.concatenate([d0, d1], axis=1).astype(BF16)
    dfilm_ref[...] = dfilm
    dmem = nt(dfilm, apack_ref[:, C : C + 2 * csh])
    dpool = nt(dmem.astype(BF16), apack_ref[:, 0:C])
    for s in range(count):
        group, part = s // 2, s % 2
        rolled = pltpu.roll(dpool, RP - part * rows, 0) if part else dpool
        out_ref[s, 2 * RP : 3 * RP, 0:csh] = dmem[:, s * csh : (s + 1) * csh]
        out_ref[s, 2 * RP : 3 * RP, csh : 2 * csh] = jnp.zeros((RP, csh), F32)
        out_ref[s, 3 * RP : 4 * RP] = rolled[:, group * wide : (group + 1) * wide]


def coef_columns(csh, coef_ref, rows_ref, cols_ref):
    rows_ref[...] = jnp.zeros(rows_ref.shape, F32)
    for s in range(C // csh):
        cols = slice(s * csh, (s + 1) * csh)
        rows_ref[0 : 2 * RP, cols] = coef_ref[s, 0 : 2 * RP, 0:csh]
        rows_ref[2 * RP : 4 * RP, cols] = coef_ref[s, 0 : 2 * RP, csh : 2 * csh]
    cols_ref[...] = rows_ref[...].T


def skip_grad_kernel(gated_ref, dskip_ref, out_ref, right):
    for r in range(dskip_ref.shape[0]):
        right[:, r * LANES : (r + 1) * LANES] = dskip_ref[r]
    out_ref[...] = nt(gated_ref[...], right[...]).astype(BF16)


def backward_kernel(meta, dp, csh, gates, order_ref, off_ref, coef_ref, mid_ref, dout_ref, dskip_ref, fa_ref, fb_ref, inp_ref, gated_ref, gskip_ref, flags_ref, *refs):
    turned, refs = refs[: len(meta)], refs[len(meta) :]
    dpre_ref, dres_ref, sums_ref, refs = refs[0], refs[1], refs[2], refs[3:]
    outs, refs = (refs[0:2], refs[2:4]), refs[4:]
    rows_ref, cols_ref, w_ref, both_ref, dpt_ref, drt_ref, sems = refs
    cs = C // dp
    span = NR * LANES
    i = pl.program_id(0)

    @pl.when(i == 0)
    def _():
        copies = turned_copies(
            meta, turned, off_ref, cs, None, ((w_ref, 0), (w_ref, C), None), sems
        )
        begin(copies)
        coef_columns(csh, coef_ref, rows_ref, cols_ref)
        sums_ref[...] = jnp.zeros(sums_ref.shape, F32)
        finish(copies)

    @pl.when(i < gates)
    def _():
        coef = pltpu.roll(cols_ref[...], lax.rem(LANES - NR * i, LANES), 1)
        for j in range(NR):
            cols = slice(j * LANES, (j + 1) * LANES)
            mf = mid_ref[:, cols].astype(F32)
            df = dout_ref[j].astype(F32)
            a = coef[:, j : j + 1]
            be = coef[:, 2 * RP + j : 2 * RP + j + 1]
            ga = coef[:, 3 * RP + j : 3 * RP + j + 1]
            dmid = (a * df + (be * mf + ga)).astype(BF16).astype(F32)
            both_ref[0:C, cols] = (dmid * SQRT_HALF).astype(BF16)
            both_ref[C : 2 * C, cols] = dskip_ref[j]
        dres = both_ref[0:C]
        dres_ref[...] = dres
        dg = nn(w_ref[...], both_ref[...])
        dt = (dg * fa_ref[...].astype(F32)).astype(BF16)
        ds = (dg * fb_ref[...].astype(F32)).astype(BF16)
        dpre_ref[0:C] = dt
        dpre_ref[C : 2 * C] = ds
        at = pl.ds(pl.multiple_of(i * span, span), span)
        dpt_ref[at, 0:C] = dt.T
        dpt_ref[at, C : 2 * C] = ds.T
        drt_ref[at] = dres.T
        frame = lax.broadcasted_iota(jnp.int32, (span, LANES), 0)
        column = lane_ids((span, LANES))
        place = frame % LANES
        which = frame // LANES
        keep_l = jnp.zeros((span, LANES), jnp.int32)
        keep_r = jnp.zeros((span, LANES), jnp.int32)
        for j in range(NR):
            keep_l = jnp.where(which == j, flags_ref[0, NR * i + j], keep_l)
            keep_r = jnp.where(which == j, flags_ref[1, NR * i + j], keep_r)
        row = NR * i + which
        use0 = (column == row) & ((place >= SHIFT) | (keep_l > 0))
        use1 = column == RP + row
        use2 = (column == 2 * RP + row) & ((place < LANES - SHIFT) | (keep_r > 0))
        pick = jnp.where(use0 | use1 | use2, 1.0, 0.0).astype(BF16)
        sums_ref[...] = sums_ref[...] + nn(dpre_ref[...], pick)

    @pl.when(i >= gates)
    def _():
        g = nn(inp_ref[...], dpt_ref[...]).astype(BF16)
        h = nn(gated_ref[...], drt_ref[...]).astype(BF16)
        k = i - gates
        for parity, (one, two) in enumerate(outs):

            @pl.when(lax.rem(k, 2) == parity)
            def _():
                for t in range(4):
                    rows = slice(t * cs, (t + 1) * cs)
                    lanes = slice(t * LANES, (t + 1) * LANES)
                    one[0, rows, 0:LANES] = h[:, lanes]
                    one[0, rows, LANES : 2 * LANES] = gskip_ref[:, lanes]
                one[0, :, 2 * LANES :] = g[:, 0:EARLY]
                two[0] = g[:, EARLY:]


def step_grad_kernel(meta, dp, off_ref, sums_ref, emb_ref, *refs):
    turned, refs = refs[: len(meta)], refs[len(meta) :]
    keep_ref, give_ref, wt_ref, scr, sems = refs
    cs = C // dp
    copies = turned_copies(meta, turned, off_ref, cs, wt_ref, (None,) * 3, sems)
    begin(copies)
    sums = sums_ref[...].T
    emb = emb_ref[...].T
    finish(copies)
    total = jnp.zeros((RP, 4 * C), F32)
    lane = lane_ids((RP, 4 * C))
    all_taps = fold(nn(parts(sums[0 : 3 * RP], 2), wt_ref[...]), 2)
    for t in range(3):
        g = all_taps[t * RP : (t + 1) * RP]
        total = total + jnp.where((lane // cs) % 4 == t, g, 0.0)
    out = []
    for d in range(dp):
        block = total[:, d * 4 * cs : (d + 1) * 4 * cs]
        out.append(block[:, 0:cs] + block[:, cs : 2 * cs] + block[:, 2 * cs : 3 * cs])
    g = jnp.concatenate(out, axis=1)
    g = jnp.concatenate([g, jnp.zeros((LANES - RP, C), F32)], axis=0)
    hi = g.astype(BF16)
    lo = (g - hi.astype(F32)).astype(BF16)
    scr[...] = nn(emb, hi) + nn(emb, lo)
    for k in range(dp):
        v = scr[pl.ds(pl.multiple_of(off_ref[k], 16), cs)].astype(BF16)
        for t in range(4):
            (keep_ref, give_ref)[k % 2][k // 2, t * cs : (t + 1) * cs] = v[
                :, t * LANES : (t + 1) * LANES
            ]


def input_grad_kernel(meta, dp, off_ref, dpre_ref, dres_ref, *refs):
    turned, refs = refs[: len(meta)], refs[len(meta) :]
    base_ref, first_ref, last_ref, wt_ref, w_ref, facc_ref, lacc_ref, sems = refs
    cs = C // dp
    i = pl.program_id(0)
    lane = lane_ids((C, LANES))

    @pl.when(i == 0)
    def _():
        copies = turned_copies(meta, turned, off_ref, cs, wt_ref, (None,) * 3, sems)
        begin(copies)
        facc_ref[...] = jnp.zeros((C, LANES), F32)
        lacc_ref[...] = jnp.zeros((C, LANES), F32)
        finish(copies)
        for d in range(dp):
            v = wt_ref[:, d * 4 * cs : (d + 1) * 4 * cs].T
            for t in range(3):
                w_ref[t, d * cs : (d + 1) * cs] = v[t * cs : (t + 1) * cs]

    dpre = dpre_ref[...]
    y0 = nn(w_ref[0], dpre)
    y1 = nn(w_ref[1], dpre)
    y2 = nn(w_ref[2], dpre)
    facc = facc_ref[...]
    lacc = lacc_ref[...]
    for j in range(NR):
        r = NR * i + j
        cols = slice(j * LANES, (j + 1) * LANES)
        z0 = pltpu.roll(y0[:, cols], LANES - SHIFT, 1)
        z2 = pltpu.roll(y2[:, cols], SHIFT, 1)
        inner0 = lane < LANES - SHIFT
        inner2 = lane >= SHIFT
        v = y1[:, cols]
        base_ref[:, cols] = (
            v
            + jnp.where(inner0, z0, 0.0)
            + jnp.where(inner2, z2, 0.0)
            + dres_ref[:, cols].astype(F32)
        ).astype(BF16)
        here = (lane // SHIFT) == r
        facc = jnp.where(here, pltpu.roll(z0, lax.rem(SHIFT * r + SHIFT, LANES), 1), facc)
        lacc = jnp.where(here, pltpu.roll(z2, SHIFT * r, 1), lacc)
    facc_ref[...] = facc
    lacc_ref[...] = lacc

    @pl.when(i == pl.num_programs(0) - 1)
    def _():
        first_ref[...] = facc.astype(BF16)
        last_ref[...] = lacc.astype(BF16)


def finish_kernel(csh, flags_ref, base_ref, left_ref, right_ref, mid_ref, coef_ref, out_ref, layer_ref, rows_ref, cols_ref):
    i = pl.program_id(0)
    lane = lane_ids((C, LANES))

    @pl.when(i == 0)
    def _():
        coef_columns(csh, coef_ref, rows_ref, cols_ref)

    coef = pltpu.roll(cols_ref[...], lax.rem(LANES - NR * i, LANES), 1)
    left = left_ref[...].astype(F32)
    right = right_ref[...].astype(F32)
    for j in range(NR):
        r = NR * i + j
        cols = slice(j * LANES, (j + 1) * LANES)
        lh = pltpu.roll(left, lax.rem(LANES - SHIFT * r, LANES), 1)
        rh = pltpu.roll(right, LANES - SHIFT - SHIFT * r, 1)
        lh = jnp.where((lane < SHIFT) & (flags_ref[0, r] > 0), lh, 0.0)
        rh = jnp.where((lane >= LANES - SHIFT) & (flags_ref[1, r] > 0), rh, 0.0)
        out_ref[j] = (base_ref[:, cols].astype(F32) + lh + rh).astype(BF16)
        a = coef[:, j : j + 1]
        b = coef[:, RP + j : RP + j + 1]
        layer_ref[j] = (a * mid_ref[:, cols].astype(F32) + b).astype(BF16)


def add_blocks_kernel(count, *refs):
    ins, (keep_ref, give_ref) = refs[: 2 * count], refs[2 * count :]
    at = 0
    for p in range(count):
        a_ref, b_ref = ins[2 * p : 2 * p + 2]
        width = a_ref.shape[2]
        for j in range(a_ref.shape[0]):
            v = a_ref[j].astype(F32) + b_ref[j].astype(F32)
            (keep_ref, give_ref)[j % 2][j // 2, :, at : at + width] = v.astype(BF16)
        at += width


def add_pair_kernel(count, side_ref, *refs):
    ins, out_ref = refs[: 2 * count], refs[2 * count]
    at = 0
    for p in range(count):
        a_ref, b_ref = ins[2 * p : 2 * p + 2]
        lanes = slice(at, at + a_ref.shape[2])
        own = a_ref[0].astype(F32) + b_ref[0].astype(F32)
        far = a_ref[1].astype(F32) + b_ref[1].astype(F32)
        first = side_ref[0] == 0
        out_ref[0, :, lanes] = jnp.where(first, own, far).astype(BF16)
        out_ref[1, :, lanes] = jnp.where(first, far, own).astype(BF16)
        at += a_ref.shape[2]


def add_pieces_kernel(a_ref, out_ref):
    v = a_ref[0].astype(F32) + a_ref[1].astype(F32)
    size = out_ref.shape[1]
    for p in range(out_ref.shape[0]):
        out_ref[p] = v[p * size : (p + 1) * size].astype(BF16)


def sum_copies_kernel(a_ref, *refs):
    out_ref = refs[-1]
    v = a_ref[0].astype(F32)
    for p in range(1, a_ref.shape[0]):
        v = v + a_ref[p].astype(F32)
    v = v.astype(BF16)
    for p in range(out_ref.shape[0]):
        out_ref[p, :, 0 : v.shape[1]] = v
        if len(refs) > 1:
            out_ref[p, :, v.shape[1] :] = refs[0][...]


def small_sum_kernel(csh, wide, bit_ref, got_ref, film_ref, attn_ref, mine_ref, other_ref, turn):
    v = got_ref[0].astype(F32) + got_ref[1].astype(F32)
    cs = v.shape[0]
    film = 2 * wide + csh
    turn[...] = jnp.zeros(turn.shape, F32)
    turn[0:cs, 0 : 2 * csh] = v[:, film : film + 2 * csh]
    film_ref[...] = turn[...].T[0 : 2 * csh, 0:cs]
    attn_ref[...] = v[:, 2 * wide : film]
    last = film + 2 * csh
    even = bit_ref[0] == 0
    for one, two, rows, width in (
        (v[:, 0:wide], v[:, wide : 2 * wide], slice(0, cs), wide),
        (
            v[0:QUERIES, last : last + wide // 2],
            v[0:QUERIES, last + wide // 2 : last + wide],
            slice(cs, cs + QUERIES),
            wide // 2,
        ),
    ):
        mine_ref[rows, 0:width] = jnp.where(even, one, two).astype(BF16)
        other_ref[rows, 0:width] = jnp.where(even, two, one).astype(BF16)
    mine_ref[cs:, wide // 2 :] = jnp.zeros((QUERIES, wide // 2), BF16)
    other_ref[cs:, wide // 2 :] = jnp.zeros((QUERIES, wide // 2), BF16)


def small_piece_kernel(csh, wide, attn_ref, mine_ref, got_ref, out_ref):
    v = mine_ref[...].astype(F32) + got_ref[...].astype(F32)
    attn = attn_ref[...]
    cs = attn.shape[0]
    rows = out_ref.shape[0]
    at = 0
    for row in range(0, cs, rows):
        out_ref[:, at : at + wide] = v[row : row + rows].astype(BF16)
        out_ref[:, at + wide : at + wide + csh] = attn[row : row + rows].astype(BF16)
        at += wide + csh
    for row in range(0, QUERIES, rows):
        block = v[cs + row : cs + min(row + rows, QUERIES), 0 : wide // 2]
        if block.shape[0] < rows:
            pad = jnp.zeros((rows - block.shape[0], wide // 2), F32)
            block = jnp.concatenate([block, pad], axis=0)
        out_ref[:, at : at + wide // 2] = block.astype(BF16)
        at += wide // 2


def output_kernel(
    cs,
    csh,
    wide,
    seq,
    bit_ref,
    *refs,
):
    own1, got1, all2, refs = *refs[:3], refs[3:]
    (
        queries_ref,
        wq_ref,
        step_ref,
        conv_ref,
        cond_ref,
        res_ref,
        skip_ref,
        gqueries_ref,
        gquery_ref,
        key_ref,
        value_ref,
        attn_ref,
        scr1,
        scr2,
        small,
        qscr,
        dq,
    ) = refs
    count, size = own1.shape[0], own1.shape[1]
    wide2 = scr2.shape[1]
    bit = bit_ref[0]
    for one, side in ((own1, bit), (got1, 1 - bit)):
        for p in range(count):
            rows = pl.ds(pl.multiple_of((2 * p + side) * size, 8), size)
            scr1[rows] = one[p].astype(F32)
    for s in range(seq):
        at = s * size
        v = all2[s].astype(F32)
        scr2[at : at + size] = v[:, 0:wide2]
        small[s * size : (s + 1) * size] = v[:, wide2:]
    for t in range(4):
        rows = slice(t * cs, (t + 1) * cs)
        lanes = slice(t * LANES, (t + 1) * LANES)
        res_ref[:, lanes] = scr1[rows, 0:LANES]
        skip_ref[:, lanes] = scr1[rows, LANES : 2 * LANES]
        rest = 2 * C - EARLY
        step_ref[:, lanes] = scr2[rows, rest : rest + LANES]
        if t < 3:
            conv_ref[t, :, 0:EARLY] = scr1[rows, 2 * LANES : 2 * LANES + EARLY]
            conv_ref[t, :, EARLY:] = scr2[rows, 0:rest]
        else:
            cond_ref[:, 0:EARLY] = scr1[rows, 2 * LANES : 2 * LANES + EARLY]
            cond_ref[:, EARLY:] = scr2[rows, 0:rest]
    dq[...] = jnp.zeros(dq.shape, F32)
    for s in range(seq):
        v = small[s * size : (s + 1) * size]
        group, even = s // 2, s % 2 == 0
        out = key_ref if even else value_ref
        at = 0
        for row in range(0, cs, size):
            out[row : row + size, group * wide : (group + 1) * wide] = v[:, at : at + wide]
            attn_ref[row : row + size, s * csh : (s + 1) * csh] = v[:, at + wide : at + wide + csh]
            at += wide + csh
        first = group * wide + (0 if even else wide // 2)
        for row in range(0, QUERIES, size):
            count = min(size, QUERIES - row)
            dq[row : row + count, first : first + wide // 2] = v[0:count, at : at + wide // 2]
            at += wide // 2
    qscr[...] = jnp.zeros((LANES, LANES), F32)
    qscr[0:QUERIES, 0:cs] = queries_ref[...].astype(F32)
    qt = qscr[...].T.astype(BF16)
    d = dq[...]
    hi = d.astype(BF16)
    lo = (d - hi.astype(F32)).astype(BF16)
    gquery_ref[...] = (nn(qt, hi) + nn(qt, lo))[0:cs]
    gqueries_ref[...] = fold(nt(parts(d[0:QUERIES], 2), wq_ref[...]), 2)


def attention_back_kernel(
    rows,
    csh,
    dp,
    off_ref,
    prow,
    probs_ref,
    u_ref,
    qp_ref,
    qkv_ref,
    pooled_ref,
    memory_ref,
    dfilm_ref,
    got_ref,
    keep_ref,
    give_ref,
    ds,
    stack,
    right,
    out,
):
    count = got_ref.shape[0]
    total = prow.shape[1] * prow.shape[2]
    cs = C // dp
    table = prow[...].reshape(rows * total, C)
    wide = qp_ref.shape[1]
    heads = wide // HEAD_DIM
    datt = got_ref[0, 3 * RP : 4 * RP, 0:wide]
    dmem = got_ref[0, 2 * RP : 3 * RP, 0:csh]
    for s in range(1, count):
        datt = datt + got_ref[s, 3 * RP : 4 * RP, 0:wide]
        dmem = dmem + got_ref[s, 2 * RP : 3 * RP, 0:csh]
    datt = datt[0:8] * (1.0 / QUERIES)
    vh = []
    for g in range(heads):
        first = 2 * wide + g * HEAD_DIM
        v = parts(datt[:, g * HEAD_DIM : (g + 1) * HEAD_DIM], 2)
        vh.append(fold(nn(v, qkv_ref[first : first + HEAD_DIM]), 2))
    vh = jnp.concatenate(vh, axis=0)
    dp_all = fold(nt(parts(vh, 2), table), 2)
    for r in range(rows):
        cols = slice(r * total, (r + 1) * total)
        for g in range(heads):
            mine = slice(g * QUERIES, (g + 1) * QUERIES)
            p = probs_ref[mine, cols]
            dpr = dp_all[8 * g + r : 8 * g + r + 1, cols]
            inner = jnp.sum(p * dpr, axis=1, keepdims=True)
            ds[mine, cols] = p * (dpr - inner)
    tt = fold(nn(parts(ds[...], 2), table), 2)
    scale = 1.0 / math.sqrt(HEAD_DIM)
    dq = []
    stack[...] = jnp.zeros(stack.shape, F32)
    right[...] = jnp.zeros(right.shape, F32)
    stack[0 : heads * QUERIES] = tt
    stack[64:80] = u_ref[...]
    stack[80:96] = pooled_ref[...].astype(F32)
    stack[96:112] = memory_ref[...].astype(F32)
    for g in range(heads):
        cols = slice(g * HEAD_DIM, (g + 1) * HEAD_DIM)
        mine = slice(g * QUERIES, (g + 1) * QUERIES)
        wk = qkv_ref[wide + g * HEAD_DIM : wide + (g + 1) * HEAD_DIM]
        dq.append(fold(nt(parts(tt[mine], 2), wk), 2) * scale)
        right[mine, cols] = qp_ref[:, cols] * scale
        right[64 + 8 * g : 72 + 8 * g, wide + cols.start : wide + cols.stop] = datt[:, cols]
    right[80:96, 2 * wide : 2 * wide + csh] = dmem
    right[96:112, 2 * wide + csh : 2 * wide + 3 * csh] = dfilm_ref[...].astype(F32)
    out[...] = lax.dot_general(
        stack[...].T,
        right[...],
        (((1,), (0,)), ((), ())),
        precision=lax.Precision.HIGHEST,
        preferred_element_type=F32,
    )
    last = 2 * wide + 3 * csh
    for k in range(dp):
        ref = (keep_ref, give_ref)[k % 2]
        ref[k // 2] = out[pl.ds(pl.multiple_of(off_ref[k], 16), cs)].astype(BF16)
        for g in range(heads):
            first = last + g * HEAD_DIM
            ref[k // 2, 0:QUERIES, first : first + HEAD_DIM] = dq[g].astype(BF16)


def exchange(pieces, axis, groups=None):
    return lax.all_to_all(
        pieces, axis, split_axis=0, concat_axis=0, axis_index_groups=groups, tiled=True
    )


def flipped(v, axis, size, bit):
    return lax.ppermute(v, axis, [(d, d ^ bit) for d in range(size)])


class Reduction:
    def __init__(self, call, name, keep, give, dp, seq, side):
        self.call, self.name, self.dp, self.seq, self.side = call, name, dp, seq, side
        self.keep, self.flip = keep, 1
        self.got = flipped(give, "dp", dp, 1)

    def over_blocks(self, after=(), others=()):
        while 2 * self.flip < self.dp:
            group = (self,) + tuple(others)
            others = ()
            args = []
            for part in group:
                args += [part.keep, Got(part.got)]
            rows, width = self.keep.shape[1], sum(part.keep.shape[2] for part in group)
            self.flip *= 2
            if 2 * self.flip < self.dp:
                half = sds((self.keep.shape[0] // 2, rows, width), BF16)
                self.keep, give = self.call(
                    functools.partial(add_blocks_kernel, len(group)),
                    (half, half),
                    "blocks_" + self.name,
                    args,
                    after=after,
                    in_specs=[VM] * len(args),
                    out_specs=(VM, VM),
                )
                self.got = flipped(give, "dp", self.dp, self.flip)
        pair = self.call(
            functools.partial(add_pair_kernel, len(group)),
            sds((2, rows, width), BF16),
            "blocks_" + self.name,
            [self.side] + args,
            after=after,
            in_specs=[SM] + [VM] * len(args),
            out_specs=VM,
        )
        far = self.dp // 2
        self.got = exchange(pair, "dp", [[k, k + far] for k in range(far)])
        self.rest = (rows, width)

    def over_pieces(self, after=()):
        rows, width = self.rest
        pieces = self.call(
            add_pieces_kernel,
            sds((self.seq, rows // self.seq, width), BF16),
            "pieces_" + self.name,
            (Got(self.got),),
            after=after,
            in_specs=[VM],
            out_specs=VM,
        )
        self.got = exchange(pieces, "seq")

    def over_copies(self, after=(), extra=None):
        args, (count, rows, width) = [Got(self.got)], self.got.shape
        if extra is None:
            count = self.seq // 2
        if extra is not None:
            args.append(extra)
            width += extra.shape[1]
        copies = self.call(
            sum_copies_kernel,
            sds((count, rows, width), BF16),
            "copies_" + self.name,
            args,
            after=after,
            in_specs=[VM] * len(args),
            out_specs=VM,
        )
        if extra is not None:
            return (Got(exchange(copies, "seq")),)
        groups = [[2 * k + b for k in range(count)] for b in range(2)]
        own = exchange(copies, "seq", groups)
        return Got(own), Got(flipped(own, "seq", self.seq, 1))


def body(
    dp,
    seq,
    x_in,
    cond,
    segment_ids,
    diffusion_steps,
    prompt,
    prompt_lengths,
    w_step,
    w_conv,
    w_cond,
    w_res,
    w_skip,
    queries,
    w_query,
    w_key,
    w_value,
    w_attn_out,
    w_film,
    d_out,
    d_skip,
):
    call = Caller()
    rows = x_in.shape[0]
    frames = x_in.shape[2]
    steps = rows // NR
    cols = rows * frames
    cs = C // dp
    csh = C // seq
    heads = 2 * HEADS // seq
    wide = heads * HEAD_DIM
    arows = rows // 2
    pl_local = prompt.shape[1]
    prompt_all = pl_local * seq
    sidx = lax.axis_index("seq")
    didx = lax.axis_index("dp")
    group = (sidx // 2).astype(jnp.int32).reshape(1)
    bit = (sidx % 2).astype(jnp.int32).reshape(1)
    up = [(i, i + 1) for i in range(seq - 1)]
    down = [(i + 1, i) for i in range(seq - 1)]
    order = jnp.bitwise_xor(didx, jnp.arange(dp, dtype=jnp.int32)).astype(jnp.int32)
    offsets = jnp.concatenate([order * cs, bit, 1 - bit])
    far_side = (didx // (dp // 2)).astype(jnp.int32).reshape(1)

    def gather(pack, side=None, middle=None):
        if dp == 4 and side is not None:
            mine = flipped(side, "dp", dp, 2)
            inner = flipped(middle, "dp", dp, 2)
            other = flipped(mine, "seq", seq, 1)
            near = [(0, None, pack), (2, 0, mine), (2, 2, inner), (2, 1, other)]
            pieces = near + [(k + 1, h, flipped(v, "dp", dp, 1)) for k, h, v in near]
        else:
            pieces = [(0, None, pack)]
            flip = dp // 2
            while flip:
                pieces += [(k + flip, h, flipped(v, "dp", dp, flip)) for k, h, v in pieces]
                flip //= 2
        pieces.sort(key=lambda piece: piece[0])
        meta = [(k, h) for k, h, _ in pieces]
        return meta, [v if k == 0 else Got(v) for k, _, v in pieces]

    off_qkv = C + 2 * csh
    qkv_rows = -(-(3 * wide + QUERIES) // LANES) * LANES
    head_width = -(-(off_qkv + qkv_rows) // LANES) * LANES
    pack, mine, other = call(
        functools.partial(head_pack_kernel, csh, wide),
        (
            sds((cs, head_width), BF16),
            sds((arows, pl_local, C), BF16),
            sds((arows, pl_local, C), BF16),
        ),
        "head_pack",
        (
            group,
            bit,
            w_attn_out,
            jnp.transpose(w_film, (1, 2, 0)).reshape(2 * csh, cs),
            w_query,
            w_key,
            w_value,
            queries,
            prompt,
        ),
        in_specs=[SM, SM] + [VM] * 7,
        out_specs=(VM,) * 3,
        scratch_shapes=[pltpu.VMEM((2 * LANES, LANES), F32)],
    )
    _, head_pieces = gather(pack)
    partner = flipped(other, "seq", seq, 1)
    first, last = call(
        edge_kernel,
        (sds((C, LANES), BF16), sds((C, LANES), BF16)),
        "edges",
        (x_in,),
        after=("head_pack",),
        in_specs=[VM],
        out_specs=(VM, VM),
    )
    left_halo = lax.ppermute(last, "seq", up)
    right_halo = lax.ppermute(first, "seq", down)
    pair = call(
        pair_kernel,
        sds((seq // 2, 2, arows, pl_local, C), BF16),
        "pair",
        (mine, Got(partner)),
        after=("edges",),
        in_specs=[VM, VM],
        out_specs=VM,
    )
    middle = 2 * C - 2 * SIDE + 3 * C // 4
    pack, side, middle = call(
        functools.partial(turned_pack_kernel, cs),
        (
            sds((2 * SIDE + middle, 4 * cs), BF16),
            sds((SIDE, 4 * cs), BF16),
            sds((middle, 4 * cs), BF16),
        ),
        "turned_pack",
        (bit, w_conv, w_cond, w_res, w_skip, w_step),
        after=("pair",),
        in_specs=[SM] + [VM] * 5,
        out_specs=(VM, VM, VM),
        scratch_shapes=[pltpu.VMEM((4 * cs, 2 * C), BF16)],
    )
    meta, turned = gather(pack, side, middle)
    copies = 4 * dp * (1 + 3 * C // (4 * cs))
    z_groups = [[2 * k + b for k in range(seq // 2)] for b in range(2)]
    prompts = Got(exchange(pair, "seq", z_groups))
    block_ids = segment_ids[:, ::frames]
    padded_ids = jnp.pad(block_ids, ((0, 0), (1, 1)), constant_values=-1)
    mine = lax.dynamic_slice_in_dim(padded_ids, sidx, 3, 1)
    flags = jnp.stack([mine[:, 0] == mine[:, 1], mine[:, 2] == mine[:, 1]]).astype(jnp.int32)
    block_ids = jnp.pad(block_ids, ((0, RP - rows), (0, 0)))
    half = C // 2
    frequency = jnp.exp(jnp.arange(half, dtype=F32) * (-math.log(10000.0) / half))
    step_rows = jnp.pad(diffusion_steps.astype(F32), (0, LANES - rows))
    live_rows = jnp.arange(LANES, dtype=jnp.int32)[:, None] < rows
    angles = step_rows[:, None] * frequency[None, :]
    embedding = jnp.concatenate([jnp.sin(angles), jnp.cos(angles)], axis=1)
    embedding = jnp.where(live_rows, embedding, 0.0).astype(BF16)
    flags, block_ids, embedding = call(
        table_kernel,
        (
            sds(flags.shape, jnp.int32),
            sds(block_ids.shape, jnp.int32),
            sds(embedding.shape, BF16),
        ),
        "tables",
        (flags, block_ids, embedding),
        after=("turned_pack", head_pieces[dp // 2].array, left_halo, right_halo),
        in_specs=[SM, VM, VM],
        out_specs=(SM, VM, VM),
    )

    lengths = lax.dynamic_slice_in_dim(prompt_lengths, (sidx % 2) * arows, arows, 0)

    apack, prow, probs, u, pooled_head, qp, qkv = call(
        functools.partial(attention_kernel, dp, arows, heads, seq // 2, off_qkv),
        (
            sds((C, head_width), BF16),
            sds((arows, seq, pl_local, C), BF16),
            sds((heads * QUERIES, arows * prompt_all), F32),
            sds((RP, C), F32),
            sds((RP, LANES), F32),
            sds((QUERIES, wide), F32),
            sds((qkv_rows, C), BF16),
        ),
        "attention",
        (offsets, bit, lengths, prompts, *head_pieces),
        in_specs=[SM, SM, SM, HB] + [HB] * dp,
        out_specs=(VM,) * 7,
        scratch_shapes=[
            pltpu.VMEM((RP, arows * prompt_all), F32),
            pltpu.SemaphoreType.DMA((dp + seq,)),
        ],
    )

    row_block = pl.BlockSpec((NR, C, LANES), lambda i: (i, 0, 0))

    def col_block(height):
        return pl.BlockSpec((height, NR * LANES), lambda i: (0, i))

    def still(shape):
        return pl.BlockSpec(shape, lambda i: (0,) * len(shape))

    inp, gated, factor_a, factor_b, skip_out, mid, stats = call(
        functools.partial(forward_kernel, meta, dp, csh),
        (
            sds((4 * C, cols), BF16),
            sds((C, cols), BF16),
            sds((C, cols), BF16),
            sds((C, cols), BF16),
            sds(x_in.shape, BF16),
            sds((C, cols), BF16),
            sds((seq, 3 * RP, 2 * csh), F32),
        ),
        "wavenet",
        (
            offsets,
            flags,
            x_in,
            cond,
            d_out,
            Got(left_halo),
            Got(right_halo),
            embedding,
            pooled_head,
            *turned,
        ),
        flops=2 * cols * (4 * C * 2 * C + 2 * C * C),
        nbytes=30e6,
        grid=(steps,),
        in_specs=[
            SM,
            SM,
            row_block,
            row_block,
            row_block,
            whole((C, LANES)),
            whole((C, LANES)),
            whole((LANES, C)),
            whole((RP, LANES)),
        ]
        + [HB] * len(turned),
        out_specs=(
            col_block(4 * C),
            col_block(C),
            col_block(C),
            col_block(C),
            row_block,
            col_block(C),
            still((seq, 3 * RP, 2 * csh)),
        ),
        scratch_shapes=[
            pltpu.VMEM((2 * C, 4 * C), BF16),
            pltpu.VMEM((C, 2 * C), BF16),
            pltpu.VMEM((C, C), BF16),
            pltpu.VMEM((2 * C, C), BF16),
            pltpu.VMEM((C, LANES), F32),
            pltpu.VMEM((C, LANES), F32),
            pltpu.SemaphoreType.DMA((copies,)),
        ],
    )
    stats_got = exchange(stats, "seq")
    gskip = call(
        skip_grad_kernel,
        sds((C, C), BF16),
        "skip",
        (gated, d_skip),
        in_specs=[VM, VM],
        out_specs=VM,
        scratch_shapes=[pltpu.VMEM((C, cols), BF16)],
    )

    coef_out, dfilm, pooled, memory = call(
        functools.partial(stats_kernel, csh, heads, arows),
        (
            sds((seq, 4 * RP, 2 * csh), F32),
            sds((RP, 2 * csh), BF16),
            sds((RP, C), BF16),
            sds((RP, C), BF16),
        ),
        "segments",
        (block_ids, Got(stats_got), apack),
        after=("skip",),
        in_specs=[VM, VM, VM],
        out_specs=(VM, VM, VM, VM),
        scratch_shapes=[pltpu.VMEM((RP, C), F32)],
    )
    coef = Got(exchange(coef_out, "seq"))

    def gate_block(i):
        return jnp.minimum(i, steps - 1)

    def shard(i):
        return jnp.maximum(i - steps, 0)

    def gate_cols(height):
        return pl.BlockSpec((height, NR * LANES), lambda i, order: (0, gate_block(i)))

    gate_rows = pl.BlockSpec((NR, C, LANES), lambda i, order: (gate_block(i), 0, 0))
    wide1, wide2 = EARLY + 2 * LANES, 2 * C - EARLY

    def part(width):
        return sds((dp // 2, 4 * cs, width), BF16)

    def part_spec(width):
        return pl.BlockSpec((1, 4 * cs, width), lambda i, order: (shard(i) // 2, 0, 0))

    outs = call(
        functools.partial(backward_kernel, meta, dp, csh, steps),
        (
            sds((2 * C, cols), BF16),
            sds((C, cols), BF16),
            sds((2 * C, LANES), F32),
            part(wide1),
            part(wide2),
            part(wide1),
            part(wide2),
        ),
        "backward",
        (order, offsets, coef, mid, d_out, d_skip, factor_a, factor_b, inp, gated, gskip, flags, *turned),
        prefetch=1,
        grid=(steps + dp,),
        in_specs=[
            SM,
            pl.BlockSpec(
                (seq, 4 * RP, 2 * csh), lambda i, order: (0, 0, 0), pipeline_mode=pl.Buffered(1)
            ),
            gate_cols(C),
            gate_rows,
            gate_rows,
            gate_cols(C),
            gate_cols(C),
            pl.BlockSpec((4 * cs, cols), lambda i, order: (order[shard(i)], 0)),
            pl.BlockSpec((cs, cols), lambda i, order: (order[shard(i)], 0)),
            pl.BlockSpec((cs, C), lambda i, order: (order[shard(i)], 0)),
            SM,
        ]
        + [HB] * len(turned),
        out_specs=(
            gate_cols(2 * C),
            gate_cols(C),
            pl.BlockSpec((2 * C, LANES), lambda i, order: (0, 0)),
            part_spec(wide1),
            part_spec(wide2),
            part_spec(wide1),
            part_spec(wide2),
        ),
        scratch_shapes=[
            pltpu.VMEM((LANES, C), F32),
            pltpu.VMEM((C, LANES), F32),
            pltpu.VMEM((C, 2 * C), BF16),
            pltpu.VMEM((2 * C, NR * LANES), BF16),
            pltpu.VMEM((cols, 2 * C), BF16),
            pltpu.VMEM((cols, C), BF16),
            pltpu.SemaphoreType.DMA((copies,)),
        ],
    )
    dpre, dres, sums = outs[0:3]
    part1 = Reduction(call, "1", outs[3], outs[5], dp, seq, far_side)
    part2 = Reduction(call, "2", outs[4], outs[6], dp, seq, far_side)
    part1.over_blocks()
    keep, give = call(
        functools.partial(step_grad_kernel, meta, dp),
        (part(LANES), part(LANES)),
        "step_grad",
        (offsets, sums, embedding, *turned),
        after=("blocks_1",),
        in_specs=[SM, VM, VM] + [HB] * len(turned),
        out_specs=(VM, VM),
        scratch_shapes=[
            pltpu.VMEM((2 * C, 4 * C), BF16),
            pltpu.VMEM((C, C), F32),
            pltpu.SemaphoreType.DMA((copies,)),
        ],
    )
    part_step = Reduction(call, "step", keep, give, dp, seq, far_side)

    right_width = -(-(3 * wide + 3 * csh) // LANES) * LANES
    block = sds((dp // 2, cs, right_width), BF16)
    keep, give = call(
        functools.partial(attention_back_kernel, arows, csh, dp),
        (block, block),
        "attention_back",
        (offsets, prow, probs, u, qp, qkv, pooled, memory, dfilm, coef),
        after=("step_grad",),
        in_specs=[SM] + [VM] * 9,
        out_specs=(VM, VM),
        scratch_shapes=[
            pltpu.VMEM((heads * QUERIES, arows * prompt_all), F32),
            pltpu.VMEM((LANES, C), F32),
            pltpu.VMEM((LANES, right_width), F32),
            pltpu.VMEM((C, right_width), F32),
        ],
    )
    small = Reduction(call, "small", keep, give, dp, seq, far_side)
    part2.over_blocks(("attention_back",), (part_step,))
    small.over_blocks(("blocks_2",))
    part1.over_pieces(("blocks_small",))
    part2.over_pieces(("pieces_1",))

    rest = 4 * cs // seq
    small_width = (cs // rest) * (wide + csh) + max(1, QUERIES // rest) * (wide // 2)
    grad_film, attn_rows, mine, other = call(
        functools.partial(small_sum_kernel, csh, wide),
        (
            sds((2 * csh, cs), F32),
            sds((cs, csh), F32),
            sds((cs + QUERIES, wide), BF16),
            sds((cs + QUERIES, wide), BF16),
        ),
        "small_sum",
        (bit, Got(small.got)),
        after=("pieces_2",),
        in_specs=[SM, VM],
        out_specs=(VM,) * 4,
        scratch_shapes=[pltpu.VMEM((LANES, LANES), F32)],
    )
    partner = flipped(other, "seq", seq, 1)
    ones = part1.over_copies(("small_sum",))
    small_piece = call(
        functools.partial(small_piece_kernel, csh, wide),
        sds((rest, small_width), BF16),
        "small_piece",
        (attn_rows, mine, Got(partner)),
        after=("copies_1",),
        in_specs=[VM] * 3,
        out_specs=VM,
    )
    twos = part2.over_copies(extra=small_piece)

    base, first, last = call(
        functools.partial(input_grad_kernel, meta, dp),
        (sds((C, cols), BF16), sds((C, LANES), BF16), sds((C, LANES), BF16)),
        "input_grad",
        (offsets, dpre, dres, *turned),
        after=("copies_2",),
        grid=(steps,),
        in_specs=[SM, col_block(2 * C), col_block(C)] + [HB] * len(turned),
        out_specs=(
            col_block(C),
            still((C, LANES)),
            still((C, LANES)),
        ),
        scratch_shapes=[
            pltpu.VMEM((2 * C, 4 * C), BF16),
            pltpu.VMEM((3, C, 2 * C), BF16),
            pltpu.VMEM((C, LANES), F32),
            pltpu.VMEM((C, LANES), F32),
            pltpu.SemaphoreType.DMA((copies,)),
        ],
    )
    from_left = lax.ppermute(last, "seq", up)
    from_right = lax.ppermute(first, "seq", down)
    grad_input, layer_out = call(
        functools.partial(finish_kernel, csh),
        (sds(x_in.shape, BF16), sds(x_in.shape, BF16)),
        "grad_input",
        (flags, base, Got(from_left), Got(from_right), mid, coef),
        after=("input_grad",),
        grid=(steps,),
        in_specs=[
            SM,
            col_block(C),
            whole((C, LANES)),
            whole((C, LANES)),
            col_block(C),
            whole((seq, 4 * RP, 2 * csh)),
        ],
        out_specs=(row_block, row_block),
        scratch_shapes=[pltpu.VMEM((LANES, C), F32), pltpu.VMEM((C, LANES), F32)],
    )

    (
        grad_step,
        grad_conv,
        grad_cond,
        grad_res,
        grad_skip,
        grad_queries,
        grad_query,
        grad_key,
        grad_value,
        grad_attn,
    ) = call(
        functools.partial(output_kernel, cs, csh, wide, seq),
        (
            sds((cs, C), F32),
            sds((3, cs, 2 * C), F32),
            sds((cs, 2 * C), F32),
            sds((cs, C), F32),
            sds((cs, C), F32),
            sds((QUERIES, cs), F32),
            sds((cs, C), F32),
            sds((cs, C), F32),
            sds((cs, C), F32),
            sds((cs, C), F32),
        ),
        "outputs",
        after=("grad_input",),
        args=(bit, *ones, *twos, queries, w_query),
        in_specs=[SM] + [VM] * 5,
        out_specs=(VM,) * 10,
        scratch_shapes=[
            pltpu.VMEM((4 * cs, wide1), F32),
            pltpu.VMEM((4 * cs, wide2 + LANES), F32),
            pltpu.VMEM((4 * cs, small_width), F32),
            pltpu.VMEM((LANES, LANES), F32),
            pltpu.VMEM((LANES, C), F32),
        ],
    )
    return (
        layer_out,
        skip_out,
        grad_input,
        grad_step,
        grad_conv,
        grad_cond,
        grad_res,
        grad_skip,
        grad_queries,
        grad_query,
        grad_key,
        grad_value,
        grad_attn,
        jnp.transpose(grad_film.reshape(2, csh, cs), (2, 0, 1)),
    )


def solution(mesh):
    frames = P("dp", None, "seq")
    matrix = P("dp", None)
    return jax.shard_map(
        functools.partial(body, mesh.shape["dp"], mesh.shape["seq"]),
        mesh=mesh,
        in_specs=(
            frames,
            frames,
            P("dp", None),
            P("dp"),
            P("dp", "seq", None),
            P("dp"),
            matrix,
            P(None, "dp", None),
            matrix,
            matrix,
            matrix,
            P(None, "dp"),
            matrix,
            matrix,
            matrix,
            matrix,
            frames,
            frames,
            frames,
        ),
        out_specs=(
            frames,
            frames,
            frames,
            matrix,
            P(None, "dp", None),
            matrix,
            matrix,
            matrix,
            P(None, "dp"),
            matrix,
            matrix,
            matrix,
            matrix,
            frames,
        ),
        check_vma=False,
    )
```

```python
import functools
import math

import jax
import jax.numpy as jnp
from jax import lax
from jax.experimental import pallas as pl
from jax.experimental.pallas import tpu as pltpu
from jax.sharding import PartitionSpec as P

C = 512
HEADS = 8
QUERIES = 32
HEAD_DIM = 64
SHIFT = 4
SQRT_HALF = 0.7071067811865476
NORM_EPS = 1e-05
MASKED_SCORE = -1e30
LANES = 128
RP = 16
NR = 4
EARLY = 640
F32 = jnp.float32
BF16 = jnp.bfloat16
VMEM_BYTES = 50 * 1024 * 1024


def nn(a, b):
    return lax.dot_general(a, b, (((1,), (0,)), ((), ())), preferred_element_type=F32)


def nt(a, b):
    return lax.dot_general(a, b, (((1,), (1,)), ((), ())), preferred_element_type=F32)


def parts(v, count):
    out = []
    for _ in range(count):
        low = v.astype(BF16).astype(F32)
        out.append(low)
        v = v - low
    return jnp.concatenate(out, axis=0).astype(BF16)


def fold(v, count):
    rows = v.shape[0] // count
    total = v[:rows]
    for k in range(1, count):
        total = total + v[k * rows : (k + 1) * rows]
    return total


def lane_ids(shape):
    return lax.broadcasted_iota(jnp.int32, shape, len(shape) - 1)


def sds(shape, dtype):
    return jax.ShapeDtypeStruct(shape, dtype)


VM = pl.BlockSpec(memory_space=pltpu.VMEM)
HB = pl.BlockSpec(memory_space=pl.ANY)
SM = pl.BlockSpec(memory_space=pltpu.SMEM)


def whole(shape):
    return pl.BlockSpec(shape, lambda i: (0,) * len(shape), pipeline_mode=pl.Buffered(1))


class Got:
    def __init__(self, array):
        self.array = array


class Caller:
    def __init__(self):
        self.done = {}

    def __call__(self, kernel, out_shape, name, args, flops=0, nbytes=0, prefetch=0, after=(), **kw):
        single = not isinstance(out_shape, tuple)
        shapes = (out_shape,) if single else out_shape
        specs = kw["out_specs"]
        specs = (specs,) if single else specs
        pinned = tuple(
            v if spec is SM else pltpu.HBM(v.shape, v.dtype) for v, spec in zip(shapes, specs)
        )
        in_specs = list(kw.pop("in_specs"))
        count = prefetch + len(in_specs)
        args = list(args)
        extra = len(after)
        for before in after:
            in_specs.append(HB)
            args.append(self.done[before] if isinstance(before, str) else before)

        def run(*refs):
            return kernel(*refs[:count], *refs[count + extra :])

        values = []
        for k, v in enumerate(args):
            spec = SM if k < prefetch else in_specs[k - prefetch]
            if isinstance(v, Got):
                values.append(v.array)
            elif spec is SM:
                values.append(v)
            else:
                values.append(pltpu.with_memory_space_constraint(v, pltpu.HBM))
        spec = pltpu.PrefetchScalarGridSpec(
            num_scalar_prefetch=prefetch,
            grid=kw.pop("grid", ()),
            in_specs=in_specs,
            out_specs=kw.pop("out_specs"),
            scratch_shapes=kw.pop("scratch_shapes", ()),
        )
        out = pl.pallas_call(
            run,
            out_shape=pinned[0] if single else pinned,
            name=name,
            grid_spec=spec,
            cost_estimate=pl.CostEstimate(
                flops=1, bytes_accessed=1, transcendentals=0
            ),
            compiler_params=pltpu.CompilerParams(vmem_limit_bytes=VMEM_BYTES),
        )(*values)
        self.done[name] = out if single else out[0]
        return out


def head_pack_kernel(
    csh,
    local,
    group_ref,
    bit_ref,
    attn_ref,
    film_ref,
    wq_ref,
    wk_ref,
    wv_ref,
    queries_ref,
    prompt_ref,
    out_ref,
    mine_ref,
    other_ref,
    scr,
):
    cs = attn_ref.shape[0]
    arows = mine_ref.shape[0]
    mine_ref[...] = prompt_ref[pl.ds(bit_ref[0] * arows, arows)]
    other_ref[...] = prompt_ref[pl.ds((1 - bit_ref[0]) * arows, arows)]
    out_ref[:, 0:C] = attn_ref[...]
    off = C
    scr[...] = jnp.zeros((2 * LANES, LANES), F32)
    scr[0 : 2 * csh, 0:cs] = film_ref[...].astype(F32)
    scr[LANES : LANES + QUERIES, 0:cs] = queries_ref[...].astype(F32)
    film = scr[0:LANES].T[0:cs]
    table = scr[LANES : 2 * LANES].T[0:cs]
    turn = lax.rem(C - local * group_ref[0], C)
    blocks = [film[:, 0 : 2 * csh]]
    for ref in (wq_ref, wk_ref, wv_ref):
        blocks.append(pltpu.roll(ref[...].astype(F32), turn, 1)[:, 0:local])
    blocks.append(table)
    for block in blocks:
        width = min(block.shape[1], out_ref.shape[1] - off)
        out_ref[:, off : off + width] = block[:, 0:width].astype(BF16)
        off += width
    if off < out_ref.shape[1]:
        out_ref[:, off:] = jnp.zeros((cs, out_ref.shape[1] - off), BF16)


SIDE = 480


def turned_pack_kernel(cs, bit_ref, conv_ref, cond_ref, res_ref, skip_ref, step_ref, out_ref, side_ref, middle_ref, scr):
    for k in range(3):
        scr[k * cs : (k + 1) * cs] = conv_ref[k]
    scr[3 * cs : 4 * cs] = cond_ref[...]
    turned = scr[...].T
    out_ref[0 : 2 * C - SIDE] = turned[0 : 2 * C - SIDE]
    at = 2 * C - SIDE
    for ref in (res_ref, skip_ref, step_ref):
        for lane in range(0, C, 4 * cs):
            out_ref[at : at + cs] = ref[:, lane : lane + 4 * cs]
            at += cs
    out_ref[at : at + SIDE] = turned[2 * C - SIDE :]
    middle_ref[...] = out_ref[SIDE:at]
    side_ref[...] = out_ref[pl.ds(pl.multiple_of(bit_ref[0] * at, 16), SIDE)]


def pair_kernel(a_ref, b_ref, out_ref):
    for p in range(out_ref.shape[0]):
        out_ref[p, 0] = a_ref[...]
        out_ref[p, 1] = b_ref[...]


def table_kernel(flags_ref, ids_ref, emb_ref, flags_out, ids_out, emb_out):
    for side in range(2):
        for r in range(flags_ref.shape[1]):
            flags_out[side, r] = flags_ref[side, r]
    ids_out[...] = ids_ref[...]
    emb_out[...] = emb_ref[...]


def edge_kernel(x_ref, first_ref, last_ref):
    rows = x_ref.shape[0]
    lane = lane_ids((C, LANES))
    first = jnp.zeros((C, LANES), F32)
    last = jnp.zeros((C, LANES), F32)
    for r in range(rows):
        v = x_ref[r].astype(F32)
        here = (lane // SHIFT) == r
        first = jnp.where(here, pltpu.roll(v, SHIFT * r, 1) if r else v, first)
        last = jnp.where(here, pltpu.roll(v, SHIFT * r + SHIFT, 1), last)
    first_ref[...] = first.astype(BF16)
    last_ref[...] = last.astype(BF16)


def begin(copies):
    for copy in copies:
        copy.start()


def finish(copies):
    for copy in copies:
        copy.wait()


def turned_copies(meta, refs, off_ref, cs, wt, others, sems):
    dp = len({k for k, _ in meta})
    pairs = []

    def conv(k, ref, first, row, rows):
        if wt is not None:
            lanes = pl.ds(pl.multiple_of(off_ref[k] * 4, LANES), 4 * cs)
            at = row if isinstance(row, int) else pl.multiple_of(row, 16)
            pairs.append((ref.at[pl.ds(first, rows)], wt.at[pl.ds(at, rows), lanes]))

    def rest(k, ref, at):
        row = pl.ds(pl.multiple_of(off_ref[k], 16), cs)
        for other in others:
            for lane in range(0, C, 4 * cs):
                if other is not None:
                    dst, start = other
                    pairs.append((ref.at[pl.ds(at, cs)], dst.at[row, pl.ds(start + lane, 4 * cs)]))
                at += cs

    inner = 2 * C - 2 * SIDE
    for (k, which), ref in zip(meta, refs):
        if which is None:
            conv(k, ref, 0, 0, SIDE + inner)
            rest(k, ref, SIDE + inner)
            conv(k, ref, ref.shape[0] - SIDE, 2 * C - SIDE, SIDE)
        elif which == 2:
            conv(k, ref, 0, SIDE, inner)
            rest(k, ref, inner)
        else:
            conv(k, ref, 0, off_ref[dp + which] * (2 * C - SIDE), SIDE)
    return [pltpu.make_async_copy(a, b, sems.at[n]) for n, (a, b) in enumerate(pairs)]


def head_copies(refs, off_ref, dst, sems):
    copies = []
    for k, ref in enumerate(refs):
        row = pl.ds(pl.multiple_of(off_ref[k], 16), ref.shape[0])
        copies.append(pltpu.make_async_copy(ref, dst.at[row], sems.at[k]))
    return copies


def forward_kernel(
    meta, dp, csh, off_ref, flags_ref, x_ref, cond_ref, dout_ref, left_ref, right_ref, emb_ref, pooled_ref, *refs
):
    turned, refs = refs[: len(meta)], refs[len(meta) :]
    (
        inp_ref,
        gated_ref,
        fa_ref,
        fb_ref,
        skip_ref,
        mid_ref,
        stats_ref,
        wt_ref,
        rn_ref,
        step_ref,
        rst_ref,
        lift_ref,
        acc_ref,
        sems,
    ) = refs
    cs = C // dp
    i = pl.program_id(0)
    lane = lane_ids((C, LANES))

    @pl.when(i == 0)
    def _():
        copies = turned_copies(
            meta,
            turned,
            off_ref,
            cs,
            wt_ref,
            ((rn_ref, 0), (rn_ref, C), (step_ref, 0)),
            sems,
        )
        begin(copies)
        acc_ref[...] = jnp.zeros((C, LANES), F32)
        finish(copies)
        lift = nn(emb_ref[0:RP], step_ref[...])
        lift = jnp.concatenate([lift, jnp.zeros((LANES - RP, C), F32)], axis=0)
        lift_ref[...] = lift.T
        rst_ref[...] = rn_ref[...].T

    lift = pltpu.roll(lift_ref[...], lax.rem(LANES - NR * i, LANES), 1)
    left = left_ref[...].astype(F32)
    right = right_ref[...].astype(F32)

    def put(tap, cols, value):
        for d in range(dp):
            at = d * 4 * cs + tap * cs
            inp_ref[at : at + cs, cols] = value[d * cs : (d + 1) * cs]

    for j in range(NR):
        r = NR * i + j
        lc = lift[:, j : j + 1]
        sh = (x_ref[j].astype(F32) + lc).astype(BF16)
        shf = sh.astype(F32)
        lh = pltpu.roll(left, lax.rem(LANES - SHIFT * r, LANES), 1)
        lh = jnp.where(flags_ref[0, r] > 0, (lh + lc).astype(BF16).astype(F32), 0.0)
        rh = pltpu.roll(right, LANES - SHIFT - SHIFT * r, 1)
        rh = jnp.where(flags_ref[1, r] > 0, (rh + lc).astype(BF16).astype(F32), 0.0)
        cols = slice(j * LANES, (j + 1) * LANES)
        put(0, cols, jnp.where(lane < SHIFT, lh, pltpu.roll(shf, SHIFT, 1)).astype(BF16))
        put(1, cols, sh)
        put(
            2,
            cols,
            jnp.where(lane >= LANES - SHIFT, rh, pltpu.roll(shf, LANES - SHIFT, 1)).astype(BF16),
        )
        put(3, cols, cond_ref[j])
    pre = nn(wt_ref[...], inp_ref[...])
    th = jnp.tanh(pre[:C])
    sg = jax.nn.sigmoid(pre[C:])
    gf = th * sg
    fa_ref[...] = (sg - gf * th).astype(BF16)
    fb_ref[...] = (gf * (1.0 - sg)).astype(BF16)
    g = gf.astype(BF16)
    gated_ref[...] = g
    rs = nn(rst_ref[...], g)
    acc = acc_ref[...]
    for j in range(NR):
        r = NR * i + j
        cols = slice(j * LANES, (j + 1) * LANES)
        skip_ref[j] = rs[C:, cols].astype(BF16)
        mid = ((x_ref[j].astype(F32) + rs[:C, cols]) * SQRT_HALF).astype(BF16)
        mid_ref[:, cols] = mid
        mf = mid.astype(F32)
        df = dout_ref[j].astype(F32)
        total = jnp.sum(mf, axis=1, keepdims=True)
        dev = mf - total * (1.0 / LANES)
        acc = jnp.where(lane == r, total, acc)
        acc = jnp.where(lane == RP + r, jnp.sum(dev * dev, axis=1, keepdims=True), acc)
        acc = jnp.where(lane == 2 * RP + r, jnp.sum(df, axis=1, keepdims=True), acc)
        acc = jnp.where(lane == 3 * RP + r, jnp.sum(df * dev, axis=1, keepdims=True), acc)
    acc_ref[...] = acc

    @pl.when(i == pl.num_programs(0) - 1)
    def _():
        t = acc.T
        for s in range(C // csh):
            cols = slice(s * csh, (s + 1) * csh)
            stats_ref[s, 0 : 2 * RP, 0:csh] = t[0 : 2 * RP, cols]
            stats_ref[s, 0 : 2 * RP, csh : 2 * csh] = t[2 * RP : 4 * RP, cols]
            stats_ref[s, 2 * RP : 3 * RP] = pooled_ref[:, 0 : 2 * csh]


def attention_kernel(dp, rows, heads, pairs, off, off_ref, bit_ref, len_ref, prompts, *refs):
    pieces, refs = refs[:dp], refs[dp:]
    apack_ref, prow, probs_ref, u_ref, pooled_ref, qp_ref, qkv_ref, abd, sems = refs
    copies = head_copies(pieces, off_ref, apack_ref, sems)
    count = len(copies)
    for j in range(pairs):
        for i in range(2):
            copies.append(
                pltpu.make_async_copy(
                    prompts.at[j, i], prow.at[:, 2 * j + i], sems.at[count + 2 * j + i]
                )
            )
    begin(copies)
    local = prow.shape[2]
    total = 2 * pairs * local
    abd[...] = jnp.zeros(abd.shape, F32)
    lane = lane_ids((heads * QUERIES, total))
    place = jnp.zeros((heads * QUERIES, total), jnp.int32)
    for k in range(2 * pairs):
        here = (k // 2) * 2 + (bit_ref[0] if k % 2 == 0 else 1 - bit_ref[0])
        place = jnp.where(lane // local == k, here * local + lane % local, place)
    finish(copies)
    wide = heads * HEAD_DIM
    qkv = apack_ref[:, off : off + qkv_ref.shape[0]].T
    qkv_ref[...] = qkv
    qp = nt(qkv[3 * wide : 3 * wide + QUERIES], qkv[0:wide])
    qp_ref[...] = qp
    st = []
    for g in range(heads):
        cols = slice(g * HEAD_DIM, (g + 1) * HEAD_DIM)
        st.append(fold(nn(parts(qp[:, cols], 3), qkv[wide + cols.start : wide + cols.stop]), 3))
    st = jnp.concatenate(st, axis=0) * (1.0 / math.sqrt(HEAD_DIM))
    table = prow[...].reshape(rows * total, C)
    scores = fold(nt(parts(st, 3), table), 3)
    for r in range(rows):
        cols = slice(r * total, (r + 1) * total)
        live = place < len_ref[r]
        s = jnp.where(live, scores[:, cols], MASKED_SCORE)
        e = jnp.where(live, jnp.exp(s - jnp.max(s, axis=1, keepdims=True)), 0.0)
        p = e / jnp.sum(e, axis=1, keepdims=True)
        probs_ref[:, cols] = p
        for g in range(heads):
            abd[8 * g + r : 8 * g + r + 1, cols] = jnp.sum(
                p[g * QUERIES : (g + 1) * QUERIES], axis=0, keepdims=True
            )
    u = fold(nn(parts(abd[...], 2), table), 2)
    u_ref[...] = u
    pooled_ref[...] = jnp.zeros(pooled_ref.shape, F32)
    for g in range(heads):
        first = 2 * wide + g * HEAD_DIM
        v = parts(u[8 * g : 8 * g + 8] * (1.0 / QUERIES), 2)
        pooled_ref[0:8, g * HEAD_DIM : (g + 1) * HEAD_DIM] = fold(
            nt(v, qkv[first : first + HEAD_DIM]), 2
        )


def stats_kernel(
    csh, heads, rows, seg_ref, x_ref, apack_ref, out_ref, dfilm_ref, pooled_ref, memory_ref, scratch
):
    count = x_ref.shape[0]
    wide = heads * HEAD_DIM
    seg = seg_ref[...]
    scratch[...] = jnp.zeros(scratch.shape, F32)
    for s in range(count):
        group, part = s // 2, s % 2
        scratch[part * rows : (part + 1) * rows, group * wide : (group + 1) * wide] = x_ref[
            s, 2 * RP : 2 * RP + rows, 0:wide
        ]
    pooled = scratch[...].astype(BF16)
    pooled_ref[...] = pooled
    memory = nn(pooled, apack_ref[:, 0:C]).astype(BF16)
    memory_ref[...] = memory
    film = nn(memory, apack_ref[:, C : C + 2 * csh])
    f0 = film[:, 0:csh]
    f1 = film[:, csh : 2 * csh]
    total = [x_ref[s, 0:RP, 0:csh] for s in range(count)]
    second = [x_ref[s, RP : 2 * RP, 0:csh] for s in range(count)]
    dsum = [x_ref[s, 0:RP, csh : 2 * csh] for s in range(count)]
    cross = [x_ref[s, RP : 2 * RP, csh : 2 * csh] for s in range(count)]
    means = [v * (1.0 / LANES) for v in total]
    d0 = jnp.zeros((RP, csh), F32)
    d1 = jnp.zeros((RP, csh), F32)
    for me in range(count):
        same = [(seg[:, s : s + 1] == seg[:, me : me + 1]).astype(F32) for s in range(count)]
        frames = sum(same) * float(LANES)
        inv = 1.0 / frames
        mean = sum(m * v for m, v in zip(same, total)) * inv
        var = (
            sum(
                m * (v + float(LANES) * (u - mean) * (u - mean))
                for m, v, u in zip(same, second, means)
            )
            * inv
        )
        scale = lax.rsqrt(var + NORM_EPS)
        dtot = sum(m * v for m, v in zip(same, dsum))
        xtot = sum(m * (v + (u - mean) * d) for m, v, u, d in zip(same, cross, means, dsum)) * scale
        mean_part = f0 * dtot * inv
        cross_part = f0 * xtot * inv
        slope = scale * scale * cross_part
        out_ref[me, 0:RP, 0:csh] = 1.0 + f0 * scale
        out_ref[me, RP : 2 * RP, 0:csh] = f1 - f0 * scale * mean
        out_ref[me, 0:RP, csh : 2 * csh] = -slope
        out_ref[me, RP : 2 * RP, csh : 2 * csh] = slope * mean - scale * mean_part
        d0 = d0 + (cross[me] + (means[me] - mean) * dsum[me]) * scale
        d1 = d1 + dsum[me]
    dfilm = jnp.concatenate([d0, d1], axis=1).astype(BF16)
    dfilm_ref[...] = dfilm
    dmem = nt(dfilm, apack_ref[:, C : C + 2 * csh])
    dpool = nt(dmem.astype(BF16), apack_ref[:, 0:C])
    for s in range(count):
        group, part = s // 2, s % 2
        rolled = pltpu.roll(dpool, RP - part * rows, 0) if part else dpool
        out_ref[s, 2 * RP : 3 * RP, 0:csh] = dmem[:, s * csh : (s + 1) * csh]
        out_ref[s, 2 * RP : 3 * RP, csh : 2 * csh] = jnp.zeros((RP, csh), F32)
        out_ref[s, 3 * RP : 4 * RP] = rolled[:, group * wide : (group + 1) * wide]


def coef_columns(csh, coef_ref, rows_ref, cols_ref):
    rows_ref[...] = jnp.zeros(rows_ref.shape, F32)
    for s in range(C // csh):
        cols = slice(s * csh, (s + 1) * csh)
        rows_ref[0 : 2 * RP, cols] = coef_ref[s, 0 : 2 * RP, 0:csh]
        rows_ref[2 * RP : 4 * RP, cols] = coef_ref[s, 0 : 2 * RP, csh : 2 * csh]
    cols_ref[...] = rows_ref[...].T


def skip_grad_kernel(gated_ref, dskip_ref, out_ref, right):
    for r in range(dskip_ref.shape[0]):
        right[:, r * LANES : (r + 1) * LANES] = dskip_ref[r]
    out_ref[...] = nt(gated_ref[...], right[...]).astype(BF16)


def backward_kernel(meta, dp, csh, gates, order_ref, off_ref, coef_ref, mid_ref, dout_ref, dskip_ref, fa_ref, fb_ref, inp_ref, gated_ref, gskip_ref, flags_ref, *refs):
    turned, refs = refs[: len(meta)], refs[len(meta) :]
    dpre_ref, dres_ref, sums_ref, refs = refs[0], refs[1], refs[2], refs[3:]
    outs, refs = (refs[0:2], refs[2:4]), refs[4:]
    rows_ref, cols_ref, w_ref, both_ref, dpt_ref, drt_ref, sems = refs
    cs = C // dp
    span = NR * LANES
    i = pl.program_id(0)

    @pl.when(i == 0)
    def _():
        copies = turned_copies(
            meta, turned, off_ref, cs, None, ((w_ref, 0), (w_ref, C), None), sems
        )
        begin(copies)
        coef_columns(csh, coef_ref, rows_ref, cols_ref)
        sums_ref[...] = jnp.zeros(sums_ref.shape, F32)
        finish(copies)

    @pl.when(i < gates)
    def _():
        coef = pltpu.roll(cols_ref[...], lax.rem(LANES - NR * i, LANES), 1)
        for j in range(NR):
            cols = slice(j * LANES, (j + 1) * LANES)
            mf = mid_ref[:, cols].astype(F32)
            df = dout_ref[j].astype(F32)
            a = coef[:, j : j + 1]
            be = coef[:, 2 * RP + j : 2 * RP + j + 1]
            ga = coef[:, 3 * RP + j : 3 * RP + j + 1]
            dmid = (a * df + (be * mf + ga)).astype(BF16).astype(F32)
            both_ref[0:C, cols] = (dmid * SQRT_HALF).astype(BF16)
            both_ref[C : 2 * C, cols] = dskip_ref[j]
        dres = both_ref[0:C]
        dres_ref[...] = dres
        dg = nn(w_ref[...], both_ref[...])
        dt = (dg * fa_ref[...].astype(F32)).astype(BF16)
        ds = (dg * fb_ref[...].astype(F32)).astype(BF16)
        dpre_ref[0:C] = dt
        dpre_ref[C : 2 * C] = ds
        at = pl.ds(pl.multiple_of(i * span, span), span)
        dpt_ref[at, 0:C] = dt.T
        dpt_ref[at, C : 2 * C] = ds.T
        drt_ref[at] = dres.T
        frame = lax.broadcasted_iota(jnp.int32, (span, LANES), 0)
        column = lane_ids((span, LANES))
        place = frame % LANES
        which = frame // LANES
        keep_l = jnp.zeros((span, LANES), jnp.int32)
        keep_r = jnp.zeros((span, LANES), jnp.int32)
        for j in range(NR):
            keep_l = jnp.where(which == j, flags_ref[0, NR * i + j], keep_l)
            keep_r = jnp.where(which == j, flags_ref[1, NR * i + j], keep_r)
        row = NR * i + which
        use0 = (column == row) & ((place >= SHIFT) | (keep_l > 0))
        use1 = column == RP + row
        use2 = (column == 2 * RP + row) & ((place < LANES - SHIFT) | (keep_r > 0))
        pick = jnp.where(use0 | use1 | use2, 1.0, 0.0).astype(BF16)
        sums_ref[...] = sums_ref[...] + nn(dpre_ref[...], pick)

    @pl.when(i >= gates)
    def _():
        g = nn(inp_ref[...], dpt_ref[...]).astype(BF16)
        h = nn(gated_ref[...], drt_ref[...]).astype(BF16)
        k = i - gates
        for parity, (one, two) in enumerate(outs):

            @pl.when(lax.rem(k, 2) == parity)
            def _():
                for t in range(4):
                    rows = slice(t * cs, (t + 1) * cs)
                    lanes = slice(t * LANES, (t + 1) * LANES)
                    one[0, rows, 0:LANES] = h[:, lanes]
                    one[0, rows, LANES : 2 * LANES] = gskip_ref[:, lanes]
                one[0, :, 2 * LANES :] = g[:, 0:EARLY]
                two[0] = g[:, EARLY:]


def step_grad_kernel(meta, dp, off_ref, sums_ref, emb_ref, *refs):
    turned, refs = refs[: len(meta)], refs[len(meta) :]
    keep_ref, give_ref, wt_ref, scr, sems = refs
    cs = C // dp
    copies = turned_copies(meta, turned, off_ref, cs, wt_ref, (None,) * 3, sems)
    begin(copies)
    sums = sums_ref[...].T
    emb = emb_ref[...].T
    finish(copies)
    total = jnp.zeros((RP, 4 * C), F32)
    lane = lane_ids((RP, 4 * C))
    all_taps = fold(nn(parts(sums[0 : 3 * RP], 2), wt_ref[...]), 2)
    for t in range(3):
        g = all_taps[t * RP : (t + 1) * RP]
        total = total + jnp.where((lane // cs) % 4 == t, g, 0.0)
    out = []
    for d in range(dp):
        block = total[:, d * 4 * cs : (d + 1) * 4 * cs]
        out.append(block[:, 0:cs] + block[:, cs : 2 * cs] + block[:, 2 * cs : 3 * cs])
    g = jnp.concatenate(out, axis=1)
    g = jnp.concatenate([g, jnp.zeros((LANES - RP, C), F32)], axis=0)
    hi = g.astype(BF16)
    lo = (g - hi.astype(F32)).astype(BF16)
    scr[...] = nn(emb, hi) + nn(emb, lo)
    for k in range(dp):
        v = scr[pl.ds(pl.multiple_of(off_ref[k], 16), cs)].astype(BF16)
        for t in range(4):
            (keep_ref, give_ref)[k % 2][k // 2, t * cs : (t + 1) * cs] = v[
                :, t * LANES : (t + 1) * LANES
            ]


def input_grad_kernel(meta, dp, off_ref, dpre_ref, dres_ref, *refs):
    turned, refs = refs[: len(meta)], refs[len(meta) :]
    base_ref, first_ref, last_ref, wt_ref, w_ref, facc_ref, lacc_ref, sems = refs
    cs = C // dp
    i = pl.program_id(0)
    lane = lane_ids((C, LANES))

    @pl.when(i == 0)
    def _():
        copies = turned_copies(meta, turned, off_ref, cs, wt_ref, (None,) * 3, sems)
        begin(copies)
        facc_ref[...] = jnp.zeros((C, LANES), F32)
        lacc_ref[...] = jnp.zeros((C, LANES), F32)
        finish(copies)
        for d in range(dp):
            v = wt_ref[:, d * 4 * cs : (d + 1) * 4 * cs].T
            for t in range(3):
                w_ref[t, d * cs : (d + 1) * cs] = v[t * cs : (t + 1) * cs]

    dpre = dpre_ref[...]
    y0 = nn(w_ref[0], dpre)
    y1 = nn(w_ref[1], dpre)
    y2 = nn(w_ref[2], dpre)
    facc = facc_ref[...]
    lacc = lacc_ref[...]
    for j in range(NR):
        r = NR * i + j
        cols = slice(j * LANES, (j + 1) * LANES)
        z0 = pltpu.roll(y0[:, cols], LANES - SHIFT, 1)
        z2 = pltpu.roll(y2[:, cols], SHIFT, 1)
        inner0 = lane < LANES - SHIFT
        inner2 = lane >= SHIFT
        v = y1[:, cols]
        base_ref[:, cols] = (
            v
            + jnp.where(inner0, z0, 0.0)
            + jnp.where(inner2, z2, 0.0)
            + dres_ref[:, cols].astype(F32)
        ).astype(BF16)
        here = (lane // SHIFT) == r
        facc = jnp.where(here, pltpu.roll(z0, lax.rem(SHIFT * r + SHIFT, LANES), 1), facc)
        lacc = jnp.where(here, pltpu.roll(z2, SHIFT * r, 1), lacc)
    facc_ref[...] = facc
    lacc_ref[...] = lacc

    @pl.when(i == pl.num_programs(0) - 1)
    def _():
        first_ref[...] = facc.astype(BF16)
        last_ref[...] = lacc.astype(BF16)


def finish_kernel(csh, flags_ref, base_ref, left_ref, right_ref, mid_ref, coef_ref, out_ref, layer_ref, rows_ref, cols_ref):
    i = pl.program_id(0)
    lane = lane_ids((C, LANES))

    @pl.when(i == 0)
    def _():
        coef_columns(csh, coef_ref, rows_ref, cols_ref)

    coef = pltpu.roll(cols_ref[...], lax.rem(LANES - NR * i, LANES), 1)
    left = left_ref[...].astype(F32)
    right = right_ref[...].astype(F32)
    for j in range(NR):
        r = NR * i + j
        cols = slice(j * LANES, (j + 1) * LANES)
        lh = pltpu.roll(left, lax.rem(LANES - SHIFT * r, LANES), 1)
        rh = pltpu.roll(right, LANES - SHIFT - SHIFT * r, 1)
        lh = jnp.where((lane < SHIFT) & (flags_ref[0, r] > 0), lh, 0.0)
        rh = jnp.where((lane >= LANES - SHIFT) & (flags_ref[1, r] > 0), rh, 0.0)
        out_ref[j] = (base_ref[:, cols].astype(F32) + lh + rh).astype(BF16)
        a = coef[:, j : j + 1]
        b = coef[:, RP + j : RP + j + 1]
        layer_ref[j] = (a * mid_ref[:, cols].astype(F32) + b).astype(BF16)


def add_blocks_kernel(count, *refs):
    ins, (keep_ref, give_ref) = refs[: 2 * count], refs[2 * count :]
    at = 0
    for p in range(count):
        a_ref, b_ref = ins[2 * p : 2 * p + 2]
        width = a_ref.shape[2]
        for j in range(a_ref.shape[0]):
            v = a_ref[j].astype(F32) + b_ref[j].astype(F32)
            (keep_ref, give_ref)[j % 2][j // 2, :, at : at + width] = v.astype(BF16)
        at += width


def add_halves_kernel(bit, index_ref, a_ref, b_ref, keep_ref, give_ref, scr):
    half = a_ref.shape[0] // 2
    mine = lax.rem(index_ref[0] // bit, 2)
    scr[...] = a_ref[...].astype(F32) + b_ref[...].astype(F32)
    keep_ref[...] = scr[pl.ds(pl.multiple_of(mine * half, 8), half)].astype(BF16)
    give_ref[...] = scr[pl.ds(pl.multiple_of((1 - mine) * half, 8), half)].astype(BF16)


def add_pieces_kernel(a_ref, b_ref, out_ref):
    v = a_ref[...].astype(F32) + b_ref[...].astype(F32)
    size = out_ref.shape[1]
    for p in range(out_ref.shape[0]):
        out_ref[p] = v[p * size : (p + 1) * size].astype(BF16)


def sum_copies_kernel(a_ref, *refs):
    out_ref = refs[-1]
    v = a_ref[0].astype(F32)
    for p in range(1, a_ref.shape[0]):
        v = v + a_ref[p].astype(F32)
    out_ref[:, 0 : v.shape[1]] = v.astype(BF16)
    if len(refs) > 1:
        out_ref[:, v.shape[1] :] = refs[0][...]


def small_sum_kernel(csh, wide, bit_ref, keep_ref, got_ref, film_ref, attn_ref, mine_ref, other_ref, turn):
    v = keep_ref[0].astype(F32) + got_ref[0].astype(F32)
    cs = v.shape[0]
    film = 2 * wide + csh
    turn[...] = jnp.zeros(turn.shape, F32)
    turn[0:cs, 0 : 2 * csh] = v[:, film : film + 2 * csh]
    film_ref[...] = turn[...].T[0 : 2 * csh, 0:cs]
    attn_ref[...] = v[:, 2 * wide : film]
    last = film + 2 * csh
    even = bit_ref[0] == 0
    for one, two, rows, width in (
        (v[:, 0:wide], v[:, wide : 2 * wide], slice(0, cs), wide),
        (
            v[0:QUERIES, last : last + wide // 2],
            v[0:QUERIES, last + wide // 2 : last + wide],
            slice(cs, cs + QUERIES),
            wide // 2,
        ),
    ):
        mine_ref[rows, 0:width] = jnp.where(even, one, two).astype(BF16)
        other_ref[rows, 0:width] = jnp.where(even, two, one).astype(BF16)
    mine_ref[cs:, wide // 2 :] = jnp.zeros((QUERIES, wide // 2), BF16)
    other_ref[cs:, wide // 2 :] = jnp.zeros((QUERIES, wide // 2), BF16)


def small_piece_kernel(csh, wide, attn_ref, mine_ref, got_ref, out_ref):
    v = mine_ref[...].astype(F32) + got_ref[...].astype(F32)
    attn = attn_ref[...]
    cs = attn.shape[0]
    rows = out_ref.shape[0]
    at = 0
    for row in range(0, cs, rows):
        out_ref[:, at : at + wide] = v[row : row + rows].astype(BF16)
        out_ref[:, at + wide : at + wide + csh] = attn[row : row + rows].astype(BF16)
        at += wide + csh
    for row in range(0, QUERIES, rows):
        block = v[cs + row : cs + min(row + rows, QUERIES), 0 : wide // 2]
        if block.shape[0] < rows:
            pad = jnp.zeros((rows - block.shape[0], wide // 2), F32)
            block = jnp.concatenate([block, pad], axis=0)
        out_ref[:, at : at + wide // 2] = block.astype(BF16)
        at += wide // 2


def output_kernel(
    cs,
    csh,
    wide,
    seq,
    peer_ref,
    *refs,
):
    ones, twos, refs = refs[:seq], refs[seq : 2 * seq], refs[2 * seq :]
    (
        queries_ref,
        wq_ref,
        step_ref,
        conv_ref,
        cond_ref,
        res_ref,
        skip_ref,
        gqueries_ref,
        gquery_ref,
        key_ref,
        value_ref,
        attn_ref,
        scr1,
        scr2,
        small,
        qscr,
        dq,
    ) = refs
    count, size = seq // 2, ones[0].shape[0]
    wide2 = scr2.shape[1]
    for k in range(seq):
        peer = peer_ref[k]
        at = (lax.rem(peer, 2) * count + peer // 2) * size
        rows = pl.ds(pl.multiple_of(at, 8), size)
        scr1[rows] = ones[k][...].astype(F32)
        v = twos[k][...].astype(F32)
        scr2[rows] = v[:, 0:wide2]
        small[pl.ds(pl.multiple_of(peer * size, 8), size)] = v[:, wide2:]
    for t in range(4):
        rows = slice(t * cs, (t + 1) * cs)
        lanes = slice(t * LANES, (t + 1) * LANES)
        res_ref[:, lanes] = scr1[rows, 0:LANES]
        skip_ref[:, lanes] = scr1[rows, LANES : 2 * LANES]
        rest = 2 * C - EARLY
        step_ref[:, lanes] = scr2[rows, rest : rest + LANES]
        if t < 3:
            conv_ref[t, :, 0:EARLY] = scr1[rows, 2 * LANES : 2 * LANES + EARLY]
            conv_ref[t, :, EARLY:] = scr2[rows, 0:rest]
        else:
            cond_ref[:, 0:EARLY] = scr1[rows, 2 * LANES : 2 * LANES + EARLY]
            cond_ref[:, EARLY:] = scr2[rows, 0:rest]
    dq[...] = jnp.zeros(dq.shape, F32)
    for s in range(seq):
        v = small[s * size : (s + 1) * size]
        group, even = s // 2, s % 2 == 0
        out = key_ref if even else value_ref
        at = 0
        for row in range(0, cs, size):
            out[row : row + size, group * wide : (group + 1) * wide] = v[:, at : at + wide]
            attn_ref[row : row + size, s * csh : (s + 1) * csh] = v[:, at + wide : at + wide + csh]
            at += wide + csh
        first = group * wide + (0 if even else wide // 2)
        for row in range(0, QUERIES, size):
            count = min(size, QUERIES - row)
            dq[row : row + count, first : first + wide // 2] = v[0:count, at : at + wide // 2]
            at += wide // 2
    qscr[...] = jnp.zeros((LANES, LANES), F32)
    qscr[0:QUERIES, 0:cs] = queries_ref[...].astype(F32)
    qt = qscr[...].T.astype(BF16)
    d = dq[...]
    hi = d.astype(BF16)
    lo = (d - hi.astype(F32)).astype(BF16)
    gquery_ref[...] = (nn(qt, hi) + nn(qt, lo))[0:cs]
    gqueries_ref[...] = fold(nt(parts(d[0:QUERIES], 2), wq_ref[...]), 2)


def attention_back_kernel(
    rows,
    csh,
    dp,
    off_ref,
    prow,
    probs_ref,
    u_ref,
    qp_ref,
    qkv_ref,
    pooled_ref,
    memory_ref,
    dfilm_ref,
    got_ref,
    keep_ref,
    give_ref,
    ds,
    stack,
    right,
    out,
):
    count = got_ref.shape[0]
    total = prow.shape[1] * prow.shape[2]
    cs = C // dp
    table = prow[...].reshape(rows * total, C)
    wide = qp_ref.shape[1]
    heads = wide // HEAD_DIM
    datt = got_ref[0, 3 * RP : 4 * RP, 0:wide]
    dmem = got_ref[0, 2 * RP : 3 * RP, 0:csh]
    for s in range(1, count):
        datt = datt + got_ref[s, 3 * RP : 4 * RP, 0:wide]
        dmem = dmem + got_ref[s, 2 * RP : 3 * RP, 0:csh]
    datt = datt[0:8] * (1.0 / QUERIES)
    vh = []
    for g in range(heads):
        first = 2 * wide + g * HEAD_DIM
        v = parts(datt[:, g * HEAD_DIM : (g + 1) * HEAD_DIM], 2)
        vh.append(fold(nn(v, qkv_ref[first : first + HEAD_DIM]), 2))
    vh = jnp.concatenate(vh, axis=0)
    dp_all = fold(nt(parts(vh, 2), table), 2)
    for r in range(rows):
        cols = slice(r * total, (r + 1) * total)
        for g in range(heads):
            mine = slice(g * QUERIES, (g + 1) * QUERIES)
            p = probs_ref[mine, cols]
            dpr = dp_all[8 * g + r : 8 * g + r + 1, cols]
            inner = jnp.sum(p * dpr, axis=1, keepdims=True)
            ds[mine, cols] = p * (dpr - inner)
    tt = fold(nn(parts(ds[...], 2), table), 2)
    scale = 1.0 / math.sqrt(HEAD_DIM)
    dq = []
    stack[...] = jnp.zeros(stack.shape, F32)
    right[...] = jnp.zeros(right.shape, F32)
    stack[0 : heads * QUERIES] = tt
    stack[64:80] = u_ref[...]
    stack[80:96] = pooled_ref[...].astype(F32)
    stack[96:112] = memory_ref[...].astype(F32)
    for g in range(heads):
        cols = slice(g * HEAD_DIM, (g + 1) * HEAD_DIM)
        mine = slice(g * QUERIES, (g + 1) * QUERIES)
        wk = qkv_ref[wide + g * HEAD_DIM : wide + (g + 1) * HEAD_DIM]
        dq.append(fold(nt(parts(tt[mine], 2), wk), 2) * scale)
        right[mine, cols] = qp_ref[:, cols] * scale
        right[64 + 8 * g : 72 + 8 * g, wide + cols.start : wide + cols.stop] = datt[:, cols]
    right[80:96, 2 * wide : 2 * wide + csh] = dmem
    right[96:112, 2 * wide + csh : 2 * wide + 3 * csh] = dfilm_ref[...].astype(F32)
    out[...] = lax.dot_general(
        stack[...].T,
        right[...],
        (((1,), (0,)), ((), ())),
        precision=lax.Precision.HIGHEST,
        preferred_element_type=F32,
    )
    last = 2 * wide + 3 * csh
    for k in range(dp):
        ref = (keep_ref, give_ref)[k % 2]
        ref[k // 2] = out[pl.ds(pl.multiple_of(off_ref[k], 16), cs)].astype(BF16)
        for g in range(heads):
            first = last + g * HEAD_DIM
            ref[k // 2, 0:QUERIES, first : first + HEAD_DIM] = dq[g].astype(BF16)


def exchange(pieces, axis, groups=None):
    return lax.all_to_all(
        pieces, axis, split_axis=0, concat_axis=0, axis_index_groups=groups, tiled=True
    )


def flipped(v, axis, size, bit):
    return lax.ppermute(v, axis, [(d, d ^ bit) for d in range(size)])


class Reduction:
    def __init__(self, call, name, keep, give, dp, seq, index):
        self.call, self.name, self.dp, self.seq, self.index = call, name, dp, seq, index
        self.keep, self.flip = keep, 1
        self.got = flipped(give, "dp", dp, 1)

    def over_blocks(self, after=(), others=()):
        while 2 * self.flip < self.dp:
            group = (self,) + tuple(others)
            others = ()
            args = []
            for part in group:
                args += [part.keep, Got(part.got)]
            width = sum(part.keep.shape[2] for part in group)
            half = sds((self.keep.shape[0] // 2, self.keep.shape[1], width), BF16)
            self.keep, give = self.call(
                functools.partial(add_blocks_kernel, len(group)),
                (half, half),
                "blocks_" + self.name,
                args,
                after=after,
                in_specs=[VM] * len(args),
                out_specs=(VM, VM),
            )
            self.flip *= 2
            self.got = flipped(give, "dp", self.dp, self.flip)
        self.rest = self.keep.shape[1:]

    def over_half(self, after=()):
        rows, width = self.rest
        half = sds((rows // 2, width), BF16)
        self.keep, give = self.call(
            functools.partial(add_halves_kernel, 1),
            (half, half),
            "half_" + self.name,
            (self.index, self.keep.reshape(rows, width), Got(self.got.reshape(rows, width))),
            after=after,
            in_specs=[SM, VM, VM],
            out_specs=(VM, VM),
            scratch_shapes=[pltpu.VMEM((rows, width), F32)],
        )
        self.got = flipped(give, "seq", self.seq, 1)

    def over_pieces(self, after=()):
        rows, width = self.rest
        count = self.seq // 2
        self.groups = [[2 * k + b for k in range(count)] for b in range(2)]
        pieces = self.call(
            add_pieces_kernel,
            sds((count, rows // self.seq, width), BF16),
            "pieces_" + self.name,
            (self.keep, Got(self.got)),
            after=after,
            in_specs=[VM, VM],
            out_specs=VM,
        )
        self.got = exchange(pieces, "seq", self.groups)

    def over_copies(self, after=(), extra=None, bits=()):
        args, (_, rows, width) = [Got(self.got)], self.got.shape
        if extra is not None:
            args.append(extra)
            width += extra.shape[1]
        piece = self.call(
            sum_copies_kernel,
            sds((rows, width), BF16),
            "copies_" + self.name,
            args,
            after=after,
            in_specs=[VM] * len(args),
            out_specs=VM,
        )
        have = {0: piece}
        for bit in bits:
            for k in sorted(have):
                have[k + bit] = flipped(have[k], "seq", self.seq, bit)
        return [have[k] if k == 0 else Got(have[k]) for k in range(self.seq)]


def body(
    dp,
    seq,
    x_in,
    cond,
    segment_ids,
    diffusion_steps,
    prompt,
    prompt_lengths,
    w_step,
    w_conv,
    w_cond,
    w_res,
    w_skip,
    queries,
    w_query,
    w_key,
    w_value,
    w_attn_out,
    w_film,
    d_out,
    d_skip,
):
    call = Caller()
    rows = x_in.shape[0]
    frames = x_in.shape[2]
    steps = rows // NR
    cols = rows * frames
    cs = C // dp
    csh = C // seq
    heads = 2 * HEADS // seq
    wide = heads * HEAD_DIM
    arows = rows // 2
    pl_local = prompt.shape[1]
    prompt_all = pl_local * seq
    sidx = lax.axis_index("seq")
    didx = lax.axis_index("dp")
    group = (sidx // 2).astype(jnp.int32).reshape(1)
    bit = (sidx % 2).astype(jnp.int32).reshape(1)
    up = [(i, i + 1) for i in range(seq - 1)]
    down = [(i + 1, i) for i in range(seq - 1)]
    order = jnp.bitwise_xor(didx, jnp.arange(dp, dtype=jnp.int32)).astype(jnp.int32)
    offsets = jnp.concatenate([order * cs, bit, 1 - bit])
    index = sidx.astype(jnp.int32).reshape(1)
    peers = jnp.bitwise_xor(sidx, jnp.arange(seq, dtype=jnp.int32)).astype(jnp.int32)

    def gather(pack, side=None, middle=None):
        if dp == 4 and side is not None:
            mine = flipped(side, "dp", dp, 2)
            inner = flipped(middle, "dp", dp, 2)
            other = flipped(mine, "seq", seq, 1)
            near = [(0, None, pack), (2, 0, mine), (2, 2, inner), (2, 1, other)]
            pieces = near + [(k + 1, h, flipped(v, "dp", dp, 1)) for k, h, v in near]
        else:
            pieces = [(0, None, pack)]
            flip = dp // 2
            while flip:
                pieces += [(k + flip, h, flipped(v, "dp", dp, flip)) for k, h, v in pieces]
                flip //= 2
        pieces.sort(key=lambda piece: piece[0])
        meta = [(k, h) for k, h, _ in pieces]
        return meta, [v if k == 0 else Got(v) for k, _, v in pieces]

    off_qkv = C + 2 * csh
    qkv_rows = -(-(3 * wide + QUERIES) // LANES) * LANES
    head_width = -(-(off_qkv + qkv_rows) // LANES) * LANES
    pack, mine, other = call(
        functools.partial(head_pack_kernel, csh, wide),
        (
            sds((cs, head_width), BF16),
            sds((arows, pl_local, C), BF16),
            sds((arows, pl_local, C), BF16),
        ),
        "head_pack",
        (
            group,
            bit,
            w_attn_out,
            jnp.transpose(w_film, (1, 2, 0)).reshape(2 * csh, cs),
            w_query,
            w_key,
            w_value,
            queries,
            prompt,
        ),
        in_specs=[SM, SM] + [VM] * 7,
        out_specs=(VM,) * 3,
        scratch_shapes=[pltpu.VMEM((2 * LANES, LANES), F32)],
    )
    _, head_pieces = gather(pack)
    partner = flipped(other, "seq", seq, 1)
    first, last = call(
        edge_kernel,
        (sds((C, LANES), BF16), sds((C, LANES), BF16)),
        "edges",
        (x_in,),
        after=("head_pack",),
        in_specs=[VM],
        out_specs=(VM, VM),
    )
    left_halo = lax.ppermute(last, "seq", up)
    right_halo = lax.ppermute(first, "seq", down)
    pair = call(
        pair_kernel,
        sds((seq // 2, 2, arows, pl_local, C), BF16),
        "pair",
        (mine, Got(partner)),
        after=("edges",),
        in_specs=[VM, VM],
        out_specs=VM,
    )
    middle = 2 * C - 2 * SIDE + 3 * C // 4
    pack, side, middle = call(
        functools.partial(turned_pack_kernel, cs),
        (
            sds((2 * SIDE + middle, 4 * cs), BF16),
            sds((SIDE, 4 * cs), BF16),
            sds((middle, 4 * cs), BF16),
        ),
        "turned_pack",
        (bit, w_conv, w_cond, w_res, w_skip, w_step),
        after=("pair", head_pieces[dp // 2].array, left_halo, right_halo),
        in_specs=[SM] + [VM] * 5,
        out_specs=(VM, VM, VM),
        scratch_shapes=[pltpu.VMEM((4 * cs, 2 * C), BF16)],
    )
    meta, turned = gather(pack, side, middle)
    copies = 4 * dp * (1 + 3 * C // (4 * cs))
    z_groups = [[2 * k + b for k in range(seq // 2)] for b in range(2)]
    prompts = Got(exchange(pair, "seq", z_groups))
    block_ids = segment_ids[:, ::frames]
    padded_ids = jnp.pad(block_ids, ((0, 0), (1, 1)), constant_values=-1)
    mine = lax.dynamic_slice_in_dim(padded_ids, sidx, 3, 1)
    flags = jnp.stack([mine[:, 0] == mine[:, 1], mine[:, 2] == mine[:, 1]]).astype(jnp.int32)
    block_ids = jnp.pad(block_ids, ((0, RP - rows), (0, 0)))
    half = C // 2
    frequency = jnp.exp(jnp.arange(half, dtype=F32) * (-math.log(10000.0) / half))
    step_rows = jnp.pad(diffusion_steps.astype(F32), (0, LANES - rows))
    live_rows = jnp.arange(LANES, dtype=jnp.int32)[:, None] < rows
    angles = step_rows[:, None] * frequency[None, :]
    embedding = jnp.concatenate([jnp.sin(angles), jnp.cos(angles)], axis=1)
    embedding = jnp.where(live_rows, embedding, 0.0).astype(BF16)
    flags, block_ids, embedding = call(
        table_kernel,
        (
            sds(flags.shape, jnp.int32),
            sds(block_ids.shape, jnp.int32),
            sds(embedding.shape, BF16),
        ),
        "tables",
        (flags, block_ids, embedding),
        after=("turned_pack",),
        in_specs=[SM, VM, VM],
        out_specs=(SM, VM, VM),
    )

    lengths = lax.dynamic_slice_in_dim(prompt_lengths, (sidx % 2) * arows, arows, 0)

    apack, prow, probs, u, pooled_head, qp, qkv = call(
        functools.partial(attention_kernel, dp, arows, heads, seq // 2, off_qkv),
        (
            sds((C, head_width), BF16),
            sds((arows, seq, pl_local, C), BF16),
            sds((heads * QUERIES, arows * prompt_all), F32),
            sds((RP, C), F32),
            sds((RP, LANES), F32),
            sds((QUERIES, wide), F32),
            sds((qkv_rows, C), BF16),
        ),
        "attention",
        (offsets, bit, lengths, prompts, *head_pieces),
        in_specs=[SM, SM, SM, HB] + [HB] * dp,
        out_specs=(VM,) * 7,
        scratch_shapes=[
            pltpu.VMEM((RP, arows * prompt_all), F32),
            pltpu.SemaphoreType.DMA((dp + seq,)),
        ],
    )

    row_block = pl.BlockSpec((NR, C, LANES), lambda i: (i, 0, 0))

    def col_block(height):
        return pl.BlockSpec((height, NR * LANES), lambda i: (0, i))

    def still(shape):
        return pl.BlockSpec(shape, lambda i: (0,) * len(shape))

    inp, gated, factor_a, factor_b, skip_out, mid, stats = call(
        functools.partial(forward_kernel, meta, dp, csh),
        (
            sds((4 * C, cols), BF16),
            sds((C, cols), BF16),
            sds((C, cols), BF16),
            sds((C, cols), BF16),
            sds(x_in.shape, BF16),
            sds((C, cols), BF16),
            sds((seq, 3 * RP, 2 * csh), F32),
        ),
        "wavenet",
        (
            offsets,
            flags,
            x_in,
            cond,
            d_out,
            Got(left_halo),
            Got(right_halo),
            embedding,
            pooled_head,
            *turned,
        ),
        flops=2 * cols * (4 * C * 2 * C + 2 * C * C),
        nbytes=30e6,
        grid=(steps,),
        in_specs=[
            SM,
            SM,
            row_block,
            row_block,
            row_block,
            whole((C, LANES)),
            whole((C, LANES)),
            whole((LANES, C)),
            whole((RP, LANES)),
        ]
        + [HB] * len(turned),
        out_specs=(
            col_block(4 * C),
            col_block(C),
            col_block(C),
            col_block(C),
            row_block,
            col_block(C),
            still((seq, 3 * RP, 2 * csh)),
        ),
        scratch_shapes=[
            pltpu.VMEM((2 * C, 4 * C), BF16),
            pltpu.VMEM((C, 2 * C), BF16),
            pltpu.VMEM((C, C), BF16),
            pltpu.VMEM((2 * C, C), BF16),
            pltpu.VMEM((C, LANES), F32),
            pltpu.VMEM((C, LANES), F32),
            pltpu.SemaphoreType.DMA((copies,)),
        ],
    )
    stats_got = exchange(stats, "seq")
    gskip = call(
        skip_grad_kernel,
        sds((C, C), BF16),
        "skip",
        (gated, d_skip),
        in_specs=[VM, VM],
        out_specs=VM,
        scratch_shapes=[pltpu.VMEM((C, cols), BF16)],
    )

    coef_out, dfilm, pooled, memory = call(
        functools.partial(stats_kernel, csh, heads, arows),
        (
            sds((seq, 4 * RP, 2 * csh), F32),
            sds((RP, 2 * csh), BF16),
            sds((RP, C), BF16),
            sds((RP, C), BF16),
        ),
        "segments",
        (block_ids, Got(stats_got), apack),
        after=("skip",),
        in_specs=[VM, VM, VM],
        out_specs=(VM, VM, VM, VM),
        scratch_shapes=[pltpu.VMEM((RP, C), F32)],
    )
    coef = Got(exchange(coef_out, "seq"))

    def gate_block(i):
        return jnp.minimum(i, steps - 1)

    def shard(i):
        return jnp.maximum(i - steps, 0)

    def gate_cols(height):
        return pl.BlockSpec((height, NR * LANES), lambda i, order: (0, gate_block(i)))

    gate_rows = pl.BlockSpec((NR, C, LANES), lambda i, order: (gate_block(i), 0, 0))
    wide1, wide2 = EARLY + 2 * LANES, 2 * C - EARLY

    def part(width):
        return sds((dp // 2, 4 * cs, width), BF16)

    def part_spec(width):
        return pl.BlockSpec((1, 4 * cs, width), lambda i, order: (shard(i) // 2, 0, 0))

    outs = call(
        functools.partial(backward_kernel, meta, dp, csh, steps),
        (
            sds((2 * C, cols), BF16),
            sds((C, cols), BF16),
            sds((2 * C, LANES), F32),
            part(wide1),
            part(wide2),
            part(wide1),
            part(wide2),
        ),
        "backward",
        (order, offsets, coef, mid, d_out, d_skip, factor_a, factor_b, inp, gated, gskip, flags, *turned),
        prefetch=1,
        grid=(steps + dp,),
        in_specs=[
            SM,
            pl.BlockSpec(
                (seq, 4 * RP, 2 * csh), lambda i, order: (0, 0, 0), pipeline_mode=pl.Buffered(1)
            ),
            gate_cols(C),
            gate_rows,
            gate_rows,
            gate_cols(C),
            gate_cols(C),
            pl.BlockSpec((4 * cs, cols), lambda i, order: (order[shard(i)], 0)),
            pl.BlockSpec((cs, cols), lambda i, order: (order[shard(i)], 0)),
            pl.BlockSpec((cs, C), lambda i, order: (order[shard(i)], 0)),
            SM,
        ]
        + [HB] * len(turned),
        out_specs=(
            gate_cols(2 * C),
            gate_cols(C),
            pl.BlockSpec((2 * C, LANES), lambda i, order: (0, 0)),
            part_spec(wide1),
            part_spec(wide2),
            part_spec(wide1),
            part_spec(wide2),
        ),
        scratch_shapes=[
            pltpu.VMEM((LANES, C), F32),
            pltpu.VMEM((C, LANES), F32),
            pltpu.VMEM((C, 2 * C), BF16),
            pltpu.VMEM((2 * C, NR * LANES), BF16),
            pltpu.VMEM((cols, 2 * C), BF16),
            pltpu.VMEM((cols, C), BF16),
            pltpu.SemaphoreType.DMA((copies,)),
        ],
    )
    dpre, dres, sums = outs[0:3]
    part1 = Reduction(call, "1", outs[3], outs[5], dp, seq, index)
    part2 = Reduction(call, "2", outs[4], outs[6], dp, seq, index)
    part1.over_blocks()
    keep, give = call(
        functools.partial(step_grad_kernel, meta, dp),
        (part(LANES), part(LANES)),
        "step_grad",
        (offsets, sums, embedding, *turned),
        after=("blocks_1",),
        in_specs=[SM, VM, VM] + [HB] * len(turned),
        out_specs=(VM, VM),
        scratch_shapes=[
            pltpu.VMEM((2 * C, 4 * C), BF16),
            pltpu.VMEM((C, C), F32),
            pltpu.SemaphoreType.DMA((copies,)),
        ],
    )
    part_step = Reduction(call, "step", keep, give, dp, seq, index)

    right_width = -(-(3 * wide + 3 * csh) // LANES) * LANES
    block = sds((dp // 2, cs, right_width), BF16)
    keep, give = call(
        functools.partial(attention_back_kernel, arows, csh, dp),
        (block, block),
        "attention_back",
        (offsets, prow, probs, u, qp, qkv, pooled, memory, dfilm, coef),
        after=("step_grad",),
        in_specs=[SM] + [VM] * 9,
        out_specs=(VM, VM),
        scratch_shapes=[
            pltpu.VMEM((heads * QUERIES, arows * prompt_all), F32),
            pltpu.VMEM((LANES, C), F32),
            pltpu.VMEM((LANES, right_width), F32),
            pltpu.VMEM((C, right_width), F32),
        ],
    )
    small = Reduction(call, "small", keep, give, dp, seq, index)
    part2.over_blocks(("attention_back",), (part_step,))
    small.over_blocks(("blocks_2",))
    base, first, last = call(
        functools.partial(input_grad_kernel, meta, dp),
        (sds((C, cols), BF16), sds((C, LANES), BF16), sds((C, LANES), BF16)),
        "input_grad",
        (offsets, dpre, dres, *turned),
        after=("blocks_small",),
        grid=(steps,),
        in_specs=[SM, col_block(2 * C), col_block(C)] + [HB] * len(turned),
        out_specs=(
            col_block(C),
            still((C, LANES)),
            still((C, LANES)),
        ),
        scratch_shapes=[
            pltpu.VMEM((2 * C, 4 * C), BF16),
            pltpu.VMEM((3, C, 2 * C), BF16),
            pltpu.VMEM((C, LANES), F32),
            pltpu.VMEM((C, LANES), F32),
            pltpu.SemaphoreType.DMA((copies,)),
        ],
    )
    from_left = lax.ppermute(last, "seq", up)
    from_right = lax.ppermute(first, "seq", down)
    part1.over_half(("input_grad",))

    rest = 4 * cs // seq
    small_width = (cs // rest) * (wide + csh) + max(1, QUERIES // rest) * (wide // 2)
    part2.over_half(("half_1",))
    grad_film, attn_rows, mine, other = call(
        functools.partial(small_sum_kernel, csh, wide),
        (
            sds((2 * csh, cs), F32),
            sds((cs, csh), F32),
            sds((cs + QUERIES, wide), BF16),
            sds((cs + QUERIES, wide), BF16),
        ),
        "small_sum",
        (bit, small.keep, Got(small.got)),
        after=("half_2",),
        in_specs=[SM, VM, VM],
        out_specs=(VM,) * 4,
        scratch_shapes=[pltpu.VMEM((LANES, LANES), F32)],
    )
    partner = flipped(other, "seq", seq, 1)
    part1.over_pieces(("small_sum",))
    part2.over_pieces(("pieces_1",))
    bits = [1 << b for b in range(seq.bit_length() - 1)]
    ones = part1.over_copies(("pieces_2",), bits=bits[::-1])
    grad_input, layer_out = call(
        functools.partial(finish_kernel, csh),
        (sds(x_in.shape, BF16), sds(x_in.shape, BF16)),
        "grad_input",
        (flags, base, Got(from_left), Got(from_right), mid, coef),
        after=(ones[seq // 2].array,),
        grid=(steps,),
        in_specs=[
            SM,
            col_block(C),
            whole((C, LANES)),
            whole((C, LANES)),
            col_block(C),
            whole((seq, 4 * RP, 2 * csh)),
        ],
        out_specs=(row_block, row_block),
        scratch_shapes=[pltpu.VMEM((LANES, C), F32), pltpu.VMEM((C, LANES), F32)],
    )

    small_piece = call(
        functools.partial(small_piece_kernel, csh, wide),
        sds((rest, small_width), BF16),
        "small_piece",
        (attn_rows, mine, Got(partner)),
        after=("grad_input", ones[seq // 4].array, ones[3 * seq // 4].array),
        in_specs=[VM] * 3,
        out_specs=VM,
    )
    twos = part2.over_copies(extra=small_piece, bits=bits[:1:-1] + bits[:2])

    (
        grad_step,
        grad_conv,
        grad_cond,
        grad_res,
        grad_skip,
        grad_queries,
        grad_query,
        grad_key,
        grad_value,
        grad_attn,
    ) = call(
        functools.partial(output_kernel, cs, csh, wide, seq),
        (
            sds((cs, C), F32),
            sds((3, cs, 2 * C), F32),
            sds((cs, 2 * C), F32),
            sds((cs, C), F32),
            sds((cs, C), F32),
            sds((QUERIES, cs), F32),
            sds((cs, C), F32),
            sds((cs, C), F32),
            sds((cs, C), F32),
            sds((cs, C), F32),
        ),
        "outputs",
        args=(peers, *ones, *twos, queries, w_query),
        in_specs=[SM] + [VM] * (2 * seq + 2),
        out_specs=(VM,) * 10,
        scratch_shapes=[
            pltpu.VMEM((4 * cs, wide1), F32),
            pltpu.VMEM((4 * cs, wide2 + LANES), F32),
            pltpu.VMEM((4 * cs, small_width), F32),
            pltpu.VMEM((LANES, LANES), F32),
            pltpu.VMEM((LANES, C), F32),
        ],
    )
    return (
        layer_out,
        skip_out,
        grad_input,
        grad_step,
        grad_conv,
        grad_cond,
        grad_res,
        grad_skip,
        grad_queries,
        grad_query,
        grad_key,
        grad_value,
        grad_attn,
        jnp.transpose(grad_film.reshape(2, csh, cs), (2, 0, 1)),
    )


def solution(mesh):
    frames = P("dp", None, "seq")
    matrix = P("dp", None)
    return jax.shard_map(
        functools.partial(body, mesh.shape["dp"], mesh.shape["seq"]),
        mesh=mesh,
        in_specs=(
            frames,
            frames,
            P("dp", None),
            P("dp"),
            P("dp", "seq", None),
            P("dp"),
            matrix,
            P(None, "dp", None),
            matrix,
            matrix,
            matrix,
            P(None, "dp"),
            matrix,
            matrix,
            matrix,
            matrix,
            frames,
            frames,
            frames,
        ),
        out_specs=(
            frames,
            frames,
            frames,
            matrix,
            P(None, "dp", None),
            matrix,
            matrix,
            matrix,
            P(None, "dp"),
            matrix,
            matrix,
            matrix,
            matrix,
            frames,
        ),
        check_vma=False,
    )
```

```python
import functools
import math

import jax
import jax.numpy as jnp
from jax import lax
from jax.experimental import pallas as pl
from jax.experimental.pallas import tpu as pltpu
from jax.sharding import PartitionSpec as P

C = 512
HEADS = 8
QUERIES = 32
HEAD_DIM = 64
SHIFT = 4
SQRT_HALF = 0.7071067811865476
NORM_EPS = 1e-05
MASKED_SCORE = -1e30
LANES = 128
RP = 16
NR = 4
EARLY = 640
F32 = jnp.float32
BF16 = jnp.bfloat16
VMEM_BYTES = 50 * 1024 * 1024


def nn(a, b):
    return lax.dot_general(a, b, (((1,), (0,)), ((), ())), preferred_element_type=F32)


def nt(a, b):
    return lax.dot_general(a, b, (((1,), (1,)), ((), ())), preferred_element_type=F32)


def parts(v, count):
    out = []
    for _ in range(count):
        low = v.astype(BF16).astype(F32)
        out.append(low)
        v = v - low
    return jnp.concatenate(out, axis=0).astype(BF16)


def fold(v, count):
    rows = v.shape[0] // count
    total = v[:rows]
    for k in range(1, count):
        total = total + v[k * rows : (k + 1) * rows]
    return total


def lane_ids(shape):
    return lax.broadcasted_iota(jnp.int32, shape, len(shape) - 1)


def sds(shape, dtype):
    return jax.ShapeDtypeStruct(shape, dtype)


VM = pl.BlockSpec(memory_space=pltpu.VMEM)
HB = pl.BlockSpec(memory_space=pl.ANY)
SM = pl.BlockSpec(memory_space=pltpu.SMEM)


def whole(shape):
    return pl.BlockSpec(shape, lambda i: (0,) * len(shape), pipeline_mode=pl.Buffered(1))


class Got:
    def __init__(self, array):
        self.array = array


class Caller:
    def __init__(self):
        self.done = {}

    def __call__(self, kernel, out_shape, name, args, flops=0, nbytes=0, prefetch=0, after=(), **kw):
        single = not isinstance(out_shape, tuple)
        shapes = (out_shape,) if single else out_shape
        specs = kw["out_specs"]
        specs = (specs,) if single else specs
        pinned = tuple(
            v if spec is SM else pltpu.HBM(v.shape, v.dtype) for v, spec in zip(shapes, specs)
        )
        in_specs = list(kw.pop("in_specs"))
        count = prefetch + len(in_specs)
        args = list(args)
        extra = len(after)
        for before in after:
            in_specs.append(HB)
            args.append(self.done[before] if isinstance(before, str) else before)

        def run(*refs):
            return kernel(*refs[:count], *refs[count + extra :])

        values = []
        for k, v in enumerate(args):
            spec = SM if k < prefetch else in_specs[k - prefetch]
            if isinstance(v, Got):
                values.append(v.array)
            elif spec is SM:
                values.append(v)
            else:
                values.append(pltpu.with_memory_space_constraint(v, pltpu.HBM))
        spec = pltpu.PrefetchScalarGridSpec(
            num_scalar_prefetch=prefetch,
            grid=kw.pop("grid", ()),
            in_specs=in_specs,
            out_specs=kw.pop("out_specs"),
            scratch_shapes=kw.pop("scratch_shapes", ()),
        )
        out = pl.pallas_call(
            run,
            out_shape=pinned[0] if single else pinned,
            name=name,
            grid_spec=spec,
            cost_estimate=pl.CostEstimate(
                flops=1, bytes_accessed=1, transcendentals=0
            ),
            compiler_params=pltpu.CompilerParams(vmem_limit_bytes=VMEM_BYTES),
        )(*values)
        self.done[name] = out if single else out[0]
        return out


def head_pack_kernel(
    csh,
    local,
    group_ref,
    bit_ref,
    attn_ref,
    film_ref,
    wq_ref,
    wk_ref,
    wv_ref,
    queries_ref,
    prompt_ref,
    out_ref,
    mine_ref,
    other_ref,
    scr,
):
    cs = attn_ref.shape[0]
    arows = mine_ref.shape[0]
    mine_ref[...] = prompt_ref[pl.ds(bit_ref[0] * arows, arows)]
    other_ref[...] = prompt_ref[pl.ds((1 - bit_ref[0]) * arows, arows)]
    out_ref[:, 0:C] = attn_ref[...]
    off = C
    scr[...] = jnp.zeros((2 * LANES, LANES), F32)
    scr[0 : 2 * csh, 0:cs] = film_ref[...].astype(F32)
    scr[LANES : LANES + QUERIES, 0:cs] = queries_ref[...].astype(F32)
    film = scr[0:LANES].T[0:cs]
    table = scr[LANES : 2 * LANES].T[0:cs]
    turn = lax.rem(C - local * group_ref[0], C)
    blocks = [film[:, 0 : 2 * csh]]
    for ref in (wq_ref, wk_ref, wv_ref):
        blocks.append(pltpu.roll(ref[...].astype(F32), turn, 1)[:, 0:local])
    blocks.append(table)
    for block in blocks:
        width = min(block.shape[1], out_ref.shape[1] - off)
        out_ref[:, off : off + width] = block[:, 0:width].astype(BF16)
        off += width
    if off < out_ref.shape[1]:
        out_ref[:, off:] = jnp.zeros((cs, out_ref.shape[1] - off), BF16)


SIDE = 480


def turned_pack_kernel(cs, bit_ref, conv_ref, cond_ref, res_ref, skip_ref, step_ref, out_ref, side_ref, middle_ref, scr):
    for k in range(3):
        scr[k * cs : (k + 1) * cs] = conv_ref[k]
    scr[3 * cs : 4 * cs] = cond_ref[...]
    turned = scr[...].T
    out_ref[0 : 2 * C - SIDE] = turned[0 : 2 * C - SIDE]
    at = 2 * C - SIDE
    for ref in (res_ref, skip_ref, step_ref):
        for lane in range(0, C, 4 * cs):
            out_ref[at : at + cs] = ref[:, lane : lane + 4 * cs]
            at += cs
    out_ref[at : at + SIDE] = turned[2 * C - SIDE :]
    middle_ref[...] = out_ref[SIDE:at]
    side_ref[...] = out_ref[pl.ds(pl.multiple_of(bit_ref[0] * at, 16), SIDE)]


def pair_kernel(a_ref, b_ref, out_ref):
    for p in range(out_ref.shape[0]):
        out_ref[p, 0] = a_ref[...]
        out_ref[p, 1] = b_ref[...]


def table_kernel(
    frames, index_ref, steps_ref, ids_smem, ids_ref, flags_ref, blocks_ref, emb_ref
):
    rows, length = ids_ref.shape
    count = length // frames
    me = index_ref[0]
    for r in range(rows):
        here = ids_smem[r, me * frames]
        before = ids_smem[r, jnp.maximum(me * frames - 1, 0)]
        after = ids_smem[r, jnp.minimum((me + 1) * frames, length - 1)]
        flags_ref[0, r] = jnp.where((me > 0) & (before == here), 1, 0).astype(jnp.int32)
        flags_ref[1, r] = jnp.where((me < count - 1) & (after == here), 1, 0).astype(jnp.int32)
    blocks_ref[...] = jnp.zeros(blocks_ref.shape, jnp.int32)
    for s in range(count):
        blocks_ref[0:rows, s : s + 1] = ids_ref[:, s * frames : s * frames + 1]
    half = C // 2
    row = lax.broadcasted_iota(jnp.int32, (RP, half), 0)
    at = lane_ids((RP, half)).astype(F32)
    frequency = jnp.exp(at * (-math.log(10000.0) / half))
    step = jnp.zeros((RP, half), F32)
    for r in range(rows):
        step = jnp.where(row == r, steps_ref[r].astype(F32), step)
    angle = step * frequency
    emb_ref[...] = jnp.zeros(emb_ref.shape, BF16)
    emb_ref[0:RP, 0:half] = jnp.where(row < rows, jnp.sin(angle), 0.0).astype(BF16)
    emb_ref[0:RP, half:C] = jnp.where(row < rows, jnp.cos(angle), 0.0).astype(BF16)


def edge_kernel(x_ref, first_ref, last_ref):
    rows = x_ref.shape[0]
    lane = lane_ids((C, LANES))
    first = jnp.zeros((C, LANES), F32)
    last = jnp.zeros((C, LANES), F32)
    for r in range(rows):
        v = x_ref[r].astype(F32)
        here = (lane // SHIFT) == r
        first = jnp.where(here, pltpu.roll(v, SHIFT * r, 1) if r else v, first)
        last = jnp.where(here, pltpu.roll(v, SHIFT * r + SHIFT, 1), last)
    first_ref[...] = first.T[0 : rows * SHIFT].astype(BF16)
    last_ref[...] = last.T[0 : rows * SHIFT].astype(BF16)


def halo_columns(ref):
    v = ref[...].astype(F32)
    return jnp.concatenate([v, jnp.zeros((LANES - v.shape[0], C), F32)], axis=0).T


def begin(copies):
    for copy in copies:
        copy.start()


def finish(copies):
    for copy in copies:
        copy.wait()


def turned_copies(meta, refs, off_ref, cs, wt, others, sems):
    dp = len({k for k, _ in meta})
    pairs = []

    def conv(k, ref, first, row, rows):
        if wt is not None:
            lanes = pl.ds(pl.multiple_of(off_ref[k] * 4, LANES), 4 * cs)
            at = row if isinstance(row, int) else pl.multiple_of(row, 16)
            pairs.append((ref.at[pl.ds(first, rows)], wt.at[pl.ds(at, rows), lanes]))

    def rest(k, ref, at):
        row = pl.ds(pl.multiple_of(off_ref[k], 16), cs)
        for other in others:
            for lane in range(0, C, 4 * cs):
                if other is not None:
                    dst, start = other
                    pairs.append((ref.at[pl.ds(at, cs)], dst.at[row, pl.ds(start + lane, 4 * cs)]))
                at += cs

    inner = 2 * C - 2 * SIDE
    for (k, which), ref in zip(meta, refs):
        if which is None:
            conv(k, ref, 0, 0, SIDE + inner)
            rest(k, ref, SIDE + inner)
            conv(k, ref, ref.shape[0] - SIDE, 2 * C - SIDE, SIDE)
        elif which == 2:
            conv(k, ref, 0, SIDE, inner)
            rest(k, ref, inner)
        else:
            conv(k, ref, 0, off_ref[dp + which] * (2 * C - SIDE), SIDE)
    return [pltpu.make_async_copy(a, b, sems.at[n]) for n, (a, b) in enumerate(pairs)]


def head_copies(refs, off_ref, dst, sems):
    copies = []
    for k, ref in enumerate(refs):
        row = pl.ds(pl.multiple_of(off_ref[k], 16), ref.shape[0])
        copies.append(pltpu.make_async_copy(ref, dst.at[row], sems.at[k]))
    return copies


def forward_kernel(
    meta, dp, csh, off_ref, flags_ref, x_ref, cond_ref, dout_ref, left_ref, right_ref, emb_ref, pooled_ref, *refs
):
    turned, refs = refs[: len(meta)], refs[len(meta) :]
    (
        inp_ref,
        gated_ref,
        fa_ref,
        fb_ref,
        skip_ref,
        mid_ref,
        stats_ref,
        wt_ref,
        rn_ref,
        step_ref,
        rst_ref,
        lift_ref,
        acc_ref,
        left_scr,
        right_scr,
        sems,
    ) = refs
    cs = C // dp
    i = pl.program_id(0)
    lane = lane_ids((C, LANES))

    @pl.when(i == 0)
    def _():
        copies = turned_copies(
            meta,
            turned,
            off_ref,
            cs,
            wt_ref,
            ((rn_ref, 0), (rn_ref, C), (step_ref, 0)),
            sems,
        )
        begin(copies)
        acc_ref[...] = jnp.zeros((C, LANES), F32)
        left_scr[...] = halo_columns(left_ref)
        right_scr[...] = halo_columns(right_ref)
        finish(copies)
        lift = nn(emb_ref[0:RP], step_ref[...])
        lift = jnp.concatenate([lift, jnp.zeros((LANES - RP, C), F32)], axis=0)
        lift_ref[...] = lift.T
        rst_ref[...] = rn_ref[...].T

    lift = pltpu.roll(lift_ref[...], lax.rem(LANES - NR * i, LANES), 1)
    left = left_scr[...]
    right = right_scr[...]

    def put(tap, cols, value):
        for d in range(dp):
            at = d * 4 * cs + tap * cs
            inp_ref[at : at + cs, cols] = value[d * cs : (d + 1) * cs]

    for j in range(NR):
        r = NR * i + j
        lc = lift[:, j : j + 1]
        sh = (x_ref[j].astype(F32) + lc).astype(BF16)
        shf = sh.astype(F32)
        lh = pltpu.roll(left, lax.rem(LANES - SHIFT * r, LANES), 1)
        lh = jnp.where(flags_ref[0, r] > 0, (lh + lc).astype(BF16).astype(F32), 0.0)
        rh = pltpu.roll(right, LANES - SHIFT - SHIFT * r, 1)
        rh = jnp.where(flags_ref[1, r] > 0, (rh + lc).astype(BF16).astype(F32), 0.0)
        cols = slice(j * LANES, (j + 1) * LANES)
        put(0, cols, jnp.where(lane < SHIFT, lh, pltpu.roll(shf, SHIFT, 1)).astype(BF16))
        put(1, cols, sh)
        put(
            2,
            cols,
            jnp.where(lane >= LANES - SHIFT, rh, pltpu.roll(shf, LANES - SHIFT, 1)).astype(BF16),
        )
        put(3, cols, cond_ref[j])
    pre = nn(wt_ref[...], inp_ref[...])
    th = jnp.tanh(pre[:C])
    sg = jax.nn.sigmoid(pre[C:])
    gf = th * sg
    fa_ref[...] = (sg - gf * th).astype(BF16)
    fb_ref[...] = (gf * (1.0 - sg)).astype(BF16)
    g = gf.astype(BF16)
    gated_ref[...] = g
    rs = nn(rst_ref[...], g)
    acc = acc_ref[...]
    for j in range(NR):
        r = NR * i + j
        cols = slice(j * LANES, (j + 1) * LANES)
        skip_ref[j] = rs[C:, cols].astype(BF16)
        mid = ((x_ref[j].astype(F32) + rs[:C, cols]) * SQRT_HALF).astype(BF16)
        mid_ref[:, cols] = mid
        mf = mid.astype(F32)
        df = dout_ref[j].astype(F32)
        total = jnp.sum(mf, axis=1, keepdims=True)
        dev = mf - total * (1.0 / LANES)
        acc = jnp.where(lane == r, total, acc)
        acc = jnp.where(lane == RP + r, jnp.sum(dev * dev, axis=1, keepdims=True), acc)
        acc = jnp.where(lane == 2 * RP + r, jnp.sum(df, axis=1, keepdims=True), acc)
        acc = jnp.where(lane == 3 * RP + r, jnp.sum(df * dev, axis=1, keepdims=True), acc)
    acc_ref[...] = acc

    @pl.when(i == pl.num_programs(0) - 1)
    def _():
        t = acc.T
        for s in range(C // csh):
            cols = slice(s * csh, (s + 1) * csh)
            stats_ref[s, 0 : 2 * RP, 0:csh] = t[0 : 2 * RP, cols]
            stats_ref[s, 0 : 2 * RP, csh : 2 * csh] = t[2 * RP : 4 * RP, cols]
            stats_ref[s, 2 * RP : 3 * RP] = pooled_ref[:, 0 : 2 * csh]


def attention_kernel(dp, rows, heads, pairs, off, off_ref, bit_ref, len_ref, prompts, *refs):
    pieces, refs = refs[:dp], refs[dp:]
    apack_ref, prow, probs_ref, u_ref, pooled_ref, qp_ref, qkv_ref, abd, sems = refs
    copies = head_copies(pieces, off_ref, apack_ref, sems)
    count = len(copies)
    for j in range(pairs):
        for i in range(2):
            copies.append(
                pltpu.make_async_copy(
                    prompts.at[j, i], prow.at[:, 2 * j + i], sems.at[count + 2 * j + i]
                )
            )
    begin(copies)
    local = prow.shape[2]
    total = 2 * pairs * local
    abd[...] = jnp.zeros(abd.shape, F32)
    lane = lane_ids((heads * QUERIES, total))
    place = jnp.zeros((heads * QUERIES, total), jnp.int32)
    for k in range(2 * pairs):
        here = (k // 2) * 2 + (bit_ref[0] if k % 2 == 0 else 1 - bit_ref[0])
        place = jnp.where(lane // local == k, here * local + lane % local, place)
    finish(copies)
    wide = heads * HEAD_DIM
    qkv = apack_ref[:, off : off + qkv_ref.shape[0]].T
    qkv_ref[...] = qkv
    qp = nt(qkv[3 * wide : 3 * wide + QUERIES], qkv[0:wide])
    qp_ref[...] = qp
    st = []
    for g in range(heads):
        cols = slice(g * HEAD_DIM, (g + 1) * HEAD_DIM)
        st.append(fold(nn(parts(qp[:, cols], 3), qkv[wide + cols.start : wide + cols.stop]), 3))
    st = jnp.concatenate(st, axis=0) * (1.0 / math.sqrt(HEAD_DIM))
    table = prow[...].reshape(rows * total, C)
    scores = fold(nt(parts(st, 3), table), 3)
    for r in range(rows):
        cols = slice(r * total, (r + 1) * total)
        live = place < len_ref[bit_ref[0] * rows + r]
        s = jnp.where(live, scores[:, cols], MASKED_SCORE)
        e = jnp.where(live, jnp.exp(s - jnp.max(s, axis=1, keepdims=True)), 0.0)
        p = e / jnp.sum(e, axis=1, keepdims=True)
        probs_ref[:, cols] = p
        for g in range(heads):
            abd[8 * g + r : 8 * g + r + 1, cols] = jnp.sum(
                p[g * QUERIES : (g + 1) * QUERIES], axis=0, keepdims=True
            )
    u = fold(nn(parts(abd[...], 2), table), 2)
    u_ref[...] = u
    pooled_ref[...] = jnp.zeros(pooled_ref.shape, F32)
    for g in range(heads):
        first = 2 * wide + g * HEAD_DIM
        v = parts(u[8 * g : 8 * g + 8] * (1.0 / QUERIES), 2)
        pooled_ref[0:8, g * HEAD_DIM : (g + 1) * HEAD_DIM] = fold(
            nt(v, qkv[first : first + HEAD_DIM]), 2
        )


def stats_kernel(
    csh, heads, rows, seg_ref, x_ref, apack_ref, out_ref, dfilm_ref, pooled_ref, memory_ref, scratch
):
    count = x_ref.shape[0]
    wide = heads * HEAD_DIM
    seg = seg_ref[...]
    scratch[...] = jnp.zeros(scratch.shape, F32)
    for s in range(count):
        group, part = s // 2, s % 2
        scratch[part * rows : (part + 1) * rows, group * wide : (group + 1) * wide] = x_ref[
            s, 2 * RP : 2 * RP + rows, 0:wide
        ]
    pooled = scratch[...].astype(BF16)
    pooled_ref[...] = pooled
    memory = nn(pooled, apack_ref[:, 0:C]).astype(BF16)
    memory_ref[...] = memory
    film = nn(memory, apack_ref[:, C : C + 2 * csh])
    f0 = film[:, 0:csh]
    f1 = film[:, csh : 2 * csh]
    total = [x_ref[s, 0:RP, 0:csh] for s in range(count)]
    second = [x_ref[s, RP : 2 * RP, 0:csh] for s in range(count)]
    dsum = [x_ref[s, 0:RP, csh : 2 * csh] for s in range(count)]
    cross = [x_ref[s, RP : 2 * RP, csh : 2 * csh] for s in range(count)]
    means = [v * (1.0 / LANES) for v in total]
    d0 = jnp.zeros((RP, csh), F32)
    d1 = jnp.zeros((RP, csh), F32)
    for me in range(count):
        same = [(seg[:, s : s + 1] == seg[:, me : me + 1]).astype(F32) for s in range(count)]
        frames = sum(same) * float(LANES)
        inv = 1.0 / frames
        mean = sum(m * v for m, v in zip(same, total)) * inv
        var = (
            sum(
                m * (v + float(LANES) * (u - mean) * (u - mean))
                for m, v, u in zip(same, second, means)
            )
            * inv
        )
        scale = lax.rsqrt(var + NORM_EPS)
        dtot = sum(m * v for m, v in zip(same, dsum))
        xtot = sum(m * (v + (u - mean) * d) for m, v, u, d in zip(same, cross, means, dsum)) * scale
        mean_part = f0 * dtot * inv
        cross_part = f0 * xtot * inv
        slope = scale * scale * cross_part
        out_ref[me, 0:RP, 0:csh] = 1.0 + f0 * scale
        out_ref[me, RP : 2 * RP, 0:csh] = f1 - f0 * scale * mean
        out_ref[me, 0:RP, csh : 2 * csh] = -slope
        out_ref[me, RP : 2 * RP, csh : 2 * csh] = slope * mean - scale * mean_part
        d0 = d0 + (cross[me] + (means[me] - mean) * dsum[me]) * scale
        d1 = d1 + dsum[me]
    dfilm = jnp.concatenate([d0, d1], axis=1).astype(BF16)
    dfilm_ref[...] = dfilm
    dmem = nt(dfilm, apack_ref[:, C : C + 2 * csh])
    dpool = nt(dmem.astype(BF16), apack_ref[:, 0:C])
    for s in range(count):
        group, part = s // 2, s % 2
        rolled = pltpu.roll(dpool, RP - part * rows, 0) if part else dpool
        out_ref[s, 2 * RP : 3 * RP, 0:csh] = dmem[:, s * csh : (s + 1) * csh]
        out_ref[s, 2 * RP : 3 * RP, csh : 2 * csh] = jnp.zeros((RP, csh), F32)
        out_ref[s, 3 * RP : 4 * RP] = rolled[:, group * wide : (group + 1) * wide]


def coef_columns(csh, coef_ref, rows_ref, cols_ref):
    rows_ref[...] = jnp.zeros(rows_ref.shape, F32)
    for s in range(C // csh):
        cols = slice(s * csh, (s + 1) * csh)
        rows_ref[0 : 2 * RP, cols] = coef_ref[s, 0 : 2 * RP, 0:csh]
        rows_ref[2 * RP : 4 * RP, cols] = coef_ref[s, 0 : 2 * RP, csh : 2 * csh]
    cols_ref[...] = rows_ref[...].T


def skip_grad_kernel(gated_ref, dskip_ref, out_ref, right):
    for r in range(dskip_ref.shape[0]):
        right[:, r * LANES : (r + 1) * LANES] = dskip_ref[r]
    out_ref[...] = nt(gated_ref[...], right[...]).astype(BF16)


def backward_kernel(meta, dp, csh, gates, order_ref, off_ref, coef_ref, mid_ref, dout_ref, dskip_ref, fa_ref, fb_ref, inp_ref, gated_ref, gskip_ref, flags_ref, *refs):
    turned, refs = refs[: len(meta)], refs[len(meta) :]
    dpre_ref, dres_ref, sums_ref, refs = refs[0], refs[1], refs[2], refs[3:]
    outs, refs = (refs[0:2], refs[2:4]), refs[4:]
    rows_ref, cols_ref, w_ref, both_ref, dpt_ref, drt_ref, sems = refs
    cs = C // dp
    span = NR * LANES
    i = pl.program_id(0)

    @pl.when(i == 0)
    def _():
        copies = turned_copies(
            meta, turned, off_ref, cs, None, ((w_ref, 0), (w_ref, C), None), sems
        )
        begin(copies)
        coef_columns(csh, coef_ref, rows_ref, cols_ref)
        sums_ref[...] = jnp.zeros(sums_ref.shape, F32)
        finish(copies)

    @pl.when(i < gates)
    def _():
        coef = pltpu.roll(cols_ref[...], lax.rem(LANES - NR * i, LANES), 1)
        for j in range(NR):
            cols = slice(j * LANES, (j + 1) * LANES)
            mf = mid_ref[:, cols].astype(F32)
            df = dout_ref[j].astype(F32)
            a = coef[:, j : j + 1]
            be = coef[:, 2 * RP + j : 2 * RP + j + 1]
            ga = coef[:, 3 * RP + j : 3 * RP + j + 1]
            dmid = (a * df + (be * mf + ga)).astype(BF16).astype(F32)
            both_ref[0:C, cols] = (dmid * SQRT_HALF).astype(BF16)
            both_ref[C : 2 * C, cols] = dskip_ref[j]
        dres = both_ref[0:C]
        dres_ref[...] = dres
        dg = nn(w_ref[...], both_ref[...])
        dt = (dg * fa_ref[...].astype(F32)).astype(BF16)
        ds = (dg * fb_ref[...].astype(F32)).astype(BF16)
        dpre_ref[0:C] = dt
        dpre_ref[C : 2 * C] = ds
        at = pl.ds(pl.multiple_of(i * span, span), span)
        dpt_ref[at, 0:C] = dt.T
        dpt_ref[at, C : 2 * C] = ds.T
        drt_ref[at] = dres.T
        frame = lax.broadcasted_iota(jnp.int32, (span, LANES), 0)
        column = lane_ids((span, LANES))
        place = frame % LANES
        which = frame // LANES
        keep_l = jnp.zeros((span, LANES), jnp.int32)
        keep_r = jnp.zeros((span, LANES), jnp.int32)
        for j in range(NR):
            keep_l = jnp.where(which == j, flags_ref[0, NR * i + j], keep_l)
            keep_r = jnp.where(which == j, flags_ref[1, NR * i + j], keep_r)
        row = NR * i + which
        use0 = (column == row) & ((place >= SHIFT) | (keep_l > 0))
        use1 = column == RP + row
        use2 = (column == 2 * RP + row) & ((place < LANES - SHIFT) | (keep_r > 0))
        pick = jnp.where(use0 | use1 | use2, 1.0, 0.0).astype(BF16)
        sums_ref[...] = sums_ref[...] + nn(dpre_ref[...], pick)

    @pl.when(i >= gates)
    def _():
        g = nn(inp_ref[...], dpt_ref[...]).astype(BF16)
        h = nn(gated_ref[...], drt_ref[...]).astype(BF16)
        k = i - gates
        for parity, (one, two) in enumerate(outs):

            @pl.when(lax.rem(k, 2) == parity)
            def _():
                for t in range(4):
                    rows = slice(t * cs, (t + 1) * cs)
                    lanes = slice(t * LANES, (t + 1) * LANES)
                    one[0, rows, 0:LANES] = h[:, lanes]
                    one[0, rows, LANES : 2 * LANES] = gskip_ref[:, lanes]
                one[0, :, 2 * LANES :] = g[:, 0:EARLY]
                two[0] = g[:, EARLY:]


def step_grad_kernel(meta, dp, off_ref, sums_ref, emb_ref, *refs):
    turned, refs = refs[: len(meta)], refs[len(meta) :]
    keep_ref, give_ref, wt_ref, scr, sems = refs
    cs = C // dp
    copies = turned_copies(meta, turned, off_ref, cs, wt_ref, (None,) * 3, sems)
    begin(copies)
    sums = sums_ref[...].T
    emb = emb_ref[...].T
    finish(copies)
    total = jnp.zeros((RP, 4 * C), F32)
    lane = lane_ids((RP, 4 * C))
    all_taps = fold(nn(parts(sums[0 : 3 * RP], 2), wt_ref[...]), 2)
    for t in range(3):
        g = all_taps[t * RP : (t + 1) * RP]
        total = total + jnp.where((lane // cs) % 4 == t, g, 0.0)
    out = []
    for d in range(dp):
        block = total[:, d * 4 * cs : (d + 1) * 4 * cs]
        out.append(block[:, 0:cs] + block[:, cs : 2 * cs] + block[:, 2 * cs : 3 * cs])
    g = jnp.concatenate(out, axis=1)
    g = jnp.concatenate([g, jnp.zeros((LANES - RP, C), F32)], axis=0)
    hi = g.astype(BF16)
    lo = (g - hi.astype(F32)).astype(BF16)
    scr[...] = nn(emb, hi) + nn(emb, lo)
    for k in range(dp):
        v = scr[pl.ds(pl.multiple_of(off_ref[k], 16), cs)].astype(BF16)
        for t in range(4):
            (keep_ref, give_ref)[k % 2][k // 2, t * cs : (t + 1) * cs] = v[
                :, t * LANES : (t + 1) * LANES
            ]


def input_grad_kernel(meta, dp, off_ref, dpre_ref, dres_ref, *refs):
    turned, refs = refs[: len(meta)], refs[len(meta) :]
    base_ref, first_ref, last_ref, wt_ref, w_ref, facc_ref, lacc_ref, sems = refs
    cs = C // dp
    i = pl.program_id(0)
    lane = lane_ids((C, LANES))

    @pl.when(i == 0)
    def _():
        copies = turned_copies(meta, turned, off_ref, cs, wt_ref, (None,) * 3, sems)
        begin(copies)
        facc_ref[...] = jnp.zeros((C, LANES), F32)
        lacc_ref[...] = jnp.zeros((C, LANES), F32)
        finish(copies)
        for d in range(dp):
            v = wt_ref[:, d * 4 * cs : (d + 1) * 4 * cs].T
            for t in range(3):
                w_ref[t, d * cs : (d + 1) * cs] = v[t * cs : (t + 1) * cs]

    dpre = dpre_ref[...]
    y0 = nn(w_ref[0], dpre)
    y1 = nn(w_ref[1], dpre)
    y2 = nn(w_ref[2], dpre)
    facc = facc_ref[...]
    lacc = lacc_ref[...]
    for j in range(NR):
        r = NR * i + j
        cols = slice(j * LANES, (j + 1) * LANES)
        z0 = pltpu.roll(y0[:, cols], LANES - SHIFT, 1)
        z2 = pltpu.roll(y2[:, cols], SHIFT, 1)
        inner0 = lane < LANES - SHIFT
        inner2 = lane >= SHIFT
        v = y1[:, cols]
        base_ref[:, cols] = (
            v
            + jnp.where(inner0, z0, 0.0)
            + jnp.where(inner2, z2, 0.0)
            + dres_ref[:, cols].astype(F32)
        ).astype(BF16)
        here = (lane // SHIFT) == r
        facc = jnp.where(here, pltpu.roll(z0, lax.rem(SHIFT * r + SHIFT, LANES), 1), facc)
        lacc = jnp.where(here, pltpu.roll(z2, SHIFT * r, 1), lacc)
    facc_ref[...] = facc
    lacc_ref[...] = lacc

    @pl.when(i == pl.num_programs(0) - 1)
    def _():
        first_ref[...] = facc.T[0 : first_ref.shape[0]].astype(BF16)
        last_ref[...] = lacc.T[0 : last_ref.shape[0]].astype(BF16)


def finish_kernel(csh, flags_ref, base_ref, left_ref, right_ref, mid_ref, coef_ref, out_ref, layer_ref, rows_ref, cols_ref, left_scr, right_scr):
    i = pl.program_id(0)
    lane = lane_ids((C, LANES))

    @pl.when(i == 0)
    def _():
        coef_columns(csh, coef_ref, rows_ref, cols_ref)
        left_scr[...] = halo_columns(left_ref)
        right_scr[...] = halo_columns(right_ref)

    coef = pltpu.roll(cols_ref[...], lax.rem(LANES - NR * i, LANES), 1)
    left = left_scr[...]
    right = right_scr[...]
    for j in range(NR):
        r = NR * i + j
        cols = slice(j * LANES, (j + 1) * LANES)
        lh = pltpu.roll(left, lax.rem(LANES - SHIFT * r, LANES), 1)
        rh = pltpu.roll(right, LANES - SHIFT - SHIFT * r, 1)
        lh = jnp.where((lane < SHIFT) & (flags_ref[0, r] > 0), lh, 0.0)
        rh = jnp.where((lane >= LANES - SHIFT) & (flags_ref[1, r] > 0), rh, 0.0)
        out_ref[j] = (base_ref[:, cols].astype(F32) + lh + rh).astype(BF16)
        a = coef[:, j : j + 1]
        b = coef[:, RP + j : RP + j + 1]
        layer_ref[j] = (a * mid_ref[:, cols].astype(F32) + b).astype(BF16)


def add_blocks_kernel(count, *refs):
    ins, (keep_ref, give_ref) = refs[: 2 * count], refs[2 * count :]
    at = 0
    for p in range(count):
        a_ref, b_ref = ins[2 * p : 2 * p + 2]
        width = a_ref.shape[2]
        for j in range(a_ref.shape[0]):
            v = a_ref[j].astype(F32) + b_ref[j].astype(F32)
            (keep_ref, give_ref)[j % 2][j // 2, :, at : at + width] = v.astype(BF16)
        at += width


def add_halves_kernel(bit, index_ref, a_ref, b_ref, keep_ref, give_ref, scr):
    half = a_ref.shape[0] // 2
    mine = lax.rem(index_ref[0] // bit, 2)
    scr[...] = a_ref[...].astype(F32) + b_ref[...].astype(F32)
    keep_ref[...] = scr[pl.ds(pl.multiple_of(mine * half, 8), half)].astype(BF16)
    give_ref[...] = scr[pl.ds(pl.multiple_of((1 - mine) * half, 8), half)].astype(BF16)


def add_pieces_kernel(a_ref, b_ref, out_ref):
    v = a_ref[...].astype(F32) + b_ref[...].astype(F32)
    size = out_ref.shape[1]
    for p in range(out_ref.shape[0]):
        out_ref[p] = v[p * size : (p + 1) * size].astype(BF16)


def sum_copies_kernel(a_ref, *refs):
    out_ref = refs[-1]
    v = a_ref[0].astype(F32)
    for p in range(1, a_ref.shape[0]):
        v = v + a_ref[p].astype(F32)
    v = v.astype(BF16)
    for p in range(out_ref.shape[0]):
        out_ref[p, :, 0 : v.shape[1]] = v
        if len(refs) > 1:
            out_ref[p, :, v.shape[1] :] = refs[0][...]


def small_sum_kernel(csh, wide, bit_ref, keep_ref, got_ref, film_ref, attn_ref, mine_ref, other_ref, turn):
    v = keep_ref[0].astype(F32) + got_ref[0].astype(F32)
    cs = v.shape[0]
    film = 2 * wide + csh
    turn[...] = jnp.zeros(turn.shape, F32)
    turn[0:cs, 0 : 2 * csh] = v[:, film : film + 2 * csh]
    film_ref[...] = turn[...].T[0 : 2 * csh, 0:cs]
    attn_ref[...] = v[:, 2 * wide : film]
    last = film + 2 * csh
    even = bit_ref[0] == 0
    for one, two, rows, width in (
        (v[:, 0:wide], v[:, wide : 2 * wide], slice(0, cs), wide),
        (
            v[0:QUERIES, last : last + wide // 2],
            v[0:QUERIES, last + wide // 2 : last + wide],
            slice(cs, cs + QUERIES),
            wide // 2,
        ),
    ):
        mine_ref[rows, 0:width] = jnp.where(even, one, two).astype(BF16)
        other_ref[rows, 0:width] = jnp.where(even, two, one).astype(BF16)
    mine_ref[cs:, wide // 2 :] = jnp.zeros((QUERIES, wide // 2), BF16)
    other_ref[cs:, wide // 2 :] = jnp.zeros((QUERIES, wide // 2), BF16)


def small_piece_kernel(csh, wide, attn_ref, mine_ref, got_ref, out_ref):
    v = mine_ref[...].astype(F32) + got_ref[...].astype(F32)
    attn = attn_ref[...]
    cs = attn.shape[0]
    rows = out_ref.shape[0]
    at = 0
    for row in range(0, cs, rows):
        out_ref[:, at : at + wide] = v[row : row + rows].astype(BF16)
        out_ref[:, at + wide : at + wide + csh] = attn[row : row + rows].astype(BF16)
        at += wide + csh
    for row in range(0, QUERIES, rows):
        block = v[cs + row : cs + min(row + rows, QUERIES), 0 : wide // 2]
        if block.shape[0] < rows:
            pad = jnp.zeros((rows - block.shape[0], wide // 2), F32)
            block = jnp.concatenate([block, pad], axis=0)
        out_ref[:, at : at + wide // 2] = block.astype(BF16)
        at += wide // 2


def output_kernel(
    cs,
    csh,
    wide,
    seq,
    bit_ref,
    *refs,
):
    own1, got1, all2, refs = *refs[:3], refs[3:]
    (
        queries_ref,
        wq_ref,
        step_ref,
        conv_ref,
        cond_ref,
        res_ref,
        skip_ref,
        gqueries_ref,
        gquery_ref,
        key_ref,
        value_ref,
        attn_ref,
        scr1,
        scr2,
        small,
        qscr,
        dq,
    ) = refs
    count, size = own1.shape[0], own1.shape[1]
    wide2 = scr2.shape[1]
    bit = bit_ref[0]
    for one, side in ((own1, bit), (got1, 1 - bit)):
        for p in range(count):
            rows = pl.ds(pl.multiple_of((side * count + p) * size, 8), size)
            scr1[rows] = one[p].astype(F32)
    for s in range(seq):
        at = ((s % 2) * count + s // 2) * size
        v = all2[s].astype(F32)
        scr2[at : at + size] = v[:, 0:wide2]
        small[s * size : (s + 1) * size] = v[:, wide2:]
    for t in range(4):
        rows = slice(t * cs, (t + 1) * cs)
        lanes = slice(t * LANES, (t + 1) * LANES)
        res_ref[:, lanes] = scr1[rows, 0:LANES]
        skip_ref[:, lanes] = scr1[rows, LANES : 2 * LANES]
        rest = 2 * C - EARLY
        step_ref[:, lanes] = scr2[rows, rest : rest + LANES]
        if t < 3:
            conv_ref[t, :, 0:EARLY] = scr1[rows, 2 * LANES : 2 * LANES + EARLY]
            conv_ref[t, :, EARLY:] = scr2[rows, 0:rest]
        else:
            cond_ref[:, 0:EARLY] = scr1[rows, 2 * LANES : 2 * LANES + EARLY]
            cond_ref[:, EARLY:] = scr2[rows, 0:rest]
    dq[...] = jnp.zeros(dq.shape, F32)
    for s in range(seq):
        v = small[s * size : (s + 1) * size]
        group, even = s // 2, s % 2 == 0
        out = key_ref if even else value_ref
        at = 0
        for row in range(0, cs, size):
            out[row : row + size, group * wide : (group + 1) * wide] = v[:, at : at + wide]
            attn_ref[row : row + size, s * csh : (s + 1) * csh] = v[:, at + wide : at + wide + csh]
            at += wide + csh
        first = group * wide + (0 if even else wide // 2)
        for row in range(0, QUERIES, size):
            count = min(size, QUERIES - row)
            dq[row : row + count, first : first + wide // 2] = v[0:count, at : at + wide // 2]
            at += wide // 2
    qscr[...] = jnp.zeros((LANES, LANES), F32)
    qscr[0:QUERIES, 0:cs] = queries_ref[...].astype(F32)
    qt = qscr[...].T.astype(BF16)
    d = dq[...]
    hi = d.astype(BF16)
    lo = (d - hi.astype(F32)).astype(BF16)
    gquery_ref[...] = (nn(qt, hi) + nn(qt, lo))[0:cs]
    gqueries_ref[...] = fold(nt(parts(d[0:QUERIES], 2), wq_ref[...]), 2)


def attention_back_kernel(
    rows,
    csh,
    dp,
    off_ref,
    prow,
    probs_ref,
    u_ref,
    qp_ref,
    qkv_ref,
    pooled_ref,
    memory_ref,
    dfilm_ref,
    got_ref,
    keep_ref,
    give_ref,
    ds,
    stack,
    right,
    out,
):
    count = got_ref.shape[0]
    total = prow.shape[1] * prow.shape[2]
    cs = C // dp
    table = prow[...].reshape(rows * total, C)
    wide = qp_ref.shape[1]
    heads = wide // HEAD_DIM
    datt = got_ref[0, 3 * RP : 4 * RP, 0:wide]
    dmem = got_ref[0, 2 * RP : 3 * RP, 0:csh]
    for s in range(1, count):
        datt = datt + got_ref[s, 3 * RP : 4 * RP, 0:wide]
        dmem = dmem + got_ref[s, 2 * RP : 3 * RP, 0:csh]
    datt = datt[0:8] * (1.0 / QUERIES)
    vh = []
    for g in range(heads):
        first = 2 * wide + g * HEAD_DIM
        v = parts(datt[:, g * HEAD_DIM : (g + 1) * HEAD_DIM], 2)
        vh.append(fold(nn(v, qkv_ref[first : first + HEAD_DIM]), 2))
    vh = jnp.concatenate(vh, axis=0)
    dp_all = fold(nt(parts(vh, 2), table), 2)
    for r in range(rows):
        cols = slice(r * total, (r + 1) * total)
        for g in range(heads):
            mine = slice(g * QUERIES, (g + 1) * QUERIES)
            p = probs_ref[mine, cols]
            dpr = dp_all[8 * g + r : 8 * g + r + 1, cols]
            inner = jnp.sum(p * dpr, axis=1, keepdims=True)
            ds[mine, cols] = p * (dpr - inner)
    tt = fold(nn(parts(ds[...], 2), table), 2)
    scale = 1.0 / math.sqrt(HEAD_DIM)
    dq = []
    stack[...] = jnp.zeros(stack.shape, F32)
    right[...] = jnp.zeros(right.shape, F32)
    stack[0 : heads * QUERIES] = tt
    stack[64:80] = u_ref[...]
    stack[80:96] = pooled_ref[...].astype(F32)
    stack[96:112] = memory_ref[...].astype(F32)
    for g in range(heads):
        cols = slice(g * HEAD_DIM, (g + 1) * HEAD_DIM)
        mine = slice(g * QUERIES, (g + 1) * QUERIES)
        wk = qkv_ref[wide + g * HEAD_DIM : wide + (g + 1) * HEAD_DIM]
        dq.append(fold(nt(parts(tt[mine], 2), wk), 2) * scale)
        right[mine, cols] = qp_ref[:, cols] * scale
        right[64 + 8 * g : 72 + 8 * g, wide + cols.start : wide + cols.stop] = datt[:, cols]
    right[80:96, 2 * wide : 2 * wide + csh] = dmem
    right[96:112, 2 * wide + csh : 2 * wide + 3 * csh] = dfilm_ref[...].astype(F32)
    out[...] = lax.dot_general(
        stack[...].T,
        right[...],
        (((1,), (0,)), ((), ())),
        precision=lax.Precision.HIGHEST,
        preferred_element_type=F32,
    )
    last = 2 * wide + 3 * csh
    for k in range(dp):
        ref = (keep_ref, give_ref)[k % 2]
        ref[k // 2] = out[pl.ds(pl.multiple_of(off_ref[k], 16), cs)].astype(BF16)
        for g in range(heads):
            first = last + g * HEAD_DIM
            ref[k // 2, 0:QUERIES, first : first + HEAD_DIM] = dq[g].astype(BF16)


def exchange(pieces, axis, groups=None):
    return lax.all_to_all(
        pieces, axis, split_axis=0, concat_axis=0, axis_index_groups=groups, tiled=True
    )


def flipped(v, axis, size, bit):
    return lax.ppermute(v, axis, [(d, d ^ bit) for d in range(size)])


class Reduction:
    def __init__(self, call, name, keep, give, dp, seq, index):
        self.call, self.name, self.dp, self.seq, self.index = call, name, dp, seq, index
        self.keep, self.flip = keep, 1
        self.got = flipped(give, "dp", dp, 1)

    def over_blocks(self, after=(), others=()):
        while 2 * self.flip < self.dp:
            group = (self,) + tuple(others)
            others = ()
            args = []
            for part in group:
                args += [part.keep, Got(part.got)]
            width = sum(part.keep.shape[2] for part in group)
            half = sds((self.keep.shape[0] // 2, self.keep.shape[1], width), BF16)
            self.keep, give = self.call(
                functools.partial(add_blocks_kernel, len(group)),
                (half, half),
                "blocks_" + self.name,
                args,
                after=after,
                in_specs=[VM] * len(args),
                out_specs=(VM, VM),
            )
            self.flip *= 2
            self.got = flipped(give, "dp", self.dp, self.flip)
        self.rest = self.keep.shape[1:]

    def over_half(self, after=()):
        rows, width = self.rest
        half = sds((rows // 2, width), BF16)
        self.keep, give = self.call(
            functools.partial(add_halves_kernel, 1),
            (half, half),
            "half_" + self.name,
            (self.index, self.keep.reshape(rows, width), Got(self.got.reshape(rows, width))),
            after=after,
            in_specs=[SM, VM, VM],
            out_specs=(VM, VM),
            scratch_shapes=[pltpu.VMEM((rows, width), F32)],
        )
        self.got = flipped(give, "seq", self.seq, 1)

    def over_pieces(self, after=()):
        rows, width = self.rest
        count = self.seq // 2
        self.groups = [[2 * k + b for k in range(count)] for b in range(2)]
        pieces = self.call(
            add_pieces_kernel,
            sds((count, rows // self.seq, width), BF16),
            "pieces_" + self.name,
            (self.keep, Got(self.got)),
            after=after,
            in_specs=[VM, VM],
            out_specs=VM,
        )
        self.got = exchange(pieces, "seq", self.groups)

    def over_copies(self, after=(), extra=None):
        args, (count, rows, width) = [Got(self.got)], self.got.shape
        if extra is not None:
            count = self.seq
        if extra is not None:
            args.append(extra)
            width += extra.shape[1]
        copies = self.call(
            sum_copies_kernel,
            sds((count, rows, width), BF16),
            "copies_" + self.name,
            args,
            after=after,
            in_specs=[VM] * len(args),
            out_specs=VM,
        )
        if extra is not None:
            return (Got(exchange(copies, "seq")),)
        own = exchange(copies, "seq", self.groups)
        return Got(own), Got(flipped(own, "seq", self.seq, 1))


def body(
    dp,
    seq,
    x_in,
    cond,
    segment_ids,
    diffusion_steps,
    prompt,
    prompt_lengths,
    w_step,
    w_conv,
    w_cond,
    w_res,
    w_skip,
    queries,
    w_query,
    w_key,
    w_value,
    w_attn_out,
    w_film,
    d_out,
    d_skip,
):
    call = Caller()
    rows = x_in.shape[0]
    frames = x_in.shape[2]
    steps = rows // NR
    cols = rows * frames
    cs = C // dp
    csh = C // seq
    heads = 2 * HEADS // seq
    wide = heads * HEAD_DIM
    arows = rows // 2
    pl_local = prompt.shape[1]
    prompt_all = pl_local * seq
    sidx = lax.axis_index("seq")
    didx = lax.axis_index("dp")
    group = (sidx // 2).astype(jnp.int32).reshape(1)
    bit = (sidx % 2).astype(jnp.int32).reshape(1)
    up = [(i, i + 1) for i in range(seq - 1)]
    down = [(i + 1, i) for i in range(seq - 1)]
    order = jnp.bitwise_xor(didx, jnp.arange(dp, dtype=jnp.int32)).astype(jnp.int32)
    offsets = jnp.concatenate([order * cs, bit, 1 - bit])
    index = sidx.astype(jnp.int32).reshape(1)

    def gather(pack, side=None, middle=None):
        if dp == 4 and side is not None:
            mine = flipped(side, "dp", dp, 2)
            inner = flipped(middle, "dp", dp, 2)
            other = flipped(mine, "seq", seq, 1)
            near = [(0, None, pack), (2, 0, mine), (2, 2, inner), (2, 1, other)]
            pieces = near + [(k + 1, h, flipped(v, "dp", dp, 1)) for k, h, v in near]
        else:
            pieces = [(0, None, pack)]
            flip = dp // 2
            while flip:
                pieces += [(k + flip, h, flipped(v, "dp", dp, flip)) for k, h, v in pieces]
                flip //= 2
        pieces.sort(key=lambda piece: piece[0])
        meta = [(k, h) for k, h, _ in pieces]
        return meta, [v if k == 0 else Got(v) for k, _, v in pieces]

    off_qkv = C + 2 * csh
    qkv_rows = -(-(3 * wide + QUERIES) // LANES) * LANES
    head_width = -(-(off_qkv + qkv_rows) // LANES) * LANES
    middle = 2 * C - 2 * SIDE + 3 * C // 4
    pack, side, middle = call(
        functools.partial(turned_pack_kernel, cs),
        (
            sds((2 * SIDE + middle, 4 * cs), BF16),
            sds((SIDE, 4 * cs), BF16),
            sds((middle, 4 * cs), BF16),
        ),
        "turned_pack",
        (bit, w_conv, w_cond, w_res, w_skip, w_step),
        in_specs=[SM] + [VM] * 5,
        out_specs=(VM, VM, VM),
        scratch_shapes=[pltpu.VMEM((4 * cs, 2 * C), BF16)],
    )
    meta, turned = gather(pack, side, middle)
    copies = 4 * dp * (1 + 3 * C // (4 * cs))
    pack, mine, other = call(
        functools.partial(head_pack_kernel, csh, wide),
        (
            sds((cs, head_width), BF16),
            sds((arows, pl_local, C), BF16),
            sds((arows, pl_local, C), BF16),
        ),
        "head_pack",
        (
            group,
            bit,
            w_attn_out,
            jnp.transpose(w_film, (1, 2, 0)).reshape(2 * csh, cs),
            w_query,
            w_key,
            w_value,
            queries,
            prompt,
        ),
        after=("turned_pack",),
        in_specs=[SM, SM] + [VM] * 7,
        out_specs=(VM,) * 3,
        scratch_shapes=[pltpu.VMEM((2 * LANES, LANES), F32)],
    )
    _, head_pieces = gather(pack)
    partner = flipped(other, "seq", seq, 1)
    pair = call(
        pair_kernel,
        sds((seq // 2, 2, arows, pl_local, C), BF16),
        "pair",
        (mine, Got(partner)),
        in_specs=[VM, VM],
        out_specs=VM,
    )
    first, last = call(
        edge_kernel,
        (sds((rows * SHIFT, C), BF16), sds((rows * SHIFT, C), BF16)),
        "edges",
        (x_in,),
        after=("pair", head_pieces[dp // 2].array),
        in_specs=[VM],
        out_specs=(VM, VM),
    )
    z_groups = [[2 * k + b for k in range(seq // 2)] for b in range(2)]
    prompts = Got(exchange(pair, "seq", z_groups))
    flags, block_ids, embedding = call(
        functools.partial(table_kernel, frames),
        (
            sds((2, rows), jnp.int32),
            sds((RP, seq), jnp.int32),
            sds((LANES, C), BF16),
        ),
        "tables",
        (index, diffusion_steps, segment_ids, segment_ids),
        after=("edges",),
        in_specs=[SM, SM, SM, VM],
        out_specs=(SM, VM, VM),
    )
    left_halo = lax.ppermute(last, "seq", up)
    right_halo = lax.ppermute(first, "seq", down)


    apack, prow, probs, u, pooled_head, qp, qkv = call(
        functools.partial(attention_kernel, dp, arows, heads, seq // 2, off_qkv),
        (
            sds((C, head_width), BF16),
            sds((arows, seq, pl_local, C), BF16),
            sds((heads * QUERIES, arows * prompt_all), F32),
            sds((RP, C), F32),
            sds((RP, LANES), F32),
            sds((QUERIES, wide), F32),
            sds((qkv_rows, C), BF16),
        ),
        "attention",
        (offsets, bit, prompt_lengths, prompts, *head_pieces),
        in_specs=[SM, SM, SM, HB] + [HB] * dp,
        out_specs=(VM,) * 7,
        scratch_shapes=[
            pltpu.VMEM((RP, arows * prompt_all), F32),
            pltpu.SemaphoreType.DMA((dp + seq,)),
        ],
    )

    row_block = pl.BlockSpec((NR, C, LANES), lambda i: (i, 0, 0))

    def col_block(height):
        return pl.BlockSpec((height, NR * LANES), lambda i: (0, i))

    def still(shape):
        return pl.BlockSpec(shape, lambda i: (0,) * len(shape))

    inp, gated, factor_a, factor_b, skip_out, mid, stats = call(
        functools.partial(forward_kernel, meta, dp, csh),
        (
            sds((4 * C, cols), BF16),
            sds((C, cols), BF16),
            sds((C, cols), BF16),
            sds((C, cols), BF16),
            sds(x_in.shape, BF16),
            sds((C, cols), BF16),
            sds((seq, 3 * RP, 2 * csh), F32),
        ),
        "wavenet",
        (
            offsets,
            flags,
            x_in,
            cond,
            d_out,
            Got(left_halo),
            Got(right_halo),
            embedding,
            pooled_head,
            *turned,
        ),
        flops=2 * cols * (4 * C * 2 * C + 2 * C * C),
        nbytes=30e6,
        grid=(steps,),
        in_specs=[
            SM,
            SM,
            row_block,
            row_block,
            row_block,
            whole((rows * SHIFT, C)),
            whole((rows * SHIFT, C)),
            whole((LANES, C)),
            whole((RP, LANES)),
        ]
        + [HB] * len(turned),
        out_specs=(
            col_block(4 * C),
            col_block(C),
            col_block(C),
            col_block(C),
            row_block,
            col_block(C),
            still((seq, 3 * RP, 2 * csh)),
        ),
        scratch_shapes=[
            pltpu.VMEM((2 * C, 4 * C), BF16),
            pltpu.VMEM((C, 2 * C), BF16),
            pltpu.VMEM((C, C), BF16),
            pltpu.VMEM((2 * C, C), BF16),
            pltpu.VMEM((C, LANES), F32),
            pltpu.VMEM((C, LANES), F32),
            pltpu.VMEM((C, LANES), F32),
            pltpu.VMEM((C, LANES), F32),
            pltpu.SemaphoreType.DMA((copies,)),
        ],
    )
    stats_got = exchange(stats, "seq")
    gskip = call(
        skip_grad_kernel,
        sds((C, C), BF16),
        "skip",
        (gated, d_skip),
        in_specs=[VM, VM],
        out_specs=VM,
        scratch_shapes=[pltpu.VMEM((C, cols), BF16)],
    )

    coef_out, dfilm, pooled, memory = call(
        functools.partial(stats_kernel, csh, heads, arows),
        (
            sds((seq, 4 * RP, 2 * csh), F32),
            sds((RP, 2 * csh), BF16),
            sds((RP, C), BF16),
            sds((RP, C), BF16),
        ),
        "segments",
        (block_ids, Got(stats_got), apack),
        after=("skip",),
        in_specs=[VM, VM, VM],
        out_specs=(VM, VM, VM, VM),
        scratch_shapes=[pltpu.VMEM((RP, C), F32)],
    )
    coef = Got(exchange(coef_out, "seq"))

    def gate_block(i):
        return jnp.minimum(i, steps - 1)

    def shard(i):
        return jnp.maximum(i - steps, 0)

    def gate_cols(height):
        return pl.BlockSpec((height, NR * LANES), lambda i, order: (0, gate_block(i)))

    gate_rows = pl.BlockSpec((NR, C, LANES), lambda i, order: (gate_block(i), 0, 0))
    wide1, wide2 = EARLY + 2 * LANES, 2 * C - EARLY

    def part(width):
        return sds((dp // 2, 4 * cs, width), BF16)

    def part_spec(width):
        return pl.BlockSpec((1, 4 * cs, width), lambda i, order: (shard(i) // 2, 0, 0))

    outs = call(
        functools.partial(backward_kernel, meta, dp, csh, steps),
        (
            sds((2 * C, cols), BF16),
            sds((C, cols), BF16),
            sds((2 * C, LANES), F32),
            part(wide1),
            part(wide2),
            part(wide1),
            part(wide2),
        ),
        "backward",
        (order, offsets, coef, mid, d_out, d_skip, factor_a, factor_b, inp, gated, gskip, flags, *turned),
        prefetch=1,
        grid=(steps + dp,),
        in_specs=[
            SM,
            pl.BlockSpec(
                (seq, 4 * RP, 2 * csh), lambda i, order: (0, 0, 0), pipeline_mode=pl.Buffered(1)
            ),
            gate_cols(C),
            gate_rows,
            gate_rows,
            gate_cols(C),
            gate_cols(C),
            pl.BlockSpec((4 * cs, cols), lambda i, order: (order[shard(i)], 0)),
            pl.BlockSpec((cs, cols), lambda i, order: (order[shard(i)], 0)),
            pl.BlockSpec((cs, C), lambda i, order: (order[shard(i)], 0)),
            SM,
        ]
        + [HB] * len(turned),
        out_specs=(
            gate_cols(2 * C),
            gate_cols(C),
            pl.BlockSpec((2 * C, LANES), lambda i, order: (0, 0)),
            part_spec(wide1),
            part_spec(wide2),
            part_spec(wide1),
            part_spec(wide2),
        ),
        scratch_shapes=[
            pltpu.VMEM((LANES, C), F32),
            pltpu.VMEM((C, LANES), F32),
            pltpu.VMEM((C, 2 * C), BF16),
            pltpu.VMEM((2 * C, NR * LANES), BF16),
            pltpu.VMEM((cols, 2 * C), BF16),
            pltpu.VMEM((cols, C), BF16),
            pltpu.SemaphoreType.DMA((copies,)),
        ],
    )
    dpre, dres, sums = outs[0:3]
    part1 = Reduction(call, "1", outs[3], outs[5], dp, seq, index)
    part2 = Reduction(call, "2", outs[4], outs[6], dp, seq, index)
    part1.over_blocks()
    keep, give = call(
        functools.partial(step_grad_kernel, meta, dp),
        (part(LANES), part(LANES)),
        "step_grad",
        (offsets, sums, embedding, *turned),
        after=("blocks_1",),
        in_specs=[SM, VM, VM] + [HB] * len(turned),
        out_specs=(VM, VM),
        scratch_shapes=[
            pltpu.VMEM((2 * C, 4 * C), BF16),
            pltpu.VMEM((C, C), F32),
            pltpu.SemaphoreType.DMA((copies,)),
        ],
    )
    part_step = Reduction(call, "step", keep, give, dp, seq, index)

    right_width = -(-(3 * wide + 3 * csh) // LANES) * LANES
    block = sds((dp // 2, cs, right_width), BF16)
    keep, give = call(
        functools.partial(attention_back_kernel, arows, csh, dp),
        (block, block),
        "attention_back",
        (offsets, prow, probs, u, qp, qkv, pooled, memory, dfilm, coef),
        after=("step_grad",),
        in_specs=[SM] + [VM] * 9,
        out_specs=(VM, VM),
        scratch_shapes=[
            pltpu.VMEM((heads * QUERIES, arows * prompt_all), F32),
            pltpu.VMEM((LANES, C), F32),
            pltpu.VMEM((LANES, right_width), F32),
            pltpu.VMEM((C, right_width), F32),
        ],
    )
    small = Reduction(call, "small", keep, give, dp, seq, index)
    part2.over_blocks(("attention_back",), (part_step,))
    small.over_blocks(("blocks_2",))
    part1.over_half(("blocks_small",))

    rest = 4 * cs // seq
    small_width = (cs // rest) * (wide + csh) + max(1, QUERIES // rest) * (wide // 2)
    part2.over_half(("half_1",))
    part1.over_pieces(("half_2",))
    grad_film, attn_rows, mine, other = call(
        functools.partial(small_sum_kernel, csh, wide),
        (
            sds((2 * csh, cs), F32),
            sds((cs, csh), F32),
            sds((cs + QUERIES, wide), BF16),
            sds((cs + QUERIES, wide), BF16),
        ),
        "small_sum",
        (bit, small.keep, Got(small.got)),
        after=("pieces_1",),
        in_specs=[SM, VM, VM],
        out_specs=(VM,) * 4,
        scratch_shapes=[pltpu.VMEM((LANES, LANES), F32)],
    )
    partner = flipped(other, "seq", seq, 1)
    part2.over_pieces(("small_sum",))
    small_piece = call(
        functools.partial(small_piece_kernel, csh, wide),
        sds((rest, small_width), BF16),
        "small_piece",
        (attn_rows, mine, Got(partner)),
        after=("pieces_2",),
        in_specs=[VM] * 3,
        out_specs=VM,
    )
    ones = part1.over_copies(("small_piece",))
    base, first, last = call(
        functools.partial(input_grad_kernel, meta, dp),
        (sds((C, cols), BF16), sds((rows * SHIFT, C), BF16), sds((rows * SHIFT, C), BF16)),
        "input_grad",
        (offsets, dpre, dres, *turned),
        after=("copies_1",),
        grid=(steps,),
        in_specs=[SM, col_block(2 * C), col_block(C)] + [HB] * len(turned),
        out_specs=(
            col_block(C),
            still((rows * SHIFT, C)),
            still((rows * SHIFT, C)),
        ),
        scratch_shapes=[
            pltpu.VMEM((2 * C, 4 * C), BF16),
            pltpu.VMEM((3, C, 2 * C), BF16),
            pltpu.VMEM((C, LANES), F32),
            pltpu.VMEM((C, LANES), F32),
            pltpu.SemaphoreType.DMA((copies,)),
        ],
    )
    from_left = lax.ppermute(last, "seq", up)
    from_right = lax.ppermute(first, "seq", down)
    twos = part2.over_copies(("input_grad", ones[0].array), extra=small_piece)

    grad_input, layer_out = call(
        functools.partial(finish_kernel, csh),
        (sds(x_in.shape, BF16), sds(x_in.shape, BF16)),
        "grad_input",
        (flags, base, Got(from_left), Got(from_right), mid, coef),
        after=("input_grad",),
        grid=(steps,),
        in_specs=[
            SM,
            col_block(C),
            whole((rows * SHIFT, C)),
            whole((rows * SHIFT, C)),
            col_block(C),
            whole((seq, 4 * RP, 2 * csh)),
        ],
        out_specs=(row_block, row_block),
        scratch_shapes=[pltpu.VMEM((LANES, C), F32)] + [pltpu.VMEM((C, LANES), F32)] * 3,
    )

    (
        grad_step,
        grad_conv,
        grad_cond,
        grad_res,
        grad_skip,
        grad_queries,
        grad_query,
        grad_key,
        grad_value,
        grad_attn,
    ) = call(
        functools.partial(output_kernel, cs, csh, wide, seq),
        (
            sds((cs, C), F32),
            sds((3, cs, 2 * C), F32),
            sds((cs, 2 * C), F32),
            sds((cs, C), F32),
            sds((cs, C), F32),
            sds((QUERIES, cs), F32),
            sds((cs, C), F32),
            sds((cs, C), F32),
            sds((cs, C), F32),
            sds((cs, C), F32),
        ),
        "outputs",
        after=("grad_input",),
        args=(bit, *ones, *twos, queries, w_query),
        in_specs=[SM] + [VM] * 5,
        out_specs=(VM,) * 10,
        scratch_shapes=[
            pltpu.VMEM((4 * cs, wide1), F32),
            pltpu.VMEM((4 * cs, wide2 + LANES), F32),
            pltpu.VMEM((4 * cs, small_width), F32),
            pltpu.VMEM((LANES, LANES), F32),
            pltpu.VMEM((LANES, C), F32),
        ],
    )
    return (
        layer_out,
        skip_out,
        grad_input,
        grad_step,
        grad_conv,
        grad_cond,
        grad_res,
        grad_skip,
        grad_queries,
        grad_query,
        grad_key,
        grad_value,
        grad_attn,
        jnp.transpose(grad_film.reshape(2, csh, cs), (2, 0, 1)),
    )


def solution(mesh):
    frames = P("dp", None, "seq")
    matrix = P("dp", None)
    return jax.shard_map(
        functools.partial(body, mesh.shape["dp"], mesh.shape["seq"]),
        mesh=mesh,
        in_specs=(
            frames,
            frames,
            P("dp", None),
            P("dp"),
            P("dp", "seq", None),
            P("dp"),
            matrix,
            P(None, "dp", None),
            matrix,
            matrix,
            matrix,
            P(None, "dp"),
            matrix,
            matrix,
            matrix,
            matrix,
            frames,
            frames,
            frames,
        ),
        out_specs=(
            frames,
            frames,
            frames,
            matrix,
            P(None, "dp", None),
            matrix,
            matrix,
            matrix,
            P(None, "dp"),
            matrix,
            matrix,
            matrix,
            matrix,
            frames,
        ),
        check_vma=False,
    )
```

```python
import functools
import math

import jax
import jax.numpy as jnp
from jax import lax
from jax.experimental import pallas as pl
from jax.experimental.pallas import tpu as pltpu
from jax.sharding import PartitionSpec as P

C = 512
HEADS = 8
QUERIES = 32
HEAD_DIM = 64
SHIFT = 4
SQRT_HALF = 0.7071067811865476
NORM_EPS = 1e-05
MASKED_SCORE = -1e30
LANES = 128
RP = 16
NR = 4
EARLY = 640
F32 = jnp.float32
BF16 = jnp.bfloat16
VMEM_BYTES = 50 * 1024 * 1024


def nn(a, b):
    return lax.dot_general(a, b, (((1,), (0,)), ((), ())), preferred_element_type=F32)


def nt(a, b):
    return lax.dot_general(a, b, (((1,), (1,)), ((), ())), preferred_element_type=F32)


def parts(v, count):
    out = []
    for _ in range(count):
        low = v.astype(BF16).astype(F32)
        out.append(low)
        v = v - low
    return jnp.concatenate(out, axis=0).astype(BF16)


def fold(v, count):
    rows = v.shape[0] // count
    total = v[:rows]
    for k in range(1, count):
        total = total + v[k * rows : (k + 1) * rows]
    return total


def lane_ids(shape):
    return lax.broadcasted_iota(jnp.int32, shape, len(shape) - 1)


def sds(shape, dtype):
    return jax.ShapeDtypeStruct(shape, dtype)


VM = pl.BlockSpec(memory_space=pltpu.VMEM)
HB = pl.BlockSpec(memory_space=pl.ANY)
SM = pl.BlockSpec(memory_space=pltpu.SMEM)


def whole(shape):
    return pl.BlockSpec(shape, lambda i: (0,) * len(shape), pipeline_mode=pl.Buffered(1))


class Got:
    def __init__(self, array):
        self.array = array


class Caller:
    def __init__(self):
        self.done = {}

    def __call__(self, kernel, out_shape, name, args, flops=0, nbytes=0, prefetch=0, after=(), **kw):
        single = not isinstance(out_shape, tuple)
        shapes = (out_shape,) if single else out_shape
        specs = kw["out_specs"]
        specs = (specs,) if single else specs
        pinned = tuple(
            v if spec is SM else pltpu.HBM(v.shape, v.dtype) for v, spec in zip(shapes, specs)
        )
        in_specs = list(kw.pop("in_specs"))
        count = prefetch + len(in_specs)
        args = list(args)
        extra = len(after)
        for before in after:
            in_specs.append(HB)
            args.append(self.done[before] if isinstance(before, str) else before)

        def run(*refs):
            return kernel(*refs[:count], *refs[count + extra :])

        values = []
        for k, v in enumerate(args):
            spec = SM if k < prefetch else in_specs[k - prefetch]
            if isinstance(v, Got):
                values.append(v.array)
            elif spec is SM:
                values.append(v)
            else:
                values.append(pltpu.with_memory_space_constraint(v, pltpu.HBM))
        spec = pltpu.PrefetchScalarGridSpec(
            num_scalar_prefetch=prefetch,
            grid=kw.pop("grid", ()),
            in_specs=in_specs,
            out_specs=kw.pop("out_specs"),
            scratch_shapes=kw.pop("scratch_shapes", ()),
        )
        out = pl.pallas_call(
            run,
            out_shape=pinned[0] if single else pinned,
            name=name,
            grid_spec=spec,
            cost_estimate=pl.CostEstimate(
                flops=1, bytes_accessed=1, transcendentals=0
            ),
            compiler_params=pltpu.CompilerParams(vmem_limit_bytes=VMEM_BYTES),
        )(*values)
        self.done[name] = out if single else out[0]
        return out


def head_pack_kernel(
    csh,
    local,
    group_ref,
    bit_ref,
    attn_ref,
    film_ref,
    wq_ref,
    wk_ref,
    wv_ref,
    queries_ref,
    prompt_ref,
    out_ref,
    mine_ref,
    other_ref,
    scr,
):
    cs = attn_ref.shape[0]
    arows = mine_ref.shape[0]
    mine_ref[...] = prompt_ref[pl.ds(bit_ref[0] * arows, arows)]
    other_ref[...] = prompt_ref[pl.ds((1 - bit_ref[0]) * arows, arows)]
    out_ref[:, 0:C] = attn_ref[...]
    off = C
    scr[...] = jnp.zeros((2 * LANES, LANES), F32)
    scr[0 : 2 * csh, 0:cs] = film_ref[...].astype(F32)
    scr[LANES : LANES + QUERIES, 0:cs] = queries_ref[...].astype(F32)
    film = scr[0:LANES].T[0:cs]
    table = scr[LANES : 2 * LANES].T[0:cs]
    turn = lax.rem(C - local * group_ref[0], C)
    blocks = [film[:, 0 : 2 * csh]]
    for ref in (wq_ref, wk_ref, wv_ref):
        blocks.append(pltpu.roll(ref[...].astype(F32), turn, 1)[:, 0:local])
    blocks.append(table)
    for block in blocks:
        width = min(block.shape[1], out_ref.shape[1] - off)
        out_ref[:, off : off + width] = block[:, 0:width].astype(BF16)
        off += width
    if off < out_ref.shape[1]:
        out_ref[:, off:] = jnp.zeros((cs, out_ref.shape[1] - off), BF16)


SIDE = 480


def turned_pack_kernel(cs, bit_ref, conv_ref, cond_ref, res_ref, skip_ref, step_ref, out_ref, side_ref, middle_ref, scr):
    for k in range(3):
        scr[k * cs : (k + 1) * cs] = conv_ref[k]
    scr[3 * cs : 4 * cs] = cond_ref[...]
    turned = scr[...].T
    out_ref[0 : 2 * C - SIDE] = turned[0 : 2 * C - SIDE]
    at = 2 * C - SIDE
    for ref in (res_ref, skip_ref, step_ref):
        for lane in range(0, C, 4 * cs):
            out_ref[at : at + cs] = ref[:, lane : lane + 4 * cs]
            at += cs
    out_ref[at : at + SIDE] = turned[2 * C - SIDE :]
    middle_ref[...] = out_ref[SIDE:at]
    side_ref[...] = out_ref[pl.ds(pl.multiple_of(bit_ref[0] * at, 16), SIDE)]


def pair_kernel(a_ref, b_ref, out_ref):
    for p in range(out_ref.shape[0]):
        out_ref[p, 0] = a_ref[...]
        out_ref[p, 1] = b_ref[...]


def table_kernel(
    frames, index_ref, steps_ref, ids_smem, ids_ref, flags_ref, blocks_ref, emb_ref
):
    rows, length = ids_ref.shape
    count = length // frames
    me = index_ref[0]
    for r in range(rows):
        here = ids_smem[r, me * frames]
        before = ids_smem[r, jnp.maximum(me * frames - 1, 0)]
        after = ids_smem[r, jnp.minimum((me + 1) * frames, length - 1)]
        flags_ref[0, r] = jnp.where((me > 0) & (before == here), 1, 0).astype(jnp.int32)
        flags_ref[1, r] = jnp.where((me < count - 1) & (after == here), 1, 0).astype(jnp.int32)
    blocks_ref[...] = jnp.zeros(blocks_ref.shape, jnp.int32)
    for s in range(count):
        blocks_ref[0:rows, s : s + 1] = ids_ref[:, s * frames : s * frames + 1]
    half = C // 2
    row = lax.broadcasted_iota(jnp.int32, (RP, half), 0)
    at = lane_ids((RP, half)).astype(F32)
    frequency = jnp.exp(at * (-math.log(10000.0) / half))
    step = jnp.zeros((RP, half), F32)
    for r in range(rows):
        step = jnp.where(row == r, steps_ref[r].astype(F32), step)
    angle = step * frequency
    emb_ref[...] = jnp.zeros(emb_ref.shape, BF16)
    emb_ref[0:RP, 0:half] = jnp.where(row < rows, jnp.sin(angle), 0.0).astype(BF16)
    emb_ref[0:RP, half:C] = jnp.where(row < rows, jnp.cos(angle), 0.0).astype(BF16)


def edge_kernel(x_ref, first_ref, last_ref):
    rows = x_ref.shape[0]
    lane = lane_ids((C, LANES))
    first = jnp.zeros((C, LANES), F32)
    last = jnp.zeros((C, LANES), F32)
    for r in range(rows):
        v = x_ref[r].astype(F32)
        here = (lane // SHIFT) == r
        first = jnp.where(here, pltpu.roll(v, SHIFT * r, 1) if r else v, first)
        last = jnp.where(here, pltpu.roll(v, SHIFT * r + SHIFT, 1), last)
    first_ref[...] = first.T[0 : rows * SHIFT].astype(BF16)
    last_ref[...] = last.T[0 : rows * SHIFT].astype(BF16)


def halo_columns(ref):
    v = ref[...].astype(F32)
    return jnp.concatenate([v, jnp.zeros((LANES - v.shape[0], C), F32)], axis=0).T


def begin(copies):
    for copy in copies:
        copy.start()


def finish(copies):
    for copy in copies:
        copy.wait()


def turned_copies(meta, refs, off_ref, cs, wt, others, sems):
    dp = len({k for k, _ in meta})
    pairs = []

    def conv(k, ref, first, row, rows):
        if wt is not None:
            lanes = pl.ds(pl.multiple_of(off_ref[k] * 4, LANES), 4 * cs)
            at = row if isinstance(row, int) else pl.multiple_of(row, 16)
            pairs.append((ref.at[pl.ds(first, rows)], wt.at[pl.ds(at, rows), lanes]))

    def rest(k, ref, at):
        row = pl.ds(pl.multiple_of(off_ref[k], 16), cs)
        for other in others:
            for lane in range(0, C, 4 * cs):
                if other is not None:
                    dst, start = other
                    pairs.append((ref.at[pl.ds(at, cs)], dst.at[row, pl.ds(start + lane, 4 * cs)]))
                at += cs

    inner = 2 * C - 2 * SIDE
    for (k, which), ref in zip(meta, refs):
        if which is None:
            conv(k, ref, 0, 0, SIDE + inner)
            rest(k, ref, SIDE + inner)
            conv(k, ref, ref.shape[0] - SIDE, 2 * C - SIDE, SIDE)
        elif which == 2:
            conv(k, ref, 0, SIDE, inner)
            rest(k, ref, inner)
        else:
            conv(k, ref, 0, off_ref[dp + which] * (2 * C - SIDE), SIDE)
    return [pltpu.make_async_copy(a, b, sems.at[n]) for n, (a, b) in enumerate(pairs)]


def head_copies(refs, off_ref, dst, sems):
    copies = []
    for k, ref in enumerate(refs):
        row = pl.ds(pl.multiple_of(off_ref[k], 16), ref.shape[0])
        copies.append(pltpu.make_async_copy(ref, dst.at[row], sems.at[k]))
    return copies


def forward_kernel(
    meta, dp, csh, off_ref, flags_ref, x_ref, cond_ref, dout_ref, left_ref, right_ref, emb_ref, pooled_ref, *refs
):
    turned, refs = refs[: len(meta)], refs[len(meta) :]
    (
        inp_ref,
        gated_ref,
        fa_ref,
        fb_ref,
        skip_ref,
        mid_ref,
        stats_ref,
        wt_ref,
        rn_ref,
        step_ref,
        rst_ref,
        lift_ref,
        acc_ref,
        left_scr,
        right_scr,
        sems,
    ) = refs
    cs = C // dp
    i = pl.program_id(0)
    lane = lane_ids((C, LANES))

    @pl.when(i == 0)
    def _():
        copies = turned_copies(
            meta,
            turned,
            off_ref,
            cs,
            wt_ref,
            ((rn_ref, 0), (rn_ref, C), (step_ref, 0)),
            sems,
        )
        begin(copies)
        acc_ref[...] = jnp.zeros((C, LANES), F32)
        left_scr[...] = halo_columns(left_ref)
        right_scr[...] = halo_columns(right_ref)
        finish(copies)
        lift = nn(emb_ref[0:RP], step_ref[...])
        lift = jnp.concatenate([lift, jnp.zeros((LANES - RP, C), F32)], axis=0)
        lift_ref[...] = lift.T
        rst_ref[...] = rn_ref[...].T

    lift = pltpu.roll(lift_ref[...], lax.rem(LANES - NR * i, LANES), 1)
    left = left_scr[...]
    right = right_scr[...]

    def put(tap, cols, value):
        for d in range(dp):
            at = d * 4 * cs + tap * cs
            inp_ref[at : at + cs, cols] = value[d * cs : (d + 1) * cs]

    for j in range(NR):
        r = NR * i + j
        lc = lift[:, j : j + 1]
        sh = (x_ref[j].astype(F32) + lc).astype(BF16)
        shf = sh.astype(F32)
        lh = pltpu.roll(left, lax.rem(LANES - SHIFT * r, LANES), 1)
        lh = jnp.where(flags_ref[0, r] > 0, (lh + lc).astype(BF16).astype(F32), 0.0)
        rh = pltpu.roll(right, LANES - SHIFT - SHIFT * r, 1)
        rh = jnp.where(flags_ref[1, r] > 0, (rh + lc).astype(BF16).astype(F32), 0.0)
        cols = slice(j * LANES, (j + 1) * LANES)
        put(0, cols, jnp.where(lane < SHIFT, lh, pltpu.roll(shf, SHIFT, 1)).astype(BF16))
        put(1, cols, sh)
        put(
            2,
            cols,
            jnp.where(lane >= LANES - SHIFT, rh, pltpu.roll(shf, LANES - SHIFT, 1)).astype(BF16),
        )
        put(3, cols, cond_ref[j])
    pre = nn(wt_ref[...], inp_ref[...])
    th = jnp.tanh(pre[:C])
    sg = jax.nn.sigmoid(pre[C:])
    gf = th * sg
    fa_ref[...] = (sg - gf * th).astype(BF16)
    fb_ref[...] = (gf * (1.0 - sg)).astype(BF16)
    g = gf.astype(BF16)
    gated_ref[...] = g
    rs = nn(rst_ref[...], g)
    acc = acc_ref[...]
    for j in range(NR):
        r = NR * i + j
        cols = slice(j * LANES, (j + 1) * LANES)
        skip_ref[j] = rs[C:, cols].astype(BF16)
        mid = ((x_ref[j].astype(F32) + rs[:C, cols]) * SQRT_HALF).astype(BF16)
        mid_ref[:, cols] = mid
        mf = mid.astype(F32)
        df = dout_ref[j].astype(F32)
        total = jnp.sum(mf, axis=1, keepdims=True)
        dev = mf - total * (1.0 / LANES)
        acc = jnp.where(lane == r, total, acc)
        acc = jnp.where(lane == RP + r, jnp.sum(dev * dev, axis=1, keepdims=True), acc)
        acc = jnp.where(lane == 2 * RP + r, jnp.sum(df, axis=1, keepdims=True), acc)
        acc = jnp.where(lane == 3 * RP + r, jnp.sum(df * dev, axis=1, keepdims=True), acc)
    acc_ref[...] = acc

    @pl.when(i == pl.num_programs(0) - 1)
    def _():
        t = acc.T
        for s in range(C // csh):
            cols = slice(s * csh, (s + 1) * csh)
            stats_ref[s, 0 : 2 * RP, 0:csh] = t[0 : 2 * RP, cols]
            stats_ref[s, 0 : 2 * RP, csh : 2 * csh] = t[2 * RP : 4 * RP, cols]
            stats_ref[s, 2 * RP : 3 * RP] = pooled_ref[:, 0 : 2 * csh]


def attention_kernel(dp, rows, heads, pairs, off, off_ref, bit_ref, len_ref, prompts, *refs):
    pieces, refs = refs[:dp], refs[dp:]
    apack_ref, prow, probs_ref, u_ref, pooled_ref, qp_ref, qkv_ref, abd, sems = refs
    copies = head_copies(pieces, off_ref, apack_ref, sems)
    count = len(copies)
    for j in range(pairs):
        for i in range(2):
            copies.append(
                pltpu.make_async_copy(
                    prompts.at[j, i], prow.at[:, 2 * j + i], sems.at[count + 2 * j + i]
                )
            )
    begin(copies)
    local = prow.shape[2]
    total = 2 * pairs * local
    abd[...] = jnp.zeros(abd.shape, F32)
    lane = lane_ids((heads * QUERIES, total))
    place = jnp.zeros((heads * QUERIES, total), jnp.int32)
    for k in range(2 * pairs):
        here = (k // 2) * 2 + (bit_ref[0] if k % 2 == 0 else 1 - bit_ref[0])
        place = jnp.where(lane // local == k, here * local + lane % local, place)
    finish(copies)
    wide = heads * HEAD_DIM
    qkv = apack_ref[:, off : off + qkv_ref.shape[0]].T
    qkv_ref[...] = qkv
    qp = nt(qkv[3 * wide : 3 * wide + QUERIES], qkv[0:wide])
    qp_ref[...] = qp
    st = []
    for g in range(heads):
        cols = slice(g * HEAD_DIM, (g + 1) * HEAD_DIM)
        st.append(fold(nn(parts(qp[:, cols], 3), qkv[wide + cols.start : wide + cols.stop]), 3))
    st = jnp.concatenate(st, axis=0) * (1.0 / math.sqrt(HEAD_DIM))
    table = prow[...].reshape(rows * total, C)
    scores = fold(nt(parts(st, 3), table), 3)
    for r in range(rows):
        cols = slice(r * total, (r + 1) * total)
        live = place < len_ref[bit_ref[0] * rows + r]
        s = jnp.where(live, scores[:, cols], MASKED_SCORE)
        e = jnp.where(live, jnp.exp(s - jnp.max(s, axis=1, keepdims=True)), 0.0)
        p = e / jnp.sum(e, axis=1, keepdims=True)
        probs_ref[:, cols] = p
        for g in range(heads):
            abd[8 * g + r : 8 * g + r + 1, cols] = jnp.sum(
                p[g * QUERIES : (g + 1) * QUERIES], axis=0, keepdims=True
            )
    u = fold(nn(parts(abd[...], 2), table), 2)
    u_ref[...] = u
    pooled_ref[...] = jnp.zeros(pooled_ref.shape, F32)
    for g in range(heads):
        first = 2 * wide + g * HEAD_DIM
        v = parts(u[8 * g : 8 * g + 8] * (1.0 / QUERIES), 2)
        pooled_ref[0:8, g * HEAD_DIM : (g + 1) * HEAD_DIM] = fold(
            nt(v, qkv[first : first + HEAD_DIM]), 2
        )


def stats_kernel(
    csh, heads, rows, seg_ref, x_ref, apack_ref, out_ref, dfilm_ref, pooled_ref, memory_ref, scratch
):
    count = x_ref.shape[0]
    wide = heads * HEAD_DIM
    seg = seg_ref[...]
    scratch[...] = jnp.zeros(scratch.shape, F32)
    for s in range(count):
        group, part = s // 2, s % 2
        scratch[part * rows : (part + 1) * rows, group * wide : (group + 1) * wide] = x_ref[
            s, 2 * RP : 2 * RP + rows, 0:wide
        ]
    pooled = scratch[...].astype(BF16)
    pooled_ref[...] = pooled
    memory = nn(pooled, apack_ref[:, 0:C]).astype(BF16)
    memory_ref[...] = memory
    film = nn(memory, apack_ref[:, C : C + 2 * csh])
    f0 = film[:, 0:csh]
    f1 = film[:, csh : 2 * csh]
    total = [x_ref[s, 0:RP, 0:csh] for s in range(count)]
    second = [x_ref[s, RP : 2 * RP, 0:csh] for s in range(count)]
    dsum = [x_ref[s, 0:RP, csh : 2 * csh] for s in range(count)]
    cross = [x_ref[s, RP : 2 * RP, csh : 2 * csh] for s in range(count)]
    means = [v * (1.0 / LANES) for v in total]
    d0 = jnp.zeros((RP, csh), F32)
    d1 = jnp.zeros((RP, csh), F32)
    for me in range(count):
        same = [(seg[:, s : s + 1] == seg[:, me : me + 1]).astype(F32) for s in range(count)]
        frames = sum(same) * float(LANES)
        inv = 1.0 / frames
        mean = sum(m * v for m, v in zip(same, total)) * inv
        var = (
            sum(
                m * (v + float(LANES) * (u - mean) * (u - mean))
                for m, v, u in zip(same, second, means)
            )
            * inv
        )
        scale = lax.rsqrt(var + NORM_EPS)
        dtot = sum(m * v for m, v in zip(same, dsum))
        xtot = sum(m * (v + (u - mean) * d) for m, v, u, d in zip(same, cross, means, dsum)) * scale
        mean_part = f0 * dtot * inv
        cross_part = f0 * xtot * inv
        slope = scale * scale * cross_part
        out_ref[me, 0:RP, 0:csh] = 1.0 + f0 * scale
        out_ref[me, RP : 2 * RP, 0:csh] = f1 - f0 * scale * mean
        out_ref[me, 0:RP, csh : 2 * csh] = -slope
        out_ref[me, RP : 2 * RP, csh : 2 * csh] = slope * mean - scale * mean_part
        d0 = d0 + (cross[me] + (means[me] - mean) * dsum[me]) * scale
        d1 = d1 + dsum[me]
    dfilm = jnp.concatenate([d0, d1], axis=1).astype(BF16)
    dfilm_ref[...] = dfilm
    dmem = nt(dfilm, apack_ref[:, C : C + 2 * csh])
    dpool = nt(dmem.astype(BF16), apack_ref[:, 0:C])
    for s in range(count):
        group, part = s // 2, s % 2
        rolled = pltpu.roll(dpool, RP - part * rows, 0) if part else dpool
        out_ref[s, 2 * RP : 3 * RP, 0:csh] = dmem[:, s * csh : (s + 1) * csh]
        out_ref[s, 2 * RP : 3 * RP, csh : 2 * csh] = jnp.zeros((RP, csh), F32)
        out_ref[s, 3 * RP : 4 * RP] = rolled[:, group * wide : (group + 1) * wide]


def coef_columns(csh, coef_ref, rows_ref, cols_ref):
    rows_ref[...] = jnp.zeros(rows_ref.shape, F32)
    for s in range(C // csh):
        cols = slice(s * csh, (s + 1) * csh)
        rows_ref[0 : 2 * RP, cols] = coef_ref[s, 0 : 2 * RP, 0:csh]
        rows_ref[2 * RP : 4 * RP, cols] = coef_ref[s, 0 : 2 * RP, csh : 2 * csh]
    cols_ref[...] = rows_ref[...].T


def skip_grad_kernel(gated_ref, dskip_ref, out_ref, right):
    for r in range(dskip_ref.shape[0]):
        right[:, r * LANES : (r + 1) * LANES] = dskip_ref[r]
    out_ref[...] = nt(gated_ref[...], right[...]).astype(BF16)


def backward_kernel(meta, dp, csh, gates, order_ref, off_ref, coef_ref, mid_ref, dout_ref, dskip_ref, fa_ref, fb_ref, inp_ref, gated_ref, gskip_ref, flags_ref, *refs):
    turned, refs = refs[: len(meta)], refs[len(meta) :]
    dpre_ref, dres_ref, sums_ref, refs = refs[0], refs[1], refs[2], refs[3:]
    outs, refs = (refs[0:2], refs[2:4]), refs[4:]
    rows_ref, cols_ref, w_ref, both_ref, dpt_ref, drt_ref, sems = refs
    cs = C // dp
    span = NR * LANES
    i = pl.program_id(0)

    @pl.when(i == 0)
    def _():
        copies = turned_copies(
            meta, turned, off_ref, cs, None, ((w_ref, 0), (w_ref, C), None), sems
        )
        begin(copies)
        coef_columns(csh, coef_ref, rows_ref, cols_ref)
        sums_ref[...] = jnp.zeros(sums_ref.shape, F32)
        finish(copies)

    @pl.when(i < gates)
    def _():
        coef = pltpu.roll(cols_ref[...], lax.rem(LANES - NR * i, LANES), 1)
        for j in range(NR):
            cols = slice(j * LANES, (j + 1) * LANES)
            mf = mid_ref[:, cols].astype(F32)
            df = dout_ref[j].astype(F32)
            a = coef[:, j : j + 1]
            be = coef[:, 2 * RP + j : 2 * RP + j + 1]
            ga = coef[:, 3 * RP + j : 3 * RP + j + 1]
            dmid = (a * df + (be * mf + ga)).astype(BF16).astype(F32)
            both_ref[0:C, cols] = (dmid * SQRT_HALF).astype(BF16)
            both_ref[C : 2 * C, cols] = dskip_ref[j]
        dres = both_ref[0:C]
        dres_ref[...] = dres
        dg = nn(w_ref[...], both_ref[...])
        dt = (dg * fa_ref[...].astype(F32)).astype(BF16)
        ds = (dg * fb_ref[...].astype(F32)).astype(BF16)
        dpre_ref[0:C] = dt
        dpre_ref[C : 2 * C] = ds
        at = pl.ds(pl.multiple_of(i * span, span), span)
        dpt_ref[at, 0:C] = dt.T
        dpt_ref[at, C : 2 * C] = ds.T
        drt_ref[at] = dres.T
        frame = lax.broadcasted_iota(jnp.int32, (span, LANES), 0)
        column = lane_ids((span, LANES))
        place = frame % LANES
        which = frame // LANES
        keep_l = jnp.zeros((span, LANES), jnp.int32)
        keep_r = jnp.zeros((span, LANES), jnp.int32)
        for j in range(NR):
            keep_l = jnp.where(which == j, flags_ref[0, NR * i + j], keep_l)
            keep_r = jnp.where(which == j, flags_ref[1, NR * i + j], keep_r)
        row = NR * i + which
        use0 = (column == row) & ((place >= SHIFT) | (keep_l > 0))
        use1 = column == RP + row
        use2 = (column == 2 * RP + row) & ((place < LANES - SHIFT) | (keep_r > 0))
        pick = jnp.where(use0 | use1 | use2, 1.0, 0.0).astype(BF16)
        sums_ref[...] = sums_ref[...] + nn(dpre_ref[...], pick)

    @pl.when(i >= gates)
    def _():
        g = nn(inp_ref[...], dpt_ref[...]).astype(BF16)
        h = nn(gated_ref[...], drt_ref[...]).astype(BF16)
        k = i - gates
        for parity, (one, two) in enumerate(outs):

            @pl.when(lax.rem(k, 2) == parity)
            def _():
                for t in range(4):
                    rows = slice(t * cs, (t + 1) * cs)
                    lanes = slice(t * LANES, (t + 1) * LANES)
                    one[0, rows, 0:LANES] = h[:, lanes]
                    one[0, rows, LANES : 2 * LANES] = gskip_ref[:, lanes]
                one[0, :, 2 * LANES :] = g[:, 0:EARLY]
                two[0] = g[:, EARLY:]


def step_grad_kernel(meta, dp, off_ref, sums_ref, emb_ref, *refs):
    turned, refs = refs[: len(meta)], refs[len(meta) :]
    keep_ref, give_ref, wt_ref, scr, sems = refs
    cs = C // dp
    copies = turned_copies(meta, turned, off_ref, cs, wt_ref, (None,) * 3, sems)
    begin(copies)
    sums = sums_ref[...].T
    emb = emb_ref[...].T
    finish(copies)
    total = jnp.zeros((RP, 4 * C), F32)
    lane = lane_ids((RP, 4 * C))
    all_taps = fold(nn(parts(sums[0 : 3 * RP], 2), wt_ref[...]), 2)
    for t in range(3):
        g = all_taps[t * RP : (t + 1) * RP]
        total = total + jnp.where((lane // cs) % 4 == t, g, 0.0)
    out = []
    for d in range(dp):
        block = total[:, d * 4 * cs : (d + 1) * 4 * cs]
        out.append(block[:, 0:cs] + block[:, cs : 2 * cs] + block[:, 2 * cs : 3 * cs])
    g = jnp.concatenate(out, axis=1)
    g = jnp.concatenate([g, jnp.zeros((LANES - RP, C), F32)], axis=0)
    hi = g.astype(BF16)
    lo = (g - hi.astype(F32)).astype(BF16)
    scr[...] = nn(emb, hi) + nn(emb, lo)
    for k in range(dp):
        v = scr[pl.ds(pl.multiple_of(off_ref[k], 16), cs)].astype(BF16)
        for t in range(4):
            (keep_ref, give_ref)[k % 2][k // 2, t * cs : (t + 1) * cs] = v[
                :, t * LANES : (t + 1) * LANES
            ]


def input_grad_kernel(meta, dp, off_ref, dpre_ref, dres_ref, *refs):
    turned, refs = refs[: len(meta)], refs[len(meta) :]
    base_ref, first_ref, last_ref, wt_ref, w_ref, facc_ref, lacc_ref, sems = refs
    cs = C // dp
    i = pl.program_id(0)
    lane = lane_ids((C, LANES))

    @pl.when(i == 0)
    def _():
        copies = turned_copies(meta, turned, off_ref, cs, wt_ref, (None,) * 3, sems)
        begin(copies)
        facc_ref[...] = jnp.zeros((C, LANES), F32)
        lacc_ref[...] = jnp.zeros((C, LANES), F32)
        finish(copies)
        for d in range(dp):
            v = wt_ref[:, d * 4 * cs : (d + 1) * 4 * cs].T
            for t in range(3):
                w_ref[t, d * cs : (d + 1) * cs] = v[t * cs : (t + 1) * cs]

    dpre = dpre_ref[...]
    y0 = nn(w_ref[0], dpre)
    y1 = nn(w_ref[1], dpre)
    y2 = nn(w_ref[2], dpre)
    facc = facc_ref[...]
    lacc = lacc_ref[...]
    for j in range(NR):
        r = NR * i + j
        cols = slice(j * LANES, (j + 1) * LANES)
        z0 = pltpu.roll(y0[:, cols], LANES - SHIFT, 1)
        z2 = pltpu.roll(y2[:, cols], SHIFT, 1)
        inner0 = lane < LANES - SHIFT
        inner2 = lane >= SHIFT
        v = y1[:, cols]
        base_ref[:, cols] = (
            v
            + jnp.where(inner0, z0, 0.0)
            + jnp.where(inner2, z2, 0.0)
            + dres_ref[:, cols].astype(F32)
        ).astype(BF16)
        here = (lane // SHIFT) == r
        facc = jnp.where(here, pltpu.roll(z0, lax.rem(SHIFT * r + SHIFT, LANES), 1), facc)
        lacc = jnp.where(here, pltpu.roll(z2, SHIFT * r, 1), lacc)
    facc_ref[...] = facc
    lacc_ref[...] = lacc

    @pl.when(i == pl.num_programs(0) - 1)
    def _():
        first_ref[...] = facc.T[0 : first_ref.shape[0]].astype(BF16)
        last_ref[...] = lacc.T[0 : last_ref.shape[0]].astype(BF16)


def finish_kernel(csh, flags_ref, base_ref, left_ref, right_ref, mid_ref, coef_ref, out_ref, layer_ref, rows_ref, cols_ref, left_scr, right_scr):
    i = pl.program_id(0)
    lane = lane_ids((C, LANES))

    @pl.when(i == 0)
    def _():
        coef_columns(csh, coef_ref, rows_ref, cols_ref)
        left_scr[...] = halo_columns(left_ref)
        right_scr[...] = halo_columns(right_ref)

    coef = pltpu.roll(cols_ref[...], lax.rem(LANES - NR * i, LANES), 1)
    left = left_scr[...]
    right = right_scr[...]
    for j in range(NR):
        r = NR * i + j
        cols = slice(j * LANES, (j + 1) * LANES)
        lh = pltpu.roll(left, lax.rem(LANES - SHIFT * r, LANES), 1)
        rh = pltpu.roll(right, LANES - SHIFT - SHIFT * r, 1)
        lh = jnp.where((lane < SHIFT) & (flags_ref[0, r] > 0), lh, 0.0)
        rh = jnp.where((lane >= LANES - SHIFT) & (flags_ref[1, r] > 0), rh, 0.0)
        out_ref[j] = (base_ref[:, cols].astype(F32) + lh + rh).astype(BF16)
        a = coef[:, j : j + 1]
        b = coef[:, RP + j : RP + j + 1]
        layer_ref[j] = (a * mid_ref[:, cols].astype(F32) + b).astype(BF16)


def add_blocks_kernel(count, *refs):
    ins, (keep_ref, give_ref) = refs[: 2 * count], refs[2 * count :]
    at = 0
    for p in range(count):
        a_ref, b_ref = ins[2 * p : 2 * p + 2]
        width = a_ref.shape[2]
        for j in range(a_ref.shape[0]):
            v = a_ref[j].astype(F32) + b_ref[j].astype(F32)
            (keep_ref, give_ref)[j % 2][j // 2, :, at : at + width] = v.astype(BF16)
        at += width


def add_halves_kernel(bit, index_ref, a_ref, b_ref, keep_ref, give_ref, scr):
    half = a_ref.shape[0] // 2
    mine = lax.rem(index_ref[0] // bit, 2)
    scr[...] = a_ref[...].astype(F32) + b_ref[...].astype(F32)
    keep_ref[...] = scr[pl.ds(pl.multiple_of(mine * half, 8), half)].astype(BF16)
    give_ref[...] = scr[pl.ds(pl.multiple_of((1 - mine) * half, 8), half)].astype(BF16)


def add_pieces_kernel(a_ref, b_ref, out_ref):
    v = a_ref[...].astype(F32) + b_ref[...].astype(F32)
    size = out_ref.shape[1]
    for p in range(out_ref.shape[0]):
        out_ref[p] = v[p * size : (p + 1) * size].astype(BF16)


def sum_copies_kernel(a_ref, *refs):
    out_ref = refs[-1]
    v = a_ref[0].astype(F32)
    for p in range(1, a_ref.shape[0]):
        v = v + a_ref[p].astype(F32)
    v = v.astype(BF16)
    for p in range(out_ref.shape[0]):
        out_ref[p, :, 0 : v.shape[1]] = v
        if len(refs) > 1:
            out_ref[p, :, v.shape[1] :] = refs[0][...]


def small_sum_kernel(csh, wide, bit_ref, keep_ref, got_ref, film_ref, attn_ref, mine_ref, other_ref, turn):
    v = keep_ref[0].astype(F32) + got_ref[0].astype(F32)
    cs = v.shape[0]
    film = 2 * wide + csh
    turn[...] = jnp.zeros(turn.shape, F32)
    turn[0:cs, 0 : 2 * csh] = v[:, film : film + 2 * csh]
    film_ref[...] = turn[...].T[0 : 2 * csh, 0:cs]
    attn_ref[...] = v[:, 2 * wide : film]
    last = film + 2 * csh
    even = bit_ref[0] == 0
    for one, two, rows, width in (
        (v[:, 0:wide], v[:, wide : 2 * wide], slice(0, cs), wide),
        (
            v[0:QUERIES, last : last + wide // 2],
            v[0:QUERIES, last + wide // 2 : last + wide],
            slice(cs, cs + QUERIES),
            wide // 2,
        ),
    ):
        mine_ref[rows, 0:width] = jnp.where(even, one, two).astype(BF16)
        other_ref[rows, 0:width] = jnp.where(even, two, one).astype(BF16)
    mine_ref[cs:, wide // 2 :] = jnp.zeros((QUERIES, wide // 2), BF16)
    other_ref[cs:, wide // 2 :] = jnp.zeros((QUERIES, wide // 2), BF16)


def small_piece_kernel(csh, wide, attn_ref, mine_ref, got_ref, out_ref):
    v = mine_ref[...].astype(F32) + got_ref[...].astype(F32)
    attn = attn_ref[...]
    cs = attn.shape[0]
    rows = out_ref.shape[0]
    at = 0
    for row in range(0, cs, rows):
        out_ref[:, at : at + wide] = v[row : row + rows].astype(BF16)
        out_ref[:, at + wide : at + wide + csh] = attn[row : row + rows].astype(BF16)
        at += wide + csh
    for row in range(0, QUERIES, rows):
        block = v[cs + row : cs + min(row + rows, QUERIES), 0 : wide // 2]
        if block.shape[0] < rows:
            pad = jnp.zeros((rows - block.shape[0], wide // 2), F32)
            block = jnp.concatenate([block, pad], axis=0)
        out_ref[:, at : at + wide // 2] = block.astype(BF16)
        at += wide // 2


def output_kernel(
    cs,
    csh,
    wide,
    seq,
    bit_ref,
    *refs,
):
    own1, got1, all2, refs = *refs[:3], refs[3:]
    (
        queries_ref,
        wq_ref,
        step_ref,
        conv_ref,
        cond_ref,
        res_ref,
        skip_ref,
        gqueries_ref,
        gquery_ref,
        key_ref,
        value_ref,
        attn_ref,
        scr1,
        scr2,
        small,
        qscr,
        dq,
    ) = refs
    count, size = own1.shape[0], own1.shape[1]
    wide2 = scr2.shape[1]
    bit = bit_ref[0]
    for one, side in ((own1, bit), (got1, 1 - bit)):
        for p in range(count):
            rows = pl.ds(pl.multiple_of((side * count + p) * size, 8), size)
            scr1[rows] = one[p].astype(F32)
    for s in range(seq):
        at = ((s % 2) * count + s // 2) * size
        v = all2[s].astype(F32)
        scr2[at : at + size] = v[:, 0:wide2]
        small[s * size : (s + 1) * size] = v[:, wide2:]
    for t in range(4):
        rows = slice(t * cs, (t + 1) * cs)
        lanes = slice(t * LANES, (t + 1) * LANES)
        res_ref[:, lanes] = scr1[rows, 0:LANES]
        skip_ref[:, lanes] = scr1[rows, LANES : 2 * LANES]
        rest = 2 * C - EARLY
        step_ref[:, lanes] = scr2[rows, rest : rest + LANES]
        if t < 3:
            conv_ref[t, :, 0:EARLY] = scr1[rows, 2 * LANES : 2 * LANES + EARLY]
            conv_ref[t, :, EARLY:] = scr2[rows, 0:rest]
        else:
            cond_ref[:, 0:EARLY] = scr1[rows, 2 * LANES : 2 * LANES + EARLY]
            cond_ref[:, EARLY:] = scr2[rows, 0:rest]
    dq[...] = jnp.zeros(dq.shape, F32)
    for s in range(seq):
        v = small[s * size : (s + 1) * size]
        group, even = s // 2, s % 2 == 0
        out = key_ref if even else value_ref
        at = 0
        for row in range(0, cs, size):
            out[row : row + size, group * wide : (group + 1) * wide] = v[:, at : at + wide]
            attn_ref[row : row + size, s * csh : (s + 1) * csh] = v[:, at + wide : at + wide + csh]
            at += wide + csh
        first = group * wide + (0 if even else wide // 2)
        for row in range(0, QUERIES, size):
            count = min(size, QUERIES - row)
            dq[row : row + count, first : first + wide // 2] = v[0:count, at : at + wide // 2]
            at += wide // 2
    qscr[...] = jnp.zeros((LANES, LANES), F32)
    qscr[0:QUERIES, 0:cs] = queries_ref[...].astype(F32)
    qt = qscr[...].T.astype(BF16)
    d = dq[...]
    hi = d.astype(BF16)
    lo = (d - hi.astype(F32)).astype(BF16)
    gquery_ref[...] = (nn(qt, hi) + nn(qt, lo))[0:cs]
    gqueries_ref[...] = fold(nt(parts(d[0:QUERIES], 2), wq_ref[...]), 2)


def attention_back_kernel(
    rows,
    csh,
    dp,
    off_ref,
    prow,
    probs_ref,
    u_ref,
    qp_ref,
    qkv_ref,
    pooled_ref,
    memory_ref,
    dfilm_ref,
    got_ref,
    keep_ref,
    give_ref,
    ds,
    stack,
    right,
    out,
):
    count = got_ref.shape[0]
    total = prow.shape[1] * prow.shape[2]
    cs = C // dp
    table = prow[...].reshape(rows * total, C)
    wide = qp_ref.shape[1]
    heads = wide // HEAD_DIM
    datt = got_ref[0, 3 * RP : 4 * RP, 0:wide]
    dmem = got_ref[0, 2 * RP : 3 * RP, 0:csh]
    for s in range(1, count):
        datt = datt + got_ref[s, 3 * RP : 4 * RP, 0:wide]
        dmem = dmem + got_ref[s, 2 * RP : 3 * RP, 0:csh]
    datt = datt[0:8] * (1.0 / QUERIES)
    vh = []
    for g in range(heads):
        first = 2 * wide + g * HEAD_DIM
        v = parts(datt[:, g * HEAD_DIM : (g + 1) * HEAD_DIM], 2)
        vh.append(fold(nn(v, qkv_ref[first : first + HEAD_DIM]), 2))
    vh = jnp.concatenate(vh, axis=0)
    dp_all = fold(nt(parts(vh, 2), table), 2)
    for r in range(rows):
        cols = slice(r * total, (r + 1) * total)
        for g in range(heads):
            mine = slice(g * QUERIES, (g + 1) * QUERIES)
            p = probs_ref[mine, cols]
            dpr = dp_all[8 * g + r : 8 * g + r + 1, cols]
            inner = jnp.sum(p * dpr, axis=1, keepdims=True)
            ds[mine, cols] = p * (dpr - inner)
    tt = fold(nn(parts(ds[...], 2), table), 2)
    scale = 1.0 / math.sqrt(HEAD_DIM)
    dq = []
    stack[...] = jnp.zeros(stack.shape, F32)
    right[...] = jnp.zeros(right.shape, F32)
    stack[0 : heads * QUERIES] = tt
    stack[64:80] = u_ref[...]
    stack[80:96] = pooled_ref[...].astype(F32)
    stack[96:112] = memory_ref[...].astype(F32)
    for g in range(heads):
        cols = slice(g * HEAD_DIM, (g + 1) * HEAD_DIM)
        mine = slice(g * QUERIES, (g + 1) * QUERIES)
        wk = qkv_ref[wide + g * HEAD_DIM : wide + (g + 1) * HEAD_DIM]
        dq.append(fold(nt(parts(tt[mine], 2), wk), 2) * scale)
        right[mine, cols] = qp_ref[:, cols] * scale
        right[64 + 8 * g : 72 + 8 * g, wide + cols.start : wide + cols.stop] = datt[:, cols]
    right[80:96, 2 * wide : 2 * wide + csh] = dmem
    right[96:112, 2 * wide + csh : 2 * wide + 3 * csh] = dfilm_ref[...].astype(F32)
    out[...] = lax.dot_general(
        stack[...].T,
        right[...],
        (((1,), (0,)), ((), ())),
        precision=lax.Precision.HIGHEST,
        preferred_element_type=F32,
    )
    last = 2 * wide + 3 * csh
    for k in range(dp):
        ref = (keep_ref, give_ref)[k % 2]
        ref[k // 2] = out[pl.ds(pl.multiple_of(off_ref[k], 16), cs)].astype(BF16)
        for g in range(heads):
            first = last + g * HEAD_DIM
            ref[k // 2, 0:QUERIES, first : first + HEAD_DIM] = dq[g].astype(BF16)


def exchange(pieces, axis, groups=None):
    return lax.all_to_all(
        pieces, axis, split_axis=0, concat_axis=0, axis_index_groups=groups, tiled=True
    )


def flipped(v, axis, size, bit):
    return lax.ppermute(v, axis, [(d, d ^ bit) for d in range(size)])


class Reduction:
    def __init__(self, call, name, keep, give, dp, seq, index):
        self.call, self.name, self.dp, self.seq, self.index = call, name, dp, seq, index
        self.keep, self.flip = keep, 1
        self.got = flipped(give, "dp", dp, 1)

    def over_blocks(self, after=(), others=()):
        while 2 * self.flip < self.dp:
            group = (self,) + tuple(others)
            others = ()
            args = []
            for part in group:
                args += [part.keep, Got(part.got)]
            width = sum(part.keep.shape[2] for part in group)
            half = sds((self.keep.shape[0] // 2, self.keep.shape[1], width), BF16)
            self.keep, give = self.call(
                functools.partial(add_blocks_kernel, len(group)),
                (half, half),
                "blocks_" + self.name,
                args,
                after=after,
                in_specs=[VM] * len(args),
                out_specs=(VM, VM),
            )
            self.flip *= 2
            self.got = flipped(give, "dp", self.dp, self.flip)
        self.rest = self.keep.shape[1:]

    def over_half(self, after=()):
        rows, width = self.rest
        half = sds((rows // 2, width), BF16)
        self.keep, give = self.call(
            functools.partial(add_halves_kernel, 1),
            (half, half),
            "half_" + self.name,
            (self.index, self.keep.reshape(rows, width), Got(self.got.reshape(rows, width))),
            after=after,
            in_specs=[SM, VM, VM],
            out_specs=(VM, VM),
            scratch_shapes=[pltpu.VMEM((rows, width), F32)],
        )
        self.got = flipped(give, "seq", self.seq, 1)

    def over_pieces(self, after=()):
        rows, width = self.rest
        count = self.seq // 2
        self.groups = [[2 * k + b for k in range(count)] for b in range(2)]
        pieces = self.call(
            add_pieces_kernel,
            sds((count, rows // self.seq, width), BF16),
            "pieces_" + self.name,
            (self.keep, Got(self.got)),
            after=after,
            in_specs=[VM, VM],
            out_specs=VM,
        )
        self.got = exchange(pieces, "seq", self.groups)

    def over_copies(self, after=(), extra=None):
        args, (count, rows, width) = [Got(self.got)], self.got.shape
        if extra is not None:
            count = self.seq
        if extra is not None:
            args.append(extra)
            width += extra.shape[1]
        copies = self.call(
            sum_copies_kernel,
            sds((count, rows, width), BF16),
            "copies_" + self.name,
            args,
            after=after,
            in_specs=[VM] * len(args),
            out_specs=VM,
        )
        if extra is not None:
            return (Got(exchange(copies, "seq")),)
        own = exchange(copies, "seq", self.groups)
        return Got(own), Got(flipped(own, "seq", self.seq, 1))


def body(
    dp,
    seq,
    x_in,
    cond,
    segment_ids,
    diffusion_steps,
    prompt,
    prompt_lengths,
    w_step,
    w_conv,
    w_cond,
    w_res,
    w_skip,
    queries,
    w_query,
    w_key,
    w_value,
    w_attn_out,
    w_film,
    d_out,
    d_skip,
):
    call = Caller()
    rows = x_in.shape[0]
    frames = x_in.shape[2]
    steps = rows // NR
    cols = rows * frames
    cs = C // dp
    csh = C // seq
    heads = 2 * HEADS // seq
    wide = heads * HEAD_DIM
    arows = rows // 2
    pl_local = prompt.shape[1]
    prompt_all = pl_local * seq
    sidx = lax.axis_index("seq")
    didx = lax.axis_index("dp")
    group = (sidx // 2).astype(jnp.int32).reshape(1)
    bit = (sidx % 2).astype(jnp.int32).reshape(1)
    up = [(i, i + 1) for i in range(seq - 1)]
    down = [(i + 1, i) for i in range(seq - 1)]
    order = jnp.bitwise_xor(didx, jnp.arange(dp, dtype=jnp.int32)).astype(jnp.int32)
    offsets = jnp.concatenate([order * cs, bit, 1 - bit])
    index = sidx.astype(jnp.int32).reshape(1)

    def gather(pack, side=None, middle=None):
        if dp == 4 and side is not None:
            mine = flipped(side, "dp", dp, 2)
            inner = flipped(middle, "dp", dp, 2)
            other = flipped(mine, "seq", seq, 1)
            near = [(0, None, pack), (2, 0, mine), (2, 2, inner), (2, 1, other)]
            pieces = near + [(k + 1, h, flipped(v, "dp", dp, 1)) for k, h, v in near]
        else:
            pieces = [(0, None, pack)]
            flip = dp // 2
            while flip:
                pieces += [(k + flip, h, flipped(v, "dp", dp, flip)) for k, h, v in pieces]
                flip //= 2
        pieces.sort(key=lambda piece: piece[0])
        meta = [(k, h) for k, h, _ in pieces]
        return meta, [v if k == 0 else Got(v) for k, _, v in pieces]

    off_qkv = C + 2 * csh
    qkv_rows = -(-(3 * wide + QUERIES) // LANES) * LANES
    head_width = -(-(off_qkv + qkv_rows) // LANES) * LANES
    pack, mine, other = call(
        functools.partial(head_pack_kernel, csh, wide),
        (
            sds((cs, head_width), BF16),
            sds((arows, pl_local, C), BF16),
            sds((arows, pl_local, C), BF16),
        ),
        "head_pack",
        (
            group,
            bit,
            w_attn_out,
            jnp.transpose(w_film, (1, 2, 0)).reshape(2 * csh, cs),
            w_query,
            w_key,
            w_value,
            queries,
            prompt,
        ),
        in_specs=[SM, SM] + [VM] * 7,
        out_specs=(VM,) * 3,
        scratch_shapes=[pltpu.VMEM((2 * LANES, LANES), F32)],
    )
    _, head_pieces = gather(pack)
    partner = flipped(other, "seq", seq, 1)
    pair = call(
        pair_kernel,
        sds((seq // 2, 2, arows, pl_local, C), BF16),
        "pair",
        (mine, Got(partner)),
        in_specs=[VM, VM],
        out_specs=VM,
    )
    z_groups = [[2 * k + b for k in range(seq // 2)] for b in range(2)]
    prompts = Got(exchange(pair, "seq", z_groups))
    middle = 2 * C - 2 * SIDE + 3 * C // 4
    pack, side, middle = call(
        functools.partial(turned_pack_kernel, cs),
        (
            sds((2 * SIDE + middle, 4 * cs), BF16),
            sds((SIDE, 4 * cs), BF16),
            sds((middle, 4 * cs), BF16),
        ),
        "turned_pack",
        (bit, w_conv, w_cond, w_res, w_skip, w_step),
        after=("pair", head_pieces[dp // 2].array),
        in_specs=[SM] + [VM] * 5,
        out_specs=(VM, VM, VM),
        scratch_shapes=[pltpu.VMEM((4 * cs, 2 * C), BF16)],
    )
    meta, turned = gather(pack, side, middle)
    copies = 4 * dp * (1 + 3 * C // (4 * cs))
    first, last = call(
        edge_kernel,
        (sds((rows * SHIFT, C), BF16), sds((rows * SHIFT, C), BF16)),
        "edges",
        (x_in,),
        after=("turned_pack",),
        in_specs=[VM],
        out_specs=(VM, VM),
    )
    left_halo = lax.ppermute(last, "seq", up)
    right_halo = lax.ppermute(first, "seq", down)
    flags, block_ids, embedding = call(
        functools.partial(table_kernel, frames),
        (
            sds((2, rows), jnp.int32),
            sds((RP, seq), jnp.int32),
            sds((LANES, C), BF16),
        ),
        "tables",
        (index, diffusion_steps, segment_ids, segment_ids),
        after=("edges", left_halo, right_halo),
        in_specs=[SM, SM, SM, VM],
        out_specs=(SM, VM, VM),
    )


    apack, prow, probs, u, pooled_head, qp, qkv = call(
        functools.partial(attention_kernel, dp, arows, heads, seq // 2, off_qkv),
        (
            sds((C, head_width), BF16),
            sds((arows, seq, pl_local, C), BF16),
            sds((heads * QUERIES, arows * prompt_all), F32),
            sds((RP, C), F32),
            sds((RP, LANES), F32),
            sds((QUERIES, wide), F32),
            sds((qkv_rows, C), BF16),
        ),
        "attention",
        (offsets, bit, prompt_lengths, prompts, *head_pieces),
        after=("tables",),
        in_specs=[SM, SM, SM, HB] + [HB] * dp,
        out_specs=(VM,) * 7,
        scratch_shapes=[
            pltpu.VMEM((RP, arows * prompt_all), F32),
            pltpu.SemaphoreType.DMA((dp + seq,)),
        ],
    )

    row_block = pl.BlockSpec((NR, C, LANES), lambda i: (i, 0, 0))

    def col_block(height):
        return pl.BlockSpec((height, NR * LANES), lambda i: (0, i))

    def still(shape):
        return pl.BlockSpec(shape, lambda i: (0,) * len(shape))

    inp, gated, factor_a, factor_b, skip_out, mid, stats = call(
        functools.partial(forward_kernel, meta, dp, csh),
        (
            sds((4 * C, cols), BF16),
            sds((C, cols), BF16),
            sds((C, cols), BF16),
            sds((C, cols), BF16),
            sds(x_in.shape, BF16),
            sds((C, cols), BF16),
            sds((seq, 3 * RP, 2 * csh), F32),
        ),
        "wavenet",
        (
            offsets,
            flags,
            x_in,
            cond,
            d_out,
            Got(left_halo),
            Got(right_halo),
            embedding,
            pooled_head,
            *turned,
        ),
        flops=2 * cols * (4 * C * 2 * C + 2 * C * C),
        nbytes=30e6,
        grid=(steps,),
        in_specs=[
            SM,
            SM,
            row_block,
            row_block,
            row_block,
            whole((rows * SHIFT, C)),
            whole((rows * SHIFT, C)),
            whole((LANES, C)),
            whole((RP, LANES)),
        ]
        + [HB] * len(turned),
        out_specs=(
            col_block(4 * C),
            col_block(C),
            col_block(C),
            col_block(C),
            row_block,
            col_block(C),
            still((seq, 3 * RP, 2 * csh)),
        ),
        scratch_shapes=[
            pltpu.VMEM((2 * C, 4 * C), BF16),
            pltpu.VMEM((C, 2 * C), BF16),
            pltpu.VMEM((C, C), BF16),
            pltpu.VMEM((2 * C, C), BF16),
            pltpu.VMEM((C, LANES), F32),
            pltpu.VMEM((C, LANES), F32),
            pltpu.VMEM((C, LANES), F32),
            pltpu.VMEM((C, LANES), F32),
            pltpu.SemaphoreType.DMA((copies,)),
        ],
    )
    stats_got = exchange(stats, "seq")
    gskip = call(
        skip_grad_kernel,
        sds((C, C), BF16),
        "skip",
        (gated, d_skip),
        in_specs=[VM, VM],
        out_specs=VM,
        scratch_shapes=[pltpu.VMEM((C, cols), BF16)],
    )

    coef_out, dfilm, pooled, memory = call(
        functools.partial(stats_kernel, csh, heads, arows),
        (
            sds((seq, 4 * RP, 2 * csh), F32),
            sds((RP, 2 * csh), BF16),
            sds((RP, C), BF16),
            sds((RP, C), BF16),
        ),
        "segments",
        (block_ids, Got(stats_got), apack),
        after=("skip",),
        in_specs=[VM, VM, VM],
        out_specs=(VM, VM, VM, VM),
        scratch_shapes=[pltpu.VMEM((RP, C), F32)],
    )
    coef = Got(exchange(coef_out, "seq"))

    def gate_block(i):
        return jnp.minimum(i, steps - 1)

    def shard(i):
        return jnp.maximum(i - steps, 0)

    def gate_cols(height):
        return pl.BlockSpec((height, NR * LANES), lambda i, order: (0, gate_block(i)))

    gate_rows = pl.BlockSpec((NR, C, LANES), lambda i, order: (gate_block(i), 0, 0))
    wide1, wide2 = EARLY + 2 * LANES, 2 * C - EARLY

    def part(width):
        return sds((dp // 2, 4 * cs, width), BF16)

    def part_spec(width):
        return pl.BlockSpec((1, 4 * cs, width), lambda i, order: (shard(i) // 2, 0, 0))

    outs = call(
        functools.partial(backward_kernel, meta, dp, csh, steps),
        (
            sds((2 * C, cols), BF16),
            sds((C, cols), BF16),
            sds((2 * C, LANES), F32),
            part(wide1),
            part(wide2),
            part(wide1),
            part(wide2),
        ),
        "backward",
        (order, offsets, coef, mid, d_out, d_skip, factor_a, factor_b, inp, gated, gskip, flags, *turned),
        prefetch=1,
        grid=(steps + dp,),
        in_specs=[
            SM,
            pl.BlockSpec(
                (seq, 4 * RP, 2 * csh), lambda i, order: (0, 0, 0), pipeline_mode=pl.Buffered(1)
            ),
            gate_cols(C),
            gate_rows,
            gate_rows,
            gate_cols(C),
            gate_cols(C),
            pl.BlockSpec((4 * cs, cols), lambda i, order: (order[shard(i)], 0)),
            pl.BlockSpec((cs, cols), lambda i, order: (order[shard(i)], 0)),
            pl.BlockSpec((cs, C), lambda i, order: (order[shard(i)], 0)),
            SM,
        ]
        + [HB] * len(turned),
        out_specs=(
            gate_cols(2 * C),
            gate_cols(C),
            pl.BlockSpec((2 * C, LANES), lambda i, order: (0, 0)),
            part_spec(wide1),
            part_spec(wide2),
            part_spec(wide1),
            part_spec(wide2),
        ),
        scratch_shapes=[
            pltpu.VMEM((LANES, C), F32),
            pltpu.VMEM((C, LANES), F32),
            pltpu.VMEM((C, 2 * C), BF16),
            pltpu.VMEM((2 * C, NR * LANES), BF16),
            pltpu.VMEM((cols, 2 * C), BF16),
            pltpu.VMEM((cols, C), BF16),
            pltpu.SemaphoreType.DMA((copies,)),
        ],
    )
    dpre, dres, sums = outs[0:3]
    part1 = Reduction(call, "1", outs[3], outs[5], dp, seq, index)
    part2 = Reduction(call, "2", outs[4], outs[6], dp, seq, index)
    part1.over_blocks()
    keep, give = call(
        functools.partial(step_grad_kernel, meta, dp),
        (part(LANES), part(LANES)),
        "step_grad",
        (offsets, sums, embedding, *turned),
        after=("blocks_1",),
        in_specs=[SM, VM, VM] + [HB] * len(turned),
        out_specs=(VM, VM),
        scratch_shapes=[
            pltpu.VMEM((2 * C, 4 * C), BF16),
            pltpu.VMEM((C, C), F32),
            pltpu.SemaphoreType.DMA((copies,)),
        ],
    )
    part_step = Reduction(call, "step", keep, give, dp, seq, index)

    right_width = -(-(3 * wide + 3 * csh) // LANES) * LANES
    block = sds((dp // 2, cs, right_width), BF16)
    keep, give = call(
        functools.partial(attention_back_kernel, arows, csh, dp),
        (block, block),
        "attention_back",
        (offsets, prow, probs, u, qp, qkv, pooled, memory, dfilm, coef),
        after=("step_grad",),
        in_specs=[SM] + [VM] * 9,
        out_specs=(VM, VM),
        scratch_shapes=[
            pltpu.VMEM((heads * QUERIES, arows * prompt_all), F32),
            pltpu.VMEM((LANES, C), F32),
            pltpu.VMEM((LANES, right_width), F32),
            pltpu.VMEM((C, right_width), F32),
        ],
    )
    small = Reduction(call, "small", keep, give, dp, seq, index)
    part2.over_blocks(("attention_back",), (part_step,))
    small.over_blocks(("blocks_2",))
    part1.over_half(("blocks_small",))

    rest = 4 * cs // seq
    small_width = (cs // rest) * (wide + csh) + max(1, QUERIES // rest) * (wide // 2)
    part2.over_half(("half_1",))
    part1.over_pieces(("half_2",))
    grad_film, attn_rows, mine, other = call(
        functools.partial(small_sum_kernel, csh, wide),
        (
            sds((2 * csh, cs), F32),
            sds((cs, csh), F32),
            sds((cs + QUERIES, wide), BF16),
            sds((cs + QUERIES, wide), BF16),
        ),
        "small_sum",
        (bit, small.keep, Got(small.got)),
        after=("pieces_1",),
        in_specs=[SM, VM, VM],
        out_specs=(VM,) * 4,
        scratch_shapes=[pltpu.VMEM((LANES, LANES), F32)],
    )
    partner = flipped(other, "seq", seq, 1)
    part2.over_pieces(("small_sum",))
    small_piece = call(
        functools.partial(small_piece_kernel, csh, wide),
        sds((rest, small_width), BF16),
        "small_piece",
        (attn_rows, mine, Got(partner)),
        after=("pieces_2",),
        in_specs=[VM] * 3,
        out_specs=VM,
    )
    ones = part1.over_copies(("small_piece",))
    base, first, last = call(
        functools.partial(input_grad_kernel, meta, dp),
        (sds((C, cols), BF16), sds((rows * SHIFT, C), BF16), sds((rows * SHIFT, C), BF16)),
        "input_grad",
        (offsets, dpre, dres, *turned),
        after=("copies_1",),
        grid=(steps,),
        in_specs=[SM, col_block(2 * C), col_block(C)] + [HB] * len(turned),
        out_specs=(
            col_block(C),
            still((rows * SHIFT, C)),
            still((rows * SHIFT, C)),
        ),
        scratch_shapes=[
            pltpu.VMEM((2 * C, 4 * C), BF16),
            pltpu.VMEM((3, C, 2 * C), BF16),
            pltpu.VMEM((C, LANES), F32),
            pltpu.VMEM((C, LANES), F32),
            pltpu.SemaphoreType.DMA((copies,)),
        ],
    )
    from_left = lax.ppermute(last, "seq", up)
    from_right = lax.ppermute(first, "seq", down)
    twos = part2.over_copies(
        ("input_grad", ones[0].array, from_left, from_right), extra=small_piece
    )

    grad_input, layer_out = call(
        functools.partial(finish_kernel, csh),
        (sds(x_in.shape, BF16), sds(x_in.shape, BF16)),
        "grad_input",
        (flags, base, Got(from_left), Got(from_right), mid, coef),
        after=("input_grad",),
        grid=(steps,),
        in_specs=[
            SM,
            col_block(C),
            whole((rows * SHIFT, C)),
            whole((rows * SHIFT, C)),
            col_block(C),
            whole((seq, 4 * RP, 2 * csh)),
        ],
        out_specs=(row_block, row_block),
        scratch_shapes=[pltpu.VMEM((LANES, C), F32)] + [pltpu.VMEM((C, LANES), F32)] * 3,
    )

    (
        grad_step,
        grad_conv,
        grad_cond,
        grad_res,
        grad_skip,
        grad_queries,
        grad_query,
        grad_key,
        grad_value,
        grad_attn,
    ) = call(
        functools.partial(output_kernel, cs, csh, wide, seq),
        (
            sds((cs, C), F32),
            sds((3, cs, 2 * C), F32),
            sds((cs, 2 * C), F32),
            sds((cs, C), F32),
            sds((cs, C), F32),
            sds((QUERIES, cs), F32),
            sds((cs, C), F32),
            sds((cs, C), F32),
            sds((cs, C), F32),
            sds((cs, C), F32),
        ),
        "outputs",
        after=("grad_input",),
        args=(bit, *ones, *twos, queries, w_query),
        in_specs=[SM] + [VM] * 5,
        out_specs=(VM,) * 10,
        scratch_shapes=[
            pltpu.VMEM((4 * cs, wide1), F32),
            pltpu.VMEM((4 * cs, wide2 + LANES), F32),
            pltpu.VMEM((4 * cs, small_width), F32),
            pltpu.VMEM((LANES, LANES), F32),
            pltpu.VMEM((LANES, C), F32),
        ],
    )
    return (
        layer_out,
        skip_out,
        grad_input,
        grad_step,
        grad_conv,
        grad_cond,
        grad_res,
        grad_skip,
        grad_queries,
        grad_query,
        grad_key,
        grad_value,
        grad_attn,
        jnp.transpose(grad_film.reshape(2, csh, cs), (2, 0, 1)),
    )


def solution(mesh):
    frames = P("dp", None, "seq")
    matrix = P("dp", None)
    return jax.shard_map(
        functools.partial(body, mesh.shape["dp"], mesh.shape["seq"]),
        mesh=mesh,
        in_specs=(
            frames,
            frames,
            P("dp", None),
            P("dp"),
            P("dp", "seq", None),
            P("dp"),
            matrix,
            P(None, "dp", None),
            matrix,
            matrix,
            matrix,
            P(None, "dp"),
            matrix,
            matrix,
            matrix,
            matrix,
            frames,
            frames,
            frames,
        ),
        out_specs=(
            frames,
            frames,
            frames,
            matrix,
            P(None, "dp", None),
            matrix,
            matrix,
            matrix,
            P(None, "dp"),
            matrix,
            matrix,
            matrix,
            matrix,
            frames,
        ),
        check_vma=False,
    )
```

```python
import functools
import math

import jax
import jax.numpy as jnp
from jax import lax
from jax.experimental import pallas as pl
from jax.experimental.pallas import tpu as pltpu
from jax.sharding import PartitionSpec as P

C = 512
HEADS = 8
QUERIES = 32
HEAD_DIM = 64
SHIFT = 4
SQRT_HALF = 0.7071067811865476
NORM_EPS = 1e-05
MASKED_SCORE = -1e30
LANES = 128
RP = 16
NR = 4
EARLY = 640
F32 = jnp.float32
BF16 = jnp.bfloat16
VMEM_BYTES = 50 * 1024 * 1024


def nn(a, b):
    return lax.dot_general(a, b, (((1,), (0,)), ((), ())), preferred_element_type=F32)


def nt(a, b):
    return lax.dot_general(a, b, (((1,), (1,)), ((), ())), preferred_element_type=F32)


def parts(v, count):
    out = []
    for _ in range(count):
        low = v.astype(BF16).astype(F32)
        out.append(low)
        v = v - low
    return jnp.concatenate(out, axis=0).astype(BF16)


def fold(v, count):
    rows = v.shape[0] // count
    total = v[:rows]
    for k in range(1, count):
        total = total + v[k * rows : (k + 1) * rows]
    return total


def lane_ids(shape):
    return lax.broadcasted_iota(jnp.int32, shape, len(shape) - 1)


def sds(shape, dtype):
    return jax.ShapeDtypeStruct(shape, dtype)


VM = pl.BlockSpec(memory_space=pltpu.VMEM)
HB = pl.BlockSpec(memory_space=pl.ANY)
SM = pl.BlockSpec(memory_space=pltpu.SMEM)


def whole(shape):
    return pl.BlockSpec(shape, lambda i: (0,) * len(shape), pipeline_mode=pl.Buffered(1))


class Got:
    def __init__(self, array):
        self.array = array


class Caller:
    def __init__(self):
        self.done = {}

    def __call__(self, kernel, out_shape, name, args, flops=0, nbytes=0, prefetch=0, after=(), **kw):
        single = not isinstance(out_shape, tuple)
        shapes = (out_shape,) if single else out_shape
        specs = kw["out_specs"]
        specs = (specs,) if single else specs
        pinned = tuple(
            v if spec is SM else pltpu.HBM(v.shape, v.dtype) for v, spec in zip(shapes, specs)
        )
        in_specs = list(kw.pop("in_specs"))
        count = prefetch + len(in_specs)
        args = list(args)
        extra = len(after)
        for before in after:
            in_specs.append(HB)
            args.append(self.done[before] if isinstance(before, str) else before)

        def run(*refs):
            return kernel(*refs[:count], *refs[count + extra :])

        values = []
        for k, v in enumerate(args):
            spec = SM if k < prefetch else in_specs[k - prefetch]
            if isinstance(v, Got):
                values.append(v.array)
            elif spec is SM:
                values.append(v)
            else:
                values.append(pltpu.with_memory_space_constraint(v, pltpu.HBM))
        spec = pltpu.PrefetchScalarGridSpec(
            num_scalar_prefetch=prefetch,
            grid=kw.pop("grid", ()),
            in_specs=in_specs,
            out_specs=kw.pop("out_specs"),
            scratch_shapes=kw.pop("scratch_shapes", ()),
        )
        out = pl.pallas_call(
            run,
            out_shape=pinned[0] if single else pinned,
            name=name,
            grid_spec=spec,
            cost_estimate=pl.CostEstimate(
                flops=1, bytes_accessed=1, transcendentals=0
            ),
            compiler_params=pltpu.CompilerParams(vmem_limit_bytes=VMEM_BYTES),
        )(*values)
        self.done[name] = out if single else out[0]
        return out


def head_pack_kernel(
    csh,
    local,
    group_ref,
    bit_ref,
    attn_ref,
    film_ref,
    wq_ref,
    wk_ref,
    wv_ref,
    queries_ref,
    prompt_ref,
    out_ref,
    mine_ref,
    other_ref,
    scr,
):
    cs = attn_ref.shape[0]
    arows = mine_ref.shape[0]
    mine_ref[...] = prompt_ref[pl.ds(bit_ref[0] * arows, arows)]
    other_ref[...] = prompt_ref[pl.ds((1 - bit_ref[0]) * arows, arows)]
    out_ref[:, 0:C] = attn_ref[...]
    off = C
    scr[...] = jnp.zeros((2 * LANES, LANES), F32)
    scr[0 : 2 * csh, 0:cs] = film_ref[...].astype(F32)
    scr[LANES : LANES + QUERIES, 0:cs] = queries_ref[...].astype(F32)
    film = scr[0:LANES].T[0:cs]
    table = scr[LANES : 2 * LANES].T[0:cs]
    turn = lax.rem(C - local * group_ref[0], C)
    blocks = [film[:, 0 : 2 * csh]]
    for ref in (wq_ref, wk_ref, wv_ref):
        blocks.append(pltpu.roll(ref[...].astype(F32), turn, 1)[:, 0:local])
    blocks.append(table)
    for block in blocks:
        width = min(block.shape[1], out_ref.shape[1] - off)
        out_ref[:, off : off + width] = block[:, 0:width].astype(BF16)
        off += width
    if off < out_ref.shape[1]:
        out_ref[:, off:] = jnp.zeros((cs, out_ref.shape[1] - off), BF16)


SIDE = 480


def turned_pack_kernel(cs, bit_ref, conv_ref, cond_ref, res_ref, skip_ref, step_ref, out_ref, side_ref, middle_ref, scr):
    for k in range(3):
        scr[k * cs : (k + 1) * cs] = conv_ref[k]
    scr[3 * cs : 4 * cs] = cond_ref[...]
    turned = scr[...].T
    out_ref[0 : 2 * C - SIDE] = turned[0 : 2 * C - SIDE]
    at = 2 * C - SIDE
    for ref in (res_ref, skip_ref, step_ref):
        for lane in range(0, C, 4 * cs):
            out_ref[at : at + cs] = ref[:, lane : lane + 4 * cs]
            at += cs
    out_ref[at : at + SIDE] = turned[2 * C - SIDE :]
    middle_ref[...] = out_ref[SIDE:at]
    side_ref[...] = out_ref[pl.ds(pl.multiple_of(bit_ref[0] * at, 16), SIDE)]


def pair_kernel(a_ref, b_ref, out_ref):
    for p in range(out_ref.shape[0]):
        out_ref[p, 0] = a_ref[...]
        out_ref[p, 1] = b_ref[...]


def edge_kernel(x_ref, flags_ref, ids_ref, emb_ref, first_ref, last_ref, flags_out, ids_out, emb_out):
    for side in range(2):
        for r in range(x_ref.shape[0]):
            flags_out[side, r] = flags_ref[side, r]
    ids_out[...] = ids_ref[...]
    emb_out[...] = emb_ref[...]
    rows = x_ref.shape[0]
    lane = lane_ids((C, LANES))
    first = jnp.zeros((C, LANES), F32)
    last = jnp.zeros((C, LANES), F32)
    for r in range(rows):
        v = x_ref[r].astype(F32)
        here = (lane // SHIFT) == r
        first = jnp.where(here, pltpu.roll(v, SHIFT * r, 1) if r else v, first)
        last = jnp.where(here, pltpu.roll(v, SHIFT * r + SHIFT, 1), last)
    first_ref[...] = first.astype(BF16)
    last_ref[...] = last.astype(BF16)


def begin(copies):
    for copy in copies:
        copy.start()


def finish(copies):
    for copy in copies:
        copy.wait()


def turned_copies(meta, refs, off_ref, cs, wt, others, sems):
    dp = len({k for k, _ in meta})
    pairs = []

    def conv(k, ref, first, row, rows):
        if wt is not None:
            lanes = pl.ds(pl.multiple_of(off_ref[k] * 4, LANES), 4 * cs)
            at = row if isinstance(row, int) else pl.multiple_of(row, 16)
            pairs.append((ref.at[pl.ds(first, rows)], wt.at[pl.ds(at, rows), lanes]))

    def rest(k, ref, at):
        row = pl.ds(pl.multiple_of(off_ref[k], 16), cs)
        for other in others:
            for lane in range(0, C, 4 * cs):
                if other is not None:
                    dst, start = other
                    pairs.append((ref.at[pl.ds(at, cs)], dst.at[row, pl.ds(start + lane, 4 * cs)]))
                at += cs

    inner = 2 * C - 2 * SIDE
    for (k, which), ref in zip(meta, refs):
        if which is None:
            conv(k, ref, 0, 0, SIDE + inner)
            rest(k, ref, SIDE + inner)
            conv(k, ref, ref.shape[0] - SIDE, 2 * C - SIDE, SIDE)
        elif which == 2:
            conv(k, ref, 0, SIDE, inner)
            rest(k, ref, inner)
        else:
            conv(k, ref, 0, off_ref[dp + which] * (2 * C - SIDE), SIDE)
    return [pltpu.make_async_copy(a, b, sems.at[n]) for n, (a, b) in enumerate(pairs)]


def head_copies(refs, off_ref, dst, sems):
    copies = []
    for k, ref in enumerate(refs):
        row = pl.ds(pl.multiple_of(off_ref[k], 16), ref.shape[0])
        copies.append(pltpu.make_async_copy(ref, dst.at[row], sems.at[k]))
    return copies


def forward_kernel(
    meta, dp, csh, off_ref, flags_ref, x_ref, cond_ref, dout_ref, left_ref, right_ref, emb_ref, pooled_ref, *refs
):
    turned, refs = refs[: len(meta)], refs[len(meta) :]
    (
        inp_ref,
        gated_ref,
        fa_ref,
        fb_ref,
        skip_ref,
        mid_ref,
        stats_ref,
        wt_ref,
        rn_ref,
        step_ref,
        rst_ref,
        lift_ref,
        acc_ref,
        sems,
    ) = refs
    cs = C // dp
    i = pl.program_id(0)
    lane = lane_ids((C, LANES))

    @pl.when(i == 0)
    def _():
        copies = turned_copies(
            meta,
            turned,
            off_ref,
            cs,
            wt_ref,
            ((rn_ref, 0), (rn_ref, C), (step_ref, 0)),
            sems,
        )
        begin(copies)
        acc_ref[...] = jnp.zeros((C, LANES), F32)
        finish(copies)
        lift = nn(emb_ref[0:RP], step_ref[...])
        lift = jnp.concatenate([lift, jnp.zeros((LANES - RP, C), F32)], axis=0)
        lift_ref[...] = lift.T
        rst_ref[...] = rn_ref[...].T

    lift = pltpu.roll(lift_ref[...], lax.rem(LANES - NR * i, LANES), 1)
    left = left_ref[...].astype(F32)
    right = right_ref[...].astype(F32)

    def put(tap, cols, value):
        for d in range(dp):
            at = d * 4 * cs + tap * cs
            inp_ref[at : at + cs, cols] = value[d * cs : (d + 1) * cs]

    for j in range(NR):
        r = NR * i + j
        lc = lift[:, j : j + 1]
        sh = (x_ref[j].astype(F32) + lc).astype(BF16)
        shf = sh.astype(F32)
        lh = pltpu.roll(left, lax.rem(LANES - SHIFT * r, LANES), 1)
        lh = jnp.where(flags_ref[0, r] > 0, (lh + lc).astype(BF16).astype(F32), 0.0)
        rh = pltpu.roll(right, LANES - SHIFT - SHIFT * r, 1)
        rh = jnp.where(flags_ref[1, r] > 0, (rh + lc).astype(BF16).astype(F32), 0.0)
        cols = slice(j * LANES, (j + 1) * LANES)
        put(0, cols, jnp.where(lane < SHIFT, lh, pltpu.roll(shf, SHIFT, 1)).astype(BF16))
        put(1, cols, sh)
        put(
            2,
            cols,
            jnp.where(lane >= LANES - SHIFT, rh, pltpu.roll(shf, LANES - SHIFT, 1)).astype(BF16),
        )
        put(3, cols, cond_ref[j])
    pre = nn(wt_ref[...], inp_ref[...])
    th = jnp.tanh(pre[:C])
    sg = jax.nn.sigmoid(pre[C:])
    gf = th * sg
    fa_ref[...] = (sg - gf * th).astype(BF16)
    fb_ref[...] = (gf * (1.0 - sg)).astype(BF16)
    g = gf.astype(BF16)
    gated_ref[...] = g
    rs = nn(rst_ref[...], g)
    acc = acc_ref[...]
    for j in range(NR):
        r = NR * i + j
        cols = slice(j * LANES, (j + 1) * LANES)
        skip_ref[j] = rs[C:, cols].astype(BF16)
        mid = ((x_ref[j].astype(F32) + rs[:C, cols]) * SQRT_HALF).astype(BF16)
        mid_ref[:, cols] = mid
        mf = mid.astype(F32)
        df = dout_ref[j].astype(F32)
        total = jnp.sum(mf, axis=1, keepdims=True)
        dev = mf - total * (1.0 / LANES)
        acc = jnp.where(lane == r, total, acc)
        acc = jnp.where(lane == RP + r, jnp.sum(dev * dev, axis=1, keepdims=True), acc)
        acc = jnp.where(lane == 2 * RP + r, jnp.sum(df, axis=1, keepdims=True), acc)
        acc = jnp.where(lane == 3 * RP + r, jnp.sum(df * dev, axis=1, keepdims=True), acc)
    acc_ref[...] = acc

    @pl.when(i == pl.num_programs(0) - 1)
    def _():
        t = acc.T
        for s in range(C // csh):
            cols = slice(s * csh, (s + 1) * csh)
            stats_ref[s, 0 : 2 * RP, 0:csh] = t[0 : 2 * RP, cols]
            stats_ref[s, 0 : 2 * RP, csh : 2 * csh] = t[2 * RP : 4 * RP, cols]
            stats_ref[s, 2 * RP : 3 * RP] = pooled_ref[:, 0 : 2 * csh]


def attention_kernel(dp, rows, heads, pairs, off, off_ref, bit_ref, len_ref, prompts, *refs):
    pieces, refs = refs[:dp], refs[dp:]
    apack_ref, prow, probs_ref, u_ref, pooled_ref, qp_ref, qkv_ref, abd, sems = refs
    copies = head_copies(pieces, off_ref, apack_ref, sems)
    count = len(copies)
    for j in range(pairs):
        for i in range(2):
            copies.append(
                pltpu.make_async_copy(
                    prompts.at[j, i], prow.at[:, 2 * j + i], sems.at[count + 2 * j + i]
                )
            )
    begin(copies)
    local = prow.shape[2]
    total = 2 * pairs * local
    abd[...] = jnp.zeros(abd.shape, F32)
    lane = lane_ids((heads * QUERIES, total))
    place = jnp.zeros((heads * QUERIES, total), jnp.int32)
    for k in range(2 * pairs):
        here = (k // 2) * 2 + (bit_ref[0] if k % 2 == 0 else 1 - bit_ref[0])
        place = jnp.where(lane // local == k, here * local + lane % local, place)
    finish(copies)
    wide = heads * HEAD_DIM
    qkv = apack_ref[:, off : off + qkv_ref.shape[0]].T
    qkv_ref[...] = qkv
    qp = nt(qkv[3 * wide : 3 * wide + QUERIES], qkv[0:wide])
    qp_ref[...] = qp
    st = []
    for g in range(heads):
        cols = slice(g * HEAD_DIM, (g + 1) * HEAD_DIM)
        st.append(fold(nn(parts(qp[:, cols], 3), qkv[wide + cols.start : wide + cols.stop]), 3))
    st = jnp.concatenate(st, axis=0) * (1.0 / math.sqrt(HEAD_DIM))
    table = prow[...].reshape(rows * total, C)
    scores = fold(nt(parts(st, 3), table), 3)
    for r in range(rows):
        cols = slice(r * total, (r + 1) * total)
        live = place < len_ref[r]
        s = jnp.where(live, scores[:, cols], MASKED_SCORE)
        e = jnp.where(live, jnp.exp(s - jnp.max(s, axis=1, keepdims=True)), 0.0)
        p = e / jnp.sum(e, axis=1, keepdims=True)
        probs_ref[:, cols] = p
        for g in range(heads):
            abd[8 * g + r : 8 * g + r + 1, cols] = jnp.sum(
                p[g * QUERIES : (g + 1) * QUERIES], axis=0, keepdims=True
            )
    u = fold(nn(parts(abd[...], 2), table), 2)
    u_ref[...] = u
    pooled_ref[...] = jnp.zeros(pooled_ref.shape, F32)
    for g in range(heads):
        first = 2 * wide + g * HEAD_DIM
        v = parts(u[8 * g : 8 * g + 8] * (1.0 / QUERIES), 2)
        pooled_ref[0:8, g * HEAD_DIM : (g + 1) * HEAD_DIM] = fold(
            nt(v, qkv[first : first + HEAD_DIM]), 2
        )


def stats_kernel(
    csh, heads, rows, seg_ref, x_ref, apack_ref, out_ref, dfilm_ref, pooled_ref, memory_ref, scratch
):
    count = x_ref.shape[0]
    wide = heads * HEAD_DIM
    seg = seg_ref[...]
    scratch[...] = jnp.zeros(scratch.shape, F32)
    for s in range(count):
        group, part = s // 2, s % 2
        scratch[part * rows : (part + 1) * rows, group * wide : (group + 1) * wide] = x_ref[
            s, 2 * RP : 2 * RP + rows, 0:wide
        ]
    pooled = scratch[...].astype(BF16)
    pooled_ref[...] = pooled
    memory = nn(pooled, apack_ref[:, 0:C]).astype(BF16)
    memory_ref[...] = memory
    film = nn(memory, apack_ref[:, C : C + 2 * csh])
    f0 = film[:, 0:csh]
    f1 = film[:, csh : 2 * csh]
    total = [x_ref[s, 0:RP, 0:csh] for s in range(count)]
    second = [x_ref[s, RP : 2 * RP, 0:csh] for s in range(count)]
    dsum = [x_ref[s, 0:RP, csh : 2 * csh] for s in range(count)]
    cross = [x_ref[s, RP : 2 * RP, csh : 2 * csh] for s in range(count)]
    means = [v * (1.0 / LANES) for v in total]
    d0 = jnp.zeros((RP, csh), F32)
    d1 = jnp.zeros((RP, csh), F32)
    for me in range(count):
        same = [(seg[:, s : s + 1] == seg[:, me : me + 1]).astype(F32) for s in range(count)]
        frames = sum(same) * float(LANES)
        inv = 1.0 / frames
        mean = sum(m * v for m, v in zip(same, total)) * inv
        var = (
            sum(
                m * (v + float(LANES) * (u - mean) * (u - mean))
                for m, v, u in zip(same, second, means)
            )
            * inv
        )
        scale = lax.rsqrt(var + NORM_EPS)
        dtot = sum(m * v for m, v in zip(same, dsum))
        xtot = sum(m * (v + (u - mean) * d) for m, v, u, d in zip(same, cross, means, dsum)) * scale
        mean_part = f0 * dtot * inv
        cross_part = f0 * xtot * inv
        slope = scale * scale * cross_part
        out_ref[me, 0:RP, 0:csh] = 1.0 + f0 * scale
        out_ref[me, RP : 2 * RP, 0:csh] = f1 - f0 * scale * mean
        out_ref[me, 0:RP, csh : 2 * csh] = -slope
        out_ref[me, RP : 2 * RP, csh : 2 * csh] = slope * mean - scale * mean_part
        d0 = d0 + (cross[me] + (means[me] - mean) * dsum[me]) * scale
        d1 = d1 + dsum[me]
    dfilm = jnp.concatenate([d0, d1], axis=1).astype(BF16)
    dfilm_ref[...] = dfilm
    dmem = nt(dfilm, apack_ref[:, C : C + 2 * csh])
    dpool = nt(dmem.astype(BF16), apack_ref[:, 0:C])
    for s in range(count):
        group, part = s // 2, s % 2
        rolled = pltpu.roll(dpool, RP - part * rows, 0) if part else dpool
        out_ref[s, 2 * RP : 3 * RP, 0:csh] = dmem[:, s * csh : (s + 1) * csh]
        out_ref[s, 2 * RP : 3 * RP, csh : 2 * csh] = jnp.zeros((RP, csh), F32)
        out_ref[s, 3 * RP : 4 * RP] = rolled[:, group * wide : (group + 1) * wide]


def coef_columns(csh, coef_ref, rows_ref, cols_ref):
    rows_ref[...] = jnp.zeros(rows_ref.shape, F32)
    for s in range(C // csh):
        cols = slice(s * csh, (s + 1) * csh)
        rows_ref[0 : 2 * RP, cols] = coef_ref[s, 0 : 2 * RP, 0:csh]
        rows_ref[2 * RP : 4 * RP, cols] = coef_ref[s, 0 : 2 * RP, csh : 2 * csh]
    cols_ref[...] = rows_ref[...].T


def skip_grad_kernel(gated_ref, dskip_ref, out_ref, right):
    for r in range(dskip_ref.shape[0]):
        right[:, r * LANES : (r + 1) * LANES] = dskip_ref[r]
    out_ref[...] = nt(gated_ref[...], right[...]).astype(BF16)


def backward_kernel(meta, dp, csh, gates, order_ref, off_ref, coef_ref, mid_ref, dout_ref, dskip_ref, fa_ref, fb_ref, inp_ref, gated_ref, gskip_ref, flags_ref, *refs):
    turned, refs = refs[: len(meta)], refs[len(meta) :]
    dpre_ref, dres_ref, sums_ref, refs = refs[0], refs[1], refs[2], refs[3:]
    outs, refs = (refs[0:2], refs[2:4]), refs[4:]
    rows_ref, cols_ref, w_ref, both_ref, dpt_ref, drt_ref, sems = refs
    cs = C // dp
    span = NR * LANES
    i = pl.program_id(0)

    @pl.when(i == 0)
    def _():
        copies = turned_copies(
            meta, turned, off_ref, cs, None, ((w_ref, 0), (w_ref, C), None), sems
        )
        begin(copies)
        coef_columns(csh, coef_ref, rows_ref, cols_ref)
        sums_ref[...] = jnp.zeros(sums_ref.shape, F32)
        finish(copies)

    @pl.when(i < gates)
    def _():
        coef = pltpu.roll(cols_ref[...], lax.rem(LANES - NR * i, LANES), 1)
        for j in range(NR):
            cols = slice(j * LANES, (j + 1) * LANES)
            mf = mid_ref[:, cols].astype(F32)
            df = dout_ref[j].astype(F32)
            a = coef[:, j : j + 1]
            be = coef[:, 2 * RP + j : 2 * RP + j + 1]
            ga = coef[:, 3 * RP + j : 3 * RP + j + 1]
            dmid = (a * df + (be * mf + ga)).astype(BF16).astype(F32)
            both_ref[0:C, cols] = (dmid * SQRT_HALF).astype(BF16)
            both_ref[C : 2 * C, cols] = dskip_ref[j]
        dres = both_ref[0:C]
        dres_ref[...] = dres
        dg = nn(w_ref[...], both_ref[...])
        dt = (dg * fa_ref[...].astype(F32)).astype(BF16)
        ds = (dg * fb_ref[...].astype(F32)).astype(BF16)
        dpre_ref[0:C] = dt
        dpre_ref[C : 2 * C] = ds
        at = pl.ds(pl.multiple_of(i * span, span), span)
        dpt_ref[at, 0:C] = dt.T
        dpt_ref[at, C : 2 * C] = ds.T
        drt_ref[at] = dres.T
        frame = lax.broadcasted_iota(jnp.int32, (span, LANES), 0)
        column = lane_ids((span, LANES))
        place = frame % LANES
        which = frame // LANES
        keep_l = jnp.zeros((span, LANES), jnp.int32)
        keep_r = jnp.zeros((span, LANES), jnp.int32)
        for j in range(NR):
            keep_l = jnp.where(which == j, flags_ref[0, NR * i + j], keep_l)
            keep_r = jnp.where(which == j, flags_ref[1, NR * i + j], keep_r)
        row = NR * i + which
        use0 = (column == row) & ((place >= SHIFT) | (keep_l > 0))
        use1 = column == RP + row
        use2 = (column == 2 * RP + row) & ((place < LANES - SHIFT) | (keep_r > 0))
        pick = jnp.where(use0 | use1 | use2, 1.0, 0.0).astype(BF16)
        sums_ref[...] = sums_ref[...] + nn(dpre_ref[...], pick)

    @pl.when(i >= gates)
    def _():
        g = nn(inp_ref[...], dpt_ref[...]).astype(BF16)
        h = nn(gated_ref[...], drt_ref[...]).astype(BF16)
        k = i - gates
        for parity, (one, two) in enumerate(outs):

            @pl.when(lax.rem(k, 2) == parity)
            def _():
                for t in range(4):
                    rows = slice(t * cs, (t + 1) * cs)
                    lanes = slice(t * LANES, (t + 1) * LANES)
                    one[0, rows, 0:LANES] = h[:, lanes]
                    one[0, rows, LANES : 2 * LANES] = gskip_ref[:, lanes]
                one[0, :, 2 * LANES :] = g[:, 0:EARLY]
                two[0] = g[:, EARLY:]


def step_grad_kernel(meta, dp, off_ref, sums_ref, emb_ref, *refs):
    turned, refs = refs[: len(meta)], refs[len(meta) :]
    keep_ref, give_ref, wt_ref, scr, sems = refs
    cs = C // dp
    copies = turned_copies(meta, turned, off_ref, cs, wt_ref, (None,) * 3, sems)
    begin(copies)
    sums = sums_ref[...].T
    emb = emb_ref[...].T
    finish(copies)
    total = jnp.zeros((RP, 4 * C), F32)
    lane = lane_ids((RP, 4 * C))
    all_taps = fold(nn(parts(sums[0 : 3 * RP], 2), wt_ref[...]), 2)
    for t in range(3):
        g = all_taps[t * RP : (t + 1) * RP]
        total = total + jnp.where((lane // cs) % 4 == t, g, 0.0)
    out = []
    for d in range(dp):
        block = total[:, d * 4 * cs : (d + 1) * 4 * cs]
        out.append(block[:, 0:cs] + block[:, cs : 2 * cs] + block[:, 2 * cs : 3 * cs])
    g = jnp.concatenate(out, axis=1)
    g = jnp.concatenate([g, jnp.zeros((LANES - RP, C), F32)], axis=0)
    hi = g.astype(BF16)
    lo = (g - hi.astype(F32)).astype(BF16)
    scr[...] = nn(emb, hi) + nn(emb, lo)
    for k in range(dp):
        v = scr[pl.ds(pl.multiple_of(off_ref[k], 16), cs)].astype(BF16)
        for t in range(4):
            (keep_ref, give_ref)[k % 2][k // 2, t * cs : (t + 1) * cs] = v[
                :, t * LANES : (t + 1) * LANES
            ]


def input_grad_kernel(meta, dp, off_ref, dpre_ref, dres_ref, *refs):
    turned, refs = refs[: len(meta)], refs[len(meta) :]
    base_ref, first_ref, last_ref, wt_ref, w_ref, facc_ref, lacc_ref, sems = refs
    cs = C // dp
    i = pl.program_id(0)
    lane = lane_ids((C, LANES))

    @pl.when(i == 0)
    def _():
        copies = turned_copies(meta, turned, off_ref, cs, wt_ref, (None,) * 3, sems)
        begin(copies)
        facc_ref[...] = jnp.zeros((C, LANES), F32)
        lacc_ref[...] = jnp.zeros((C, LANES), F32)
        finish(copies)
        for d in range(dp):
            v = wt_ref[:, d * 4 * cs : (d + 1) * 4 * cs].T
            for t in range(3):
                w_ref[t, d * cs : (d + 1) * cs] = v[t * cs : (t + 1) * cs]

    dpre = dpre_ref[...]
    y0 = nn(w_ref[0], dpre)
    y1 = nn(w_ref[1], dpre)
    y2 = nn(w_ref[2], dpre)
    facc = facc_ref[...]
    lacc = lacc_ref[...]
    for j in range(NR):
        r = NR * i + j
        cols = slice(j * LANES, (j + 1) * LANES)
        z0 = pltpu.roll(y0[:, cols], LANES - SHIFT, 1)
        z2 = pltpu.roll(y2[:, cols], SHIFT, 1)
        inner0 = lane < LANES - SHIFT
        inner2 = lane >= SHIFT
        v = y1[:, cols]
        base_ref[:, cols] = (
            v
            + jnp.where(inner0, z0, 0.0)
            + jnp.where(inner2, z2, 0.0)
            + dres_ref[:, cols].astype(F32)
        ).astype(BF16)
        here = (lane // SHIFT) == r
        facc = jnp.where(here, pltpu.roll(z0, lax.rem(SHIFT * r + SHIFT, LANES), 1), facc)
        lacc = jnp.where(here, pltpu.roll(z2, SHIFT * r, 1), lacc)
    facc_ref[...] = facc
    lacc_ref[...] = lacc

    @pl.when(i == pl.num_programs(0) - 1)
    def _():
        first_ref[...] = facc.astype(BF16)
        last_ref[...] = lacc.astype(BF16)


def finish_kernel(csh, flags_ref, base_ref, left_ref, right_ref, mid_ref, coef_ref, out_ref, layer_ref, rows_ref, cols_ref):
    i = pl.program_id(0)
    lane = lane_ids((C, LANES))

    @pl.when(i == 0)
    def _():
        coef_columns(csh, coef_ref, rows_ref, cols_ref)

    coef = pltpu.roll(cols_ref[...], lax.rem(LANES - NR * i, LANES), 1)
    left = left_ref[...].astype(F32)
    right = right_ref[...].astype(F32)
    for j in range(NR):
        r = NR * i + j
        cols = slice(j * LANES, (j + 1) * LANES)
        lh = pltpu.roll(left, lax.rem(LANES - SHIFT * r, LANES), 1)
        rh = pltpu.roll(right, LANES - SHIFT - SHIFT * r, 1)
        lh = jnp.where((lane < SHIFT) & (flags_ref[0, r] > 0), lh, 0.0)
        rh = jnp.where((lane >= LANES - SHIFT) & (flags_ref[1, r] > 0), rh, 0.0)
        out_ref[j] = (base_ref[:, cols].astype(F32) + lh + rh).astype(BF16)
        a = coef[:, j : j + 1]
        b = coef[:, RP + j : RP + j + 1]
        layer_ref[j] = (a * mid_ref[:, cols].astype(F32) + b).astype(BF16)


def add_blocks_kernel(count, *refs):
    ins, (keep_ref, give_ref) = refs[: 2 * count], refs[2 * count :]
    at = 0
    for p in range(count):
        a_ref, b_ref = ins[2 * p : 2 * p + 2]
        width = a_ref.shape[2]
        for j in range(a_ref.shape[0]):
            v = a_ref[j].astype(F32) + b_ref[j].astype(F32)
            (keep_ref, give_ref)[j % 2][j // 2, :, at : at + width] = v.astype(BF16)
        at += width


def add_halves_kernel(bit, index_ref, a_ref, b_ref, keep_ref, give_ref, scr):
    half = a_ref.shape[0] // 2
    mine = lax.rem(index_ref[0] // bit, 2)
    scr[...] = a_ref[...].astype(F32) + b_ref[...].astype(F32)
    keep_ref[...] = scr[pl.ds(pl.multiple_of(mine * half, 8), half)].astype(BF16)
    give_ref[...] = scr[pl.ds(pl.multiple_of((1 - mine) * half, 8), half)].astype(BF16)


def add_pieces_kernel(a_ref, b_ref, out_ref):
    v = a_ref[...].astype(F32) + b_ref[...].astype(F32)
    size = out_ref.shape[1]
    for p in range(out_ref.shape[0]):
        out_ref[p] = v[p * size : (p + 1) * size].astype(BF16)


def sum_copies_kernel(a_ref, *refs):
    out_ref = refs[-1]
    v = a_ref[0].astype(F32)
    for p in range(1, a_ref.shape[0]):
        v = v + a_ref[p].astype(F32)
    v = v.astype(BF16)
    for p in range(out_ref.shape[0]):
        out_ref[p, :, 0 : v.shape[1]] = v
        if len(refs) > 1:
            out_ref[p, :, v.shape[1] :] = refs[0][...]


def small_sum_kernel(csh, wide, bit_ref, keep_ref, got_ref, film_ref, attn_ref, mine_ref, other_ref, turn):
    v = keep_ref[0].astype(F32) + got_ref[0].astype(F32)
    cs = v.shape[0]
    film = 2 * wide + csh
    turn[...] = jnp.zeros(turn.shape, F32)
    turn[0:cs, 0 : 2 * csh] = v[:, film : film + 2 * csh]
    film_ref[...] = turn[...].T[0 : 2 * csh, 0:cs]
    attn_ref[...] = v[:, 2 * wide : film]
    last = film + 2 * csh
    even = bit_ref[0] == 0
    for one, two, rows, width in (
        (v[:, 0:wide], v[:, wide : 2 * wide], slice(0, cs), wide),
        (
            v[0:QUERIES, last : last + wide // 2],
            v[0:QUERIES, last + wide // 2 : last + wide],
            slice(cs, cs + QUERIES),
            wide // 2,
        ),
    ):
        mine_ref[rows, 0:width] = jnp.where(even, one, two).astype(BF16)
        other_ref[rows, 0:width] = jnp.where(even, two, one).astype(BF16)
    mine_ref[cs:, wide // 2 :] = jnp.zeros((QUERIES, wide // 2), BF16)
    other_ref[cs:, wide // 2 :] = jnp.zeros((QUERIES, wide // 2), BF16)


def small_piece_kernel(csh, wide, attn_ref, mine_ref, got_ref, out_ref):
    v = mine_ref[...].astype(F32) + got_ref[...].astype(F32)
    attn = attn_ref[...]
    cs = attn.shape[0]
    rows = out_ref.shape[0]
    at = 0
    for row in range(0, cs, rows):
        out_ref[:, at : at + wide] = v[row : row + rows].astype(BF16)
        out_ref[:, at + wide : at + wide + csh] = attn[row : row + rows].astype(BF16)
        at += wide + csh
    for row in range(0, QUERIES, rows):
        block = v[cs + row : cs + min(row + rows, QUERIES), 0 : wide // 2]
        if block.shape[0] < rows:
            pad = jnp.zeros((rows - block.shape[0], wide // 2), F32)
            block = jnp.concatenate([block, pad], axis=0)
        out_ref[:, at : at + wide // 2] = block.astype(BF16)
        at += wide // 2


def output_kernel(
    cs,
    csh,
    wide,
    seq,
    bit_ref,
    *refs,
):
    own1, got1, all2, refs = *refs[:3], refs[3:]
    (
        queries_ref,
        wq_ref,
        step_ref,
        conv_ref,
        cond_ref,
        res_ref,
        skip_ref,
        gqueries_ref,
        gquery_ref,
        key_ref,
        value_ref,
        attn_ref,
        scr1,
        scr2,
        small,
        qscr,
        dq,
    ) = refs
    count, size = own1.shape[0], own1.shape[1]
    wide2 = scr2.shape[1]
    bit = bit_ref[0]
    for one, side in ((own1, bit), (got1, 1 - bit)):
        for p in range(count):
            rows = pl.ds(pl.multiple_of((side * count + p) * size, 8), size)
            scr1[rows] = one[p].astype(F32)
    for s in range(seq):
        at = ((s % 2) * count + s // 2) * size
        v = all2[s].astype(F32)
        scr2[at : at + size] = v[:, 0:wide2]
        small[s * size : (s + 1) * size] = v[:, wide2:]
    for t in range(4):
        rows = slice(t * cs, (t + 1) * cs)
        lanes = slice(t * LANES, (t + 1) * LANES)
        res_ref[:, lanes] = scr1[rows, 0:LANES]
        skip_ref[:, lanes] = scr1[rows, LANES : 2 * LANES]
        rest = 2 * C - EARLY
        step_ref[:, lanes] = scr2[rows, rest : rest + LANES]
        if t < 3:
            conv_ref[t, :, 0:EARLY] = scr1[rows, 2 * LANES : 2 * LANES + EARLY]
            conv_ref[t, :, EARLY:] = scr2[rows, 0:rest]
        else:
            cond_ref[:, 0:EARLY] = scr1[rows, 2 * LANES : 2 * LANES + EARLY]
            cond_ref[:, EARLY:] = scr2[rows, 0:rest]
    dq[...] = jnp.zeros(dq.shape, F32)
    for s in range(seq):
        v = small[s * size : (s + 1) * size]
        group, even = s // 2, s % 2 == 0
        out = key_ref if even else value_ref
        at = 0
        for row in range(0, cs, size):
            out[row : row + size, group * wide : (group + 1) * wide] = v[:, at : at + wide]
            attn_ref[row : row + size, s * csh : (s + 1) * csh] = v[:, at + wide : at + wide + csh]
            at += wide + csh
        first = group * wide + (0 if even else wide // 2)
        for row in range(0, QUERIES, size):
            count = min(size, QUERIES - row)
            dq[row : row + count, first : first + wide // 2] = v[0:count, at : at + wide // 2]
            at += wide // 2
    qscr[...] = jnp.zeros((LANES, LANES), F32)
    qscr[0:QUERIES, 0:cs] = queries_ref[...].astype(F32)
    qt = qscr[...].T.astype(BF16)
    d = dq[...]
    hi = d.astype(BF16)
    lo = (d - hi.astype(F32)).astype(BF16)
    gquery_ref[...] = (nn(qt, hi) + nn(qt, lo))[0:cs]
    gqueries_ref[...] = fold(nt(parts(d[0:QUERIES], 2), wq_ref[...]), 2)


def attention_back_kernel(
    rows,
    csh,
    dp,
    off_ref,
    prow,
    probs_ref,
    u_ref,
    qp_ref,
    qkv_ref,
    pooled_ref,
    memory_ref,
    dfilm_ref,
    got_ref,
    keep_ref,
    give_ref,
    ds,
    stack,
    right,
    out,
):
    count = got_ref.shape[0]
    total = prow.shape[1] * prow.shape[2]
    cs = C // dp
    table = prow[...].reshape(rows * total, C)
    wide = qp_ref.shape[1]
    heads = wide // HEAD_DIM
    datt = got_ref[0, 3 * RP : 4 * RP, 0:wide]
    dmem = got_ref[0, 2 * RP : 3 * RP, 0:csh]
    for s in range(1, count):
        datt = datt + got_ref[s, 3 * RP : 4 * RP, 0:wide]
        dmem = dmem + got_ref[s, 2 * RP : 3 * RP, 0:csh]
    datt = datt[0:8] * (1.0 / QUERIES)
    vh = []
    for g in range(heads):
        first = 2 * wide + g * HEAD_DIM
        v = parts(datt[:, g * HEAD_DIM : (g + 1) * HEAD_DIM], 2)
        vh.append(fold(nn(v, qkv_ref[first : first + HEAD_DIM]), 2))
    vh = jnp.concatenate(vh, axis=0)
    dp_all = fold(nt(parts(vh, 2), table), 2)
    for r in range(rows):
        cols = slice(r * total, (r + 1) * total)
        for g in range(heads):
            mine = slice(g * QUERIES, (g + 1) * QUERIES)
            p = probs_ref[mine, cols]
            dpr = dp_all[8 * g + r : 8 * g + r + 1, cols]
            inner = jnp.sum(p * dpr, axis=1, keepdims=True)
            ds[mine, cols] = p * (dpr - inner)
    tt = fold(nn(parts(ds[...], 2), table), 2)
    scale = 1.0 / math.sqrt(HEAD_DIM)
    dq = []
    stack[...] = jnp.zeros(stack.shape, F32)
    right[...] = jnp.zeros(right.shape, F32)
    stack[0 : heads * QUERIES] = tt
    stack[64:80] = u_ref[...]
    stack[80:96] = pooled_ref[...].astype(F32)
    stack[96:112] = memory_ref[...].astype(F32)
    for g in range(heads):
        cols = slice(g * HEAD_DIM, (g + 1) * HEAD_DIM)
        mine = slice(g * QUERIES, (g + 1) * QUERIES)
        wk = qkv_ref[wide + g * HEAD_DIM : wide + (g + 1) * HEAD_DIM]
        dq.append(fold(nt(parts(tt[mine], 2), wk), 2) * scale)
        right[mine, cols] = qp_ref[:, cols] * scale
        right[64 + 8 * g : 72 + 8 * g, wide + cols.start : wide + cols.stop] = datt[:, cols]
    right[80:96, 2 * wide : 2 * wide + csh] = dmem
    right[96:112, 2 * wide + csh : 2 * wide + 3 * csh] = dfilm_ref[...].astype(F32)
    out[...] = lax.dot_general(
        stack[...].T,
        right[...],
        (((1,), (0,)), ((), ())),
        precision=lax.Precision.HIGHEST,
        preferred_element_type=F32,
    )
    last = 2 * wide + 3 * csh
    for k in range(dp):
        ref = (keep_ref, give_ref)[k % 2]
        ref[k // 2] = out[pl.ds(pl.multiple_of(off_ref[k], 16), cs)].astype(BF16)
        for g in range(heads):
            first = last + g * HEAD_DIM
            ref[k // 2, 0:QUERIES, first : first + HEAD_DIM] = dq[g].astype(BF16)


def exchange(pieces, axis, groups=None):
    return lax.all_to_all(
        pieces, axis, split_axis=0, concat_axis=0, axis_index_groups=groups, tiled=True
    )


def flipped(v, axis, size, bit):
    return lax.ppermute(v, axis, [(d, d ^ bit) for d in range(size)])


class Reduction:
    def __init__(self, call, name, keep, give, dp, seq, index):
        self.call, self.name, self.dp, self.seq, self.index = call, name, dp, seq, index
        self.keep, self.flip = keep, 1
        self.got = flipped(give, "dp", dp, 1)

    def over_blocks(self, after=(), others=()):
        while 2 * self.flip < self.dp:
            group = (self,) + tuple(others)
            others = ()
            args = []
            for part in group:
                args += [part.keep, Got(part.got)]
            width = sum(part.keep.shape[2] for part in group)
            half = sds((self.keep.shape[0] // 2, self.keep.shape[1], width), BF16)
            self.keep, give = self.call(
                functools.partial(add_blocks_kernel, len(group)),
                (half, half),
                "blocks_" + self.name,
                args,
                after=after,
                in_specs=[VM] * len(args),
                out_specs=(VM, VM),
            )
            self.flip *= 2
            self.got = flipped(give, "dp", self.dp, self.flip)
        self.rest = self.keep.shape[1:]

    def over_half(self, after=()):
        rows, width = self.rest
        half = sds((rows // 2, width), BF16)
        self.keep, give = self.call(
            functools.partial(add_halves_kernel, 1),
            (half, half),
            "half_" + self.name,
            (self.index, self.keep.reshape(rows, width), Got(self.got.reshape(rows, width))),
            after=after,
            in_specs=[SM, VM, VM],
            out_specs=(VM, VM),
            scratch_shapes=[pltpu.VMEM((rows, width), F32)],
        )
        self.got = flipped(give, "seq", self.seq, 1)

    def over_pieces(self, after=()):
        rows, width = self.rest
        count = self.seq // 2
        self.groups = [[2 * k + b for k in range(count)] for b in range(2)]
        pieces = self.call(
            add_pieces_kernel,
            sds((count, rows // self.seq, width), BF16),
            "pieces_" + self.name,
            (self.keep, Got(self.got)),
            after=after,
            in_specs=[VM, VM],
            out_specs=VM,
        )
        self.got = exchange(pieces, "seq", self.groups)

    def over_copies(self, after=(), extra=None):
        args, (count, rows, width) = [Got(self.got)], self.got.shape
        if extra is not None:
            count = self.seq
        if extra is not None:
            args.append(extra)
            width += extra.shape[1]
        copies = self.call(
            sum_copies_kernel,
            sds((count, rows, width), BF16),
            "copies_" + self.name,
            args,
            after=after,
            in_specs=[VM] * len(args),
            out_specs=VM,
        )
        if extra is not None:
            return (Got(exchange(copies, "seq")),)
        own = exchange(copies, "seq", self.groups)
        return Got(own), Got(flipped(own, "seq", self.seq, 1))


def body(
    dp,
    seq,
    x_in,
    cond,
    segment_ids,
    diffusion_steps,
    prompt,
    prompt_lengths,
    w_step,
    w_conv,
    w_cond,
    w_res,
    w_skip,
    queries,
    w_query,
    w_key,
    w_value,
    w_attn_out,
    w_film,
    d_out,
    d_skip,
):
    call = Caller()
    rows = x_in.shape[0]
    frames = x_in.shape[2]
    steps = rows // NR
    cols = rows * frames
    cs = C // dp
    csh = C // seq
    heads = 2 * HEADS // seq
    wide = heads * HEAD_DIM
    arows = rows // 2
    pl_local = prompt.shape[1]
    prompt_all = pl_local * seq
    sidx = lax.axis_index("seq")
    didx = lax.axis_index("dp")
    group = (sidx // 2).astype(jnp.int32).reshape(1)
    bit = (sidx % 2).astype(jnp.int32).reshape(1)
    up = [(i, i + 1) for i in range(seq - 1)]
    down = [(i + 1, i) for i in range(seq - 1)]
    order = jnp.bitwise_xor(didx, jnp.arange(dp, dtype=jnp.int32)).astype(jnp.int32)
    offsets = jnp.concatenate([order * cs, bit, 1 - bit])
    index = sidx.astype(jnp.int32).reshape(1)

    def gather(pack, side=None, middle=None):
        if dp == 4 and side is not None:
            mine = flipped(side, "dp", dp, 2)
            inner = flipped(middle, "dp", dp, 2)
            other = flipped(mine, "seq", seq, 1)
            near = [(0, None, pack), (2, 0, mine), (2, 2, inner), (2, 1, other)]
            pieces = near + [(k + 1, h, flipped(v, "dp", dp, 1)) for k, h, v in near]
        else:
            pieces = [(0, None, pack)]
            flip = dp // 2
            while flip:
                pieces += [(k + flip, h, flipped(v, "dp", dp, flip)) for k, h, v in pieces]
                flip //= 2
        pieces.sort(key=lambda piece: piece[0])
        meta = [(k, h) for k, h, _ in pieces]
        return meta, [v if k == 0 else Got(v) for k, _, v in pieces]

    off_qkv = C + 2 * csh
    qkv_rows = -(-(3 * wide + QUERIES) // LANES) * LANES
    head_width = -(-(off_qkv + qkv_rows) // LANES) * LANES
    pack, mine, other = call(
        functools.partial(head_pack_kernel, csh, wide),
        (
            sds((cs, head_width), BF16),
            sds((arows, pl_local, C), BF16),
            sds((arows, pl_local, C), BF16),
        ),
        "head_pack",
        (
            group,
            bit,
            w_attn_out,
            jnp.transpose(w_film, (1, 2, 0)).reshape(2 * csh, cs),
            w_query,
            w_key,
            w_value,
            queries,
            prompt,
        ),
        in_specs=[SM, SM] + [VM] * 7,
        out_specs=(VM,) * 3,
        scratch_shapes=[pltpu.VMEM((2 * LANES, LANES), F32)],
    )
    _, head_pieces = gather(pack)
    partner = flipped(other, "seq", seq, 1)
    pair = call(
        pair_kernel,
        sds((seq // 2, 2, arows, pl_local, C), BF16),
        "pair",
        (mine, Got(partner)),
        in_specs=[VM, VM],
        out_specs=VM,
    )
    middle = 2 * C - 2 * SIDE + 3 * C // 4
    pack, side, middle = call(
        functools.partial(turned_pack_kernel, cs),
        (
            sds((2 * SIDE + middle, 4 * cs), BF16),
            sds((SIDE, 4 * cs), BF16),
            sds((middle, 4 * cs), BF16),
        ),
        "turned_pack",
        (bit, w_conv, w_cond, w_res, w_skip, w_step),
        after=("pair", head_pieces[dp // 2].array),
        in_specs=[SM] + [VM] * 5,
        out_specs=(VM, VM, VM),
        scratch_shapes=[pltpu.VMEM((4 * cs, 2 * C), BF16)],
    )
    meta, turned = gather(pack, side, middle)
    copies = 4 * dp * (1 + 3 * C // (4 * cs))
    z_groups = [[2 * k + b for k in range(seq // 2)] for b in range(2)]
    prompts = Got(exchange(pair, "seq", z_groups))
    block_ids = segment_ids[:, ::frames]
    padded_ids = jnp.pad(block_ids, ((0, 0), (1, 1)), constant_values=-1)
    mine = lax.dynamic_slice_in_dim(padded_ids, sidx, 3, 1)
    flags = jnp.stack([mine[:, 0] == mine[:, 1], mine[:, 2] == mine[:, 1]]).astype(jnp.int32)
    block_ids = jnp.pad(block_ids, ((0, RP - rows), (0, 0)))
    half = C // 2
    frequency = jnp.exp(jnp.arange(half, dtype=F32) * (-math.log(10000.0) / half))
    step_rows = jnp.pad(diffusion_steps.astype(F32), (0, LANES - rows))
    live_rows = jnp.arange(LANES, dtype=jnp.int32)[:, None] < rows
    angles = step_rows[:, None] * frequency[None, :]
    embedding = jnp.concatenate([jnp.sin(angles), jnp.cos(angles)], axis=1)
    embedding = jnp.where(live_rows, embedding, 0.0).astype(BF16)
    first, last, flags, block_ids, embedding = call(
        edge_kernel,
        (
            sds((C, LANES), BF16),
            sds((C, LANES), BF16),
            sds(flags.shape, jnp.int32),
            sds(block_ids.shape, jnp.int32),
            sds(embedding.shape, BF16),
        ),
        "edges",
        (x_in, flags, block_ids, embedding),
        after=("turned_pack",),
        in_specs=[VM, SM, VM, VM],
        out_specs=(VM, VM, SM, VM, VM),
    )
    left_halo = lax.ppermute(last, "seq", up)
    right_halo = lax.ppermute(first, "seq", down)

    lengths = lax.dynamic_slice_in_dim(prompt_lengths, (sidx % 2) * arows, arows, 0)

    apack, prow, probs, u, pooled_head, qp, qkv = call(
        functools.partial(attention_kernel, dp, arows, heads, seq // 2, off_qkv),
        (
            sds((C, head_width), BF16),
            sds((arows, seq, pl_local, C), BF16),
            sds((heads * QUERIES, arows * prompt_all), F32),
            sds((RP, C), F32),
            sds((RP, LANES), F32),
            sds((QUERIES, wide), F32),
            sds((qkv_rows, C), BF16),
        ),
        "attention",
        (offsets, bit, lengths, prompts, *head_pieces),
        in_specs=[SM, SM, SM, HB] + [HB] * dp,
        out_specs=(VM,) * 7,
        scratch_shapes=[
            pltpu.VMEM((RP, arows * prompt_all), F32),
            pltpu.SemaphoreType.DMA((dp + seq,)),
        ],
    )

    row_block = pl.BlockSpec((NR, C, LANES), lambda i: (i, 0, 0))

    def col_block(height):
        return pl.BlockSpec((height, NR * LANES), lambda i: (0, i))

    def still(shape):
        return pl.BlockSpec(shape, lambda i: (0,) * len(shape))

    inp, gated, factor_a, factor_b, skip_out, mid, stats = call(
        functools.partial(forward_kernel, meta, dp, csh),
        (
            sds((4 * C, cols), BF16),
            sds((C, cols), BF16),
            sds((C, cols), BF16),
            sds((C, cols), BF16),
            sds(x_in.shape, BF16),
            sds((C, cols), BF16),
            sds((seq, 3 * RP, 2 * csh), F32),
        ),
        "wavenet",
        (
            offsets,
            flags,
            x_in,
            cond,
            d_out,
            Got(left_halo),
            Got(right_halo),
            embedding,
            pooled_head,
            *turned,
        ),
        flops=2 * cols * (4 * C * 2 * C + 2 * C * C),
        nbytes=30e6,
        grid=(steps,),
        in_specs=[
            SM,
            SM,
            row_block,
            row_block,
            row_block,
            whole((C, LANES)),
            whole((C, LANES)),
            whole((LANES, C)),
            whole((RP, LANES)),
        ]
        + [HB] * len(turned),
        out_specs=(
            col_block(4 * C),
            col_block(C),
            col_block(C),
            col_block(C),
            row_block,
            col_block(C),
            still((seq, 3 * RP, 2 * csh)),
        ),
        scratch_shapes=[
            pltpu.VMEM((2 * C, 4 * C), BF16),
            pltpu.VMEM((C, 2 * C), BF16),
            pltpu.VMEM((C, C), BF16),
            pltpu.VMEM((2 * C, C), BF16),
            pltpu.VMEM((C, LANES), F32),
            pltpu.VMEM((C, LANES), F32),
            pltpu.SemaphoreType.DMA((copies,)),
        ],
    )
    stats_got = exchange(stats, "seq")
    gskip = call(
        skip_grad_kernel,
        sds((C, C), BF16),
        "skip",
        (gated, d_skip),
        in_specs=[VM, VM],
        out_specs=VM,
        scratch_shapes=[pltpu.VMEM((C, cols), BF16)],
    )

    coef_out, dfilm, pooled, memory = call(
        functools.partial(stats_kernel, csh, heads, arows),
        (
            sds((seq, 4 * RP, 2 * csh), F32),
            sds((RP, 2 * csh), BF16),
            sds((RP, C), BF16),
            sds((RP, C), BF16),
        ),
        "segments",
        (block_ids, Got(stats_got), apack),
        after=("skip",),
        in_specs=[VM, VM, VM],
        out_specs=(VM, VM, VM, VM),
        scratch_shapes=[pltpu.VMEM((RP, C), F32)],
    )
    coef = Got(exchange(coef_out, "seq"))

    def gate_block(i):
        return jnp.minimum(i, steps - 1)

    def shard(i):
        return jnp.maximum(i - steps, 0)

    def gate_cols(height):
        return pl.BlockSpec((height, NR * LANES), lambda i, order: (0, gate_block(i)))

    gate_rows = pl.BlockSpec((NR, C, LANES), lambda i, order: (gate_block(i), 0, 0))
    wide1, wide2 = EARLY + 2 * LANES, 2 * C - EARLY

    def part(width):
        return sds((dp // 2, 4 * cs, width), BF16)

    def part_spec(width):
        return pl.BlockSpec((1, 4 * cs, width), lambda i, order: (shard(i) // 2, 0, 0))

    outs = call(
        functools.partial(backward_kernel, meta, dp, csh, steps),
        (
            sds((2 * C, cols), BF16),
            sds((C, cols), BF16),
            sds((2 * C, LANES), F32),
            part(wide1),
            part(wide2),
            part(wide1),
            part(wide2),
        ),
        "backward",
        (order, offsets, coef, mid, d_out, d_skip, factor_a, factor_b, inp, gated, gskip, flags, *turned),
        prefetch=1,
        grid=(steps + dp,),
        in_specs=[
            SM,
            pl.BlockSpec(
                (seq, 4 * RP, 2 * csh), lambda i, order: (0, 0, 0), pipeline_mode=pl.Buffered(1)
            ),
            gate_cols(C),
            gate_rows,
            gate_rows,
            gate_cols(C),
            gate_cols(C),
            pl.BlockSpec((4 * cs, cols), lambda i, order: (order[shard(i)], 0)),
            pl.BlockSpec((cs, cols), lambda i, order: (order[shard(i)], 0)),
            pl.BlockSpec((cs, C), lambda i, order: (order[shard(i)], 0)),
            SM,
        ]
        + [HB] * len(turned),
        out_specs=(
            gate_cols(2 * C),
            gate_cols(C),
            pl.BlockSpec((2 * C, LANES), lambda i, order: (0, 0)),
            part_spec(wide1),
            part_spec(wide2),
            part_spec(wide1),
            part_spec(wide2),
        ),
        scratch_shapes=[
            pltpu.VMEM((LANES, C), F32),
            pltpu.VMEM((C, LANES), F32),
            pltpu.VMEM((C, 2 * C), BF16),
            pltpu.VMEM((2 * C, NR * LANES), BF16),
            pltpu.VMEM((cols, 2 * C), BF16),
            pltpu.VMEM((cols, C), BF16),
            pltpu.SemaphoreType.DMA((copies,)),
        ],
    )
    dpre, dres, sums = outs[0:3]
    part1 = Reduction(call, "1", outs[3], outs[5], dp, seq, index)
    part2 = Reduction(call, "2", outs[4], outs[6], dp, seq, index)
    part1.over_blocks()
    keep, give = call(
        functools.partial(step_grad_kernel, meta, dp),
        (part(LANES), part(LANES)),
        "step_grad",
        (offsets, sums, embedding, *turned),
        after=("blocks_1",),
        in_specs=[SM, VM, VM] + [HB] * len(turned),
        out_specs=(VM, VM),
        scratch_shapes=[
            pltpu.VMEM((2 * C, 4 * C), BF16),
            pltpu.VMEM((C, C), F32),
            pltpu.SemaphoreType.DMA((copies,)),
        ],
    )
    part_step = Reduction(call, "step", keep, give, dp, seq, index)

    right_width = -(-(3 * wide + 3 * csh) // LANES) * LANES
    block = sds((dp // 2, cs, right_width), BF16)
    keep, give = call(
        functools.partial(attention_back_kernel, arows, csh, dp),
        (block, block),
        "attention_back",
        (offsets, prow, probs, u, qp, qkv, pooled, memory, dfilm, coef),
        after=("step_grad",),
        in_specs=[SM] + [VM] * 9,
        out_specs=(VM, VM),
        scratch_shapes=[
            pltpu.VMEM((heads * QUERIES, arows * prompt_all), F32),
            pltpu.VMEM((LANES, C), F32),
            pltpu.VMEM((LANES, right_width), F32),
            pltpu.VMEM((C, right_width), F32),
        ],
    )
    small = Reduction(call, "small", keep, give, dp, seq, index)
    part2.over_blocks(("attention_back",), (part_step,))
    small.over_blocks(("blocks_2",))
    part1.over_half(("blocks_small",))

    rest = 4 * cs // seq
    small_width = (cs // rest) * (wide + csh) + max(1, QUERIES // rest) * (wide // 2)
    part2.over_half(("half_1",))
    part1.over_pieces(("half_2",))
    grad_film, attn_rows, mine, other = call(
        functools.partial(small_sum_kernel, csh, wide),
        (
            sds((2 * csh, cs), F32),
            sds((cs, csh), F32),
            sds((cs + QUERIES, wide), BF16),
            sds((cs + QUERIES, wide), BF16),
        ),
        "small_sum",
        (bit, small.keep, Got(small.got)),
        after=("pieces_1",),
        in_specs=[SM, VM, VM],
        out_specs=(VM,) * 4,
        scratch_shapes=[pltpu.VMEM((LANES, LANES), F32)],
    )
    partner = flipped(other, "seq", seq, 1)
    part2.over_pieces(("small_sum",))
    small_piece = call(
        functools.partial(small_piece_kernel, csh, wide),
        sds((rest, small_width), BF16),
        "small_piece",
        (attn_rows, mine, Got(partner)),
        after=("pieces_2",),
        in_specs=[VM] * 3,
        out_specs=VM,
    )
    ones = part1.over_copies(("small_piece",))
    base, first, last = call(
        functools.partial(input_grad_kernel, meta, dp),
        (sds((C, cols), BF16), sds((C, LANES), BF16), sds((C, LANES), BF16)),
        "input_grad",
        (offsets, dpre, dres, *turned),
        after=("copies_1",),
        grid=(steps,),
        in_specs=[SM, col_block(2 * C), col_block(C)] + [HB] * len(turned),
        out_specs=(
            col_block(C),
            still((C, LANES)),
            still((C, LANES)),
        ),
        scratch_shapes=[
            pltpu.VMEM((2 * C, 4 * C), BF16),
            pltpu.VMEM((3, C, 2 * C), BF16),
            pltpu.VMEM((C, LANES), F32),
            pltpu.VMEM((C, LANES), F32),
            pltpu.SemaphoreType.DMA((copies,)),
        ],
    )
    from_left = lax.ppermute(last, "seq", up)
    from_right = lax.ppermute(first, "seq", down)
    twos = part2.over_copies(("input_grad", ones[0].array), extra=small_piece)

    grad_input, layer_out = call(
        functools.partial(finish_kernel, csh),
        (sds(x_in.shape, BF16), sds(x_in.shape, BF16)),
        "grad_input",
        (flags, base, Got(from_left), Got(from_right), mid, coef),
        after=("input_grad",),
        grid=(steps,),
        in_specs=[
            SM,
            col_block(C),
            whole((C, LANES)),
            whole((C, LANES)),
            col_block(C),
            whole((seq, 4 * RP, 2 * csh)),
        ],
        out_specs=(row_block, row_block),
        scratch_shapes=[pltpu.VMEM((LANES, C), F32), pltpu.VMEM((C, LANES), F32)],
    )

    (
        grad_step,
        grad_conv,
        grad_cond,
        grad_res,
        grad_skip,
        grad_queries,
        grad_query,
        grad_key,
        grad_value,
        grad_attn,
    ) = call(
        functools.partial(output_kernel, cs, csh, wide, seq),
        (
            sds((cs, C), F32),
            sds((3, cs, 2 * C), F32),
            sds((cs, 2 * C), F32),
            sds((cs, C), F32),
            sds((cs, C), F32),
            sds((QUERIES, cs), F32),
            sds((cs, C), F32),
            sds((cs, C), F32),
            sds((cs, C), F32),
            sds((cs, C), F32),
        ),
        "outputs",
        after=("grad_input",),
        args=(bit, *ones, *twos, queries, w_query),
        in_specs=[SM] + [VM] * 5,
        out_specs=(VM,) * 10,
        scratch_shapes=[
            pltpu.VMEM((4 * cs, wide1), F32),
            pltpu.VMEM((4 * cs, wide2 + LANES), F32),
            pltpu.VMEM((4 * cs, small_width), F32),
            pltpu.VMEM((LANES, LANES), F32),
            pltpu.VMEM((LANES, C), F32),
        ],
    )
    return (
        layer_out,
        skip_out,
        grad_input,
        grad_step,
        grad_conv,
        grad_cond,
        grad_res,
        grad_skip,
        grad_queries,
        grad_query,
        grad_key,
        grad_value,
        grad_attn,
        jnp.transpose(grad_film.reshape(2, csh, cs), (2, 0, 1)),
    )


def solution(mesh):
    frames = P("dp", None, "seq")
    matrix = P("dp", None)
    return jax.shard_map(
        functools.partial(body, mesh.shape["dp"], mesh.shape["seq"]),
        mesh=mesh,
        in_specs=(
            frames,
            frames,
            P("dp", None),
            P("dp"),
            P("dp", "seq", None),
            P("dp"),
            matrix,
            P(None, "dp", None),
            matrix,
            matrix,
            matrix,
            P(None, "dp"),
            matrix,
            matrix,
            matrix,
            matrix,
            frames,
            frames,
            frames,
        ),
        out_specs=(
            frames,
            frames,
            frames,
            matrix,
            P(None, "dp", None),
            matrix,
            matrix,
            matrix,
            P(None, "dp"),
            matrix,
            matrix,
            matrix,
            matrix,
            frames,
        ),
        check_vma=False,
    )
```
